32 devices in a mesh: seq: 8 (over z, x), fsdp: 4 (over y, core).
Axes of the slice: x: 2, y: 2, z: 4, core: 2. Of those that a mesh axis runs over, the one named last changes fastest.
Arguments:
- states: bfloat16 [4, 1024, 276], P('fsdp', 'seq'), may hold values from -6 to 6
- targets: bfloat16 [4, 1024, 276], P('fsdp', 'seq'), may hold values from -6 to 6
- lengths: int32 [4], P('fsdp'), may hold values from 1 to 2, as said below
- intervals: int32 [4], replicated, may hold values from 0 to 2
- qkv_copy: bfloat16 [1024, 3072], P(None, 'fsdp'), may hold values from -0.1875 to 0.1875
- qkv_master: float32 [1024, 3072], P('seq', 'fsdp'), may hold values from -0.1875 to 0.1875
- qkv_moment: float32 [1024, 3072], P('seq', 'fsdp')
- out_copy: bfloat16 [1024, 1024], P(None, 'fsdp'), may hold values from -0.1875 to 0.1875
- out_master: float32 [1024, 1024], P('seq', 'fsdp'), may hold values from -0.1875 to 0.1875
- out_moment: float32 [1024, 1024], P('seq', 'fsdp')
- up_copy: bfloat16 [1024, 4096], P(None, 'fsdp'), may hold values from -0.1875 to 0.1875
- up_master: float32 [1024, 4096], P('seq', 'fsdp'), may hold values from -0.1875 to 0.1875
- up_moment: float32 [1024, 4096], P('seq', 'fsdp')
- down_copy: bfloat16 [1024, 4096], P(None, 'fsdp'), may hold values from -0.09375 to 0.09375
- down_master: float32 [1024, 4096], P('seq', 'fsdp'), may hold values from -0.09375 to 0.09375
- down_moment: float32 [1024, 4096], P('seq', 'fsdp')
- ada_copy: bfloat16 [1024, 6144], P(None, 'fsdp'), may hold values from -0.1875 to 0.1875
- ada_master: float32 [1024, 6144], P('seq', 'fsdp'), may hold values from -0.1875 to 0.1875
- ada_first: float32 [1024, 6144], P('seq', 'fsdp'), may hold values from -3.8146973e-06 to 3.8146973e-06
- ada_second: float32 [1024, 6144], P('seq', 'fsdp'), may hold values from 2.5853053e-13 to 1.0243662e-12
- io_proj: float32 [2, 276, 1024], P(None, None, 'fsdp'), may hold values from -0.375 to 0.375
- io_first: float32 [2, 276, 1024], P(None, None, 'fsdp'), may hold values from -3.8146973e-06 to 3.8146973e-06
- io_second: float32 [2, 276, 1024], P(None, None, 'fsdp'), may hold values from 2.5853053e-13 to 1.0243662e-12
- cond_table: float32 [5, 1024], P(None, 'fsdp'), may hold values from -6 to 6
- cond_first: float32 [5, 1024], P(None, 'fsdp'), may hold values from -3.8146973e-06 to 3.8146973e-06
- cond_second: float32 [5, 1024], P(None, 'fsdp'), may hold values from 2.5853053e-13 to 1.0243662e-12
- pos_table: float32 [1024, 1024], P('seq', 'fsdp'), may hold values from -6 to 6
- pos_first: float32 [1024, 1024], P('seq', 'fsdp'), may hold values from -1.1920929e-07 to 1.1920929e-07
- pos_second: float32 [1024, 1024], P('seq', 'fsdp'), may hold values from 2.5247122e-16 to 1.0003577e-15
- biases: float32 [7168], P('fsdp'), may hold values from -1.5 to 1.5
- bias_first: float32 [7168], P('fsdp'), may hold values from -3.8146973e-06 to 3.8146973e-06
- bias_second: float32 [7168], P('fsdp'), may hold values from 2.5853053e-13 to 1.0243662e-12
Outputs:
- loss_total: float32 [], replicated
- grad_norm: float32 [], replicated
- moment_sizes: float32 [4], replicated
- qkv_new: float32 [1024, 3072], P('seq', 'fsdp')
- qkv_moment_new: float32 [1024, 3072], P('seq', 'fsdp')
- qkv_copy_new: bfloat16 [1024, 3072], P(None, 'fsdp')
- out_new: float32 [1024, 1024], P('seq', 'fsdp')
- out_moment_new: float32 [1024, 1024], P('seq', 'fsdp')
- out_copy_new: bfloat16 [1024, 1024], P(None, 'fsdp')
- up_new: float32 [1024, 4096], P('seq', 'fsdp')
- up_moment_new: float32 [1024, 4096], P('seq', 'fsdp')
- up_copy_new: bfloat16 [1024, 4096], P(None, 'fsdp')
- down_new: float32 [1024, 4096], P('seq', 'fsdp')
- down_moment_new: float32 [1024, 4096], P('seq', 'fsdp')
- down_copy_new: bfloat16 [1024, 4096], P(None, 'fsdp')
- ada_new: float32 [1024, 6144], P('seq', 'fsdp')
- ada_first_new: float32 [1024, 6144], P('seq', 'fsdp')
- ada_second_new: float32 [1024, 6144], P('seq', 'fsdp')
- io_new: float32 [2, 276, 1024], P(None, None, 'fsdp')
- io_first_new: float32 [2, 276, 1024], P(None, None, 'fsdp')
- io_second_new: float32 [2, 276, 1024], P(None, None, 'fsdp')
- cond_new: float32 [5, 1024], P(None, 'fsdp')
- cond_first_new: float32 [5, 1024], P(None, 'fsdp')
- cond_second_new: float32 [5, 1024], P(None, 'fsdp')
- pos_new: float32 [1024, 1024], P('seq', 'fsdp')
- pos_first_new: float32 [1024, 1024], P('seq', 'fsdp')
- pos_second_new: float32 [1024, 1024], P('seq', 'fsdp')
- bias_new: float32 [7168], P('fsdp')
- bias_first_new: float32 [7168], P('fsdp')
- bias_second_new: float32 [7168], P('fsdp')
The draws below stay inside these ranges and needn't reach their ends.
Inputs may be any that keep to these rules, and one draw needn't show every extreme that they name: `lengths`: every value is reached by some sample, 1 and 2 in every draw.
All inputs are finite; a program needn't handle non-finite values.
Results may differ from the reference program's by a relative error of at most 0.03.
Values may be sent and summed in bfloat16 or wider, within the bound.
A program may use at most 448 MiB of HBM per device.

```python
import math
import jax
import jax.numpy as jnp
from jax import lax

D = 1024
HEADS = 16
HEAD = 64
FF = 4096
NI = 3
ROLL = 2
NS_ITERS = 5
STEP_NUM = 10
LON = 32
S_DEV = 1
PIN = 276
SEQ = 1024
SAMPLES = 4


def draw_lengths(key, part):
    key = jax.random.fold_in(key, 11)
    first_key, second_key = jax.random.split(key)
    drawn = jax.random.randint(first_key, (SAMPLES,), 1, ROLL + 1)
    picked = jax.random.permutation(second_key, SAMPLES)
    drawn = drawn.at[picked[0]].set(ROLL)
    drawn = drawn.at[picked[1]].set(1)
    return drawn.astype(jnp.int32)


def rising(key, rows, cols, top):
    base = 0.003 * (10 * D * D + 2 * D * FF + 2 * PIN * D + SEQ * D + (NI + ROLL) * D + 7 * D) ** (-0.5)
    noise = jnp.clip(jax.random.normal(key, (rows, cols), jnp.float32), -6.0, 6.0)
    row_factor = 1.0 + top * jnp.arange(rows, dtype=jnp.float32) / (rows - 1)
    col_factor = 1.0 + top * jnp.arange(cols, dtype=jnp.float32) / (cols - 1)
    return base * noise * row_factor[:, None] * col_factor[None]


def draw_qkv_moment(key, part):
    key = jax.random.fold_in(key, 21)
    top = 2.0
    return rising(key, D, 3 * D, top)


def draw_out_moment(key, part):
    key = jax.random.fold_in(key, 22)
    top = 2.0
    return rising(key, D, D, top)


def draw_up_moment(key, part):
    key = jax.random.fold_in(key, 23)
    top = 2.0
    return rising(key, D, FF, top)


def draw_down_moment(key, part):
    key = jax.random.fold_in(key, 24)
    top = 2.0
    return rising(key, D, FF, top)


def set_ends(entries, own_key, smallest, high):
    longest = entries.shape.index(max(entries.shape))
    spots = []
    for shift in (0, 1):
        where = [jax.random.randint(jax.random.fold_in(own_key, axis), (), 0, length) for axis, length in enumerate(entries.shape)]
        where[longest] = (where[longest] + shift) % entries.shape[longest]
        spots.append(tuple(where))
    return entries.at[spots[0]].set(smallest).at[spots[1]].set(high)


def shard_levels(own_key, dims, cuts, low, high):
    loudness = 1.0
    for axis_at, blocks in cuts:
        draws = jax.random.uniform(jax.random.fold_in(jax.random.fold_in(own_key, 6), axis_at), (blocks,), jnp.float32, low / len(cuts), high / len(cuts))
        loudness = loudness * jnp.repeat(jnp.exp(draws), dims[axis_at] // blocks).reshape((-1,) + (1,) * (len(dims) - 1 - axis_at))
    return loudness


def scatter_about(key, dims, deviation, bound, cuts=(), kind=jnp.bfloat16):
    loudness = shard_levels(key, dims, cuts, -0.22, 0.18) if cuts else 1.0
    result = jax.random.normal(key, dims, jnp.float32) * deviation * loudness
    return jnp.minimum(jnp.maximum(result, -bound), bound).astype(kind)


def setup_inputs(seed: int = 0) -> dict:
    streams_of = jax.random.split(jax.random.key(seed), 33)
    return {
        "states": scatter_about(streams_of[0], (SAMPLES, SEQ, PIN), 1.0, 6.0, ((0, 4), (1, 8))),
        "targets": scatter_about(streams_of[1], (SAMPLES, SEQ, PIN), 1.0, 6.0, ((0, 4), (1, 8))),
        "lengths": draw_lengths(jax.random.fold_in(streams_of[32], 71), 0),
        "intervals": set_ends(jax.random.randint(streams_of[3], (SAMPLES,), 0, NI), jax.random.fold_in(streams_of[3], 1), 0, NI - 1).astype(jnp.int32),
        "qkv_copy": scatter_about(streams_of[4], (D, 3 * D), D ** -0.5, 0.1875, ((1, 4),)),
        "qkv_master": scatter_about(streams_of[5], (D, 3 * D), D ** -0.5, 0.1875, ((0, 8), (1, 4)), jnp.float32),
        "qkv_moment": draw_qkv_moment(jax.random.fold_in(streams_of[32], 71), 0),
        "out_copy": scatter_about(streams_of[7], (D, D), D ** -0.5, 0.1875, ((1, 4),)),
        "out_master": scatter_about(streams_of[8], (D, D), D ** -0.5, 0.1875, ((0, 8), (1, 4)), jnp.float32),
        "out_moment": draw_out_moment(jax.random.fold_in(streams_of[32], 71), 0),
        "up_copy": scatter_about(streams_of[10], (D, FF), D ** -0.5, 0.1875, ((1, 4),)),
        "up_master": scatter_about(streams_of[11], (D, FF), D ** -0.5, 0.1875, ((0, 8), (1, 4)), jnp.float32),
        "up_moment": draw_up_moment(jax.random.fold_in(streams_of[32], 71), 0),
        "down_copy": scatter_about(streams_of[13], (D, FF), FF ** -0.5, 0.09375, ((1, 4),)),
        "down_master": scatter_about(streams_of[14], (D, FF), FF ** -0.5, 0.09375, ((0, 8), (1, 4)), jnp.float32),
        "down_moment": draw_down_moment(jax.random.fold_in(streams_of[32], 71), 0),
        "ada_copy": scatter_about(streams_of[16], (D, 6 * D), D ** -0.5, 0.1875, ((1, 4),)),
        "ada_master": scatter_about(streams_of[17], (D, 6 * D), D ** -0.5, 0.1875, ((0, 8), (1, 4)), jnp.float32),
        "ada_first": scatter_about(streams_of[18], (D, 6 * D), (0.0011 * (10*D*D + 2*D*FF + 2*PIN*D + SEQ*D + (NI+ROLL)*D + 7*D) ** -0.5), 3.814697265625e-06, ((0, 8), (1, 4)), jnp.float32),
        "ada_second": jnp.clip(jnp.exp(math.log(1.0243662472084192e-12) - 1.37681562 * jax.random.uniform(streams_of[19], (D, 6 * D), jnp.float32) ** shard_levels(streams_of[19], (D, 6 * D), ((0, 8), (1, 4)), -0.2, 0.2)), 2.5853052879921956e-13, 1.0243662472084192e-12),
        "io_proj": scatter_about(streams_of[20], (2, PIN, D), PIN ** -0.5, 0.375, ((2, 4),), jnp.float32),
        "io_first": scatter_about(streams_of[21], (2, PIN, D), (0.0011 * (10*D*D + 2*D*FF + 2*PIN*D + SEQ*D + (NI+ROLL)*D + 7*D) ** -0.5), 3.814697265625e-06, ((2, 4),), jnp.float32),
        "io_second": jnp.clip(jnp.exp(math.log(1.0243662472084192e-12) - 1.37681562 * jax.random.uniform(streams_of[22], (2, PIN, D), jnp.float32) ** shard_levels(streams_of[22], (2, PIN, D), ((2, 4),), -0.2, 0.2)), 2.5853052879921956e-13, 1.0243662472084192e-12),
        "cond_table": scatter_about(streams_of[23], (NI + ROLL, D), 1.0, 6.0, ((1, 4),), jnp.float32),
        "cond_first": scatter_about(streams_of[24], (NI + ROLL, D), (0.0011 * (10*D*D + 2*D*FF + 2*PIN*D + SEQ*D + (NI+ROLL)*D + 7*D) ** -0.5), 3.814697265625e-06, ((1, 4),), jnp.float32),
        "cond_second": jnp.clip(jnp.exp(math.log(1.0243662472084192e-12) - 1.37681562 * jax.random.uniform(streams_of[25], (NI + ROLL, D), jnp.float32) ** shard_levels(streams_of[25], (NI + ROLL, D), ((1, 4),), -0.2, 0.2)), 2.5853052879921956e-13, 1.0243662472084192e-12),
        "pos_table": scatter_about(streams_of[26], (SEQ, D), 0.5, 6.0, ((0, 8), (1, 4)), jnp.float32),
        "pos_first": scatter_about(streams_of[27], (SEQ, D), (0.0011 * (10*D*D + 2*D*FF + 2*PIN*D + SEQ*D + (NI+ROLL)*D + 7*D) ** -0.5 * SEQ ** -0.5), 1.1920928955078125e-07, ((0, 8), (1, 4)), jnp.float32),
        "pos_second": jnp.clip(jnp.exp(math.log(1.0003576632894719e-15) - 1.37681562 * jax.random.uniform(streams_of[28], (SEQ, D), jnp.float32) ** shard_levels(streams_of[28], (SEQ, D), ((0, 8), (1, 4)), -0.2, 0.2)), 2.5247121953048785e-16, 1.0003576632894719e-15),
        "biases": scatter_about(streams_of[29], (7 * D,), 0.1, 1.5, ((0, 4),), jnp.float32),
        "bias_first": scatter_about(streams_of[30], (7 * D,), (0.0011 * (10*D*D + 2*D*FF + 2*PIN*D + SEQ*D + (NI+ROLL)*D + 7*D) ** -0.5), 3.814697265625e-06, ((0, 4),), jnp.float32),
        "bias_second": jnp.clip(jnp.exp(math.log(1.0243662472084192e-12) - 1.37681562 * jax.random.uniform(streams_of[31], (7 * D,), jnp.float32) ** shard_levels(streams_of[31], (7 * D,), ((0, 4),), -0.2, 0.2)), 2.5853052879921956e-13, 1.0243662472084192e-12),
    }


@jax.custom_vjp
def low(v):
    return lax.optimization_barrier(v.astype(jnp.bfloat16)).astype(jnp.float32)

@jax.custom_vjp
def low_back(v):
    return v

def low_keep(v):
    return (low(v), None)

def low_pass(kept, grad):
    return (grad,)

def back_keep(v):
    return (v, None)

def back_low(kept, grad):
    return (low(grad),)
low.defvjp(low_keep, low_pass)
low_back.defvjp(back_keep, back_low)
HIGHEST_PRECISION = lax.Precision.HIGHEST
EPS_NORM = 1e-06
NS_A = 3.4445
NS_B = -4.775
NS_C = 2.0315
MOMENTUM = 0.5
RATE_MUON = 0.15
DECAY_MUON = 0.1
RATE_ADAM = 0.05
RATE_TABLE = 0.5
DECAY_ADAM = 0.1
BETA_FIRST = 0.9
BETA_SECOND = 0.95
CLIP_LIMIT = 0.01

def matmul_high(left, right):
    return jnp.matmul(left, right, precision=HIGHEST_PRECISION)

def layer_norm(values):
    centred = values - lax.optimization_barrier(jnp.mean(values, -1, keepdims=True))
    return centred * lax.rsqrt(lax.optimization_barrier(jnp.mean(centred * centred, -1, keepdims=True)) + EPS_NORM)

def lat_weights():
    band_row = (jnp.arange(SEQ, dtype=jnp.int32) // LON).astype(jnp.float32)
    latitude = (band_row + 0.5) * (math.pi / (SEQ // LON)) - math.pi / 2
    cosine = jnp.cos(latitude)
    return cosine / jnp.mean(cosine)

@jax.checkpoint
def attend(queries, keys, values):
    q_heads = queries.reshape(SEQ, HEADS, HEAD)
    k_heads = keys.reshape(SEQ, HEADS, HEAD)
    v_heads = values.reshape(SEQ, HEADS, HEAD)
    raw = jnp.einsum('qhd,khd->hqk', q_heads, k_heads, precision=HIGHEST_PRECISION)
    scores = low_back(raw) * HEAD ** (-0.5)
    expo = jnp.exp(scores - lax.optimization_barrier(jnp.max(scores, -1, keepdims=True)))
    probs = low(expo / lax.optimization_barrier(jnp.sum(expo, -1, keepdims=True)))
    mixed = jnp.einsum('hqk,khd->qhd', probs, v_heads, precision=HIGHEST_PRECISION)
    return low(low_back(mixed.reshape(SEQ, D)))

def block(params, state, cond_vec, active):
    w_qkv, w_out, w_up, w_down, w_ada, io_all, table, pos, bias = params
    silu_low = low(jax.nn.silu(cond_vec))
    modul = matmul_high(silu_low, w_ada) + bias[:6 * D]
    shift1, scale1, gate1, shift2, scale2, gate2 = [modul[:, None, column * D:(column + 1) * D] for column in range(6)]
    embedded = low_back(matmul_high(low(state), io_all[0])) + bias[6 * D:] + pos
    normed_a = low(layer_norm(embedded) * (1.0 + scale1) + shift1)
    qkv = low(low_back(matmul_high(normed_a, w_qkv)))
    mixed = jax.vmap(attend)(qkv[..., :D], qkv[..., D:2 * D], qkv[..., 2 * D:])
    after_attn = embedded + gate1 * low_back(matmul_high(mixed, w_out))
    normed_b = low(layer_norm(after_attn) * (1.0 + scale2) + shift2)
    hidden = low(jax.nn.gelu(low_back(matmul_high(normed_b, w_up))))
    after_mlp = after_attn + gate2 * low_back(matmul_high(hidden, w_down.T))
    delta = low_back(matmul_high(low(layer_norm(after_mlp)), io_all[1].T))
    return state + active[:, None, None] * delta

def group_loss(params, state, target, lens, ids, weight):
    table = low(params[6])
    params = params[:5] + (low(params[5]), table, low(params[7]), low(params[8]))
    rows_iota = jnp.arange(NI + ROLL, dtype=jnp.int32)
    select_ids = (ids[:, None] == rows_iota[None]).astype(jnp.float32)
    for step in range(ROLL):
        select = select_ids + (rows_iota == NI + step).astype(jnp.float32)[None]
        state = block(params, state, matmul_high(select, table), (step < lens).astype(jnp.float32))
    diff = state - target
    err = lax.optimization_barrier(jnp.sum(lax.optimization_barrier(jnp.sum(diff * diff, -1)) * lat_weights()[None], -1))
    return jnp.sum(weight * err)

def muon(master, moment, grad, clip):
    mom = MOMENTUM * moment + clip * grad
    size = jnp.sqrt(jnp.sum(mom * mom))
    iterate = low(mom / (size + 1e-07))
    for turn in range(NS_ITERS):
        gram = low(matmul_high(iterate, iterate.T))
        poly = low(NS_B * gram + NS_C * matmul_high(gram, gram))
        iterate = low(NS_A * iterate + matmul_high(poly, iterate))
    fresh = master * (1.0 - RATE_MUON * DECAY_MUON) - RATE_MUON * 0.2 * math.sqrt(master.shape[1]) * iterate
    return (fresh, mom, fresh.astype(jnp.bfloat16), size / CLIP_LIMIT)

def adam_update(weight, first, second, grad, rate):
    first_new = BETA_FIRST * first + (1.0 - BETA_FIRST) * grad
    second_new = BETA_SECOND * second + (1.0 - BETA_SECOND) * grad * grad
    unbiased = first_new / (1.0 - BETA_FIRST ** STEP_NUM)
    spread = jnp.sqrt(second_new / (1.0 - BETA_SECOND ** STEP_NUM)) + 1e-08
    return (weight * (1.0 - rate * DECAY_ADAM) - rate * unbiased / spread, first_new, second_new)

def reference(states, targets, lengths, intervals, qkv_copy, qkv_master, qkv_moment, out_copy, out_master, out_moment, up_copy, up_master, up_moment, down_copy, down_master, down_moment, ada_copy, ada_master, ada_first, ada_second, io_proj, io_first, io_second, cond_table, cond_first, cond_second, pos_table, pos_first, pos_second, biases, bias_first, bias_second):
    counts = lax.optimization_barrier(jnp.sum((intervals[:, None] == jnp.arange(NI, dtype=jnp.int32)[None]).astype(jnp.float32), 0))
    weight = 1.0 / (NI * SEQ * PIN * counts[intervals])
    params = tuple((item.astype(jnp.float32) for item in (qkv_copy, out_copy, up_copy, down_copy, ada_copy))) + (io_proj, cond_table, pos_table, biases)
    zeros = jax.tree.map(jnp.zeros_like, params)

    def scan_body(carry, index):

        def take(array):
            return lax.dynamic_slice_in_dim(array, index * S_DEV, S_DEV, 0)
        loss, pull = jax.vjp(lambda par: group_loss(par, take(states).astype(jnp.float32), take(targets).astype(jnp.float32), take(lengths), take(intervals), take(weight)), params)
        grads = pull(jnp.float32(1.0))[0]
        return ((carry[0] + loss, jax.tree.map(jnp.add, carry[1], grads)), None)
    (loss_total, grads), unused = lax.scan(scan_body, (jnp.float32(0.0), zeros), jnp.arange(SAMPLES // S_DEV, dtype=jnp.int32))
    squares = jnp.float32(0.0)
    for item in grads:
        squares = squares + jnp.sum(item * item)
    grad_norm = jnp.sqrt(squares)
    clip = jnp.minimum(1.0, CLIP_LIMIT / (grad_norm + 1e-06))
    qkv_res = muon(qkv_master, qkv_moment, grads[0], clip)
    out_res = muon(out_master, out_moment, grads[1], clip)
    up_res = muon(up_master, up_moment, grads[2], clip)
    down_res = muon(down_master, down_moment, grads[3], clip)
    moment_sizes = jnp.stack([qkv_res[3], out_res[3], up_res[3], down_res[3]])
    ada_res = adam_update(ada_master, ada_first, ada_second, clip * grads[4], RATE_ADAM)
    io_res = adam_update(io_proj, io_first, io_second, clip * grads[5], RATE_ADAM)
    cond_res = adam_update(cond_table, cond_first, cond_second, clip * grads[6], RATE_TABLE)
    pos_res = adam_update(pos_table, pos_first, pos_second, clip * grads[7], RATE_TABLE)
    bias_res = adam_update(biases, bias_first, bias_second, clip * grads[8], RATE_ADAM)
    return (loss_total, grad_norm, moment_sizes, qkv_res[0], qkv_res[1], qkv_res[2], out_res[0], out_res[1], out_res[2], up_res[0], up_res[1], up_res[2], down_res[0], down_res[1], down_res[2], ada_res[0], ada_res[1], ada_res[2], io_res[0], io_res[1], io_res[2], cond_res[0], cond_res[1], cond_res[2], pos_res[0], pos_res[1], pos_res[2], bias_res[0], bias_res[1], bias_res[2])
```

```python
import functools
import math

import jax
import jax.numpy as jnp
from jax import lax
from jax.experimental import pallas as pl
from jax.experimental.pallas import tpu as pltpu
from jax.sharding import PartitionSpec as P

HEADS = 16
HEAD = 64
NI = 3
ROLL = 2
NS_ITERS = 5
STEP_NUM = 10
LON = 32


EPS_NORM = 1e-06
NS_A = 3.4445
NS_B = -4.775
NS_C = 2.0315
MOMENTUM = 0.5
RATE_MUON = 0.15
DECAY_MUON = 0.1
RATE_ADAM = 0.05
RATE_TABLE = 0.5
DECAY_ADAM = 0.1
BETA_FIRST = 0.9
BETA_SECOND = 0.95
CLIP_LIMIT = 0.01
HIGHEST_PRECISION = lax.Precision.HIGHEST


def broadcast(block, axis, owner):
    block = jnp.where(lax.axis_index(axis) == owner, block, jnp.zeros_like(block))
    return lax.psum(block, axis)


def product(left, right):
    return jnp.dot(left, right, preferred_element_type=jnp.float32)


def dot_last(left, right):
    return lax.dot_general(
        left, right, (((left.ndim - 1,), (1,)), ((), ())), preferred_element_type=jnp.float32
    )


def rows_product(left, right):
    flat_left = left.reshape(-1, left.shape[-1])
    flat_right = right.reshape(-1, right.shape[-1])
    return lax.dot_general(
        flat_left, flat_right, (((0,), (0,)), ((), ())), preferred_element_type=jnp.float32
    )


def layer_norm(values):
    centred = values - jnp.mean(values, -1, keepdims=True)
    inverse = lax.rsqrt(jnp.mean(centred * centred, -1, keepdims=True) + EPS_NORM)
    return (centred * inverse, inverse)


def norm_back(grad, normed, inverse):
    return inverse * (
        grad
        - jnp.mean(grad, -1, keepdims=True)
        - normed * jnp.mean(grad * normed, -1, keepdims=True)
    )


def heads_view(values):
    return values.reshape(values.shape[0], values.shape[1], HEADS, HEAD)


def modulation(modul, width):
    return [modul[:, None, column * width : (column + 1) * width] for column in range(6)]


def latitude_weights(local):
    all_patches = local * lax.axis_size("seq")
    band_row = (jnp.arange(all_patches, dtype=jnp.int32) // LON).astype(jnp.float32)
    latitude = (band_row + 0.5) * (math.pi / (all_patches // LON)) - math.pi / 2
    cosine = jnp.cos(latitude)
    weights = cosine / jnp.mean(cosine)
    return lax.dynamic_slice_in_dim(weights, lax.axis_index("seq") * local, local)


def forward_step(weights, state, active, select):
    w_qkv, w_out, w_up, w_down, w_ada, io_all, table, pos, bias = weights
    width = w_out.shape[0]
    cond_vec = jnp.dot(select, table.astype(jnp.float32), precision=HIGHEST_PRECISION)
    silu_low = jax.nn.silu(cond_vec).astype(jnp.bfloat16)
    modul = product(silu_low, w_ada) + bias[: 6 * width].astype(jnp.float32)
    shift1, scale1, gate1, shift2, scale2, gate2 = modulation(modul, width)
    state_low = state.astype(jnp.bfloat16)
    embedded = (
        product(state_low, io_all[0])
        + bias[6 * width :].astype(jnp.float32)
        + pos.astype(jnp.float32)
    )
    normed_one, inverse_one = layer_norm(embedded)
    normed_a = (normed_one * (1.0 + scale1) + shift1).astype(jnp.bfloat16)
    qkv = product(normed_a, w_qkv).astype(jnp.bfloat16)
    queries = qkv[..., :width]
    keys, values = (
        lax.all_gather(qkv[..., width : 2 * width], "seq", axis=1, tiled=True),
        lax.all_gather(qkv[..., 2 * width :], "seq", axis=1, tiled=True),
    )
    scores = jnp.einsum(
        "sphd,snhd->shpn", heads_view(queries), heads_view(keys), preferred_element_type=jnp.float32
    ) * HEAD ** (-0.5)
    top_score = jnp.max(scores, -1, keepdims=True)
    expo = jnp.exp(scores - top_score)
    total_exp = jnp.sum(expo, -1, keepdims=True)
    log_total = top_score + jnp.log(total_exp)
    probs_low = (expo / total_exp).astype(jnp.bfloat16)
    mixed = jnp.einsum(
        "shpn,snhd->sphd", probs_low, heads_view(values), preferred_element_type=jnp.float32
    )
    mixed_low = mixed.reshape(queries.shape).astype(jnp.bfloat16)
    attended = product(mixed_low, w_out)
    after_attn = embedded + gate1 * attended
    normed_two, inverse_two = layer_norm(after_attn)
    normed_b = (normed_two * (1.0 + scale2) + shift2).astype(jnp.bfloat16)
    upward = product(normed_b, w_up)
    hidden = jax.nn.gelu(upward).astype(jnp.bfloat16)
    downward = dot_last(hidden, w_down)
    after_mlp = after_attn + gate2 * downward
    normed_three, inverse_three = layer_norm(after_mlp)
    normed_c = normed_three.astype(jnp.bfloat16)
    delta = dot_last(normed_c, io_all[1])
    kept = (
        cond_vec,
        silu_low,
        modul,
        state_low,
        normed_one,
        inverse_one,
        normed_a,
        queries,
        keys,
        values,
        log_total,
        mixed_low,
        attended,
        normed_two,
        inverse_two,
        normed_b,
        upward,
        hidden,
        downward,
        normed_three,
        inverse_three,
        normed_c,
    )
    return (state + active * delta, kept)


def backward_step(weights, kept, grad_state, active, select):
    w_qkv, w_out, w_up, w_down, w_ada, io_all, table, pos, bias = weights
    (
        cond_vec,
        silu_low,
        modul,
        state_low,
        normed_one,
        inverse_one,
        normed_a,
        queries,
        keys,
        values,
        log_total,
        mixed_low,
        attended,
        normed_two,
        inverse_two,
        normed_b,
        upward,
        hidden,
        downward,
        normed_three,
        inverse_three,
        normed_c,
    ) = kept
    width = w_out.shape[0]
    shift1, scale1, gate1, shift2, scale2, gate2 = modulation(modul, width)
    delta_grad = (active * grad_state).astype(jnp.bfloat16)
    grad_head = rows_product(delta_grad, normed_c)
    grad_mlp = norm_back(product(delta_grad, io_all[1]), normed_three, inverse_three)
    grad_gate2 = jnp.sum(grad_mlp * downward, 1)
    down_grad = (gate2 * grad_mlp).astype(jnp.bfloat16)
    grad_down = rows_product(down_grad, hidden)
    grad_hidden = product(down_grad, w_down)
    up_grad = jax.vjp(jax.nn.gelu, upward)[1](grad_hidden)[0].astype(jnp.bfloat16)
    grad_up = rows_product(normed_b, up_grad)
    grad_normed_b = dot_last(up_grad, w_up)
    grad_scale2 = jnp.sum(grad_normed_b * normed_two, 1)
    grad_shift2 = jnp.sum(grad_normed_b, 1)
    grad_attn = grad_mlp + norm_back(grad_normed_b * (1.0 + scale2), normed_two, inverse_two)
    grad_gate1 = jnp.sum(grad_attn * attended, 1)
    attn_grad = (gate1 * grad_attn).astype(jnp.bfloat16)
    grad_out = rows_product(mixed_low, attn_grad)
    mixed_grad = dot_last(attn_grad, w_out).astype(jnp.bfloat16)
    q_heads = heads_view(queries)
    k_heads = heads_view(keys)
    v_heads = heads_view(values)
    g_heads = heads_view(mixed_grad)
    scores = jnp.einsum(
        "sphd,snhd->shpn", q_heads, k_heads, preferred_element_type=jnp.float32
    ) * HEAD ** (-0.5)
    probs = jnp.exp(scores - log_total)
    probs_low = probs.astype(jnp.bfloat16)
    grad_probs = jnp.einsum("sphd,snhd->shpn", g_heads, v_heads, preferred_element_type=jnp.float32)
    score_grad = (
        HEAD ** (-0.5) * probs * (grad_probs - jnp.sum(grad_probs * probs, -1, keepdims=True))
    ).astype(jnp.bfloat16)
    grad_queries = jnp.einsum(
        "shpn,snhd->sphd", score_grad, k_heads, preferred_element_type=jnp.float32
    ).reshape(queries.shape)
    key_part = jnp.einsum(
        "shpn,sphd->snhd", score_grad, q_heads, preferred_element_type=jnp.float32
    ).reshape(keys.shape)
    value_part = jnp.einsum(
        "shpn,sphd->snhd", probs_low, g_heads, preferred_element_type=jnp.float32
    ).reshape(values.shape)
    grad_keys, grad_values = (
        lax.psum_scatter(key_part, "seq", scatter_dimension=1, tiled=True),
        lax.psum_scatter(value_part, "seq", scatter_dimension=1, tiled=True),
    )
    qkv_grad = jnp.concatenate([grad_queries, grad_keys, grad_values], -1).astype(jnp.bfloat16)
    grad_qkv = rows_product(normed_a, qkv_grad)
    grad_normed_a = dot_last(qkv_grad, w_qkv)
    grad_scale1 = jnp.sum(grad_normed_a * normed_one, 1)
    grad_shift1 = jnp.sum(grad_normed_a, 1)
    grad_embedded = grad_attn + norm_back(grad_normed_a * (1.0 + scale1), normed_one, inverse_one)
    embed_grad = grad_embedded.astype(jnp.bfloat16)
    grad_embed = rows_product(state_low, embed_grad)
    grad_prev = grad_state + dot_last(embed_grad, io_all[0])
    grad_modul = jnp.concatenate(
        [grad_shift1, grad_scale1, grad_gate1, grad_shift2, grad_scale2, grad_gate2], -1
    )
    grad_ada = lax.dot_general(
        silu_low.astype(jnp.float32),
        grad_modul,
        (((0,), (0,)), ((), ())),
        precision=HIGHEST_PRECISION,
    )
    grad_silu = lax.dot_general(
        grad_modul, w_ada.astype(jnp.float32), (((1,), (1,)), ((), ())), precision=HIGHEST_PRECISION
    )
    grad_cond = jax.vjp(jax.nn.silu, cond_vec)[1](grad_silu)[0]
    grad_table = lax.dot_general(
        select, grad_cond, (((0,), (0,)), ((), ())), precision=HIGHEST_PRECISION
    )
    grad_bias = jnp.concatenate([jnp.sum(grad_modul, 0), jnp.sum(grad_embedded, (0, 1))])
    grad_pos = jnp.sum(grad_embedded, 0)
    grads = (
        grad_qkv,
        grad_out,
        grad_up,
        grad_down,
        grad_ada,
        jnp.stack([grad_embed, grad_head]),
        grad_table,
        grad_pos,
        grad_bias,
    )
    return (grad_prev, grads)


def gram_part(block_cols):
    return lax.dot_general(
        block_cols, block_cols, (((1,), (1,)), ((), ())), preferred_element_type=jnp.float32
    )


def zero_gram(block_cols):
    return jnp.zeros((block_cols.shape[0], block_cols.shape[0]), jnp.float32)


def newton_step(block_cols, gram):
    gram_low = gram.astype(jnp.bfloat16)
    poly = (NS_B * gram_low.astype(jnp.float32) + NS_C * product(gram_low, gram_low)).astype(
        jnp.bfloat16
    )
    return (NS_A * block_cols.astype(jnp.float32) + product(poly, block_cols)).astype(jnp.bfloat16)


def keep_block(block_cols, gram):
    return block_cols


def adam_update(weight, first, second, grad, rate):
    first_new = BETA_FIRST * first + (1.0 - BETA_FIRST) * grad
    second_new = BETA_SECOND * second + (1.0 - BETA_SECOND) * grad * grad
    unbiased = first_new / (1.0 - BETA_FIRST**STEP_NUM)
    spread = jnp.sqrt(second_new / (1.0 - BETA_SECOND**STEP_NUM)) + 1e-08
    return (weight * (1.0 - rate * DECAY_ADAM) - rate * unbiased / spread, first_new, second_new)


def general_body(
    states,
    targets,
    lengths,
    intervals,
    qkv_copy,
    qkv_master,
    qkv_moment,
    out_copy,
    out_master,
    out_moment,
    up_copy,
    up_master,
    up_moment,
    down_copy,
    down_master,
    down_moment,
    ada_copy,
    ada_master,
    ada_first,
    ada_second,
    io_proj,
    io_first,
    io_second,
    cond_table,
    cond_first,
    cond_second,
    pos_table,
    pos_first,
    pos_second,
    biases,
    bias_first,
    bias_second,
):
    weights = (
        lax.all_gather(qkv_copy, "fsdp", axis=1, tiled=True),
        lax.all_gather(out_copy, "fsdp", axis=1, tiled=True),
        lax.all_gather(up_copy, "fsdp", axis=1, tiled=True),
        lax.all_gather(down_copy, "fsdp", axis=1, tiled=True),
        lax.all_gather(ada_copy, "fsdp", axis=1, tiled=True),
        lax.all_gather(io_proj.astype(jnp.bfloat16), "fsdp", axis=2, tiled=True),
        lax.all_gather(cond_table.astype(jnp.bfloat16), "fsdp", axis=1, tiled=True),
        lax.all_gather(pos_table.astype(jnp.bfloat16), "fsdp", axis=1, tiled=True),
        lax.all_gather(biases.astype(jnp.bfloat16), "fsdp", axis=0, tiled=True),
    )
    samples, local, values_count = states.shape
    table_rows = cond_table.shape[0]
    my_ids = lax.dynamic_slice_in_dim(intervals, lax.axis_index("fsdp") * samples, samples)
    counts = jnp.sum(
        (intervals[:, None] == jnp.arange(NI, dtype=jnp.int32)[None]).astype(jnp.float32), 0
    )
    id_counts = jnp.sum(
        (my_ids[:, None] == jnp.arange(NI, dtype=jnp.int32)[None]).astype(jnp.float32)
        * counts[None],
        1,
    )
    weight = 1.0 / (NI * local * lax.axis_size("seq") * values_count * id_counts)
    rows_iota = jnp.arange(table_rows, dtype=jnp.int32)
    id_select = (my_ids[:, None] == rows_iota[None]).astype(jnp.float32)
    state = states.astype(jnp.float32)
    seen_states = []
    kept_all = []
    for step in range(ROLL):
        select = id_select + (rows_iota == NI + step).astype(jnp.float32)[None]
        active = (step < lengths).astype(jnp.float32)[:, None, None]
        seen_states.append(state)
        state, kept = forward_step(weights, state, active, select)
        kept_all.append(kept)
    lat = latitude_weights(local)
    diff = state - targets.astype(jnp.float32)
    err = jnp.sum(jnp.sum(diff * diff, -1) * lat[None], -1)
    loss_local = jnp.sum(weight * err)
    grad_state = 2.0 * weight[:, None, None] * lat[None, :, None] * diff
    totals = None
    for step in reversed(range(ROLL)):
        select = id_select + (rows_iota == NI + step).astype(jnp.float32)[None]
        active = (step < lengths).astype(jnp.float32)[:, None, None]
        kept = kept_all[step]
        grad_state, grads = backward_step(weights, kept, grad_state, active, select)
        totals = grads if totals is None else jax.tree.map(jnp.add, totals, grads)
    reduced = (
        lax.psum_scatter(totals[0], "fsdp", scatter_dimension=1, tiled=True),
        lax.psum_scatter(totals[1], "fsdp", scatter_dimension=1, tiled=True),
        lax.psum_scatter(totals[2], "fsdp", scatter_dimension=1, tiled=True),
        lax.psum_scatter(totals[3], "fsdp", scatter_dimension=1, tiled=True),
        lax.psum_scatter(totals[4], "fsdp", scatter_dimension=1, tiled=True),
        lax.psum_scatter(totals[5], "fsdp", scatter_dimension=2, tiled=True),
        lax.psum_scatter(totals[6], "fsdp", scatter_dimension=1, tiled=True),
        lax.psum_scatter(totals[7], "fsdp", scatter_dimension=1, tiled=True),
        lax.psum_scatter(totals[8], "fsdp", scatter_dimension=0, tiled=True),
    )
    large = (
        lax.psum_scatter(reduced[0], "seq", scatter_dimension=0, tiled=True),
        lax.psum_scatter(reduced[1], "seq", scatter_dimension=0, tiled=True),
        lax.psum_scatter(reduced[2], "seq", scatter_dimension=0, tiled=True),
        lax.psum_scatter(reduced[3], "seq", scatter_dimension=0, tiled=True),
        lax.psum_scatter(reduced[4], "seq", scatter_dimension=0, tiled=True),
    )
    small = lax.psum((reduced[5], reduced[6], reduced[8]), "seq")
    grad_pos = reduced[7]
    first_copy = (lax.axis_index("seq") == 0).astype(jnp.float32)
    squares = jnp.sum(grad_pos * grad_pos)
    for item in large:
        squares = squares + jnp.sum(item * item)
    small_squares = jnp.float32(0.0)
    for item in small:
        small_squares = small_squares + jnp.sum(item * item)
    squares, loss_total = lax.psum(
        (squares + first_copy * small_squares, loss_local), ("seq", "fsdp")
    )
    grad_norm = jnp.sqrt(squares)
    clip = jnp.minimum(1.0, CLIP_LIMIT / (grad_norm + 1e-06))
    masters = (qkv_master, out_master, up_master, down_master)
    moments = [
        MOMENTUM * old + clip * grad
        for old, grad in zip((qkv_moment, out_moment, up_moment, down_moment), large[:4])
    ]
    norms = lax.psum(
        (
            jnp.sum(moments[0] * moments[0]),
            jnp.sum(moments[1] * moments[1]),
            jnp.sum(moments[2] * moments[2]),
            jnp.sum(moments[3] * moments[3]),
        ),
        ("seq", "fsdp"),
    )
    sizes = [jnp.sqrt(norms[which]) for which in range(4)]
    moment_sizes = jnp.stack(sizes) / CLIP_LIMIT
    scaled = [(moments[which] / (sizes[which] + 1e-07)).astype(jnp.bfloat16) for which in range(4)]
    columns = (
        lax.all_gather(scaled[0], "seq", axis=0, tiled=True),
        lax.all_gather(scaled[1], "seq", axis=0, tiled=True),
        lax.all_gather(scaled[2], "seq", axis=0, tiled=True),
        lax.all_gather(scaled[3], "seq", axis=0, tiled=True),
    )
    seq_index = lax.axis_index("seq")
    seq_count = lax.axis_size("seq")
    owners = [seq_index == which % seq_count for which in range(4)]
    blocks = list(columns)
    for turn in range(NS_ITERS):
        partial_value = [
            lax.cond(owners[which], gram_part, zero_gram, blocks[which]) for which in range(4)
        ]
        grams = lax.psum(
            (partial_value[0], partial_value[1], partial_value[2], partial_value[3]), "fsdp"
        )
        blocks = [
            lax.cond(owners[which], newton_step, keep_block, blocks[which], grams[which])
            for which in range(4)
        ]
    blocks = [broadcast(blocks[which], "seq", which % seq_count) for which in range(4)]
    row_count = qkv_master.shape[0]
    fresh = []
    for which in range(4):
        my_rows = lax.dynamic_slice_in_dim(
            blocks[which], seq_index * row_count, row_count, 0
        ).astype(jnp.float32)
        all_cols = masters[which].shape[1] * lax.axis_size("fsdp")
        fresh.append(
            masters[which] * (1.0 - RATE_MUON * DECAY_MUON)
            - RATE_MUON * 0.2 * math.sqrt(all_cols) * my_rows
        )
    copies = (
        lax.all_gather(fresh[0].astype(jnp.bfloat16), "seq", axis=0, tiled=True),
        lax.all_gather(fresh[1].astype(jnp.bfloat16), "seq", axis=0, tiled=True),
        lax.all_gather(fresh[2].astype(jnp.bfloat16), "seq", axis=0, tiled=True),
        lax.all_gather(fresh[3].astype(jnp.bfloat16), "seq", axis=0, tiled=True),
    )
    ada_res = adam_update(ada_master, ada_first, ada_second, clip * large[4], RATE_ADAM)
    io_res = adam_update(io_proj, io_first, io_second, clip * small[0], RATE_ADAM)
    cond_res = adam_update(cond_table, cond_first, cond_second, clip * small[1], RATE_TABLE)
    pos_res = adam_update(pos_table, pos_first, pos_second, clip * grad_pos, RATE_TABLE)
    bias_res = adam_update(biases, bias_first, bias_second, clip * small[2], RATE_ADAM)
    return (
        loss_total,
        grad_norm,
        moment_sizes,
        fresh[0],
        moments[0],
        copies[0],
        fresh[1],
        moments[1],
        copies[1],
        fresh[2],
        moments[2],
        copies[2],
        fresh[3],
        moments[3],
        copies[3],
        ada_res[0],
        ada_res[1],
        ada_res[2],
        io_res[0],
        io_res[1],
        io_res[2],
        cond_res[0],
        cond_res[1],
        cond_res[2],
        pos_res[0],
        pos_res[1],
        pos_res[2],
        bias_res[0],
        bias_res[1],
        bias_res[2],
    )


LANES = 128
MATRICES = 4
LOW = jnp.bfloat16
MESH = pl.DeviceIdType.MESH


def round_up(value, unit):
    return -(-value // unit) * unit


class Moves:
    def __init__(self, name, ids):
        self.name = name
        self.ids = ids
        self.operands = []
        self.outputs = []
        self.moves = []
        self.locals = []
        self.peers = {}

    def operand(self, array):
        self.operands.append(array)
        return (0, len(self.operands) - 1)

    def output(self, shape, dtype):
        self.outputs.append(jax.ShapeDtypeStruct(shape, dtype))
        return (1, len(self.outputs) - 1)

    def keep(self, source, source_at, target, target_at):
        self.locals.append((source, source_at, target, target_at))

    def move(self, peer_key, peer, source, source_at, target, target_at, after=()):
        self.peers.setdefault(peer_key, peer)
        self.moves.append((peer_key, source, source_at, target, target_at, after))
        return len(self.moves) - 1

    def kernel(self, *refs):
        ins = refs[: len(self.operands)]
        outs = refs[len(self.operands) : len(self.operands) + len(self.outputs)]
        local_sem, send_sem, recv_sem = refs[len(self.operands) + len(self.outputs) :]

        def view(which, index):
            ref = (ins, outs)[which[0]][which[1]]
            return ref.at[index()] if index is not None else ref

        devices = {key: peer() for key, peer in self.peers.items()}
        barrier = pltpu.get_barrier_semaphore()
        for device in devices.values():
            pl.semaphore_signal(barrier, inc=1, device_id=device, device_id_type=MESH)
        pl.semaphore_wait(barrier, len(devices))
        remote = []
        for number, (key, source, source_at, target, target_at, after) in enumerate(self.moves):
            remote.append(
                pltpu.make_async_remote_copy(
                    src_ref=view(source, source_at),
                    dst_ref=view(target, target_at),
                    send_sem=send_sem.at[number],
                    recv_sem=recv_sem.at[number],
                    device_id=devices[key],
                    device_id_type=MESH,
                )
            )
            if not after:
                remote[number].start()
        local = [
            pltpu.make_async_copy(view(source, source_at), view(target, target_at), local_sem.at[number])
            for number, (source, source_at, target, target_at) in enumerate(self.locals)
        ]
        for copy in local:
            copy.start()
        arrived = set()
        for number, entry in enumerate(self.moves):
            if entry[-1]:
                for earlier in entry[-1]:
                    if earlier not in arrived:
                        remote[earlier].wait_recv()
                        arrived.add(earlier)
                remote[number].start()
        for copy in local:
            copy.wait()
        for number, copy in enumerate(remote):
            if number not in arrived:
                copy.wait_recv()
            copy.wait_send()

    def run(self):
        in_any = pl.BlockSpec(memory_space=pl.ANY)
        return pl.pallas_call(
            self.kernel,
            out_shape=self.outputs,
            in_specs=[in_any] * len(self.operands),
            out_specs=[in_any] * len(self.outputs),
            scratch_shapes=[
                pltpu.SemaphoreType.DMA((max(1, len(self.locals)),)),
                pltpu.SemaphoreType.DMA((len(self.moves),)),
                pltpu.SemaphoreType.DMA((len(self.moves),)),
            ],
            compiler_params=pltpu.CompilerParams(
                collective_id=self.ids.setdefault(self.name, len(self.ids)), has_side_effects=True
            ),
            name=self.name,
        )(*self.operands)

    def along(self, axis, source, target, pairs):
        count = lax.axis_size(axis)

        def other(shift):
            return lax.rem(lax.axis_index(axis) + shift, count)

        for shift in range(1, count):
            for source_at, target_at in pairs:
                self.move(
                    (axis, shift),
                    lambda shift=shift: {axis: other(shift)},
                    source,
                    None if source_at is None else (lambda at=source_at, shift=shift: at(other(shift))),
                    target,
                    lambda at=target_at: at(lax.axis_index(axis)),
                )
        for source_at, target_at in pairs:
            self.keep(
                source,
                None if source_at is None else (lambda at=source_at: at(lax.axis_index(axis))),
                target,
                lambda at=target_at: at(lax.axis_index(axis)),
            )

    def gather(self, axis, array):
        target = self.output((lax.axis_size(axis),) + array.shape, array.dtype)
        self.along(axis, self.operand(array), target, [(None, lambda sender: (sender,))])

    def gather_columns(self, axis, array):
        width = array.shape[-1]
        target = self.output(array.shape[:-1] + (lax.axis_size(axis) * width,), array.dtype)
        lead = (slice(None),) * (array.ndim - 1)
        self.along(
            axis,
            self.operand(array),
            target,
            [(None, lambda sender: lead + (pl.ds(pl.multiple_of(sender * width, LANES), width),))],
        )

    def exchange(self, axis, array):
        target = self.output(array.shape, array.dtype)
        self.along(axis, self.operand(array), target, [(lambda receiver: (receiver,), lambda sender: (sender,))])

    def exchange_columns(self, axis, array):
        width = array.shape[-1] // lax.axis_size(axis)
        target = self.output((lax.axis_size(axis), array.shape[0], width), array.dtype)
        self.along(
            axis,
            self.operand(array),
            target,
            [
                (
                    lambda receiver: (slice(None), pl.ds(pl.multiple_of(receiver * width, LANES), width)),
                    lambda sender: (sender,),
                )
            ],
        )

    def rows_to_heads(self, axis, array, planes):
        count, rows = lax.axis_size(axis), array.shape[0]
        columns = array.shape[1] // planes
        width = columns // count
        target = self.output((planes, rows * count, width), array.dtype)
        self.along(
            axis,
            self.operand(array),
            target,
            [
                (
                    lambda receiver, plane=plane: (
                        slice(None),
                        pl.ds(pl.multiple_of(plane * columns + receiver * width, LANES), width),
                    ),
                    lambda sender, plane=plane: (plane, pl.ds(pl.multiple_of(sender * rows, rows), rows)),
                )
                for plane in range(planes)
            ],
        )

    def heads_to_rows(self, axis, array):
        count = lax.axis_size(axis)
        planes, all_rows, width = array.shape
        rows, columns = all_rows // count, width * count
        target = self.output((rows, planes * columns), array.dtype)
        self.along(
            axis,
            self.operand(array),
            target,
            [
                (
                    lambda receiver, plane=plane: (plane, pl.ds(pl.multiple_of(receiver * rows, rows), rows)),
                    lambda sender, plane=plane: (
                        slice(None),
                        pl.ds(pl.multiple_of(plane * columns + sender * width, LANES), width),
                    ),
                )
                for plane in range(planes)
            ],
        )


def total_kernel(x_ref, o_ref, near, far, near_send, near_recv, far_send, far_recv):
    near_count, far_count = near.shape[0], far.shape[0]
    near_me, far_me = lax.axis_index("fsdp"), lax.axis_index("seq")
    barrier = pltpu.get_barrier_semaphore()
    for shift in range(1, near_count):
        pl.semaphore_signal(
            barrier, inc=1, device_id={"fsdp": lax.rem(near_me + shift, near_count)}, device_id_type=MESH
        )
    for shift in range(1, far_count):
        pl.semaphore_signal(
            barrier, inc=1, device_id={"seq": lax.rem(far_me + shift, far_count)}, device_id_type=MESH
        )
    pl.semaphore_wait(barrier, near_count + far_count - 2)

    def spread(axis, me, count, buffer, send, recv):
        copies = []
        for shift in range(1, count):
            copy = pltpu.make_async_remote_copy(
                src_ref=buffer.at[me],
                dst_ref=buffer.at[me],
                send_sem=send.at[shift - 1],
                recv_sem=recv.at[shift - 1],
                device_id={axis: lax.rem(me + shift, count)},
                device_id_type=MESH,
            )
            copy.start()
            copies.append(copy)
        for copy in copies:
            copy.wait()
        return jnp.sum(buffer[...], 0)

    near[near_me] = x_ref[...]
    far[far_me] = spread("fsdp", near_me, near_count, near, near_send, near_recv)
    o_ref[...] = spread("seq", far_me, far_count, far, far_send, far_recv)


def total_of(ids, values):
    near_count, far_count = lax.axis_size("fsdp"), lax.axis_size("seq")
    in_vmem = pl.BlockSpec(memory_space=pltpu.VMEM)
    return pl.pallas_call(
        total_kernel,
        out_shape=jax.ShapeDtypeStruct(values.shape, values.dtype),
        in_specs=[in_vmem],
        out_specs=in_vmem,
        scratch_shapes=[
            pltpu.VMEM((near_count,) + values.shape, values.dtype),
            pltpu.VMEM((far_count,) + values.shape, values.dtype),
            pltpu.SemaphoreType.DMA((near_count - 1,)),
            pltpu.SemaphoreType.DMA((near_count - 1,)),
            pltpu.SemaphoreType.DMA((far_count - 1,)),
            pltpu.SemaphoreType.DMA((far_count - 1,)),
        ],
        compiler_params=pltpu.CompilerParams(
            collective_id=ids.setdefault("total", len(ids)), has_side_effects=True
        ),
        name="total",
    )(values)


def contract(left, right, left_dim, right_dim):
    return lax.dot_general(
        left, right, (((left_dim,), (right_dim,)), ((), ())), preferred_element_type=jnp.float32
    )


QUERY_BLOCK = 256


def attention_kernel(heads, qkv_ref, mixed_ref):
    rows = pl.ds(pl.multiple_of(pl.program_id(0) * QUERY_BLOCK, QUERY_BLOCK), QUERY_BLOCK)
    mixed = []
    for head in range(heads):
        lanes = pl.ds(head * HEAD, HEAD)
        queries, keys, values = qkv_ref[0, rows, lanes], qkv_ref[1, :, lanes], qkv_ref[2, :, lanes]
        scores = contract(queries, keys, 1, 1) * HEAD ** (-0.5)
        expo = jnp.exp(scores - jnp.max(scores, -1, keepdims=True))
        probs = (expo / jnp.sum(expo, -1, keepdims=True)).astype(LOW)
        mixed.append(contract(probs, values, 1, 0))
    mixed_ref[...] = jnp.concatenate(mixed, -1).astype(LOW)


def attention(qkv):
    _, patches, width = qkv.shape
    return pl.pallas_call(
        functools.partial(attention_kernel, width // HEAD),
        out_shape=jax.ShapeDtypeStruct((patches, width), LOW),
        grid=(patches // QUERY_BLOCK,),
        in_specs=[pl.BlockSpec(qkv.shape, lambda block: (0, 0, 0))],
        out_specs=pl.BlockSpec((QUERY_BLOCK, width), lambda block: (block, 0)),
        compiler_params=pltpu.CompilerParams(vmem_limit_bytes=48 * 2**20),
        name="attention",
    )(qkv)


def attention_back_kernel(heads, qkv_ref, grad_ref, out_ref, key_total, value_total):
    block = pl.program_id(0)
    rows = pl.ds(pl.multiple_of(block * QUERY_BLOCK, QUERY_BLOCK), QUERY_BLOCK)

    @pl.when(block == 0)
    def _():
        key_total[...] = jnp.zeros_like(key_total)
        value_total[...] = jnp.zeros_like(value_total)

    query_parts = []
    for head in range(heads):
        lanes = pl.ds(head * HEAD, HEAD)
        queries, keys, values = qkv_ref[0, rows, lanes], qkv_ref[1, :, lanes], qkv_ref[2, :, lanes]
        grads = grad_ref[rows, lanes]
        scores = contract(keys, queries, 1, 1) * HEAD ** (-0.5)
        expo = jnp.exp(scores - jnp.max(scores, 0, keepdims=True))
        probs = expo / jnp.sum(expo, 0, keepdims=True)
        grad_probs = contract(values, grads, 1, 1)
        shared = jnp.sum(grad_probs * probs, 0, keepdims=True)
        score_grad = (HEAD ** (-0.5) * probs * (grad_probs - shared)).astype(LOW)
        query_parts.append(contract(score_grad, keys, 0, 0))
        key_total[head] += contract(score_grad, queries, 1, 0)
        value_total[head] += contract(probs.astype(LOW), grads, 1, 0)
    out_ref[0, rows, :] = jnp.concatenate(query_parts, -1).astype(LOW)

    @pl.when(block == pl.num_programs(0) - 1)
    def _():
        out_ref[1] = jnp.concatenate([key_total[head] for head in range(heads)], -1).astype(LOW)
        out_ref[2] = jnp.concatenate([value_total[head] for head in range(heads)], -1).astype(LOW)


def attention_back(qkv, grads):
    _, patches, width = qkv.shape
    heads = width // HEAD
    return pl.pallas_call(
        functools.partial(attention_back_kernel, heads),
        out_shape=jax.ShapeDtypeStruct(qkv.shape, LOW),
        grid=(patches // QUERY_BLOCK,),
        in_specs=[
            pl.BlockSpec(qkv.shape, lambda block: (0, 0, 0)),
            pl.BlockSpec(grads.shape, lambda block: (0, 0)),
        ],
        out_specs=pl.BlockSpec(qkv.shape, lambda block: (0, 0, 0)),
        scratch_shapes=[
            pltpu.VMEM((heads, patches, HEAD), jnp.float32),
            pltpu.VMEM((heads, patches, HEAD), jnp.float32),
        ],
        compiler_params=pltpu.CompilerParams(vmem_limit_bytes=48 * 2**20),
        name="attention_back",
    )(qkv, grads)


def product_high(left, right):
    left_high, right_high = left.astype(LOW), right.astype(LOW)
    left_rest = (left - left_high.astype(jnp.float32)).astype(LOW)
    right_rest = (right - right_high.astype(jnp.float32)).astype(LOW)
    return product(left_high, right_high) + (product(left_high, right_rest) + product(left_rest, right_high))


def product_low(left, right):
    return product(left.astype(LOW), right.astype(LOW))


def newton_schulz(block, gram):
    for turn in range(NS_ITERS):
        times = product_high if 2 <= turn < NS_ITERS - 1 else product_low
        poly = NS_B * gram + NS_C * times(gram, gram)
        if turn < NS_ITERS - 1:
            once = times(poly, gram)
            gram = NS_A * NS_A * gram + 2.0 * NS_A * once + times(poly, once)
        block = (NS_A * block.astype(jnp.float32) + product(poly.astype(LOW), block)).astype(LOW)
    return block


def fast_body(
    states,
    targets,
    lengths,
    intervals,
    qkv_copy,
    qkv_master,
    qkv_moment,
    out_copy,
    out_master,
    out_moment,
    up_copy,
    up_master,
    up_moment,
    down_copy,
    down_master,
    down_moment,
    ada_copy,
    ada_master,
    ada_first,
    ada_second,
    io_proj,
    io_first,
    io_second,
    cond_table,
    cond_first,
    cond_second,
    pos_table,
    pos_first,
    pos_second,
    biases,
    bias_first,
    bias_second,
):
    ids = {}
    f32 = jnp.float32
    seq_count, shards = lax.axis_size("seq"), lax.axis_size("fsdp")
    seq_index, shard = lax.axis_index("seq"), lax.axis_index("fsdp")
    members = seq_count // MATRICES
    group, member = seq_index // members, lax.rem(seq_index, members)
    samples, local, values_count = states.shape
    table_rows, table_cols = cond_table.shape
    width = table_cols * shards
    ada_cols = ada_copy.shape[1]
    padded = round_up(values_count, LANES)

    moves = Moves("embeddings", ids)
    moves.gather("fsdp", jnp.pad(io_proj.astype(LOW), ((0, 0), (0, padded - values_count), (0, 0))))
    moves.gather("fsdp", cond_table)
    moves.gather("fsdp", pos_table.astype(LOW))
    moves.gather("fsdp", biases[None])
    io_parts, table_parts, pos_parts, bias_parts = moves.run()
    io_all = jnp.moveaxis(io_parts, 0, 2).reshape(2, padded, width)
    table = jnp.moveaxis(table_parts, 0, 1).reshape(table_rows, width).astype(LOW).astype(f32)
    pos = jnp.moveaxis(pos_parts, 0, 1).reshape(local, width).astype(f32)
    bias = bias_parts.reshape(-1).astype(LOW).astype(f32)
    w_qkv = lax.all_gather(qkv_copy, "fsdp", axis=1, tiled=True)
    w_out = lax.all_gather(out_copy, "fsdp", axis=1, tiled=True)

    rows_iota = jnp.arange(table_rows, dtype=jnp.int32)
    id_rows = (intervals[:, None] == rows_iota[None]).astype(f32)
    step_rows = (rows_iota[None] == NI + jnp.arange(ROLL, dtype=jnp.int32)[:, None]).astype(f32)
    select = (id_rows[:, None] + step_rows[None]).reshape(-1, table_rows)
    cond_vec = jnp.sum(select[:, :, None] * table[None], 1)
    silu_low = jax.nn.silu(cond_vec).astype(LOW)
    modul_shard = product(silu_low, ada_copy) + lax.dynamic_slice_in_dim(bias, shard * ada_cols, ada_cols)[None]
    moves = Moves("modulation", ids)
    moves.exchange("fsdp", modul_shard.reshape(shards, ROLL, ada_cols))
    modul = jnp.moveaxis(moves.run()[0], 0, 1).reshape(ROLL, 6 * width)

    momenta = (qkv_moment, out_moment, up_moment, down_moment)
    group_cols = [item.shape[1] // members for item in momenta]
    most_cols = max(group_cols)

    def widen(item):
        return jnp.pad(item, ((0, 0), (0, most_cols - item.shape[1])))

    moment_parts = jnp.stack(
        [
            widen(item[:, part * cols : (part + 1) * cols].astype(LOW))
            for item, cols in zip(momenta, group_cols)
            for part in range(members)
        ]
    )

    counts = jnp.sum((intervals[:, None] == jnp.arange(NI, dtype=jnp.int32)[None]).astype(f32), 0)
    my_id = lax.dynamic_slice_in_dim(intervals, shard, 1)
    id_count = jnp.sum((my_id == jnp.arange(NI, dtype=jnp.int32)).astype(f32) * counts)
    weight = 1.0 / (NI * local * seq_count * values_count * id_count)
    length = lengths[0]
    value_pad = ((0, 0), (0, padded - values_count))
    state = jnp.pad(states[0].astype(f32), value_pad)
    embed_bias = bias[6 * width :]
    kept = []
    moment_group = None
    for step in range(ROLL):
        shift1, scale1, gate1, shift2, scale2, gate2 = jnp.split(modul[step][None], 6, -1)
        state_low = state.astype(LOW)
        embedded = product(state_low, io_all[0]) + embed_bias + pos
        normed_one, inverse_one = layer_norm(embedded)
        normed_a = (normed_one * (1.0 + scale1) + shift1).astype(LOW)
        qkv_rows = product(normed_a, w_qkv).astype(LOW)
        moves = Moves("qkv_heads", ids)
        moves.rows_to_heads("seq", qkv_rows, 3)
        qkv = moves.run()[0]
        mixed_heads = attention(qkv)
        moves = Moves("mixed_rows", ids)
        moves.heads_to_rows("seq", mixed_heads[None])
        mixed = moves.run()[0]
        attended = product(mixed, w_out)
        after_attn = embedded + gate1 * attended
        normed_two, inverse_two = layer_norm(after_attn)
        normed_b = (normed_two * (1.0 + scale2) + shift2).astype(LOW)
        moves = Moves("tokens" if step else "tokens_momenta", ids)
        moves.gather("fsdp", normed_b)
        if step == 0:
            moves.exchange("seq", moment_parts)
            tokens_b, moment_group = moves.run()
        else:
            tokens_b = moves.run()[0]
        tokens_b = tokens_b.reshape(shards * local, width)
        upward = product(tokens_b, up_copy)
        hidden = jax.nn.gelu(upward).astype(LOW)
        down_part = contract(hidden, down_copy, 1, 1).astype(LOW).reshape(shards, local, width)
        moves = Moves("token_sums", ids)
        moves.exchange("fsdp", down_part)
        downward = jnp.sum(moves.run()[0].astype(f32), 0)
        after_mlp = after_attn + gate2 * downward
        normed_three, inverse_three = layer_norm(after_mlp)
        normed_c = normed_three.astype(LOW)
        delta = contract(normed_c, io_all[1], 1, 1)
        kept.append(
            (
                state_low,
                normed_one,
                inverse_one,
                normed_a,
                qkv,
                mixed,
                attended,
                normed_two,
                inverse_two,
                tokens_b,
                upward,
                hidden,
                downward,
                normed_three,
                inverse_three,
                normed_c,
            )
        )
        state = state + (step < length).astype(f32) * delta

    lat = latitude_weights(local)
    diff = state - jnp.pad(targets[0].astype(f32), value_pad)
    loss_local = weight * jnp.sum(jnp.sum(diff * diff, -1) * lat)
    grad_state = 2.0 * weight * lat[:, None] * diff

    back = [None] * ROLL
    for step in reversed(range(ROLL)):
        (
            state_low,
            normed_one,
            inverse_one,
            normed_a,
            qkv,
            mixed,
            attended,
            normed_two,
            inverse_two,
            tokens_b,
            upward,
            hidden,
            downward,
            normed_three,
            inverse_three,
            normed_c,
        ) = kept[step]
        shift1, scale1, gate1, shift2, scale2, gate2 = jnp.split(modul[step][None], 6, -1)
        delta_grad = ((step < length).astype(f32) * grad_state).astype(LOW)
        grad_mlp = norm_back(product(delta_grad, io_all[1]), normed_three, inverse_three)
        grad_gate2 = jnp.sum(grad_mlp * downward, 0)
        moves = Moves("tokens", ids)
        moves.gather("fsdp", (gate2 * grad_mlp).astype(LOW))
        tokens_down = moves.run()[0].reshape(shards * local, width)
        grad_hidden = product(tokens_down, down_copy)
        up_grad = jax.vjp(jax.nn.gelu, upward)[1](grad_hidden)[0].astype(LOW)
        up_part = contract(up_grad, up_copy, 1, 1).astype(LOW).reshape(shards, local, width)
        moves = Moves("token_sums", ids)
        moves.exchange("fsdp", up_part)
        grad_normed_b = jnp.sum(moves.run()[0].astype(f32), 0)
        grad_scale2 = jnp.sum(grad_normed_b * normed_two, 0)
        grad_shift2 = jnp.sum(grad_normed_b, 0)
        grad_attn = grad_mlp + norm_back(grad_normed_b * (1.0 + scale2), normed_two, inverse_two)
        grad_gate1 = jnp.sum(grad_attn * attended, 0)
        attn_grad = (gate1 * grad_attn).astype(LOW)
        mixed_grad = contract(attn_grad, w_out, 1, 1).astype(LOW)
        moves = Moves("mixed_heads", ids)
        moves.rows_to_heads("seq", mixed_grad, 1)
        qkv_grad_heads = attention_back(qkv, moves.run()[0][0])
        moves = Moves("qkv_rows", ids)
        moves.heads_to_rows("seq", qkv_grad_heads)
        qkv_grad = moves.run()[0]
        grad_normed_a = contract(qkv_grad, w_qkv, 1, 1)
        grad_scale1 = jnp.sum(grad_normed_a * normed_one, 0)
        grad_shift1 = jnp.sum(grad_normed_a, 0)
        grad_embedded = grad_attn + norm_back(grad_normed_a * (1.0 + scale1), normed_one, inverse_one)
        embed_grad = grad_embedded.astype(LOW)
        grad_state = grad_state + contract(embed_grad, io_all[0], 1, 1)
        grad_modul = jnp.concatenate([grad_shift1, grad_scale1, grad_gate1, grad_shift2, grad_scale2, grad_gate2])
        back[step] = (
            normed_a,
            mixed,
            state_low,
            delta_grad,
            qkv_grad,
            attn_grad,
            embed_grad,
            normed_c,
            grad_modul,
            jnp.sum(grad_embedded, 0),
            tokens_b,
            up_grad,
            tokens_down,
            hidden,
        )

    (
        all_a,
        all_mixed,
        all_state,
        all_delta,
        all_qkv,
        all_attn,
        all_embed,
        all_c,
        grad_modul,
        grad_bias_embed,
        all_b,
        all_up,
        all_down,
        all_hidden,
    ) = [jnp.concatenate([item if item.ndim == 2 else item[None] for item in items], 0) for items in zip(*back)]
    modul_parts = jnp.moveaxis(grad_modul.reshape(ROLL, shards, ada_cols), 1, 0)
    embed_parts = jnp.sum(grad_bias_embed, 0).reshape(shards, 1, -1)
    vectors = jnp.concatenate(
        [modul_parts, jnp.pad(embed_parts, ((0, 0), (0, 0), (0, ada_cols - embed_parts.shape[-1])))], 1
    )
    moves = Moves("samples", ids)
    for array in (all_a, all_mixed, all_state, all_delta):
        moves.gather("fsdp", array)
    for array in (all_qkv, all_attn, all_embed, all_c):
        moves.exchange_columns("fsdp", array)
    moves.exchange("fsdp", vectors)
    all_a, all_mixed, all_state, all_delta, all_qkv, all_attn, all_embed, all_c, vectors = moves.run()
    grad_pos = jnp.sum(all_embed.reshape(shards * ROLL, local, -1).astype(f32), 0)
    grads_here = (
        rows_product(all_a, all_qkv),
        rows_product(all_mixed, all_attn),
        rows_product(all_b, all_up),
        rows_product(all_down, all_hidden),
    )
    io_here = jnp.stack([rows_product(all_state, all_embed), rows_product(all_delta, all_c)])
    io_cols = io_here.shape[-1]

    def member_peer(shift):
        seq_me = lax.axis_index("seq")
        return {"seq": seq_me // members * members + lax.rem(lax.rem(seq_me, members) + shift, members)}

    moves = Moves("member_sums", ids)
    halves = []
    for item, cols in zip(grads_here, group_cols):
        source = moves.operand(item.astype(LOW))
        target = moves.output((members - 1, item.shape[0], cols), LOW)
        for shift in range(1, members):
            moves.move(
                ("member", shift),
                functools.partial(member_peer, shift),
                source,
                lambda shift=shift, cols=cols: (
                    slice(None),
                    pl.ds(
                        pl.multiple_of(
                            lax.rem(lax.rem(lax.axis_index("seq"), members) + shift, members) * cols, LANES
                        ),
                        cols,
                    ),
                ),
                target,
                lambda shift=shift: (shift - 1,),
            )
    moves.gather("seq", vectors.reshape(-1, ada_cols))
    moves.exchange("seq", io_here.reshape(seq_count, -1, io_cols).astype(LOW))
    *halves, vectors, io_parts = moves.run()
    vectors = jnp.sum(vectors, 0).reshape(shards, ROLL + 1, ada_cols)
    io_slice = jnp.sum(io_parts.astype(f32), 0)
    member_sums = [
        lax.dynamic_slice_in_dim(item, member * cols, cols, 1) + jnp.sum(half.astype(f32), 0)
        for item, half, cols in zip(grads_here, halves, group_cols)
    ]
    modul_all = vectors[:, :ROLL].reshape(-1, ada_cols)
    bias_part = jnp.concatenate([jnp.sum(modul_all, 0), jnp.sum(vectors[:, ROLL, : width // shards], 0)])
    silu_part = lax.dot_general(
        modul_all, ada_copy.astype(f32), (((1,), (1,)), ((), ())), precision=HIGHEST_PRECISION
    )

    moves = Moves("group_sums", ids)
    source = moves.operand(jnp.stack([widen(item.astype(LOW)) for item in member_sums]))
    target = moves.output((MATRICES,) + (member_sums[0].shape[0], most_cols), LOW)
    for shift in range(1, MATRICES):
        moves.move(
            ("group", shift),
            lambda shift=shift: {"seq": lax.rem(lax.axis_index("seq") + shift * members, seq_count)},
            source,
            lambda shift=shift: (lax.rem(lax.axis_index("seq") // members + shift, MATRICES),),
            target,
            lambda: (lax.axis_index("seq") // members,),
        )
    moves.keep(source, lambda: (lax.axis_index("seq") // members,), target, lambda: (lax.axis_index("seq") // members,))
    moves.gather("fsdp", silu_part)
    moves.gather("fsdp", bias_part[None])
    grad_parts, silu_parts, bias_parts = moves.run()
    grad_group = jnp.sum(grad_parts.astype(f32), 0)
    grad_silu = jnp.sum(silu_parts, 0)
    grad_cond = jax.vjp(jax.nn.silu, cond_vec)[1](grad_silu)[0]
    grad_table_all = lax.dot_general(select, grad_cond, (((0,), (0,)), ((), ())), precision=HIGHEST_PRECISION)
    grad_table = lax.dynamic_slice_in_dim(grad_table_all, shard * table_cols, table_cols, 1)
    bias_parts = bias_parts[:, 0]
    grad_bias_all = jnp.concatenate([bias_parts[:, :ada_cols].reshape(-1), bias_parts[:, ada_cols:].reshape(-1)])
    grad_bias = lax.dynamic_slice_in_dim(grad_bias_all, shard * biases.shape[0], biases.shape[0])
    silu_rows = lax.dynamic_slice_in_dim(silu_low, seq_index * ada_master.shape[0], ada_master.shape[0], 1)
    grad_ada = lax.dot_general(
        silu_rows.astype(f32), modul_all, (((0,), (0,)), ((), ())), precision=HIGHEST_PRECISION
    )

    moment_group = moment_group.reshape(-1, most_cols).astype(f32)
    grad_squares = jnp.sum(grad_group * grad_group)
    squares = (
        grad_squares
        + jnp.sum(grad_ada * grad_ada)
        + jnp.sum(io_slice * io_slice)
        + jnp.sum(grad_pos * grad_pos)
        + (seq_index == 0).astype(f32) * (jnp.sum(grad_table * grad_table) + jnp.sum(grad_bias * grad_bias))
    )
    lane = jnp.arange(LANES, dtype=jnp.int32)
    place = 2 + 3 * group
    entries = jnp.where(lane == 0, squares, 0.0) + jnp.where(lane == 1, loss_local, 0.0)
    entries = entries + jnp.where(lane == place, jnp.sum(moment_group * moment_group), 0.0)
    entries = entries + jnp.where(lane == place + 1, jnp.sum(moment_group * grad_group), 0.0)
    entries = entries + jnp.where(lane == place + 2, grad_squares, 0.0)
    sums = total_of(ids, jnp.broadcast_to(entries[None], (8, LANES)))[0]
    grad_norm = jnp.sqrt(sums[0])
    loss_total = sums[1]
    clip = jnp.minimum(1.0, CLIP_LIMIT / (grad_norm + 1e-06))
    terms = sums[2 : 2 + 3 * MATRICES].reshape(MATRICES, 3)
    size_squares = MOMENTUM * MOMENTUM * terms[:, 0] + 2.0 * MOMENTUM * clip * terms[:, 1] + clip * clip * terms[:, 2]
    sizes = jnp.sqrt(jnp.maximum(size_squares, 0.0))
    moment_sizes = sizes / CLIP_LIMIT
    my_size = lax.dynamic_slice_in_dim(sizes, group, 1)[0]
    block = ((MOMENTUM * moment_group + clip * grad_group) / (my_size + 1e-07)).astype(LOW)

    moves = Moves("columns", ids)
    source = moves.operand(block)
    block_rows = block.shape[0]
    peers = members * shards
    target = moves.output((block_rows, peers * most_cols), LOW)

    def slot(back_member, back_pair):
        who_member = lax.rem(lax.rem(lax.axis_index("seq"), members) + members - back_member, members)
        who_shard = lax.rem(lax.axis_index("fsdp") + shards - 2 * back_pair, shards)
        start = (who_member * shards + who_shard) * most_cols
        return (slice(None), pl.ds(pl.multiple_of(start, LANES), most_cols))

    def sibling():
        index = lax.axis_index("fsdp")
        return {"fsdp": index + 1 - 2 * lax.rem(index, 2)}

    moves.move(("sibling",), sibling, source, None, target, lambda: slot(0, 0))
    moves.keep(source, None, target, lambda: slot(0, 0))
    for far_member in range(members):
        for far_pair in range(shards // 2):
            if far_member or far_pair:

                def peer(far_member=far_member, far_pair=far_pair):
                    seq_me = lax.axis_index("seq")
                    return {
                        "seq": seq_me // members * members + lax.rem(lax.rem(seq_me, members) + far_member, members),
                        "fsdp": lax.rem(lax.axis_index("fsdp") + 2 * far_pair, shards),
                    }

                number = moves.move(("plane", far_member, far_pair), peer, source, None, target, lambda: slot(0, 0))
                arrived = functools.partial(slot, far_member, far_pair)
                moves.move(("sibling",), sibling, target, arrived, target, arrived, (number,))
    moves.exchange("seq", grad_group.astype(LOW).reshape(seq_count, -1, most_cols))
    moves.gather("seq", io_slice)
    columns, grad_rows, io_slices = moves.run()

    def row_blocks(parts):
        return [
            jnp.concatenate(
                [parts[which * members + part][:, : group_cols[which]] for part in range(members)], -1
            ).astype(f32)
            for which in range(MATRICES)
        ]

    moments = [MOMENTUM * old + clip * grad for old, grad in zip(momenta, row_blocks(grad_rows))]
    block = newton_schulz(block, contract(columns, columns, 1, 1))
    moves = Moves("update_rows", ids)
    moves.exchange("seq", block.reshape(seq_count, -1, most_cols))
    masters = (qkv_master, out_master, up_master, down_master)
    fresh = [
        master * (1.0 - RATE_MUON * DECAY_MUON) - RATE_MUON * 0.2 * math.sqrt(master.shape[1] * shards) * rows
        for master, rows in zip(masters, row_blocks(moves.run()[0]))
    ]

    moves = Moves("copies", ids)
    rows = qkv_master.shape[0]

    def row_place(back_group, back_member):
        seq_me = lax.axis_index("seq")
        who = lax.rem(seq_me // members + MATRICES - back_group, MATRICES) * members
        who = who + lax.rem(lax.rem(seq_me, members) + members - back_member, members)
        return (pl.ds(pl.multiple_of(who * rows, rows), rows),)

    places = []
    for item in fresh:
        source = moves.operand(item.astype(LOW))
        target = moves.output((rows * seq_count, item.shape[1]), LOW)
        moves.keep(source, None, target, lambda: row_place(0, 0))
        places.append((source, target, []))
    for shift in range(1, MATRICES):
        for source, target, numbers in places:
            numbers.append(
                moves.move(
                    ("group", shift),
                    lambda shift=shift: {"seq": lax.rem(lax.axis_index("seq") + shift * members, seq_count)},
                    source,
                    None,
                    target,
                    lambda: row_place(0, 0),
                )
            )
    for shift in range(1, members):
        for source, target, numbers in places:
            moves.move(
                ("member", shift),
                functools.partial(member_peer, shift),
                source,
                None,
                target,
                lambda: row_place(0, 0),
            )
    for far in range(1, MATRICES):
        for source, target, numbers in places:
            for shift in range(1, members):
                place = functools.partial(row_place, far, 0)
                moves.move(
                    ("member", shift),
                    functools.partial(member_peer, shift),
                    target,
                    place,
                    target,
                    place,
                    (numbers[far - 1],),
                )
    copies = moves.run()

    io_grad = io_slices.reshape(2, padded, io_cols)[:, :values_count]
    ada_res = adam_update(ada_master, ada_first, ada_second, clip * grad_ada, RATE_ADAM)
    io_res = adam_update(io_proj, io_first, io_second, clip * io_grad, RATE_ADAM)
    cond_res = adam_update(cond_table, cond_first, cond_second, clip * grad_table, RATE_TABLE)
    pos_res = adam_update(pos_table, pos_first, pos_second, clip * grad_pos, RATE_TABLE)
    bias_res = adam_update(biases, bias_first, bias_second, clip * grad_bias, RATE_ADAM)
    matrices = []
    for which in range(MATRICES):
        matrices += [fresh[which], moments[which], copies[which]]
    return (loss_total, grad_norm, moment_sizes, *matrices, *ada_res, *io_res, *cond_res, *pos_res, *bias_res)


def fits_fast(mesh):
    seq, shards = mesh.shape["seq"], mesh.shape["fsdp"]
    return HEADS % seq == 0 and (HEADS // seq * HEAD) % LANES == 0 and seq % MATRICES == 0 and shards % 2 == 0


def solution(mesh):
    body = fast_body if fits_fast(mesh) else general_body
    return jax.shard_map(
        body,
        mesh=mesh,
        in_specs=(
            P("fsdp", "seq", None),
            P("fsdp", "seq", None),
            P("fsdp"),
            P(),
            P(None, "fsdp"),
            P("seq", "fsdp"),
            P("seq", "fsdp"),
            P(None, "fsdp"),
            P("seq", "fsdp"),
            P("seq", "fsdp"),
            P(None, "fsdp"),
            P("seq", "fsdp"),
            P("seq", "fsdp"),
            P(None, "fsdp"),
            P("seq", "fsdp"),
            P("seq", "fsdp"),
            P(None, "fsdp"),
            P("seq", "fsdp"),
            P("seq", "fsdp"),
            P("seq", "fsdp"),
            P(None, None, "fsdp"),
            P(None, None, "fsdp"),
            P(None, None, "fsdp"),
            P(None, "fsdp"),
            P(None, "fsdp"),
            P(None, "fsdp"),
            P("seq", "fsdp"),
            P("seq", "fsdp"),
            P("seq", "fsdp"),
            P("fsdp"),
            P("fsdp"),
            P("fsdp"),
        ),
        out_specs=(
            P(),
            P(),
            P(),
            P("seq", "fsdp"),
            P("seq", "fsdp"),
            P(None, "fsdp"),
            P("seq", "fsdp"),
            P("seq", "fsdp"),
            P(None, "fsdp"),
            P("seq", "fsdp"),
            P("seq", "fsdp"),
            P(None, "fsdp"),
            P("seq", "fsdp"),
            P("seq", "fsdp"),
            P(None, "fsdp"),
            P("seq", "fsdp"),
            P("seq", "fsdp"),
            P("seq", "fsdp"),
            P(None, None, "fsdp"),
            P(None, None, "fsdp"),
            P(None, None, "fsdp"),
            P(None, "fsdp"),
            P(None, "fsdp"),
            P(None, "fsdp"),
            P("seq", "fsdp"),
            P("seq", "fsdp"),
            P("seq", "fsdp"),
            P("fsdp"),
            P("fsdp"),
            P("fsdp"),
        ),
        check_vma=False,
    )
```

```python
import functools
import math

import jax
import jax.numpy as jnp
from jax import lax
from jax.experimental import pallas as pl
from jax.experimental.pallas import tpu as pltpu
from jax.sharding import PartitionSpec as P

PATCHES = "seq"
SHARDS = "fsdp"
HEADS = 16
HEAD = 64
NI = 3
ROLL = 2
NS_ITERS = 5
STEP_NUM = 10
LON = 32


EPS_NORM = 1e-06
NS_A = 3.4445
NS_B = -4.775
NS_C = 2.0315
MOMENTUM = 0.5
RATE_MUON = 0.15
DECAY_MUON = 0.1
RATE_ADAM = 0.05
RATE_TABLE = 0.5
DECAY_ADAM = 0.1
BETA_FIRST = 0.9
BETA_SECOND = 0.95
CLIP_LIMIT = 0.01
HIGHEST_PRECISION = lax.Precision.HIGHEST


def broadcast(block, axis, owner):
    block = jnp.where(lax.axis_index(axis) == owner, block, jnp.zeros_like(block))
    return lax.psum(block, axis)


def product(left, right):
    return jnp.dot(left, right, preferred_element_type=jnp.float32)


def dot_last(left, right):
    return lax.dot_general(
        left, right, (((left.ndim - 1,), (1,)), ((), ())), preferred_element_type=jnp.float32
    )


def rows_product(left, right):
    flat_left = left.reshape(-1, left.shape[-1])
    flat_right = right.reshape(-1, right.shape[-1])
    return lax.dot_general(
        flat_left, flat_right, (((0,), (0,)), ((), ())), preferred_element_type=jnp.float32
    )


def layer_norm(values):
    centred = values - jnp.mean(values, -1, keepdims=True)
    inverse = lax.rsqrt(jnp.mean(centred * centred, -1, keepdims=True) + EPS_NORM)
    return (centred * inverse, inverse)


def norm_back(grad, normed, inverse):
    return inverse * (
        grad
        - jnp.mean(grad, -1, keepdims=True)
        - normed * jnp.mean(grad * normed, -1, keepdims=True)
    )


def heads_view(values):
    return values.reshape(values.shape[0], values.shape[1], HEADS, HEAD)


def modulation(modul, width):
    return [modul[:, None, column * width : (column + 1) * width] for column in range(6)]


def latitude_weights(local):
    all_patches = local * lax.axis_size(PATCHES)
    band_row = (jnp.arange(all_patches, dtype=jnp.int32) // LON).astype(jnp.float32)
    latitude = (band_row + 0.5) * (math.pi / (all_patches // LON)) - math.pi / 2
    cosine = jnp.cos(latitude)
    weights = cosine / jnp.mean(cosine)
    return lax.dynamic_slice_in_dim(weights, lax.axis_index(PATCHES) * local, local)


def forward_step(weights, state, active, select):
    w_qkv, w_out, w_up, w_down, w_ada, io_all, table, pos, bias = weights
    width = w_out.shape[0]
    cond_vec = jnp.dot(select, table.astype(jnp.float32), precision=HIGHEST_PRECISION)
    silu_low = jax.nn.silu(cond_vec).astype(jnp.bfloat16)
    modul = product(silu_low, w_ada) + bias[: 6 * width].astype(jnp.float32)
    shift1, scale1, gate1, shift2, scale2, gate2 = modulation(modul, width)
    state_low = state.astype(jnp.bfloat16)
    embedded = (
        product(state_low, io_all[0])
        + bias[6 * width :].astype(jnp.float32)
        + pos.astype(jnp.float32)
    )
    normed_one, inverse_one = layer_norm(embedded)
    normed_a = (normed_one * (1.0 + scale1) + shift1).astype(jnp.bfloat16)
    qkv = product(normed_a, w_qkv).astype(jnp.bfloat16)
    queries = qkv[..., :width]
    keys, values = (
        lax.all_gather(qkv[..., width : 2 * width], PATCHES, axis=1, tiled=True),
        lax.all_gather(qkv[..., 2 * width :], PATCHES, axis=1, tiled=True),
    )
    scores = jnp.einsum(
        "sphd,snhd->shpn", heads_view(queries), heads_view(keys), preferred_element_type=jnp.float32
    ) * HEAD ** (-0.5)
    top_score = jnp.max(scores, -1, keepdims=True)
    expo = jnp.exp(scores - top_score)
    total_exp = jnp.sum(expo, -1, keepdims=True)
    log_total = top_score + jnp.log(total_exp)
    probs_low = (expo / total_exp).astype(jnp.bfloat16)
    mixed = jnp.einsum(
        "shpn,snhd->sphd", probs_low, heads_view(values), preferred_element_type=jnp.float32
    )
    mixed_low = mixed.reshape(queries.shape).astype(jnp.bfloat16)
    attended = product(mixed_low, w_out)
    after_attn = embedded + gate1 * attended
    normed_two, inverse_two = layer_norm(after_attn)
    normed_b = (normed_two * (1.0 + scale2) + shift2).astype(jnp.bfloat16)
    upward = product(normed_b, w_up)
    hidden = jax.nn.gelu(upward).astype(jnp.bfloat16)
    downward = dot_last(hidden, w_down)
    after_mlp = after_attn + gate2 * downward
    normed_three, inverse_three = layer_norm(after_mlp)
    normed_c = normed_three.astype(jnp.bfloat16)
    delta = dot_last(normed_c, io_all[1])
    kept = (
        cond_vec,
        silu_low,
        modul,
        state_low,
        normed_one,
        inverse_one,
        normed_a,
        queries,
        keys,
        values,
        log_total,
        mixed_low,
        attended,
        normed_two,
        inverse_two,
        normed_b,
        upward,
        hidden,
        downward,
        normed_three,
        inverse_three,
        normed_c,
    )
    return (state + active * delta, kept)


def backward_step(weights, kept, grad_state, active, select):
    w_qkv, w_out, w_up, w_down, w_ada, io_all, table, pos, bias = weights
    (
        cond_vec,
        silu_low,
        modul,
        state_low,
        normed_one,
        inverse_one,
        normed_a,
        queries,
        keys,
        values,
        log_total,
        mixed_low,
        attended,
        normed_two,
        inverse_two,
        normed_b,
        upward,
        hidden,
        downward,
        normed_three,
        inverse_three,
        normed_c,
    ) = kept
    width = w_out.shape[0]
    shift1, scale1, gate1, shift2, scale2, gate2 = modulation(modul, width)
    delta_grad = (active * grad_state).astype(jnp.bfloat16)
    grad_head = rows_product(delta_grad, normed_c)
    grad_mlp = norm_back(product(delta_grad, io_all[1]), normed_three, inverse_three)
    grad_gate2 = jnp.sum(grad_mlp * downward, 1)
    down_grad = (gate2 * grad_mlp).astype(jnp.bfloat16)
    grad_down = rows_product(down_grad, hidden)
    grad_hidden = product(down_grad, w_down)
    up_grad = jax.vjp(jax.nn.gelu, upward)[1](grad_hidden)[0].astype(jnp.bfloat16)
    grad_up = rows_product(normed_b, up_grad)
    grad_normed_b = dot_last(up_grad, w_up)
    grad_scale2 = jnp.sum(grad_normed_b * normed_two, 1)
    grad_shift2 = jnp.sum(grad_normed_b, 1)
    grad_attn = grad_mlp + norm_back(grad_normed_b * (1.0 + scale2), normed_two, inverse_two)
    grad_gate1 = jnp.sum(grad_attn * attended, 1)
    attn_grad = (gate1 * grad_attn).astype(jnp.bfloat16)
    grad_out = rows_product(mixed_low, attn_grad)
    mixed_grad = dot_last(attn_grad, w_out).astype(jnp.bfloat16)
    q_heads = heads_view(queries)
    k_heads = heads_view(keys)
    v_heads = heads_view(values)
    g_heads = heads_view(mixed_grad)
    scores = jnp.einsum(
        "sphd,snhd->shpn", q_heads, k_heads, preferred_element_type=jnp.float32
    ) * HEAD ** (-0.5)
    probs = jnp.exp(scores - log_total)
    probs_low = probs.astype(jnp.bfloat16)
    grad_probs = jnp.einsum("sphd,snhd->shpn", g_heads, v_heads, preferred_element_type=jnp.float32)
    score_grad = (
        HEAD ** (-0.5) * probs * (grad_probs - jnp.sum(grad_probs * probs, -1, keepdims=True))
    ).astype(jnp.bfloat16)
    grad_queries = jnp.einsum(
        "shpn,snhd->sphd", score_grad, k_heads, preferred_element_type=jnp.float32
    ).reshape(queries.shape)
    key_part = jnp.einsum(
        "shpn,sphd->snhd", score_grad, q_heads, preferred_element_type=jnp.float32
    ).reshape(keys.shape)
    value_part = jnp.einsum(
        "shpn,sphd->snhd", probs_low, g_heads, preferred_element_type=jnp.float32
    ).reshape(values.shape)
    grad_keys, grad_values = (
        lax.psum_scatter(key_part, PATCHES, scatter_dimension=1, tiled=True),
        lax.psum_scatter(value_part, PATCHES, scatter_dimension=1, tiled=True),
    )
    qkv_grad = jnp.concatenate([grad_queries, grad_keys, grad_values], -1).astype(jnp.bfloat16)
    grad_qkv = rows_product(normed_a, qkv_grad)
    grad_normed_a = dot_last(qkv_grad, w_qkv)
    grad_scale1 = jnp.sum(grad_normed_a * normed_one, 1)
    grad_shift1 = jnp.sum(grad_normed_a, 1)
    grad_embedded = grad_attn + norm_back(grad_normed_a * (1.0 + scale1), normed_one, inverse_one)
    embed_grad = grad_embedded.astype(jnp.bfloat16)
    grad_embed = rows_product(state_low, embed_grad)
    grad_prev = grad_state + dot_last(embed_grad, io_all[0])
    grad_modul = jnp.concatenate(
        [grad_shift1, grad_scale1, grad_gate1, grad_shift2, grad_scale2, grad_gate2], -1
    )
    grad_ada = lax.dot_general(
        silu_low.astype(jnp.float32),
        grad_modul,
        (((0,), (0,)), ((), ())),
        precision=HIGHEST_PRECISION,
    )
    grad_silu = lax.dot_general(
        grad_modul, w_ada.astype(jnp.float32), (((1,), (1,)), ((), ())), precision=HIGHEST_PRECISION
    )
    grad_cond = jax.vjp(jax.nn.silu, cond_vec)[1](grad_silu)[0]
    grad_table = lax.dot_general(
        select, grad_cond, (((0,), (0,)), ((), ())), precision=HIGHEST_PRECISION
    )
    grad_bias = jnp.concatenate([jnp.sum(grad_modul, 0), jnp.sum(grad_embedded, (0, 1))])
    grad_pos = jnp.sum(grad_embedded, 0)
    grads = (
        grad_qkv,
        grad_out,
        grad_up,
        grad_down,
        grad_ada,
        jnp.stack([grad_embed, grad_head]),
        grad_table,
        grad_pos,
        grad_bias,
    )
    return (grad_prev, grads)


def gram_part(block_cols):
    return lax.dot_general(
        block_cols, block_cols, (((1,), (1,)), ((), ())), preferred_element_type=jnp.float32
    )


def zero_gram(block_cols):
    return jnp.zeros((block_cols.shape[0], block_cols.shape[0]), jnp.float32)


def newton_step(block_cols, gram):
    gram_low = gram.astype(jnp.bfloat16)
    poly = (NS_B * gram_low.astype(jnp.float32) + NS_C * product(gram_low, gram_low)).astype(
        jnp.bfloat16
    )
    return (NS_A * block_cols.astype(jnp.float32) + product(poly, block_cols)).astype(jnp.bfloat16)


def keep_block(block_cols, gram):
    return block_cols


def adam_update(weight, first, second, grad, rate):
    first_new = BETA_FIRST * first + (1.0 - BETA_FIRST) * grad
    second_new = BETA_SECOND * second + (1.0 - BETA_SECOND) * grad * grad
    unbiased = first_new / (1.0 - BETA_FIRST**STEP_NUM)
    spread = jnp.sqrt(second_new / (1.0 - BETA_SECOND**STEP_NUM)) + 1e-08
    return (weight * (1.0 - rate * DECAY_ADAM) - rate * unbiased / spread, first_new, second_new)


def general_body(
    states,
    targets,
    lengths,
    intervals,
    qkv_copy,
    qkv_master,
    qkv_moment,
    out_copy,
    out_master,
    out_moment,
    up_copy,
    up_master,
    up_moment,
    down_copy,
    down_master,
    down_moment,
    ada_copy,
    ada_master,
    ada_first,
    ada_second,
    io_proj,
    io_first,
    io_second,
    cond_table,
    cond_first,
    cond_second,
    pos_table,
    pos_first,
    pos_second,
    biases,
    bias_first,
    bias_second,
):
    weights = (
        lax.all_gather(qkv_copy, SHARDS, axis=1, tiled=True),
        lax.all_gather(out_copy, SHARDS, axis=1, tiled=True),
        lax.all_gather(up_copy, SHARDS, axis=1, tiled=True),
        lax.all_gather(down_copy, SHARDS, axis=1, tiled=True),
        lax.all_gather(ada_copy, SHARDS, axis=1, tiled=True),
        lax.all_gather(io_proj.astype(jnp.bfloat16), SHARDS, axis=2, tiled=True),
        lax.all_gather(cond_table.astype(jnp.bfloat16), SHARDS, axis=1, tiled=True),
        lax.all_gather(pos_table.astype(jnp.bfloat16), SHARDS, axis=1, tiled=True),
        lax.all_gather(biases.astype(jnp.bfloat16), SHARDS, axis=0, tiled=True),
    )
    samples, local, values_count = states.shape
    table_rows = cond_table.shape[0]
    my_ids = lax.dynamic_slice_in_dim(intervals, lax.axis_index(SHARDS) * samples, samples)
    counts = jnp.sum(
        (intervals[:, None] == jnp.arange(NI, dtype=jnp.int32)[None]).astype(jnp.float32), 0
    )
    id_counts = jnp.sum(
        (my_ids[:, None] == jnp.arange(NI, dtype=jnp.int32)[None]).astype(jnp.float32)
        * counts[None],
        1,
    )
    weight = 1.0 / (NI * local * lax.axis_size(PATCHES) * values_count * id_counts)
    rows_iota = jnp.arange(table_rows, dtype=jnp.int32)
    id_select = (my_ids[:, None] == rows_iota[None]).astype(jnp.float32)
    state = states.astype(jnp.float32)
    seen_states = []
    kept_all = []
    for step in range(ROLL):
        select = id_select + (rows_iota == NI + step).astype(jnp.float32)[None]
        active = (step < lengths).astype(jnp.float32)[:, None, None]
        seen_states.append(state)
        state, kept = forward_step(weights, state, active, select)
        kept_all.append(kept)
    lat = latitude_weights(local)
    diff = state - targets.astype(jnp.float32)
    err = jnp.sum(jnp.sum(diff * diff, -1) * lat[None], -1)
    loss_local = jnp.sum(weight * err)
    grad_state = 2.0 * weight[:, None, None] * lat[None, :, None] * diff
    totals = None
    for step in reversed(range(ROLL)):
        select = id_select + (rows_iota == NI + step).astype(jnp.float32)[None]
        active = (step < lengths).astype(jnp.float32)[:, None, None]
        kept = kept_all[step]
        grad_state, grads = backward_step(weights, kept, grad_state, active, select)
        totals = grads if totals is None else jax.tree.map(jnp.add, totals, grads)
    reduced = (
        lax.psum_scatter(totals[0], SHARDS, scatter_dimension=1, tiled=True),
        lax.psum_scatter(totals[1], SHARDS, scatter_dimension=1, tiled=True),
        lax.psum_scatter(totals[2], SHARDS, scatter_dimension=1, tiled=True),
        lax.psum_scatter(totals[3], SHARDS, scatter_dimension=1, tiled=True),
        lax.psum_scatter(totals[4], SHARDS, scatter_dimension=1, tiled=True),
        lax.psum_scatter(totals[5], SHARDS, scatter_dimension=2, tiled=True),
        lax.psum_scatter(totals[6], SHARDS, scatter_dimension=1, tiled=True),
        lax.psum_scatter(totals[7], SHARDS, scatter_dimension=1, tiled=True),
        lax.psum_scatter(totals[8], SHARDS, scatter_dimension=0, tiled=True),
    )
    large = (
        lax.psum_scatter(reduced[0], PATCHES, scatter_dimension=0, tiled=True),
        lax.psum_scatter(reduced[1], PATCHES, scatter_dimension=0, tiled=True),
        lax.psum_scatter(reduced[2], PATCHES, scatter_dimension=0, tiled=True),
        lax.psum_scatter(reduced[3], PATCHES, scatter_dimension=0, tiled=True),
        lax.psum_scatter(reduced[4], PATCHES, scatter_dimension=0, tiled=True),
    )
    small = lax.psum((reduced[5], reduced[6], reduced[8]), PATCHES)
    grad_pos = reduced[7]
    first_copy = (lax.axis_index(PATCHES) == 0).astype(jnp.float32)
    squares = jnp.sum(grad_pos * grad_pos)
    for item in large:
        squares = squares + jnp.sum(item * item)
    small_squares = jnp.float32(0.0)
    for item in small:
        small_squares = small_squares + jnp.sum(item * item)
    squares, loss_total = lax.psum(
        (squares + first_copy * small_squares, loss_local), (PATCHES, SHARDS)
    )
    grad_norm = jnp.sqrt(squares)
    clip = jnp.minimum(1.0, CLIP_LIMIT / (grad_norm + 1e-06))
    masters = (qkv_master, out_master, up_master, down_master)
    moments = [
        MOMENTUM * old + clip * grad
        for old, grad in zip((qkv_moment, out_moment, up_moment, down_moment), large[:4])
    ]
    norms = lax.psum(
        (
            jnp.sum(moments[0] * moments[0]),
            jnp.sum(moments[1] * moments[1]),
            jnp.sum(moments[2] * moments[2]),
            jnp.sum(moments[3] * moments[3]),
        ),
        (PATCHES, SHARDS),
    )
    sizes = [jnp.sqrt(norms[which]) for which in range(4)]
    moment_sizes = jnp.stack(sizes) / CLIP_LIMIT
    scaled = [(moments[which] / (sizes[which] + 1e-07)).astype(jnp.bfloat16) for which in range(4)]
    columns = (
        lax.all_gather(scaled[0], PATCHES, axis=0, tiled=True),
        lax.all_gather(scaled[1], PATCHES, axis=0, tiled=True),
        lax.all_gather(scaled[2], PATCHES, axis=0, tiled=True),
        lax.all_gather(scaled[3], PATCHES, axis=0, tiled=True),
    )
    seq_index = lax.axis_index(PATCHES)
    seq_count = lax.axis_size(PATCHES)
    owners = [seq_index == which % seq_count for which in range(4)]
    blocks = list(columns)
    for turn in range(NS_ITERS):
        partial_value = [
            lax.cond(owners[which], gram_part, zero_gram, blocks[which]) for which in range(4)
        ]
        grams = lax.psum(
            (partial_value[0], partial_value[1], partial_value[2], partial_value[3]), SHARDS
        )
        blocks = [
            lax.cond(owners[which], newton_step, keep_block, blocks[which], grams[which])
            for which in range(4)
        ]
    blocks = [broadcast(blocks[which], PATCHES, which % seq_count) for which in range(4)]
    row_count = qkv_master.shape[0]
    fresh = []
    for which in range(4):
        my_rows = lax.dynamic_slice_in_dim(
            blocks[which], seq_index * row_count, row_count, 0
        ).astype(jnp.float32)
        all_cols = masters[which].shape[1] * lax.axis_size(SHARDS)
        fresh.append(
            masters[which] * (1.0 - RATE_MUON * DECAY_MUON)
            - RATE_MUON * 0.2 * math.sqrt(all_cols) * my_rows
        )
    copies = (
        lax.all_gather(fresh[0].astype(jnp.bfloat16), PATCHES, axis=0, tiled=True),
        lax.all_gather(fresh[1].astype(jnp.bfloat16), PATCHES, axis=0, tiled=True),
        lax.all_gather(fresh[2].astype(jnp.bfloat16), PATCHES, axis=0, tiled=True),
        lax.all_gather(fresh[3].astype(jnp.bfloat16), PATCHES, axis=0, tiled=True),
    )
    ada_res = adam_update(ada_master, ada_first, ada_second, clip * large[4], RATE_ADAM)
    io_res = adam_update(io_proj, io_first, io_second, clip * small[0], RATE_ADAM)
    cond_res = adam_update(cond_table, cond_first, cond_second, clip * small[1], RATE_TABLE)
    pos_res = adam_update(pos_table, pos_first, pos_second, clip * grad_pos, RATE_TABLE)
    bias_res = adam_update(biases, bias_first, bias_second, clip * small[2], RATE_ADAM)
    return (
        loss_total,
        grad_norm,
        moment_sizes,
        fresh[0],
        moments[0],
        copies[0],
        fresh[1],
        moments[1],
        copies[1],
        fresh[2],
        moments[2],
        copies[2],
        fresh[3],
        moments[3],
        copies[3],
        ada_res[0],
        ada_res[1],
        ada_res[2],
        io_res[0],
        io_res[1],
        io_res[2],
        cond_res[0],
        cond_res[1],
        cond_res[2],
        pos_res[0],
        pos_res[1],
        pos_res[2],
        bias_res[0],
        bias_res[1],
        bias_res[2],
    )


LANES = 128
MATRICES = 4
LOW = jnp.bfloat16
MESH = pl.DeviceIdType.MESH


def round_up(value, unit):
    return -(-value // unit) * unit


def member_peer(members, shift):
    index = lax.axis_index(PATCHES)
    return {PATCHES: index // members * members + lax.rem(lax.rem(index, members) + shift, members)}


def group_peer(members, shift):
    return {PATCHES: lax.rem(lax.axis_index(PATCHES) + shift * members, lax.axis_size(PATCHES))}


def sibling_peer():
    index = lax.axis_index(SHARDS)
    return {SHARDS: index + 1 - 2 * lax.rem(index, 2)}


def where(condition, action):
    if condition is None:
        action()
    else:
        pl.when(condition())(action)


class Moves:
    def __init__(self, name, ids, vmem=None):
        self.name = name
        self.ids = ids
        self.vmem = vmem
        self.operands = []
        self.operand_specs = []
        self.outputs = []
        self.output_specs = []
        self.scratches = []
        self.moves = []
        self.locals = []
        self.steps = []
        self.peers = {}

    def operand(self, array, space=pl.ANY):
        self.operands.append(array)
        self.operand_specs.append(pl.BlockSpec(memory_space=space))
        return (0, len(self.operands) - 1)

    def output(self, shape, dtype, space=pl.ANY):
        self.outputs.append(jax.ShapeDtypeStruct(shape, dtype))
        self.output_specs.append(pl.BlockSpec(memory_space=space))
        return (1, len(self.outputs) - 1)

    def scratch(self, shape, dtype):
        self.scratches.append(pltpu.VMEM(shape, dtype))
        return (2, len(self.scratches) - 1)

    def keep(self, source, source_at, target, target_at):
        self.locals.append((source, source_at, target, target_at))
        return len(self.locals) - 1

    def move(
        self, peer_key, peer, source, source_at, target, target_at, after=(), sends=None, takes=None, later=False
    ):
        number = len(self.moves)
        self.peers.setdefault(peer_key, peer)
        self.moves.append((peer_key, source, source_at, target, target_at, sends, takes, later or bool(after)))
        for earlier in after:
            self.steps.append((self.await_move, earlier))
        if after:
            self.steps.append((self.start_move, number))
        return number

    def wait_for(self, number):
        self.steps.append((self.await_move, number))

    def start(self, number):
        self.steps.append((self.start_move, number))

    def wait_local(self, number):
        self.steps.append((self.await_local, number))

    def task(self, action):
        self.steps.append((self.do_task, action))

    def await_move(self, number):
        if number not in self.arrived:
            self.arrived.add(number)
            where(self.moves[number][6], self.remote[number].wait_recv)

    def start_move(self, number):
        where(self.moves[number][5], self.remote[number].start)

    def await_local(self, number):
        if number not in self.kept:
            self.kept.add(number)
            self.local[number].wait()

    def do_task(self, action):
        action(self.ref)

    def ref(self, which):
        return self.refs[which[0]][which[1]]

    def view(self, which, index):
        ref = self.ref(which)
        return ref.at[index()] if index is not None else ref

    def kernel(self, *refs):
        sizes = (len(self.operands), len(self.outputs), len(self.scratches))
        self.refs = (refs[: sizes[0]], refs[sizes[0] : sizes[0] + sizes[1]], refs[sizes[0] + sizes[1] : sum(sizes)])
        local_sem, send_sem, recv_sem = refs[sum(sizes) :]
        self.arrived, self.kept = set(), set()
        devices = {key: peer() for key, peer in self.peers.items()}
        barrier = pltpu.get_barrier_semaphore()
        for device in devices.values():
            pl.semaphore_signal(barrier, inc=1, device_id=device, device_id_type=MESH)
        pl.semaphore_wait(barrier, len(devices))
        self.remote = []
        for number, (key, source, source_at, target, target_at, _, _, later) in enumerate(self.moves):
            self.remote.append(
                pltpu.make_async_remote_copy(
                    src_ref=self.view(source, source_at),
                    dst_ref=self.view(target, target_at),
                    send_sem=send_sem.at[number],
                    recv_sem=recv_sem.at[number],
                    device_id=devices[key],
                    device_id_type=MESH,
                )
            )
            if not later:
                self.start_move(number)
        self.local = [
            pltpu.make_async_copy(self.view(source, source_at), self.view(target, target_at), local_sem.at[number])
            for number, (source, source_at, target, target_at) in enumerate(self.locals)
        ]
        for copy in self.local:
            copy.start()
        for action, number in self.steps:
            action(number)
        for number in range(len(self.locals)):
            self.await_local(number)
        for number, copy in enumerate(self.remote):
            self.await_move(number)
            where(self.moves[number][5], copy.wait_send)

    def run(self):
        return pl.pallas_call(
            self.kernel,
            out_shape=self.outputs,
            in_specs=self.operand_specs,
            out_specs=self.output_specs,
            scratch_shapes=[
                *self.scratches,
                pltpu.SemaphoreType.DMA((max(1, len(self.locals)),)),
                pltpu.SemaphoreType.DMA((len(self.moves),)),
                pltpu.SemaphoreType.DMA((len(self.moves),)),
            ],
            compiler_params=pltpu.CompilerParams(
                collective_id=self.ids.setdefault(self.name, len(self.ids)),
                has_side_effects=True,
                vmem_limit_bytes=self.vmem,
            ),
            name=self.name,
        )(*self.operands)

    def along(self, axis, source, target, pairs):
        count = lax.axis_size(axis)

        def other(shift):
            return lax.rem(lax.axis_index(axis) + shift, count)

        for shift in range(1, count):
            for source_at, target_at in pairs:
                self.move(
                    (axis, shift),
                    lambda shift=shift: {axis: other(shift)},
                    source,
                    None if source_at is None else (lambda at=source_at, shift=shift: at(other(shift))),
                    target,
                    lambda at=target_at: at(lax.axis_index(axis)),
                )
        for source_at, target_at in pairs:
            self.keep(
                source,
                None if source_at is None else (lambda at=source_at: at(lax.axis_index(axis))),
                target,
                lambda at=target_at: at(lax.axis_index(axis)),
            )

    def gather(self, axis, array):
        target = self.output((lax.axis_size(axis),) + array.shape, array.dtype)
        self.along(axis, self.operand(array), target, [(None, lambda sender: (sender,))])

    def gather_columns(self, axis, array):
        width = array.shape[-1]
        target = self.output(array.shape[:-1] + (lax.axis_size(axis) * width,), array.dtype)
        lead = (slice(None),) * (array.ndim - 1)
        self.along(
            axis,
            self.operand(array),
            target,
            [(None, lambda sender: lead + (pl.ds(pl.multiple_of(sender * width, LANES), width),))],
        )

    def gather_twice(self, arrays, members):
        shards = lax.axis_size(SHARDS)
        entries = []
        for array in arrays:
            source = self.operand(array)
            target = self.output((shards,) + array.shape, array.dtype)
            rows = array.shape[0] // members

            def place(back_member, back_pair, rows=rows):
                index = lax.rem(lax.rem(lax.axis_index(PATCHES), members) + members - back_member, members)
                who = lax.rem(lax.axis_index(SHARDS) + shards - 2 * back_pair, shards)
                return (who, pl.ds(pl.multiple_of(index * rows, rows), rows))

            def mine(rows=rows):
                index = lax.rem(lax.axis_index(PATCHES), members)
                return (pl.ds(pl.multiple_of(index * rows, rows), rows),)

            firsts = [
                self.move(
                    (SHARDS, 2 * pair),
                    lambda pair=pair: {SHARDS: lax.rem(lax.axis_index(SHARDS) + 2 * pair, shards)},
                    source,
                    mine,
                    target,
                    functools.partial(place, 0, 0),
                )
                for pair in range(1, shards // 2)
            ]
            entries.append((source, target, place, firsts))
        for source, target, _, _ in entries:
            own = lambda: (lax.axis_index(SHARDS),)
            self.move((SHARDS,), sibling_peer, source, None, target, own)
            self.keep(source, None, target, own)
        last = []
        for _, target, place, firsts in entries:
            for pair, first in enumerate(firsts, 1):
                near = functools.partial(place, 0, pair)
                for shift in range(1, members):
                    number = self.move(
                        (PATCHES, members, shift),
                        functools.partial(member_peer, members, shift),
                        target,
                        near,
                        target,
                        near,
                        (first,),
                    )
                    last.append((target, functools.partial(place, shift, pair), number))
                self.move((SHARDS,), sibling_peer, target, near, target, near, (first,))
        self.to_sibling(last)

    def to_sibling(self, waiting):
        for target, place, number in waiting:
            self.move((SHARDS,), sibling_peer, target, place, target, place, (number,))

    def exchange(self, axis, array):
        target = self.output(array.shape, array.dtype)
        self.along(axis, self.operand(array), target, [(lambda receiver: (receiver,), lambda sender: (sender,))])

    def exchange_columns(self, axis, array):
        width = array.shape[-1] // lax.axis_size(axis)
        target = self.output((lax.axis_size(axis), array.shape[0], width), array.dtype)
        self.along(
            axis,
            self.operand(array),
            target,
            [
                (
                    lambda receiver: (slice(None), pl.ds(pl.multiple_of(receiver * width, LANES), width)),
                    lambda sender: (sender,),
                )
            ],
        )

    def rows_to_heads(self, axis, array, planes):
        count, rows = lax.axis_size(axis), array.shape[0]
        columns = array.shape[1] // planes
        width = columns // count
        target = self.output((planes, rows * count, width), array.dtype)
        self.along(
            axis,
            self.operand(array),
            target,
            [
                (
                    lambda receiver, plane=plane: (
                        slice(None),
                        pl.ds(pl.multiple_of(plane * columns + receiver * width, LANES), width),
                    ),
                    lambda sender, plane=plane: (plane, pl.ds(pl.multiple_of(sender * rows, rows), rows)),
                )
                for plane in range(planes)
            ],
        )

    def heads_to_rows(self, axis, array):
        count = lax.axis_size(axis)
        planes, all_rows, width = array.shape
        rows, columns = all_rows // count, width * count
        target = self.output((rows, planes * columns), array.dtype)
        self.along(
            axis,
            self.operand(array),
            target,
            [
                (
                    lambda receiver, plane=plane: (plane, pl.ds(pl.multiple_of(receiver * rows, rows), rows)),
                    lambda sender, plane=plane: (
                        slice(None),
                        pl.ds(pl.multiple_of(plane * columns + sender * width, LANES), width),
                    ),
                )
                for plane in range(planes)
            ],
        )


def total_kernel(x_ref, o_ref, near, far, near_send, near_recv, far_send, far_recv):
    near_count, far_count = near.shape[0], far.shape[0]
    near_me, far_me = lax.axis_index(SHARDS), lax.axis_index(PATCHES)
    barrier = pltpu.get_barrier_semaphore()
    for shift in range(1, near_count):
        pl.semaphore_signal(
            barrier, inc=1, device_id={SHARDS: lax.rem(near_me + shift, near_count)}, device_id_type=MESH
        )
    for shift in range(1, far_count):
        pl.semaphore_signal(
            barrier, inc=1, device_id={PATCHES: lax.rem(far_me + shift, far_count)}, device_id_type=MESH
        )
    pl.semaphore_wait(barrier, near_count + far_count - 2)

    def spread(axis, me, count, buffer, send, recv):
        copies = []
        for shift in range(1, count):
            copy = pltpu.make_async_remote_copy(
                src_ref=buffer.at[me],
                dst_ref=buffer.at[me],
                send_sem=send.at[shift - 1],
                recv_sem=recv.at[shift - 1],
                device_id={axis: lax.rem(me + shift, count)},
                device_id_type=MESH,
            )
            copy.start()
            copies.append(copy)
        for copy in copies:
            copy.wait()
        return jnp.sum(buffer[...], 0)

    near[near_me] = x_ref[...]
    far[far_me] = spread(SHARDS, near_me, near_count, near, near_send, near_recv)
    o_ref[...] = spread(PATCHES, far_me, far_count, far, far_send, far_recv)


def total_of(ids, values):
    near_count, far_count = lax.axis_size(SHARDS), lax.axis_size(PATCHES)
    in_vmem = pl.BlockSpec(memory_space=pltpu.VMEM)
    return pl.pallas_call(
        total_kernel,
        out_shape=jax.ShapeDtypeStruct(values.shape, values.dtype),
        in_specs=[in_vmem],
        out_specs=in_vmem,
        scratch_shapes=[
            pltpu.VMEM((near_count,) + values.shape, values.dtype),
            pltpu.VMEM((far_count,) + values.shape, values.dtype),
            pltpu.SemaphoreType.DMA((near_count - 1,)),
            pltpu.SemaphoreType.DMA((near_count - 1,)),
            pltpu.SemaphoreType.DMA((far_count - 1,)),
            pltpu.SemaphoreType.DMA((far_count - 1,)),
        ],
        compiler_params=pltpu.CompilerParams(
            collective_id=ids.setdefault("total", len(ids)), has_side_effects=True
        ),
        name="total",
    )(values)


def contract(left, right, left_dim, right_dim):
    return lax.dot_general(
        left, right, (((left_dim,), (right_dim,)), ((), ())), preferred_element_type=jnp.float32
    )


QUERY_BLOCK = 256
CHAIN_CHUNKS = 4
GRAM_ROWS = 256


def attention_kernel(heads, qkv_ref, mixed_ref):
    rows = pl.ds(pl.multiple_of(pl.program_id(0) * QUERY_BLOCK, QUERY_BLOCK), QUERY_BLOCK)
    mixed = []
    for head in range(heads):
        lanes = pl.ds(head * HEAD, HEAD)
        queries, keys, values = qkv_ref[0, rows, lanes], qkv_ref[1, :, lanes], qkv_ref[2, :, lanes]
        scores = contract(queries, keys, 1, 1) * HEAD ** (-0.5)
        expo = jnp.exp(scores - jnp.max(scores, -1, keepdims=True))
        probs = (expo / jnp.sum(expo, -1, keepdims=True)).astype(LOW)
        mixed.append(contract(probs, values, 1, 0))
    mixed_ref[...] = jnp.concatenate(mixed, -1).astype(LOW)


def attention(qkv):
    _, patches, width = qkv.shape
    return pl.pallas_call(
        functools.partial(attention_kernel, width // HEAD),
        out_shape=jax.ShapeDtypeStruct((patches, width), LOW),
        grid=(patches // QUERY_BLOCK,),
        in_specs=[pl.BlockSpec(qkv.shape, lambda block: (0, 0, 0))],
        out_specs=pl.BlockSpec((QUERY_BLOCK, width), lambda block: (block, 0)),
        compiler_params=pltpu.CompilerParams(vmem_limit_bytes=48 * 2**20),
        name="attention",
    )(qkv)


def attention_back_kernel(heads, qkv_ref, grad_ref, out_ref, key_total, value_total):
    block = pl.program_id(0)
    rows = pl.ds(pl.multiple_of(block * QUERY_BLOCK, QUERY_BLOCK), QUERY_BLOCK)

    @pl.when(block == 0)
    def _():
        key_total[...] = jnp.zeros_like(key_total)
        value_total[...] = jnp.zeros_like(value_total)

    query_parts = []
    for head in range(heads):
        lanes = pl.ds(head * HEAD, HEAD)
        queries, keys, values = qkv_ref[0, rows, lanes], qkv_ref[1, :, lanes], qkv_ref[2, :, lanes]
        grads = grad_ref[rows, lanes]
        scores = contract(keys, queries, 1, 1) * HEAD ** (-0.5)
        expo = jnp.exp(scores - jnp.max(scores, 0, keepdims=True))
        probs = expo / jnp.sum(expo, 0, keepdims=True)
        grad_probs = contract(values, grads, 1, 1)
        shared = jnp.sum(grad_probs * probs, 0, keepdims=True)
        score_grad = (HEAD ** (-0.5) * probs * (grad_probs - shared)).astype(LOW)
        query_parts.append(contract(score_grad, keys, 0, 0))
        key_total[head] += contract(score_grad, queries, 1, 0)
        value_total[head] += contract(probs.astype(LOW), grads, 1, 0)
    out_ref[0, rows, :] = jnp.concatenate(query_parts, -1).astype(LOW)

    @pl.when(block == pl.num_programs(0) - 1)
    def _():
        out_ref[1] = jnp.concatenate([key_total[head] for head in range(heads)], -1).astype(LOW)
        out_ref[2] = jnp.concatenate([value_total[head] for head in range(heads)], -1).astype(LOW)


def attention_back(qkv, grads):
    _, patches, width = qkv.shape
    heads = width // HEAD
    return pl.pallas_call(
        functools.partial(attention_back_kernel, heads),
        out_shape=jax.ShapeDtypeStruct(qkv.shape, LOW),
        grid=(patches // QUERY_BLOCK,),
        in_specs=[
            pl.BlockSpec(qkv.shape, lambda block: (0, 0, 0)),
            pl.BlockSpec(grads.shape, lambda block: (0, 0)),
        ],
        out_specs=pl.BlockSpec(qkv.shape, lambda block: (0, 0, 0)),
        scratch_shapes=[
            pltpu.VMEM((heads, patches, HEAD), jnp.float32),
            pltpu.VMEM((heads, patches, HEAD), jnp.float32),
        ],
        compiler_params=pltpu.CompilerParams(vmem_limit_bytes=48 * 2**20),
        name="attention_back",
    )(qkv, grads)


def newton_kernel(gram_ref, block_ref, out_ref, gram, poly, once, gram_low, poly_low, once_low, block):
    size = gram_ref.shape[0]
    tiles = size // GRAM_ROWS
    eye = jnp.equal(
        lax.broadcasted_iota(jnp.int32, (GRAM_ROWS, GRAM_ROWS), 0),
        lax.broadcasted_iota(jnp.int32, (GRAM_ROWS, GRAM_ROWS), 1),
    ).astype(jnp.float32)

    def rows_at(tile):
        return pl.ds(pl.multiple_of(tile * GRAM_ROWS, GRAM_ROWS), GRAM_ROWS)

    def split(full, low):
        def add(tile, total):
            return total + jnp.sum(full[rows_at(tile), rows_at(tile)] * eye)

        mean = lax.fori_loop(0, tiles, add, jnp.float32(0.0)) / size

        @pl.loop(0, tiles)
        def _(tile):
            rows = rows_at(tile)
            low[rows, :] = full[rows, :].astype(LOW)
            low[rows, rows] = (full[rows, rows] - mean * eye).astype(LOW)

        return mean

    def multiply(target, left, left_mean, left_low, right, right_mean, right_low, finish):
        @pl.loop(0, tiles)
        def _(tile):
            rows = rows_at(tile)
            value = contract(left_low[rows, :], right_low[...], 1, 0)
            value = value + left_mean * right[rows, :] + right_mean * left[rows, :]
            target[rows, :] = finish(value, rows)

    def mend(target, amount):
        @pl.loop(0, tiles)
        def _(tile):
            rows = rows_at(tile)
            target[rows, rows] -= amount * eye

    def advance(last):
        gram_mean = split(gram, gram_low)
        multiply(
            poly,
            gram,
            gram_mean,
            gram_low,
            gram,
            gram_mean,
            gram_low,
            lambda value, rows: NS_B * gram[rows, :] + NS_C * value,
        )
        mend(poly, NS_C * gram_mean * gram_mean)
        poly_mean = split(poly, poly_low)
        out_ref[...] = block[...]

        @pl.loop(0, tiles)
        def _(tile):
            rows = rows_at(tile)
            value = contract(poly_low[rows, :], out_ref[...], 1, 0)
            block[rows, :] = (value + (NS_A + poly_mean) * out_ref[rows, :].astype(jnp.float32)).astype(LOW)

        if not last:
            multiply(once, poly, poly_mean, poly_low, gram, gram_mean, gram_low, lambda value, rows: value)
            mend(once, poly_mean * gram_mean)
            once_mean = split(once, once_low)
            multiply(
                gram,
                poly,
                poly_mean,
                poly_low,
                once,
                once_mean,
                once_low,
                lambda value, rows: NS_A * NS_A * gram[rows, :] + 2.0 * NS_A * once[rows, :] + value,
            )
            mend(gram, poly_mean * once_mean)

    gram[...] = gram_ref[...]
    block[...] = block_ref[...]

    @pl.loop(0, NS_ITERS - 1)
    def _(turn):
        advance(False)

    advance(True)
    out_ref[...] = block[...]


def newton_schulz(gram, block):
    in_vmem = pl.BlockSpec(memory_space=pltpu.VMEM)
    full, low = pltpu.VMEM(gram.shape, jnp.float32), pltpu.VMEM(gram.shape, LOW)
    return pl.pallas_call(
        newton_kernel,
        out_shape=jax.ShapeDtypeStruct(block.shape, block.dtype),
        in_specs=[in_vmem, in_vmem],
        out_specs=in_vmem,
        scratch_shapes=[full, full, full, low, low, low, pltpu.VMEM(block.shape, LOW)],
        compiler_params=pltpu.CompilerParams(vmem_limit_bytes=48 * 2**20),
        name="newton",
    )(gram, block)


def fast_body(
    states,
    targets,
    lengths,
    intervals,
    qkv_copy,
    qkv_master,
    qkv_moment,
    out_copy,
    out_master,
    out_moment,
    up_copy,
    up_master,
    up_moment,
    down_copy,
    down_master,
    down_moment,
    ada_copy,
    ada_master,
    ada_first,
    ada_second,
    io_proj,
    io_first,
    io_second,
    cond_table,
    cond_first,
    cond_second,
    pos_table,
    pos_first,
    pos_second,
    biases,
    bias_first,
    bias_second,
):
    ids = {}
    f32 = jnp.float32
    seq_count, shards = lax.axis_size(PATCHES), lax.axis_size(SHARDS)
    seq_index, shard = lax.axis_index(PATCHES), lax.axis_index(SHARDS)
    members = seq_count // MATRICES
    group, member = seq_index // members, lax.rem(seq_index, members)
    samples, local, values_count = states.shape
    table_rows, table_cols = cond_table.shape
    width = table_cols * shards
    ada_cols = ada_copy.shape[1]
    padded = round_up(values_count, LANES)

    moves = Moves("tables", ids)
    moves.gather(SHARDS, cond_table)
    moves.gather(SHARDS, biases[None])
    table_parts, bias_parts = moves.run()
    table = jnp.moveaxis(table_parts, 0, 1).reshape(table_rows, width).astype(LOW).astype(f32)
    bias = bias_parts.reshape(-1).astype(LOW).astype(f32)
    rows_iota = jnp.arange(table_rows, dtype=jnp.int32)
    id_rows = (intervals[:, None] == rows_iota[None]).astype(f32)
    step_rows = (rows_iota[None] == NI + jnp.arange(ROLL, dtype=jnp.int32)[:, None]).astype(f32)
    select = (id_rows[:, None] + step_rows[None]).reshape(-1, table_rows)
    cond_vec = jnp.sum(select[:, :, None] * table[None], 1)
    silu_low = jax.nn.silu(cond_vec).astype(LOW)
    modul_shard = product(silu_low, ada_copy) + lax.dynamic_slice_in_dim(bias, shard * ada_cols, ada_cols)[None]

    moves = Moves("weights", ids)
    moves.exchange(SHARDS, modul_shard.reshape(shards, ROLL, ada_cols))
    moves.gather_columns(SHARDS, pos_table.astype(LOW))
    io_low = jnp.pad(io_proj.astype(LOW), ((0, 0), (0, padded - values_count), (0, 0)))
    moves.gather_twice((io_low.reshape(2 * padded, -1), out_copy, qkv_copy), members)
    modul, pos, *parts = moves.run()
    io_all, w_out, w_qkv = [jnp.moveaxis(item, 0, 1).reshape(item.shape[1], -1) for item in parts]
    io_all = io_all.reshape(2, padded, width)
    modul = jnp.moveaxis(modul, 0, 1).reshape(ROLL, 6 * width)
    pos = pos.astype(f32)

    masters = (qkv_master, up_master, down_master, out_master)
    momenta = (qkv_moment, up_moment, down_moment, out_moment)
    group_cols = [item.shape[1] // members for item in momenta]
    most_cols = max(group_cols)

    def widen(item):
        return jnp.pad(item, ((0, 0), (0, most_cols - item.shape[1])))

    moment_parts = jnp.stack(
        [
            widen(item[:, part * cols : (part + 1) * cols].astype(LOW))
            for item, cols in zip(momenta, group_cols)
            for part in range(members)
        ]
    )
    half_rows = moment_parts.shape[1] // 2

    counts = jnp.sum((intervals[:, None] == jnp.arange(NI, dtype=jnp.int32)[None]).astype(f32), 0)
    my_id = lax.dynamic_slice_in_dim(intervals, shard, 1)
    id_count = jnp.sum((my_id == jnp.arange(NI, dtype=jnp.int32)).astype(f32) * counts)
    weight = 1.0 / (NI * local * seq_count * values_count * id_count)
    length = lengths[0]
    value_pad = ((0, 0), (0, padded - values_count))
    state = jnp.pad(states[0].astype(f32), value_pad)
    embed_bias = bias[6 * width :]
    kept = []
    gathered = {}
    moment_halves = []

    def run_with(moves, names):
        results = moves.run()
        first = len(results) - len(names)
        for name, result in zip(names, results[first:]):
            gathered.setdefault(name, {})[step] = result
        return results[:first]

    for step in range(ROLL):
        shift1, scale1, gate1, shift2, scale2, gate2 = jnp.split(modul[step][None], 6, -1)
        state_low = state.astype(LOW)
        embedded = product(state_low, io_all[0]) + embed_bias + pos
        normed_one, inverse_one = layer_norm(embedded)
        normed_a = (normed_one * (1.0 + scale1) + shift1).astype(LOW)
        qkv_rows = product(normed_a, w_qkv).astype(LOW)
        moves = Moves(f"heads{step}", ids)
        moves.rows_to_heads(PATCHES, qkv_rows, 3)
        moves.gather(SHARDS, normed_a)
        if step:
            moves.gather(SHARDS, kept[-1][5])
            qkv, gathered_a, gathered_mixed = moves.run()
            gathered["mixed"] = {step - 1: gathered_mixed}
        else:
            qkv, gathered_a = moves.run()
        gathered.setdefault("a", {})[step] = gathered_a
        mixed_heads = attention(qkv)
        moves = Moves("mixed_rows", ids)
        moves.heads_to_rows(PATCHES, mixed_heads[None])
        moves.gather(SHARDS, state_low)
        (mixed,) = run_with(moves, ["state"])
        attended = product(mixed, w_out)
        after_attn = embedded + gate1 * attended
        normed_two, inverse_two = layer_norm(after_attn)
        normed_b = (normed_two * (1.0 + scale2) + shift2).astype(LOW)
        moves = Moves("tokens_moment", ids)
        moves.gather(SHARDS, normed_b)
        moves.exchange(PATCHES, moment_parts[:, step * half_rows : (step + 1) * half_rows])
        tokens_b, moment_half = moves.run()
        moment_halves.append(moment_half)
        tokens_b = tokens_b.reshape(shards * local, width)
        upward = product(tokens_b, up_copy)
        hidden = jax.nn.gelu(upward).astype(LOW)
        down_part = contract(hidden, down_copy, 1, 1).astype(LOW).reshape(shards, local, width)
        moves = Moves("token_sums", ids)
        moves.exchange(SHARDS, down_part)
        downward = jnp.sum(moves.run()[0].astype(f32), 0)
        after_mlp = after_attn + gate2 * downward
        normed_three, inverse_three = layer_norm(after_mlp)
        normed_c = normed_three.astype(LOW)
        delta = contract(normed_c, io_all[1], 1, 1)
        kept.append(
            (
                state_low,
                normed_one,
                inverse_one,
                normed_a,
                qkv,
                mixed,
                attended,
                normed_two,
                inverse_two,
                tokens_b,
                upward,
                hidden,
                downward,
                normed_three,
                inverse_three,
                normed_c,
            )
        )
        state = state + (step < length).astype(f32) * delta

    lat = latitude_weights(local)
    diff = state - jnp.pad(targets[0].astype(f32), value_pad)
    loss_local = weight * jnp.sum(jnp.sum(diff * diff, -1) * lat)
    grad_state = 2.0 * weight * lat[:, None] * diff

    back = [None] * ROLL
    mlp_back = []

    def patch_sum(item, cols):
        mine = lax.dynamic_slice_in_dim(item, member * cols, cols, 1)
        low = item.astype(LOW)
        for shift in range(1, members):
            pairs = [
                (index, index // members * members + (index + shift) % members) for index in range(seq_count)
            ]
            to_member = lax.rem(member + shift, members)
            outgoing = lax.dynamic_slice_in_dim(low, to_member * cols, cols, 1)
            mine = mine + lax.ppermute(outgoing, PATCHES, pairs).astype(f32)
        return mine

    for step in reversed(range(ROLL)):
        (
            state_low,
            normed_one,
            inverse_one,
            normed_a,
            qkv,
            mixed,
            attended,
            normed_two,
            inverse_two,
            tokens_b,
            upward,
            hidden,
            downward,
            normed_three,
            inverse_three,
            normed_c,
        ) = kept[step]
        shift1, scale1, gate1, shift2, scale2, gate2 = jnp.split(modul[step][None], 6, -1)
        delta_grad = ((step < length).astype(f32) * grad_state).astype(LOW)
        grad_mlp = norm_back(product(delta_grad, io_all[1]), normed_three, inverse_three)
        grad_gate2 = jnp.sum(grad_mlp * downward, 0)
        moves = Moves("tokens", ids)
        moves.gather(SHARDS, (gate2 * grad_mlp).astype(LOW))
        tokens_down = moves.run()[0].reshape(shards * local, width)
        grad_hidden = product(tokens_down, down_copy)
        up_grad = jax.vjp(jax.nn.gelu, upward)[1](grad_hidden)[0].astype(LOW)
        mlp_back.append((tokens_b, up_grad, tokens_down, hidden))
        if step == 0:
            all_b, all_up, all_down, all_hidden = [jnp.concatenate(items, 0) for items in zip(*mlp_back)]
            mlp_sums = [
                patch_sum(rows_product(left, right), cols)
                for left, right, cols in ((all_b, all_up, group_cols[1]), (all_down, all_hidden, group_cols[2]))
            ]
        up_part = contract(up_grad, up_copy, 1, 1).astype(LOW).reshape(shards, local, width)
        moves = Moves("token_sums", ids)
        moves.exchange(SHARDS, up_part)
        grad_normed_b = jnp.sum(moves.run()[0].astype(f32), 0)
        grad_scale2 = jnp.sum(grad_normed_b * normed_two, 0)
        grad_shift2 = jnp.sum(grad_normed_b, 0)
        grad_attn = grad_mlp + norm_back(grad_normed_b * (1.0 + scale2), normed_two, inverse_two)
        grad_gate1 = jnp.sum(grad_attn * attended, 0)
        attn_grad = (gate1 * grad_attn).astype(LOW)
        mixed_grad = contract(attn_grad, w_out, 1, 1).astype(LOW)
        moves = Moves(f"mixed_heads{step}", ids)
        moves.rows_to_heads(PATCHES, mixed_grad, 1)
        if step < ROLL - 1:
            moves.exchange_columns(SHARDS, back[step + 1][0])
            moves.exchange_columns(SHARDS, back[step + 1][1])
            mixed_grad_heads, gathered_qkv, gathered_embed = moves.run()
            gathered.setdefault("qkv", {})[step + 1] = gathered_qkv
            gathered.setdefault("embed", {})[step + 1] = gathered_embed
        else:
            (mixed_grad_heads,) = moves.run()
        qkv_grad_heads = attention_back(qkv, mixed_grad_heads[0])
        moves = Moves(f"rows{step}", ids)
        moves.heads_to_rows(PATCHES, qkv_grad_heads)
        moves.exchange_columns(SHARDS, attn_grad)
        moves.exchange_columns(SHARDS, normed_c)
        moves.gather(SHARDS, delta_grad)
        names = ["attn", "c", "delta"]
        if step == ROLL - 1:
            moves.gather(SHARDS, mixed)
            names.append("mixed")
        (qkv_grad,) = run_with(moves, names)
        grad_normed_a = contract(qkv_grad, w_qkv, 1, 1)
        grad_scale1 = jnp.sum(grad_normed_a * normed_one, 0)
        grad_shift1 = jnp.sum(grad_normed_a, 0)
        grad_embedded = grad_attn + norm_back(grad_normed_a * (1.0 + scale1), normed_one, inverse_one)
        embed_grad = grad_embedded.astype(LOW)
        grad_state = grad_state + contract(embed_grad, io_all[0], 1, 1)
        grad_modul = jnp.concatenate([grad_shift1, grad_scale1, grad_gate1, grad_shift2, grad_scale2, grad_gate2])
        back[step] = (qkv_grad, embed_grad, grad_modul, jnp.sum(grad_embedded, 0))

    qkv_grad, embed_grad, _, _ = back[0]
    mlp_low = [item.astype(LOW) for item in mlp_sums]
    modul_parts = jnp.stack([item[2].reshape(shards, ada_cols) for item in back], 1)
    embed_parts = sum(item[3] for item in back).reshape(shards, 1, -1)
    vectors = jnp.concatenate(
        [modul_parts, jnp.pad(embed_parts, ((0, 0), (0, 0), (0, ada_cols - embed_parts.shape[-1])))], 1
    )

    def to_group(moves, item, which, start, size):
        source = moves.operand(item)
        target = moves.output((MATRICES - 1, size, item.shape[1]), LOW)
        for shift in range(1, MATRICES):
            moves.move(
                (PATCHES, seq_count, shift),
                functools.partial(group_peer, members, shift),
                source,
                lambda: (pl.ds(start, size),),
                target,
                lambda shift=shift: (shift - 1,),
                sends=lambda shift=shift: lax.axis_index(PATCHES) // members == (which - shift) % MATRICES,
                takes=lambda: lax.axis_index(PATCHES) // members == which,
            )

    block_rows = qkv_copy.shape[0]
    early = (1, 2)
    first_rows = block_rows * 7 // 16
    moves = Moves("samples", ids)
    moves.exchange_columns(SHARDS, qkv_grad)
    moves.exchange_columns(SHARDS, embed_grad)
    moves.exchange(SHARDS, vectors)
    for item, which in zip(mlp_low, early):
        to_group(moves, item, which, 0, first_rows)
    gathered["qkv"][0], gathered["embed"][0], vectors, *mlp_first = moves.run()
    grad_pos = sum(jnp.sum(item.astype(f32), 0) for item in gathered["embed"].values())

    def from_all(left, right):
        both = [
            jnp.concatenate([gathered[name][step].reshape(shards * local, -1) for step in range(ROLL)], 0)
            for name in (left, right)
        ]
        return rows_product(*both)

    io_here = jnp.stack([from_all("state", "embed"), from_all("delta", "c")])
    io_cols = io_here.shape[-1]
    grads_here = [from_all("a", "qkv"), from_all("mixed", "attn")]
    late = (0, MATRICES - 1)

    moves = Moves("member_sums", ids)
    for item, which in zip(grads_here, late):
        cols = group_cols[which]
        source = moves.operand(item.astype(LOW))
        target = moves.output((members - 1, item.shape[0], cols), LOW)
        for shift in range(1, members):

            def source_at(shift=shift, cols=cols):
                to_member = lax.rem(lax.rem(lax.axis_index(PATCHES), members) + shift, members)
                return (slice(None), pl.ds(pl.multiple_of(to_member * cols, LANES), cols))

            moves.move(
                (PATCHES, members, shift),
                functools.partial(member_peer, members, shift),
                source,
                source_at,
                target,
                lambda shift=shift: (shift - 1,),
            )
    modul_here, embed_here = vectors[:, :ROLL].reshape(-1), jnp.sum(vectors[:, ROLL, : width // shards], 0)
    flat = jnp.concatenate([modul_here, embed_here]).astype(LOW)
    flat_rows = round_up(flat.size, 16 * LANES) // LANES
    moves.gather(PATCHES, jnp.pad(flat, (0, flat_rows * LANES - flat.size)).reshape(flat_rows, LANES))
    moves.exchange(PATCHES, io_here.reshape(seq_count, -1, io_cols).astype(LOW))
    for item, which in zip(mlp_low, early):
        to_group(moves, item, which, first_rows, block_rows - first_rows)
    *halves, vectors, io_parts, up_rest, down_rest = moves.run()
    mlp_sums = [
        mine + jnp.concatenate([jnp.sum(part.astype(f32), 0) for part in parts], 0)
        for mine, *parts in zip(mlp_sums, mlp_first, (up_rest, down_rest))
    ]
    vectors = jnp.sum(vectors.astype(f32), 0).reshape(-1)
    io_slice = jnp.sum(io_parts.astype(f32), 0)
    late_sums = [
        lax.dynamic_slice_in_dim(item, member * group_cols[which], group_cols[which], 1)
        + jnp.sum(half.astype(f32), 0)
        for item, half, which in zip(grads_here, halves, late)
    ]
    modul_all = vectors[: modul_here.size].reshape(-1, ada_cols)
    bias_part = jnp.concatenate([jnp.sum(modul_all, 0), vectors[modul_here.size : flat.size]])
    silu_part = lax.dot_general(
        modul_all, ada_copy.astype(f32), (((1,), (1,)), ((), ())), precision=HIGHEST_PRECISION
    )

    moves = Moves("group_sums", ids)
    moves.vmem = 32 * 2**20
    chains = []
    for item, which in zip(late_sums, late):
        away = -1 if which else 1

        def has_source(which=which):
            return lax.axis_index(PATCHES) // members != (0 if which else MATRICES - 1)

        def is_source(which=which):
            return lax.axis_index(PATCHES) // members != which

        mine = moves.operand(item, pltpu.VMEM)
        total = moves.output(item.shape, f32, pltpu.VMEM)
        arriving, leaving = moves.scratch(item.shape, LOW), moves.scratch(item.shape, LOW)
        chains.append((mine, total, arriving, leaving, away, has_source, is_source))
    chunk = block_rows // CHAIN_CHUNKS
    for part in range(CHAIN_CHUNKS):
        for mine, total, arriving, leaving, away, has_source, is_source in chains:
            place = (pl.ds(part * chunk, chunk),)
            number = moves.move(
                (PATCHES, seq_count, away),
                functools.partial(group_peer, members, MATRICES - away),
                leaving,
                lambda place=place: place,
                arriving,
                lambda place=place: place,
                sends=is_source,
                takes=has_source,
                later=True,
            )

            def add(ref, mine=mine, total=total, arriving=arriving, leaving=leaving, has_source=has_source, place=place):
                def with_arriving():
                    ref(total)[place] = ref(mine)[place] + ref(arriving)[place].astype(f32)

                def alone():
                    ref(total)[place] = ref(mine)[place]

                pl.when(has_source())(with_arriving)
                pl.when(jnp.logical_not(has_source()))(alone)
                ref(leaving)[place] = ref(total)[place].astype(LOW)

            moves.wait_for(number)
            moves.task(add)
            moves.start(number)
    moves.gather(SHARDS, silu_part)
    moves.gather(SHARDS, bias_part[None])
    *late_sums, silu_parts, bias_parts = moves.run()
    late_sums = [widen(item) for item in late_sums]
    grad_group = jnp.where(
        group == late[0],
        late_sums[0],
        jnp.where(group == late[1], late_sums[1], widen(jnp.where(group == early[0], *mlp_sums))),
    )
    grad_silu = jnp.sum(silu_parts, 0)
    grad_cond = jax.vjp(jax.nn.silu, cond_vec)[1](grad_silu)[0]
    grad_table_all = lax.dot_general(select, grad_cond, (((0,), (0,)), ((), ())), precision=HIGHEST_PRECISION)
    grad_table = lax.dynamic_slice_in_dim(grad_table_all, shard * table_cols, table_cols, 1)
    bias_parts = bias_parts[:, 0]
    grad_bias_all = jnp.concatenate([bias_parts[:, :ada_cols].reshape(-1), bias_parts[:, ada_cols:].reshape(-1)])
    grad_bias = lax.dynamic_slice_in_dim(grad_bias_all, shard * biases.shape[0], biases.shape[0])
    silu_rows = lax.dynamic_slice_in_dim(silu_low, seq_index * ada_master.shape[0], ada_master.shape[0], 1)
    grad_ada = lax.dot_general(
        silu_rows.astype(f32), modul_all, (((0,), (0,)), ((), ())), precision=HIGHEST_PRECISION
    )

    io_rows = io_slice.size // most_cols
    outgoing = jnp.concatenate(
        [
            grad_group.astype(LOW).reshape(MATRICES, members, -1, most_cols),
            jnp.broadcast_to(io_slice.astype(LOW).reshape(1, 1, -1, most_cols), (MATRICES, members, io_rows, most_cols)),
        ],
        2,
    )
    by_member = [lax.dynamic_index_in_dim(outgoing, member, 1, False)]
    for shift in range(1, members):
        part = lax.dynamic_index_in_dim(outgoing, lax.rem(member + shift, members), 1, False)
        routes = [(index, index // members * members + (index + shift) % members) for index in range(seq_count)]
        by_member.append(lax.ppermute(part, PATCHES, routes))

    moment_group = jnp.concatenate(moment_halves, 1).reshape(-1, most_cols).astype(f32)
    grad_squares = jnp.sum(grad_group * grad_group)
    squares = (
        grad_squares
        + jnp.sum(grad_ada * grad_ada)
        + jnp.sum(io_slice * io_slice)
        + jnp.sum(grad_pos * grad_pos)
        + (seq_index == 0).astype(f32) * (jnp.sum(grad_table * grad_table) + jnp.sum(grad_bias * grad_bias))
    )
    lane = jnp.arange(LANES, dtype=jnp.int32)
    place = 2 + 3 * group
    entries = jnp.where(lane == 0, squares, 0.0) + jnp.where(lane == 1, loss_local, 0.0)
    entries = entries + jnp.where(lane == place, jnp.sum(moment_group * moment_group), 0.0)
    entries = entries + jnp.where(lane == place + 1, jnp.sum(moment_group * grad_group), 0.0)
    entries = entries + jnp.where(lane == place + 2, grad_squares, 0.0)
    entries, by_member = lax.optimization_barrier((entries, by_member))
    order = lax.rem(member + members - jnp.arange(members, dtype=jnp.int32), members)
    by_member = jnp.take(jnp.stack(by_member), order, axis=0)
    by_group = [lax.dynamic_index_in_dim(by_member, group, 1, False)]
    for shift in range(1, MATRICES):
        part = lax.dynamic_index_in_dim(by_member, lax.rem(group + shift, MATRICES), 1, False)
        routes = [(index, (index + shift * members) % seq_count) for index in range(seq_count)]
        by_group.append(lax.ppermute(part, PATCHES, routes))

    sums = total_of(ids, jnp.broadcast_to(entries[None], (8, LANES)))[0]
    grad_norm = jnp.sqrt(sums[0])
    loss_total = sums[1]
    clip = jnp.minimum(1.0, CLIP_LIMIT / (grad_norm + 1e-06))
    terms = sums[2 : 2 + 3 * MATRICES].reshape(MATRICES, 3)
    size_squares = MOMENTUM * MOMENTUM * terms[:, 0] + 2.0 * MOMENTUM * clip * terms[:, 1] + clip * clip * terms[:, 2]
    sizes = jnp.sqrt(jnp.maximum(size_squares, 0.0))
    moment_sizes = sizes[jnp.array([0, 3, 1, 2])] / CLIP_LIMIT
    my_size = lax.dynamic_slice_in_dim(sizes, group, 1)[0]
    block = ((MOMENTUM * moment_group + clip * grad_group) / (my_size + 1e-07)).astype(LOW)

    moves = Moves("columns", ids, 40 * 2**20)
    source = moves.operand(block)
    target = moves.scratch((members * shards, block_rows, most_cols), LOW)
    gram = moves.output((block_rows, block_rows), f32, pltpu.VMEM)
    pairs = shards // 2

    def slot(back_member, back_pair, part=None):
        who_member = lax.rem(lax.rem(lax.axis_index(PATCHES), members) + members - back_member, members)
        who_shard = lax.rem(lax.axis_index(SHARDS) + shards - 2 * back_pair, shards)
        index = who_member * shards + who_shard
        return (index,) if part is None else (index, pl.ds(part * block_rows // 2, block_rows // 2))

    def add_gram(place):
        def action(ref):
            (index,) = place()

            @pl.loop(0, block_rows // GRAM_ROWS)
            def _(tile):
                rows = pl.ds(pl.multiple_of(tile * GRAM_ROWS, GRAM_ROWS), GRAM_ROWS)
                ref(gram)[rows, :] += contract(ref(target)[index, rows, :], ref(target)[index], 1, 1)

        return action

    def start_gram(ref):
        ref(gram)[...] = jnp.zeros((block_rows, block_rows), f32)

    def pair_peer(shift):
        return {SHARDS: lax.rem(lax.axis_index(SHARDS) + 2 * shift, shards)}

    slot_own = functools.partial(slot, 0, 0)
    own_copy = moves.keep(source, None, target, slot_own)
    by_member = {
        shift: moves.move(
            (PATCHES, members, shift), functools.partial(member_peer, members, shift), source, None, target, slot_own
        )
        for shift in range(1, members)
    }
    by_pair = {
        shift: moves.move((SHARDS, 2 * shift), functools.partial(pair_peer, shift), source, None, target, slot_own)
        for shift in range(1, pairs)
    }
    from_sibling = [(moves.move((SHARDS,), sibling_peer, source, None, target, slot_own), slot_own)]
    moves.task(start_gram)
    moves.wait_local(own_copy)
    moves.task(add_gram(slot_own))

    def sibling_place(place):
        def at():
            (index,) = place()
            return (index + 1 - 2 * lax.rem(index, 2),)

        return at

    def hand_on(place, arrivals):
        if len(arrivals) == 1:
            parts = [(place, arrivals[0])]
        else:
            parts = [(functools.partial(place, part), number) for part, number in enumerate(arrivals)]
        numbers = [
            moves.move((SHARDS,), sibling_peer, target, at, target, at, (number,)) for at, number in parts
        ]
        from_sibling.append((numbers, place))
        moves.task(add_gram(place))

    across = []
    for shift_member, first in by_member.items():
        for shift_pair, second in by_pair.items():
            top = functools.partial(slot, shift_member, 0, 0)
            bottom = functools.partial(slot, 0, shift_pair, 1)
            halves = [
                moves.move(
                    (SHARDS, 2 * shift_pair),
                    functools.partial(pair_peer, shift_pair),
                    target,
                    top,
                    target,
                    top,
                    (first,),
                ),
                moves.move(
                    (PATCHES, members, shift_member),
                    functools.partial(member_peer, members, shift_member),
                    target,
                    bottom,
                    target,
                    bottom,
                    (second,),
                ),
            ]
            across.append((functools.partial(slot, shift_member, shift_pair), halves))
    for shift, number in by_member.items():
        hand_on(functools.partial(slot, shift, 0), [number])
    for shift, number in by_pair.items():
        hand_on(functools.partial(slot, 0, shift), [number])
    moves.wait_for(from_sibling[0][0])
    moves.task(add_gram(sibling_place(slot_own)))
    for place, halves in across:
        hand_on(place, halves)
    for numbers, place in from_sibling[1:]:
        for number in numbers:
            moves.wait_for(number)
        moves.task(add_gram(sibling_place(place)))
    (gram,) = moves.run()
    gram, by_group = lax.optimization_barrier((gram, by_group))
    order = lax.rem(group + MATRICES - jnp.arange(MATRICES, dtype=jnp.int32), MATRICES)
    arrived = jnp.take(jnp.stack(by_group), order, axis=0).reshape(seq_count, -1, most_cols)
    grad_rows = arrived[:, : block_rows // seq_count]
    io_slices = arrived[:, block_rows // seq_count :].astype(f32)
    block = newton_schulz(gram, block)
    block, grad_ada, grad_table, grad_pos, grad_bias, grad_rows, io_slices = lax.optimization_barrier(
        (block, grad_ada, grad_table, grad_pos, grad_bias, grad_rows, io_slices)
    )

    def row_blocks(parts):
        return [
            jnp.concatenate(
                [parts[which * members + part][:, : group_cols[which]] for part in range(members)], -1
            ).astype(f32)
            for which in range(MATRICES)
        ]

    moments = [MOMENTUM * old + clip * grad for old, grad in zip(momenta, row_blocks(grad_rows))]
    moves = Moves("update_rows", ids)
    moves.exchange(PATCHES, block.reshape(seq_count, -1, most_cols))
    fresh = [
        master * (1.0 - RATE_MUON * DECAY_MUON) - RATE_MUON * 0.2 * math.sqrt(master.shape[1] * shards) * rows
        for master, rows in zip(masters, row_blocks(moves.run()[0]))
    ]

    moves = Moves("copies", ids)
    rows = qkv_master.shape[0]

    def row_place(back_group):
        who = lax.axis_index(PATCHES) - back_group * members
        return (pl.ds(pl.multiple_of(who * rows, rows), rows),)

    def has_group(offset):
        place = lax.axis_index(PATCHES) // members + offset
        return jnp.logical_and(place >= 0, place < MATRICES)

    def member_copies(source, source_at, target, target_at, after, there):
        for shift in range(1, members):
            moves.move(
                (PATCHES, members, shift),
                functools.partial(member_peer, members, shift),
                source,
                source_at,
                target,
                target_at,
                after,
                there,
                there,
            )

    places = []
    for item in fresh:
        source = moves.operand(item.astype(LOW))
        target = moves.output((rows * seq_count, item.shape[1]), LOW)
        own = functools.partial(row_place, 0)
        moves.keep(source, None, target, own)
        places.append((source, target, {}))

    def along_line(distance, way, source, target, numbers):
        both = lambda: jnp.logical_and(has_group(way), has_group(-distance * way))
        place = functools.partial(row_place, distance * way)
        numbers[way] = moves.move(
            (PATCHES, seq_count, way),
            functools.partial(group_peer, members, (MATRICES + way) % MATRICES),
            target if distance else source,
            place if distance else None,
            target,
            place,
            (numbers[way],) if distance else (),
            both,
            functools.partial(has_group, -(distance + 1) * way),
        )

    for source, target, numbers in places:
        for way in (1, -1):
            along_line(0, way, source, target, numbers)
    for source, target, numbers in places:
        member_copies(source, None, target, own, (), None)
    for distance in range(1, MATRICES):
        for source, target, numbers in places:
            for way in (1, -1):
                number = numbers[way]
                if distance < MATRICES - 1:
                    along_line(distance, way, source, target, numbers)
                place = functools.partial(row_place, distance * way)
                member_copies(
                    target, place, target, place, (number,), functools.partial(has_group, -distance * way)
                )
    copies = moves.run()

    io_grad = io_slices.reshape(2, padded, io_cols)[:, :values_count]
    ada_res = adam_update(ada_master, ada_first, ada_second, clip * grad_ada, RATE_ADAM)
    io_res = adam_update(io_proj, io_first, io_second, clip * io_grad, RATE_ADAM)
    cond_res = adam_update(cond_table, cond_first, cond_second, clip * grad_table, RATE_TABLE)
    pos_res = adam_update(pos_table, pos_first, pos_second, clip * grad_pos, RATE_TABLE)
    bias_res = adam_update(biases, bias_first, bias_second, clip * grad_bias, RATE_ADAM)
    matrices = []
    for which in (0, 3, 1, 2):
        matrices += [fresh[which], moments[which], copies[which]]
    return (loss_total, grad_norm, moment_sizes, *matrices, *ada_res, *io_res, *cond_res, *pos_res, *bias_res)


def fits_fast(mesh):
    seq, shards = mesh.shape[PATCHES], mesh.shape[SHARDS]
    return HEADS % seq == 0 and (HEADS // seq * HEAD) % LANES == 0 and seq % MATRICES == 0 and shards % 2 == 0


def solution(mesh):
    body = fast_body if fits_fast(mesh) else general_body
    return jax.shard_map(
        body,
        mesh=mesh,
        in_specs=(
            P(SHARDS, PATCHES, None),
            P(SHARDS, PATCHES, None),
            P(SHARDS),
            P(),
            P(None, SHARDS),
            P(PATCHES, SHARDS),
            P(PATCHES, SHARDS),
            P(None, SHARDS),
            P(PATCHES, SHARDS),
            P(PATCHES, SHARDS),
            P(None, SHARDS),
            P(PATCHES, SHARDS),
            P(PATCHES, SHARDS),
            P(None, SHARDS),
            P(PATCHES, SHARDS),
            P(PATCHES, SHARDS),
            P(None, SHARDS),
            P(PATCHES, SHARDS),
            P(PATCHES, SHARDS),
            P(PATCHES, SHARDS),
            P(None, None, SHARDS),
            P(None, None, SHARDS),
            P(None, None, SHARDS),
            P(None, SHARDS),
            P(None, SHARDS),
            P(None, SHARDS),
            P(PATCHES, SHARDS),
            P(PATCHES, SHARDS),
            P(PATCHES, SHARDS),
            P(SHARDS),
            P(SHARDS),
            P(SHARDS),
        ),
        out_specs=(
            P(),
            P(),
            P(),
            P(PATCHES, SHARDS),
            P(PATCHES, SHARDS),
            P(None, SHARDS),
            P(PATCHES, SHARDS),
            P(PATCHES, SHARDS),
            P(None, SHARDS),
            P(PATCHES, SHARDS),
            P(PATCHES, SHARDS),
            P(None, SHARDS),
            P(PATCHES, SHARDS),
            P(PATCHES, SHARDS),
            P(None, SHARDS),
            P(PATCHES, SHARDS),
            P(PATCHES, SHARDS),
            P(PATCHES, SHARDS),
            P(None, None, SHARDS),
            P(None, None, SHARDS),
            P(None, None, SHARDS),
            P(None, SHARDS),
            P(None, SHARDS),
            P(None, SHARDS),
            P(PATCHES, SHARDS),
            P(PATCHES, SHARDS),
            P(PATCHES, SHARDS),
            P(SHARDS),
            P(SHARDS),
            P(SHARDS),
        ),
        check_vma=False,
    )
```

```python
import functools
import math

import jax
import jax.numpy as jnp
from jax import lax
from jax.experimental import pallas as pl
from jax.experimental.pallas import tpu as pltpu
from jax.sharding import PartitionSpec as P

PATCHES = "seq"
SHARDS = "fsdp"
HEADS = 16
HEAD = 64
NI = 3
ROLL = 2
NS_ITERS = 5
STEP_NUM = 10
LON = 32


EPS_NORM = 1e-06
NS_A = 3.4445
NS_B = -4.775
NS_C = 2.0315
MOMENTUM = 0.5
RATE_MUON = 0.15
DECAY_MUON = 0.1
RATE_ADAM = 0.05
RATE_TABLE = 0.5
DECAY_ADAM = 0.1
BETA_FIRST = 0.9
BETA_SECOND = 0.95
CLIP_LIMIT = 0.01
HIGHEST_PRECISION = lax.Precision.HIGHEST


def broadcast(block, axis, owner):
    block = jnp.where(lax.axis_index(axis) == owner, block, jnp.zeros_like(block))
    return lax.psum(block, axis)


def product(left, right):
    return jnp.dot(left, right, preferred_element_type=jnp.float32)


def dot_last(left, right):
    return lax.dot_general(
        left, right, (((left.ndim - 1,), (1,)), ((), ())), preferred_element_type=jnp.float32
    )


def rows_product(left, right):
    flat_left = left.reshape(-1, left.shape[-1])
    flat_right = right.reshape(-1, right.shape[-1])
    return lax.dot_general(
        flat_left, flat_right, (((0,), (0,)), ((), ())), preferred_element_type=jnp.float32
    )


def layer_norm(values):
    centred = values - jnp.mean(values, -1, keepdims=True)
    inverse = lax.rsqrt(jnp.mean(centred * centred, -1, keepdims=True) + EPS_NORM)
    return (centred * inverse, inverse)


def norm_back(grad, normed, inverse):
    return inverse * (
        grad
        - jnp.mean(grad, -1, keepdims=True)
        - normed * jnp.mean(grad * normed, -1, keepdims=True)
    )


def heads_view(values):
    return values.reshape(values.shape[0], values.shape[1], HEADS, HEAD)


def modulation(modul, width):
    return [modul[:, None, column * width : (column + 1) * width] for column in range(6)]


def latitude_weights(local):
    all_patches = local * lax.axis_size(PATCHES)
    band_row = (jnp.arange(all_patches, dtype=jnp.int32) // LON).astype(jnp.float32)
    latitude = (band_row + 0.5) * (math.pi / (all_patches // LON)) - math.pi / 2
    cosine = jnp.cos(latitude)
    weights = cosine / jnp.mean(cosine)
    return lax.dynamic_slice_in_dim(weights, lax.axis_index(PATCHES) * local, local)


def forward_step(weights, state, active, select):
    w_qkv, w_out, w_up, w_down, w_ada, io_all, table, pos, bias = weights
    width = w_out.shape[0]
    cond_vec = jnp.dot(select, table.astype(jnp.float32), precision=HIGHEST_PRECISION)
    silu_low = jax.nn.silu(cond_vec).astype(jnp.bfloat16)
    modul = product(silu_low, w_ada) + bias[: 6 * width].astype(jnp.float32)
    shift1, scale1, gate1, shift2, scale2, gate2 = modulation(modul, width)
    state_low = state.astype(jnp.bfloat16)
    embedded = (
        product(state_low, io_all[0])
        + bias[6 * width :].astype(jnp.float32)
        + pos.astype(jnp.float32)
    )
    normed_one, inverse_one = layer_norm(embedded)
    normed_a = (normed_one * (1.0 + scale1) + shift1).astype(jnp.bfloat16)
    qkv = product(normed_a, w_qkv).astype(jnp.bfloat16)
    queries = qkv[..., :width]
    keys, values = (
        lax.all_gather(qkv[..., width : 2 * width], PATCHES, axis=1, tiled=True),
        lax.all_gather(qkv[..., 2 * width :], PATCHES, axis=1, tiled=True),
    )
    scores = jnp.einsum(
        "sphd,snhd->shpn", heads_view(queries), heads_view(keys), preferred_element_type=jnp.float32
    ) * HEAD ** (-0.5)
    top_score = jnp.max(scores, -1, keepdims=True)
    expo = jnp.exp(scores - top_score)
    total_exp = jnp.sum(expo, -1, keepdims=True)
    log_total = top_score + jnp.log(total_exp)
    probs_low = (expo / total_exp).astype(jnp.bfloat16)
    mixed = jnp.einsum(
        "shpn,snhd->sphd", probs_low, heads_view(values), preferred_element_type=jnp.float32
    )
    mixed_low = mixed.reshape(queries.shape).astype(jnp.bfloat16)
    attended = product(mixed_low, w_out)
    after_attn = embedded + gate1 * attended
    normed_two, inverse_two = layer_norm(after_attn)
    normed_b = (normed_two * (1.0 + scale2) + shift2).astype(jnp.bfloat16)
    upward = product(normed_b, w_up)
    hidden = jax.nn.gelu(upward).astype(jnp.bfloat16)
    downward = dot_last(hidden, w_down)
    after_mlp = after_attn + gate2 * downward
    normed_three, inverse_three = layer_norm(after_mlp)
    normed_c = normed_three.astype(jnp.bfloat16)
    delta = dot_last(normed_c, io_all[1])
    kept = (
        cond_vec,
        silu_low,
        modul,
        state_low,
        normed_one,
        inverse_one,
        normed_a,
        queries,
        keys,
        values,
        log_total,
        mixed_low,
        attended,
        normed_two,
        inverse_two,
        normed_b,
        upward,
        hidden,
        downward,
        normed_three,
        inverse_three,
        normed_c,
    )
    return (state + active * delta, kept)


def backward_step(weights, kept, grad_state, active, select):
    w_qkv, w_out, w_up, w_down, w_ada, io_all, table, pos, bias = weights
    (
        cond_vec,
        silu_low,
        modul,
        state_low,
        normed_one,
        inverse_one,
        normed_a,
        queries,
        keys,
        values,
        log_total,
        mixed_low,
        attended,
        normed_two,
        inverse_two,
        normed_b,
        upward,
        hidden,
        downward,
        normed_three,
        inverse_three,
        normed_c,
    ) = kept
    width = w_out.shape[0]
    shift1, scale1, gate1, shift2, scale2, gate2 = modulation(modul, width)
    delta_grad = (active * grad_state).astype(jnp.bfloat16)
    grad_head = rows_product(delta_grad, normed_c)
    grad_mlp = norm_back(product(delta_grad, io_all[1]), normed_three, inverse_three)
    grad_gate2 = jnp.sum(grad_mlp * downward, 1)
    down_grad = (gate2 * grad_mlp).astype(jnp.bfloat16)
    grad_down = rows_product(down_grad, hidden)
    grad_hidden = product(down_grad, w_down)
    up_grad = jax.vjp(jax.nn.gelu, upward)[1](grad_hidden)[0].astype(jnp.bfloat16)
    grad_up = rows_product(normed_b, up_grad)
    grad_normed_b = dot_last(up_grad, w_up)
    grad_scale2 = jnp.sum(grad_normed_b * normed_two, 1)
    grad_shift2 = jnp.sum(grad_normed_b, 1)
    grad_attn = grad_mlp + norm_back(grad_normed_b * (1.0 + scale2), normed_two, inverse_two)
    grad_gate1 = jnp.sum(grad_attn * attended, 1)
    attn_grad = (gate1 * grad_attn).astype(jnp.bfloat16)
    grad_out = rows_product(mixed_low, attn_grad)
    mixed_grad = dot_last(attn_grad, w_out).astype(jnp.bfloat16)
    q_heads = heads_view(queries)
    k_heads = heads_view(keys)
    v_heads = heads_view(values)
    g_heads = heads_view(mixed_grad)
    scores = jnp.einsum(
        "sphd,snhd->shpn", q_heads, k_heads, preferred_element_type=jnp.float32
    ) * HEAD ** (-0.5)
    probs = jnp.exp(scores - log_total)
    probs_low = probs.astype(jnp.bfloat16)
    grad_probs = jnp.einsum("sphd,snhd->shpn", g_heads, v_heads, preferred_element_type=jnp.float32)
    score_grad = (
        HEAD ** (-0.5) * probs * (grad_probs - jnp.sum(grad_probs * probs, -1, keepdims=True))
    ).astype(jnp.bfloat16)
    grad_queries = jnp.einsum(
        "shpn,snhd->sphd", score_grad, k_heads, preferred_element_type=jnp.float32
    ).reshape(queries.shape)
    key_part = jnp.einsum(
        "shpn,sphd->snhd", score_grad, q_heads, preferred_element_type=jnp.float32
    ).reshape(keys.shape)
    value_part = jnp.einsum(
        "shpn,sphd->snhd", probs_low, g_heads, preferred_element_type=jnp.float32
    ).reshape(values.shape)
    grad_keys, grad_values = (
        lax.psum_scatter(key_part, PATCHES, scatter_dimension=1, tiled=True),
        lax.psum_scatter(value_part, PATCHES, scatter_dimension=1, tiled=True),
    )
    qkv_grad = jnp.concatenate([grad_queries, grad_keys, grad_values], -1).astype(jnp.bfloat16)
    grad_qkv = rows_product(normed_a, qkv_grad)
    grad_normed_a = dot_last(qkv_grad, w_qkv)
    grad_scale1 = jnp.sum(grad_normed_a * normed_one, 1)
    grad_shift1 = jnp.sum(grad_normed_a, 1)
    grad_embedded = grad_attn + norm_back(grad_normed_a * (1.0 + scale1), normed_one, inverse_one)
    embed_grad = grad_embedded.astype(jnp.bfloat16)
    grad_embed = rows_product(state_low, embed_grad)
    grad_prev = grad_state + dot_last(embed_grad, io_all[0])
    grad_modul = jnp.concatenate(
        [grad_shift1, grad_scale1, grad_gate1, grad_shift2, grad_scale2, grad_gate2], -1
    )
    grad_ada = lax.dot_general(
        silu_low.astype(jnp.float32),
        grad_modul,
        (((0,), (0,)), ((), ())),
        precision=HIGHEST_PRECISION,
    )
    grad_silu = lax.dot_general(
        grad_modul, w_ada.astype(jnp.float32), (((1,), (1,)), ((), ())), precision=HIGHEST_PRECISION
    )
    grad_cond = jax.vjp(jax.nn.silu, cond_vec)[1](grad_silu)[0]
    grad_table = lax.dot_general(
        select, grad_cond, (((0,), (0,)), ((), ())), precision=HIGHEST_PRECISION
    )
    grad_bias = jnp.concatenate([jnp.sum(grad_modul, 0), jnp.sum(grad_embedded, (0, 1))])
    grad_pos = jnp.sum(grad_embedded, 0)
    grads = (
        grad_qkv,
        grad_out,
        grad_up,
        grad_down,
        grad_ada,
        jnp.stack([grad_embed, grad_head]),
        grad_table,
        grad_pos,
        grad_bias,
    )
    return (grad_prev, grads)


def gram_part(block_cols):
    return lax.dot_general(
        block_cols, block_cols, (((1,), (1,)), ((), ())), preferred_element_type=jnp.float32
    )


def zero_gram(block_cols):
    return jnp.zeros((block_cols.shape[0], block_cols.shape[0]), jnp.float32)


def newton_step(block_cols, gram):
    gram_low = gram.astype(jnp.bfloat16)
    poly = (NS_B * gram_low.astype(jnp.float32) + NS_C * product(gram_low, gram_low)).astype(
        jnp.bfloat16
    )
    return (NS_A * block_cols.astype(jnp.float32) + product(poly, block_cols)).astype(jnp.bfloat16)


def keep_block(block_cols, gram):
    return block_cols


def adam_update(weight, first, second, grad, rate):
    first_new = BETA_FIRST * first + (1.0 - BETA_FIRST) * grad
    second_new = BETA_SECOND * second + (1.0 - BETA_SECOND) * grad * grad
    unbiased = first_new / (1.0 - BETA_FIRST**STEP_NUM)
    spread = jnp.sqrt(second_new / (1.0 - BETA_SECOND**STEP_NUM)) + 1e-08
    return (weight * (1.0 - rate * DECAY_ADAM) - rate * unbiased / spread, first_new, second_new)


def general_body(
    states,
    targets,
    lengths,
    intervals,
    qkv_copy,
    qkv_master,
    qkv_moment,
    out_copy,
    out_master,
    out_moment,
    up_copy,
    up_master,
    up_moment,
    down_copy,
    down_master,
    down_moment,
    ada_copy,
    ada_master,
    ada_first,
    ada_second,
    io_proj,
    io_first,
    io_second,
    cond_table,
    cond_first,
    cond_second,
    pos_table,
    pos_first,
    pos_second,
    biases,
    bias_first,
    bias_second,
):
    weights = (
        lax.all_gather(qkv_copy, SHARDS, axis=1, tiled=True),
        lax.all_gather(out_copy, SHARDS, axis=1, tiled=True),
        lax.all_gather(up_copy, SHARDS, axis=1, tiled=True),
        lax.all_gather(down_copy, SHARDS, axis=1, tiled=True),
        lax.all_gather(ada_copy, SHARDS, axis=1, tiled=True),
        lax.all_gather(io_proj.astype(jnp.bfloat16), SHARDS, axis=2, tiled=True),
        lax.all_gather(cond_table.astype(jnp.bfloat16), SHARDS, axis=1, tiled=True),
        lax.all_gather(pos_table.astype(jnp.bfloat16), SHARDS, axis=1, tiled=True),
        lax.all_gather(biases.astype(jnp.bfloat16), SHARDS, axis=0, tiled=True),
    )
    samples, local, values_count = states.shape
    table_rows = cond_table.shape[0]
    my_ids = lax.dynamic_slice_in_dim(intervals, lax.axis_index(SHARDS) * samples, samples)
    counts = jnp.sum(
        (intervals[:, None] == jnp.arange(NI, dtype=jnp.int32)[None]).astype(jnp.float32), 0
    )
    id_counts = jnp.sum(
        (my_ids[:, None] == jnp.arange(NI, dtype=jnp.int32)[None]).astype(jnp.float32)
        * counts[None],
        1,
    )
    weight = 1.0 / (NI * local * lax.axis_size(PATCHES) * values_count * id_counts)
    rows_iota = jnp.arange(table_rows, dtype=jnp.int32)
    id_select = (my_ids[:, None] == rows_iota[None]).astype(jnp.float32)
    state = states.astype(jnp.float32)
    seen_states = []
    kept_all = []
    for step in range(ROLL):
        select = id_select + (rows_iota == NI + step).astype(jnp.float32)[None]
        active = (step < lengths).astype(jnp.float32)[:, None, None]
        seen_states.append(state)
        state, kept = forward_step(weights, state, active, select)
        kept_all.append(kept)
    lat = latitude_weights(local)
    diff = state - targets.astype(jnp.float32)
    err = jnp.sum(jnp.sum(diff * diff, -1) * lat[None], -1)
    loss_local = jnp.sum(weight * err)
    grad_state = 2.0 * weight[:, None, None] * lat[None, :, None] * diff
    totals = None
    for step in reversed(range(ROLL)):
        select = id_select + (rows_iota == NI + step).astype(jnp.float32)[None]
        active = (step < lengths).astype(jnp.float32)[:, None, None]
        kept = kept_all[step]
        grad_state, grads = backward_step(weights, kept, grad_state, active, select)
        totals = grads if totals is None else jax.tree.map(jnp.add, totals, grads)
    reduced = (
        lax.psum_scatter(totals[0], SHARDS, scatter_dimension=1, tiled=True),
        lax.psum_scatter(totals[1], SHARDS, scatter_dimension=1, tiled=True),
        lax.psum_scatter(totals[2], SHARDS, scatter_dimension=1, tiled=True),
        lax.psum_scatter(totals[3], SHARDS, scatter_dimension=1, tiled=True),
        lax.psum_scatter(totals[4], SHARDS, scatter_dimension=1, tiled=True),
        lax.psum_scatter(totals[5], SHARDS, scatter_dimension=2, tiled=True),
        lax.psum_scatter(totals[6], SHARDS, scatter_dimension=1, tiled=True),
        lax.psum_scatter(totals[7], SHARDS, scatter_dimension=1, tiled=True),
        lax.psum_scatter(totals[8], SHARDS, scatter_dimension=0, tiled=True),
    )
    large = (
        lax.psum_scatter(reduced[0], PATCHES, scatter_dimension=0, tiled=True),
        lax.psum_scatter(reduced[1], PATCHES, scatter_dimension=0, tiled=True),
        lax.psum_scatter(reduced[2], PATCHES, scatter_dimension=0, tiled=True),
        lax.psum_scatter(reduced[3], PATCHES, scatter_dimension=0, tiled=True),
        lax.psum_scatter(reduced[4], PATCHES, scatter_dimension=0, tiled=True),
    )
    small = lax.psum((reduced[5], reduced[6], reduced[8]), PATCHES)
    grad_pos = reduced[7]
    first_copy = (lax.axis_index(PATCHES) == 0).astype(jnp.float32)
    squares = jnp.sum(grad_pos * grad_pos)
    for item in large:
        squares = squares + jnp.sum(item * item)
    small_squares = jnp.float32(0.0)
    for item in small:
        small_squares = small_squares + jnp.sum(item * item)
    squares, loss_total = lax.psum(
        (squares + first_copy * small_squares, loss_local), (PATCHES, SHARDS)
    )
    grad_norm = jnp.sqrt(squares)
    clip = jnp.minimum(1.0, CLIP_LIMIT / (grad_norm + 1e-06))
    masters = (qkv_master, out_master, up_master, down_master)
    moments = [
        MOMENTUM * old + clip * grad
        for old, grad in zip((qkv_moment, out_moment, up_moment, down_moment), large[:4])
    ]
    norms = lax.psum(
        (
            jnp.sum(moments[0] * moments[0]),
            jnp.sum(moments[1] * moments[1]),
            jnp.sum(moments[2] * moments[2]),
            jnp.sum(moments[3] * moments[3]),
        ),
        (PATCHES, SHARDS),
    )
    sizes = [jnp.sqrt(norms[which]) for which in range(4)]
    moment_sizes = jnp.stack(sizes) / CLIP_LIMIT
    scaled = [(moments[which] / (sizes[which] + 1e-07)).astype(jnp.bfloat16) for which in range(4)]
    columns = (
        lax.all_gather(scaled[0], PATCHES, axis=0, tiled=True),
        lax.all_gather(scaled[1], PATCHES, axis=0, tiled=True),
        lax.all_gather(scaled[2], PATCHES, axis=0, tiled=True),
        lax.all_gather(scaled[3], PATCHES, axis=0, tiled=True),
    )
    seq_index = lax.axis_index(PATCHES)
    seq_count = lax.axis_size(PATCHES)
    owners = [seq_index == which % seq_count for which in range(4)]
    blocks = list(columns)
    for turn in range(NS_ITERS):
        partial_value = [
            lax.cond(owners[which], gram_part, zero_gram, blocks[which]) for which in range(4)
        ]
        grams = lax.psum(
            (partial_value[0], partial_value[1], partial_value[2], partial_value[3]), SHARDS
        )
        blocks = [
            lax.cond(owners[which], newton_step, keep_block, blocks[which], grams[which])
            for which in range(4)
        ]
    blocks = [broadcast(blocks[which], PATCHES, which % seq_count) for which in range(4)]
    row_count = qkv_master.shape[0]
    fresh = []
    for which in range(4):
        my_rows = lax.dynamic_slice_in_dim(
            blocks[which], seq_index * row_count, row_count, 0
        ).astype(jnp.float32)
        all_cols = masters[which].shape[1] * lax.axis_size(SHARDS)
        fresh.append(
            masters[which] * (1.0 - RATE_MUON * DECAY_MUON)
            - RATE_MUON * 0.2 * math.sqrt(all_cols) * my_rows
        )
    copies = (
        lax.all_gather(fresh[0].astype(jnp.bfloat16), PATCHES, axis=0, tiled=True),
        lax.all_gather(fresh[1].astype(jnp.bfloat16), PATCHES, axis=0, tiled=True),
        lax.all_gather(fresh[2].astype(jnp.bfloat16), PATCHES, axis=0, tiled=True),
        lax.all_gather(fresh[3].astype(jnp.bfloat16), PATCHES, axis=0, tiled=True),
    )
    ada_res = adam_update(ada_master, ada_first, ada_second, clip * large[4], RATE_ADAM)
    io_res = adam_update(io_proj, io_first, io_second, clip * small[0], RATE_ADAM)
    cond_res = adam_update(cond_table, cond_first, cond_second, clip * small[1], RATE_TABLE)
    pos_res = adam_update(pos_table, pos_first, pos_second, clip * grad_pos, RATE_TABLE)
    bias_res = adam_update(biases, bias_first, bias_second, clip * small[2], RATE_ADAM)
    return (
        loss_total,
        grad_norm,
        moment_sizes,
        fresh[0],
        moments[0],
        copies[0],
        fresh[1],
        moments[1],
        copies[1],
        fresh[2],
        moments[2],
        copies[2],
        fresh[3],
        moments[3],
        copies[3],
        ada_res[0],
        ada_res[1],
        ada_res[2],
        io_res[0],
        io_res[1],
        io_res[2],
        cond_res[0],
        cond_res[1],
        cond_res[2],
        pos_res[0],
        pos_res[1],
        pos_res[2],
        bias_res[0],
        bias_res[1],
        bias_res[2],
    )


LANES = 128
MATRICES = 4
LOW = jnp.bfloat16
MESH = pl.DeviceIdType.MESH


def round_up(value, unit):
    return -(-value // unit) * unit


def member_peer(members, shift):
    index = lax.axis_index(PATCHES)
    return {PATCHES: index // members * members + lax.rem(lax.rem(index, members) + shift, members)}


def group_peer(members, shift):
    return {PATCHES: lax.rem(lax.axis_index(PATCHES) + shift * members, lax.axis_size(PATCHES))}


def sibling_peer():
    index = lax.axis_index(SHARDS)
    return {SHARDS: index + 1 - 2 * lax.rem(index, 2)}


def where(condition, action):
    if condition is None:
        action()
    else:
        pl.when(condition())(action)


class Moves:
    def __init__(self, name, ids, vmem=None):
        self.name = name
        self.ids = ids
        self.vmem = vmem
        self.operands = []
        self.operand_specs = []
        self.outputs = []
        self.output_specs = []
        self.scratches = []
        self.moves = []
        self.locals = []
        self.steps = []
        self.peers = {}

    def operand(self, array, space=pl.ANY):
        self.operands.append(array)
        self.operand_specs.append(pl.BlockSpec(memory_space=space))
        return (0, len(self.operands) - 1)

    def output(self, shape, dtype, space=pl.ANY):
        self.outputs.append(jax.ShapeDtypeStruct(shape, dtype))
        self.output_specs.append(pl.BlockSpec(memory_space=space))
        return (1, len(self.outputs) - 1)

    def scratch(self, shape, dtype):
        self.scratches.append(pltpu.VMEM(shape, dtype))
        return (2, len(self.scratches) - 1)

    def keep(self, source, source_at, target, target_at):
        self.locals.append((source, source_at, target, target_at))
        return len(self.locals) - 1

    def move(
        self, peer_key, peer, source, source_at, target, target_at, after=(), sends=None, takes=None, later=False
    ):
        number = len(self.moves)
        self.peers.setdefault(peer_key, peer)
        self.moves.append((peer_key, source, source_at, target, target_at, sends, takes, later or bool(after)))
        for earlier in after:
            self.steps.append((self.await_move, earlier))
        if after:
            self.steps.append((self.start_move, number))
        return number

    def wait_for(self, number):
        self.steps.append((self.await_move, number))

    def start(self, number):
        self.steps.append((self.start_move, number))

    def wait_local(self, number):
        self.steps.append((self.await_local, number))

    def task(self, action):
        self.steps.append((self.do_task, action))

    def await_move(self, number):
        if number not in self.arrived:
            self.arrived.add(number)
            where(self.moves[number][6], self.remote[number].wait_recv)

    def start_move(self, number):
        where(self.moves[number][5], self.remote[number].start)

    def await_local(self, number):
        if number not in self.kept:
            self.kept.add(number)
            self.local[number].wait()

    def do_task(self, action):
        action(self.ref)

    def ref(self, which):
        return self.refs[which[0]][which[1]]

    def view(self, which, index):
        ref = self.ref(which)
        return ref.at[index()] if index is not None else ref

    def kernel(self, *refs):
        sizes = (len(self.operands), len(self.outputs), len(self.scratches))
        self.refs = (refs[: sizes[0]], refs[sizes[0] : sizes[0] + sizes[1]], refs[sizes[0] + sizes[1] : sum(sizes)])
        local_sem, send_sem, recv_sem = refs[sum(sizes) :]
        self.arrived, self.kept = set(), set()
        devices = {key: peer() for key, peer in self.peers.items()}
        barrier = pltpu.get_barrier_semaphore()
        for device in devices.values():
            pl.semaphore_signal(barrier, inc=1, device_id=device, device_id_type=MESH)
        pl.semaphore_wait(barrier, len(devices))
        self.remote = []
        for number, (key, source, source_at, target, target_at, _, _, later) in enumerate(self.moves):
            self.remote.append(
                pltpu.make_async_remote_copy(
                    src_ref=self.view(source, source_at),
                    dst_ref=self.view(target, target_at),
                    send_sem=send_sem.at[number],
                    recv_sem=recv_sem.at[number],
                    device_id=devices[key],
                    device_id_type=MESH,
                )
            )
            if not later:
                self.start_move(number)
        self.local = [
            pltpu.make_async_copy(self.view(source, source_at), self.view(target, target_at), local_sem.at[number])
            for number, (source, source_at, target, target_at) in enumerate(self.locals)
        ]
        for copy in self.local:
            copy.start()
        for action, number in self.steps:
            action(number)
        for number in range(len(self.locals)):
            self.await_local(number)
        for number, copy in enumerate(self.remote):
            self.await_move(number)
            where(self.moves[number][5], copy.wait_send)

    def run(self):
        return pl.pallas_call(
            self.kernel,
            out_shape=self.outputs,
            in_specs=self.operand_specs,
            out_specs=self.output_specs,
            scratch_shapes=[
                *self.scratches,
                pltpu.SemaphoreType.DMA((max(1, len(self.locals)),)),
                pltpu.SemaphoreType.DMA((len(self.moves),)),
                pltpu.SemaphoreType.DMA((len(self.moves),)),
            ],
            compiler_params=pltpu.CompilerParams(
                collective_id=self.ids.setdefault(self.name, len(self.ids)),
                has_side_effects=True,
                vmem_limit_bytes=self.vmem,
            ),
            name=self.name,
        )(*self.operands)

    def along(self, axis, source, target, pairs):
        count = lax.axis_size(axis)

        def other(shift):
            return lax.rem(lax.axis_index(axis) + shift, count)

        for shift in range(1, count):
            for source_at, target_at in pairs:
                self.move(
                    (axis, shift),
                    lambda shift=shift: {axis: other(shift)},
                    source,
                    None if source_at is None else (lambda at=source_at, shift=shift: at(other(shift))),
                    target,
                    lambda at=target_at: at(lax.axis_index(axis)),
                )
        for source_at, target_at in pairs:
            self.keep(
                source,
                None if source_at is None else (lambda at=source_at: at(lax.axis_index(axis))),
                target,
                lambda at=target_at: at(lax.axis_index(axis)),
            )

    def gather(self, axis, array):
        target = self.output((lax.axis_size(axis),) + array.shape, array.dtype)
        self.along(axis, self.operand(array), target, [(None, lambda sender: (sender,))])

    def gather_pairs(self, array, parts=1):
        shards = lax.axis_size(SHARDS)
        source = self.operand(array)
        target = self.output((shards,) + array.shape, array.dtype)
        rows = array.shape[0] // parts

        def place(back_pair, part):
            return (lax.rem(lax.axis_index(SHARDS) + shards - 2 * back_pair, shards), pl.ds(part * rows, rows))

        firsts = []
        for part in range(parts):
            for pair in range(1, shards // 2):
                number = self.move(
                    (SHARDS, 2 * pair),
                    lambda pair=pair: {SHARDS: lax.rem(lax.axis_index(SHARDS) + 2 * pair, shards)},
                    source,
                    lambda part=part: (pl.ds(part * rows, rows),),
                    target,
                    functools.partial(place, 0, part),
                )
                firsts.append((functools.partial(place, pair, part), number))
        own = lambda: (lax.axis_index(SHARDS),)
        self.move((SHARDS,), sibling_peer, source, None, target, own)
        self.keep(source, None, target, own)
        self.to_sibling([(target, at, number) for at, number in firsts])

    def gather_columns(self, axis, array):
        width = array.shape[-1]
        target = self.output(array.shape[:-1] + (lax.axis_size(axis) * width,), array.dtype)
        lead = (slice(None),) * (array.ndim - 1)
        self.along(
            axis,
            self.operand(array),
            target,
            [(None, lambda sender: lead + (pl.ds(pl.multiple_of(sender * width, LANES), width),))],
        )

    def gather_twice(self, arrays, members):
        shards = lax.axis_size(SHARDS)
        entries = []
        for array in arrays:
            source = self.operand(array)
            width = array.shape[1]
            target = self.output((array.shape[0], shards * width), array.dtype)
            rows = array.shape[0] // members

            def columns(back_pair, width=width):
                who = lax.rem(lax.axis_index(SHARDS) + shards - 2 * back_pair, shards)
                return pl.ds(pl.multiple_of(who * width, LANES), width)

            def place(back_member, back_pair, rows=rows, columns=columns):
                index = lax.rem(lax.rem(lax.axis_index(PATCHES), members) + members - back_member, members)
                return (pl.ds(pl.multiple_of(index * rows, rows), rows), columns(back_pair))

            def mine(rows=rows):
                index = lax.rem(lax.axis_index(PATCHES), members)
                return (pl.ds(pl.multiple_of(index * rows, rows), rows),)

            firsts = [
                self.move(
                    (SHARDS, 2 * pair),
                    lambda pair=pair: {SHARDS: lax.rem(lax.axis_index(SHARDS) + 2 * pair, shards)},
                    source,
                    mine,
                    target,
                    functools.partial(place, 0, 0),
                )
                for pair in range(1, shards // 2)
            ]
            entries.append((source, target, place, firsts))
            self.move((SHARDS,), sibling_peer, source, None, target, lambda columns=columns: (slice(None), columns(0)))
        last = []
        for _, target, place, firsts in entries:
            for pair, first in enumerate(firsts, 1):
                near = functools.partial(place, 0, pair)
                for shift in range(1, members):
                    number = self.move(
                        (PATCHES, members, shift),
                        functools.partial(member_peer, members, shift),
                        target,
                        near,
                        target,
                        near,
                        (first,),
                    )
                    last.append((target, functools.partial(place, shift, pair), number))
                self.move((SHARDS,), sibling_peer, target, near, target, near, (first,))
        self.to_sibling(last)

    def to_sibling(self, waiting):
        for target, place, number in waiting:
            self.move((SHARDS,), sibling_peer, target, place, target, place, (number,))

    def exchange(self, axis, array):
        target = self.output(array.shape, array.dtype)
        self.along(axis, self.operand(array), target, [(lambda receiver: (receiver,), lambda sender: (sender,))])

    def exchange_columns(self, axis, array):
        width = array.shape[-1] // lax.axis_size(axis)
        target = self.output((lax.axis_size(axis), array.shape[0], width), array.dtype)
        self.along(
            axis,
            self.operand(array),
            target,
            [
                (
                    lambda receiver: (slice(None), pl.ds(pl.multiple_of(receiver * width, LANES), width)),
                    lambda sender: (sender,),
                )
            ],
        )

    def rows_to_heads(self, axis, array, planes):
        count, rows = lax.axis_size(axis), array.shape[0]
        columns = array.shape[1] // planes
        width = columns // count
        target = self.output((planes, rows * count, width), array.dtype)
        self.along(
            axis,
            self.operand(array),
            target,
            [
                (
                    lambda receiver, plane=plane: (
                        slice(None),
                        pl.ds(pl.multiple_of(plane * columns + receiver * width, LANES), width),
                    ),
                    lambda sender, plane=plane: (plane, pl.ds(pl.multiple_of(sender * rows, rows), rows)),
                )
                for plane in range(planes)
            ],
        )

    def heads_to_rows(self, axis, array):
        count = lax.axis_size(axis)
        planes, all_rows, width = array.shape
        rows, columns = all_rows // count, width * count
        target = self.output((rows, planes * columns), array.dtype)
        self.along(
            axis,
            self.operand(array),
            target,
            [
                (
                    lambda receiver, plane=plane: (plane, pl.ds(pl.multiple_of(receiver * rows, rows), rows)),
                    lambda sender, plane=plane: (
                        slice(None),
                        pl.ds(pl.multiple_of(plane * columns + sender * width, LANES), width),
                    ),
                )
                for plane in range(planes)
            ],
        )


def total_kernel(x_ref, o_ref, near, far, near_send, near_recv, far_send, far_recv):
    near_count, far_count = near.shape[0], far.shape[0]
    near_me, far_me = lax.axis_index(SHARDS), lax.axis_index(PATCHES)
    barrier = pltpu.get_barrier_semaphore()
    for shift in range(1, near_count):
        pl.semaphore_signal(
            barrier, inc=1, device_id={SHARDS: lax.rem(near_me + shift, near_count)}, device_id_type=MESH
        )
    for shift in range(1, far_count):
        pl.semaphore_signal(
            barrier, inc=1, device_id={PATCHES: lax.rem(far_me + shift, far_count)}, device_id_type=MESH
        )
    pl.semaphore_wait(barrier, near_count + far_count - 2)

    def spread(axis, me, count, buffer, send, recv):
        copies = []
        for shift in range(1, count):
            copy = pltpu.make_async_remote_copy(
                src_ref=buffer.at[me],
                dst_ref=buffer.at[me],
                send_sem=send.at[shift - 1],
                recv_sem=recv.at[shift - 1],
                device_id={axis: lax.rem(me + shift, count)},
                device_id_type=MESH,
            )
            copy.start()
            copies.append(copy)
        for copy in copies:
            copy.wait()
        return jnp.sum(buffer[...], 0)

    near[near_me] = x_ref[...]
    far[far_me] = spread(SHARDS, near_me, near_count, near, near_send, near_recv)
    o_ref[...] = spread(PATCHES, far_me, far_count, far, far_send, far_recv)


def total_of(ids, values):
    near_count, far_count = lax.axis_size(SHARDS), lax.axis_size(PATCHES)
    in_vmem = pl.BlockSpec(memory_space=pltpu.VMEM)
    return pl.pallas_call(
        total_kernel,
        out_shape=jax.ShapeDtypeStruct(values.shape, values.dtype),
        in_specs=[in_vmem],
        out_specs=in_vmem,
        scratch_shapes=[
            pltpu.VMEM((near_count,) + values.shape, values.dtype),
            pltpu.VMEM((far_count,) + values.shape, values.dtype),
            pltpu.SemaphoreType.DMA((near_count - 1,)),
            pltpu.SemaphoreType.DMA((near_count - 1,)),
            pltpu.SemaphoreType.DMA((far_count - 1,)),
            pltpu.SemaphoreType.DMA((far_count - 1,)),
        ],
        compiler_params=pltpu.CompilerParams(
            collective_id=ids.setdefault("total", len(ids)), has_side_effects=True
        ),
        name="total",
    )(values)


def contract(left, right, left_dim, right_dim):
    return lax.dot_general(
        left, right, (((left_dim,), (right_dim,)), ((), ())), preferred_element_type=jnp.float32
    )


QUERY_BLOCK = 256
CHAIN_CHUNKS = 8
GRAM_ROWS = 256


def attention_kernel(heads, qkv_ref, mixed_ref):
    rows = pl.ds(pl.multiple_of(pl.program_id(0) * QUERY_BLOCK, QUERY_BLOCK), QUERY_BLOCK)
    mixed = []
    for head in range(heads):
        lanes = pl.ds(head * HEAD, HEAD)
        queries, keys, values = qkv_ref[0, rows, lanes], qkv_ref[1, :, lanes], qkv_ref[2, :, lanes]
        scores = contract(queries, keys, 1, 1) * HEAD ** (-0.5)
        expo = jnp.exp(scores - jnp.max(scores, -1, keepdims=True))
        probs = (expo / jnp.sum(expo, -1, keepdims=True)).astype(LOW)
        mixed.append(contract(probs, values, 1, 0))
    mixed_ref[...] = jnp.concatenate(mixed, -1).astype(LOW)


def attention(qkv):
    _, patches, width = qkv.shape
    return pl.pallas_call(
        functools.partial(attention_kernel, width // HEAD),
        out_shape=jax.ShapeDtypeStruct((patches, width), LOW),
        grid=(patches // QUERY_BLOCK,),
        in_specs=[pl.BlockSpec(qkv.shape, lambda block: (0, 0, 0))],
        out_specs=pl.BlockSpec((QUERY_BLOCK, width), lambda block: (block, 0)),
        compiler_params=pltpu.CompilerParams(vmem_limit_bytes=48 * 2**20),
        name="attention",
    )(qkv)


def attention_back_kernel(heads, qkv_ref, grad_ref, out_ref, key_total, value_total):
    block = pl.program_id(0)
    rows = pl.ds(pl.multiple_of(block * QUERY_BLOCK, QUERY_BLOCK), QUERY_BLOCK)

    @pl.when(block == 0)
    def _():
        key_total[...] = jnp.zeros_like(key_total)
        value_total[...] = jnp.zeros_like(value_total)

    query_parts = []
    for head in range(heads):
        lanes = pl.ds(head * HEAD, HEAD)
        queries, keys, values = qkv_ref[0, rows, lanes], qkv_ref[1, :, lanes], qkv_ref[2, :, lanes]
        grads = grad_ref[rows, lanes]
        scores = contract(keys, queries, 1, 1) * HEAD ** (-0.5)
        expo = jnp.exp(scores - jnp.max(scores, 0, keepdims=True))
        probs = expo / jnp.sum(expo, 0, keepdims=True)
        grad_probs = contract(values, grads, 1, 1)
        shared = jnp.sum(grad_probs * probs, 0, keepdims=True)
        score_grad = (HEAD ** (-0.5) * probs * (grad_probs - shared)).astype(LOW)
        query_parts.append(contract(score_grad, keys, 0, 0))
        key_total[head] += contract(score_grad, queries, 1, 0)
        value_total[head] += contract(probs.astype(LOW), grads, 1, 0)
    out_ref[0, rows, :] = jnp.concatenate(query_parts, -1).astype(LOW)

    @pl.when(block == pl.num_programs(0) - 1)
    def _():
        out_ref[1] = jnp.concatenate([key_total[head] for head in range(heads)], -1).astype(LOW)
        out_ref[2] = jnp.concatenate([value_total[head] for head in range(heads)], -1).astype(LOW)


def attention_back(qkv, grads):
    _, patches, width = qkv.shape
    heads = width // HEAD
    return pl.pallas_call(
        functools.partial(attention_back_kernel, heads),
        out_shape=jax.ShapeDtypeStruct(qkv.shape, LOW),
        grid=(patches // QUERY_BLOCK,),
        in_specs=[
            pl.BlockSpec(qkv.shape, lambda block: (0, 0, 0)),
            pl.BlockSpec(grads.shape, lambda block: (0, 0)),
        ],
        out_specs=pl.BlockSpec(qkv.shape, lambda block: (0, 0, 0)),
        scratch_shapes=[
            pltpu.VMEM((heads, patches, HEAD), jnp.float32),
            pltpu.VMEM((heads, patches, HEAD), jnp.float32),
        ],
        compiler_params=pltpu.CompilerParams(vmem_limit_bytes=48 * 2**20),
        name="attention_back",
    )(qkv, grads)


def newton_kernel(gram_ref, block_ref, out_ref, gram, poly, once, gram_low, poly_low, once_low, block):
    size = gram_ref.shape[0]
    tiles = size // GRAM_ROWS
    eye = jnp.equal(
        lax.broadcasted_iota(jnp.int32, (GRAM_ROWS, GRAM_ROWS), 0),
        lax.broadcasted_iota(jnp.int32, (GRAM_ROWS, GRAM_ROWS), 1),
    ).astype(jnp.float32)

    def rows_at(tile):
        return pl.ds(pl.multiple_of(tile * GRAM_ROWS, GRAM_ROWS), GRAM_ROWS)

    def over_tiles(action):
        return lax.fori_loop(0, tiles, lambda tile, total: total + action(rows_at(tile)), jnp.float32(0.0))

    def store(full, low, rows, value, mean, excess):
        full[rows, :] = value
        low[rows, :] = value.astype(LOW)
        corner = full[rows, rows] - excess * eye
        full[rows, rows] = corner
        low[rows, rows] = (corner - mean * eye).astype(LOW)

    def advance(gram_mean, gram_squares, last):
        poly_mean = NS_B * gram_mean + NS_C * gram_squares / size

        def poly_rows(rows):
            own = gram[rows, :]
            value = contract(gram_low[rows, :], gram_low[...], 1, 0)
            value = NS_C * value + (NS_B + 2.0 * NS_C * gram_mean) * own
            store(poly, poly_low, rows, value, poly_mean, NS_C * gram_mean * gram_mean)
            return jnp.sum(value * own)

        poly_gram = over_tiles(poly_rows) - NS_C * gram_mean * gram_mean * gram_mean * size
        once_mean = poly_gram / size
        out_ref[...] = block[...]

        def block_rows(rows):
            left = poly_low[rows, :]
            value = contract(left, out_ref[...], 1, 0)
            block[rows, :] = (value + (NS_A + poly_mean) * out_ref[rows, :].astype(jnp.float32)).astype(LOW)
            if last:
                return jnp.float32(0.0)
            value = contract(left, gram_low[...], 1, 0)
            own = poly[rows, :]
            value = value + poly_mean * gram[rows, :] + gram_mean * own
            store(once, once_low, rows, value, once_mean, poly_mean * gram_mean)
            return jnp.sum(value * own)

        poly_once = over_tiles(block_rows) - poly_mean * gram_mean * poly_mean * size
        if last:
            return None
        mean_next = NS_A * NS_A * gram_mean + 2.0 * NS_A * once_mean + poly_once / size

        def gram_rows(rows):
            value = contract(poly_low[rows, :], once_low[...], 1, 0)
            value = value + (2.0 * NS_A + poly_mean) * once[rows, :] + once_mean * poly[rows, :]
            value = value + NS_A * NS_A * gram[rows, :]
            store(gram, gram_low, rows, value, mean_next, poly_mean * once_mean)
            return jnp.sum(value * value)

        excess = poly_mean * once_mean
        return mean_next, over_tiles(gram_rows) - excess * (2.0 * mean_next + excess) * size

    block[...] = block_ref[...]
    mean = over_tiles(lambda rows: jnp.sum(gram_ref[rows, rows] * eye)) / size

    def start(rows):
        value = gram_ref[rows, :]
        store(gram, gram_low, rows, value, mean, 0.0)
        return jnp.sum(value * value)

    state = lax.fori_loop(0, NS_ITERS - 1, lambda turn, state: advance(*state, False), (mean, over_tiles(start)))
    advance(*state, True)
    out_ref[...] = block[...]


def newton_schulz(gram, block):
    in_vmem = pl.BlockSpec(memory_space=pltpu.VMEM)
    full, low = pltpu.VMEM(gram.shape, jnp.float32), pltpu.VMEM(gram.shape, LOW)
    return pl.pallas_call(
        newton_kernel,
        out_shape=jax.ShapeDtypeStruct(block.shape, block.dtype),
        in_specs=[in_vmem, in_vmem],
        out_specs=in_vmem,
        scratch_shapes=[full, full, full, low, low, low, pltpu.VMEM(block.shape, LOW)],
        compiler_params=pltpu.CompilerParams(vmem_limit_bytes=48 * 2**20),
        name="newton",
    )(gram, block)


def fast_body(
    states,
    targets,
    lengths,
    intervals,
    qkv_copy,
    qkv_master,
    qkv_moment,
    out_copy,
    out_master,
    out_moment,
    up_copy,
    up_master,
    up_moment,
    down_copy,
    down_master,
    down_moment,
    ada_copy,
    ada_master,
    ada_first,
    ada_second,
    io_proj,
    io_first,
    io_second,
    cond_table,
    cond_first,
    cond_second,
    pos_table,
    pos_first,
    pos_second,
    biases,
    bias_first,
    bias_second,
):
    ids = {}
    f32 = jnp.float32
    seq_count, shards = lax.axis_size(PATCHES), lax.axis_size(SHARDS)
    seq_index, shard = lax.axis_index(PATCHES), lax.axis_index(SHARDS)
    members = seq_count // MATRICES
    group, member = seq_index // members, lax.rem(seq_index, members)
    samples, local, values_count = states.shape
    table_rows, table_cols = cond_table.shape
    width = table_cols * shards
    ada_cols = ada_copy.shape[1]
    padded = round_up(values_count, LANES)

    moves = Moves("tables", ids)
    moves.gather(SHARDS, cond_table)
    moves.gather(SHARDS, biases[None])
    table_parts, bias_parts = moves.run()
    table = jnp.moveaxis(table_parts, 0, 1).reshape(table_rows, width).astype(LOW).astype(f32)
    bias = bias_parts.reshape(-1).astype(LOW).astype(f32)
    rows_iota = jnp.arange(table_rows, dtype=jnp.int32)
    id_rows = (intervals[:, None] == rows_iota[None]).astype(f32)
    step_rows = (rows_iota[None] == NI + jnp.arange(ROLL, dtype=jnp.int32)[:, None]).astype(f32)
    select = (id_rows[:, None] + step_rows[None]).reshape(-1, table_rows)
    cond_vec = jnp.sum(select[:, :, None] * table[None], 1)
    silu_low = jax.nn.silu(cond_vec).astype(LOW)
    modul_shard = product(silu_low, ada_copy) + lax.dynamic_slice_in_dim(bias, shard * ada_cols, ada_cols)[None]

    moves = Moves("weights", ids)
    moves.exchange(SHARDS, modul_shard.reshape(shards, ROLL, ada_cols))
    moves.gather_columns(SHARDS, pos_table.astype(LOW))
    io_low = jnp.pad(io_proj.astype(LOW), ((0, 0), (0, padded - values_count), (0, 0)))
    own_parts = (io_low.reshape(2 * padded, -1), out_copy, qkv_copy)
    moves.gather_twice(own_parts, members)
    modul, pos, *parts = moves.run()
    io_all, w_out, w_qkv = [
        lax.dynamic_update_slice_in_dim(part, own, shard * own.shape[1], 1) for part, own in zip(parts, own_parts)
    ]
    io_all = io_all.reshape(2, padded, width)
    modul = jnp.moveaxis(modul, 0, 1).reshape(ROLL, 6 * width)
    pos = pos.astype(f32)

    masters = (qkv_master, up_master, down_master, out_master)
    momenta = (qkv_moment, up_moment, down_moment, out_moment)
    group_cols = [item.shape[1] // members for item in momenta]
    most_cols = max(group_cols)

    def widen(item):
        return jnp.pad(item, ((0, 0), (0, most_cols - item.shape[1])))

    moment_parts = jnp.stack(
        [
            widen(item[:, part * cols : (part + 1) * cols].astype(LOW))
            for item, cols in zip(momenta, group_cols)
            for part in range(members)
        ]
    )
    half_rows = moment_parts.shape[1] // 2

    counts = jnp.sum((intervals[:, None] == jnp.arange(NI, dtype=jnp.int32)[None]).astype(f32), 0)
    my_id = lax.dynamic_slice_in_dim(intervals, shard, 1)
    id_count = jnp.sum((my_id == jnp.arange(NI, dtype=jnp.int32)).astype(f32) * counts)
    weight = 1.0 / (NI * local * seq_count * values_count * id_count)
    length = lengths[0]
    value_pad = ((0, 0), (0, padded - values_count))
    state = jnp.pad(states[0].astype(f32), value_pad)
    embed_bias = bias[6 * width :]
    kept = []
    gathered = {}
    moment_halves = []

    def run_with(moves, names):
        results = moves.run()
        first = len(results) - len(names)
        for name, result in zip(names, results[first:]):
            gathered.setdefault(name, {})[step] = result
        return results[:first]

    for step in range(ROLL):
        shift1, scale1, gate1, shift2, scale2, gate2 = jnp.split(modul[step][None], 6, -1)
        state_low = state.astype(LOW)
        embedded = product(state_low, io_all[0]) + embed_bias + pos
        normed_one, inverse_one = layer_norm(embedded)
        normed_a = (normed_one * (1.0 + scale1) + shift1).astype(LOW)
        qkv_rows = product(normed_a, w_qkv).astype(LOW)
        moves = Moves(f"heads{step}", ids)
        moves.rows_to_heads(PATCHES, qkv_rows, 3)
        moves.gather_pairs(normed_a)
        if step:
            moves.gather_pairs(kept[-1][5])
            qkv, gathered_a, gathered_mixed = moves.run()
            gathered["mixed"] = {step - 1: gathered_mixed}
        else:
            qkv, gathered_a = moves.run()
        gathered.setdefault("a", {})[step] = gathered_a
        mixed_heads = attention(qkv)
        moves = Moves("mixed_rows", ids)
        moves.heads_to_rows(PATCHES, mixed_heads[None])
        moves.gather_pairs(state_low)
        (mixed,) = run_with(moves, ["state"])
        attended = product(mixed, w_out)
        after_attn = embedded + gate1 * attended
        normed_two, inverse_two = layer_norm(after_attn)
        normed_b = (normed_two * (1.0 + scale2) + shift2).astype(LOW)
        moves = Moves("tokens_moment", ids)
        moves.gather_pairs(normed_b, 2)
        moves.exchange(PATCHES, moment_parts[:, step * half_rows : (step + 1) * half_rows])
        tokens_b, moment_half = moves.run()
        moment_halves.append(moment_half)
        tokens_b = tokens_b.reshape(shards * local, width)
        upward = product(tokens_b, up_copy)
        hidden = jax.nn.gelu(upward).astype(LOW)
        down_part = contract(hidden, down_copy, 1, 1).astype(LOW).reshape(shards, local, width)
        moves = Moves("token_sums", ids)
        moves.exchange(SHARDS, down_part)
        downward = jnp.sum(moves.run()[0].astype(f32), 0)
        after_mlp = after_attn + gate2 * downward
        normed_three, inverse_three = layer_norm(after_mlp)
        normed_c = normed_three.astype(LOW)
        delta = contract(normed_c, io_all[1], 1, 1)
        kept.append(
            (
                state_low,
                normed_one,
                inverse_one,
                normed_a,
                qkv,
                mixed,
                attended,
                normed_two,
                inverse_two,
                tokens_b,
                upward,
                hidden,
                downward,
                normed_three,
                inverse_three,
                normed_c,
            )
        )
        state = state + (step < length).astype(f32) * delta

    lat = latitude_weights(local)
    diff = state - jnp.pad(targets[0].astype(f32), value_pad)
    loss_local = weight * jnp.sum(jnp.sum(diff * diff, -1) * lat)
    grad_state = 2.0 * weight * lat[:, None] * diff

    back = [None] * ROLL
    mlp_back = []

    def patch_sum(item, cols):
        mine = lax.dynamic_slice_in_dim(item, member * cols, cols, 1)
        low = item.astype(LOW)
        for shift in range(1, members):
            pairs = [
                (index, index // members * members + (index + shift) % members) for index in range(seq_count)
            ]
            to_member = lax.rem(member + shift, members)
            outgoing = lax.dynamic_slice_in_dim(low, to_member * cols, cols, 1)
            mine = mine + lax.ppermute(outgoing, PATCHES, pairs).astype(f32)
        return mine

    for step in reversed(range(ROLL)):
        (
            state_low,
            normed_one,
            inverse_one,
            normed_a,
            qkv,
            mixed,
            attended,
            normed_two,
            inverse_two,
            tokens_b,
            upward,
            hidden,
            downward,
            normed_three,
            inverse_three,
            normed_c,
        ) = kept[step]
        shift1, scale1, gate1, shift2, scale2, gate2 = jnp.split(modul[step][None], 6, -1)
        delta_grad = ((step < length).astype(f32) * grad_state).astype(LOW)
        grad_mlp = norm_back(product(delta_grad, io_all[1]), normed_three, inverse_three)
        grad_gate2 = jnp.sum(grad_mlp * downward, 0)
        moves = Moves("tokens", ids)
        moves.gather_pairs((gate2 * grad_mlp).astype(LOW), 2)
        tokens_down = moves.run()[0].reshape(shards * local, width)
        grad_hidden = product(tokens_down, down_copy)
        up_grad = jax.vjp(jax.nn.gelu, upward)[1](grad_hidden)[0].astype(LOW)
        mlp_back.append((tokens_b, up_grad, tokens_down, hidden))
        if step == 0:
            all_b, all_up, all_down, all_hidden = [jnp.concatenate(items, 0) for items in zip(*mlp_back)]
            mlp_sums = [
                patch_sum(rows_product(left, right), cols)
                for left, right, cols in ((all_b, all_up, group_cols[1]), (all_down, all_hidden, group_cols[2]))
            ]
        up_part = contract(up_grad, up_copy, 1, 1).astype(LOW).reshape(shards, local, width)
        moves = Moves("token_sums", ids)
        moves.exchange(SHARDS, up_part)
        grad_normed_b = jnp.sum(moves.run()[0].astype(f32), 0)
        grad_scale2 = jnp.sum(grad_normed_b * normed_two, 0)
        grad_shift2 = jnp.sum(grad_normed_b, 0)
        grad_attn = grad_mlp + norm_back(grad_normed_b * (1.0 + scale2), normed_two, inverse_two)
        grad_gate1 = jnp.sum(grad_attn * attended, 0)
        attn_grad = (gate1 * grad_attn).astype(LOW)
        mixed_grad = contract(attn_grad, w_out, 1, 1).astype(LOW)
        moves = Moves(f"mixed_heads{step}", ids)
        moves.rows_to_heads(PATCHES, mixed_grad, 1)
        if step < ROLL - 1:
            moves.exchange_columns(SHARDS, back[step + 1][0])
            moves.exchange_columns(SHARDS, back[step + 1][1])
            mixed_grad_heads, gathered_qkv, gathered_embed = moves.run()
            gathered.setdefault("qkv", {})[step + 1] = gathered_qkv
            gathered.setdefault("embed", {})[step + 1] = gathered_embed
        else:
            (mixed_grad_heads,) = moves.run()
        qkv_grad_heads = attention_back(qkv, mixed_grad_heads[0])
        moves = Moves(f"rows{step}", ids)
        moves.heads_to_rows(PATCHES, qkv_grad_heads)
        moves.exchange_columns(SHARDS, attn_grad)
        moves.exchange_columns(SHARDS, normed_c)
        moves.gather_pairs(delta_grad)
        names = ["attn", "c", "delta"]
        if step == ROLL - 1:
            moves.gather_pairs(mixed)
            names.append("mixed")
        (qkv_grad,) = run_with(moves, names)
        grad_normed_a = contract(qkv_grad, w_qkv, 1, 1)
        grad_scale1 = jnp.sum(grad_normed_a * normed_one, 0)
        grad_shift1 = jnp.sum(grad_normed_a, 0)
        grad_embedded = grad_attn + norm_back(grad_normed_a * (1.0 + scale1), normed_one, inverse_one)
        embed_grad = grad_embedded.astype(LOW)
        grad_state = grad_state + contract(embed_grad, io_all[0], 1, 1)
        grad_modul = jnp.concatenate([grad_shift1, grad_scale1, grad_gate1, grad_shift2, grad_scale2, grad_gate2])
        back[step] = (qkv_grad, embed_grad, grad_modul, jnp.sum(grad_embedded, 0))

    qkv_grad, embed_grad, _, _ = back[0]
    mlp_low = [item.astype(LOW) for item in mlp_sums]
    modul_parts = jnp.stack([item[2].reshape(shards, ada_cols) for item in back], 1)
    embed_parts = sum(item[3] for item in back).reshape(shards, 1, -1)
    vectors = jnp.concatenate(
        [modul_parts, jnp.pad(embed_parts, ((0, 0), (0, 0), (0, ada_cols - embed_parts.shape[-1])))], 1
    )

    def to_group(moves, item, which, start, size):
        source = moves.operand(item)
        target = moves.output((MATRICES - 1, size, item.shape[1]), LOW)
        for shift in range(1, MATRICES):
            moves.move(
                (PATCHES, seq_count, shift),
                functools.partial(group_peer, members, shift),
                source,
                lambda: (pl.ds(start, size),),
                target,
                lambda shift=shift: (shift - 1,),
                sends=lambda shift=shift: lax.axis_index(PATCHES) // members == (which - shift) % MATRICES,
                takes=lambda: lax.axis_index(PATCHES) // members == which,
            )

    block_rows = qkv_copy.shape[0]
    early = (1, 2)
    first_rows = block_rows * 7 // 16
    moves = Moves("samples", ids)
    moves.exchange_columns(SHARDS, qkv_grad)
    moves.exchange_columns(SHARDS, embed_grad)
    moves.exchange(SHARDS, vectors)
    for item, which in zip(mlp_low, early):
        to_group(moves, item, which, 0, first_rows)
    gathered["qkv"][0], gathered["embed"][0], vectors, *mlp_first = moves.run()
    grad_pos = sum(jnp.sum(item.astype(f32), 0) for item in gathered["embed"].values())

    def from_all(left, right):
        both = [
            jnp.concatenate([gathered[name][step].reshape(shards * local, -1) for step in range(ROLL)], 0)
            for name in (left, right)
        ]
        return rows_product(*both)

    io_here = jnp.stack([from_all("state", "embed"), from_all("delta", "c")])
    io_cols = io_here.shape[-1]
    grads_here = [from_all("a", "qkv"), from_all("mixed", "attn")]
    late = (0, MATRICES - 1)

    moves = Moves("member_sums", ids)
    for item, which in zip(grads_here, late):
        cols = group_cols[which]
        source = moves.operand(item.astype(LOW))
        target = moves.output((members - 1, item.shape[0], cols), LOW)
        for shift in range(1, members):

            def source_at(shift=shift, cols=cols):
                to_member = lax.rem(lax.rem(lax.axis_index(PATCHES), members) + shift, members)
                return (slice(None), pl.ds(pl.multiple_of(to_member * cols, LANES), cols))

            moves.move(
                (PATCHES, members, shift),
                functools.partial(member_peer, members, shift),
                source,
                source_at,
                target,
                lambda shift=shift: (shift - 1,),
            )
    modul_here, embed_here = vectors[:, :ROLL].reshape(-1), jnp.sum(vectors[:, ROLL, : width // shards], 0)
    flat = jnp.concatenate([modul_here, embed_here]).astype(LOW)
    flat_rows = round_up(flat.size, 16 * LANES) // LANES
    moves.gather(PATCHES, jnp.pad(flat, (0, flat_rows * LANES - flat.size)).reshape(flat_rows, LANES))
    moves.exchange(PATCHES, io_here.reshape(seq_count, -1, io_cols).astype(LOW))
    for item, which in zip(mlp_low, early):
        to_group(moves, item, which, first_rows, block_rows - first_rows)
    *halves, vectors, io_parts, up_rest, down_rest = moves.run()
    mlp_sums = [
        mine + jnp.concatenate([jnp.sum(part.astype(f32), 0) for part in parts], 0)
        for mine, *parts in zip(mlp_sums, mlp_first, (up_rest, down_rest))
    ]
    vectors = jnp.sum(vectors.astype(f32), 0).reshape(-1)
    io_slice = jnp.sum(io_parts.astype(f32), 0)
    late_sums = [
        lax.dynamic_slice_in_dim(item, member * group_cols[which], group_cols[which], 1)
        + jnp.sum(half.astype(f32), 0)
        for item, half, which in zip(grads_here, halves, late)
    ]
    modul_all = vectors[: modul_here.size].reshape(-1, ada_cols)
    bias_part = jnp.concatenate([jnp.sum(modul_all, 0), vectors[modul_here.size : flat.size]])
    silu_part = lax.dot_general(
        modul_all, ada_copy.astype(f32), (((1,), (1,)), ((), ())), precision=HIGHEST_PRECISION
    )

    moves = Moves("group_sums", ids)
    moves.vmem = 32 * 2**20
    to_group(moves, late_sums[1].astype(LOW), late[1], 0, block_rows)

    def has_source():
        return lax.axis_index(PATCHES) // members < MATRICES - 1

    def is_source():
        return lax.axis_index(PATCHES) // members > 0

    chain = late_sums[0]
    mine = moves.operand(chain, pltpu.VMEM)
    chain_total = moves.output(chain.shape, f32, pltpu.VMEM)
    arriving, leaving = moves.scratch(chain.shape, LOW), moves.scratch(chain.shape, LOW)
    chunk = block_rows // CHAIN_CHUNKS
    for part in range(CHAIN_CHUNKS):
        place = (pl.ds(part * chunk, chunk),)
        number = moves.move(
            (PATCHES, seq_count, MATRICES - 1),
            functools.partial(group_peer, members, MATRICES - 1),
            leaving,
            lambda place=place: place,
            arriving,
            lambda place=place: place,
            sends=is_source,
            takes=has_source,
            later=True,
        )

        def add(ref, place=place):
            def with_arriving():
                ref(chain_total)[place] = ref(mine)[place] + ref(arriving)[place].astype(f32)

            def alone():
                ref(chain_total)[place] = ref(mine)[place]

            pl.when(has_source())(with_arriving)
            pl.when(jnp.logical_not(has_source()))(alone)
            ref(leaving)[place] = ref(chain_total)[place].astype(LOW)

        moves.wait_for(number)
        moves.task(add)
        moves.start(number)
    moves.gather(SHARDS, silu_part)
    moves.gather(SHARDS, bias_part[None])
    out_parts, chain, silu_parts, bias_parts = moves.run()
    late_sums = [widen(chain), widen(late_sums[1] + jnp.sum(out_parts.astype(f32), 0))]
    grad_group = jnp.where(
        group == late[0],
        late_sums[0],
        jnp.where(group == late[1], late_sums[1], widen(jnp.where(group == early[0], *mlp_sums))),
    )
    grad_silu = jnp.sum(silu_parts, 0)
    grad_cond = jax.vjp(jax.nn.silu, cond_vec)[1](grad_silu)[0]
    grad_table_all = lax.dot_general(select, grad_cond, (((0,), (0,)), ((), ())), precision=HIGHEST_PRECISION)
    grad_table = lax.dynamic_slice_in_dim(grad_table_all, shard * table_cols, table_cols, 1)
    bias_parts = bias_parts[:, 0]
    grad_bias_all = jnp.concatenate([bias_parts[:, :ada_cols].reshape(-1), bias_parts[:, ada_cols:].reshape(-1)])
    grad_bias = lax.dynamic_slice_in_dim(grad_bias_all, shard * biases.shape[0], biases.shape[0])
    silu_rows = lax.dynamic_slice_in_dim(silu_low, seq_index * ada_master.shape[0], ada_master.shape[0], 1)
    grad_ada = lax.dot_general(
        silu_rows.astype(f32), modul_all, (((0,), (0,)), ((), ())), precision=HIGHEST_PRECISION
    )

    io_rows = io_slice.size // most_cols
    outgoing = jnp.concatenate(
        [
            grad_group.astype(LOW).reshape(MATRICES, members, -1, most_cols),
            jnp.broadcast_to(io_slice.astype(LOW).reshape(1, 1, -1, most_cols), (MATRICES, members, io_rows, most_cols)),
        ],
        2,
    )
    by_member = [lax.dynamic_index_in_dim(outgoing, member, 1, False)]
    for shift in range(1, members):
        part = lax.dynamic_index_in_dim(outgoing, lax.rem(member + shift, members), 1, False)
        routes = [(index, index // members * members + (index + shift) % members) for index in range(seq_count)]
        by_member.append(lax.ppermute(part, PATCHES, routes))

    moment_group = jnp.concatenate(moment_halves, 1).reshape(-1, most_cols).astype(f32)
    grad_squares = jnp.sum(grad_group * grad_group)
    squares = (
        grad_squares
        + jnp.sum(grad_ada * grad_ada)
        + jnp.sum(io_slice * io_slice)
        + jnp.sum(grad_pos * grad_pos)
        + (seq_index == 0).astype(f32) * (jnp.sum(grad_table * grad_table) + jnp.sum(grad_bias * grad_bias))
    )
    lane = jnp.arange(LANES, dtype=jnp.int32)
    place = 2 + 3 * group
    entries = jnp.where(lane == 0, squares, 0.0) + jnp.where(lane == 1, loss_local, 0.0)
    entries = entries + jnp.where(lane == place, jnp.sum(moment_group * moment_group), 0.0)
    entries = entries + jnp.where(lane == place + 1, jnp.sum(moment_group * grad_group), 0.0)
    entries = entries + jnp.where(lane == place + 2, grad_squares, 0.0)
    entries, by_member = lax.optimization_barrier((entries, by_member))
    by_member = jnp.stack(by_member)
    by_group = [lax.dynamic_index_in_dim(by_member, group, 1, False)]
    for shift in range(1, MATRICES):
        part = lax.dynamic_index_in_dim(by_member, lax.rem(group + shift, MATRICES), 1, False)
        routes = [(index, (index + shift * members) % seq_count) for index in range(seq_count)]
        by_group.append(lax.ppermute(part, PATCHES, routes))
    sums = total_of(ids, jnp.broadcast_to(entries[None], (8, LANES)))[0]
    grad_norm = jnp.sqrt(sums[0])
    loss_total = sums[1]
    clip = jnp.minimum(1.0, CLIP_LIMIT / (grad_norm + 1e-06))
    terms = sums[2 : 2 + 3 * MATRICES].reshape(MATRICES, 3)
    size_squares = MOMENTUM * MOMENTUM * terms[:, 0] + 2.0 * MOMENTUM * clip * terms[:, 1] + clip * clip * terms[:, 2]
    sizes = jnp.sqrt(jnp.maximum(size_squares, 0.0))
    moment_sizes = sizes[jnp.array([0, 3, 1, 2])] / CLIP_LIMIT
    my_size = lax.dynamic_slice_in_dim(sizes, group, 1)[0]
    block = ((MOMENTUM * moment_group + clip * grad_group) / (my_size + 1e-07)).astype(LOW)

    moves = Moves("columns", ids, 40 * 2**20)
    source = moves.operand(block)
    target = moves.scratch((members * shards, block_rows, most_cols), LOW)
    gram = moves.output((block_rows, block_rows), f32, pltpu.VMEM)
    pairs = shards // 2

    def slot(back_member, back_pair, part=None):
        who_member = lax.rem(lax.rem(lax.axis_index(PATCHES), members) + members - back_member, members)
        who_shard = lax.rem(lax.axis_index(SHARDS) + shards - 2 * back_pair, shards)
        index = who_member * shards + who_shard
        return (index,) if part is None else (index, pl.ds(part * block_rows // 2, block_rows // 2))

    def add_gram(place):
        def action(ref):
            (index,) = place()

            @pl.loop(0, block_rows // GRAM_ROWS)
            def _(tile):
                rows = pl.ds(pl.multiple_of(tile * GRAM_ROWS, GRAM_ROWS), GRAM_ROWS)
                ref(gram)[rows, :] += contract(ref(target)[index, rows, :], ref(target)[index], 1, 1)

        return action

    def start_gram(ref):
        ref(gram)[...] = jnp.zeros((block_rows, block_rows), f32)

    def pair_peer(shift):
        return {SHARDS: lax.rem(lax.axis_index(SHARDS) + 2 * shift, shards)}

    slot_own = functools.partial(slot, 0, 0)
    own_copy = moves.keep(source, None, target, slot_own)
    by_member = {
        shift: moves.move(
            (PATCHES, members, shift), functools.partial(member_peer, members, shift), source, None, target, slot_own
        )
        for shift in range(1, members)
    }
    by_pair = {
        shift: moves.move((SHARDS, 2 * shift), functools.partial(pair_peer, shift), source, None, target, slot_own)
        for shift in range(1, pairs)
    }
    from_sibling = [(moves.move((SHARDS,), sibling_peer, source, None, target, slot_own), slot_own)]
    moves.task(start_gram)
    moves.wait_local(own_copy)
    moves.task(add_gram(slot_own))

    def sibling_place(place):
        def at():
            (index,) = place()
            return (index + 1 - 2 * lax.rem(index, 2),)

        return at

    def hand_on(place, arrivals):
        if len(arrivals) == 1:
            parts = [(place, arrivals[0])]
        else:
            parts = [(functools.partial(place, part), number) for part, number in enumerate(arrivals)]
        numbers = [
            moves.move((SHARDS,), sibling_peer, target, at, target, at, (number,)) for at, number in parts
        ]
        from_sibling.append((numbers, place))
        moves.task(add_gram(place))

    across = []
    for shift_member, first in by_member.items():
        for shift_pair, second in by_pair.items():
            top = functools.partial(slot, shift_member, 0, 0)
            bottom = functools.partial(slot, 0, shift_pair, 1)
            halves = [
                moves.move(
                    (SHARDS, 2 * shift_pair),
                    functools.partial(pair_peer, shift_pair),
                    target,
                    top,
                    target,
                    top,
                    (first,),
                ),
                moves.move(
                    (PATCHES, members, shift_member),
                    functools.partial(member_peer, members, shift_member),
                    target,
                    bottom,
                    target,
                    bottom,
                    (second,),
                ),
            ]
            across.append((functools.partial(slot, shift_member, shift_pair), halves))
    for shift, number in by_member.items():
        hand_on(functools.partial(slot, shift, 0), [number])
    for shift, number in by_pair.items():
        hand_on(functools.partial(slot, 0, shift), [number])
    moves.wait_for(from_sibling[0][0])
    moves.task(add_gram(sibling_place(slot_own)))
    for place, halves in across:
        hand_on(place, halves)
    for numbers, place in from_sibling[1:]:
        for number in numbers:
            moves.wait_for(number)
        moves.task(add_gram(sibling_place(place)))
    (gram,) = moves.run()
    gram, by_group = lax.optimization_barrier((gram, by_group))
    block = newton_schulz(gram, block)
    block, grad_ada, grad_table, grad_pos, grad_bias, by_group = lax.optimization_barrier(
        (block, grad_ada, grad_table, grad_pos, grad_bias, by_group)
    )

    def pick(parts, index):
        value = parts[0]
        for number, part in enumerate(parts[1:], 1):
            value = jnp.where(index == number, part, value)
        return value

    def came_from(which, part):
        back_group = lax.rem(group + MATRICES - which, MATRICES)
        back_member = lax.rem(member + members - part, members)
        return pick([pick([item[back] for back in range(members)], back_member) for item in by_group], back_group)

    def rows_of(which, of_part):
        return jnp.concatenate(
            [of_part(which, part)[: block_rows // seq_count, : group_cols[which]] for part in range(members)], -1
        ).astype(f32)

    moments = [MOMENTUM * old + clip * rows_of(which, came_from) for which, old in enumerate(momenta)]
    io_slices = jnp.stack(
        [
            came_from(which, part)[block_rows // seq_count :].astype(f32)
            for which in range(MATRICES)
            for part in range(members)
        ]
    )
    moves = Moves("update_rows", ids)
    moves.exchange(PATCHES, block.reshape(seq_count, -1, most_cols))
    (update,) = moves.run()
    fresh = [
        master * (1.0 - RATE_MUON * DECAY_MUON)
        - RATE_MUON
        * 0.2
        * math.sqrt(master.shape[1] * shards)
        * rows_of(which, lambda which, part: update[which * members + part])
        for which, master in enumerate(masters)
    ]

    moves = Moves("copies", ids)
    rows = qkv_master.shape[0]

    def row_place(back_group):
        who = lax.axis_index(PATCHES) - back_group * members
        return (pl.ds(pl.multiple_of(who * rows, rows), rows),)

    def has_group(offset):
        place = lax.axis_index(PATCHES) // members + offset
        return jnp.logical_and(place >= 0, place < MATRICES)

    def member_copies(source, source_at, target, target_at, after, there):
        for shift in range(1, members):
            moves.move(
                (PATCHES, members, shift),
                functools.partial(member_peer, members, shift),
                source,
                source_at,
                target,
                target_at,
                after,
                there,
                there,
            )

    places = []
    for item in fresh:
        source = moves.operand(item.astype(LOW))
        target = moves.output((rows * seq_count, item.shape[1]), LOW)
        own = functools.partial(row_place, 0)
        moves.keep(source, None, target, own)
        places.append((source, target, {}))

    def along_line(distance, way, source, target, numbers):
        both = lambda: jnp.logical_and(has_group(way), has_group(-distance * way))
        place = functools.partial(row_place, distance * way)
        numbers[way] = moves.move(
            (PATCHES, seq_count, way),
            functools.partial(group_peer, members, (MATRICES + way) % MATRICES),
            target if distance else source,
            place if distance else None,
            target,
            place,
            (numbers[way],) if distance else (),
            both,
            functools.partial(has_group, -(distance + 1) * way),
        )

    for source, target, numbers in places:
        for way in (1, -1):
            along_line(0, way, source, target, numbers)
    for source, target, numbers in places:
        member_copies(source, None, target, own, (), None)
    for distance in range(1, MATRICES):
        for source, target, numbers in places:
            for way in (1, -1):
                number = numbers[way]
                if distance < MATRICES - 1:
                    along_line(distance, way, source, target, numbers)
                place = functools.partial(row_place, distance * way)
                member_copies(
                    target, place, target, place, (number,), functools.partial(has_group, -distance * way)
                )
    copies = moves.run()

    io_grad = io_slices.reshape(2, padded, io_cols)[:, :values_count]
    ada_res = adam_update(ada_master, ada_first, ada_second, clip * grad_ada, RATE_ADAM)
    io_res = adam_update(io_proj, io_first, io_second, clip * io_grad, RATE_ADAM)
    cond_res = adam_update(cond_table, cond_first, cond_second, clip * grad_table, RATE_TABLE)
    pos_res = adam_update(pos_table, pos_first, pos_second, clip * grad_pos, RATE_TABLE)
    bias_res = adam_update(biases, bias_first, bias_second, clip * grad_bias, RATE_ADAM)
    matrices = []
    for which in (0, 3, 1, 2):
        matrices += [fresh[which], moments[which], copies[which]]
    return (loss_total, grad_norm, moment_sizes, *matrices, *ada_res, *io_res, *cond_res, *pos_res, *bias_res)


def fits_fast(mesh):
    seq, shards = mesh.shape[PATCHES], mesh.shape[SHARDS]
    return HEADS % seq == 0 and (HEADS // seq * HEAD) % LANES == 0 and seq % MATRICES == 0 and shards % 2 == 0


def solution(mesh):
    body = fast_body if fits_fast(mesh) else general_body
    return jax.shard_map(
        body,
        mesh=mesh,
        in_specs=(
            P(SHARDS, PATCHES, None),
            P(SHARDS, PATCHES, None),
            P(SHARDS),
            P(),
            P(None, SHARDS),
            P(PATCHES, SHARDS),
            P(PATCHES, SHARDS),
            P(None, SHARDS),
            P(PATCHES, SHARDS),
            P(PATCHES, SHARDS),
            P(None, SHARDS),
            P(PATCHES, SHARDS),
            P(PATCHES, SHARDS),
            P(None, SHARDS),
            P(PATCHES, SHARDS),
            P(PATCHES, SHARDS),
            P(None, SHARDS),
            P(PATCHES, SHARDS),
            P(PATCHES, SHARDS),
            P(PATCHES, SHARDS),
            P(None, None, SHARDS),
            P(None, None, SHARDS),
            P(None, None, SHARDS),
            P(None, SHARDS),
            P(None, SHARDS),
            P(None, SHARDS),
            P(PATCHES, SHARDS),
            P(PATCHES, SHARDS),
            P(PATCHES, SHARDS),
            P(SHARDS),
            P(SHARDS),
            P(SHARDS),
        ),
        out_specs=(
            P(),
            P(),
            P(),
            P(PATCHES, SHARDS),
            P(PATCHES, SHARDS),
            P(None, SHARDS),
            P(PATCHES, SHARDS),
            P(PATCHES, SHARDS),
            P(None, SHARDS),
            P(PATCHES, SHARDS),
            P(PATCHES, SHARDS),
            P(None, SHARDS),
            P(PATCHES, SHARDS),
            P(PATCHES, SHARDS),
            P(None, SHARDS),
            P(PATCHES, SHARDS),
            P(PATCHES, SHARDS),
            P(PATCHES, SHARDS),
            P(None, None, SHARDS),
            P(None, None, SHARDS),
            P(None, None, SHARDS),
            P(None, SHARDS),
            P(None, SHARDS),
            P(None, SHARDS),
            P(PATCHES, SHARDS),
            P(PATCHES, SHARDS),
            P(PATCHES, SHARDS),
            P(SHARDS),
            P(SHARDS),
            P(SHARDS),
        ),
        check_vma=False,
    )
```

```python
import functools
import math

import jax
import jax.numpy as jnp
from jax import lax
from jax.experimental import pallas as pl
from jax.experimental.pallas import tpu as pltpu
from jax.sharding import PartitionSpec as P

PATCHES = "seq"
SHARDS = "fsdp"
HEADS = 16
HEAD = 64
NI = 3
ROLL = 2
NS_ITERS = 5
STEP_NUM = 10
LON = 32


EPS_NORM = 1e-06
NS_A = 3.4445
NS_B = -4.775
NS_C = 2.0315
MOMENTUM = 0.5
RATE_MUON = 0.15
DECAY_MUON = 0.1
RATE_ADAM = 0.05
RATE_TABLE = 0.5
DECAY_ADAM = 0.1
BETA_FIRST = 0.9
BETA_SECOND = 0.95
CLIP_LIMIT = 0.01
HIGHEST_PRECISION = lax.Precision.HIGHEST


def broadcast(block, axis, owner):
    block = jnp.where(lax.axis_index(axis) == owner, block, jnp.zeros_like(block))
    return lax.psum(block, axis)


def product(left, right):
    return jnp.dot(left, right, preferred_element_type=jnp.float32)


def dot_last(left, right):
    return lax.dot_general(
        left, right, (((left.ndim - 1,), (1,)), ((), ())), preferred_element_type=jnp.float32
    )


def rows_product(left, right):
    flat_left = left.reshape(-1, left.shape[-1])
    flat_right = right.reshape(-1, right.shape[-1])
    return lax.dot_general(
        flat_left, flat_right, (((0,), (0,)), ((), ())), preferred_element_type=jnp.float32
    )


def layer_norm(values):
    centred = values - jnp.mean(values, -1, keepdims=True)
    inverse = lax.rsqrt(jnp.mean(centred * centred, -1, keepdims=True) + EPS_NORM)
    return (centred * inverse, inverse)


def norm_back(grad, normed, inverse):
    return inverse * (
        grad
        - jnp.mean(grad, -1, keepdims=True)
        - normed * jnp.mean(grad * normed, -1, keepdims=True)
    )


def heads_view(values):
    return values.reshape(values.shape[0], values.shape[1], HEADS, HEAD)


def modulation(modul, width):
    return [modul[:, None, column * width : (column + 1) * width] for column in range(6)]


def latitude_weights(local):
    all_patches = local * lax.axis_size(PATCHES)
    band_row = (jnp.arange(all_patches, dtype=jnp.int32) // LON).astype(jnp.float32)
    latitude = (band_row + 0.5) * (math.pi / (all_patches // LON)) - math.pi / 2
    cosine = jnp.cos(latitude)
    weights = cosine / jnp.mean(cosine)
    return lax.dynamic_slice_in_dim(weights, lax.axis_index(PATCHES) * local, local)


def forward_step(weights, state, active, select):
    w_qkv, w_out, w_up, w_down, w_ada, io_all, table, pos, bias = weights
    width = w_out.shape[0]
    cond_vec = jnp.dot(select, table.astype(jnp.float32), precision=HIGHEST_PRECISION)
    silu_low = jax.nn.silu(cond_vec).astype(jnp.bfloat16)
    modul = product(silu_low, w_ada) + bias[: 6 * width].astype(jnp.float32)
    shift1, scale1, gate1, shift2, scale2, gate2 = modulation(modul, width)
    state_low = state.astype(jnp.bfloat16)
    embedded = (
        product(state_low, io_all[0])
        + bias[6 * width :].astype(jnp.float32)
        + pos.astype(jnp.float32)
    )
    normed_one, inverse_one = layer_norm(embedded)
    normed_a = (normed_one * (1.0 + scale1) + shift1).astype(jnp.bfloat16)
    qkv = product(normed_a, w_qkv).astype(jnp.bfloat16)
    queries = qkv[..., :width]
    keys, values = (
        lax.all_gather(qkv[..., width : 2 * width], PATCHES, axis=1, tiled=True),
        lax.all_gather(qkv[..., 2 * width :], PATCHES, axis=1, tiled=True),
    )
    scores = jnp.einsum(
        "sphd,snhd->shpn", heads_view(queries), heads_view(keys), preferred_element_type=jnp.float32
    ) * HEAD ** (-0.5)
    top_score = jnp.max(scores, -1, keepdims=True)
    expo = jnp.exp(scores - top_score)
    total_exp = jnp.sum(expo, -1, keepdims=True)
    log_total = top_score + jnp.log(total_exp)
    probs_low = (expo / total_exp).astype(jnp.bfloat16)
    mixed = jnp.einsum(
        "shpn,snhd->sphd", probs_low, heads_view(values), preferred_element_type=jnp.float32
    )
    mixed_low = mixed.reshape(queries.shape).astype(jnp.bfloat16)
    attended = product(mixed_low, w_out)
    after_attn = embedded + gate1 * attended
    normed_two, inverse_two = layer_norm(after_attn)
    normed_b = (normed_two * (1.0 + scale2) + shift2).astype(jnp.bfloat16)
    upward = product(normed_b, w_up)
    hidden = jax.nn.gelu(upward).astype(jnp.bfloat16)
    downward = dot_last(hidden, w_down)
    after_mlp = after_attn + gate2 * downward
    normed_three, inverse_three = layer_norm(after_mlp)
    normed_c = normed_three.astype(jnp.bfloat16)
    delta = dot_last(normed_c, io_all[1])
    kept = (
        cond_vec,
        silu_low,
        modul,
        state_low,
        normed_one,
        inverse_one,
        normed_a,
        queries,
        keys,
        values,
        log_total,
        mixed_low,
        attended,
        normed_two,
        inverse_two,
        normed_b,
        upward,
        hidden,
        downward,
        normed_three,
        inverse_three,
        normed_c,
    )
    return (state + active * delta, kept)


def backward_step(weights, kept, grad_state, active, select):
    w_qkv, w_out, w_up, w_down, w_ada, io_all, table, pos, bias = weights
    (
        cond_vec,
        silu_low,
        modul,
        state_low,
        normed_one,
        inverse_one,
        normed_a,
        queries,
        keys,
        values,
        log_total,
        mixed_low,
        attended,
        normed_two,
        inverse_two,
        normed_b,
        upward,
        hidden,
        downward,
        normed_three,
        inverse_three,
        normed_c,
    ) = kept
    width = w_out.shape[0]
    shift1, scale1, gate1, shift2, scale2, gate2 = modulation(modul, width)
    delta_grad = (active * grad_state).astype(jnp.bfloat16)
    grad_head = rows_product(delta_grad, normed_c)
    grad_mlp = norm_back(product(delta_grad, io_all[1]), normed_three, inverse_three)
    grad_gate2 = jnp.sum(grad_mlp * downward, 1)
    down_grad = (gate2 * grad_mlp).astype(jnp.bfloat16)
    grad_down = rows_product(down_grad, hidden)
    grad_hidden = product(down_grad, w_down)
    up_grad = jax.vjp(jax.nn.gelu, upward)[1](grad_hidden)[0].astype(jnp.bfloat16)
    grad_up = rows_product(normed_b, up_grad)
    grad_normed_b = dot_last(up_grad, w_up)
    grad_scale2 = jnp.sum(grad_normed_b * normed_two, 1)
    grad_shift2 = jnp.sum(grad_normed_b, 1)
    grad_attn = grad_mlp + norm_back(grad_normed_b * (1.0 + scale2), normed_two, inverse_two)
    grad_gate1 = jnp.sum(grad_attn * attended, 1)
    attn_grad = (gate1 * grad_attn).astype(jnp.bfloat16)
    grad_out = rows_product(mixed_low, attn_grad)
    mixed_grad = dot_last(attn_grad, w_out).astype(jnp.bfloat16)
    q_heads = heads_view(queries)
    k_heads = heads_view(keys)
    v_heads = heads_view(values)
    g_heads = heads_view(mixed_grad)
    scores = jnp.einsum(
        "sphd,snhd->shpn", q_heads, k_heads, preferred_element_type=jnp.float32
    ) * HEAD ** (-0.5)
    probs = jnp.exp(scores - log_total)
    probs_low = probs.astype(jnp.bfloat16)
    grad_probs = jnp.einsum("sphd,snhd->shpn", g_heads, v_heads, preferred_element_type=jnp.float32)
    score_grad = (
        HEAD ** (-0.5) * probs * (grad_probs - jnp.sum(grad_probs * probs, -1, keepdims=True))
    ).astype(jnp.bfloat16)
    grad_queries = jnp.einsum(
        "shpn,snhd->sphd", score_grad, k_heads, preferred_element_type=jnp.float32
    ).reshape(queries.shape)
    key_part = jnp.einsum(
        "shpn,sphd->snhd", score_grad, q_heads, preferred_element_type=jnp.float32
    ).reshape(keys.shape)
    value_part = jnp.einsum(
        "shpn,sphd->snhd", probs_low, g_heads, preferred_element_type=jnp.float32
    ).reshape(values.shape)
    grad_keys, grad_values = (
        lax.psum_scatter(key_part, PATCHES, scatter_dimension=1, tiled=True),
        lax.psum_scatter(value_part, PATCHES, scatter_dimension=1, tiled=True),
    )
    qkv_grad = jnp.concatenate([grad_queries, grad_keys, grad_values], -1).astype(jnp.bfloat16)
    grad_qkv = rows_product(normed_a, qkv_grad)
    grad_normed_a = dot_last(qkv_grad, w_qkv)
    grad_scale1 = jnp.sum(grad_normed_a * normed_one, 1)
    grad_shift1 = jnp.sum(grad_normed_a, 1)
    grad_embedded = grad_attn + norm_back(grad_normed_a * (1.0 + scale1), normed_one, inverse_one)
    embed_grad = grad_embedded.astype(jnp.bfloat16)
    grad_embed = rows_product(state_low, embed_grad)
    grad_prev = grad_state + dot_last(embed_grad, io_all[0])
    grad_modul = jnp.concatenate(
        [grad_shift1, grad_scale1, grad_gate1, grad_shift2, grad_scale2, grad_gate2], -1
    )
    grad_ada = lax.dot_general(
        silu_low.astype(jnp.float32),
        grad_modul,
        (((0,), (0,)), ((), ())),
        precision=HIGHEST_PRECISION,
    )
    grad_silu = lax.dot_general(
        grad_modul, w_ada.astype(jnp.float32), (((1,), (1,)), ((), ())), precision=HIGHEST_PRECISION
    )
    grad_cond = jax.vjp(jax.nn.silu, cond_vec)[1](grad_silu)[0]
    grad_table = lax.dot_general(
        select, grad_cond, (((0,), (0,)), ((), ())), precision=HIGHEST_PRECISION
    )
    grad_bias = jnp.concatenate([jnp.sum(grad_modul, 0), jnp.sum(grad_embedded, (0, 1))])
    grad_pos = jnp.sum(grad_embedded, 0)
    grads = (
        grad_qkv,
        grad_out,
        grad_up,
        grad_down,
        grad_ada,
        jnp.stack([grad_embed, grad_head]),
        grad_table,
        grad_pos,
        grad_bias,
    )
    return (grad_prev, grads)


def gram_part(block_cols):
    return lax.dot_general(
        block_cols, block_cols, (((1,), (1,)), ((), ())), preferred_element_type=jnp.float32
    )


def zero_gram(block_cols):
    return jnp.zeros((block_cols.shape[0], block_cols.shape[0]), jnp.float32)


def newton_step(block_cols, gram):
    gram_low = gram.astype(jnp.bfloat16)
    poly = (NS_B * gram_low.astype(jnp.float32) + NS_C * product(gram_low, gram_low)).astype(
        jnp.bfloat16
    )
    return (NS_A * block_cols.astype(jnp.float32) + product(poly, block_cols)).astype(jnp.bfloat16)


def keep_block(block_cols, gram):
    return block_cols


def adam_update(weight, first, second, grad, rate):
    first_new = BETA_FIRST * first + (1.0 - BETA_FIRST) * grad
    second_new = BETA_SECOND * second + (1.0 - BETA_SECOND) * grad * grad
    unbiased = first_new / (1.0 - BETA_FIRST**STEP_NUM)
    spread = jnp.sqrt(second_new / (1.0 - BETA_SECOND**STEP_NUM)) + 1e-08
    return (weight * (1.0 - rate * DECAY_ADAM) - rate * unbiased / spread, first_new, second_new)


def general_body(
    states,
    targets,
    lengths,
    intervals,
    qkv_copy,
    qkv_master,
    qkv_moment,
    out_copy,
    out_master,
    out_moment,
    up_copy,
    up_master,
    up_moment,
    down_copy,
    down_master,
    down_moment,
    ada_copy,
    ada_master,
    ada_first,
    ada_second,
    io_proj,
    io_first,
    io_second,
    cond_table,
    cond_first,
    cond_second,
    pos_table,
    pos_first,
    pos_second,
    biases,
    bias_first,
    bias_second,
):
    weights = (
        lax.all_gather(qkv_copy, SHARDS, axis=1, tiled=True),
        lax.all_gather(out_copy, SHARDS, axis=1, tiled=True),
        lax.all_gather(up_copy, SHARDS, axis=1, tiled=True),
        lax.all_gather(down_copy, SHARDS, axis=1, tiled=True),
        lax.all_gather(ada_copy, SHARDS, axis=1, tiled=True),
        lax.all_gather(io_proj.astype(jnp.bfloat16), SHARDS, axis=2, tiled=True),
        lax.all_gather(cond_table.astype(jnp.bfloat16), SHARDS, axis=1, tiled=True),
        lax.all_gather(pos_table.astype(jnp.bfloat16), SHARDS, axis=1, tiled=True),
        lax.all_gather(biases.astype(jnp.bfloat16), SHARDS, axis=0, tiled=True),
    )
    samples, local, values_count = states.shape
    table_rows = cond_table.shape[0]
    my_ids = lax.dynamic_slice_in_dim(intervals, lax.axis_index(SHARDS) * samples, samples)
    counts = jnp.sum(
        (intervals[:, None] == jnp.arange(NI, dtype=jnp.int32)[None]).astype(jnp.float32), 0
    )
    id_counts = jnp.sum(
        (my_ids[:, None] == jnp.arange(NI, dtype=jnp.int32)[None]).astype(jnp.float32)
        * counts[None],
        1,
    )
    weight = 1.0 / (NI * local * lax.axis_size(PATCHES) * values_count * id_counts)
    rows_iota = jnp.arange(table_rows, dtype=jnp.int32)
    id_select = (my_ids[:, None] == rows_iota[None]).astype(jnp.float32)
    state = states.astype(jnp.float32)
    seen_states = []
    kept_all = []
    for step in range(ROLL):
        select = id_select + (rows_iota == NI + step).astype(jnp.float32)[None]
        active = (step < lengths).astype(jnp.float32)[:, None, None]
        seen_states.append(state)
        state, kept = forward_step(weights, state, active, select)
        kept_all.append(kept)
    lat = latitude_weights(local)
    diff = state - targets.astype(jnp.float32)
    err = jnp.sum(jnp.sum(diff * diff, -1) * lat[None], -1)
    loss_local = jnp.sum(weight * err)
    grad_state = 2.0 * weight[:, None, None] * lat[None, :, None] * diff
    totals = None
    for step in reversed(range(ROLL)):
        select = id_select + (rows_iota == NI + step).astype(jnp.float32)[None]
        active = (step < lengths).astype(jnp.float32)[:, None, None]
        kept = kept_all[step]
        grad_state, grads = backward_step(weights, kept, grad_state, active, select)
        totals = grads if totals is None else jax.tree.map(jnp.add, totals, grads)
    reduced = (
        lax.psum_scatter(totals[0], SHARDS, scatter_dimension=1, tiled=True),
        lax.psum_scatter(totals[1], SHARDS, scatter_dimension=1, tiled=True),
        lax.psum_scatter(totals[2], SHARDS, scatter_dimension=1, tiled=True),
        lax.psum_scatter(totals[3], SHARDS, scatter_dimension=1, tiled=True),
        lax.psum_scatter(totals[4], SHARDS, scatter_dimension=1, tiled=True),
        lax.psum_scatter(totals[5], SHARDS, scatter_dimension=2, tiled=True),
        lax.psum_scatter(totals[6], SHARDS, scatter_dimension=1, tiled=True),
        lax.psum_scatter(totals[7], SHARDS, scatter_dimension=1, tiled=True),
        lax.psum_scatter(totals[8], SHARDS, scatter_dimension=0, tiled=True),
    )
    large = (
        lax.psum_scatter(reduced[0], PATCHES, scatter_dimension=0, tiled=True),
        lax.psum_scatter(reduced[1], PATCHES, scatter_dimension=0, tiled=True),
        lax.psum_scatter(reduced[2], PATCHES, scatter_dimension=0, tiled=True),
        lax.psum_scatter(reduced[3], PATCHES, scatter_dimension=0, tiled=True),
        lax.psum_scatter(reduced[4], PATCHES, scatter_dimension=0, tiled=True),
    )
    small = lax.psum((reduced[5], reduced[6], reduced[8]), PATCHES)
    grad_pos = reduced[7]
    first_copy = (lax.axis_index(PATCHES) == 0).astype(jnp.float32)
    squares = jnp.sum(grad_pos * grad_pos)
    for item in large:
        squares = squares + jnp.sum(item * item)
    small_squares = jnp.float32(0.0)
    for item in small:
        small_squares = small_squares + jnp.sum(item * item)
    squares, loss_total = lax.psum(
        (squares + first_copy * small_squares, loss_local), (PATCHES, SHARDS)
    )
    grad_norm = jnp.sqrt(squares)
    clip = jnp.minimum(1.0, CLIP_LIMIT / (grad_norm + 1e-06))
    masters = (qkv_master, out_master, up_master, down_master)
    moments = [
        MOMENTUM * old + clip * grad
        for old, grad in zip((qkv_moment, out_moment, up_moment, down_moment), large[:4])
    ]
    norms = lax.psum(
        (
            jnp.sum(moments[0] * moments[0]),
            jnp.sum(moments[1] * moments[1]),
            jnp.sum(moments[2] * moments[2]),
            jnp.sum(moments[3] * moments[3]),
        ),
        (PATCHES, SHARDS),
    )
    sizes = [jnp.sqrt(norms[which]) for which in range(4)]
    moment_sizes = jnp.stack(sizes) / CLIP_LIMIT
    scaled = [(moments[which] / (sizes[which] + 1e-07)).astype(jnp.bfloat16) for which in range(4)]
    columns = (
        lax.all_gather(scaled[0], PATCHES, axis=0, tiled=True),
        lax.all_gather(scaled[1], PATCHES, axis=0, tiled=True),
        lax.all_gather(scaled[2], PATCHES, axis=0, tiled=True),
        lax.all_gather(scaled[3], PATCHES, axis=0, tiled=True),
    )
    seq_index = lax.axis_index(PATCHES)
    seq_count = lax.axis_size(PATCHES)
    owners = [seq_index == which % seq_count for which in range(4)]
    blocks = list(columns)
    for turn in range(NS_ITERS):
        partial_value = [
            lax.cond(owners[which], gram_part, zero_gram, blocks[which]) for which in range(4)
        ]
        grams = lax.psum(
            (partial_value[0], partial_value[1], partial_value[2], partial_value[3]), SHARDS
        )
        blocks = [
            lax.cond(owners[which], newton_step, keep_block, blocks[which], grams[which])
            for which in range(4)
        ]
    blocks = [broadcast(blocks[which], PATCHES, which % seq_count) for which in range(4)]
    row_count = qkv_master.shape[0]
    fresh = []
    for which in range(4):
        my_rows = lax.dynamic_slice_in_dim(
            blocks[which], seq_index * row_count, row_count, 0
        ).astype(jnp.float32)
        all_cols = masters[which].shape[1] * lax.axis_size(SHARDS)
        fresh.append(
            masters[which] * (1.0 - RATE_MUON * DECAY_MUON)
            - RATE_MUON * 0.2 * math.sqrt(all_cols) * my_rows
        )
    copies = (
        lax.all_gather(fresh[0].astype(jnp.bfloat16), PATCHES, axis=0, tiled=True),
        lax.all_gather(fresh[1].astype(jnp.bfloat16), PATCHES, axis=0, tiled=True),
        lax.all_gather(fresh[2].astype(jnp.bfloat16), PATCHES, axis=0, tiled=True),
        lax.all_gather(fresh[3].astype(jnp.bfloat16), PATCHES, axis=0, tiled=True),
    )
    ada_res = adam_update(ada_master, ada_first, ada_second, clip * large[4], RATE_ADAM)
    io_res = adam_update(io_proj, io_first, io_second, clip * small[0], RATE_ADAM)
    cond_res = adam_update(cond_table, cond_first, cond_second, clip * small[1], RATE_TABLE)
    pos_res = adam_update(pos_table, pos_first, pos_second, clip * grad_pos, RATE_TABLE)
    bias_res = adam_update(biases, bias_first, bias_second, clip * small[2], RATE_ADAM)
    return (
        loss_total,
        grad_norm,
        moment_sizes,
        fresh[0],
        moments[0],
        copies[0],
        fresh[1],
        moments[1],
        copies[1],
        fresh[2],
        moments[2],
        copies[2],
        fresh[3],
        moments[3],
        copies[3],
        ada_res[0],
        ada_res[1],
        ada_res[2],
        io_res[0],
        io_res[1],
        io_res[2],
        cond_res[0],
        cond_res[1],
        cond_res[2],
        pos_res[0],
        pos_res[1],
        pos_res[2],
        bias_res[0],
        bias_res[1],
        bias_res[2],
    )


LANES = 128
MATRICES = 4
LOW = jnp.bfloat16
MESH = pl.DeviceIdType.MESH


def round_up(value, unit):
    return -(-value // unit) * unit


def member_peer(members, shift):
    index = lax.axis_index(PATCHES)
    return {PATCHES: index // members * members + lax.rem(lax.rem(index, members) + shift, members)}


def group_peer(members, shift):
    return {PATCHES: lax.rem(lax.axis_index(PATCHES) + shift * members, lax.axis_size(PATCHES))}


def sibling_peer():
    index = lax.axis_index(SHARDS)
    return {SHARDS: index + 1 - 2 * lax.rem(index, 2)}


def where(condition, action):
    if condition is None:
        action()
    else:
        pl.when(condition())(action)


class Moves:
    def __init__(self, name, ids, vmem=None):
        self.name = name
        self.ids = ids
        self.vmem = vmem
        self.operands = []
        self.operand_specs = []
        self.outputs = []
        self.output_specs = []
        self.scratches = []
        self.moves = []
        self.locals = []
        self.steps = []
        self.peers = {}

    def operand(self, array, space=pl.ANY):
        self.operands.append(array)
        self.operand_specs.append(pl.BlockSpec(memory_space=space))
        return (0, len(self.operands) - 1)

    def output(self, shape, dtype, space=pl.ANY):
        self.outputs.append(jax.ShapeDtypeStruct(shape, dtype))
        self.output_specs.append(pl.BlockSpec(memory_space=space))
        return (1, len(self.outputs) - 1)

    def scratch(self, shape, dtype):
        self.scratches.append(pltpu.VMEM(shape, dtype))
        return (2, len(self.scratches) - 1)

    def keep(self, source, source_at, target, target_at):
        self.locals.append((source, source_at, target, target_at))
        return len(self.locals) - 1

    def move(
        self, peer_key, peer, source, source_at, target, target_at, after=(), sends=None, takes=None, later=False
    ):
        number = len(self.moves)
        self.peers.setdefault(peer_key, peer)
        self.moves.append((peer_key, source, source_at, target, target_at, sends, takes, later or bool(after)))
        for earlier in after:
            self.steps.append((self.await_move, earlier))
        if after:
            self.steps.append((self.start_move, number))
        return number

    def wait_for(self, number):
        self.steps.append((self.await_move, number))

    def start(self, number):
        self.steps.append((self.start_move, number))

    def wait_local(self, number):
        self.steps.append((self.await_local, number))

    def task(self, action):
        self.steps.append((self.do_task, action))

    def await_move(self, number):
        if number not in self.arrived:
            self.arrived.add(number)
            where(self.moves[number][6], self.remote[number].wait_recv)

    def start_move(self, number):
        where(self.moves[number][5], self.remote[number].start)

    def await_local(self, number):
        if number not in self.kept:
            self.kept.add(number)
            self.local[number].wait()

    def do_task(self, action):
        action(self.ref)

    def ref(self, which):
        return self.refs[which[0]][which[1]]

    def view(self, which, index):
        ref = self.ref(which)
        return ref.at[index()] if index is not None else ref

    def kernel(self, *refs):
        sizes = (len(self.operands), len(self.outputs), len(self.scratches))
        self.refs = (refs[: sizes[0]], refs[sizes[0] : sizes[0] + sizes[1]], refs[sizes[0] + sizes[1] : sum(sizes)])
        local_sem, send_sem, recv_sem = refs[sum(sizes) :]
        self.arrived, self.kept = set(), set()
        devices = {key: peer() for key, peer in self.peers.items()}
        barrier = pltpu.get_barrier_semaphore()
        for device in devices.values():
            pl.semaphore_signal(barrier, inc=1, device_id=device, device_id_type=MESH)
        pl.semaphore_wait(barrier, len(devices))
        self.remote = []
        for number, (key, source, source_at, target, target_at, _, _, later) in enumerate(self.moves):
            self.remote.append(
                pltpu.make_async_remote_copy(
                    src_ref=self.view(source, source_at),
                    dst_ref=self.view(target, target_at),
                    send_sem=send_sem.at[number],
                    recv_sem=recv_sem.at[number],
                    device_id=devices[key],
                    device_id_type=MESH,
                )
            )
            if not later:
                self.start_move(number)
        self.local = [
            pltpu.make_async_copy(self.view(source, source_at), self.view(target, target_at), local_sem.at[number])
            for number, (source, source_at, target, target_at) in enumerate(self.locals)
        ]
        for copy in self.local:
            copy.start()
        for action, number in self.steps:
            action(number)
        for number in range(len(self.locals)):
            self.await_local(number)
        for number, copy in enumerate(self.remote):
            self.await_move(number)
            where(self.moves[number][5], copy.wait_send)

    def run(self):
        return pl.pallas_call(
            self.kernel,
            out_shape=self.outputs,
            in_specs=self.operand_specs,
            out_specs=self.output_specs,
            scratch_shapes=[
                *self.scratches,
                pltpu.SemaphoreType.DMA((max(1, len(self.locals)),)),
                pltpu.SemaphoreType.DMA((len(self.moves),)),
                pltpu.SemaphoreType.DMA((len(self.moves),)),
            ],
            compiler_params=pltpu.CompilerParams(
                collective_id=self.ids.setdefault(self.name, len(self.ids)),
                has_side_effects=True,
                vmem_limit_bytes=self.vmem,
            ),
            name=self.name,
        )(*self.operands)

    def along(self, axis, source, target, pairs, later=False):
        numbers = []
        count = lax.axis_size(axis)

        def other(shift):
            return lax.rem(lax.axis_index(axis) + shift, count)

        for shift in range(1, count):
            for source_at, target_at in pairs:
                numbers.append(
                    self.move(
                        (axis, shift),
                        lambda shift=shift: {axis: other(shift)},
                        source,
                        None if source_at is None else (lambda at=source_at, shift=shift: at(other(shift))),
                        target,
                        lambda at=target_at: at(lax.axis_index(axis)),
                        later=later,
                    )
                )
        for source_at, target_at in pairs:
            self.keep(
                source,
                None if source_at is None else (lambda at=source_at: at(lax.axis_index(axis))),
                target,
                lambda at=target_at: at(lax.axis_index(axis)),
            )
        return numbers

    def gather(self, axis, array):
        target = self.output((lax.axis_size(axis),) + array.shape, array.dtype)
        self.along(axis, self.operand(array), target, [(None, lambda sender: (sender,))])

    def gather_pairs(self, array, parts=1, hold=False):
        shards = lax.axis_size(SHARDS)
        source = self.operand(array)
        target = self.output((shards,) + array.shape, array.dtype)
        rows = array.shape[0] // parts

        def place(back_pair, part):
            return (lax.rem(lax.axis_index(SHARDS) + shards - 2 * back_pair, shards), pl.ds(part * rows, rows))

        firsts = []
        for part in range(parts):
            for pair in range(1, shards // 2):
                number = self.move(
                    (SHARDS, 2 * pair),
                    lambda pair=pair: {SHARDS: lax.rem(lax.axis_index(SHARDS) + 2 * pair, shards)},
                    source,
                    lambda part=part: (pl.ds(part * rows, rows),),
                    target,
                    functools.partial(place, 0, part),
                )
                firsts.append((functools.partial(place, pair, part), number))
        own = lambda: (lax.axis_index(SHARDS),)
        self.move((SHARDS,), sibling_peer, source, None, target, own)
        self.keep(source, None, target, own)
        waiting = [(target, at, number) for at, number in firsts]
        if hold:
            return waiting
        self.to_sibling(waiting)

    def gather_columns(self, axis, array):
        width = array.shape[-1]
        target = self.output(array.shape[:-1] + (lax.axis_size(axis) * width,), array.dtype)
        lead = (slice(None),) * (array.ndim - 1)
        self.along(
            axis,
            self.operand(array),
            target,
            [(None, lambda sender: lead + (pl.ds(pl.multiple_of(sender * width, LANES), width),))],
        )

    def gather_twice(self, arrays, members):
        shards = lax.axis_size(SHARDS)
        entries = []
        for array in arrays:
            source = self.operand(array)
            width = array.shape[1]
            target = self.output((array.shape[0], shards * width), array.dtype)
            rows = array.shape[0] // members

            def columns(back_pair, width=width):
                who = lax.rem(lax.axis_index(SHARDS) + shards - 2 * back_pair, shards)
                return pl.ds(pl.multiple_of(who * width, LANES), width)

            def place(back_member, back_pair, rows=rows, columns=columns):
                index = lax.rem(lax.rem(lax.axis_index(PATCHES), members) + members - back_member, members)
                return (pl.ds(pl.multiple_of(index * rows, rows), rows), columns(back_pair))

            def mine(rows=rows):
                index = lax.rem(lax.axis_index(PATCHES), members)
                return (pl.ds(pl.multiple_of(index * rows, rows), rows),)

            firsts = [
                self.move(
                    (SHARDS, 2 * pair),
                    lambda pair=pair: {SHARDS: lax.rem(lax.axis_index(SHARDS) + 2 * pair, shards)},
                    source,
                    mine,
                    target,
                    functools.partial(place, 0, 0),
                )
                for pair in range(1, shards // 2)
            ]
            entries.append((source, target, place, firsts))
            self.move((SHARDS,), sibling_peer, source, None, target, lambda columns=columns: (slice(None), columns(0)))
        last = []
        for _, target, place, firsts in entries:
            for pair, first in enumerate(firsts, 1):
                near = functools.partial(place, 0, pair)
                for shift in range(1, members):
                    number = self.move(
                        (PATCHES, members, shift),
                        functools.partial(member_peer, members, shift),
                        target,
                        near,
                        target,
                        near,
                        (first,),
                    )
                    last.append((target, functools.partial(place, shift, pair), number))
                self.move((SHARDS,), sibling_peer, target, near, target, near, (first,))
        self.to_sibling(last)

    def to_sibling(self, waiting):
        for target, place, number in waiting:
            self.move((SHARDS,), sibling_peer, target, place, target, place, (number,))

    def exchange(self, axis, array, later=False):
        target = self.output(array.shape, array.dtype)
        return self.along(
            axis, self.operand(array), target, [(lambda receiver: (receiver,), lambda sender: (sender,))], later
        )

    def exchange_columns(self, axis, array):
        width = array.shape[-1] // lax.axis_size(axis)
        target = self.output((lax.axis_size(axis), array.shape[0], width), array.dtype)
        self.along(
            axis,
            self.operand(array),
            target,
            [
                (
                    lambda receiver: (slice(None), pl.ds(pl.multiple_of(receiver * width, LANES), width)),
                    lambda sender: (sender,),
                )
            ],
        )

    def rows_to_heads(self, axis, array, planes, target):
        count, rows = lax.axis_size(axis), array.shape[0]
        columns = array.shape[1] // planes
        width = columns // count
        return self.along(
            axis,
            self.operand(array),
            target,
            [
                (
                    lambda receiver, plane=plane: (
                        slice(None),
                        pl.ds(pl.multiple_of(plane * columns + receiver * width, LANES), width),
                    ),
                    lambda sender, plane=plane: (plane, pl.ds(pl.multiple_of(sender * rows, rows), rows)),
                )
                for plane in range(planes)
            ],
        )

    def head_rows(self, source, target, planes, rows, columns, members, back_group):
        count = lax.axis_size(PATCHES)
        width = columns // count
        for shift_member in range(members):
            for plane in planes:

                def peer(shift_member=shift_member):
                    index = lax.axis_index(PATCHES)
                    there = lax.rem(index // members + back_group, MATRICES) * members
                    return there + lax.rem(lax.rem(index, members) + shift_member, members)

                def source_at(peer=peer, plane=plane):
                    return (plane, pl.ds(pl.multiple_of(peer() * rows, rows), rows))

                def target_at(plane=plane):
                    start = plane * columns + lax.axis_index(PATCHES) * width
                    return (slice(None), pl.ds(pl.multiple_of(start, LANES), width))

                if shift_member or back_group:
                    self.start(
                        self.move(
                            (PATCHES, count, back_group, shift_member),
                            lambda peer=peer: {PATCHES: peer()},
                            source,
                            source_at,
                            target,
                            target_at,
                            later=True,
                        )
                    )
                else:

                    def own(ref, source_at=source_at, target_at=target_at):
                        ref(target)[target_at()] = ref(source)[source_at()]

                    self.task(own)


def total_of(ids, values, shared):
    moves = Moves("total", ids)
    source, result = moves.operand(values, pltpu.VMEM), moves.output(values.shape, values.dtype, pltpu.VMEM)
    moves.gather(PATCHES, shared)
    for axis in (SHARDS, PATCHES):
        count = lax.axis_size(axis)
        buffer = moves.scratch((count,) + values.shape, values.dtype)

        def own(axis=axis):
            return (lax.axis_index(axis),)

        def put(ref, source=source, buffer=buffer, own=own):
            ref(buffer)[own()] = ref(source)[...]

        moves.task(put)
        numbers = []
        for shift in range(1, count):
            numbers.append(
                moves.move(
                    (axis, shift),
                    lambda axis=axis, shift=shift, count=count: {axis: lax.rem(lax.axis_index(axis) + shift, count)},
                    buffer,
                    own,
                    buffer,
                    own,
                    later=True,
                )
            )
            moves.start(numbers[-1])
        for number in numbers:
            moves.wait_for(number)

        def add(ref, buffer=buffer):
            ref(result)[...] = jnp.sum(ref(buffer)[...], 0)

        moves.task(add)
        source = result
    return moves.run()


def contract(left, right, left_dim, right_dim):
    return lax.dot_general(
        left, right, (((left_dim,), (right_dim,)), ((), ())), preferred_element_type=jnp.float32
    )


CHAIN_CHUNKS = 8
GRAM_COLS = 256


def attend(queries, keys, values):
    scores = contract(queries, keys, 1, 1) * HEAD ** (-0.5)
    expo = jnp.exp(scores - jnp.max(scores, -1, keepdims=True))
    probs = (expo / jnp.sum(expo, -1, keepdims=True)).astype(LOW)
    return contract(probs, values, 1, 0)


def group_rows(rows, members, shift):
    size = rows * members
    there = lax.rem(lax.axis_index(PATCHES) // members + shift, MATRICES)
    return pl.ds(pl.multiple_of(there * size, size), size)


def add_attention(moves, qkv, mixed, arrivals, rows, members, waiting):
    for number in arrivals:
        moves.wait_for(number)
    for number in range(3):
        moves.wait_local(number)
    moves.to_sibling(waiting)
    count = lax.axis_size(PATCHES)
    width = HEADS // count * HEAD
    buffer = moves.scratch((1, rows * count, width), LOW)
    for shift in (*range(1, MATRICES), 0):

        def work(ref, shift=shift):
            at = group_rows(rows, members, shift)
            parts = []
            for head in range(width // HEAD):
                lanes = pl.ds(head * HEAD, HEAD)
                parts.append(attend(ref(qkv)[0, at, lanes], ref(qkv)[1, :, lanes], ref(qkv)[2, :, lanes]))
            ref(buffer)[0, at, :] = jnp.concatenate(parts, -1).astype(LOW)

        moves.task(work)
        moves.head_rows(buffer, mixed, (0,), rows, width * count, members, shift)


def add_attention_back(moves, qkv, grads, result, arrivals, rows, members, waiting):
    for number in arrivals:
        moves.wait_for(number)
    moves.wait_local(0)
    moves.to_sibling(waiting)
    count = lax.axis_size(PATCHES)
    width = HEADS // count * HEAD
    heads = width // HEAD
    buffer = moves.scratch((3, rows * count, width), LOW)
    key_total = moves.scratch((heads, rows * count, HEAD), jnp.float32)
    value_total = moves.scratch((heads, rows * count, HEAD), jnp.float32)
    for shift in (*range(1, MATRICES), 0):

        def work(ref, shift=shift):
            at = group_rows(rows, members, shift)
            parts = []
            for head in range(heads):
                lanes = pl.ds(head * HEAD, HEAD)
                queries, keys, values = ref(qkv)[0, at, lanes], ref(qkv)[1, :, lanes], ref(qkv)[2, :, lanes]
                grad = ref(grads)[0, at, lanes]
                scores = contract(keys, queries, 1, 1) * HEAD ** (-0.5)
                expo = jnp.exp(scores - jnp.max(scores, 0, keepdims=True))
                probs = expo / jnp.sum(expo, 0, keepdims=True)
                grad_probs = contract(values, grad, 1, 1)
                shared = jnp.sum(grad_probs * probs, 0, keepdims=True)
                score_grad = (HEAD ** (-0.5) * probs * (grad_probs - shared)).astype(LOW)
                parts.append(contract(score_grad, keys, 0, 0))
                key_part = contract(score_grad, queries, 1, 0)
                value_part = contract(probs.astype(LOW), grad, 1, 0)
                if shift == 1:
                    ref(key_total)[head] = key_part
                    ref(value_total)[head] = value_part
                else:
                    ref(key_total)[head] += key_part
                    ref(value_total)[head] += value_part
            ref(buffer)[0, at, :] = jnp.concatenate(parts, -1).astype(LOW)

        moves.task(work)
        moves.head_rows(buffer, result, (0,), rows, width * count, members, shift)

    def finish(ref):
        for plane, total in ((1, key_total), (2, value_total)):
            ref(buffer)[plane] = jnp.concatenate([ref(total)[head] for head in range(heads)], -1).astype(LOW)

    moves.task(finish)
    for shift in (*range(1, MATRICES), 0):
        moves.head_rows(buffer, result, (1, 2), rows, width * count, members, shift)


def newton_schulz(source, gram, poly, once, gram_low, poly_low, once_low, block, block_next):
    size = gram.shape[0]
    eye = jnp.equal(
        lax.broadcasted_iota(jnp.int32, (GRAM_COLS, GRAM_COLS), 0),
        lax.broadcasted_iota(jnp.int32, (GRAM_COLS, GRAM_COLS), 1),
    ).astype(jnp.float32)

    def over_tiles(action, width=size):
        def step(tile, total):
            return total + action(pl.ds(pl.multiple_of(tile * GRAM_COLS, GRAM_COLS), GRAM_COLS))

        return lax.fori_loop(0, width // GRAM_COLS, step, jnp.float32(0.0))

    def store(full, low, cols, value, mean, excess):
        full[:, cols] = value
        low[:, cols] = value.astype(LOW)
        corner = full[cols, cols] - excess * eye
        full[cols, cols] = corner
        low[cols, cols] = (corner - mean * eye).astype(LOW)

    def advance(gram_mean, gram_squares, last):
        poly_mean = NS_B * gram_mean + NS_C * gram_squares / size

        def poly_cols(cols):
            own = gram[:, cols]
            value = contract(gram_low[...], gram_low[:, cols], 1, 0)
            value = NS_C * value + (NS_B + 2.0 * NS_C * gram_mean) * own
            store(poly, poly_low, cols, value, poly_mean, NS_C * gram_mean * gram_mean)
            return jnp.sum(value * own)

        once_mean = over_tiles(poly_cols) / size - NS_C * gram_mean * gram_mean * gram_mean

        def block_cols(cols):
            value = contract(poly_low[...], block[:, cols], 1, 0)
            block_next[:, cols] = (value + (NS_A + poly_mean) * block[:, cols].astype(jnp.float32)).astype(LOW)
            return jnp.float32(0.0)

        over_tiles(block_cols, block.shape[1])
        block[...] = block_next[...]
        if last:
            return None

        def once_cols(cols):
            own = poly[:, cols]
            value = contract(poly_low[...], gram_low[:, cols], 1, 0)
            value = value + poly_mean * gram[:, cols] + gram_mean * own
            store(once, once_low, cols, value, once_mean, poly_mean * gram_mean)
            return jnp.sum(value * own)

        poly_once = over_tiles(once_cols) / size - poly_mean * gram_mean * poly_mean
        mean_next = NS_A * NS_A * gram_mean + 2.0 * NS_A * once_mean + poly_once
        excess = poly_mean * once_mean

        def gram_cols(cols):
            value = contract(poly_low[...], once_low[:, cols], 1, 0)
            value = value + (2.0 * NS_A + poly_mean) * once[:, cols] + once_mean * poly[:, cols]
            value = value + NS_A * NS_A * gram[:, cols]
            store(gram, gram_low, cols, value, mean_next, excess)
            return jnp.sum(value * value)

        return mean_next, over_tiles(gram_cols) - excess * (2.0 * mean_next + excess) * size

    block[...] = source[...]
    mean = over_tiles(lambda cols: jnp.sum(gram[cols, cols] * eye)) / size

    def start(cols):
        value = gram[:, cols]
        gram_low[:, cols] = value.astype(LOW)
        gram_low[cols, cols] = (gram[cols, cols] - mean * eye).astype(LOW)
        return jnp.sum(value * value)

    state = lax.fori_loop(0, NS_ITERS - 1, lambda turn, state: advance(*state, False), (mean, over_tiles(start)))
    advance(*state, True)


def fast_body(
    states,
    targets,
    lengths,
    intervals,
    qkv_copy,
    qkv_master,
    qkv_moment,
    out_copy,
    out_master,
    out_moment,
    up_copy,
    up_master,
    up_moment,
    down_copy,
    down_master,
    down_moment,
    ada_copy,
    ada_master,
    ada_first,
    ada_second,
    io_proj,
    io_first,
    io_second,
    cond_table,
    cond_first,
    cond_second,
    pos_table,
    pos_first,
    pos_second,
    biases,
    bias_first,
    bias_second,
):
    ids = {}
    f32 = jnp.float32
    seq_count, shards = lax.axis_size(PATCHES), lax.axis_size(SHARDS)
    seq_index, shard = lax.axis_index(PATCHES), lax.axis_index(SHARDS)
    members = seq_count // MATRICES
    group, member = seq_index // members, lax.rem(seq_index, members)
    samples, local, values_count = states.shape
    table_rows, table_cols = cond_table.shape
    width = table_cols * shards
    ada_cols = ada_copy.shape[1]
    padded = round_up(values_count, LANES)

    moves = Moves("tables", ids)
    moves.gather(SHARDS, cond_table)
    moves.gather(SHARDS, biases[None])
    table_parts, bias_parts = moves.run()
    table = jnp.moveaxis(table_parts, 0, 1).reshape(table_rows, width).astype(LOW).astype(f32)
    bias = bias_parts.reshape(-1).astype(LOW).astype(f32)
    rows_iota = jnp.arange(table_rows, dtype=jnp.int32)
    id_rows = (intervals[:, None] == rows_iota[None]).astype(f32)
    step_rows = (rows_iota[None] == NI + jnp.arange(ROLL, dtype=jnp.int32)[:, None]).astype(f32)
    select = (id_rows[:, None] + step_rows[None]).reshape(-1, table_rows)
    cond_vec = jnp.sum(select[:, :, None] * table[None], 1)
    silu_low = jax.nn.silu(cond_vec).astype(LOW)
    modul_shard = product(silu_low, ada_copy) + lax.dynamic_slice_in_dim(bias, shard * ada_cols, ada_cols)[None]

    moves = Moves("weights", ids)
    moves.exchange(SHARDS, modul_shard.reshape(shards, ROLL, ada_cols))
    moves.gather_columns(SHARDS, pos_table.astype(LOW))
    io_low = jnp.pad(io_proj.astype(LOW), ((0, 0), (0, padded - values_count), (0, 0)))
    own_parts = (io_low.reshape(2 * padded, -1), out_copy, qkv_copy)
    moves.gather_twice(own_parts, members)
    modul, pos, *parts = moves.run()
    io_all, w_out, w_qkv = [
        lax.dynamic_update_slice_in_dim(part, own, shard * own.shape[1], 1) for part, own in zip(parts, own_parts)
    ]
    io_all = io_all.reshape(2, padded, width)
    modul = jnp.moveaxis(modul, 0, 1).reshape(ROLL, 6 * width)
    pos = pos.astype(f32)

    masters = (qkv_master, up_master, down_master, out_master)
    momenta = (qkv_moment, up_moment, down_moment, out_moment)
    group_cols = [item.shape[1] // members for item in momenta]
    most_cols = max(group_cols)

    def widen(item):
        return jnp.pad(item, ((0, 0), (0, most_cols - item.shape[1])))

    moment_parts = jnp.stack(
        [
            widen(item[:, part * cols : (part + 1) * cols].astype(LOW))
            for item, cols in zip(momenta, group_cols)
            for part in range(members)
        ]
    )
    half_rows = moment_parts.shape[1] // 2

    counts = jnp.sum((intervals[:, None] == jnp.arange(NI, dtype=jnp.int32)[None]).astype(f32), 0)
    my_id = lax.dynamic_slice_in_dim(intervals, shard, 1)
    id_count = jnp.sum((my_id == jnp.arange(NI, dtype=jnp.int32)).astype(f32) * counts)
    weight = 1.0 / (NI * local * seq_count * values_count * id_count)
    length = lengths[0]
    value_pad = ((0, 0), (0, padded - values_count))
    state = jnp.pad(states[0].astype(f32), value_pad)
    embed_bias = bias[6 * width :]
    kept = []
    gathered = {}
    moment_halves = []

    for step in range(ROLL):
        shift1, scale1, gate1, shift2, scale2, gate2 = jnp.split(modul[step][None], 6, -1)
        state_low = state.astype(LOW)
        embedded = product(state_low, io_all[0]) + embed_bias + pos
        normed_one, inverse_one = layer_norm(embedded)
        normed_a = (normed_one * (1.0 + scale1) + shift1).astype(LOW)
        qkv_rows = product(normed_a, w_qkv).astype(LOW)
        moves = Moves(f"attend{step}", ids, 48 * 2**20)
        qkv_out = moves.output((3, local * seq_count, width // seq_count), LOW, pltpu.VMEM)
        mixed_out = moves.output((local, width), LOW, pltpu.VMEM)
        arrivals = moves.rows_to_heads(PATCHES, qkv_rows, 3, qkv_out)
        waiting = moves.gather_pairs(normed_a, hold=True)
        waiting += moves.gather_pairs(state_low, hold=True)
        if step:
            waiting += moves.gather_pairs(kept[-1][5], hold=True)
        add_attention(moves, qkv_out, mixed_out, arrivals, local, members, waiting)
        qkv, mixed, gathered_a, gathered_state, *gathered_mixed = moves.run()
        gathered.setdefault("a", {})[step] = gathered_a
        gathered.setdefault("state", {})[step] = gathered_state
        if step:
            gathered["mixed"] = {step - 1: gathered_mixed[0]}
        attended = product(mixed, w_out)
        after_attn = embedded + gate1 * attended
        normed_two, inverse_two = layer_norm(after_attn)
        normed_b = (normed_two * (1.0 + scale2) + shift2).astype(LOW)
        moves = Moves("tokens_moment", ids)
        moves.gather_pairs(normed_b, 2)
        moves.exchange(PATCHES, moment_parts[:, step * half_rows : (step + 1) * half_rows])
        tokens_b, moment_half = moves.run()
        moment_halves.append(moment_half)
        tokens_b = tokens_b.reshape(shards * local, width)
        upward = product(tokens_b, up_copy)
        hidden = jax.nn.gelu(upward).astype(LOW)
        down_part = contract(hidden, down_copy, 1, 1).astype(LOW).reshape(shards, local, width)
        moves = Moves("token_sums", ids)
        moves.exchange(SHARDS, down_part)
        downward = jnp.sum(moves.run()[0].astype(f32), 0)
        after_mlp = after_attn + gate2 * downward
        normed_three, inverse_three = layer_norm(after_mlp)
        normed_c = normed_three.astype(LOW)
        delta = contract(normed_c, io_all[1], 1, 1)
        kept.append(
            (
                state_low,
                normed_one,
                inverse_one,
                normed_a,
                qkv,
                mixed,
                attended,
                normed_two,
                inverse_two,
                tokens_b,
                upward,
                hidden,
                downward,
                normed_three,
                inverse_three,
                normed_c,
            )
        )
        state = state + (step < length).astype(f32) * delta

    lat = latitude_weights(local)
    diff = state - jnp.pad(targets[0].astype(f32), value_pad)
    loss_local = weight * jnp.sum(jnp.sum(diff * diff, -1) * lat)
    grad_state = 2.0 * weight * lat[:, None] * diff

    back = [None] * ROLL
    mlp_back = []

    def patch_sum(item, cols):
        mine = lax.dynamic_slice_in_dim(item, member * cols, cols, 1)
        low = item.astype(LOW)
        for shift in range(1, members):
            pairs = [
                (index, index // members * members + (index + shift) % members) for index in range(seq_count)
            ]
            to_member = lax.rem(member + shift, members)
            outgoing = lax.dynamic_slice_in_dim(low, to_member * cols, cols, 1)
            mine = mine + lax.ppermute(outgoing, PATCHES, pairs).astype(f32)
        return mine

    for step in reversed(range(ROLL)):
        (
            state_low,
            normed_one,
            inverse_one,
            normed_a,
            qkv,
            mixed,
            attended,
            normed_two,
            inverse_two,
            tokens_b,
            upward,
            hidden,
            downward,
            normed_three,
            inverse_three,
            normed_c,
        ) = kept[step]
        shift1, scale1, gate1, shift2, scale2, gate2 = jnp.split(modul[step][None], 6, -1)
        delta_grad = ((step < length).astype(f32) * grad_state).astype(LOW)
        grad_mlp = norm_back(product(delta_grad, io_all[1]), normed_three, inverse_three)
        grad_gate2 = jnp.sum(grad_mlp * downward, 0)
        moves = Moves("tokens", ids)
        moves.gather_pairs((gate2 * grad_mlp).astype(LOW), 2)
        tokens_down = moves.run()[0].reshape(shards * local, width)
        grad_hidden = product(tokens_down, down_copy)
        up_grad = jax.vjp(jax.nn.gelu, upward)[1](grad_hidden)[0].astype(LOW)
        mlp_back.append((tokens_b, up_grad, tokens_down, hidden))
        if step == 0:
            all_b, all_up, all_down, all_hidden = [jnp.concatenate(items, 0) for items in zip(*mlp_back)]
            mlp_sums = [
                patch_sum(rows_product(left, right), cols)
                for left, right, cols in ((all_b, all_up, group_cols[1]), (all_down, all_hidden, group_cols[2]))
            ]
        up_part = contract(up_grad, up_copy, 1, 1).astype(LOW).reshape(shards, local, width)
        moves = Moves("token_sums", ids)
        moves.exchange(SHARDS, up_part)
        grad_normed_b = jnp.sum(moves.run()[0].astype(f32), 0)
        grad_scale2 = jnp.sum(grad_normed_b * normed_two, 0)
        grad_shift2 = jnp.sum(grad_normed_b, 0)
        grad_attn = grad_mlp + norm_back(grad_normed_b * (1.0 + scale2), normed_two, inverse_two)
        grad_gate1 = jnp.sum(grad_attn * attended, 0)
        attn_grad = (gate1 * grad_attn).astype(LOW)
        mixed_grad = contract(attn_grad, w_out, 1, 1).astype(LOW)
        moves = Moves(f"attend_back{step}", ids, 48 * 2**20)
        grads_in = moves.scratch((1, local * seq_count, width // seq_count), LOW)
        result = moves.output((local, 3 * width), LOW, pltpu.VMEM)
        arrivals = moves.rows_to_heads(PATCHES, mixed_grad, 1, grads_in)
        names = ["attn", "c", "delta"]
        moves.exchange_columns(SHARDS, attn_grad)
        moves.exchange_columns(SHARDS, normed_c)
        waiting = moves.gather_pairs(delta_grad, hold=True)
        if step == ROLL - 1:
            waiting += moves.gather_pairs(mixed, hold=True)
            names.append("mixed")
        else:
            moves.exchange_columns(SHARDS, back[step + 1][0])
            moves.exchange_columns(SHARDS, back[step + 1][1])
            names += ["qkv", "embed"]
        add_attention_back(
            moves, moves.operand(qkv, pltpu.VMEM), grads_in, result, arrivals, local, members, waiting
        )
        qkv_grad, *others = moves.run()
        for name, item in zip(names, others):
            gathered.setdefault(name, {})[step + (name in ("qkv", "embed"))] = item
        grad_normed_a = contract(qkv_grad, w_qkv, 1, 1)
        grad_scale1 = jnp.sum(grad_normed_a * normed_one, 0)
        grad_shift1 = jnp.sum(grad_normed_a, 0)
        grad_embedded = grad_attn + norm_back(grad_normed_a * (1.0 + scale1), normed_one, inverse_one)
        embed_grad = grad_embedded.astype(LOW)
        grad_state = grad_state + contract(embed_grad, io_all[0], 1, 1)
        grad_modul = jnp.concatenate([grad_shift1, grad_scale1, grad_gate1, grad_shift2, grad_scale2, grad_gate2])
        back[step] = (qkv_grad, embed_grad, grad_modul, jnp.sum(grad_embedded, 0))

    qkv_grad, embed_grad, _, _ = back[0]
    mlp_low = [item.astype(LOW) for item in mlp_sums]
    modul_parts = jnp.stack([item[2].reshape(shards, ada_cols) for item in back], 1)
    embed_parts = sum(item[3] for item in back).reshape(shards, 1, -1)
    vectors = jnp.concatenate(
        [modul_parts, jnp.pad(embed_parts, ((0, 0), (0, 0), (0, ada_cols - embed_parts.shape[-1])))], 1
    )

    def to_group(moves, item, which, start, size):
        source = moves.operand(item)
        target = moves.output((MATRICES - 1, size, item.shape[1]), LOW)
        for shift in range(1, MATRICES):
            moves.move(
                (PATCHES, seq_count, shift),
                functools.partial(group_peer, members, shift),
                source,
                lambda: (pl.ds(start, size),),
                target,
                lambda shift=shift: (shift - 1,),
                sends=lambda shift=shift: lax.axis_index(PATCHES) // members == (which - shift) % MATRICES,
                takes=lambda: lax.axis_index(PATCHES) // members == which,
            )

    block_rows = qkv_copy.shape[0]
    early = (1, 2)
    first_rows = block_rows * 7 // 16
    moves = Moves("samples", ids)
    moves.exchange_columns(SHARDS, qkv_grad)
    moves.exchange_columns(SHARDS, embed_grad)
    moves.exchange(SHARDS, vectors)
    for item, which in zip(mlp_low, early):
        to_group(moves, item, which, 0, first_rows)
    gathered["qkv"][0], gathered["embed"][0], vectors, *mlp_first = moves.run()
    grad_pos = sum(jnp.sum(item.astype(f32), 0) for item in gathered["embed"].values())

    def from_all(left, right):
        both = [
            jnp.concatenate([gathered[name][step].reshape(shards * local, -1) for step in range(ROLL)], 0)
            for name in (left, right)
        ]
        return rows_product(*both)

    io_here = jnp.stack([from_all("state", "embed"), from_all("delta", "c")])
    io_cols = io_here.shape[-1]
    grads_here = [from_all("a", "qkv"), from_all("mixed", "attn")]
    late = (0, MATRICES - 1)

    moves = Moves("member_sums", ids)
    for item, which in zip(grads_here, late):
        cols = group_cols[which]
        source = moves.operand(item.astype(LOW))
        target = moves.output((members - 1, item.shape[0], cols), LOW)
        for shift in range(1, members):

            def source_at(shift=shift, cols=cols):
                to_member = lax.rem(lax.rem(lax.axis_index(PATCHES), members) + shift, members)
                return (slice(None), pl.ds(pl.multiple_of(to_member * cols, LANES), cols))

            moves.move(
                (PATCHES, members, shift),
                functools.partial(member_peer, members, shift),
                source,
                source_at,
                target,
                lambda shift=shift: (shift - 1,),
            )
    modul_here, embed_here = vectors[:, :ROLL].reshape(-1), jnp.sum(vectors[:, ROLL, : width // shards], 0)
    flat = jnp.concatenate([modul_here, embed_here]).astype(LOW)
    flat_rows = round_up(flat.size, 16 * LANES) // LANES
    moves.gather(PATCHES, jnp.pad(flat, (0, flat_rows * LANES - flat.size)).reshape(flat_rows, LANES))
    moves.exchange(PATCHES, io_here.reshape(seq_count, -1, io_cols).astype(LOW))
    for item, which in zip(mlp_low, early):
        to_group(moves, item, which, first_rows, block_rows - first_rows)
    *halves, vectors, io_parts, up_rest, down_rest = moves.run()
    mlp_sums = [
        mine + jnp.concatenate([jnp.sum(part.astype(f32), 0) for part in parts], 0)
        for mine, *parts in zip(mlp_sums, mlp_first, (up_rest, down_rest))
    ]
    vectors = jnp.sum(vectors.astype(f32), 0).reshape(-1)
    io_slice = jnp.sum(io_parts.astype(f32), 0)
    late_sums = [
        lax.dynamic_slice_in_dim(item, member * group_cols[which], group_cols[which], 1)
        + jnp.sum(half.astype(f32), 0)
        for item, half, which in zip(grads_here, halves, late)
    ]
    modul_all = vectors[: modul_here.size].reshape(-1, ada_cols)
    bias_part = jnp.concatenate([jnp.sum(modul_all, 0), vectors[modul_here.size : flat.size]])
    silu_part = lax.dot_general(
        modul_all, ada_copy.astype(f32), (((1,), (1,)), ((), ())), precision=HIGHEST_PRECISION
    )

    moves = Moves("group_sums", ids)
    moves.vmem = 32 * 2**20
    to_group(moves, late_sums[1].astype(LOW), late[1], 0, block_rows)

    def has_source():
        return lax.axis_index(PATCHES) // members < MATRICES - 1

    def is_source():
        return lax.axis_index(PATCHES) // members > 0

    chain = late_sums[0]
    mine = moves.operand(chain, pltpu.VMEM)
    chain_total = moves.output(chain.shape, f32, pltpu.VMEM)
    arriving, leaving = moves.scratch(chain.shape, LOW), moves.scratch(chain.shape, LOW)
    chunk = block_rows // CHAIN_CHUNKS
    for part in range(CHAIN_CHUNKS):
        place = (pl.ds(part * chunk, chunk),)
        number = moves.move(
            (PATCHES, seq_count, MATRICES - 1),
            functools.partial(group_peer, members, MATRICES - 1),
            leaving,
            lambda place=place: place,
            arriving,
            lambda place=place: place,
            sends=is_source,
            takes=has_source,
            later=True,
        )

        def add(ref, place=place):
            def with_arriving():
                ref(chain_total)[place] = ref(mine)[place] + ref(arriving)[place].astype(f32)

            def alone():
                ref(chain_total)[place] = ref(mine)[place]

            pl.when(has_source())(with_arriving)
            pl.when(jnp.logical_not(has_source()))(alone)
            ref(leaving)[place] = ref(chain_total)[place].astype(LOW)

        moves.wait_for(number)
        moves.task(add)
        moves.start(number)
    moves.gather(SHARDS, silu_part)
    moves.gather(SHARDS, bias_part[None])
    out_parts, chain, silu_parts, bias_parts = moves.run()
    late_sums = [widen(chain), widen(late_sums[1] + jnp.sum(out_parts.astype(f32), 0))]
    grad_group = jnp.where(
        group == late[0],
        late_sums[0],
        jnp.where(group == late[1], late_sums[1], widen(jnp.where(group == early[0], *mlp_sums))),
    )
    grad_silu = jnp.sum(silu_parts, 0)
    grad_cond = jax.vjp(jax.nn.silu, cond_vec)[1](grad_silu)[0]
    grad_table_all = lax.dot_general(select, grad_cond, (((0,), (0,)), ((), ())), precision=HIGHEST_PRECISION)
    grad_table = lax.dynamic_slice_in_dim(grad_table_all, shard * table_cols, table_cols, 1)
    bias_parts = bias_parts[:, 0]
    grad_bias_all = jnp.concatenate([bias_parts[:, :ada_cols].reshape(-1), bias_parts[:, ada_cols:].reshape(-1)])
    grad_bias = lax.dynamic_slice_in_dim(grad_bias_all, shard * biases.shape[0], biases.shape[0])
    silu_rows = lax.dynamic_slice_in_dim(silu_low, seq_index * ada_master.shape[0], ada_master.shape[0], 1)
    grad_ada = lax.dot_general(
        silu_rows.astype(f32), modul_all, (((0,), (0,)), ((), ())), precision=HIGHEST_PRECISION
    )

    moment_group = jnp.concatenate(moment_halves, 1).reshape(-1, most_cols).astype(f32)
    grad_squares = jnp.sum(grad_group * grad_group)
    squares = (
        grad_squares
        + jnp.sum(grad_ada * grad_ada)
        + jnp.sum(io_slice * io_slice)
        + jnp.sum(grad_pos * grad_pos)
        + (seq_index == 0).astype(f32) * (jnp.sum(grad_table * grad_table) + jnp.sum(grad_bias * grad_bias))
    )
    lane = jnp.arange(LANES, dtype=jnp.int32)
    place = 2 + 3 * group
    entries = jnp.where(lane == 0, squares, 0.0) + jnp.where(lane == 1, loss_local, 0.0)
    entries = entries + jnp.where(lane == place, jnp.sum(moment_group * moment_group), 0.0)
    entries = entries + jnp.where(lane == place + 1, jnp.sum(moment_group * grad_group), 0.0)
    entries = entries + jnp.where(lane == place + 2, grad_squares, 0.0)
    sums, io_slices = total_of(ids, jnp.broadcast_to(entries[None], (8, LANES)), io_slice.astype(LOW))
    sums = sums[0]
    grad_norm = jnp.sqrt(sums[0])
    loss_total = sums[1]
    clip = jnp.minimum(1.0, CLIP_LIMIT / (grad_norm + 1e-06))
    terms = sums[2 : 2 + 3 * MATRICES].reshape(MATRICES, 3)
    size_squares = MOMENTUM * MOMENTUM * terms[:, 0] + 2.0 * MOMENTUM * clip * terms[:, 1] + clip * clip * terms[:, 2]
    sizes = jnp.sqrt(jnp.maximum(size_squares, 0.0))
    moment_sizes = sizes[jnp.array([0, 3, 1, 2])] / CLIP_LIMIT
    my_size = lax.dynamic_slice_in_dim(sizes, group, 1)[0]
    block = ((MOMENTUM * moment_group + clip * grad_group) / (my_size + 1e-07)).astype(LOW)

    moves = Moves("muon", ids, 56 * 2**20)
    source = moves.operand(block, pltpu.VMEM)
    full, low = (block_rows, block_rows), (block_rows, most_cols)
    update = moves.output((seq_count, block_rows // seq_count, most_cols), LOW, pltpu.VMEM)
    target = moves.scratch((members * shards,) + low, LOW)
    gram, poly, once = [moves.scratch(full, f32) for _ in range(3)]
    gram_low, poly_low, once_low = [moves.scratch(full, LOW) for _ in range(3)]
    state, state_next = [moves.scratch(low, LOW) for _ in range(2)]
    pairs = shards // 2

    def slot(back_member, back_pair, part=None):
        who_member = lax.rem(lax.rem(lax.axis_index(PATCHES), members) + members - back_member, members)
        who_shard = lax.rem(lax.axis_index(SHARDS) + shards - 2 * back_pair, shards)
        index = who_member * shards + who_shard
        return (index,) if part is None else (index, pl.ds(part * block_rows // 2, block_rows // 2))

    def add_gram(place):
        def action(ref):
            (index,) = place()

            @pl.loop(0, block_rows // GRAM_COLS)
            def _(tile):
                cols = pl.ds(pl.multiple_of(tile * GRAM_COLS, GRAM_COLS), GRAM_COLS)
                ref(gram)[:, cols] += contract(ref(target)[index], ref(target)[index, cols, :], 1, 1)

        return action

    def start_gram(ref):
        @pl.loop(0, block_rows // GRAM_COLS)
        def _(tile):
            cols = pl.ds(pl.multiple_of(tile * GRAM_COLS, GRAM_COLS), GRAM_COLS)
            ref(gram)[:, cols] = contract(ref(source)[...], ref(source)[cols, :], 1, 1)

    def pair_peer(shift):
        return {SHARDS: lax.rem(lax.axis_index(SHARDS) + 2 * shift, shards)}

    slot_own = functools.partial(slot, 0, 0)
    by_member = {
        shift: moves.move(
            (PATCHES, members, shift), functools.partial(member_peer, members, shift), source, None, target, slot_own
        )
        for shift in range(1, members)
    }
    by_pair = {
        shift: moves.move((SHARDS, 2 * shift), functools.partial(pair_peer, shift), source, None, target, slot_own)
        for shift in range(1, pairs)
    }
    from_sibling = [(moves.move((SHARDS,), sibling_peer, source, None, target, slot_own), slot_own)]
    moves.task(start_gram)

    def sibling_place(place):
        def at():
            (index,) = place()
            return (index + 1 - 2 * lax.rem(index, 2),)

        return at

    def hand_on(place, arrivals):
        if len(arrivals) == 1:
            parts = [(place, arrivals[0])]
        else:
            parts = [(functools.partial(place, part), number) for part, number in enumerate(arrivals)]
        numbers = [
            moves.move((SHARDS,), sibling_peer, target, at, target, at, (number,)) for at, number in parts
        ]
        from_sibling.append((numbers, place))
        moves.task(add_gram(place))

    across = []
    for shift_member, first in by_member.items():
        for shift_pair, second in by_pair.items():
            top = functools.partial(slot, shift_member, 0, 0)
            bottom = functools.partial(slot, 0, shift_pair, 1)
            halves = [
                moves.move(
                    (SHARDS, 2 * shift_pair),
                    functools.partial(pair_peer, shift_pair),
                    target,
                    top,
                    target,
                    top,
                    (first,),
                ),
                moves.move(
                    (PATCHES, members, shift_member),
                    functools.partial(member_peer, members, shift_member),
                    target,
                    bottom,
                    target,
                    bottom,
                    (second,),
                ),
            ]
            across.append((functools.partial(slot, shift_member, shift_pair), halves))
    for shift, number in by_member.items():
        hand_on(functools.partial(slot, shift, 0), [number])
    for shift, number in by_pair.items():
        hand_on(functools.partial(slot, 0, shift), [number])
    moves.wait_for(from_sibling[0][0])
    moves.task(add_gram(sibling_place(slot_own)))
    for place, halves in across:
        hand_on(place, halves)
    for numbers, place in from_sibling[1:]:
        for number in numbers:
            moves.wait_for(number)
        moves.task(add_gram(sibling_place(place)))

    for number in moves.exchange(PATCHES, grad_group.astype(LOW).reshape(seq_count, -1, most_cols), later=True):
        moves.start(number)
    moves.task(
        lambda ref: newton_schulz(
            *[ref(item) for item in (source, gram, poly, once, gram_low, poly_low, once_low, state, state_next)]
        )
    )

    def row_part(shift):
        there = lax.rem(lax.axis_index(PATCHES) + shift, seq_count)
        size = block_rows // seq_count
        return (pl.ds(pl.multiple_of(there * size, size), size),)

    for shift in range(1, seq_count):
        moves.start(
            moves.move(
                (PATCHES, shift),
                lambda shift=shift: {PATCHES: lax.rem(lax.axis_index(PATCHES) + shift, seq_count)},
                state,
                functools.partial(row_part, shift),
                update,
                lambda: (lax.axis_index(PATCHES),),
                later=True,
            )
        )

    def keep_rows(ref):
        ref(update)[lax.axis_index(PATCHES)] = ref(state)[row_part(0)]

    moves.task(keep_rows)
    update, grad_rows = moves.run()

    def rows_of(which, parts):
        return jnp.concatenate(
            [parts[which * members + part][:, : group_cols[which]] for part in range(members)], -1
        ).astype(f32)

    moments = [MOMENTUM * old + clip * rows_of(which, grad_rows) for which, old in enumerate(momenta)]
    fresh = [
        master * (1.0 - RATE_MUON * DECAY_MUON)
        - RATE_MUON * 0.2 * math.sqrt(master.shape[1] * shards) * rows_of(which, update)
        for which, master in enumerate(masters)
    ]

    moves = Moves("copies", ids)
    rows = qkv_master.shape[0]

    def row_place(back_group):
        who = lax.axis_index(PATCHES) - back_group * members
        return (pl.ds(pl.multiple_of(who * rows, rows), rows),)

    def has_group(offset):
        place = lax.axis_index(PATCHES) // members + offset
        return jnp.logical_and(place >= 0, place < MATRICES)

    def member_copies(source, source_at, target, target_at, after, there):
        for shift in range(1, members):
            moves.move(
                (PATCHES, members, shift),
                functools.partial(member_peer, members, shift),
                source,
                source_at,
                target,
                target_at,
                after,
                there,
                there,
            )

    places = []
    for item in fresh:
        source = moves.operand(item.astype(LOW))
        target = moves.output((rows * seq_count, item.shape[1]), LOW)
        own = functools.partial(row_place, 0)
        moves.keep(source, None, target, own)
        places.append((source, target, {}))

    def along_line(distance, way, source, target, numbers):
        both = lambda: jnp.logical_and(has_group(way), has_group(-distance * way))
        place = functools.partial(row_place, distance * way)
        numbers[way] = moves.move(
            (PATCHES, seq_count, way),
            functools.partial(group_peer, members, (MATRICES + way) % MATRICES),
            target if distance else source,
            place if distance else None,
            target,
            place,
            (numbers[way],) if distance else (),
            both,
            functools.partial(has_group, -(distance + 1) * way),
        )

    for source, target, numbers in places:
        for way in (1, -1):
            along_line(0, way, source, target, numbers)
    for source, target, numbers in places:
        member_copies(source, None, target, own, (), None)
    for distance in range(1, MATRICES):
        for source, target, numbers in places:
            for way in (1, -1):
                number = numbers[way]
                if distance < MATRICES - 1:
                    along_line(distance, way, source, target, numbers)
                place = functools.partial(row_place, distance * way)
                member_copies(
                    target, place, target, place, (number,), functools.partial(has_group, -distance * way)
                )
    copies = moves.run()

    io_grad = io_slices.reshape(2, padded, io_cols)[:, :values_count].astype(f32)
    ada_res = adam_update(ada_master, ada_first, ada_second, clip * grad_ada, RATE_ADAM)
    io_res = adam_update(io_proj, io_first, io_second, clip * io_grad, RATE_ADAM)
    cond_res = adam_update(cond_table, cond_first, cond_second, clip * grad_table, RATE_TABLE)
    pos_res = adam_update(pos_table, pos_first, pos_second, clip * grad_pos, RATE_TABLE)
    bias_res = adam_update(biases, bias_first, bias_second, clip * grad_bias, RATE_ADAM)
    matrices = []
    for which in (0, 3, 1, 2):
        matrices += [fresh[which], moments[which], copies[which]]
    return (loss_total, grad_norm, moment_sizes, *matrices, *ada_res, *io_res, *cond_res, *pos_res, *bias_res)


def fits_fast(mesh):
    seq, shards = mesh.shape[PATCHES], mesh.shape[SHARDS]
    return HEADS % seq == 0 and (HEADS // seq * HEAD) % LANES == 0 and seq % MATRICES == 0 and shards % 2 == 0


def solution(mesh):
    body = fast_body if fits_fast(mesh) else general_body
    return jax.shard_map(
        body,
        mesh=mesh,
        in_specs=(
            P(SHARDS, PATCHES, None),
            P(SHARDS, PATCHES, None),
            P(SHARDS),
            P(),
            P(None, SHARDS),
            P(PATCHES, SHARDS),
            P(PATCHES, SHARDS),
            P(None, SHARDS),
            P(PATCHES, SHARDS),
            P(PATCHES, SHARDS),
            P(None, SHARDS),
            P(PATCHES, SHARDS),
            P(PATCHES, SHARDS),
            P(None, SHARDS),
            P(PATCHES, SHARDS),
            P(PATCHES, SHARDS),
            P(None, SHARDS),
            P(PATCHES, SHARDS),
            P(PATCHES, SHARDS),
            P(PATCHES, SHARDS),
            P(None, None, SHARDS),
            P(None, None, SHARDS),
            P(None, None, SHARDS),
            P(None, SHARDS),
            P(None, SHARDS),
            P(None, SHARDS),
            P(PATCHES, SHARDS),
            P(PATCHES, SHARDS),
            P(PATCHES, SHARDS),
            P(SHARDS),
            P(SHARDS),
            P(SHARDS),
        ),
        out_specs=(
            P(),
            P(),
            P(),
            P(PATCHES, SHARDS),
            P(PATCHES, SHARDS),
            P(None, SHARDS),
            P(PATCHES, SHARDS),
            P(PATCHES, SHARDS),
            P(None, SHARDS),
            P(PATCHES, SHARDS),
            P(PATCHES, SHARDS),
            P(None, SHARDS),
            P(PATCHES, SHARDS),
            P(PATCHES, SHARDS),
            P(None, SHARDS),
            P(PATCHES, SHARDS),
            P(PATCHES, SHARDS),
            P(PATCHES, SHARDS),
            P(None, None, SHARDS),
            P(None, None, SHARDS),
            P(None, None, SHARDS),
            P(None, SHARDS),
            P(None, SHARDS),
            P(None, SHARDS),
            P(PATCHES, SHARDS),
            P(PATCHES, SHARDS),
            P(PATCHES, SHARDS),
            P(SHARDS),
            P(SHARDS),
            P(SHARDS),
        ),
        check_vma=False,
    )
```

```python
import functools
import math

import jax
import jax.numpy as jnp
from jax import lax
from jax.experimental import pallas as pl
from jax.experimental.pallas import tpu as pltpu
from jax.sharding import PartitionSpec as P

PATCHES = "seq"
SHARDS = "fsdp"
HEADS = 16
HEAD = 64
NI = 3
ROLL = 2
NS_ITERS = 5
STEP_NUM = 10
LON = 32


EPS_NORM = 1e-06
NS_A = 3.4445
NS_B = -4.775
NS_C = 2.0315
MOMENTUM = 0.5
RATE_MUON = 0.15
DECAY_MUON = 0.1
RATE_ADAM = 0.05
RATE_TABLE = 0.5
DECAY_ADAM = 0.1
BETA_FIRST = 0.9
BETA_SECOND = 0.95
CLIP_LIMIT = 0.01
HIGHEST_PRECISION = lax.Precision.HIGHEST


def broadcast(block, axis, owner):
    block = jnp.where(lax.axis_index(axis) == owner, block, jnp.zeros_like(block))
    return lax.psum(block, axis)


def product(left, right):
    return jnp.dot(left, right, preferred_element_type=jnp.float32)


def dot_last(left, right):
    return lax.dot_general(
        left, right, (((left.ndim - 1,), (1,)), ((), ())), preferred_element_type=jnp.float32
    )


def rows_product(left, right):
    flat_left = left.reshape(-1, left.shape[-1])
    flat_right = right.reshape(-1, right.shape[-1])
    return lax.dot_general(
        flat_left, flat_right, (((0,), (0,)), ((), ())), preferred_element_type=jnp.float32
    )


def layer_norm(values):
    centred = values - jnp.mean(values, -1, keepdims=True)
    inverse = lax.rsqrt(jnp.mean(centred * centred, -1, keepdims=True) + EPS_NORM)
    return (centred * inverse, inverse)


def norm_back(grad, normed, inverse):
    return inverse * (
        grad
        - jnp.mean(grad, -1, keepdims=True)
        - normed * jnp.mean(grad * normed, -1, keepdims=True)
    )


def heads_view(values):
    return values.reshape(values.shape[0], values.shape[1], HEADS, HEAD)


def modulation(modul, width):
    return [modul[:, None, column * width : (column + 1) * width] for column in range(6)]


def latitude_weights(local):
    all_patches = local * lax.axis_size(PATCHES)
    band_row = (jnp.arange(all_patches, dtype=jnp.int32) // LON).astype(jnp.float32)
    latitude = (band_row + 0.5) * (math.pi / (all_patches // LON)) - math.pi / 2
    cosine = jnp.cos(latitude)
    weights = cosine / jnp.mean(cosine)
    return lax.dynamic_slice_in_dim(weights, lax.axis_index(PATCHES) * local, local)


def forward_step(weights, state, active, select):
    w_qkv, w_out, w_up, w_down, w_ada, io_all, table, pos, bias = weights
    width = w_out.shape[0]
    cond_vec = jnp.dot(select, table.astype(jnp.float32), precision=HIGHEST_PRECISION)
    silu_low = jax.nn.silu(cond_vec).astype(jnp.bfloat16)
    modul = product(silu_low, w_ada) + bias[: 6 * width].astype(jnp.float32)
    shift1, scale1, gate1, shift2, scale2, gate2 = modulation(modul, width)
    state_low = state.astype(jnp.bfloat16)
    embedded = (
        product(state_low, io_all[0])
        + bias[6 * width :].astype(jnp.float32)
        + pos.astype(jnp.float32)
    )
    normed_one, inverse_one = layer_norm(embedded)
    normed_a = (normed_one * (1.0 + scale1) + shift1).astype(jnp.bfloat16)
    qkv = product(normed_a, w_qkv).astype(jnp.bfloat16)
    queries = qkv[..., :width]
    keys, values = (
        lax.all_gather(qkv[..., width : 2 * width], PATCHES, axis=1, tiled=True),
        lax.all_gather(qkv[..., 2 * width :], PATCHES, axis=1, tiled=True),
    )
    scores = jnp.einsum(
        "sphd,snhd->shpn", heads_view(queries), heads_view(keys), preferred_element_type=jnp.float32
    ) * HEAD ** (-0.5)
    top_score = jnp.max(scores, -1, keepdims=True)
    expo = jnp.exp(scores - top_score)
    total_exp = jnp.sum(expo, -1, keepdims=True)
    log_total = top_score + jnp.log(total_exp)
    probs_low = (expo / total_exp).astype(jnp.bfloat16)
    mixed = jnp.einsum(
        "shpn,snhd->sphd", probs_low, heads_view(values), preferred_element_type=jnp.float32
    )
    mixed_low = mixed.reshape(queries.shape).astype(jnp.bfloat16)
    attended = product(mixed_low, w_out)
    after_attn = embedded + gate1 * attended
    normed_two, inverse_two = layer_norm(after_attn)
    normed_b = (normed_two * (1.0 + scale2) + shift2).astype(jnp.bfloat16)
    upward = product(normed_b, w_up)
    hidden = jax.nn.gelu(upward).astype(jnp.bfloat16)
    downward = dot_last(hidden, w_down)
    after_mlp = after_attn + gate2 * downward
    normed_three, inverse_three = layer_norm(after_mlp)
    normed_c = normed_three.astype(jnp.bfloat16)
    delta = dot_last(normed_c, io_all[1])
    kept = (
        cond_vec,
        silu_low,
        modul,
        state_low,
        normed_one,
        inverse_one,
        normed_a,
        queries,
        keys,
        values,
        log_total,
        mixed_low,
        attended,
        normed_two,
        inverse_two,
        normed_b,
        upward,
        hidden,
        downward,
        normed_three,
        inverse_three,
        normed_c,
    )
    return (state + active * delta, kept)


def backward_step(weights, kept, grad_state, active, select):
    w_qkv, w_out, w_up, w_down, w_ada, io_all, table, pos, bias = weights
    (
        cond_vec,
        silu_low,
        modul,
        state_low,
        normed_one,
        inverse_one,
        normed_a,
        queries,
        keys,
        values,
        log_total,
        mixed_low,
        attended,
        normed_two,
        inverse_two,
        normed_b,
        upward,
        hidden,
        downward,
        normed_three,
        inverse_three,
        normed_c,
    ) = kept
    width = w_out.shape[0]
    shift1, scale1, gate1, shift2, scale2, gate2 = modulation(modul, width)
    delta_grad = (active * grad_state).astype(jnp.bfloat16)
    grad_head = rows_product(delta_grad, normed_c)
    grad_mlp = norm_back(product(delta_grad, io_all[1]), normed_three, inverse_three)
    grad_gate2 = jnp.sum(grad_mlp * downward, 1)
    down_grad = (gate2 * grad_mlp).astype(jnp.bfloat16)
    grad_down = rows_product(down_grad, hidden)
    grad_hidden = product(down_grad, w_down)
    up_grad = jax.vjp(jax.nn.gelu, upward)[1](grad_hidden)[0].astype(jnp.bfloat16)
    grad_up = rows_product(normed_b, up_grad)
    grad_normed_b = dot_last(up_grad, w_up)
    grad_scale2 = jnp.sum(grad_normed_b * normed_two, 1)
    grad_shift2 = jnp.sum(grad_normed_b, 1)
    grad_attn = grad_mlp + norm_back(grad_normed_b * (1.0 + scale2), normed_two, inverse_two)
    grad_gate1 = jnp.sum(grad_attn * attended, 1)
    attn_grad = (gate1 * grad_attn).astype(jnp.bfloat16)
    grad_out = rows_product(mixed_low, attn_grad)
    mixed_grad = dot_last(attn_grad, w_out).astype(jnp.bfloat16)
    q_heads = heads_view(queries)
    k_heads = heads_view(keys)
    v_heads = heads_view(values)
    g_heads = heads_view(mixed_grad)
    scores = jnp.einsum(
        "sphd,snhd->shpn", q_heads, k_heads, preferred_element_type=jnp.float32
    ) * HEAD ** (-0.5)
    probs = jnp.exp(scores - log_total)
    probs_low = probs.astype(jnp.bfloat16)
    grad_probs = jnp.einsum("sphd,snhd->shpn", g_heads, v_heads, preferred_element_type=jnp.float32)
    score_grad = (
        HEAD ** (-0.5) * probs * (grad_probs - jnp.sum(grad_probs * probs, -1, keepdims=True))
    ).astype(jnp.bfloat16)
    grad_queries = jnp.einsum(
        "shpn,snhd->sphd", score_grad, k_heads, preferred_element_type=jnp.float32
    ).reshape(queries.shape)
    key_part = jnp.einsum(
        "shpn,sphd->snhd", score_grad, q_heads, preferred_element_type=jnp.float32
    ).reshape(keys.shape)
    value_part = jnp.einsum(
        "shpn,sphd->snhd", probs_low, g_heads, preferred_element_type=jnp.float32
    ).reshape(values.shape)
    grad_keys, grad_values = (
        lax.psum_scatter(key_part, PATCHES, scatter_dimension=1, tiled=True),
        lax.psum_scatter(value_part, PATCHES, scatter_dimension=1, tiled=True),
    )
    qkv_grad = jnp.concatenate([grad_queries, grad_keys, grad_values], -1).astype(jnp.bfloat16)
    grad_qkv = rows_product(normed_a, qkv_grad)
    grad_normed_a = dot_last(qkv_grad, w_qkv)
    grad_scale1 = jnp.sum(grad_normed_a * normed_one, 1)
    grad_shift1 = jnp.sum(grad_normed_a, 1)
    grad_embedded = grad_attn + norm_back(grad_normed_a * (1.0 + scale1), normed_one, inverse_one)
    embed_grad = grad_embedded.astype(jnp.bfloat16)
    grad_embed = rows_product(state_low, embed_grad)
    grad_prev = grad_state + dot_last(embed_grad, io_all[0])
    grad_modul = jnp.concatenate(
        [grad_shift1, grad_scale1, grad_gate1, grad_shift2, grad_scale2, grad_gate2], -1
    )
    grad_ada = lax.dot_general(
        silu_low.astype(jnp.float32),
        grad_modul,
        (((0,), (0,)), ((), ())),
        precision=HIGHEST_PRECISION,
    )
    grad_silu = lax.dot_general(
        grad_modul, w_ada.astype(jnp.float32), (((1,), (1,)), ((), ())), precision=HIGHEST_PRECISION
    )
    grad_cond = jax.vjp(jax.nn.silu, cond_vec)[1](grad_silu)[0]
    grad_table = lax.dot_general(
        select, grad_cond, (((0,), (0,)), ((), ())), precision=HIGHEST_PRECISION
    )
    grad_bias = jnp.concatenate([jnp.sum(grad_modul, 0), jnp.sum(grad_embedded, (0, 1))])
    grad_pos = jnp.sum(grad_embedded, 0)
    grads = (
        grad_qkv,
        grad_out,
        grad_up,
        grad_down,
        grad_ada,
        jnp.stack([grad_embed, grad_head]),
        grad_table,
        grad_pos,
        grad_bias,
    )
    return (grad_prev, grads)


def gram_part(block_cols):
    return lax.dot_general(
        block_cols, block_cols, (((1,), (1,)), ((), ())), preferred_element_type=jnp.float32
    )


def zero_gram(block_cols):
    return jnp.zeros((block_cols.shape[0], block_cols.shape[0]), jnp.float32)


def newton_step(block_cols, gram):
    gram_low = gram.astype(jnp.bfloat16)
    poly = (NS_B * gram_low.astype(jnp.float32) + NS_C * product(gram_low, gram_low)).astype(
        jnp.bfloat16
    )
    return (NS_A * block_cols.astype(jnp.float32) + product(poly, block_cols)).astype(jnp.bfloat16)


def keep_block(block_cols, gram):
    return block_cols


def adam_update(weight, first, second, grad, rate):
    first_new = BETA_FIRST * first + (1.0 - BETA_FIRST) * grad
    second_new = BETA_SECOND * second + (1.0 - BETA_SECOND) * grad * grad
    unbiased = first_new / (1.0 - BETA_FIRST**STEP_NUM)
    spread = jnp.sqrt(second_new / (1.0 - BETA_SECOND**STEP_NUM)) + 1e-08
    return (weight * (1.0 - rate * DECAY_ADAM) - rate * unbiased / spread, first_new, second_new)


def general_body(
    states,
    targets,
    lengths,
    intervals,
    qkv_copy,
    qkv_master,
    qkv_moment,
    out_copy,
    out_master,
    out_moment,
    up_copy,
    up_master,
    up_moment,
    down_copy,
    down_master,
    down_moment,
    ada_copy,
    ada_master,
    ada_first,
    ada_second,
    io_proj,
    io_first,
    io_second,
    cond_table,
    cond_first,
    cond_second,
    pos_table,
    pos_first,
    pos_second,
    biases,
    bias_first,
    bias_second,
):
    weights = (
        lax.all_gather(qkv_copy, SHARDS, axis=1, tiled=True),
        lax.all_gather(out_copy, SHARDS, axis=1, tiled=True),
        lax.all_gather(up_copy, SHARDS, axis=1, tiled=True),
        lax.all_gather(down_copy, SHARDS, axis=1, tiled=True),
        lax.all_gather(ada_copy, SHARDS, axis=1, tiled=True),
        lax.all_gather(io_proj.astype(jnp.bfloat16), SHARDS, axis=2, tiled=True),
        lax.all_gather(cond_table.astype(jnp.bfloat16), SHARDS, axis=1, tiled=True),
        lax.all_gather(pos_table.astype(jnp.bfloat16), SHARDS, axis=1, tiled=True),
        lax.all_gather(biases.astype(jnp.bfloat16), SHARDS, axis=0, tiled=True),
    )
    samples, local, values_count = states.shape
    table_rows = cond_table.shape[0]
    my_ids = lax.dynamic_slice_in_dim(intervals, lax.axis_index(SHARDS) * samples, samples)
    counts = jnp.sum(
        (intervals[:, None] == jnp.arange(NI, dtype=jnp.int32)[None]).astype(jnp.float32), 0
    )
    id_counts = jnp.sum(
        (my_ids[:, None] == jnp.arange(NI, dtype=jnp.int32)[None]).astype(jnp.float32)
        * counts[None],
        1,
    )
    weight = 1.0 / (NI * local * lax.axis_size(PATCHES) * values_count * id_counts)
    rows_iota = jnp.arange(table_rows, dtype=jnp.int32)
    id_select = (my_ids[:, None] == rows_iota[None]).astype(jnp.float32)
    state = states.astype(jnp.float32)
    seen_states = []
    kept_all = []
    for step in range(ROLL):
        select = id_select + (rows_iota == NI + step).astype(jnp.float32)[None]
        active = (step < lengths).astype(jnp.float32)[:, None, None]
        seen_states.append(state)
        state, kept = forward_step(weights, state, active, select)
        kept_all.append(kept)
    lat = latitude_weights(local)
    diff = state - targets.astype(jnp.float32)
    err = jnp.sum(jnp.sum(diff * diff, -1) * lat[None], -1)
    loss_local = jnp.sum(weight * err)
    grad_state = 2.0 * weight[:, None, None] * lat[None, :, None] * diff
    totals = None
    for step in reversed(range(ROLL)):
        select = id_select + (rows_iota == NI + step).astype(jnp.float32)[None]
        active = (step < lengths).astype(jnp.float32)[:, None, None]
        kept = kept_all[step]
        grad_state, grads = backward_step(weights, kept, grad_state, active, select)
        totals = grads if totals is None else jax.tree.map(jnp.add, totals, grads)
    reduced = (
        lax.psum_scatter(totals[0], SHARDS, scatter_dimension=1, tiled=True),
        lax.psum_scatter(totals[1], SHARDS, scatter_dimension=1, tiled=True),
        lax.psum_scatter(totals[2], SHARDS, scatter_dimension=1, tiled=True),
        lax.psum_scatter(totals[3], SHARDS, scatter_dimension=1, tiled=True),
        lax.psum_scatter(totals[4], SHARDS, scatter_dimension=1, tiled=True),
        lax.psum_scatter(totals[5], SHARDS, scatter_dimension=2, tiled=True),
        lax.psum_scatter(totals[6], SHARDS, scatter_dimension=1, tiled=True),
        lax.psum_scatter(totals[7], SHARDS, scatter_dimension=1, tiled=True),
        lax.psum_scatter(totals[8], SHARDS, scatter_dimension=0, tiled=True),
    )
    large = (
        lax.psum_scatter(reduced[0], PATCHES, scatter_dimension=0, tiled=True),
        lax.psum_scatter(reduced[1], PATCHES, scatter_dimension=0, tiled=True),
        lax.psum_scatter(reduced[2], PATCHES, scatter_dimension=0, tiled=True),
        lax.psum_scatter(reduced[3], PATCHES, scatter_dimension=0, tiled=True),
        lax.psum_scatter(reduced[4], PATCHES, scatter_dimension=0, tiled=True),
    )
    small = lax.psum((reduced[5], reduced[6], reduced[8]), PATCHES)
    grad_pos = reduced[7]
    first_copy = (lax.axis_index(PATCHES) == 0).astype(jnp.float32)
    squares = jnp.sum(grad_pos * grad_pos)
    for item in large:
        squares = squares + jnp.sum(item * item)
    small_squares = jnp.float32(0.0)
    for item in small:
        small_squares = small_squares + jnp.sum(item * item)
    squares, loss_total = lax.psum(
        (squares + first_copy * small_squares, loss_local), (PATCHES, SHARDS)
    )
    grad_norm = jnp.sqrt(squares)
    clip = jnp.minimum(1.0, CLIP_LIMIT / (grad_norm + 1e-06))
    masters = (qkv_master, out_master, up_master, down_master)
    moments = [
        MOMENTUM * old + clip * grad
        for old, grad in zip((qkv_moment, out_moment, up_moment, down_moment), large[:4])
    ]
    norms = lax.psum(
        (
            jnp.sum(moments[0] * moments[0]),
            jnp.sum(moments[1] * moments[1]),
            jnp.sum(moments[2] * moments[2]),
            jnp.sum(moments[3] * moments[3]),
        ),
        (PATCHES, SHARDS),
    )
    sizes = [jnp.sqrt(norms[which]) for which in range(4)]
    moment_sizes = jnp.stack(sizes) / CLIP_LIMIT
    scaled = [(moments[which] / (sizes[which] + 1e-07)).astype(jnp.bfloat16) for which in range(4)]
    columns = (
        lax.all_gather(scaled[0], PATCHES, axis=0, tiled=True),
        lax.all_gather(scaled[1], PATCHES, axis=0, tiled=True),
        lax.all_gather(scaled[2], PATCHES, axis=0, tiled=True),
        lax.all_gather(scaled[3], PATCHES, axis=0, tiled=True),
    )
    seq_index = lax.axis_index(PATCHES)
    seq_count = lax.axis_size(PATCHES)
    owners = [seq_index == which % seq_count for which in range(4)]
    blocks = list(columns)
    for turn in range(NS_ITERS):
        partial_value = [
            lax.cond(owners[which], gram_part, zero_gram, blocks[which]) for which in range(4)
        ]
        grams = lax.psum(
            (partial_value[0], partial_value[1], partial_value[2], partial_value[3]), SHARDS
        )
        blocks = [
            lax.cond(owners[which], newton_step, keep_block, blocks[which], grams[which])
            for which in range(4)
        ]
    blocks = [broadcast(blocks[which], PATCHES, which % seq_count) for which in range(4)]
    row_count = qkv_master.shape[0]
    fresh = []
    for which in range(4):
        my_rows = lax.dynamic_slice_in_dim(
            blocks[which], seq_index * row_count, row_count, 0
        ).astype(jnp.float32)
        all_cols = masters[which].shape[1] * lax.axis_size(SHARDS)
        fresh.append(
            masters[which] * (1.0 - RATE_MUON * DECAY_MUON)
            - RATE_MUON * 0.2 * math.sqrt(all_cols) * my_rows
        )
    copies = (
        lax.all_gather(fresh[0].astype(jnp.bfloat16), PATCHES, axis=0, tiled=True),
        lax.all_gather(fresh[1].astype(jnp.bfloat16), PATCHES, axis=0, tiled=True),
        lax.all_gather(fresh[2].astype(jnp.bfloat16), PATCHES, axis=0, tiled=True),
        lax.all_gather(fresh[3].astype(jnp.bfloat16), PATCHES, axis=0, tiled=True),
    )
    ada_res = adam_update(ada_master, ada_first, ada_second, clip * large[4], RATE_ADAM)
    io_res = adam_update(io_proj, io_first, io_second, clip * small[0], RATE_ADAM)
    cond_res = adam_update(cond_table, cond_first, cond_second, clip * small[1], RATE_TABLE)
    pos_res = adam_update(pos_table, pos_first, pos_second, clip * grad_pos, RATE_TABLE)
    bias_res = adam_update(biases, bias_first, bias_second, clip * small[2], RATE_ADAM)
    return (
        loss_total,
        grad_norm,
        moment_sizes,
        fresh[0],
        moments[0],
        copies[0],
        fresh[1],
        moments[1],
        copies[1],
        fresh[2],
        moments[2],
        copies[2],
        fresh[3],
        moments[3],
        copies[3],
        ada_res[0],
        ada_res[1],
        ada_res[2],
        io_res[0],
        io_res[1],
        io_res[2],
        cond_res[0],
        cond_res[1],
        cond_res[2],
        pos_res[0],
        pos_res[1],
        pos_res[2],
        bias_res[0],
        bias_res[1],
        bias_res[2],
    )


LANES = 128
MATRICES = 4
LOW = jnp.bfloat16
MESH = pl.DeviceIdType.MESH


def round_up(value, unit):
    return -(-value // unit) * unit


def member_peer(members, shift):
    index = lax.axis_index(PATCHES)
    return {PATCHES: index // members * members + lax.rem(lax.rem(index, members) + shift, members)}


def group_peer(members, shift):
    return {PATCHES: lax.rem(lax.axis_index(PATCHES) + shift * members, lax.axis_size(PATCHES))}


def sibling_peer():
    index = lax.axis_index(SHARDS)
    return {SHARDS: index + 1 - 2 * lax.rem(index, 2)}


def where(condition, action):
    if condition is None:
        action()
    else:
        pl.when(condition())(action)


class Moves:
    def __init__(self, name, ids, vmem=None):
        self.name = name
        self.ids = ids
        self.vmem = vmem
        self.operands = []
        self.operand_specs = []
        self.outputs = []
        self.output_specs = []
        self.scratches = []
        self.moves = []
        self.locals = []
        self.steps = []
        self.peers = {}

    def operand(self, array, space=pl.ANY):
        self.operands.append(array)
        self.operand_specs.append(pl.BlockSpec(memory_space=space))
        return (0, len(self.operands) - 1)

    def output(self, shape, dtype, space=pl.ANY):
        self.outputs.append(jax.ShapeDtypeStruct(shape, dtype))
        self.output_specs.append(pl.BlockSpec(memory_space=space))
        return (1, len(self.outputs) - 1)

    def scratch(self, shape, dtype):
        self.scratches.append(pltpu.VMEM(shape, dtype))
        return (2, len(self.scratches) - 1)

    def keep(self, source, source_at, target, target_at, later=False):
        self.locals.append((source, source_at, target, target_at, later))
        return len(self.locals) - 1

    def load(self, array):
        target = self.scratch(array.shape, array.dtype)
        return target, self.keep(self.operand(array), None, target, None)

    def save(self, source, shape, dtype):
        number = self.keep(source, None, self.output(shape, dtype), None, True)
        return number

    def start_local(self, number):
        self.steps.append((self.begin_local, number))

    def begin_local(self, number):
        self.local[number].start()

    def move(
        self, peer_key, peer, source, source_at, target, target_at, after=(), sends=None, takes=None, later=False
    ):
        number = len(self.moves)
        self.peers.setdefault(peer_key, peer)
        self.moves.append((peer_key, source, source_at, target, target_at, sends, takes, later or bool(after)))
        for earlier in after:
            self.steps.append((self.await_move, earlier))
        if after:
            self.steps.append((self.start_move, number))
        return number

    def wait_for(self, number):
        self.steps.append((self.await_move, number))

    def start(self, number):
        self.steps.append((self.start_move, number))

    def wait_local(self, number):
        self.steps.append((self.await_local, number))

    def task(self, action):
        self.steps.append((self.do_task, action))

    def await_move(self, number):
        if number not in self.arrived:
            self.arrived.add(number)
            where(self.moves[number][6], self.remote[number].wait_recv)

    def start_move(self, number):
        where(self.moves[number][5], self.remote[number].start)

    def await_local(self, number):
        if number not in self.kept:
            self.kept.add(number)
            self.local[number].wait()

    def do_task(self, action):
        action(self.ref)

    def ref(self, which):
        return self.refs[which[0]][which[1]]

    def view(self, which, index):
        ref = self.ref(which)
        return ref.at[index()] if index is not None else ref

    def kernel(self, *refs):
        sizes = (len(self.operands), len(self.outputs), len(self.scratches))
        self.refs = (refs[: sizes[0]], refs[sizes[0] : sizes[0] + sizes[1]], refs[sizes[0] + sizes[1] : sum(sizes)])
        local_sem, send_sem, recv_sem = refs[sum(sizes) :]
        self.arrived, self.kept = set(), set()
        devices = {key: peer() for key, peer in self.peers.items()}
        barrier = pltpu.get_barrier_semaphore()
        for device in devices.values():
            pl.semaphore_signal(barrier, inc=1, device_id=device, device_id_type=MESH)
        pl.semaphore_wait(barrier, len(devices))
        self.remote = []
        for number, (key, source, source_at, target, target_at, _, _, later) in enumerate(self.moves):
            self.remote.append(
                pltpu.make_async_remote_copy(
                    src_ref=self.view(source, source_at),
                    dst_ref=self.view(target, target_at),
                    send_sem=send_sem.at[number],
                    recv_sem=recv_sem.at[number],
                    device_id=devices[key],
                    device_id_type=MESH,
                )
            )
            if not later:
                self.start_move(number)
        self.local = [
            pltpu.make_async_copy(self.view(source, source_at), self.view(target, target_at), local_sem.at[number])
            for number, (source, source_at, target, target_at, _) in enumerate(self.locals)
        ]
        for copy, entry in zip(self.local, self.locals):
            if not entry[4]:
                copy.start()
        for action, number in self.steps:
            action(number)
        for number in range(len(self.locals)):
            self.await_local(number)
        for number, copy in enumerate(self.remote):
            self.await_move(number)
            where(self.moves[number][5], copy.wait_send)

    def run(self):
        return pl.pallas_call(
            self.kernel,
            out_shape=self.outputs,
            in_specs=self.operand_specs,
            out_specs=self.output_specs,
            scratch_shapes=[
                *self.scratches,
                pltpu.SemaphoreType.DMA((max(1, len(self.locals)),)),
                pltpu.SemaphoreType.DMA((len(self.moves),)),
                pltpu.SemaphoreType.DMA((len(self.moves),)),
            ],
            compiler_params=pltpu.CompilerParams(
                collective_id=self.ids.setdefault(self.name, len(self.ids)),
                has_side_effects=True,
                vmem_limit_bytes=self.vmem,
            ),
            name=self.name,
        )(*self.operands)

    def along(self, axis, source, target, pairs, later=False):
        numbers = []
        count = lax.axis_size(axis)

        def other(shift):
            return lax.rem(lax.axis_index(axis) + shift, count)

        for shift in range(1, count):
            for source_at, target_at in pairs:
                numbers.append(
                    self.move(
                        (axis, shift),
                        lambda shift=shift: {axis: other(shift)},
                        source,
                        None if source_at is None else (lambda at=source_at, shift=shift: at(other(shift))),
                        target,
                        lambda at=target_at: at(lax.axis_index(axis)),
                        later=later,
                    )
                )
        for source_at, target_at in pairs:
            self.keep(
                source,
                None if source_at is None else (lambda at=source_at: at(lax.axis_index(axis))),
                target,
                lambda at=target_at: at(lax.axis_index(axis)),
            )
        return numbers

    def gather(self, axis, array):
        target = self.output((lax.axis_size(axis),) + array.shape, array.dtype)
        self.along(axis, self.operand(array), target, [(None, lambda sender: (sender,))])

    def gather_pairs(self, array, parts=1, hold=False):
        shards = lax.axis_size(SHARDS)
        source = self.operand(array)
        target = self.output((shards,) + array.shape, array.dtype)
        rows = array.shape[0] // parts

        def place(back_pair, part):
            return (lax.rem(lax.axis_index(SHARDS) + shards - 2 * back_pair, shards), pl.ds(part * rows, rows))

        firsts = []
        for part in range(parts):
            for pair in range(1, shards // 2):
                number = self.move(
                    (SHARDS, 2 * pair),
                    lambda pair=pair: {SHARDS: lax.rem(lax.axis_index(SHARDS) + 2 * pair, shards)},
                    source,
                    lambda part=part: (pl.ds(part * rows, rows),),
                    target,
                    functools.partial(place, 0, part),
                )
                firsts.append((functools.partial(place, pair, part), number))
        own = lambda: (lax.axis_index(SHARDS),)
        self.move((SHARDS,), sibling_peer, source, None, target, own)
        self.keep(source, None, target, own)
        waiting = [(target, at, number) for at, number in firsts]
        if hold:
            return waiting
        self.to_sibling(waiting)

    def gather_columns(self, axis, array):
        width = array.shape[-1]
        target = self.output(array.shape[:-1] + (lax.axis_size(axis) * width,), array.dtype)
        lead = (slice(None),) * (array.ndim - 1)
        self.along(
            axis,
            self.operand(array),
            target,
            [(None, lambda sender: lead + (pl.ds(pl.multiple_of(sender * width, LANES), width),))],
        )

    def gather_twice(self, arrays, members):
        shards = lax.axis_size(SHARDS)
        entries = []
        for array in arrays:
            source = self.operand(array)
            width = array.shape[1]
            target = self.output((array.shape[0], shards * width), array.dtype)
            rows = array.shape[0] // members

            def columns(back_pair, width=width):
                who = lax.rem(lax.axis_index(SHARDS) + shards - 2 * back_pair, shards)
                return pl.ds(pl.multiple_of(who * width, LANES), width)

            def place(back_member, back_pair, rows=rows, columns=columns):
                index = lax.rem(lax.rem(lax.axis_index(PATCHES), members) + members - back_member, members)
                return (pl.ds(pl.multiple_of(index * rows, rows), rows), columns(back_pair))

            def mine(rows=rows):
                index = lax.rem(lax.axis_index(PATCHES), members)
                return (pl.ds(pl.multiple_of(index * rows, rows), rows),)

            firsts = [
                self.move(
                    (SHARDS, 2 * pair),
                    lambda pair=pair: {SHARDS: lax.rem(lax.axis_index(SHARDS) + 2 * pair, shards)},
                    source,
                    mine,
                    target,
                    functools.partial(place, 0, 0),
                )
                for pair in range(1, shards // 2)
            ]
            entries.append((source, target, place, firsts))
            self.move((SHARDS,), sibling_peer, source, None, target, lambda columns=columns: (slice(None), columns(0)))
        last = []
        for _, target, place, firsts in entries:
            for pair, first in enumerate(firsts, 1):
                near = functools.partial(place, 0, pair)
                for shift in range(1, members):
                    number = self.move(
                        (PATCHES, members, shift),
                        functools.partial(member_peer, members, shift),
                        target,
                        near,
                        target,
                        near,
                        (first,),
                    )
                    last.append((target, functools.partial(place, shift, pair), number))
                self.move((SHARDS,), sibling_peer, target, near, target, near, (first,))
        self.to_sibling(last)

    def to_sibling(self, waiting):
        for target, place, number in waiting:
            self.move((SHARDS,), sibling_peer, target, place, target, place, (number,))

    def exchange(self, axis, array, later=False):
        target = self.output(array.shape, array.dtype)
        return self.along(
            axis, self.operand(array), target, [(lambda receiver: (receiver,), lambda sender: (sender,))], later
        )

    def exchange_columns(self, axis, array):
        width = array.shape[-1] // lax.axis_size(axis)
        target = self.output((lax.axis_size(axis), array.shape[0], width), array.dtype)
        self.along(
            axis,
            self.operand(array),
            target,
            [
                (
                    lambda receiver: (slice(None), pl.ds(pl.multiple_of(receiver * width, LANES), width)),
                    lambda sender: (sender,),
                )
            ],
        )

    def rows_to_heads(self, axis, array, planes, target):
        count, rows = lax.axis_size(axis), array.shape[0]
        columns = array.shape[1] // planes
        width = columns // count
        return self.along(
            axis,
            self.operand(array),
            target,
            [
                (
                    lambda receiver, plane=plane: (
                        slice(None),
                        pl.ds(pl.multiple_of(plane * columns + receiver * width, LANES), width),
                    ),
                    lambda sender, plane=plane: (plane, pl.ds(pl.multiple_of(sender * rows, rows), rows)),
                )
                for plane in range(planes)
            ],
        )

    def head_rows(self, source, target, planes, rows, columns, members, back_group):
        count = lax.axis_size(PATCHES)
        width = columns // count
        for shift_member in range(members):
            for plane in planes:

                def peer(shift_member=shift_member):
                    index = lax.axis_index(PATCHES)
                    there = lax.rem(index // members + back_group, MATRICES) * members
                    return there + lax.rem(lax.rem(index, members) + shift_member, members)

                def source_at(peer=peer, plane=plane):
                    return (plane, pl.ds(pl.multiple_of(peer() * rows, rows), rows))

                def target_at(plane=plane):
                    start = plane * columns + lax.axis_index(PATCHES) * width
                    return (slice(None), pl.ds(pl.multiple_of(start, LANES), width))

                if shift_member or back_group:
                    self.start(
                        self.move(
                            (PATCHES, count, back_group, shift_member),
                            lambda peer=peer: {PATCHES: peer()},
                            source,
                            source_at,
                            target,
                            target_at,
                            later=True,
                        )
                    )
                else:

                    def own(ref, source_at=source_at, target_at=target_at):
                        ref(target)[target_at()] = ref(source)[source_at()]

                    self.task(own)


def total_of(ids, values, shared):
    moves = Moves("total", ids)
    source, result = moves.operand(values, pltpu.VMEM), moves.output(values.shape, values.dtype, pltpu.VMEM)
    moves.gather(PATCHES, shared)
    for axis in (SHARDS, PATCHES):
        count = lax.axis_size(axis)
        buffer = moves.scratch((count,) + values.shape, values.dtype)

        def own(axis=axis):
            return (lax.axis_index(axis),)

        def put(ref, source=source, buffer=buffer, own=own):
            ref(buffer)[own()] = ref(source)[...]

        moves.task(put)
        numbers = []
        for shift in range(1, count):
            numbers.append(
                moves.move(
                    (axis, shift),
                    lambda axis=axis, shift=shift, count=count: {axis: lax.rem(lax.axis_index(axis) + shift, count)},
                    buffer,
                    own,
                    buffer,
                    own,
                    later=True,
                )
            )
            moves.start(numbers[-1])
        for number in numbers:
            moves.wait_for(number)

        def add(ref, buffer=buffer):
            ref(result)[...] = jnp.sum(ref(buffer)[...], 0)

        moves.task(add)
        source = result
    return moves.run()


def contract(left, right, left_dim, right_dim):
    return lax.dot_general(
        left, right, (((left_dim,), (right_dim,)), ((), ())), preferred_element_type=jnp.float32
    )


CHAIN_CHUNKS = 8
GRAM_COLS = 256


def attend(queries, keys, values):
    scores = contract(queries, keys, 1, 1) * HEAD ** (-0.5)
    expo = jnp.exp(scores - jnp.max(scores, -1, keepdims=True))
    probs = (expo / jnp.sum(expo, -1, keepdims=True)).astype(LOW)
    return contract(probs, values, 1, 0)


def group_rows(rows, members, shift):
    size = rows * members
    there = lax.rem(lax.axis_index(PATCHES) // members + shift, MATRICES)
    return pl.ds(pl.multiple_of(there * size, size), size)


def add_attention(moves, qkv, mixed, arrivals, rows, members, waiting):
    for number in arrivals:
        moves.wait_for(number)
    for number in range(3):
        moves.wait_local(number)
    moves.to_sibling(waiting)
    count = lax.axis_size(PATCHES)
    width = HEADS // count * HEAD
    buffer = moves.scratch((1, rows * count, width), LOW)
    for shift in (*range(1, MATRICES), 0):

        def work(ref, shift=shift):
            at = group_rows(rows, members, shift)
            parts = []
            for head in range(width // HEAD):
                lanes = pl.ds(head * HEAD, HEAD)
                parts.append(attend(ref(qkv)[0, at, lanes], ref(qkv)[1, :, lanes], ref(qkv)[2, :, lanes]))
            ref(buffer)[0, at, :] = jnp.concatenate(parts, -1).astype(LOW)

        moves.task(work)
        moves.head_rows(buffer, mixed, (0,), rows, width * count, members, shift)


def add_attention_back(moves, qkv, grads, result, arrivals, rows, members, waiting):
    for number in arrivals:
        moves.wait_for(number)
    moves.wait_local(0)
    moves.to_sibling(waiting)
    count = lax.axis_size(PATCHES)
    width = HEADS // count * HEAD
    heads = width // HEAD
    buffer = moves.scratch((3, rows * count, width), LOW)
    key_total = moves.scratch((heads, rows * count, HEAD), jnp.float32)
    value_total = moves.scratch((heads, rows * count, HEAD), jnp.float32)
    for shift in (*range(1, MATRICES), 0):

        def work(ref, shift=shift):
            at = group_rows(rows, members, shift)
            parts = []
            for head in range(heads):
                lanes = pl.ds(head * HEAD, HEAD)
                queries, keys, values = ref(qkv)[0, at, lanes], ref(qkv)[1, :, lanes], ref(qkv)[2, :, lanes]
                grad = ref(grads)[0, at, lanes]
                scores = contract(keys, queries, 1, 1) * HEAD ** (-0.5)
                expo = jnp.exp(scores - jnp.max(scores, 0, keepdims=True))
                probs = expo / jnp.sum(expo, 0, keepdims=True)
                grad_probs = contract(values, grad, 1, 1)
                shared = jnp.sum(grad_probs * probs, 0, keepdims=True)
                score_grad = (HEAD ** (-0.5) * probs * (grad_probs - shared)).astype(LOW)
                parts.append(contract(score_grad, keys, 0, 0))
                key_part = contract(score_grad, queries, 1, 0)
                value_part = contract(probs.astype(LOW), grad, 1, 0)
                if shift == 1:
                    ref(key_total)[head] = key_part
                    ref(value_total)[head] = value_part
                else:
                    ref(key_total)[head] += key_part
                    ref(value_total)[head] += value_part
            ref(buffer)[0, at, :] = jnp.concatenate(parts, -1).astype(LOW)

        moves.task(work)
        moves.head_rows(buffer, result, (0,), rows, width * count, members, shift)

    def finish(ref):
        for plane, total in ((1, key_total), (2, value_total)):
            ref(buffer)[plane] = jnp.concatenate([ref(total)[head] for head in range(heads)], -1).astype(LOW)

    moves.task(finish)
    for shift in (*range(1, MATRICES), 0):
        moves.head_rows(buffer, result, (1, 2), rows, width * count, members, shift)


def mod_row(ref, table, row):
    return ref(table)[pl.ds(row, 1), :]


class Tokens:
    def __init__(self, moves, rows, width):
        self.moves = moves
        self.shards = lax.axis_size(SHARDS)
        self.rows = rows
        self.tokens = moves.scratch((self.shards, rows, width), LOW)
        self.own_part = moves.scratch((rows, width), jnp.float32)
        self.leaving = moves.scratch((self.shards, rows, width), LOW)
        self.arriving = moves.scratch((self.shards, rows, width), LOW)

    def me(self):
        return lax.axis_index(SHARDS)

    def back(self, pair, sibling):
        index = lax.rem(self.me() + self.shards - 2 * pair, self.shards)
        return index + 1 - 2 * lax.rem(index, 2) if sibling else index

    def part(self, pair, sibling, work):
        moves = self.moves
        slot = functools.partial(self.back, pair, sibling)

        def action(ref):
            value = work(ref, slot())
            if pair or sibling:
                ref(self.leaving)[slot()] = value.astype(LOW)
            else:
                ref(self.own_part)[...] = value

        moves.task(action)
        if pair or sibling:
            number = moves.move(
                (SHARDS, pair, sibling),
                lambda: {SHARDS: slot()},
                self.leaving,
                lambda: (slot(),),
                self.arriving,
                lambda: (self.me(),),
                later=True,
            )
            moves.start(number)
            self.parts.append(number)

    def run(self, work):
        moves, halves = self.moves, 2
        self.parts = []
        size = self.rows // halves
        pairs = self.shards // 2

        def half(pair, sibling, number):
            return (self.back(pair, sibling), pl.ds(number * size, size))

        firsts = {}
        for pair in range(1, pairs):
            for number in range(halves):
                place = functools.partial(half, 0, False, number)
                firsts[pair, number] = moves.move(
                    (SHARDS, pairs - pair, False),
                    functools.partial(lambda pair: {SHARDS: self.back(pairs - pair, False)}, pair),
                    self.tokens,
                    place,
                    self.tokens,
                    place,
                    later=True,
                )
                moves.start(firsts[pair, number])
        own = functools.partial(self.back, 0, False)
        near = moves.move(
            (SHARDS, 0, True), sibling_peer, self.tokens, lambda: (own(),), self.tokens, lambda: (own(),), later=True
        )
        moves.start(near)
        self.part(0, False, work)
        moves.wait_for(near)
        self.part(0, True, work)
        for pair in range(1, pairs):
            handed = []
            for number in range(halves):
                place = functools.partial(half, pair, False, number)
                handed.append(
                    moves.move(
                        (SHARDS, 0, True),
                        sibling_peer,
                        self.tokens,
                        place,
                        self.tokens,
                        place,
                        (firsts[pair, number],),
                    )
                )
            self.part(pair, False, work)
            for number in handed:
                moves.wait_for(number)
            self.part(pair, True, work)

    def wait(self):
        for number in self.parts:
            self.moves.wait_for(number)

    def total(self, ref):
        value = ref(self.own_part)[...]
        for shift in range(1, self.shards):
            value = value + ref(self.arriving)[lax.rem(self.me() + shift, self.shards)].astype(jnp.float32)
        return value


GELU_SCALE = math.sqrt(2.0 / math.pi)
GELU_CUBE = 0.044715


def gelu_inner(values):
    return jnp.tanh(GELU_SCALE * (values + GELU_CUBE * values * values * values))


def gelu_slope(values):
    inner = gelu_inner(values)
    rise = GELU_SCALE * (1.0 + 3.0 * GELU_CUBE * values * values)
    return 0.5 * (1.0 + inner) + 0.5 * values * (1.0 - inner * inner) * rise


def feed_forward(ids, step, mods, mods_next, mixed, embedded, state, pos, w_out, w_up, w_down, io_all, w_qkv, moment_part):
    f32 = jnp.float32
    last = mods_next is None
    rows, width = mixed.shape
    padded = state.shape[1]
    hidden_count = w_up.shape[1]
    shards = lax.axis_size(SHARDS)
    moves = Moves(f"feed{step}", ids, 56 * 2**20)
    vmem = functools.partial(moves.operand, space=pltpu.VMEM)
    out_weights, out_load = moves.load(w_out)
    mods, mixed, embedded, state = vmem(mods), vmem(mixed), vmem(embedded), vmem(state)
    up_weights, up_load = moves.load(w_up)
    down_weights, down_load = moves.load(w_down)
    io_weights, io_load = moves.load(io_all)
    attended, after_attn, downward, after_mlp = [moves.output((rows, width), f32, pltpu.VMEM) for _ in range(4)]
    normed_c = moves.output((rows, width), LOW, pltpu.VMEM)
    state_next = moves.output((rows, padded), f32, pltpu.VMEM)
    upward = moves.scratch((shards, rows, hidden_count), f32)
    hidden = moves.scratch((shards, rows, hidden_count), LOW)
    feed = Tokens(moves, rows, width)
    saves = [
        moves.save(feed.tokens, (shards, rows, width), LOW),
        moves.save(upward, (shards, rows, hidden_count), f32),
        moves.save(hidden, (shards, rows, hidden_count), LOW),
    ]
    if not last:
        mods_next, pos = vmem(mods_next), vmem(pos)
        qkv_weights, qkv_load = moves.load(w_qkv)
        embedded_next = moves.output((rows, width), f32, pltpu.VMEM)
        normed_next = moves.output((rows, width), LOW, pltpu.VMEM)
        state_low = moves.output((rows, padded), LOW, pltpu.VMEM)
        qkv_next = moves.output((rows, w_qkv.shape[1]), LOW, pltpu.VMEM)
    moves.exchange(PATCHES, moment_part)

    def begin(ref):
        value = contract(ref(mixed)[...], ref(out_weights)[...], 1, 0)
        ref(attended)[...] = value
        value = ref(embedded)[...] + mod_row(ref, mods, 2) * value
        ref(after_attn)[...] = value
        normed, _ = layer_norm(value)
        normed = normed * (1.0 + mod_row(ref, mods, 4)) + mod_row(ref, mods, 3)
        ref(feed.tokens)[feed.me()] = normed.astype(LOW)

    def work(ref, slot):
        value = contract(ref(feed.tokens)[slot], ref(up_weights)[...], 1, 0)
        ref(upward)[slot] = value
        value = (0.5 * value * (1.0 + gelu_inner(value))).astype(LOW)
        ref(hidden)[slot] = value
        return contract(value, ref(down_weights)[...], 1, 1)

    def finish(ref):
        value = feed.total(ref)
        ref(downward)[...] = value
        value = ref(after_attn)[...] + mod_row(ref, mods, 5) * value
        ref(after_mlp)[...] = value
        normed, _ = layer_norm(value)
        normed = normed.astype(LOW)
        ref(normed_c)[...] = normed
        delta = contract(normed, ref(io_weights)[1], 1, 1)
        value = ref(state)[...] + mod_row(ref, mods, 7)[:, :padded] * delta
        ref(state_next)[...] = value
        if not last:
            value = value.astype(LOW)
            ref(state_low)[...] = value
            value = contract(value, ref(io_weights)[0], 1, 0) + mod_row(ref, mods, 6) + ref(pos)[...]
            ref(embedded_next)[...] = value
            normed, _ = layer_norm(value)
            normed = (normed * (1.0 + mod_row(ref, mods_next, 1)) + mod_row(ref, mods_next, 0)).astype(LOW)
            ref(normed_next)[...] = normed

    def project(ref):
        @pl.loop(0, w_qkv.shape[1] // width)
        def _(part):
            cols = pl.ds(pl.multiple_of(part * width, width), width)
            value = contract(ref(normed_next)[...], ref(qkv_weights)[:, cols], 1, 0)
            ref(qkv_next)[:, cols] = value.astype(LOW)

    moves.wait_local(out_load)
    moves.task(begin)
    moves.wait_local(up_load)
    moves.wait_local(down_load)
    feed.run(work)
    for number in saves:
        moves.start_local(number)
    moves.wait_local(io_load)
    feed.wait()
    moves.task(finish)
    if not last:
        moves.wait_local(qkv_load)
        moves.task(project)
    return moves.run()


def feed_back(ids, step, mods, mods_later, later, grad_state, kept, w_out, w_up, w_down, io_all, w_qkv):
    f32 = jnp.float32
    attended, after_attn, downward, after_mlp, upward = kept
    rows, width = attended.shape
    padded = grad_state.shape[1]
    hidden_count = w_up.shape[1]
    shards = lax.axis_size(SHARDS)
    moves = Moves(f"feed_back{step}", ids, 56 * 2**20)
    vmem = functools.partial(moves.operand, space=pltpu.VMEM)
    io_weights, io_load = moves.load(io_all)
    if later is not None:
        qkv_weights, qkv_load = moves.load(w_qkv)
        later = [vmem(item) for item in later]
        mods_later = vmem(mods_later)
        embed_grad = moves.output((rows, width), LOW, pltpu.VMEM)
    down_weights, down_load = moves.load(w_down)
    up_weights, up_load = moves.load(w_up)
    slopes, slopes_load = moves.load(upward)
    out_weights, out_load = moves.load(w_out)
    mods, grad_state = vmem(mods), vmem(grad_state)
    attended, after_attn, downward, after_mlp = [vmem(item) for item in (attended, after_attn, downward, after_mlp)]
    vectors = moves.output((8, width), f32, pltpu.VMEM)
    state_out = moves.output((rows, padded), f32, pltpu.VMEM)
    delta_grad = moves.output((rows, padded), LOW, pltpu.VMEM)
    grad_attn = moves.output((rows, width), f32, pltpu.VMEM)
    attn_grad, mixed_grad = [moves.output((rows, width), LOW, pltpu.VMEM) for _ in range(2)]
    grad_mlp = moves.scratch((rows, width), f32)
    up_grad = moves.scratch((shards, rows, hidden_count), LOW)
    feed = Tokens(moves, rows, width)
    saves = [
        moves.save(feed.tokens, (shards, rows, width), LOW),
        moves.save(up_grad, (shards, rows, hidden_count), LOW),
    ]

    def put(ref, row, value):
        ref(vectors)[pl.ds(row, 1), :] = jnp.sum(value, 0, keepdims=True)

    def before(ref):
        qkv_grad, embedded, grad_later = later
        grad = contract(ref(qkv_grad)[...], ref(qkv_weights)[...], 1, 1)
        normed, inverse = layer_norm(ref(embedded)[...])
        put(ref, 5, grad * normed)
        put(ref, 4, grad)
        grad = grad * (1.0 + mod_row(ref, mods_later, 1))
        grad = ref(grad_later)[...] + norm_back(grad, normed, inverse)
        put(ref, 6, grad)
        grad = grad.astype(LOW)
        ref(embed_grad)[...] = grad
        ref(state_out)[...] = ref(grad_state)[...] + contract(grad, ref(io_weights)[0], 1, 1)

    def begin(ref):
        if later is None:
            ref(state_out)[...] = ref(grad_state)[...]
            ref(vectors)[...] = jnp.zeros((8, width), f32)
        grad = (mod_row(ref, mods, 7)[:, :padded] * ref(state_out)[...]).astype(LOW)
        ref(delta_grad)[...] = grad
        normed, inverse = layer_norm(ref(after_mlp)[...])
        grad = norm_back(contract(grad, ref(io_weights)[1], 1, 0), normed, inverse)
        ref(grad_mlp)[...] = grad
        put(ref, 3, grad * ref(downward)[...])
        ref(feed.tokens)[feed.me()] = (mod_row(ref, mods, 5) * grad).astype(LOW)

    def work(ref, slot):
        value = contract(ref(feed.tokens)[slot], ref(down_weights)[...], 1, 0)
        value = (value * gelu_slope(ref(slopes)[slot])).astype(LOW)
        ref(up_grad)[slot] = value
        return contract(value, ref(up_weights)[...], 1, 1)

    def finish(ref):
        grad = feed.total(ref)
        normed, inverse = layer_norm(ref(after_attn)[...])
        put(ref, 2, grad * normed)
        put(ref, 1, grad)
        grad = ref(grad_mlp)[...] + norm_back(grad * (1.0 + mod_row(ref, mods, 4)), normed, inverse)
        ref(grad_attn)[...] = grad
        put(ref, 0, grad * ref(attended)[...])
        grad = (mod_row(ref, mods, 2) * grad).astype(LOW)
        ref(attn_grad)[...] = grad
        ref(mixed_grad)[...] = contract(grad, ref(out_weights)[...], 1, 1).astype(LOW)

    moves.wait_local(io_load)
    if later is not None:
        moves.wait_local(qkv_load)
        moves.task(before)
    moves.task(begin)
    for number in (down_load, up_load, slopes_load):
        moves.wait_local(number)
    feed.run(work)
    for number in saves:
        moves.start_local(number)
    moves.wait_local(out_load)
    feed.wait()
    moves.task(finish)
    results = moves.run()
    return results if later is not None else [None, *results]


def newton_schulz(source, gram, poly, once, gram_low, poly_low, once_low, block, block_next):
    size = gram.shape[0]
    eye = jnp.equal(
        lax.broadcasted_iota(jnp.int32, (GRAM_COLS, GRAM_COLS), 0),
        lax.broadcasted_iota(jnp.int32, (GRAM_COLS, GRAM_COLS), 1),
    ).astype(jnp.float32)

    def over_tiles(action, width=size):
        def step(tile, total):
            return total + action(pl.ds(pl.multiple_of(tile * GRAM_COLS, GRAM_COLS), GRAM_COLS))

        return lax.fori_loop(0, width // GRAM_COLS, step, jnp.float32(0.0))

    def store(full, low, cols, value, mean, excess):
        full[:, cols] = value
        low[:, cols] = value.astype(LOW)
        corner = full[cols, cols] - excess * eye
        full[cols, cols] = corner
        low[cols, cols] = (corner - mean * eye).astype(LOW)

    def advance(gram_mean, gram_squares, last):
        poly_mean = NS_B * gram_mean + NS_C * gram_squares / size

        def poly_cols(cols):
            own = gram[:, cols]
            value = contract(gram_low[...], gram_low[:, cols], 1, 0)
            value = NS_C * value + (NS_B + 2.0 * NS_C * gram_mean) * own
            store(poly, poly_low, cols, value, poly_mean, NS_C * gram_mean * gram_mean)
            return jnp.sum(value * own)

        once_mean = over_tiles(poly_cols) / size - NS_C * gram_mean * gram_mean * gram_mean

        def block_cols(cols):
            value = contract(poly_low[...], block[:, cols], 1, 0)
            block_next[:, cols] = (value + (NS_A + poly_mean) * block[:, cols].astype(jnp.float32)).astype(LOW)
            return jnp.float32(0.0)

        over_tiles(block_cols, block.shape[1])
        block[...] = block_next[...]
        if last:
            return None

        def once_cols(cols):
            own = poly[:, cols]
            value = contract(poly_low[...], gram_low[:, cols], 1, 0)
            value = value + poly_mean * gram[:, cols] + gram_mean * own
            store(once, once_low, cols, value, once_mean, poly_mean * gram_mean)
            return jnp.sum(value * own)

        poly_once = over_tiles(once_cols) / size - poly_mean * gram_mean * poly_mean
        mean_next = NS_A * NS_A * gram_mean + 2.0 * NS_A * once_mean + poly_once
        excess = poly_mean * once_mean

        def gram_cols(cols):
            value = contract(poly_low[...], once_low[:, cols], 1, 0)
            value = value + (2.0 * NS_A + poly_mean) * once[:, cols] + once_mean * poly[:, cols]
            value = value + NS_A * NS_A * gram[:, cols]
            store(gram, gram_low, cols, value, mean_next, excess)
            return jnp.sum(value * value)

        return mean_next, over_tiles(gram_cols) - excess * (2.0 * mean_next + excess) * size

    block[...] = source[...]
    mean = over_tiles(lambda cols: jnp.sum(gram[cols, cols] * eye)) / size

    def start(cols):
        value = gram[:, cols]
        gram_low[:, cols] = value.astype(LOW)
        gram_low[cols, cols] = (gram[cols, cols] - mean * eye).astype(LOW)
        return jnp.sum(value * value)

    state = lax.fori_loop(0, NS_ITERS - 1, lambda turn, state: advance(*state, False), (mean, over_tiles(start)))
    advance(*state, True)


def fast_body(
    states,
    targets,
    lengths,
    intervals,
    qkv_copy,
    qkv_master,
    qkv_moment,
    out_copy,
    out_master,
    out_moment,
    up_copy,
    up_master,
    up_moment,
    down_copy,
    down_master,
    down_moment,
    ada_copy,
    ada_master,
    ada_first,
    ada_second,
    io_proj,
    io_first,
    io_second,
    cond_table,
    cond_first,
    cond_second,
    pos_table,
    pos_first,
    pos_second,
    biases,
    bias_first,
    bias_second,
):
    ids = {}
    f32 = jnp.float32
    seq_count, shards = lax.axis_size(PATCHES), lax.axis_size(SHARDS)
    seq_index, shard = lax.axis_index(PATCHES), lax.axis_index(SHARDS)
    members = seq_count // MATRICES
    group, member = seq_index // members, lax.rem(seq_index, members)
    samples, local, values_count = states.shape
    table_rows, table_cols = cond_table.shape
    width = table_cols * shards
    ada_cols = ada_copy.shape[1]
    padded = round_up(values_count, LANES)

    moves = Moves("tables", ids)
    moves.gather(SHARDS, cond_table)
    moves.gather(SHARDS, biases[None])
    table_parts, bias_parts = moves.run()
    table = jnp.moveaxis(table_parts, 0, 1).reshape(table_rows, width).astype(LOW).astype(f32)
    bias = bias_parts.reshape(-1).astype(LOW).astype(f32)
    rows_iota = jnp.arange(table_rows, dtype=jnp.int32)
    id_rows = (intervals[:, None] == rows_iota[None]).astype(f32)
    step_rows = (rows_iota[None] == NI + jnp.arange(ROLL, dtype=jnp.int32)[:, None]).astype(f32)
    select = (id_rows[:, None] + step_rows[None]).reshape(-1, table_rows)
    cond_vec = jnp.sum(select[:, :, None] * table[None], 1)
    silu_low = jax.nn.silu(cond_vec).astype(LOW)
    modul_shard = product(silu_low, ada_copy) + lax.dynamic_slice_in_dim(bias, shard * ada_cols, ada_cols)[None]

    moves = Moves("weights", ids)
    moves.exchange(SHARDS, modul_shard.reshape(shards, ROLL, ada_cols))
    moves.gather_columns(SHARDS, pos_table.astype(LOW))
    io_low = jnp.pad(io_proj.astype(LOW), ((0, 0), (0, padded - values_count), (0, 0)))
    own_parts = (io_low.reshape(2 * padded, -1), out_copy, qkv_copy)
    moves.gather_twice(own_parts, members)
    modul, pos, *parts = moves.run()
    io_all, w_out, w_qkv = [
        lax.dynamic_update_slice_in_dim(part, own, shard * own.shape[1], 1) for part, own in zip(parts, own_parts)
    ]
    io_all = io_all.reshape(2, padded, width)
    modul = jnp.moveaxis(modul, 0, 1).reshape(ROLL, 6 * width)
    pos = pos.astype(f32)

    masters = (qkv_master, up_master, down_master, out_master)
    momenta = (qkv_moment, up_moment, down_moment, out_moment)
    group_cols = [item.shape[1] // members for item in momenta]
    most_cols = max(group_cols)

    def widen(item):
        return jnp.pad(item, ((0, 0), (0, most_cols - item.shape[1])))

    moment_parts = jnp.stack(
        [
            widen(item[:, part * cols : (part + 1) * cols].astype(LOW))
            for item, cols in zip(momenta, group_cols)
            for part in range(members)
        ]
    )
    half_rows = moment_parts.shape[1] // 2

    counts = jnp.sum((intervals[:, None] == jnp.arange(NI, dtype=jnp.int32)[None]).astype(f32), 0)
    my_id = lax.dynamic_slice_in_dim(intervals, shard, 1)
    id_count = jnp.sum((my_id == jnp.arange(NI, dtype=jnp.int32)).astype(f32) * counts)
    weight = 1.0 / (NI * local * seq_count * values_count * id_count)
    length = lengths[0]
    value_pad = ((0, 0), (0, padded - values_count))
    state = jnp.pad(states[0].astype(f32), value_pad)
    embed_bias = bias[6 * width :]
    kept = []
    gathered = {}
    moment_halves = []

    extras = [
        jnp.concatenate(
            [
                modul[step].reshape(6, width),
                embed_bias[None],
                jnp.broadcast_to((step < length).astype(f32), (1, width)),
            ]
        )
        for step in range(ROLL)
    ]
    state_low = state.astype(LOW)
    embedded = product(state_low, io_all[0]) + embed_bias + pos
    normed_a = (layer_norm(embedded)[0] * (1.0 + extras[0][1]) + extras[0][0]).astype(LOW)
    qkv_rows = product(normed_a, w_qkv).astype(LOW)
    for step in range(ROLL):
        moves = Moves(f"attend{step}", ids, 48 * 2**20)
        qkv_out = moves.output((3, local * seq_count, width // seq_count), LOW, pltpu.VMEM)
        mixed_out = moves.output((local, width), LOW, pltpu.VMEM)
        arrivals = moves.rows_to_heads(PATCHES, qkv_rows, 3, qkv_out)
        waiting = moves.gather_pairs(normed_a, hold=True)
        waiting += moves.gather_pairs(state_low, hold=True)
        if step:
            waiting += moves.gather_pairs(kept[-1][2], hold=True)
        add_attention(moves, qkv_out, mixed_out, arrivals, local, members, waiting)
        qkv, mixed, gathered_a, gathered_state, *gathered_mixed = moves.run()
        gathered.setdefault("a", {})[step] = gathered_a
        gathered.setdefault("state", {})[step] = gathered_state
        if step:
            gathered["mixed"] = {step - 1: gathered_mixed[0]}
        *results, moment_half = feed_forward(
            ids,
            step,
            extras[step],
            extras[step + 1] if step + 1 < ROLL else None,
            mixed,
            embedded,
            state,
            pos,
            w_out,
            up_copy,
            down_copy,
            io_all,
            w_qkv,
            moment_parts[:, step * half_rows : (step + 1) * half_rows],
        )
        moment_halves.append(moment_half)
        attended, after_attn, downward, after_mlp, normed_c, state, tokens_b, upward, hidden, *following = results
        kept.append(
            (embedded, qkv, mixed, (attended, after_attn, downward, after_mlp, upward), normed_c, tokens_b, hidden)
        )
        if following:
            embedded, normed_a, state_low, qkv_rows = following

    lat = latitude_weights(local)
    diff = state - jnp.pad(targets[0].astype(f32), value_pad)
    loss_local = weight * jnp.sum(jnp.sum(diff * diff, -1) * lat)
    grad_state = 2.0 * weight * lat[:, None] * diff

    mlp_back = []

    def patch_sum(item, cols):
        mine = lax.dynamic_slice_in_dim(item, member * cols, cols, 1)
        low = item.astype(LOW)
        for shift in range(1, members):
            pairs = [
                (index, index // members * members + (index + shift) % members) for index in range(seq_count)
            ]
            to_member = lax.rem(member + shift, members)
            outgoing = lax.dynamic_slice_in_dim(low, to_member * cols, cols, 1)
            mine = mine + lax.ppermute(outgoing, PATCHES, pairs).astype(f32)
        return mine

    later, mods_later = None, None
    mod_grads = [[None] * 6 for _ in range(ROLL)]
    bias_grads = []

    def put_mods(step, names_and_rows):
        for place, row in names_and_rows:
            mod_grads[step][place] = row

    for step in reversed(range(ROLL)):
        embedded, qkv, mixed, for_feed, normed_c, tokens_b, hidden = kept[step]
        embed_grad, vectors, grad_state, delta_grad, grad_attn, attn_grad, mixed_grad, tokens_down, up_grad = feed_back(
            ids,
            step,
            extras[step],
            mods_later,
            later,
            grad_state,
            for_feed,
            w_out,
            up_copy,
            down_copy,
            io_all,
            w_qkv,
        )
        put_mods(step, ((2, vectors[0]), (3, vectors[1]), (4, vectors[2]), (5, vectors[3])))
        if later is not None:
            put_mods(step + 1, ((0, vectors[4]), (1, vectors[5])))
            bias_grads.append(vectors[6])
        mlp_back.append((tokens_b, up_grad, tokens_down, hidden))
        if step == 0:
            mlp_sums = []
            for left, right, cols in ((0, 1, group_cols[1]), (2, 3, group_cols[2])):
                total = sum(rows_product(items[left], items[right]) for items in mlp_back)
                mlp_sums.append(patch_sum(total, cols))
        moves = Moves(f"attend_back{step}", ids, 48 * 2**20)
        grads_in = moves.scratch((1, local * seq_count, width // seq_count), LOW)
        result = moves.output((local, 3 * width), LOW, pltpu.VMEM)
        arrivals = moves.rows_to_heads(PATCHES, mixed_grad, 1, grads_in)
        names = ["attn", "c", "delta"]
        moves.exchange_columns(SHARDS, attn_grad)
        moves.exchange_columns(SHARDS, normed_c)
        waiting = moves.gather_pairs(delta_grad, hold=True)
        if step == ROLL - 1:
            waiting += moves.gather_pairs(mixed, hold=True)
            names.append("mixed")
        else:
            moves.exchange_columns(SHARDS, later[0])
            moves.exchange_columns(SHARDS, embed_grad)
            names += ["qkv", "embed"]
        add_attention_back(
            moves, moves.operand(qkv, pltpu.VMEM), grads_in, result, arrivals, local, members, waiting
        )
        qkv_grad, *others = moves.run()
        for name, item in zip(names, others):
            gathered.setdefault(name, {})[step + (name in ("qkv", "embed"))] = item
        later, mods_later = (qkv_grad, embedded, grad_attn), extras[step]
    grad_normed_a = contract(qkv_grad, w_qkv, 1, 1)
    normed_one, inverse_one = layer_norm(embedded)
    put_mods(0, ((0, jnp.sum(grad_normed_a, 0)), (1, jnp.sum(grad_normed_a * normed_one, 0))))
    grad_embedded = grad_attn + norm_back(grad_normed_a * (1.0 + extras[0][1:2]), normed_one, inverse_one)
    embed_grad = grad_embedded.astype(LOW)
    bias_grads.append(jnp.sum(grad_embedded, 0))

    mlp_low = [item.astype(LOW) for item in mlp_sums]
    modul_parts = jnp.stack([jnp.concatenate(item).reshape(shards, ada_cols) for item in mod_grads], 1)
    embed_parts = sum(bias_grads).reshape(shards, 1, -1)
    vectors = jnp.concatenate(
        [modul_parts, jnp.pad(embed_parts, ((0, 0), (0, 0), (0, ada_cols - embed_parts.shape[-1])))], 1
    )

    def to_group(moves, item, which, start, size):
        source = moves.operand(item)
        target = moves.output((MATRICES - 1, size, item.shape[1]), LOW)
        for shift in range(1, MATRICES):
            moves.move(
                (PATCHES, seq_count, shift),
                functools.partial(group_peer, members, shift),
                source,
                lambda: (pl.ds(start, size),),
                target,
                lambda shift=shift: (shift - 1,),
                sends=lambda shift=shift: lax.axis_index(PATCHES) // members == (which - shift) % MATRICES,
                takes=lambda: lax.axis_index(PATCHES) // members == which,
            )

    block_rows = qkv_copy.shape[0]
    early = (1, 2)
    first_rows = block_rows * 7 // 16
    moves = Moves("samples", ids)
    moves.exchange_columns(SHARDS, qkv_grad)
    moves.exchange_columns(SHARDS, embed_grad)
    moves.exchange(SHARDS, vectors)
    for item, which in zip(mlp_low, early):
        to_group(moves, item, which, 0, first_rows)
    gathered["qkv"][0], gathered["embed"][0], vectors, *mlp_first = moves.run()
    grad_pos = sum(jnp.sum(item.astype(f32), 0) for item in gathered["embed"].values())

    def from_all(left, right):
        both = [
            jnp.concatenate([gathered[name][step].reshape(shards * local, -1) for step in range(ROLL)], 0)
            for name in (left, right)
        ]
        return rows_product(*both)

    io_here = jnp.stack([from_all("state", "embed"), from_all("delta", "c")])
    io_cols = io_here.shape[-1]
    grads_here = [from_all("a", "qkv"), from_all("mixed", "attn")]
    late = (0, MATRICES - 1)

    moves = Moves("member_sums", ids)
    for item, which in zip(grads_here, late):
        cols = group_cols[which]
        source = moves.operand(item.astype(LOW))
        target = moves.output((members - 1, item.shape[0], cols), LOW)
        for shift in range(1, members):

            def source_at(shift=shift, cols=cols):
                to_member = lax.rem(lax.rem(lax.axis_index(PATCHES), members) + shift, members)
                return (slice(None), pl.ds(pl.multiple_of(to_member * cols, LANES), cols))

            moves.move(
                (PATCHES, members, shift),
                functools.partial(member_peer, members, shift),
                source,
                source_at,
                target,
                lambda shift=shift: (shift - 1,),
            )
    modul_here, embed_here = vectors[:, :ROLL].reshape(-1), jnp.sum(vectors[:, ROLL, : width // shards], 0)
    flat = jnp.concatenate([modul_here, embed_here]).astype(LOW)
    flat_rows = round_up(flat.size, 16 * LANES) // LANES
    moves.gather(PATCHES, jnp.pad(flat, (0, flat_rows * LANES - flat.size)).reshape(flat_rows, LANES))
    moves.exchange(PATCHES, io_here.reshape(seq_count, -1, io_cols).astype(LOW))
    for item, which in zip(mlp_low, early):
        to_group(moves, item, which, first_rows, block_rows - first_rows)
    *halves, vectors, io_parts, up_rest, down_rest = moves.run()
    mlp_sums = [
        mine + jnp.concatenate([jnp.sum(part.astype(f32), 0) for part in parts], 0)
        for mine, *parts in zip(mlp_sums, mlp_first, (up_rest, down_rest))
    ]
    vectors = jnp.sum(vectors.astype(f32), 0).reshape(-1)
    io_slice = jnp.sum(io_parts.astype(f32), 0)
    late_sums = [
        lax.dynamic_slice_in_dim(item, member * group_cols[which], group_cols[which], 1)
        + jnp.sum(half.astype(f32), 0)
        for item, half, which in zip(grads_here, halves, late)
    ]
    modul_all = vectors[: modul_here.size].reshape(-1, ada_cols)
    bias_part = jnp.concatenate([jnp.sum(modul_all, 0), vectors[modul_here.size : flat.size]])
    silu_part = lax.dot_general(
        modul_all, ada_copy.astype(f32), (((1,), (1,)), ((), ())), precision=HIGHEST_PRECISION
    )

    moves = Moves("group_sums", ids)
    moves.vmem = 32 * 2**20
    to_group(moves, late_sums[1].astype(LOW), late[1], 0, block_rows)

    def has_source():
        return lax.axis_index(PATCHES) // members < MATRICES - 1

    def is_source():
        return lax.axis_index(PATCHES) // members > 0

    chain = late_sums[0]
    mine = moves.operand(chain, pltpu.VMEM)
    chain_total = moves.output(chain.shape, f32, pltpu.VMEM)
    arriving, leaving = moves.scratch(chain.shape, LOW), moves.scratch(chain.shape, LOW)
    chunk = block_rows // CHAIN_CHUNKS
    for part in range(CHAIN_CHUNKS):
        place = (pl.ds(part * chunk, chunk),)
        number = moves.move(
            (PATCHES, seq_count, MATRICES - 1),
            functools.partial(group_peer, members, MATRICES - 1),
            leaving,
            lambda place=place: place,
            arriving,
            lambda place=place: place,
            sends=is_source,
            takes=has_source,
            later=True,
        )

        def add(ref, place=place):
            def with_arriving():
                ref(chain_total)[place] = ref(mine)[place] + ref(arriving)[place].astype(f32)

            def alone():
                ref(chain_total)[place] = ref(mine)[place]

            pl.when(has_source())(with_arriving)
            pl.when(jnp.logical_not(has_source()))(alone)
            ref(leaving)[place] = ref(chain_total)[place].astype(LOW)

        moves.wait_for(number)
        moves.task(add)
        moves.start(number)
    moves.gather(SHARDS, silu_part)
    moves.gather(SHARDS, bias_part[None])
    out_parts, chain, silu_parts, bias_parts = moves.run()
    late_sums = [widen(chain), widen(late_sums[1] + jnp.sum(out_parts.astype(f32), 0))]
    grad_group = jnp.where(
        group == late[0],
        late_sums[0],
        jnp.where(group == late[1], late_sums[1], widen(jnp.where(group == early[0], *mlp_sums))),
    )
    grad_silu = jnp.sum(silu_parts, 0)
    grad_cond = jax.vjp(jax.nn.silu, cond_vec)[1](grad_silu)[0]
    grad_table_all = lax.dot_general(select, grad_cond, (((0,), (0,)), ((), ())), precision=HIGHEST_PRECISION)
    grad_table = lax.dynamic_slice_in_dim(grad_table_all, shard * table_cols, table_cols, 1)
    bias_parts = bias_parts[:, 0]
    grad_bias_all = jnp.concatenate([bias_parts[:, :ada_cols].reshape(-1), bias_parts[:, ada_cols:].reshape(-1)])
    grad_bias = lax.dynamic_slice_in_dim(grad_bias_all, shard * biases.shape[0], biases.shape[0])
    silu_rows = lax.dynamic_slice_in_dim(silu_low, seq_index * ada_master.shape[0], ada_master.shape[0], 1)
    grad_ada = lax.dot_general(
        silu_rows.astype(f32), modul_all, (((0,), (0,)), ((), ())), precision=HIGHEST_PRECISION
    )

    moment_group = jnp.concatenate(moment_halves, 1).reshape(-1, most_cols).astype(f32)
    grad_squares = jnp.sum(grad_group * grad_group)
    squares = (
        grad_squares
        + jnp.sum(grad_ada * grad_ada)
        + jnp.sum(io_slice * io_slice)
        + jnp.sum(grad_pos * grad_pos)
        + (seq_index == 0).astype(f32) * (jnp.sum(grad_table * grad_table) + jnp.sum(grad_bias * grad_bias))
    )
    lane = jnp.arange(LANES, dtype=jnp.int32)
    place = 2 + 3 * group
    entries = jnp.where(lane == 0, squares, 0.0) + jnp.where(lane == 1, loss_local, 0.0)
    entries = entries + jnp.where(lane == place, jnp.sum(moment_group * moment_group), 0.0)
    entries = entries + jnp.where(lane == place + 1, jnp.sum(moment_group * grad_group), 0.0)
    entries = entries + jnp.where(lane == place + 2, grad_squares, 0.0)
    sums, io_slices = total_of(ids, jnp.broadcast_to(entries[None], (8, LANES)), io_slice.astype(LOW))
    sums = sums[0]
    grad_norm = jnp.sqrt(sums[0])
    loss_total = sums[1]
    clip = jnp.minimum(1.0, CLIP_LIMIT / (grad_norm + 1e-06))
    terms = sums[2 : 2 + 3 * MATRICES].reshape(MATRICES, 3)
    size_squares = MOMENTUM * MOMENTUM * terms[:, 0] + 2.0 * MOMENTUM * clip * terms[:, 1] + clip * clip * terms[:, 2]
    sizes = jnp.sqrt(jnp.maximum(size_squares, 0.0))
    moment_sizes = sizes[jnp.array([0, 3, 1, 2])] / CLIP_LIMIT
    my_size = lax.dynamic_slice_in_dim(sizes, group, 1)[0]
    block = ((MOMENTUM * moment_group + clip * grad_group) / (my_size + 1e-07)).astype(LOW)

    moves = Moves("muon", ids, 56 * 2**20)
    source = moves.operand(block, pltpu.VMEM)
    full, low = (block_rows, block_rows), (block_rows, most_cols)
    update = moves.output((seq_count, block_rows // seq_count, most_cols), LOW, pltpu.VMEM)
    target = moves.scratch((members * shards,) + low, LOW)
    gram, poly, once = [moves.scratch(full, f32) for _ in range(3)]
    gram_low, poly_low, once_low = [moves.scratch(full, LOW) for _ in range(3)]
    state, state_next = [moves.scratch(low, LOW) for _ in range(2)]
    pairs = shards // 2

    def slot(back_member, back_pair, part=None):
        who_member = lax.rem(lax.rem(lax.axis_index(PATCHES), members) + members - back_member, members)
        who_shard = lax.rem(lax.axis_index(SHARDS) + shards - 2 * back_pair, shards)
        index = who_member * shards + who_shard
        return (index,) if part is None else (index, pl.ds(part * block_rows // 2, block_rows // 2))

    def add_gram(place):
        def action(ref):
            (index,) = place()

            @pl.loop(0, block_rows // GRAM_COLS)
            def _(tile):
                cols = pl.ds(pl.multiple_of(tile * GRAM_COLS, GRAM_COLS), GRAM_COLS)
                ref(gram)[:, cols] += contract(ref(target)[index], ref(target)[index, cols, :], 1, 1)

        return action

    def start_gram(ref):
        @pl.loop(0, block_rows // GRAM_COLS)
        def _(tile):
            cols = pl.ds(pl.multiple_of(tile * GRAM_COLS, GRAM_COLS), GRAM_COLS)
            ref(gram)[:, cols] = contract(ref(source)[...], ref(source)[cols, :], 1, 1)

    def pair_peer(shift):
        return {SHARDS: lax.rem(lax.axis_index(SHARDS) + 2 * shift, shards)}

    slot_own = functools.partial(slot, 0, 0)
    by_member = {
        shift: moves.move(
            (PATCHES, members, shift), functools.partial(member_peer, members, shift), source, None, target, slot_own
        )
        for shift in range(1, members)
    }
    by_pair = {
        shift: moves.move((SHARDS, 2 * shift), functools.partial(pair_peer, shift), source, None, target, slot_own)
        for shift in range(1, pairs)
    }
    from_sibling = [(moves.move((SHARDS,), sibling_peer, source, None, target, slot_own), slot_own)]
    moves.task(start_gram)

    def sibling_place(place):
        def at():
            (index,) = place()
            return (index + 1 - 2 * lax.rem(index, 2),)

        return at

    def hand_on(place, arrivals):
        if len(arrivals) == 1:
            parts = [(place, arrivals[0])]
        else:
            parts = [(functools.partial(place, part), number) for part, number in enumerate(arrivals)]
        numbers = [
            moves.move((SHARDS,), sibling_peer, target, at, target, at, (number,)) for at, number in parts
        ]
        from_sibling.append((numbers, place))
        moves.task(add_gram(place))

    across = []
    for shift_member, first in by_member.items():
        for shift_pair, second in by_pair.items():
            top = functools.partial(slot, shift_member, 0, 0)
            bottom = functools.partial(slot, 0, shift_pair, 1)
            halves = [
                moves.move(
                    (SHARDS, 2 * shift_pair),
                    functools.partial(pair_peer, shift_pair),
                    target,
                    top,
                    target,
                    top,
                    (first,),
                ),
                moves.move(
                    (PATCHES, members, shift_member),
                    functools.partial(member_peer, members, shift_member),
                    target,
                    bottom,
                    target,
                    bottom,
                    (second,),
                ),
            ]
            across.append((functools.partial(slot, shift_member, shift_pair), halves))
    for shift, number in by_member.items():
        hand_on(functools.partial(slot, shift, 0), [number])
    for shift, number in by_pair.items():
        hand_on(functools.partial(slot, 0, shift), [number])
    moves.wait_for(from_sibling[0][0])
    moves.task(add_gram(sibling_place(slot_own)))
    for place, halves in across:
        hand_on(place, halves)
    for numbers, place in from_sibling[1:]:
        for number in numbers:
            moves.wait_for(number)
        moves.task(add_gram(sibling_place(place)))

    for number in moves.exchange(PATCHES, grad_group.astype(LOW).reshape(seq_count, -1, most_cols), later=True):
        moves.start(number)
    moves.task(
        lambda ref: newton_schulz(
            *[ref(item) for item in (source, gram, poly, once, gram_low, poly_low, once_low, state, state_next)]
        )
    )

    def row_part(shift):
        there = lax.rem(lax.axis_index(PATCHES) + shift, seq_count)
        size = block_rows // seq_count
        return (pl.ds(pl.multiple_of(there * size, size), size),)

    for shift in range(1, seq_count):
        moves.start(
            moves.move(
                (PATCHES, shift),
                lambda shift=shift: {PATCHES: lax.rem(lax.axis_index(PATCHES) + shift, seq_count)},
                state,
                functools.partial(row_part, shift),
                update,
                lambda: (lax.axis_index(PATCHES),),
                later=True,
            )
        )

    def keep_rows(ref):
        ref(update)[lax.axis_index(PATCHES)] = ref(state)[row_part(0)]

    moves.task(keep_rows)
    update, grad_rows = moves.run()

    def rows_of(which, parts):
        return jnp.concatenate(
            [parts[which * members + part][:, : group_cols[which]] for part in range(members)], -1
        ).astype(f32)

    moments = [MOMENTUM * old + clip * rows_of(which, grad_rows) for which, old in enumerate(momenta)]
    fresh = [
        master * (1.0 - RATE_MUON * DECAY_MUON)
        - RATE_MUON * 0.2 * math.sqrt(master.shape[1] * shards) * rows_of(which, update)
        for which, master in enumerate(masters)
    ]

    moves = Moves("copies", ids)
    rows = qkv_master.shape[0]

    def row_place(back_group):
        who = lax.axis_index(PATCHES) - back_group * members
        return (pl.ds(pl.multiple_of(who * rows, rows), rows),)

    def has_group(offset):
        place = lax.axis_index(PATCHES) // members + offset
        return jnp.logical_and(place >= 0, place < MATRICES)

    def member_copies(source, source_at, target, target_at, after, there):
        for shift in range(1, members):
            moves.move(
                (PATCHES, members, shift),
                functools.partial(member_peer, members, shift),
                source,
                source_at,
                target,
                target_at,
                after,
                there,
                there,
            )

    places = []
    for item in fresh:
        source = moves.operand(item.astype(LOW))
        target = moves.output((rows * seq_count, item.shape[1]), LOW)
        own = functools.partial(row_place, 0)
        moves.keep(source, None, target, own)
        places.append((source, target, {}))

    def along_line(distance, way, source, target, numbers):
        both = lambda: jnp.logical_and(has_group(way), has_group(-distance * way))
        place = functools.partial(row_place, distance * way)
        numbers[way] = moves.move(
            (PATCHES, seq_count, way),
            functools.partial(group_peer, members, (MATRICES + way) % MATRICES),
            target if distance else source,
            place if distance else None,
            target,
            place,
            (numbers[way],) if distance else (),
            both,
            functools.partial(has_group, -(distance + 1) * way),
        )

    for source, target, numbers in places:
        for way in (1, -1):
            along_line(0, way, source, target, numbers)
    for source, target, numbers in places:
        member_copies(source, None, target, own, (), None)
    for distance in range(1, MATRICES):
        for source, target, numbers in places:
            for way in (1, -1):
                number = numbers[way]
                if distance < MATRICES - 1:
                    along_line(distance, way, source, target, numbers)
                place = functools.partial(row_place, distance * way)
                member_copies(
                    target, place, target, place, (number,), functools.partial(has_group, -distance * way)
                )
    copies = moves.run()

    io_grad = io_slices.reshape(2, padded, io_cols)[:, :values_count].astype(f32)
    ada_res = adam_update(ada_master, ada_first, ada_second, clip * grad_ada, RATE_ADAM)
    io_res = adam_update(io_proj, io_first, io_second, clip * io_grad, RATE_ADAM)
    cond_res = adam_update(cond_table, cond_first, cond_second, clip * grad_table, RATE_TABLE)
    pos_res = adam_update(pos_table, pos_first, pos_second, clip * grad_pos, RATE_TABLE)
    bias_res = adam_update(biases, bias_first, bias_second, clip * grad_bias, RATE_ADAM)
    matrices = []
    for which in (0, 3, 1, 2):
        matrices += [fresh[which], moments[which], copies[which]]
    return (loss_total, grad_norm, moment_sizes, *matrices, *ada_res, *io_res, *cond_res, *pos_res, *bias_res)


def fits_fast(mesh):
    seq, shards = mesh.shape[PATCHES], mesh.shape[SHARDS]
    return HEADS % seq == 0 and (HEADS // seq * HEAD) % LANES == 0 and seq % MATRICES == 0 and shards % 2 == 0


def solution(mesh):
    body = fast_body if fits_fast(mesh) else general_body
    return jax.shard_map(
        body,
        mesh=mesh,
        in_specs=(
            P(SHARDS, PATCHES, None),
            P(SHARDS, PATCHES, None),
            P(SHARDS),
            P(),
            P(None, SHARDS),
            P(PATCHES, SHARDS),
            P(PATCHES, SHARDS),
            P(None, SHARDS),
            P(PATCHES, SHARDS),
            P(PATCHES, SHARDS),
            P(None, SHARDS),
            P(PATCHES, SHARDS),
            P(PATCHES, SHARDS),
            P(None, SHARDS),
            P(PATCHES, SHARDS),
            P(PATCHES, SHARDS),
            P(None, SHARDS),
            P(PATCHES, SHARDS),
            P(PATCHES, SHARDS),
            P(PATCHES, SHARDS),
            P(None, None, SHARDS),
            P(None, None, SHARDS),
            P(None, None, SHARDS),
            P(None, SHARDS),
            P(None, SHARDS),
            P(None, SHARDS),
            P(PATCHES, SHARDS),
            P(PATCHES, SHARDS),
            P(PATCHES, SHARDS),
            P(SHARDS),
            P(SHARDS),
            P(SHARDS),
        ),
        out_specs=(
            P(),
            P(),
            P(),
            P(PATCHES, SHARDS),
            P(PATCHES, SHARDS),
            P(None, SHARDS),
            P(PATCHES, SHARDS),
            P(PATCHES, SHARDS),
            P(None, SHARDS),
            P(PATCHES, SHARDS),
            P(PATCHES, SHARDS),
            P(None, SHARDS),
            P(PATCHES, SHARDS),
            P(PATCHES, SHARDS),
            P(None, SHARDS),
            P(PATCHES, SHARDS),
            P(PATCHES, SHARDS),
            P(PATCHES, SHARDS),
            P(None, None, SHARDS),
            P(None, None, SHARDS),
            P(None, None, SHARDS),
            P(None, SHARDS),
            P(None, SHARDS),
            P(None, SHARDS),
            P(PATCHES, SHARDS),
            P(PATCHES, SHARDS),
            P(PATCHES, SHARDS),
            P(SHARDS),
            P(SHARDS),
            P(SHARDS),
        ),
        check_vma=False,
    )
```

```python
import functools
import math

import jax
import jax.numpy as jnp
from jax import lax
from jax.experimental import pallas as pl
from jax.experimental.pallas import tpu as pltpu
from jax.sharding import PartitionSpec as P

PATCHES = "seq"
SHARDS = "fsdp"
HEADS = 16
HEAD = 64
NI = 3
ROLL = 2
NS_ITERS = 5
STEP_NUM = 10
LON = 32


EPS_NORM = 1e-06
NS_A = 3.4445
NS_B = -4.775
NS_C = 2.0315
MOMENTUM = 0.5
RATE_MUON = 0.15
DECAY_MUON = 0.1
RATE_ADAM = 0.05
RATE_TABLE = 0.5
DECAY_ADAM = 0.1
BETA_FIRST = 0.9
BETA_SECOND = 0.95
CLIP_LIMIT = 0.01
HIGHEST_PRECISION = lax.Precision.HIGHEST


def broadcast(block, axis, owner):
    block = jnp.where(lax.axis_index(axis) == owner, block, jnp.zeros_like(block))
    return lax.psum(block, axis)


def product(left, right):
    return jnp.dot(left, right, preferred_element_type=jnp.float32)


def dot_last(left, right):
    return lax.dot_general(
        left, right, (((left.ndim - 1,), (1,)), ((), ())), preferred_element_type=jnp.float32
    )


def rows_product(left, right):
    flat_left = left.reshape(-1, left.shape[-1])
    flat_right = right.reshape(-1, right.shape[-1])
    return lax.dot_general(
        flat_left, flat_right, (((0,), (0,)), ((), ())), preferred_element_type=jnp.float32
    )


def layer_norm(values):
    centred = values - jnp.mean(values, -1, keepdims=True)
    inverse = lax.rsqrt(jnp.mean(centred * centred, -1, keepdims=True) + EPS_NORM)
    return (centred * inverse, inverse)


def norm_back(grad, normed, inverse):
    return inverse * (
        grad
        - jnp.mean(grad, -1, keepdims=True)
        - normed * jnp.mean(grad * normed, -1, keepdims=True)
    )


def heads_view(values):
    return values.reshape(values.shape[0], values.shape[1], HEADS, HEAD)


def modulation(modul, width):
    return [modul[:, None, column * width : (column + 1) * width] for column in range(6)]


def latitude_weights(local):
    all_patches = local * lax.axis_size(PATCHES)
    band_row = (jnp.arange(all_patches, dtype=jnp.int32) // LON).astype(jnp.float32)
    latitude = (band_row + 0.5) * (math.pi / (all_patches // LON)) - math.pi / 2
    cosine = jnp.cos(latitude)
    weights = cosine / jnp.mean(cosine)
    return lax.dynamic_slice_in_dim(weights, lax.axis_index(PATCHES) * local, local)


def forward_step(weights, state, active, select):
    w_qkv, w_out, w_up, w_down, w_ada, io_all, table, pos, bias = weights
    width = w_out.shape[0]
    cond_vec = jnp.dot(select, table.astype(jnp.float32), precision=HIGHEST_PRECISION)
    silu_low = jax.nn.silu(cond_vec).astype(jnp.bfloat16)
    modul = product(silu_low, w_ada) + bias[: 6 * width].astype(jnp.float32)
    shift1, scale1, gate1, shift2, scale2, gate2 = modulation(modul, width)
    state_low = state.astype(jnp.bfloat16)
    embedded = (
        product(state_low, io_all[0])
        + bias[6 * width :].astype(jnp.float32)
        + pos.astype(jnp.float32)
    )
    normed_one, inverse_one = layer_norm(embedded)
    normed_a = (normed_one * (1.0 + scale1) + shift1).astype(jnp.bfloat16)
    qkv = product(normed_a, w_qkv).astype(jnp.bfloat16)
    queries = qkv[..., :width]
    keys, values = (
        lax.all_gather(qkv[..., width : 2 * width], PATCHES, axis=1, tiled=True),
        lax.all_gather(qkv[..., 2 * width :], PATCHES, axis=1, tiled=True),
    )
    scores = jnp.einsum(
        "sphd,snhd->shpn", heads_view(queries), heads_view(keys), preferred_element_type=jnp.float32
    ) * HEAD ** (-0.5)
    top_score = jnp.max(scores, -1, keepdims=True)
    expo = jnp.exp(scores - top_score)
    total_exp = jnp.sum(expo, -1, keepdims=True)
    log_total = top_score + jnp.log(total_exp)
    probs_low = (expo / total_exp).astype(jnp.bfloat16)
    mixed = jnp.einsum(
        "shpn,snhd->sphd", probs_low, heads_view(values), preferred_element_type=jnp.float32
    )
    mixed_low = mixed.reshape(queries.shape).astype(jnp.bfloat16)
    attended = product(mixed_low, w_out)
    after_attn = embedded + gate1 * attended
    normed_two, inverse_two = layer_norm(after_attn)
    normed_b = (normed_two * (1.0 + scale2) + shift2).astype(jnp.bfloat16)
    upward = product(normed_b, w_up)
    hidden = jax.nn.gelu(upward).astype(jnp.bfloat16)
    downward = dot_last(hidden, w_down)
    after_mlp = after_attn + gate2 * downward
    normed_three, inverse_three = layer_norm(after_mlp)
    normed_c = normed_three.astype(jnp.bfloat16)
    delta = dot_last(normed_c, io_all[1])
    kept = (
        cond_vec,
        silu_low,
        modul,
        state_low,
        normed_one,
        inverse_one,
        normed_a,
        queries,
        keys,
        values,
        log_total,
        mixed_low,
        attended,
        normed_two,
        inverse_two,
        normed_b,
        upward,
        hidden,
        downward,
        normed_three,
        inverse_three,
        normed_c,
    )
    return (state + active * delta, kept)


def backward_step(weights, kept, grad_state, active, select):
    w_qkv, w_out, w_up, w_down, w_ada, io_all, table, pos, bias = weights
    (
        cond_vec,
        silu_low,
        modul,
        state_low,
        normed_one,
        inverse_one,
        normed_a,
        queries,
        keys,
        values,
        log_total,
        mixed_low,
        attended,
        normed_two,
        inverse_two,
        normed_b,
        upward,
        hidden,
        downward,
        normed_three,
        inverse_three,
        normed_c,
    ) = kept
    width = w_out.shape[0]
    shift1, scale1, gate1, shift2, scale2, gate2 = modulation(modul, width)
    delta_grad = (active * grad_state).astype(jnp.bfloat16)
    grad_head = rows_product(delta_grad, normed_c)
    grad_mlp = norm_back(product(delta_grad, io_all[1]), normed_three, inverse_three)
    grad_gate2 = jnp.sum(grad_mlp * downward, 1)
    down_grad = (gate2 * grad_mlp).astype(jnp.bfloat16)
    grad_down = rows_product(down_grad, hidden)
    grad_hidden = product(down_grad, w_down)
    up_grad = jax.vjp(jax.nn.gelu, upward)[1](grad_hidden)[0].astype(jnp.bfloat16)
    grad_up = rows_product(normed_b, up_grad)
    grad_normed_b = dot_last(up_grad, w_up)
    grad_scale2 = jnp.sum(grad_normed_b * normed_two, 1)
    grad_shift2 = jnp.sum(grad_normed_b, 1)
    grad_attn = grad_mlp + norm_back(grad_normed_b * (1.0 + scale2), normed_two, inverse_two)
    grad_gate1 = jnp.sum(grad_attn * attended, 1)
    attn_grad = (gate1 * grad_attn).astype(jnp.bfloat16)
    grad_out = rows_product(mixed_low, attn_grad)
    mixed_grad = dot_last(attn_grad, w_out).astype(jnp.bfloat16)
    q_heads = heads_view(queries)
    k_heads = heads_view(keys)
    v_heads = heads_view(values)
    g_heads = heads_view(mixed_grad)
    scores = jnp.einsum(
        "sphd,snhd->shpn", q_heads, k_heads, preferred_element_type=jnp.float32
    ) * HEAD ** (-0.5)
    probs = jnp.exp(scores - log_total)
    probs_low = probs.astype(jnp.bfloat16)
    grad_probs = jnp.einsum("sphd,snhd->shpn", g_heads, v_heads, preferred_element_type=jnp.float32)
    score_grad = (
        HEAD ** (-0.5) * probs * (grad_probs - jnp.sum(grad_probs * probs, -1, keepdims=True))
    ).astype(jnp.bfloat16)
    grad_queries = jnp.einsum(
        "shpn,snhd->sphd", score_grad, k_heads, preferred_element_type=jnp.float32
    ).reshape(queries.shape)
    key_part = jnp.einsum(
        "shpn,sphd->snhd", score_grad, q_heads, preferred_element_type=jnp.float32
    ).reshape(keys.shape)
    value_part = jnp.einsum(
        "shpn,sphd->snhd", probs_low, g_heads, preferred_element_type=jnp.float32
    ).reshape(values.shape)
    grad_keys, grad_values = (
        lax.psum_scatter(key_part, PATCHES, scatter_dimension=1, tiled=True),
        lax.psum_scatter(value_part, PATCHES, scatter_dimension=1, tiled=True),
    )
    qkv_grad = jnp.concatenate([grad_queries, grad_keys, grad_values], -1).astype(jnp.bfloat16)
    grad_qkv = rows_product(normed_a, qkv_grad)
    grad_normed_a = dot_last(qkv_grad, w_qkv)
    grad_scale1 = jnp.sum(grad_normed_a * normed_one, 1)
    grad_shift1 = jnp.sum(grad_normed_a, 1)
    grad_embedded = grad_attn + norm_back(grad_normed_a * (1.0 + scale1), normed_one, inverse_one)
    embed_grad = grad_embedded.astype(jnp.bfloat16)
    grad_embed = rows_product(state_low, embed_grad)
    grad_prev = grad_state + dot_last(embed_grad, io_all[0])
    grad_modul = jnp.concatenate(
        [grad_shift1, grad_scale1, grad_gate1, grad_shift2, grad_scale2, grad_gate2], -1
    )
    grad_ada = lax.dot_general(
        silu_low.astype(jnp.float32),
        grad_modul,
        (((0,), (0,)), ((), ())),
        precision=HIGHEST_PRECISION,
    )
    grad_silu = lax.dot_general(
        grad_modul, w_ada.astype(jnp.float32), (((1,), (1,)), ((), ())), precision=HIGHEST_PRECISION
    )
    grad_cond = jax.vjp(jax.nn.silu, cond_vec)[1](grad_silu)[0]
    grad_table = lax.dot_general(
        select, grad_cond, (((0,), (0,)), ((), ())), precision=HIGHEST_PRECISION
    )
    grad_bias = jnp.concatenate([jnp.sum(grad_modul, 0), jnp.sum(grad_embedded, (0, 1))])
    grad_pos = jnp.sum(grad_embedded, 0)
    grads = (
        grad_qkv,
        grad_out,
        grad_up,
        grad_down,
        grad_ada,
        jnp.stack([grad_embed, grad_head]),
        grad_table,
        grad_pos,
        grad_bias,
    )
    return (grad_prev, grads)


def gram_part(block_cols):
    return lax.dot_general(
        block_cols, block_cols, (((1,), (1,)), ((), ())), preferred_element_type=jnp.float32
    )


def zero_gram(block_cols):
    return jnp.zeros((block_cols.shape[0], block_cols.shape[0]), jnp.float32)


def newton_step(block_cols, gram):
    gram_low = gram.astype(jnp.bfloat16)
    poly = (NS_B * gram_low.astype(jnp.float32) + NS_C * product(gram_low, gram_low)).astype(
        jnp.bfloat16
    )
    return (NS_A * block_cols.astype(jnp.float32) + product(poly, block_cols)).astype(jnp.bfloat16)


def keep_block(block_cols, gram):
    return block_cols


def adam_update(weight, first, second, grad, rate):
    first_new = BETA_FIRST * first + (1.0 - BETA_FIRST) * grad
    second_new = BETA_SECOND * second + (1.0 - BETA_SECOND) * grad * grad
    unbiased = first_new / (1.0 - BETA_FIRST**STEP_NUM)
    spread = jnp.sqrt(second_new / (1.0 - BETA_SECOND**STEP_NUM)) + 1e-08
    return (weight * (1.0 - rate * DECAY_ADAM) - rate * unbiased / spread, first_new, second_new)


def general_body(
    states,
    targets,
    lengths,
    intervals,
    qkv_copy,
    qkv_master,
    qkv_moment,
    out_copy,
    out_master,
    out_moment,
    up_copy,
    up_master,
    up_moment,
    down_copy,
    down_master,
    down_moment,
    ada_copy,
    ada_master,
    ada_first,
    ada_second,
    io_proj,
    io_first,
    io_second,
    cond_table,
    cond_first,
    cond_second,
    pos_table,
    pos_first,
    pos_second,
    biases,
    bias_first,
    bias_second,
):
    weights = (
        lax.all_gather(qkv_copy, SHARDS, axis=1, tiled=True),
        lax.all_gather(out_copy, SHARDS, axis=1, tiled=True),
        lax.all_gather(up_copy, SHARDS, axis=1, tiled=True),
        lax.all_gather(down_copy, SHARDS, axis=1, tiled=True),
        lax.all_gather(ada_copy, SHARDS, axis=1, tiled=True),
        lax.all_gather(io_proj.astype(jnp.bfloat16), SHARDS, axis=2, tiled=True),
        lax.all_gather(cond_table.astype(jnp.bfloat16), SHARDS, axis=1, tiled=True),
        lax.all_gather(pos_table.astype(jnp.bfloat16), SHARDS, axis=1, tiled=True),
        lax.all_gather(biases.astype(jnp.bfloat16), SHARDS, axis=0, tiled=True),
    )
    samples, local, values_count = states.shape
    table_rows = cond_table.shape[0]
    my_ids = lax.dynamic_slice_in_dim(intervals, lax.axis_index(SHARDS) * samples, samples)
    counts = jnp.sum(
        (intervals[:, None] == jnp.arange(NI, dtype=jnp.int32)[None]).astype(jnp.float32), 0
    )
    id_counts = jnp.sum(
        (my_ids[:, None] == jnp.arange(NI, dtype=jnp.int32)[None]).astype(jnp.float32)
        * counts[None],
        1,
    )
    weight = 1.0 / (NI * local * lax.axis_size(PATCHES) * values_count * id_counts)
    rows_iota = jnp.arange(table_rows, dtype=jnp.int32)
    id_select = (my_ids[:, None] == rows_iota[None]).astype(jnp.float32)
    state = states.astype(jnp.float32)
    seen_states = []
    kept_all = []
    for step in range(ROLL):
        select = id_select + (rows_iota == NI + step).astype(jnp.float32)[None]
        active = (step < lengths).astype(jnp.float32)[:, None, None]
        seen_states.append(state)
        state, kept = forward_step(weights, state, active, select)
        kept_all.append(kept)
    lat = latitude_weights(local)
    diff = state - targets.astype(jnp.float32)
    err = jnp.sum(jnp.sum(diff * diff, -1) * lat[None], -1)
    loss_local = jnp.sum(weight * err)
    grad_state = 2.0 * weight[:, None, None] * lat[None, :, None] * diff
    totals = None
    for step in reversed(range(ROLL)):
        select = id_select + (rows_iota == NI + step).astype(jnp.float32)[None]
        active = (step < lengths).astype(jnp.float32)[:, None, None]
        kept = kept_all[step]
        grad_state, grads = backward_step(weights, kept, grad_state, active, select)
        totals = grads if totals is None else jax.tree.map(jnp.add, totals, grads)
    reduced = (
        lax.psum_scatter(totals[0], SHARDS, scatter_dimension=1, tiled=True),
        lax.psum_scatter(totals[1], SHARDS, scatter_dimension=1, tiled=True),
        lax.psum_scatter(totals[2], SHARDS, scatter_dimension=1, tiled=True),
        lax.psum_scatter(totals[3], SHARDS, scatter_dimension=1, tiled=True),
        lax.psum_scatter(totals[4], SHARDS, scatter_dimension=1, tiled=True),
        lax.psum_scatter(totals[5], SHARDS, scatter_dimension=2, tiled=True),
        lax.psum_scatter(totals[6], SHARDS, scatter_dimension=1, tiled=True),
        lax.psum_scatter(totals[7], SHARDS, scatter_dimension=1, tiled=True),
        lax.psum_scatter(totals[8], SHARDS, scatter_dimension=0, tiled=True),
    )
    large = (
        lax.psum_scatter(reduced[0], PATCHES, scatter_dimension=0, tiled=True),
        lax.psum_scatter(reduced[1], PATCHES, scatter_dimension=0, tiled=True),
        lax.psum_scatter(reduced[2], PATCHES, scatter_dimension=0, tiled=True),
        lax.psum_scatter(reduced[3], PATCHES, scatter_dimension=0, tiled=True),
        lax.psum_scatter(reduced[4], PATCHES, scatter_dimension=0, tiled=True),
    )
    small = lax.psum((reduced[5], reduced[6], reduced[8]), PATCHES)
    grad_pos = reduced[7]
    first_copy = (lax.axis_index(PATCHES) == 0).astype(jnp.float32)
    squares = jnp.sum(grad_pos * grad_pos)
    for item in large:
        squares = squares + jnp.sum(item * item)
    small_squares = jnp.float32(0.0)
    for item in small:
        small_squares = small_squares + jnp.sum(item * item)
    squares, loss_total = lax.psum(
        (squares + first_copy * small_squares, loss_local), (PATCHES, SHARDS)
    )
    grad_norm = jnp.sqrt(squares)
    clip = jnp.minimum(1.0, CLIP_LIMIT / (grad_norm + 1e-06))
    masters = (qkv_master, out_master, up_master, down_master)
    moments = [
        MOMENTUM * old + clip * grad
        for old, grad in zip((qkv_moment, out_moment, up_moment, down_moment), large[:4])
    ]
    norms = lax.psum(
        (
            jnp.sum(moments[0] * moments[0]),
            jnp.sum(moments[1] * moments[1]),
            jnp.sum(moments[2] * moments[2]),
            jnp.sum(moments[3] * moments[3]),
        ),
        (PATCHES, SHARDS),
    )
    sizes = [jnp.sqrt(norms[which]) for which in range(4)]
    moment_sizes = jnp.stack(sizes) / CLIP_LIMIT
    scaled = [(moments[which] / (sizes[which] + 1e-07)).astype(jnp.bfloat16) for which in range(4)]
    columns = (
        lax.all_gather(scaled[0], PATCHES, axis=0, tiled=True),
        lax.all_gather(scaled[1], PATCHES, axis=0, tiled=True),
        lax.all_gather(scaled[2], PATCHES, axis=0, tiled=True),
        lax.all_gather(scaled[3], PATCHES, axis=0, tiled=True),
    )
    seq_index = lax.axis_index(PATCHES)
    seq_count = lax.axis_size(PATCHES)
    owners = [seq_index == which % seq_count for which in range(4)]
    blocks = list(columns)
    for turn in range(NS_ITERS):
        partial_value = [
            lax.cond(owners[which], gram_part, zero_gram, blocks[which]) for which in range(4)
        ]
        grams = lax.psum(
            (partial_value[0], partial_value[1], partial_value[2], partial_value[3]), SHARDS
        )
        blocks = [
            lax.cond(owners[which], newton_step, keep_block, blocks[which], grams[which])
            for which in range(4)
        ]
    blocks = [broadcast(blocks[which], PATCHES, which % seq_count) for which in range(4)]
    row_count = qkv_master.shape[0]
    fresh = []
    for which in range(4):
        my_rows = lax.dynamic_slice_in_dim(
            blocks[which], seq_index * row_count, row_count, 0
        ).astype(jnp.float32)
        all_cols = masters[which].shape[1] * lax.axis_size(SHARDS)
        fresh.append(
            masters[which] * (1.0 - RATE_MUON * DECAY_MUON)
            - RATE_MUON * 0.2 * math.sqrt(all_cols) * my_rows
        )
    copies = (
        lax.all_gather(fresh[0].astype(jnp.bfloat16), PATCHES, axis=0, tiled=True),
        lax.all_gather(fresh[1].astype(jnp.bfloat16), PATCHES, axis=0, tiled=True),
        lax.all_gather(fresh[2].astype(jnp.bfloat16), PATCHES, axis=0, tiled=True),
        lax.all_gather(fresh[3].astype(jnp.bfloat16), PATCHES, axis=0, tiled=True),
    )
    ada_res = adam_update(ada_master, ada_first, ada_second, clip * large[4], RATE_ADAM)
    io_res = adam_update(io_proj, io_first, io_second, clip * small[0], RATE_ADAM)
    cond_res = adam_update(cond_table, cond_first, cond_second, clip * small[1], RATE_TABLE)
    pos_res = adam_update(pos_table, pos_first, pos_second, clip * grad_pos, RATE_TABLE)
    bias_res = adam_update(biases, bias_first, bias_second, clip * small[2], RATE_ADAM)
    return (
        loss_total,
        grad_norm,
        moment_sizes,
        fresh[0],
        moments[0],
        copies[0],
        fresh[1],
        moments[1],
        copies[1],
        fresh[2],
        moments[2],
        copies[2],
        fresh[3],
        moments[3],
        copies[3],
        ada_res[0],
        ada_res[1],
        ada_res[2],
        io_res[0],
        io_res[1],
        io_res[2],
        cond_res[0],
        cond_res[1],
        cond_res[2],
        pos_res[0],
        pos_res[1],
        pos_res[2],
        bias_res[0],
        bias_res[1],
        bias_res[2],
    )


LANES = 128
MATRICES = 4
LOW = jnp.bfloat16
MESH = pl.DeviceIdType.MESH


def round_up(value, unit):
    return -(-value // unit) * unit


def member_peer(members, shift):
    index = lax.axis_index(PATCHES)
    return {PATCHES: index // members * members + lax.rem(lax.rem(index, members) + shift, members)}


def group_peer(members, shift):
    return {PATCHES: lax.rem(lax.axis_index(PATCHES) + shift * members, lax.axis_size(PATCHES))}


def sibling_peer():
    index = lax.axis_index(SHARDS)
    return {SHARDS: index + 1 - 2 * lax.rem(index, 2)}


def where(condition, action):
    if condition is None:
        action()
    else:
        pl.when(condition())(action)


class Moves:
    def __init__(self, name, ids, vmem=None):
        self.name = name
        self.ids = ids
        self.vmem = vmem
        self.operands = []
        self.operand_specs = []
        self.outputs = []
        self.output_specs = []
        self.scratches = []
        self.moves = []
        self.locals = []
        self.steps = []
        self.peers = {}

    def operand(self, array, space=pl.ANY):
        self.operands.append(array)
        self.operand_specs.append(pl.BlockSpec(memory_space=space))
        return (0, len(self.operands) - 1)

    def output(self, shape, dtype, space=pl.ANY):
        self.outputs.append(jax.ShapeDtypeStruct(shape, dtype))
        self.output_specs.append(pl.BlockSpec(memory_space=space))
        return (1, len(self.outputs) - 1)

    def scratch(self, shape, dtype):
        self.scratches.append(pltpu.VMEM(shape, dtype))
        return (2, len(self.scratches) - 1)

    def keep(self, source, source_at, target, target_at, later=False):
        self.locals.append((source, source_at, target, target_at, later))
        return len(self.locals) - 1

    def shape(self, scratch):
        return self.scratches[scratch[1]].shape

    def load(self, array):
        target = self.scratch(array.shape, array.dtype)
        return target, self.keep(self.operand(array), None, target, None)

    def save(self, source, shape, dtype):
        number = self.keep(source, None, self.output(shape, dtype), None, True)
        return number

    def start_local(self, number):
        self.steps.append((self.begin_local, number))

    def begin_local(self, number):
        self.local[number].start()

    def move(
        self, peer_key, peer, source, source_at, target, target_at, after=(), sends=None, takes=None, later=False
    ):
        number = len(self.moves)
        self.peers.setdefault(peer_key, peer)
        self.moves.append((peer_key, source, source_at, target, target_at, sends, takes, later or bool(after)))
        for earlier in after:
            self.steps.append((self.await_move, earlier))
        if after:
            self.steps.append((self.start_move, number))
        return number

    def wait_for(self, number):
        self.steps.append((self.await_move, number))

    def start(self, number):
        self.steps.append((self.start_move, number))

    def wait_local(self, number):
        self.steps.append((self.await_local, number))

    def task(self, action):
        self.steps.append((self.do_task, action))

    def await_move(self, number):
        if number not in self.arrived:
            self.arrived.add(number)
            where(self.moves[number][6], self.remote[number].wait_recv)

    def start_move(self, number):
        where(self.moves[number][5], self.remote[number].start)

    def await_local(self, number):
        if number not in self.kept:
            self.kept.add(number)
            self.local[number].wait()

    def do_task(self, action):
        action(self.ref)

    def ref(self, which):
        return self.refs[which[0]][which[1]]

    def view(self, which, index):
        ref = self.ref(which)
        return ref.at[index()] if index is not None else ref

    def kernel(self, *refs):
        sizes = (len(self.operands), len(self.outputs), len(self.scratches))
        self.refs = (refs[: sizes[0]], refs[sizes[0] : sizes[0] + sizes[1]], refs[sizes[0] + sizes[1] : sum(sizes)])
        local_sem, send_sem, recv_sem = refs[sum(sizes) :]
        self.arrived, self.kept = set(), set()
        devices = {key: peer() for key, peer in self.peers.items()}
        barrier = pltpu.get_barrier_semaphore()
        for device in devices.values():
            pl.semaphore_signal(barrier, inc=1, device_id=device, device_id_type=MESH)
        pl.semaphore_wait(barrier, len(devices))
        self.remote = []
        for number, (key, source, source_at, target, target_at, _, _, later) in enumerate(self.moves):
            self.remote.append(
                pltpu.make_async_remote_copy(
                    src_ref=self.view(source, source_at),
                    dst_ref=self.view(target, target_at),
                    send_sem=send_sem.at[number],
                    recv_sem=recv_sem.at[number],
                    device_id=devices[key],
                    device_id_type=MESH,
                )
            )
            if not later:
                self.start_move(number)
        self.local = [
            pltpu.make_async_copy(self.view(source, source_at), self.view(target, target_at), local_sem.at[number])
            for number, (source, source_at, target, target_at, _) in enumerate(self.locals)
        ]
        for copy, entry in zip(self.local, self.locals):
            if not entry[4]:
                copy.start()
        for action, number in self.steps:
            action(number)
        for number in range(len(self.locals)):
            self.await_local(number)
        for number, copy in enumerate(self.remote):
            self.await_move(number)
            where(self.moves[number][5], copy.wait_send)

    def run(self):
        return pl.pallas_call(
            self.kernel,
            out_shape=self.outputs,
            in_specs=self.operand_specs,
            out_specs=self.output_specs,
            scratch_shapes=[
                *self.scratches,
                pltpu.SemaphoreType.DMA((max(1, len(self.locals)),)),
                pltpu.SemaphoreType.DMA((len(self.moves),)),
                pltpu.SemaphoreType.DMA((len(self.moves),)),
            ],
            compiler_params=pltpu.CompilerParams(
                collective_id=self.ids.setdefault(self.name, len(self.ids)),
                has_side_effects=True,
                vmem_limit_bytes=self.vmem,
            ),
            name=self.name,
        )(*self.operands)

    def along(self, axis, source, target, pairs, later=False):
        numbers = []
        count = lax.axis_size(axis)

        def other(shift):
            return lax.rem(lax.axis_index(axis) + shift, count)

        for shift in range(1, count):
            for source_at, target_at in pairs:
                numbers.append(
                    self.move(
                        (axis, shift),
                        lambda shift=shift: {axis: other(shift)},
                        source,
                        None if source_at is None else (lambda at=source_at, shift=shift: at(other(shift))),
                        target,
                        lambda at=target_at: at(lax.axis_index(axis)),
                        later=later,
                    )
                )
        for source_at, target_at in pairs:
            self.keep(
                source,
                None if source_at is None else (lambda at=source_at: at(lax.axis_index(axis))),
                target,
                lambda at=target_at: at(lax.axis_index(axis)),
            )
        return numbers

    def gather(self, axis, array):
        target = self.output((lax.axis_size(axis),) + array.shape, array.dtype)
        self.along(axis, self.operand(array), target, [(None, lambda sender: (sender,))])

    def gather_pairs(self, array, parts=1, hold=False):
        shards = lax.axis_size(SHARDS)
        source = self.operand(array)
        target = self.output((shards,) + array.shape, array.dtype)
        rows = array.shape[0] // parts

        def place(back_pair, part):
            return (lax.rem(lax.axis_index(SHARDS) + shards - 2 * back_pair, shards), pl.ds(part * rows, rows))

        firsts = []
        for part in range(parts):
            for pair in range(1, shards // 2):
                number = self.move(
                    (SHARDS, 2 * pair),
                    lambda pair=pair: {SHARDS: lax.rem(lax.axis_index(SHARDS) + 2 * pair, shards)},
                    source,
                    lambda part=part: (pl.ds(part * rows, rows),),
                    target,
                    functools.partial(place, 0, part),
                )
                firsts.append((functools.partial(place, pair, part), number))
        own = lambda: (lax.axis_index(SHARDS),)
        self.move((SHARDS,), sibling_peer, source, None, target, own)
        self.keep(source, None, target, own)
        waiting = [(target, at, number) for at, number in firsts]
        if hold:
            return waiting
        self.to_sibling(waiting)

    def gather_columns(self, axis, array, target):
        width = array.shape[-1]
        lead = (slice(None),) * (array.ndim - 1)
        numbers = self.along(
            axis,
            self.operand(array),
            target,
            [(None, lambda sender: lead + (pl.ds(pl.multiple_of(sender * width, LANES), width),))],
        )
        return numbers, len(self.locals) - 1

    def gather_twice(self, arrays, members):
        shards = lax.axis_size(SHARDS)
        entries = []
        for array in arrays:
            source = self.operand(array)
            width = array.shape[1]
            target = self.scratch((array.shape[0], shards * width), array.dtype)
            rows = array.shape[0] // members

            def columns(back_pair, width=width):
                who = lax.rem(lax.axis_index(SHARDS) + shards - 2 * back_pair, shards)
                return pl.ds(pl.multiple_of(who * width, LANES), width)

            def place(back_member, back_pair, rows=rows, columns=columns):
                index = lax.rem(lax.rem(lax.axis_index(PATCHES), members) + members - back_member, members)
                return (pl.ds(pl.multiple_of(index * rows, rows), rows), columns(back_pair))

            def mine(rows=rows):
                index = lax.rem(lax.axis_index(PATCHES), members)
                return (pl.ds(pl.multiple_of(index * rows, rows), rows),)

            def whole(columns=columns):
                return (slice(None), columns(0))

            firsts = [
                self.move(
                    (SHARDS, 2 * pair),
                    lambda pair=pair: {SHARDS: lax.rem(lax.axis_index(SHARDS) + 2 * pair, shards)},
                    source,
                    mine,
                    target,
                    functools.partial(place, 0, 0),
                )
                for pair in range(1, shards // 2)
            ]
            near = self.move((SHARDS,), sibling_peer, source, None, target, whole)
            local = self.keep(source, None, target, whole)
            entries.append((target, place, firsts, [near, *firsts], local))
        last = []
        for target, place, firsts, numbers, _ in entries:
            for pair, first in enumerate(firsts, 1):
                near = functools.partial(place, 0, pair)
                for shift in range(1, members):
                    number = self.move(
                        (PATCHES, members, shift),
                        functools.partial(member_peer, members, shift),
                        target,
                        near,
                        target,
                        near,
                        (first,),
                    )
                    last.append((target, functools.partial(place, shift, pair), number, numbers))
                numbers.append(self.move((SHARDS,), sibling_peer, target, near, target, near, (first,)))
        for target, at, number, numbers in last:
            numbers += [number, self.move((SHARDS,), sibling_peer, target, at, target, at, (number,))]
        return [(target, numbers, local) for target, _, _, numbers, local in entries]

    def to_sibling(self, waiting):
        for target, place, number in waiting:
            self.move((SHARDS,), sibling_peer, target, place, target, place, (number,))

    def exchange(self, axis, array, later=False):
        target = self.output(array.shape, array.dtype)
        return self.along(
            axis, self.operand(array), target, [(lambda receiver: (receiver,), lambda sender: (sender,))], later
        )

    def exchange_columns(self, axis, array):
        width = array.shape[-1] // lax.axis_size(axis)
        target = self.output((lax.axis_size(axis), array.shape[0], width), array.dtype)
        self.along(
            axis,
            self.operand(array),
            target,
            [
                (
                    lambda receiver: (slice(None), pl.ds(pl.multiple_of(receiver * width, LANES), width)),
                    lambda sender: (sender,),
                )
            ],
        )

    def rows_to_heads(self, axis, array, planes, target):
        count, rows = lax.axis_size(axis), array.shape[0]
        columns = array.shape[1] // planes
        width = columns // count
        return self.along(
            axis,
            self.operand(array),
            target,
            [
                (
                    lambda receiver, plane=plane: (
                        slice(None),
                        pl.ds(pl.multiple_of(plane * columns + receiver * width, LANES), width),
                    ),
                    lambda sender, plane=plane: (plane, pl.ds(pl.multiple_of(sender * rows, rows), rows)),
                )
                for plane in range(planes)
            ],
        )

    def head_rows(self, source, target, planes, rows, columns, members, back_group):
        count = lax.axis_size(PATCHES)
        width = columns // count
        for shift_member in range(members):
            for plane in planes:

                def peer(shift_member=shift_member):
                    index = lax.axis_index(PATCHES)
                    there = lax.rem(index // members + back_group, MATRICES) * members
                    return there + lax.rem(lax.rem(index, members) + shift_member, members)

                def source_at(peer=peer, plane=plane):
                    return (plane, pl.ds(pl.multiple_of(peer() * rows, rows), rows))

                def target_at(plane=plane):
                    start = plane * columns + lax.axis_index(PATCHES) * width
                    return (slice(None), pl.ds(pl.multiple_of(start, LANES), width))

                if shift_member or back_group:
                    self.start(
                        self.move(
                            (PATCHES, count, back_group, shift_member),
                            lambda peer=peer: {PATCHES: peer()},
                            source,
                            source_at,
                            target,
                            target_at,
                            later=True,
                        )
                    )
                else:

                    def own(ref, source_at=source_at, target_at=target_at):
                        ref(target)[target_at()] = ref(source)[source_at()]

                    self.task(own)


def total_of(ids, values, shared):
    moves = Moves("total", ids)
    source, result = moves.operand(values, pltpu.VMEM), moves.output(values.shape, values.dtype, pltpu.VMEM)
    moves.gather(PATCHES, shared)
    for axis in (SHARDS, PATCHES):
        count = lax.axis_size(axis)
        buffer = moves.scratch((count,) + values.shape, values.dtype)

        def own(axis=axis):
            return (lax.axis_index(axis),)

        def put(ref, source=source, buffer=buffer, own=own):
            ref(buffer)[own()] = ref(source)[...]

        moves.task(put)
        numbers = []
        for shift in range(1, count):
            numbers.append(
                moves.move(
                    (axis, shift),
                    lambda axis=axis, shift=shift, count=count: {axis: lax.rem(lax.axis_index(axis) + shift, count)},
                    buffer,
                    own,
                    buffer,
                    own,
                    later=True,
                )
            )
            moves.start(numbers[-1])
        for number in numbers:
            moves.wait_for(number)

        def add(ref, buffer=buffer):
            ref(result)[...] = jnp.sum(ref(buffer)[...], 0)

        moves.task(add)
        source = result
    return moves.run()


def contract(left, right, left_dim, right_dim):
    return lax.dot_general(
        left, right, (((left_dim,), (right_dim,)), ((), ())), preferred_element_type=jnp.float32
    )


CHAIN_CHUNKS = 8
GRAM_COLS = 256


def attend(queries, keys, values):
    scores = contract(queries, keys, 1, 1) * HEAD ** (-0.5)
    expo = jnp.exp(scores - jnp.max(scores, -1, keepdims=True))
    probs = (expo / jnp.sum(expo, -1, keepdims=True)).astype(LOW)
    return contract(probs, values, 1, 0)


def group_rows(rows, members, shift):
    size = rows * members
    there = lax.rem(lax.axis_index(PATCHES) // members + shift, MATRICES)
    return pl.ds(pl.multiple_of(there * size, size), size)


def add_attention(moves, qkv, mixed, arrivals, rows, members, waiting):
    for number in arrivals:
        moves.wait_for(number)
    for number in range(3):
        moves.wait_local(number)
    moves.to_sibling(waiting)
    count = lax.axis_size(PATCHES)
    width = HEADS // count * HEAD
    buffer = moves.scratch((1, rows * count, width), LOW)
    for shift in (*range(1, MATRICES), 0):

        def work(ref, shift=shift):
            at = group_rows(rows, members, shift)
            parts = []
            for head in range(width // HEAD):
                lanes = pl.ds(head * HEAD, HEAD)
                parts.append(attend(ref(qkv)[0, at, lanes], ref(qkv)[1, :, lanes], ref(qkv)[2, :, lanes]))
            ref(buffer)[0, at, :] = jnp.concatenate(parts, -1).astype(LOW)

        moves.task(work)
        moves.head_rows(buffer, mixed, (0,), rows, width * count, members, shift)


def add_attention_back(moves, qkv, grads, result, arrivals, rows, members, waiting):
    for number in arrivals:
        moves.wait_for(number)
    moves.wait_local(0)
    moves.to_sibling(waiting)
    count = lax.axis_size(PATCHES)
    width = HEADS // count * HEAD
    heads = width // HEAD
    buffer = moves.scratch((3, rows * count, width), LOW)
    key_total = moves.scratch((heads, rows * count, HEAD), jnp.float32)
    value_total = moves.scratch((heads, rows * count, HEAD), jnp.float32)
    for shift in (*range(1, MATRICES), 0):

        def work(ref, shift=shift):
            at = group_rows(rows, members, shift)
            parts = []
            for head in range(heads):
                lanes = pl.ds(head * HEAD, HEAD)
                queries, keys, values = ref(qkv)[0, at, lanes], ref(qkv)[1, :, lanes], ref(qkv)[2, :, lanes]
                grad = ref(grads)[0, at, lanes]
                scores = contract(keys, queries, 1, 1) * HEAD ** (-0.5)
                expo = jnp.exp(scores - jnp.max(scores, 0, keepdims=True))
                probs = expo / jnp.sum(expo, 0, keepdims=True)
                grad_probs = contract(values, grad, 1, 1)
                shared = jnp.sum(grad_probs * probs, 0, keepdims=True)
                score_grad = (HEAD ** (-0.5) * probs * (grad_probs - shared)).astype(LOW)
                parts.append(contract(score_grad, keys, 0, 0))
                key_part = contract(score_grad, queries, 1, 0)
                value_part = contract(probs.astype(LOW), grad, 1, 0)
                if shift == 1:
                    ref(key_total)[head] = key_part
                    ref(value_total)[head] = value_part
                else:
                    ref(key_total)[head] += key_part
                    ref(value_total)[head] += value_part
            ref(buffer)[0, at, :] = jnp.concatenate(parts, -1).astype(LOW)

        moves.task(work)
        moves.head_rows(buffer, result, (0,), rows, width * count, members, shift)

    def finish(ref):
        for plane, total in ((1, key_total), (2, value_total)):
            ref(buffer)[plane] = jnp.concatenate([ref(total)[head] for head in range(heads)], -1).astype(LOW)

    moves.task(finish)
    for shift in (*range(1, MATRICES), 0):
        moves.head_rows(buffer, result, (1, 2), rows, width * count, members, shift)


def mod_row(ref, table, row):
    return ref(table)[pl.ds(row, 1), :]


def project(moves, source, weights, target, count):
    def action(ref):
        width = ref(source).shape[1]

        @pl.loop(0, count // width)
        def _(part):
            cols = pl.ds(pl.multiple_of(part * width, width), width)
            ref(target)[:, cols] = contract(ref(source)[...], ref(weights)[:, cols], 1, 0).astype(LOW)

    moves.task(action)


def embed(ref, state_low, io_weights, mods, pos, embedded, normed_low):
    value = contract(ref(state_low)[...], io_weights, 1, 0) + mods(6) + ref(pos)[...].astype(jnp.float32)
    ref(embedded)[...] = value
    normed, _ = layer_norm(value)
    ref(normed_low)[...] = (normed * (1.0 + mods(1)) + mods(0)).astype(LOW)


def begin_step(ids, members, state, id_rows, active, cond_table, biases, pos, ada, io_low, w_out, w_qkv):
    f32 = jnp.float32
    shards = lax.axis_size(SHARDS)
    (rows, padded), (table_rows, _) = state.shape, cond_table.shape
    width = w_out.shape[0]
    ada_cols = ada.shape[1]
    moves = Moves("begin", ids, 56 * 2**20)
    table = moves.scratch((table_rows, width), f32)
    bias = moves.scratch((1, biases.shape[1] * shards), f32)
    pos_all = moves.scratch((rows, width), LOW)
    id_rows, active, state = [moves.operand(item, pltpu.VMEM) for item in (id_rows, active, state)]
    small = [moves.gather_columns(SHARDS, cond_table, table), moves.gather_columns(SHARDS, biases, bias)]
    pos_moves, pos_local = moves.gather_columns(SHARDS, pos, pos_all)
    ada_weights, ada_load = moves.load(ada)
    vmem = functools.partial(moves.output, space=pltpu.VMEM)
    extras = vmem((ROLL, 8, width), f32)
    cond_vec, silu_low = vmem((shards * ROLL, width), f32), vmem((shards * ROLL, width), LOW)
    embedded, normed_low = vmem((rows, width), f32), vmem((rows, width), LOW)
    state_low, qkv_rows = vmem((rows, padded), LOW), vmem((rows, 3 * width), LOW)
    parts_leaving, parts = [moves.scratch((shards, ROLL, ada_cols), f32) for _ in range(2)]

    def modulate(ref):
        row = lax.broadcasted_iota(jnp.int32, (shards * ROLL, 1), 0)
        ids_here = ref(id_rows)[:, :1]
        value = jnp.zeros((shards * ROLL, width), f32)
        for entry in range(table_rows):
            of_entry = ref(table)[pl.ds(entry, 1), :].astype(LOW).astype(f32)
            chosen = (ids_here == entry) if entry < NI else (lax.rem(row, ROLL) == entry - NI)
            value = value + jnp.where(chosen, of_entry, 0.0)
        ref(cond_vec)[...] = value
        value = (value / (1.0 + jnp.exp(-value))).astype(LOW)
        ref(silu_low)[...] = value
        start = pl.multiple_of(lax.axis_index(SHARDS) * ada_cols, LANES)
        value = contract(value, ref(ada_weights)[...], 1, 0)
        value = value + ref(bias)[:, pl.ds(start, ada_cols)].astype(LOW).astype(f32)
        for sample in range(shards):
            ref(parts_leaving)[sample] = value[sample * ROLL : (sample + 1) * ROLL]
        ref(parts)[lax.axis_index(SHARDS)] = ref(parts_leaving)[lax.axis_index(SHARDS)]

    for numbers, local in small:
        for number in numbers:
            moves.wait_for(number)
        moves.wait_local(local)
    moves.wait_local(ada_load)
    moves.task(modulate)
    modul_moves = []
    for shift in range(1, shards):

        def other(shift=shift):
            return lax.rem(lax.axis_index(SHARDS) + shift, shards)

        number = moves.move(
            (SHARDS, shift),
            lambda other=other: {SHARDS: other()},
            parts_leaving,
            lambda other=other: (other(),),
            parts,
            lambda: (lax.axis_index(SHARDS),),
            later=True,
        )
        modul_moves.append(number)
        moves.start(number)
    weights = moves.gather_twice((io_low.reshape(-1, io_low.shape[-1]), w_out, w_qkv), members)

    def collect(ref):
        bias_row = ref(bias)[:, pl.ds(6 * width, width)].astype(LOW).astype(f32)
        for step in range(ROLL):
            for piece in range(6 * 2):
                start = piece * width // 2
                value = ref(parts)[start // ada_cols, pl.ds(step, 1), pl.ds(start % ada_cols, width // 2)]
                ref(extras)[step, pl.ds(piece // 2, 1), pl.ds(piece % 2 * width // 2, width // 2)] = value
            ref(extras)[step, pl.ds(6, 1), :] = bias_row
            ref(extras)[step, pl.ds(7, 1), :] = ref(active)[pl.ds(step, 1), :]

    def start_step(ref):
        ref(state_low)[...] = ref(state)[...].astype(LOW)
        mods = lambda row: ref(extras)[0, pl.ds(row, 1), :]
        embed(ref, state_low, ref(weights[0][0])[pl.ds(0, padded), :], mods, pos_all, embedded, normed_low)

    for number in modul_moves:
        moves.wait_for(number)
    moves.task(collect)
    for number in (*pos_moves, *weights[0][1]):
        moves.wait_for(number)
    moves.wait_local(pos_local)
    moves.wait_local(weights[0][2])
    moves.task(start_step)
    for target, numbers, local in weights:
        for number in numbers:
            moves.wait_for(number)
        moves.wait_local(local)
        save = moves.save(target, moves.shape(target), LOW)
        moves.start_local(save)
    moves.start_local(moves.save(pos_all, (rows, width), LOW))
    project(moves, normed_low, weights[2][0], qkv_rows, 3 * width)
    return moves.run()


class Tokens:
    def __init__(self, moves, rows, width):
        self.moves = moves
        self.shards = lax.axis_size(SHARDS)
        self.rows = rows
        self.tokens = moves.scratch((self.shards, rows, width), LOW)
        self.own_part = moves.scratch((rows, width), jnp.float32)
        self.leaving = moves.scratch((self.shards, rows, width), LOW)
        self.arriving = moves.scratch((self.shards, rows, width), LOW)

    def me(self):
        return lax.axis_index(SHARDS)

    def back(self, pair, sibling):
        index = lax.rem(self.me() + self.shards - 2 * pair, self.shards)
        return index + 1 - 2 * lax.rem(index, 2) if sibling else index

    def part(self, pair, sibling, work):
        moves = self.moves
        slot = functools.partial(self.back, pair, sibling)

        def action(ref):
            value = work(ref, slot())
            if pair or sibling:
                ref(self.leaving)[slot()] = value.astype(LOW)
            else:
                ref(self.own_part)[...] = value

        moves.task(action)
        if pair or sibling:
            number = moves.move(
                (SHARDS, pair, sibling),
                lambda: {SHARDS: slot()},
                self.leaving,
                lambda: (slot(),),
                self.arriving,
                lambda: (self.me(),),
                later=True,
            )
            moves.start(number)
            self.parts.append(number)

    def run(self, work):
        moves, halves = self.moves, 2
        self.parts = []
        size = self.rows // halves
        pairs = self.shards // 2

        def half(pair, sibling, number):
            return (self.back(pair, sibling), pl.ds(number * size, size))

        firsts = {}
        for pair in range(1, pairs):
            for number in range(halves):
                place = functools.partial(half, 0, False, number)
                firsts[pair, number] = moves.move(
                    (SHARDS, pairs - pair, False),
                    functools.partial(lambda pair: {SHARDS: self.back(pairs - pair, False)}, pair),
                    self.tokens,
                    place,
                    self.tokens,
                    place,
                    later=True,
                )
                moves.start(firsts[pair, number])
        own = functools.partial(self.back, 0, False)
        near = moves.move(
            (SHARDS, 0, True), sibling_peer, self.tokens, lambda: (own(),), self.tokens, lambda: (own(),), later=True
        )
        moves.start(near)
        self.part(0, False, work)
        moves.wait_for(near)
        self.part(0, True, work)
        for pair in range(1, pairs):
            handed = []
            for number in range(halves):
                place = functools.partial(half, pair, False, number)
                handed.append(
                    moves.move(
                        (SHARDS, 0, True),
                        sibling_peer,
                        self.tokens,
                        place,
                        self.tokens,
                        place,
                        (firsts[pair, number],),
                    )
                )
            self.part(pair, False, work)
            for number in handed:
                moves.wait_for(number)
            self.part(pair, True, work)

    def wait(self):
        for number in self.parts:
            self.moves.wait_for(number)

    def total(self, ref):
        value = ref(self.own_part)[...]
        for shift in range(1, self.shards):
            value = value + ref(self.arriving)[lax.rem(self.me() + shift, self.shards)].astype(jnp.float32)
        return value


GELU_SCALE = math.sqrt(2.0 / math.pi)
GELU_CUBE = 0.044715


def gelu_inner(values):
    return jnp.tanh(GELU_SCALE * (values + GELU_CUBE * values * values * values))


def gelu_slope(values):
    inner = gelu_inner(values)
    rise = GELU_SCALE * (1.0 + 3.0 * GELU_CUBE * values * values)
    return 0.5 * (1.0 + inner) + 0.5 * values * (1.0 - inner * inner) * rise


def feed_forward(ids, step, mods, mods_next, mixed, embedded, state, pos, w_out, w_up, w_down, io_all, w_qkv, moment_part):
    f32 = jnp.float32
    last = mods_next is None
    rows, width = mixed.shape
    padded = state.shape[1]
    hidden_count = w_up.shape[1]
    shards = lax.axis_size(SHARDS)
    moves = Moves(f"feed{step}", ids, 56 * 2**20)
    vmem = functools.partial(moves.operand, space=pltpu.VMEM)
    out_weights, out_load = moves.load(w_out)
    mods, mixed, embedded, state = vmem(mods), vmem(mixed), vmem(embedded), vmem(state)
    up_weights, up_load = moves.load(w_up)
    down_weights, down_load = moves.load(w_down)
    io_weights, io_load = moves.load(io_all)
    attended, after_attn, downward, after_mlp = [moves.output((rows, width), f32, pltpu.VMEM) for _ in range(4)]
    normed_c = moves.output((rows, width), LOW, pltpu.VMEM)
    state_next = moves.output((rows, padded), f32, pltpu.VMEM)
    upward = moves.scratch((shards, rows, hidden_count), f32)
    hidden = moves.scratch((shards, rows, hidden_count), LOW)
    feed = Tokens(moves, rows, width)
    saves = [
        moves.save(feed.tokens, (shards, rows, width), LOW),
        moves.save(upward, (shards, rows, hidden_count), f32),
        moves.save(hidden, (shards, rows, hidden_count), LOW),
    ]
    if not last:
        mods_next, pos = vmem(mods_next), vmem(pos)
        qkv_weights, qkv_load = moves.load(w_qkv)
        embedded_next = moves.output((rows, width), f32, pltpu.VMEM)
        normed_next = moves.output((rows, width), LOW, pltpu.VMEM)
        state_low = moves.output((rows, padded), LOW, pltpu.VMEM)
        qkv_next = moves.output((rows, w_qkv.shape[1]), LOW, pltpu.VMEM)
    moves.exchange(PATCHES, moment_part)

    def begin(ref):
        value = contract(ref(mixed)[...], ref(out_weights)[...], 1, 0)
        ref(attended)[...] = value
        value = ref(embedded)[...] + mod_row(ref, mods, 2) * value
        ref(after_attn)[...] = value
        normed, _ = layer_norm(value)
        normed = normed * (1.0 + mod_row(ref, mods, 4)) + mod_row(ref, mods, 3)
        ref(feed.tokens)[feed.me()] = normed.astype(LOW)

    def work(ref, slot):
        value = contract(ref(feed.tokens)[slot], ref(up_weights)[...], 1, 0)
        ref(upward)[slot] = value
        value = (0.5 * value * (1.0 + gelu_inner(value))).astype(LOW)
        ref(hidden)[slot] = value
        return contract(value, ref(down_weights)[...], 1, 1)

    def finish(ref):
        value = feed.total(ref)
        ref(downward)[...] = value
        value = ref(after_attn)[...] + mod_row(ref, mods, 5) * value
        ref(after_mlp)[...] = value
        normed, _ = layer_norm(value)
        normed = normed.astype(LOW)
        ref(normed_c)[...] = normed
        delta = contract(normed, ref(io_weights)[1], 1, 1)
        value = ref(state)[...] + mod_row(ref, mods, 7)[:, :padded] * delta
        ref(state_next)[...] = value
        if not last:
            ref(state_low)[...] = value.astype(LOW)
            mods_there = functools.partial(mod_row, ref, mods_next)
            embed(ref, state_low, ref(io_weights)[0], mods_there, pos, embedded_next, normed_next)

    moves.wait_local(out_load)
    moves.task(begin)
    moves.wait_local(up_load)
    moves.wait_local(down_load)
    feed.run(work)
    for number in saves:
        moves.start_local(number)
    moves.wait_local(io_load)
    feed.wait()
    moves.task(finish)
    if not last:
        moves.wait_local(qkv_load)
        project(moves, normed_next, qkv_weights, qkv_next, w_qkv.shape[1])
    return moves.run()


def feed_back(ids, step, mods, mods_later, later, grad_state, kept, w_out, w_up, w_down, io_all, w_qkv):
    f32 = jnp.float32
    attended, after_attn, downward, after_mlp, upward = kept
    rows, width = attended.shape
    padded = grad_state.shape[1]
    hidden_count = w_up.shape[1]
    shards = lax.axis_size(SHARDS)
    moves = Moves(f"feed_back{step}", ids, 56 * 2**20)
    vmem = functools.partial(moves.operand, space=pltpu.VMEM)
    io_weights, io_load = moves.load(io_all)
    if later is not None:
        qkv_weights, qkv_load = moves.load(w_qkv)
        later = [vmem(item) for item in later]
        mods_later = vmem(mods_later)
        embed_grad = moves.output((rows, width), LOW, pltpu.VMEM)
    down_weights, down_load = moves.load(w_down)
    up_weights, up_load = moves.load(w_up)
    slopes, slopes_load = moves.load(upward)
    out_weights, out_load = moves.load(w_out)
    mods, grad_state = vmem(mods), vmem(grad_state)
    attended, after_attn, downward, after_mlp = [vmem(item) for item in (attended, after_attn, downward, after_mlp)]
    vectors = moves.output((8, width), f32, pltpu.VMEM)
    state_out = moves.output((rows, padded), f32, pltpu.VMEM)
    delta_grad = moves.output((rows, padded), LOW, pltpu.VMEM)
    grad_attn = moves.output((rows, width), f32, pltpu.VMEM)
    attn_grad, mixed_grad = [moves.output((rows, width), LOW, pltpu.VMEM) for _ in range(2)]
    grad_mlp = moves.scratch((rows, width), f32)
    up_grad = moves.scratch((shards, rows, hidden_count), LOW)
    feed = Tokens(moves, rows, width)
    saves = [
        moves.save(feed.tokens, (shards, rows, width), LOW),
        moves.save(up_grad, (shards, rows, hidden_count), LOW),
    ]

    def put(ref, row, value):
        ref(vectors)[pl.ds(row, 1), :] = jnp.sum(value, 0, keepdims=True)

    def before(ref):
        qkv_grad, embedded, grad_later = later
        grad = contract(ref(qkv_grad)[...], ref(qkv_weights)[...], 1, 1)
        normed, inverse = layer_norm(ref(embedded)[...])
        put(ref, 5, grad * normed)
        put(ref, 4, grad)
        grad = grad * (1.0 + mod_row(ref, mods_later, 1))
        grad = ref(grad_later)[...] + norm_back(grad, normed, inverse)
        put(ref, 6, grad)
        grad = grad.astype(LOW)
        ref(embed_grad)[...] = grad
        ref(state_out)[...] = ref(grad_state)[...] + contract(grad, ref(io_weights)[0], 1, 1)

    def begin(ref):
        if later is None:
            ref(state_out)[...] = ref(grad_state)[...]
            ref(vectors)[...] = jnp.zeros((8, width), f32)
        grad = (mod_row(ref, mods, 7)[:, :padded] * ref(state_out)[...]).astype(LOW)
        ref(delta_grad)[...] = grad
        normed, inverse = layer_norm(ref(after_mlp)[...])
        grad = norm_back(contract(grad, ref(io_weights)[1], 1, 0), normed, inverse)
        ref(grad_mlp)[...] = grad
        put(ref, 3, grad * ref(downward)[...])
        ref(feed.tokens)[feed.me()] = (mod_row(ref, mods, 5) * grad).astype(LOW)

    def work(ref, slot):
        value = contract(ref(feed.tokens)[slot], ref(down_weights)[...], 1, 0)
        value = (value * gelu_slope(ref(slopes)[slot])).astype(LOW)
        ref(up_grad)[slot] = value
        return contract(value, ref(up_weights)[...], 1, 1)

    def finish(ref):
        grad = feed.total(ref)
        normed, inverse = layer_norm(ref(after_attn)[...])
        put(ref, 2, grad * normed)
        put(ref, 1, grad)
        grad = ref(grad_mlp)[...] + norm_back(grad * (1.0 + mod_row(ref, mods, 4)), normed, inverse)
        ref(grad_attn)[...] = grad
        put(ref, 0, grad * ref(attended)[...])
        grad = (mod_row(ref, mods, 2) * grad).astype(LOW)
        ref(attn_grad)[...] = grad
        ref(mixed_grad)[...] = contract(grad, ref(out_weights)[...], 1, 1).astype(LOW)

    moves.wait_local(io_load)
    if later is not None:
        moves.wait_local(qkv_load)
        moves.task(before)
    moves.task(begin)
    for number in (down_load, up_load, slopes_load):
        moves.wait_local(number)
    feed.run(work)
    for number in saves:
        moves.start_local(number)
    moves.wait_local(out_load)
    feed.wait()
    moves.task(finish)
    results = moves.run()
    return results if later is not None else [None, *results]


def reduce_step(
    ids, members, group_cols, qkv_grad, embedded, grad_attn, mods, w_qkv, rows_late, rows_early, gathered, mlp, ada
):
    f32 = jnp.float32
    shards, seq_count = lax.axis_size(SHARDS), lax.axis_size(PATCHES)
    rows, width = embedded.shape
    block_rows, most_cols = width, max(group_cols)
    part, ada_cols = width // shards, ada.shape[1]
    up_mine, down_mine, down_leaving = mlp
    moves = Moves("reduce", ids, 60 * 2**20)
    vmem = functools.partial(moves.operand, space=pltpu.VMEM)
    qkv_grad, embedded, grad_attn, mods = vmem(qkv_grad), vmem(embedded), vmem(grad_attn), vmem(mods)
    rows_late, rows_early = vmem(rows_late), vmem(rows_early)

    def shard():
        return lax.axis_index(SHARDS)

    def patch():
        return lax.axis_index(PATCHES)

    def group():
        return patch() // members

    def member():
        return lax.rem(patch(), members)

    def columns(index, size):
        return pl.ds(pl.multiple_of(index * size, LANES), size)

    def await_all(numbers):
        for number in numbers:
            moves.wait_for(number)

    def to_others(axis, source, source_at, target, leave_own=False):
        count = lax.axis_size(axis)
        numbers = []
        for shift in range(1, count):

            def other(shift=shift):
                return lax.rem(lax.axis_index(axis) + shift, count)

            number = moves.move(
                (axis, shift),
                lambda other=other: {axis: other()},
                source,
                lambda other=other: source_at(other()),
                target,
                lambda: (lax.axis_index(axis),),
                later=True,
            )
            moves.start(number)
            numbers.append(number)

        def own(ref):
            ref(target)[lax.axis_index(axis)] = ref(source)[source_at(lax.axis_index(axis))]

        moves.task(own)
        return numbers

    def to_members(source, target, cols):
        numbers = []
        for shift in range(1, members):
            number = moves.move(
                (PATCHES, members, shift),
                functools.partial(member_peer, members, shift),
                source,
                lambda shift=shift: (slice(None), columns(lax.rem(member() + shift, members), cols)),
                target,
                lambda shift=shift: (shift - 1,),
                later=True,
            )
            moves.start(number)
            numbers.append(number)
        return numbers

    def to_group(source, target, which):
        numbers = []
        for shift in range(1, MATRICES):
            number = moves.move(
                (PATCHES, seq_count, shift),
                functools.partial(group_peer, members, shift),
                source,
                None,
                target,
                lambda shift=shift: (shift - 1,),
                sends=lambda shift=shift: group() == (which - shift) % MATRICES,
                takes=lambda: group() == which,
                later=True,
            )
            moves.start(number)
            numbers.append(number)
        return numbers

    def over_rows(action):
        @pl.loop(0, block_rows // GRAM_COLS)
        def _(tile):
            action(pl.ds(pl.multiple_of(tile * GRAM_COLS, GRAM_COLS), GRAM_COLS))

    def weight_grad(lefts, rights, full, low=None):
        depth, cols = moves.shape(lefts[0])[2], moves.shape(rights[0])[2]
        tile_rows = GRAM_COLS if depth % GRAM_COLS == 0 else LANES

        def action(ref):
            @pl.loop(0, depth // tile_rows)
            def _(tile):
                at = pl.ds(pl.multiple_of(tile * tile_rows, tile_rows), tile_rows)
                value = jnp.zeros((tile_rows, cols), f32)
                for left, right in zip(lefts, rights):
                    left_rows = ref(left)[:, :, at].reshape(-1, tile_rows)
                    value = value + contract(left_rows, ref(right)[...].reshape(-1, cols), 0, 0)
                if full is not None:
                    ref(full)[at, :] = value
                if low is not None:
                    ref(low)[at, :] = value.astype(LOW)

        moves.task(action)

    qkv_all = moves.scratch((shards, rows, 3 * part), LOW)
    qkv_moves = moves.along(
        SHARDS,
        qkv_grad,
        qkv_all,
        [(lambda receiver: (slice(None), columns(receiver, 3 * part)), lambda sender: (sender,))],
    )
    qkv_local = len(moves.locals) - 1
    down_arriving = moves.scratch((members - 1, block_rows, group_cols[2]), LOW)
    down_moves = [
        moves.move(
            (PATCHES, members, shift),
            functools.partial(member_peer, members, shift),
            moves.operand(item),
            None,
            down_arriving,
            lambda shift=shift: (shift - 1,),
        )
        for shift, item in enumerate(down_leaving, 1)
    ]
    up_full, up_load = moves.load(up_mine)
    qkv_weights, qkv_load = moves.load(w_qkv)
    loaded = {
        name: [moves.load(steps[step]) for step in range(ROLL) if step in steps] for name, steps in gathered.items()
    }
    down_full, down_load = moves.load(down_mine)
    ada_weights, ada_load = moves.load(ada)

    def ready(*names):
        for name in names:
            for _, number in loaded[name]:
                moves.wait_local(number)
        return [[item for item, _ in loaded[name]] for name in names]

    up_low, down_low = [moves.scratch((block_rows, cols), LOW) for cols in group_cols[1:3]]
    group_target = moves.scratch((MATRICES - 1, block_rows, most_cols), LOW)

    def round_up_grad(ref):
        def action(at):
            ref(up_low)[at, :] = ref(up_full)[at, :].astype(LOW)

        over_rows(action)

    moves.wait_local(up_load)
    moves.task(round_up_grad)
    up_moves = to_group(up_low, group_target, 1)

    embed_low = moves.scratch((rows, width), LOW)
    table = moves.scratch((8, 6 * width), f32)

    def back(ref):
        grad = contract(ref(qkv_grad)[...], ref(qkv_weights)[...], 1, 1)
        normed, inverse = layer_norm(ref(embedded)[...])
        ref(table)[...] = jnp.zeros((8, 6 * width), f32)
        ref(table)[pl.ds(0, 1), pl.ds(0, width)] = jnp.sum(grad, 0, keepdims=True)
        ref(table)[pl.ds(0, 1), pl.ds(width, width)] = jnp.sum(grad * normed, 0, keepdims=True)
        grad = ref(grad_attn)[...] + norm_back(grad * (1.0 + mod_row(ref, mods, 1)), normed, inverse)
        ref(embed_low)[...] = grad.astype(LOW)
        bias_row = jnp.sum(grad, 0, keepdims=True) + mod_row(ref, rows_early, 6)
        for entry in range(4):
            cols = pl.ds((2 + entry) * width, width)
            ref(table)[pl.ds(0, 1), cols] = mod_row(ref, rows_early, entry)
            ref(table)[pl.ds(1, 1), cols] = mod_row(ref, rows_late, entry)
        for entry in range(2):
            ref(table)[pl.ds(1, 1), pl.ds(entry * width, width)] = mod_row(ref, rows_early, 4 + entry)
        for entry in range(shards):
            ref(table)[pl.ds(ROLL, 1), pl.ds(entry * ada_cols, part)] = bias_row[:, entry * part : (entry + 1) * part]

    moves.wait_local(qkv_load)
    moves.task(back)
    embed_all = moves.scratch((shards, rows, part), LOW)
    table_all = moves.scratch((shards, 8, ada_cols), f32)
    embed_moves = to_others(SHARDS, embed_low, lambda there: (slice(None), columns(there, part)), embed_all)
    table_moves = to_others(SHARDS, table, lambda there: (slice(None), columns(there, ada_cols)), table_all)

    out_cols, qkv_cols = group_cols[3], group_cols[0]
    out_full, out_low = moves.scratch((width, part), f32), moves.scratch((width, part), LOW)
    qkv_full, qkv_low = moves.scratch((width, 3 * part), f32), moves.scratch((width, 3 * part), LOW)
    out_arriving = moves.scratch((members - 1, block_rows, out_cols), LOW)
    qkv_arriving = moves.scratch((members - 1, block_rows, qkv_cols), LOW)
    padded = moves.shape(loaded["state"][0][0])[2]
    io_low = moves.scratch((2 * padded, part), LOW)
    io_grads = [moves.scratch((padded, part), f32) for _ in range(2)]
    weight_grad(*ready("mixed", "attn"), out_full, out_low)
    out_moves = to_members(out_low, out_arriving, out_cols)
    weight_grad(*ready("delta", "c"), io_grads[1])
    await_all(qkv_moves)
    moves.wait_local(qkv_local)
    (a_all, qkv_later) = ready("a", "qkv")
    weight_grad(a_all, [qkv_all, *qkv_later], qkv_full, qkv_low)
    qkv_member_moves = to_members(qkv_low, qkv_arriving, qkv_cols)
    await_all(embed_moves)
    (state_all, embed_later) = ready("state", "embed")
    weight_grad(state_all, [embed_all, *embed_later], io_grads[0])
    grad_pos = moves.output((rows, part), f32, pltpu.VMEM)
    io_rows = 2 * padded // seq_count

    def pos_and_io(ref):
        value = jnp.zeros((rows, part), f32)
        for item in (embed_all, *embed_later):
            for sample in range(shards):
                value = value + ref(item)[sample].astype(f32)
        ref(grad_pos)[...] = value
        for number, item in enumerate(io_grads):
            ref(io_low)[pl.ds(number * padded, padded), :] = ref(item)[...].astype(LOW)

    moves.task(pos_and_io)
    io_all = moves.scratch((seq_count, io_rows, part), LOW)
    io_moves = to_others(
        PATCHES, io_low, lambda there: (pl.ds(pl.multiple_of(there * io_rows, io_rows), io_rows),), io_all
    )

    flat, flat_all = moves.scratch((16, ada_cols), LOW), moves.scratch((seq_count, 16, ada_cols), LOW)

    def share(ref):
        pieces = [ref(table_all)[sample, pl.ds(0, ROLL), :] for sample in range(shards)]
        bias_row = sum(ref(table_all)[sample, pl.ds(ROLL, 1), :] for sample in range(shards))
        rest = jnp.zeros((16 - shards * ROLL - 1, ada_cols), f32)
        ref(flat)[...] = jnp.concatenate([*pieces, bias_row, rest], 0).astype(LOW)

    await_all(table_moves)
    moves.task(share)
    flat_moves = to_others(PATCHES, flat, lambda there: (slice(None), slice(None)), flat_all)

    def add_member(full, arriving, target, low, cols):
        def action(ref):
            def add(at):
                value = ref(full)[at, columns(member(), cols)] if target is not full else ref(full)[at, :]
                for shift in range(members - 1):
                    value = value + ref(arriving)[shift, at, :].astype(f32)
                ref(target)[at, :] = value
                if low is not None:
                    ref(low)[at, :] = value.astype(LOW)

            over_rows(add)

        moves.task(action)

    moves.wait_local(down_load)
    await_all(down_moves)
    add_member(down_full, down_arriving, down_full, down_low, group_cols[2])
    down_group_moves = to_group(down_low, group_target, 2)
    out_mine, out_mine_low = moves.scratch((width, out_cols), f32), moves.scratch((width, out_cols), LOW)
    out_target = moves.scratch((MATRICES - 1, block_rows, out_cols), LOW)
    await_all(out_moves)
    add_member(out_full, out_arriving, out_mine, out_mine_low, out_cols)
    out_group_moves = to_group(out_mine_low, out_target, 3)

    modul_all = moves.output((shards * ROLL, ada_cols), f32, pltpu.VMEM)
    tail_all = moves.output((shards, 16, ada_cols), f32, pltpu.VMEM)
    tail = moves.scratch((16, ada_cols), f32)

    def close(ref):
        value = jnp.zeros((16, ada_cols), f32)
        for item in range(seq_count):
            value = value + ref(flat_all)[item].astype(f32)
        modul = value[: shards * ROLL]
        ref(modul_all)[...] = modul
        high = modul.astype(LOW)
        rest = (modul - high.astype(f32)).astype(LOW)
        weights = ref(ada_weights)[...]
        ref(tail)[...] = jnp.zeros((16, ada_cols), f32)
        ref(tail)[pl.ds(0, shards * ROLL), pl.ds(0, width)] = contract(high, weights, 1, 1) + contract(
            rest, weights, 1, 1
        )
        ref(tail)[pl.ds(8, 1), :] = jnp.sum(modul, 0, keepdims=True)
        ref(tail)[pl.ds(9, 1), :] = value[shards * ROLL : shards * ROLL + 1]

    await_all(flat_moves)
    moves.wait_local(ada_load)
    moves.task(close)
    to_others(SHARDS, tail, lambda there: (slice(None), slice(None)), tail_all)

    def has_source():
        return group() < MATRICES - 1

    def is_source():
        return group() > 0

    chain = moves.scratch((width, qkv_cols), f32)
    chain_in, chain_out = [moves.scratch((width, qkv_cols), LOW) for _ in range(2)]
    await_all(qkv_member_moves)
    add_member(qkv_full, qkv_arriving, chain, None, qkv_cols)
    chunk = block_rows // CHAIN_CHUNKS
    for number_of in range(CHAIN_CHUNKS):
        place = (pl.ds(number_of * chunk, chunk),)
        number = moves.move(
            (PATCHES, seq_count, MATRICES - 1),
            functools.partial(group_peer, members, MATRICES - 1),
            chain_out,
            lambda place=place: place,
            chain_in,
            lambda place=place: place,
            sends=is_source,
            takes=has_source,
            later=True,
        )

        def add(ref, place=place):
            def with_arriving():
                ref(chain)[place] += ref(chain_in)[place].astype(f32)

            pl.when(has_source())(with_arriving)
            ref(chain_out)[place] = ref(chain)[place].astype(LOW)

        moves.wait_for(number)
        moves.task(add)
        moves.start(number)

    io_slice = moves.output((io_rows, part), f32, pltpu.VMEM)

    def add_io(ref):
        value = jnp.zeros((io_rows, part), f32)
        for item in range(seq_count):
            value = value + ref(io_all)[item].astype(f32)
        ref(io_slice)[...] = value

    await_all(io_moves)
    moves.task(add_io)

    grad_group = moves.output((block_rows, most_cols), f32, pltpu.VMEM)

    def put(full, target, cols):
        def action(ref):
            def add(at):
                value = ref(full)[at, :]
                if target is not None:
                    for shift in range(MATRICES - 1):
                        value = value + ref(target)[shift, at, pl.ds(0, cols)].astype(f32)
                ref(grad_group)[at, pl.ds(0, cols)] = value
                if cols < most_cols:
                    ref(grad_group)[at, pl.ds(cols, most_cols - cols)] = jnp.zeros((GRAM_COLS, most_cols - cols), f32)

            over_rows(add)

        return action

    def settle(ref):
        entries = ((chain, None), (up_full, group_target), (down_full, group_target), (out_mine, out_target))
        for which, (full, target) in enumerate(entries):
            pl.when(group() == which)(functools.partial(put(full, target, group_cols[which]), ref))

    await_all((*up_moves, *down_group_moves, *out_group_moves))
    moves.task(settle)
    return moves.run()


def newton_schulz(source, gram, poly, once, gram_low, poly_low, once_low, block, block_next):
    size = gram.shape[0]
    eye = jnp.equal(
        lax.broadcasted_iota(jnp.int32, (GRAM_COLS, GRAM_COLS), 0),
        lax.broadcasted_iota(jnp.int32, (GRAM_COLS, GRAM_COLS), 1),
    ).astype(jnp.float32)

    def over_tiles(action, width=size):
        def step(tile, total):
            return total + action(pl.ds(pl.multiple_of(tile * GRAM_COLS, GRAM_COLS), GRAM_COLS))

        return lax.fori_loop(0, width // GRAM_COLS, step, jnp.float32(0.0))

    def store(full, low, cols, value, mean, excess):
        full[:, cols] = value
        low[:, cols] = value.astype(LOW)
        corner = full[cols, cols] - excess * eye
        full[cols, cols] = corner
        low[cols, cols] = (corner - mean * eye).astype(LOW)

    def advance(gram_mean, gram_squares, last):
        poly_mean = NS_B * gram_mean + NS_C * gram_squares / size

        def poly_cols(cols):
            own = gram[:, cols]
            value = contract(gram_low[...], gram_low[:, cols], 1, 0)
            value = NS_C * value + (NS_B + 2.0 * NS_C * gram_mean) * own
            store(poly, poly_low, cols, value, poly_mean, NS_C * gram_mean * gram_mean)
            return jnp.sum(value * own)

        once_mean = over_tiles(poly_cols) / size - NS_C * gram_mean * gram_mean * gram_mean

        def block_cols(cols):
            value = contract(poly_low[...], block[:, cols], 1, 0)
            block_next[:, cols] = (value + (NS_A + poly_mean) * block[:, cols].astype(jnp.float32)).astype(LOW)
            return jnp.float32(0.0)

        over_tiles(block_cols, block.shape[1])
        block[...] = block_next[...]
        if last:
            return None

        def once_cols(cols):
            own = poly[:, cols]
            value = contract(poly_low[...], gram_low[:, cols], 1, 0)
            value = value + poly_mean * gram[:, cols] + gram_mean * own
            store(once, once_low, cols, value, once_mean, poly_mean * gram_mean)
            return jnp.sum(value * own)

        poly_once = over_tiles(once_cols) / size - poly_mean * gram_mean * poly_mean
        mean_next = NS_A * NS_A * gram_mean + 2.0 * NS_A * once_mean + poly_once
        excess = poly_mean * once_mean

        def gram_cols(cols):
            value = contract(poly_low[...], once_low[:, cols], 1, 0)
            value = value + (2.0 * NS_A + poly_mean) * once[:, cols] + once_mean * poly[:, cols]
            value = value + NS_A * NS_A * gram[:, cols]
            store(gram, gram_low, cols, value, mean_next, excess)
            return jnp.sum(value * value)

        return mean_next, over_tiles(gram_cols) - excess * (2.0 * mean_next + excess) * size

    block[...] = source[...]
    mean = over_tiles(lambda cols: jnp.sum(gram[cols, cols] * eye)) / size

    def start(cols):
        value = gram[:, cols]
        gram_low[:, cols] = value.astype(LOW)
        gram_low[cols, cols] = (gram[cols, cols] - mean * eye).astype(LOW)
        return jnp.sum(value * value)

    state = lax.fori_loop(0, NS_ITERS - 1, lambda turn, state: advance(*state, False), (mean, over_tiles(start)))
    advance(*state, True)


def fast_body(
    states,
    targets,
    lengths,
    intervals,
    qkv_copy,
    qkv_master,
    qkv_moment,
    out_copy,
    out_master,
    out_moment,
    up_copy,
    up_master,
    up_moment,
    down_copy,
    down_master,
    down_moment,
    ada_copy,
    ada_master,
    ada_first,
    ada_second,
    io_proj,
    io_first,
    io_second,
    cond_table,
    cond_first,
    cond_second,
    pos_table,
    pos_first,
    pos_second,
    biases,
    bias_first,
    bias_second,
):
    ids = {}
    f32 = jnp.float32
    seq_count, shards = lax.axis_size(PATCHES), lax.axis_size(SHARDS)
    seq_index, shard = lax.axis_index(PATCHES), lax.axis_index(SHARDS)
    members = seq_count // MATRICES
    group, member = seq_index // members, lax.rem(seq_index, members)
    samples, local, values_count = states.shape
    table_rows, table_cols = cond_table.shape
    width = table_cols * shards
    ada_cols = ada_copy.shape[1]
    padded = round_up(values_count, LANES)

    value_pad = ((0, 0), (0, padded - values_count))
    state = jnp.pad(states[0].astype(f32), value_pad)
    length = lengths[0]
    (
        extras,
        cond_vec,
        silu_low,
        embedded,
        normed_a,
        state_low,
        qkv_rows,
        io_all,
        w_out,
        w_qkv,
        pos,
    ) = begin_step(
        ids,
        members,
        state,
        jnp.broadcast_to(intervals[:, None, None], (shards, ROLL, LANES)).reshape(-1, LANES),
        jnp.broadcast_to((jnp.arange(ROLL, dtype=jnp.int32)[:, None] < length).astype(f32), (ROLL, width)),
        cond_table,
        biases[None],
        pos_table.astype(LOW),
        ada_copy,
        jnp.pad(io_proj.astype(LOW), ((0, 0), (0, padded - values_count), (0, 0))),
        out_copy,
        qkv_copy,
    )
    io_all = io_all.reshape(2, padded, width)
    rows_iota = jnp.arange(table_rows, dtype=jnp.int32)
    id_rows = (intervals[:, None] == rows_iota[None]).astype(f32)
    step_rows = (rows_iota[None] == NI + jnp.arange(ROLL, dtype=jnp.int32)[:, None]).astype(f32)
    select = (id_rows[:, None] + step_rows[None]).reshape(-1, table_rows)

    masters = (qkv_master, up_master, down_master, out_master)
    momenta = (qkv_moment, up_moment, down_moment, out_moment)
    group_cols = [item.shape[1] // members for item in momenta]
    most_cols = max(group_cols)

    def widen(item):
        return jnp.pad(item, ((0, 0), (0, most_cols - item.shape[1])))

    moment_parts = jnp.stack(
        [
            widen(item[:, part * cols : (part + 1) * cols].astype(LOW))
            for item, cols in zip(momenta, group_cols)
            for part in range(members)
        ]
    )
    half_rows = moment_parts.shape[1] // 2

    counts = jnp.sum((intervals[:, None] == jnp.arange(NI, dtype=jnp.int32)[None]).astype(f32), 0)
    my_id = lax.dynamic_slice_in_dim(intervals, shard, 1)
    id_count = jnp.sum((my_id == jnp.arange(NI, dtype=jnp.int32)).astype(f32) * counts)
    weight = 1.0 / (NI * local * seq_count * values_count * id_count)
    kept = []
    gathered = {}
    moment_halves = []

    for step in range(ROLL):
        moves = Moves(f"attend{step}", ids, 48 * 2**20)
        qkv_out = moves.output((3, local * seq_count, width // seq_count), LOW, pltpu.VMEM)
        mixed_out = moves.output((local, width), LOW, pltpu.VMEM)
        arrivals = moves.rows_to_heads(PATCHES, qkv_rows, 3, qkv_out)
        waiting = moves.gather_pairs(normed_a, hold=True)
        waiting += moves.gather_pairs(state_low, hold=True)
        if step:
            waiting += moves.gather_pairs(kept[-1][2], hold=True)
        add_attention(moves, qkv_out, mixed_out, arrivals, local, members, waiting)
        qkv, mixed, gathered_a, gathered_state, *gathered_mixed = moves.run()
        gathered.setdefault("a", {})[step] = gathered_a
        gathered.setdefault("state", {})[step] = gathered_state
        if step:
            gathered["mixed"] = {step - 1: gathered_mixed[0]}
        *results, moment_half = feed_forward(
            ids,
            step,
            extras[step],
            extras[step + 1] if step + 1 < ROLL else None,
            mixed,
            embedded,
            state,
            pos,
            w_out,
            up_copy,
            down_copy,
            io_all,
            w_qkv,
            moment_parts[:, step * half_rows : (step + 1) * half_rows],
        )
        moment_halves.append(moment_half)
        attended, after_attn, downward, after_mlp, normed_c, state, tokens_b, upward, hidden, *following = results
        kept.append(
            (embedded, qkv, mixed, (attended, after_attn, downward, after_mlp, upward), normed_c, tokens_b, hidden)
        )
        if following:
            embedded, normed_a, state_low, qkv_rows = following

    lat = latitude_weights(local)
    diff = state - jnp.pad(targets[0].astype(f32), value_pad)
    loss_local = weight * jnp.sum(jnp.sum(diff * diff, -1) * lat)
    grad_state = 2.0 * weight * lat[:, None] * diff

    mlp_back = []

    def patch_sum(item, cols):
        mine = lax.dynamic_slice_in_dim(item, member * cols, cols, 1)
        low = item.astype(LOW)
        for shift in range(1, members):
            pairs = [
                (index, index // members * members + (index + shift) % members) for index in range(seq_count)
            ]
            to_member = lax.rem(member + shift, members)
            outgoing = lax.dynamic_slice_in_dim(low, to_member * cols, cols, 1)
            mine = mine + lax.ppermute(outgoing, PATCHES, pairs).astype(f32)
        return mine

    later, mods_later = None, None
    vector_rows = [None] * ROLL

    for step in reversed(range(ROLL)):
        embedded, qkv, mixed, for_feed, normed_c, tokens_b, hidden = kept[step]
        embed_grad, vectors, grad_state, delta_grad, grad_attn, attn_grad, mixed_grad, tokens_down, up_grad = feed_back(
            ids,
            step,
            extras[step],
            mods_later,
            later,
            grad_state,
            for_feed,
            w_out,
            up_copy,
            down_copy,
            io_all,
            w_qkv,
        )
        vector_rows[step] = vectors
        mlp_back.append((tokens_b, up_grad, tokens_down, hidden))
        if step == 0:
            up_total, down_total = [
                sum(rows_product(items[left], items[right]) for items in mlp_back) for left, right in ((0, 1), (2, 3))
            ]
            up_mine = patch_sum(up_total, group_cols[1])
            down_mine = lax.dynamic_slice_in_dim(down_total, member * group_cols[2], group_cols[2], 1)
            down_leaving = [
                lax.dynamic_slice_in_dim(
                    down_total, lax.rem(member + shift, members) * group_cols[2], group_cols[2], 1
                ).astype(LOW)
                for shift in range(1, members)
            ]
        moves = Moves(f"attend_back{step}", ids, 48 * 2**20)
        grads_in = moves.scratch((1, local * seq_count, width // seq_count), LOW)
        result = moves.output((local, 3 * width), LOW, pltpu.VMEM)
        arrivals = moves.rows_to_heads(PATCHES, mixed_grad, 1, grads_in)
        names = ["attn", "c", "delta"]
        moves.exchange_columns(SHARDS, attn_grad)
        moves.exchange_columns(SHARDS, normed_c)
        waiting = moves.gather_pairs(delta_grad, hold=True)
        if step == ROLL - 1:
            waiting += moves.gather_pairs(mixed, hold=True)
            names.append("mixed")
        else:
            moves.exchange_columns(SHARDS, later[0])
            moves.exchange_columns(SHARDS, embed_grad)
            names += ["qkv", "embed"]
        add_attention_back(
            moves, moves.operand(qkv, pltpu.VMEM), grads_in, result, arrivals, local, members, waiting
        )
        qkv_grad, *others = moves.run()
        for name, item in zip(names, others):
            gathered.setdefault(name, {})[step + (name in ("qkv", "embed"))] = item
        later, mods_later = (qkv_grad, embedded, grad_attn), extras[step]

    block_rows = qkv_copy.shape[0]
    grad_pos, modul_all, tail_all, io_slice, grad_group = reduce_step(
        ids,
        members,
        group_cols,
        qkv_grad,
        embedded,
        grad_attn,
        extras[0],
        w_qkv,
        vector_rows[1],
        vector_rows[0],
        gathered,
        (up_mine, down_mine, down_leaving),
        ada_copy,
    )
    io_cols = io_slice.shape[1]
    silu_parts = tail_all[:, : shards * ROLL, :width]
    bias_parts = jnp.concatenate([tail_all[:, 8], tail_all[:, 9, : width // shards]], -1)[:, None]
    grad_silu = jnp.sum(silu_parts, 0)
    grad_cond = jax.vjp(jax.nn.silu, cond_vec)[1](grad_silu)[0]
    grad_table_all = lax.dot_general(select, grad_cond, (((0,), (0,)), ((), ())), precision=HIGHEST_PRECISION)
    grad_table = lax.dynamic_slice_in_dim(grad_table_all, shard * table_cols, table_cols, 1)
    bias_parts = bias_parts[:, 0]
    grad_bias_all = jnp.concatenate([bias_parts[:, :ada_cols].reshape(-1), bias_parts[:, ada_cols:].reshape(-1)])
    grad_bias = lax.dynamic_slice_in_dim(grad_bias_all, shard * biases.shape[0], biases.shape[0])
    silu_rows = lax.dynamic_slice_in_dim(silu_low, seq_index * ada_master.shape[0], ada_master.shape[0], 1)
    grad_ada = lax.dot_general(
        silu_rows.astype(f32), modul_all, (((0,), (0,)), ((), ())), precision=HIGHEST_PRECISION
    )

    moment_group = jnp.concatenate(moment_halves, 1).reshape(-1, most_cols).astype(f32)
    grad_squares = jnp.sum(grad_group * grad_group)
    squares = (
        grad_squares
        + jnp.sum(grad_ada * grad_ada)
        + jnp.sum(io_slice * io_slice)
        + jnp.sum(grad_pos * grad_pos)
        + (seq_index == 0).astype(f32) * (jnp.sum(grad_table * grad_table) + jnp.sum(grad_bias * grad_bias))
    )
    lane = jnp.arange(LANES, dtype=jnp.int32)
    place = 2 + 3 * group
    entries = jnp.where(lane == 0, squares, 0.0) + jnp.where(lane == 1, loss_local, 0.0)
    entries = entries + jnp.where(lane == place, jnp.sum(moment_group * moment_group), 0.0)
    entries = entries + jnp.where(lane == place + 1, jnp.sum(moment_group * grad_group), 0.0)
    entries = entries + jnp.where(lane == place + 2, grad_squares, 0.0)
    sums, io_slices = total_of(ids, jnp.broadcast_to(entries[None], (8, LANES)), io_slice.astype(LOW))
    sums = sums[0]
    grad_norm = jnp.sqrt(sums[0])
    loss_total = sums[1]
    clip = jnp.minimum(1.0, CLIP_LIMIT / (grad_norm + 1e-06))
    terms = sums[2 : 2 + 3 * MATRICES].reshape(MATRICES, 3)
    size_squares = MOMENTUM * MOMENTUM * terms[:, 0] + 2.0 * MOMENTUM * clip * terms[:, 1] + clip * clip * terms[:, 2]
    sizes = jnp.sqrt(jnp.maximum(size_squares, 0.0))
    moment_sizes = sizes[jnp.array([0, 3, 1, 2])] / CLIP_LIMIT
    my_size = lax.dynamic_slice_in_dim(sizes, group, 1)[0]
    block = ((MOMENTUM * moment_group + clip * grad_group) / (my_size + 1e-07)).astype(LOW)

    moves = Moves("muon", ids, 56 * 2**20)
    source = moves.operand(block, pltpu.VMEM)
    full, low = (block_rows, block_rows), (block_rows, most_cols)
    update = moves.output((seq_count, block_rows // seq_count, most_cols), LOW, pltpu.VMEM)
    target = moves.scratch((members * shards,) + low, LOW)
    gram, poly, once = [moves.scratch(full, f32) for _ in range(3)]
    gram_low, poly_low, once_low = [moves.scratch(full, LOW) for _ in range(3)]
    state, state_next = [moves.scratch(low, LOW) for _ in range(2)]
    pairs = shards // 2

    def slot(back_member, back_pair, part=None):
        who_member = lax.rem(lax.rem(lax.axis_index(PATCHES), members) + members - back_member, members)
        who_shard = lax.rem(lax.axis_index(SHARDS) + shards - 2 * back_pair, shards)
        index = who_member * shards + who_shard
        return (index,) if part is None else (index, pl.ds(part * block_rows // 2, block_rows // 2))

    def add_gram(place):
        def action(ref):
            (index,) = place()

            @pl.loop(0, block_rows // GRAM_COLS)
            def _(tile):
                cols = pl.ds(pl.multiple_of(tile * GRAM_COLS, GRAM_COLS), GRAM_COLS)
                ref(gram)[:, cols] += contract(ref(target)[index], ref(target)[index, cols, :], 1, 1)

        return action

    def start_gram(ref):
        @pl.loop(0, block_rows // GRAM_COLS)
        def _(tile):
            cols = pl.ds(pl.multiple_of(tile * GRAM_COLS, GRAM_COLS), GRAM_COLS)
            ref(gram)[:, cols] = contract(ref(source)[...], ref(source)[cols, :], 1, 1)

    def pair_peer(shift):
        return {SHARDS: lax.rem(lax.axis_index(SHARDS) + 2 * shift, shards)}

    slot_own = functools.partial(slot, 0, 0)
    by_member = {
        shift: moves.move(
            (PATCHES, members, shift), functools.partial(member_peer, members, shift), source, None, target, slot_own
        )
        for shift in range(1, members)
    }
    by_pair = {
        shift: moves.move((SHARDS, 2 * shift), functools.partial(pair_peer, shift), source, None, target, slot_own)
        for shift in range(1, pairs)
    }
    from_sibling = [(moves.move((SHARDS,), sibling_peer, source, None, target, slot_own), slot_own)]
    moves.task(start_gram)

    def sibling_place(place):
        def at():
            (index,) = place()
            return (index + 1 - 2 * lax.rem(index, 2),)

        return at

    def hand_on(place, arrivals):
        if len(arrivals) == 1:
            parts = [(place, arrivals[0])]
        else:
            parts = [(functools.partial(place, part), number) for part, number in enumerate(arrivals)]
        numbers = [
            moves.move((SHARDS,), sibling_peer, target, at, target, at, (number,)) for at, number in parts
        ]
        from_sibling.append((numbers, place))
        moves.task(add_gram(place))

    across = []
    for shift_member, first in by_member.items():
        for shift_pair, second in by_pair.items():
            top = functools.partial(slot, shift_member, 0, 0)
            bottom = functools.partial(slot, 0, shift_pair, 1)
            halves = [
                moves.move(
                    (SHARDS, 2 * shift_pair),
                    functools.partial(pair_peer, shift_pair),
                    target,
                    top,
                    target,
                    top,
                    (first,),
                ),
                moves.move(
                    (PATCHES, members, shift_member),
                    functools.partial(member_peer, members, shift_member),
                    target,
                    bottom,
                    target,
                    bottom,
                    (second,),
                ),
            ]
            across.append((functools.partial(slot, shift_member, shift_pair), halves))
    for shift, number in by_member.items():
        hand_on(functools.partial(slot, shift, 0), [number])
    for shift, number in by_pair.items():
        hand_on(functools.partial(slot, 0, shift), [number])
    moves.wait_for(from_sibling[0][0])
    moves.task(add_gram(sibling_place(slot_own)))
    for place, halves in across:
        hand_on(place, halves)
    for numbers, place in from_sibling[1:]:
        for number in numbers:
            moves.wait_for(number)
        moves.task(add_gram(sibling_place(place)))

    for number in moves.exchange(PATCHES, grad_group.astype(LOW).reshape(seq_count, -1, most_cols), later=True):
        moves.start(number)
    moves.task(
        lambda ref: newton_schulz(
            *[ref(item) for item in (source, gram, poly, once, gram_low, poly_low, once_low, state, state_next)]
        )
    )

    def row_part(shift):
        there = lax.rem(lax.axis_index(PATCHES) + shift, seq_count)
        size = block_rows // seq_count
        return (pl.ds(pl.multiple_of(there * size, size), size),)

    for shift in range(1, seq_count):
        moves.start(
            moves.move(
                (PATCHES, shift),
                lambda shift=shift: {PATCHES: lax.rem(lax.axis_index(PATCHES) + shift, seq_count)},
                state,
                functools.partial(row_part, shift),
                update,
                lambda: (lax.axis_index(PATCHES),),
                later=True,
            )
        )

    def keep_rows(ref):
        ref(update)[lax.axis_index(PATCHES)] = ref(state)[row_part(0)]

    moves.task(keep_rows)
    update, grad_rows = moves.run()

    def rows_of(which, parts):
        return jnp.concatenate(
            [parts[which * members + part][:, : group_cols[which]] for part in range(members)], -1
        ).astype(f32)

    moments = [MOMENTUM * old + clip * rows_of(which, grad_rows) for which, old in enumerate(momenta)]
    fresh = [
        master * (1.0 - RATE_MUON * DECAY_MUON)
        - RATE_MUON * 0.2 * math.sqrt(master.shape[1] * shards) * rows_of(which, update)
        for which, master in enumerate(masters)
    ]

    moves = Moves("copies", ids)
    rows = qkv_master.shape[0]

    def row_place(back_group):
        who = lax.axis_index(PATCHES) - back_group * members
        return (pl.ds(pl.multiple_of(who * rows, rows), rows),)

    def has_group(offset):
        place = lax.axis_index(PATCHES) // members + offset
        return jnp.logical_and(place >= 0, place < MATRICES)

    def member_copies(source, source_at, target, target_at, after, there):
        for shift in range(1, members):
            moves.move(
                (PATCHES, members, shift),
                functools.partial(member_peer, members, shift),
                source,
                source_at,
                target,
                target_at,
                after,
                there,
                there,
            )

    places = []
    for item in fresh:
        source = moves.operand(item.astype(LOW))
        target = moves.output((rows * seq_count, item.shape[1]), LOW)
        own = functools.partial(row_place, 0)
        moves.keep(source, None, target, own)
        places.append((source, target, {}))

    def along_line(distance, way, source, target, numbers):
        both = lambda: jnp.logical_and(has_group(way), has_group(-distance * way))
        place = functools.partial(row_place, distance * way)
        numbers[way] = moves.move(
            (PATCHES, seq_count, way),
            functools.partial(group_peer, members, (MATRICES + way) % MATRICES),
            target if distance else source,
            place if distance else None,
            target,
            place,
            (numbers[way],) if distance else (),
            both,
            functools.partial(has_group, -(distance + 1) * way),
        )

    for source, target, numbers in places:
        for way in (1, -1):
            along_line(0, way, source, target, numbers)
    for source, target, numbers in places:
        member_copies(source, None, target, own, (), None)
    for distance in range(1, MATRICES):
        for source, target, numbers in places:
            for way in (1, -1):
                number = numbers[way]
                if distance < MATRICES - 1:
                    along_line(distance, way, source, target, numbers)
                place = functools.partial(row_place, distance * way)
                member_copies(
                    target, place, target, place, (number,), functools.partial(has_group, -distance * way)
                )
    copies = moves.run()

    io_grad = io_slices.reshape(2, padded, io_cols)[:, :values_count].astype(f32)
    ada_res = adam_update(ada_master, ada_first, ada_second, clip * grad_ada, RATE_ADAM)
    io_res = adam_update(io_proj, io_first, io_second, clip * io_grad, RATE_ADAM)
    cond_res = adam_update(cond_table, cond_first, cond_second, clip * grad_table, RATE_TABLE)
    pos_res = adam_update(pos_table, pos_first, pos_second, clip * grad_pos, RATE_TABLE)
    bias_res = adam_update(biases, bias_first, bias_second, clip * grad_bias, RATE_ADAM)
    matrices = []
    for which in (0, 3, 1, 2):
        matrices += [fresh[which], moments[which], copies[which]]
    return (loss_total, grad_norm, moment_sizes, *matrices, *ada_res, *io_res, *cond_res, *pos_res, *bias_res)


def fits_fast(mesh):
    seq, shards = mesh.shape[PATCHES], mesh.shape[SHARDS]
    return HEADS % seq == 0 and (HEADS // seq * HEAD) % LANES == 0 and seq % MATRICES == 0 and shards % 2 == 0


def solution(mesh):
    body = fast_body if fits_fast(mesh) else general_body
    return jax.shard_map(
        body,
        mesh=mesh,
        in_specs=(
            P(SHARDS, PATCHES, None),
            P(SHARDS, PATCHES, None),
            P(SHARDS),
            P(),
            P(None, SHARDS),
            P(PATCHES, SHARDS),
            P(PATCHES, SHARDS),
            P(None, SHARDS),
            P(PATCHES, SHARDS),
            P(PATCHES, SHARDS),
            P(None, SHARDS),
            P(PATCHES, SHARDS),
            P(PATCHES, SHARDS),
            P(None, SHARDS),
            P(PATCHES, SHARDS),
            P(PATCHES, SHARDS),
            P(None, SHARDS),
            P(PATCHES, SHARDS),
            P(PATCHES, SHARDS),
            P(PATCHES, SHARDS),
            P(None, None, SHARDS),
            P(None, None, SHARDS),
            P(None, None, SHARDS),
            P(None, SHARDS),
            P(None, SHARDS),
            P(None, SHARDS),
            P(PATCHES, SHARDS),
            P(PATCHES, SHARDS),
            P(PATCHES, SHARDS),
            P(SHARDS),
            P(SHARDS),
            P(SHARDS),
        ),
        out_specs=(
            P(),
            P(),
            P(),
            P(PATCHES, SHARDS),
            P(PATCHES, SHARDS),
            P(None, SHARDS),
            P(PATCHES, SHARDS),
            P(PATCHES, SHARDS),
            P(None, SHARDS),
            P(PATCHES, SHARDS),
            P(PATCHES, SHARDS),
            P(None, SHARDS),
            P(PATCHES, SHARDS),
            P(PATCHES, SHARDS),
            P(None, SHARDS),
            P(PATCHES, SHARDS),
            P(PATCHES, SHARDS),
            P(PATCHES, SHARDS),
            P(None, None, SHARDS),
            P(None, None, SHARDS),
            P(None, None, SHARDS),
            P(None, SHARDS),
            P(None, SHARDS),
            P(None, SHARDS),
            P(PATCHES, SHARDS),
            P(PATCHES, SHARDS),
            P(PATCHES, SHARDS),
            P(SHARDS),
            P(SHARDS),
            P(SHARDS),
        ),
        check_vma=False,
    )
```

```python
import functools
import math

import jax
import jax.numpy as jnp
from jax import lax
from jax.experimental import pallas as pl
from jax.experimental.pallas import tpu as pltpu
from jax.sharding import PartitionSpec as P

PATCHES = "seq"
SHARDS = "fsdp"
HEADS = 16
HEAD = 64
NI = 3
ROLL = 2
NS_ITERS = 5
STEP_NUM = 10
LON = 32


EPS_NORM = 1e-06
NS_A = 3.4445
NS_B = -4.775
NS_C = 2.0315
MOMENTUM = 0.5
RATE_MUON = 0.15
DECAY_MUON = 0.1
RATE_ADAM = 0.05
RATE_TABLE = 0.5
DECAY_ADAM = 0.1
BETA_FIRST = 0.9
BETA_SECOND = 0.95
CLIP_LIMIT = 0.01
HIGHEST_PRECISION = lax.Precision.HIGHEST


def broadcast(block, axis, owner):
    block = jnp.where(lax.axis_index(axis) == owner, block, jnp.zeros_like(block))
    return lax.psum(block, axis)


def product(left, right):
    return jnp.dot(left, right, preferred_element_type=jnp.float32)


def dot_last(left, right):
    return lax.dot_general(
        left, right, (((left.ndim - 1,), (1,)), ((), ())), preferred_element_type=jnp.float32
    )


def rows_product(left, right):
    flat_left = left.reshape(-1, left.shape[-1])
    flat_right = right.reshape(-1, right.shape[-1])
    return lax.dot_general(
        flat_left, flat_right, (((0,), (0,)), ((), ())), preferred_element_type=jnp.float32
    )


def layer_norm(values):
    centred = values - jnp.mean(values, -1, keepdims=True)
    inverse = lax.rsqrt(jnp.mean(centred * centred, -1, keepdims=True) + EPS_NORM)
    return (centred * inverse, inverse)


def norm_back(grad, normed, inverse):
    return inverse * (
        grad
        - jnp.mean(grad, -1, keepdims=True)
        - normed * jnp.mean(grad * normed, -1, keepdims=True)
    )


def heads_view(values):
    return values.reshape(values.shape[0], values.shape[1], HEADS, HEAD)


def modulation(modul, width):
    return [modul[:, None, column * width : (column + 1) * width] for column in range(6)]


def latitude_weights(local):
    all_patches = local * lax.axis_size(PATCHES)
    band_row = (jnp.arange(all_patches, dtype=jnp.int32) // LON).astype(jnp.float32)
    latitude = (band_row + 0.5) * (math.pi / (all_patches // LON)) - math.pi / 2
    cosine = jnp.cos(latitude)
    weights = cosine / jnp.mean(cosine)
    return lax.dynamic_slice_in_dim(weights, lax.axis_index(PATCHES) * local, local)


def forward_step(weights, state, active, select):
    w_qkv, w_out, w_up, w_down, w_ada, io_all, table, pos, bias = weights
    width = w_out.shape[0]
    cond_vec = jnp.dot(select, table.astype(jnp.float32), precision=HIGHEST_PRECISION)
    silu_low = jax.nn.silu(cond_vec).astype(jnp.bfloat16)
    modul = product(silu_low, w_ada) + bias[: 6 * width].astype(jnp.float32)
    shift1, scale1, gate1, shift2, scale2, gate2 = modulation(modul, width)
    state_low = state.astype(jnp.bfloat16)
    embedded = (
        product(state_low, io_all[0])
        + bias[6 * width :].astype(jnp.float32)
        + pos.astype(jnp.float32)
    )
    normed_one, inverse_one = layer_norm(embedded)
    normed_a = (normed_one * (1.0 + scale1) + shift1).astype(jnp.bfloat16)
    qkv = product(normed_a, w_qkv).astype(jnp.bfloat16)
    queries = qkv[..., :width]
    keys, values = (
        lax.all_gather(qkv[..., width : 2 * width], PATCHES, axis=1, tiled=True),
        lax.all_gather(qkv[..., 2 * width :], PATCHES, axis=1, tiled=True),
    )
    scores = jnp.einsum(
        "sphd,snhd->shpn", heads_view(queries), heads_view(keys), preferred_element_type=jnp.float32
    ) * HEAD ** (-0.5)
    top_score = jnp.max(scores, -1, keepdims=True)
    expo = jnp.exp(scores - top_score)
    total_exp = jnp.sum(expo, -1, keepdims=True)
    log_total = top_score + jnp.log(total_exp)
    probs_low = (expo / total_exp).astype(jnp.bfloat16)
    mixed = jnp.einsum(
        "shpn,snhd->sphd", probs_low, heads_view(values), preferred_element_type=jnp.float32
    )
    mixed_low = mixed.reshape(queries.shape).astype(jnp.bfloat16)
    attended = product(mixed_low, w_out)
    after_attn = embedded + gate1 * attended
    normed_two, inverse_two = layer_norm(after_attn)
    normed_b = (normed_two * (1.0 + scale2) + shift2).astype(jnp.bfloat16)
    upward = product(normed_b, w_up)
    hidden = jax.nn.gelu(upward).astype(jnp.bfloat16)
    downward = dot_last(hidden, w_down)
    after_mlp = after_attn + gate2 * downward
    normed_three, inverse_three = layer_norm(after_mlp)
    normed_c = normed_three.astype(jnp.bfloat16)
    delta = dot_last(normed_c, io_all[1])
    kept = (
        cond_vec,
        silu_low,
        modul,
        state_low,
        normed_one,
        inverse_one,
        normed_a,
        queries,
        keys,
        values,
        log_total,
        mixed_low,
        attended,
        normed_two,
        inverse_two,
        normed_b,
        upward,
        hidden,
        downward,
        normed_three,
        inverse_three,
        normed_c,
    )
    return (state + active * delta, kept)


def backward_step(weights, kept, grad_state, active, select):
    w_qkv, w_out, w_up, w_down, w_ada, io_all, table, pos, bias = weights
    (
        cond_vec,
        silu_low,
        modul,
        state_low,
        normed_one,
        inverse_one,
        normed_a,
        queries,
        keys,
        values,
        log_total,
        mixed_low,
        attended,
        normed_two,
        inverse_two,
        normed_b,
        upward,
        hidden,
        downward,
        normed_three,
        inverse_three,
        normed_c,
    ) = kept
    width = w_out.shape[0]
    shift1, scale1, gate1, shift2, scale2, gate2 = modulation(modul, width)
    delta_grad = (active * grad_state).astype(jnp.bfloat16)
    grad_head = rows_product(delta_grad, normed_c)
    grad_mlp = norm_back(product(delta_grad, io_all[1]), normed_three, inverse_three)
    grad_gate2 = jnp.sum(grad_mlp * downward, 1)
    down_grad = (gate2 * grad_mlp).astype(jnp.bfloat16)
    grad_down = rows_product(down_grad, hidden)
    grad_hidden = product(down_grad, w_down)
    up_grad = jax.vjp(jax.nn.gelu, upward)[1](grad_hidden)[0].astype(jnp.bfloat16)
    grad_up = rows_product(normed_b, up_grad)
    grad_normed_b = dot_last(up_grad, w_up)
    grad_scale2 = jnp.sum(grad_normed_b * normed_two, 1)
    grad_shift2 = jnp.sum(grad_normed_b, 1)
    grad_attn = grad_mlp + norm_back(grad_normed_b * (1.0 + scale2), normed_two, inverse_two)
    grad_gate1 = jnp.sum(grad_attn * attended, 1)
    attn_grad = (gate1 * grad_attn).astype(jnp.bfloat16)
    grad_out = rows_product(mixed_low, attn_grad)
    mixed_grad = dot_last(attn_grad, w_out).astype(jnp.bfloat16)
    q_heads = heads_view(queries)
    k_heads = heads_view(keys)
    v_heads = heads_view(values)
    g_heads = heads_view(mixed_grad)
    scores = jnp.einsum(
        "sphd,snhd->shpn", q_heads, k_heads, preferred_element_type=jnp.float32
    ) * HEAD ** (-0.5)
    probs = jnp.exp(scores - log_total)
    probs_low = probs.astype(jnp.bfloat16)
    grad_probs = jnp.einsum("sphd,snhd->shpn", g_heads, v_heads, preferred_element_type=jnp.float32)
    score_grad = (
        HEAD ** (-0.5) * probs * (grad_probs - jnp.sum(grad_probs * probs, -1, keepdims=True))
    ).astype(jnp.bfloat16)
    grad_queries = jnp.einsum(
        "shpn,snhd->sphd", score_grad, k_heads, preferred_element_type=jnp.float32
    ).reshape(queries.shape)
    key_part = jnp.einsum(
        "shpn,sphd->snhd", score_grad, q_heads, preferred_element_type=jnp.float32
    ).reshape(keys.shape)
    value_part = jnp.einsum(
        "shpn,sphd->snhd", probs_low, g_heads, preferred_element_type=jnp.float32
    ).reshape(values.shape)
    grad_keys, grad_values = (
        lax.psum_scatter(key_part, PATCHES, scatter_dimension=1, tiled=True),
        lax.psum_scatter(value_part, PATCHES, scatter_dimension=1, tiled=True),
    )
    qkv_grad = jnp.concatenate([grad_queries, grad_keys, grad_values], -1).astype(jnp.bfloat16)
    grad_qkv = rows_product(normed_a, qkv_grad)
    grad_normed_a = dot_last(qkv_grad, w_qkv)
    grad_scale1 = jnp.sum(grad_normed_a * normed_one, 1)
    grad_shift1 = jnp.sum(grad_normed_a, 1)
    grad_embedded = grad_attn + norm_back(grad_normed_a * (1.0 + scale1), normed_one, inverse_one)
    embed_grad = grad_embedded.astype(jnp.bfloat16)
    grad_embed = rows_product(state_low, embed_grad)
    grad_prev = grad_state + dot_last(embed_grad, io_all[0])
    grad_modul = jnp.concatenate(
        [grad_shift1, grad_scale1, grad_gate1, grad_shift2, grad_scale2, grad_gate2], -1
    )
    grad_ada = lax.dot_general(
        silu_low.astype(jnp.float32),
        grad_modul,
        (((0,), (0,)), ((), ())),
        precision=HIGHEST_PRECISION,
    )
    grad_silu = lax.dot_general(
        grad_modul, w_ada.astype(jnp.float32), (((1,), (1,)), ((), ())), precision=HIGHEST_PRECISION
    )
    grad_cond = jax.vjp(jax.nn.silu, cond_vec)[1](grad_silu)[0]
    grad_table = lax.dot_general(
        select, grad_cond, (((0,), (0,)), ((), ())), precision=HIGHEST_PRECISION
    )
    grad_bias = jnp.concatenate([jnp.sum(grad_modul, 0), jnp.sum(grad_embedded, (0, 1))])
    grad_pos = jnp.sum(grad_embedded, 0)
    grads = (
        grad_qkv,
        grad_out,
        grad_up,
        grad_down,
        grad_ada,
        jnp.stack([grad_embed, grad_head]),
        grad_table,
        grad_pos,
        grad_bias,
    )
    return (grad_prev, grads)


def gram_part(block_cols):
    return lax.dot_general(
        block_cols, block_cols, (((1,), (1,)), ((), ())), preferred_element_type=jnp.float32
    )


def zero_gram(block_cols):
    return jnp.zeros((block_cols.shape[0], block_cols.shape[0]), jnp.float32)


def newton_step(block_cols, gram):
    gram_low = gram.astype(jnp.bfloat16)
    poly = (NS_B * gram_low.astype(jnp.float32) + NS_C * product(gram_low, gram_low)).astype(
        jnp.bfloat16
    )
    return (NS_A * block_cols.astype(jnp.float32) + product(poly, block_cols)).astype(jnp.bfloat16)


def keep_block(block_cols, gram):
    return block_cols


def adam_update(weight, first, second, grad, rate):
    first_new = BETA_FIRST * first + (1.0 - BETA_FIRST) * grad
    second_new = BETA_SECOND * second + (1.0 - BETA_SECOND) * grad * grad
    unbiased = first_new / (1.0 - BETA_FIRST**STEP_NUM)
    spread = jnp.sqrt(second_new / (1.0 - BETA_SECOND**STEP_NUM)) + 1e-08
    return (weight * (1.0 - rate * DECAY_ADAM) - rate * unbiased / spread, first_new, second_new)


def general_body(
    states,
    targets,
    lengths,
    intervals,
    qkv_copy,
    qkv_master,
    qkv_moment,
    out_copy,
    out_master,
    out_moment,
    up_copy,
    up_master,
    up_moment,
    down_copy,
    down_master,
    down_moment,
    ada_copy,
    ada_master,
    ada_first,
    ada_second,
    io_proj,
    io_first,
    io_second,
    cond_table,
    cond_first,
    cond_second,
    pos_table,
    pos_first,
    pos_second,
    biases,
    bias_first,
    bias_second,
):
    weights = (
        lax.all_gather(qkv_copy, SHARDS, axis=1, tiled=True),
        lax.all_gather(out_copy, SHARDS, axis=1, tiled=True),
        lax.all_gather(up_copy, SHARDS, axis=1, tiled=True),
        lax.all_gather(down_copy, SHARDS, axis=1, tiled=True),
        lax.all_gather(ada_copy, SHARDS, axis=1, tiled=True),
        lax.all_gather(io_proj.astype(jnp.bfloat16), SHARDS, axis=2, tiled=True),
        lax.all_gather(cond_table.astype(jnp.bfloat16), SHARDS, axis=1, tiled=True),
        lax.all_gather(pos_table.astype(jnp.bfloat16), SHARDS, axis=1, tiled=True),
        lax.all_gather(biases.astype(jnp.bfloat16), SHARDS, axis=0, tiled=True),
    )
    samples, local, values_count = states.shape
    table_rows = cond_table.shape[0]
    my_ids = lax.dynamic_slice_in_dim(intervals, lax.axis_index(SHARDS) * samples, samples)
    counts = jnp.sum(
        (intervals[:, None] == jnp.arange(NI, dtype=jnp.int32)[None]).astype(jnp.float32), 0
    )
    id_counts = jnp.sum(
        (my_ids[:, None] == jnp.arange(NI, dtype=jnp.int32)[None]).astype(jnp.float32)
        * counts[None],
        1,
    )
    weight = 1.0 / (NI * local * lax.axis_size(PATCHES) * values_count * id_counts)
    rows_iota = jnp.arange(table_rows, dtype=jnp.int32)
    id_select = (my_ids[:, None] == rows_iota[None]).astype(jnp.float32)
    state = states.astype(jnp.float32)
    seen_states = []
    kept_all = []
    for step in range(ROLL):
        select = id_select + (rows_iota == NI + step).astype(jnp.float32)[None]
        active = (step < lengths).astype(jnp.float32)[:, None, None]
        seen_states.append(state)
        state, kept = forward_step(weights, state, active, select)
        kept_all.append(kept)
    lat = latitude_weights(local)
    diff = state - targets.astype(jnp.float32)
    err = jnp.sum(jnp.sum(diff * diff, -1) * lat[None], -1)
    loss_local = jnp.sum(weight * err)
    grad_state = 2.0 * weight[:, None, None] * lat[None, :, None] * diff
    totals = None
    for step in reversed(range(ROLL)):
        select = id_select + (rows_iota == NI + step).astype(jnp.float32)[None]
        active = (step < lengths).astype(jnp.float32)[:, None, None]
        kept = kept_all[step]
        grad_state, grads = backward_step(weights, kept, grad_state, active, select)
        totals = grads if totals is None else jax.tree.map(jnp.add, totals, grads)
    reduced = (
        lax.psum_scatter(totals[0], SHARDS, scatter_dimension=1, tiled=True),
        lax.psum_scatter(totals[1], SHARDS, scatter_dimension=1, tiled=True),
        lax.psum_scatter(totals[2], SHARDS, scatter_dimension=1, tiled=True),
        lax.psum_scatter(totals[3], SHARDS, scatter_dimension=1, tiled=True),
        lax.psum_scatter(totals[4], SHARDS, scatter_dimension=1, tiled=True),
        lax.psum_scatter(totals[5], SHARDS, scatter_dimension=2, tiled=True),
        lax.psum_scatter(totals[6], SHARDS, scatter_dimension=1, tiled=True),
        lax.psum_scatter(totals[7], SHARDS, scatter_dimension=1, tiled=True),
        lax.psum_scatter(totals[8], SHARDS, scatter_dimension=0, tiled=True),
    )
    large = (
        lax.psum_scatter(reduced[0], PATCHES, scatter_dimension=0, tiled=True),
        lax.psum_scatter(reduced[1], PATCHES, scatter_dimension=0, tiled=True),
        lax.psum_scatter(reduced[2], PATCHES, scatter_dimension=0, tiled=True),
        lax.psum_scatter(reduced[3], PATCHES, scatter_dimension=0, tiled=True),
        lax.psum_scatter(reduced[4], PATCHES, scatter_dimension=0, tiled=True),
    )
    small = lax.psum((reduced[5], reduced[6], reduced[8]), PATCHES)
    grad_pos = reduced[7]
    first_copy = (lax.axis_index(PATCHES) == 0).astype(jnp.float32)
    squares = jnp.sum(grad_pos * grad_pos)
    for item in large:
        squares = squares + jnp.sum(item * item)
    small_squares = jnp.float32(0.0)
    for item in small:
        small_squares = small_squares + jnp.sum(item * item)
    squares, loss_total = lax.psum(
        (squares + first_copy * small_squares, loss_local), (PATCHES, SHARDS)
    )
    grad_norm = jnp.sqrt(squares)
    clip = jnp.minimum(1.0, CLIP_LIMIT / (grad_norm + 1e-06))
    masters = (qkv_master, out_master, up_master, down_master)
    moments = [
        MOMENTUM * old + clip * grad
        for old, grad in zip((qkv_moment, out_moment, up_moment, down_moment), large[:4])
    ]
    norms = lax.psum(
        (
            jnp.sum(moments[0] * moments[0]),
            jnp.sum(moments[1] * moments[1]),
            jnp.sum(moments[2] * moments[2]),
            jnp.sum(moments[3] * moments[3]),
        ),
        (PATCHES, SHARDS),
    )
    sizes = [jnp.sqrt(norms[which]) for which in range(4)]
    moment_sizes = jnp.stack(sizes) / CLIP_LIMIT
    scaled = [(moments[which] / (sizes[which] + 1e-07)).astype(jnp.bfloat16) for which in range(4)]
    columns = (
        lax.all_gather(scaled[0], PATCHES, axis=0, tiled=True),
        lax.all_gather(scaled[1], PATCHES, axis=0, tiled=True),
        lax.all_gather(scaled[2], PATCHES, axis=0, tiled=True),
        lax.all_gather(scaled[3], PATCHES, axis=0, tiled=True),
    )
    seq_index = lax.axis_index(PATCHES)
    seq_count = lax.axis_size(PATCHES)
    owners = [seq_index == which % seq_count for which in range(4)]
    blocks = list(columns)
    for turn in range(NS_ITERS):
        partial_value = [
            lax.cond(owners[which], gram_part, zero_gram, blocks[which]) for which in range(4)
        ]
        grams = lax.psum(
            (partial_value[0], partial_value[1], partial_value[2], partial_value[3]), SHARDS
        )
        blocks = [
            lax.cond(owners[which], newton_step, keep_block, blocks[which], grams[which])
            for which in range(4)
        ]
    blocks = [broadcast(blocks[which], PATCHES, which % seq_count) for which in range(4)]
    row_count = qkv_master.shape[0]
    fresh = []
    for which in range(4):
        my_rows = lax.dynamic_slice_in_dim(
            blocks[which], seq_index * row_count, row_count, 0
        ).astype(jnp.float32)
        all_cols = masters[which].shape[1] * lax.axis_size(SHARDS)
        fresh.append(
            masters[which] * (1.0 - RATE_MUON * DECAY_MUON)
            - RATE_MUON * 0.2 * math.sqrt(all_cols) * my_rows
        )
    copies = (
        lax.all_gather(fresh[0].astype(jnp.bfloat16), PATCHES, axis=0, tiled=True),
        lax.all_gather(fresh[1].astype(jnp.bfloat16), PATCHES, axis=0, tiled=True),
        lax.all_gather(fresh[2].astype(jnp.bfloat16), PATCHES, axis=0, tiled=True),
        lax.all_gather(fresh[3].astype(jnp.bfloat16), PATCHES, axis=0, tiled=True),
    )
    ada_res = adam_update(ada_master, ada_first, ada_second, clip * large[4], RATE_ADAM)
    io_res = adam_update(io_proj, io_first, io_second, clip * small[0], RATE_ADAM)
    cond_res = adam_update(cond_table, cond_first, cond_second, clip * small[1], RATE_TABLE)
    pos_res = adam_update(pos_table, pos_first, pos_second, clip * grad_pos, RATE_TABLE)
    bias_res = adam_update(biases, bias_first, bias_second, clip * small[2], RATE_ADAM)
    return (
        loss_total,
        grad_norm,
        moment_sizes,
        fresh[0],
        moments[0],
        copies[0],
        fresh[1],
        moments[1],
        copies[1],
        fresh[2],
        moments[2],
        copies[2],
        fresh[3],
        moments[3],
        copies[3],
        ada_res[0],
        ada_res[1],
        ada_res[2],
        io_res[0],
        io_res[1],
        io_res[2],
        cond_res[0],
        cond_res[1],
        cond_res[2],
        pos_res[0],
        pos_res[1],
        pos_res[2],
        bias_res[0],
        bias_res[1],
        bias_res[2],
    )


LANES = 128
MATRICES = 4
LOW = jnp.bfloat16
MESH = pl.DeviceIdType.MESH


def round_up(value, unit):
    return -(-value // unit) * unit


def member_peer(members, shift):
    index = lax.axis_index(PATCHES)
    return {PATCHES: index // members * members + lax.rem(lax.rem(index, members) + shift, members)}


def group_peer(members, shift):
    return {PATCHES: lax.rem(lax.axis_index(PATCHES) + shift * members, lax.axis_size(PATCHES))}


def sibling_peer():
    index = lax.axis_index(SHARDS)
    return {SHARDS: index + 1 - 2 * lax.rem(index, 2)}


def where(condition, action):
    if condition is None:
        action()
    else:
        pl.when(condition())(action)


class Moves:
    def __init__(self, name, ids, vmem=None):
        self.name = name
        self.ids = ids
        self.vmem = vmem
        self.operands = []
        self.operand_specs = []
        self.outputs = []
        self.output_specs = []
        self.scratches = []
        self.moves = []
        self.locals = []
        self.steps = []
        self.peers = {}

    def operand(self, array, space=pl.ANY):
        self.operands.append(array)
        self.operand_specs.append(pl.BlockSpec(memory_space=space))
        return (0, len(self.operands) - 1)

    def output(self, shape, dtype, space=pl.ANY):
        self.outputs.append(jax.ShapeDtypeStruct(shape, dtype))
        self.output_specs.append(pl.BlockSpec(memory_space=space))
        return (1, len(self.outputs) - 1)

    def scratch(self, shape, dtype):
        self.scratches.append(pltpu.VMEM(shape, dtype))
        return (2, len(self.scratches) - 1)

    def keep(self, source, source_at, target, target_at, later=False):
        self.locals.append((source, source_at, target, target_at, later))
        return len(self.locals) - 1

    def shape(self, scratch):
        return self.scratches[scratch[1]].shape

    def load(self, array):
        target = self.scratch(array.shape, array.dtype)
        return target, self.keep(self.operand(array), None, target, None)

    def save(self, source, shape, dtype):
        number = self.keep(source, None, self.output(shape, dtype), None, True)
        return number

    def start_local(self, number):
        self.steps.append((self.begin_local, number))

    def begin_local(self, number):
        self.local[number].start()

    def move(
        self, peer_key, peer, source, source_at, target, target_at, after=(), sends=None, takes=None, later=False
    ):
        number = len(self.moves)
        self.peers.setdefault(peer_key, peer)
        self.moves.append((peer_key, source, source_at, target, target_at, sends, takes, later or bool(after)))
        for earlier in after:
            self.steps.append((self.await_move, earlier))
        if after:
            self.steps.append((self.start_move, number))
        return number

    def wait_for(self, number):
        self.steps.append((self.await_move, number))

    def start(self, number):
        self.steps.append((self.start_move, number))

    def wait_local(self, number):
        self.steps.append((self.await_local, number))

    def task(self, action):
        self.steps.append((self.do_task, action))

    def await_move(self, number):
        if number not in self.arrived:
            self.arrived.add(number)
            where(self.moves[number][6], self.remote[number].wait_recv)

    def start_move(self, number):
        where(self.moves[number][5], self.remote[number].start)

    def await_local(self, number):
        if number not in self.kept:
            self.kept.add(number)
            self.local[number].wait()

    def do_task(self, action):
        action(self.ref)

    def ref(self, which):
        return self.refs[which[0]][which[1]]

    def view(self, which, index):
        ref = self.ref(which)
        return ref.at[index()] if index is not None else ref

    def kernel(self, *refs):
        sizes = (len(self.operands), len(self.outputs), len(self.scratches))
        self.refs = (refs[: sizes[0]], refs[sizes[0] : sizes[0] + sizes[1]], refs[sizes[0] + sizes[1] : sum(sizes)])
        local_sem, send_sem, recv_sem = refs[sum(sizes) :]
        self.arrived, self.kept = set(), set()
        devices = {key: peer() for key, peer in self.peers.items()}
        barrier = pltpu.get_barrier_semaphore()
        for device in devices.values():
            pl.semaphore_signal(barrier, inc=1, device_id=device, device_id_type=MESH)
        pl.semaphore_wait(barrier, len(devices))
        self.remote = []
        for number, (key, source, source_at, target, target_at, _, _, later) in enumerate(self.moves):
            self.remote.append(
                pltpu.make_async_remote_copy(
                    src_ref=self.view(source, source_at),
                    dst_ref=self.view(target, target_at),
                    send_sem=send_sem.at[number],
                    recv_sem=recv_sem.at[number],
                    device_id=devices[key],
                    device_id_type=MESH,
                )
            )
            if not later:
                self.start_move(number)
        self.local = [
            pltpu.make_async_copy(self.view(source, source_at), self.view(target, target_at), local_sem.at[number])
            for number, (source, source_at, target, target_at, _) in enumerate(self.locals)
        ]
        for copy, entry in zip(self.local, self.locals):
            if not entry[4]:
                copy.start()
        for action, number in self.steps:
            action(number)
        for number in range(len(self.locals)):
            self.await_local(number)
        for number, copy in enumerate(self.remote):
            self.await_move(number)
            where(self.moves[number][5], copy.wait_send)

    def run(self):
        return pl.pallas_call(
            self.kernel,
            out_shape=self.outputs,
            in_specs=self.operand_specs,
            out_specs=self.output_specs,
            scratch_shapes=[
                *self.scratches,
                pltpu.SemaphoreType.DMA((max(1, len(self.locals)),)),
                pltpu.SemaphoreType.DMA((len(self.moves),)),
                pltpu.SemaphoreType.DMA((len(self.moves),)),
            ],
            compiler_params=pltpu.CompilerParams(
                collective_id=self.ids.setdefault(self.name, len(self.ids)),
                has_side_effects=True,
                vmem_limit_bytes=self.vmem,
            ),
            name=self.name,
        )(*self.operands)

    def along(self, axis, source, target, pairs, later=False):
        numbers = []
        count = lax.axis_size(axis)

        def other(shift):
            return lax.rem(lax.axis_index(axis) + shift, count)

        for shift in range(1, count):
            for source_at, target_at in pairs:
                numbers.append(
                    self.move(
                        (axis, shift),
                        lambda shift=shift: {axis: other(shift)},
                        source,
                        None if source_at is None else (lambda at=source_at, shift=shift: at(other(shift))),
                        target,
                        lambda at=target_at: at(lax.axis_index(axis)),
                        later=later,
                    )
                )
        for source_at, target_at in pairs:
            self.keep(
                source,
                None if source_at is None else (lambda at=source_at: at(lax.axis_index(axis))),
                target,
                lambda at=target_at: at(lax.axis_index(axis)),
            )
        return numbers

    def gather(self, axis, array):
        target = self.output((lax.axis_size(axis),) + array.shape, array.dtype)
        self.along(axis, self.operand(array), target, [(None, lambda sender: (sender,))])

    def gather_pairs(self, array, parts=1, hold=False):
        shards = lax.axis_size(SHARDS)
        source = self.operand(array)
        target = self.output((shards,) + array.shape, array.dtype)
        rows = array.shape[0] // parts

        def place(back_pair, part):
            return (lax.rem(lax.axis_index(SHARDS) + shards - 2 * back_pair, shards), pl.ds(part * rows, rows))

        firsts = []
        for part in range(parts):
            for pair in range(1, shards // 2):
                number = self.move(
                    (SHARDS, 2 * pair),
                    lambda pair=pair: {SHARDS: lax.rem(lax.axis_index(SHARDS) + 2 * pair, shards)},
                    source,
                    lambda part=part: (pl.ds(part * rows, rows),),
                    target,
                    functools.partial(place, 0, part),
                )
                firsts.append((functools.partial(place, pair, part), number))
        own = lambda: (lax.axis_index(SHARDS),)
        self.move((SHARDS,), sibling_peer, source, None, target, own)
        self.keep(source, None, target, own)
        waiting = [(target, at, number) for at, number in firsts]
        if hold:
            return waiting
        self.to_sibling(waiting)

    def gather_columns(self, axis, array, target):
        width = array.shape[-1]
        lead = (slice(None),) * (array.ndim - 1)
        numbers = self.along(
            axis,
            self.operand(array),
            target,
            [(None, lambda sender: lead + (pl.ds(pl.multiple_of(sender * width, LANES), width),))],
        )
        return numbers, len(self.locals) - 1

    def gather_twice(self, arrays, members):
        shards = lax.axis_size(SHARDS)
        entries = []
        for array in arrays:
            source = self.operand(array)
            width = array.shape[1]
            target = self.scratch((array.shape[0], shards * width), array.dtype)
            rows = array.shape[0] // members

            def columns(back_pair, width=width):
                who = lax.rem(lax.axis_index(SHARDS) + shards - 2 * back_pair, shards)
                return pl.ds(pl.multiple_of(who * width, LANES), width)

            def place(back_member, back_pair, rows=rows, columns=columns):
                index = lax.rem(lax.rem(lax.axis_index(PATCHES), members) + members - back_member, members)
                return (pl.ds(pl.multiple_of(index * rows, rows), rows), columns(back_pair))

            def mine(rows=rows):
                index = lax.rem(lax.axis_index(PATCHES), members)
                return (pl.ds(pl.multiple_of(index * rows, rows), rows),)

            def whole(columns=columns):
                return (slice(None), columns(0))

            firsts = [
                self.move(
                    (SHARDS, 2 * pair),
                    lambda pair=pair: {SHARDS: lax.rem(lax.axis_index(SHARDS) + 2 * pair, shards)},
                    source,
                    mine,
                    target,
                    functools.partial(place, 0, 0),
                )
                for pair in range(1, shards // 2)
            ]
            near = self.move((SHARDS,), sibling_peer, source, None, target, whole)
            local = self.keep(source, None, target, whole)
            entries.append((target, place, firsts, [near, *firsts], local))
        last = []
        for target, place, firsts, numbers, _ in entries:
            for pair, first in enumerate(firsts, 1):
                near = functools.partial(place, 0, pair)
                for shift in range(1, members):
                    number = self.move(
                        (PATCHES, members, shift),
                        functools.partial(member_peer, members, shift),
                        target,
                        near,
                        target,
                        near,
                        (first,),
                    )
                    last.append((target, functools.partial(place, shift, pair), number, numbers))
                numbers.append(self.move((SHARDS,), sibling_peer, target, near, target, near, (first,)))
        for target, at, number, numbers in last:
            numbers += [number, self.move((SHARDS,), sibling_peer, target, at, target, at, (number,))]
        return [(target, numbers, local) for target, _, _, numbers, local in entries]

    def to_sibling(self, waiting):
        for target, place, number in waiting:
            self.move((SHARDS,), sibling_peer, target, place, target, place, (number,))

    def exchange(self, axis, array, later=False):
        target = self.output(array.shape, array.dtype)
        return self.along(
            axis, self.operand(array), target, [(lambda receiver: (receiver,), lambda sender: (sender,))], later
        )

    def exchange_columns(self, axis, array):
        width = array.shape[-1] // lax.axis_size(axis)
        target = self.output((lax.axis_size(axis), array.shape[0], width), array.dtype)
        self.along(
            axis,
            self.operand(array),
            target,
            [
                (
                    lambda receiver: (slice(None), pl.ds(pl.multiple_of(receiver * width, LANES), width)),
                    lambda sender: (sender,),
                )
            ],
        )

    def rows_to_heads(self, axis, array, planes, target):
        count, rows = lax.axis_size(axis), array.shape[0]
        columns = array.shape[1] // planes
        width = columns // count
        return self.along(
            axis,
            self.operand(array),
            target,
            [
                (
                    lambda receiver, plane=plane: (
                        slice(None),
                        pl.ds(pl.multiple_of(plane * columns + receiver * width, LANES), width),
                    ),
                    lambda sender, plane=plane: (plane, pl.ds(pl.multiple_of(sender * rows, rows), rows)),
                )
                for plane in range(planes)
            ],
        )

    def head_rows(self, source, target, planes, rows, columns, members, back_group):
        count = lax.axis_size(PATCHES)
        width = columns // count
        for shift_member in range(members):
            for plane in planes:

                def peer(shift_member=shift_member):
                    index = lax.axis_index(PATCHES)
                    there = lax.rem(index // members + back_group, MATRICES) * members
                    return there + lax.rem(lax.rem(index, members) + shift_member, members)

                def source_at(peer=peer, plane=plane):
                    return (plane, pl.ds(pl.multiple_of(peer() * rows, rows), rows))

                def target_at(plane=plane):
                    start = plane * columns + lax.axis_index(PATCHES) * width
                    return (slice(None), pl.ds(pl.multiple_of(start, LANES), width))

                if shift_member or back_group:
                    self.start(
                        self.move(
                            (PATCHES, count, back_group, shift_member),
                            lambda peer=peer: {PATCHES: peer()},
                            source,
                            source_at,
                            target,
                            target_at,
                            later=True,
                        )
                    )
                else:

                    def own(ref, source_at=source_at, target_at=target_at):
                        ref(target)[target_at()] = ref(source)[source_at()]

                    self.task(own)


def contract(left, right, left_dim, right_dim):
    return lax.dot_general(
        left, right, (((left_dim,), (right_dim,)), ((), ())), preferred_element_type=jnp.float32
    )


CHAIN_CHUNKS = 8
GRAM_COLS = 256


def attend(queries, keys, values):
    scores = contract(queries, keys, 1, 1) * HEAD ** (-0.5)
    expo = jnp.exp(scores - jnp.max(scores, -1, keepdims=True))
    probs = (expo / jnp.sum(expo, -1, keepdims=True)).astype(LOW)
    return contract(probs, values, 1, 0)


def group_rows(rows, members, shift):
    size = rows * members
    there = lax.rem(lax.axis_index(PATCHES) // members + shift, MATRICES)
    return pl.ds(pl.multiple_of(there * size, size), size)


def add_attention(moves, qkv, mixed, arrivals, rows, members, waiting):
    for number in arrivals:
        moves.wait_for(number)
    for number in range(3):
        moves.wait_local(number)
    moves.to_sibling(waiting)
    count = lax.axis_size(PATCHES)
    width = HEADS // count * HEAD
    buffer = moves.scratch((1, rows * count, width), LOW)
    for shift in (*range(1, MATRICES), 0):

        def work(ref, shift=shift):
            at = group_rows(rows, members, shift)
            parts = []
            for head in range(width // HEAD):
                lanes = pl.ds(head * HEAD, HEAD)
                parts.append(attend(ref(qkv)[0, at, lanes], ref(qkv)[1, :, lanes], ref(qkv)[2, :, lanes]))
            ref(buffer)[0, at, :] = jnp.concatenate(parts, -1).astype(LOW)

        moves.task(work)
        moves.head_rows(buffer, mixed, (0,), rows, width * count, members, shift)


def add_attention_back(moves, qkv, grads, result, arrivals, rows, members, waiting):
    for number in arrivals:
        moves.wait_for(number)
    moves.wait_local(0)
    moves.to_sibling(waiting)
    count = lax.axis_size(PATCHES)
    width = HEADS // count * HEAD
    heads = width // HEAD
    buffer = moves.scratch((3, rows * count, width), LOW)
    key_total = moves.scratch((heads, rows * count, HEAD), jnp.float32)
    value_total = moves.scratch((heads, rows * count, HEAD), jnp.float32)
    for shift in (*range(1, MATRICES), 0):

        def work(ref, shift=shift):
            at = group_rows(rows, members, shift)
            parts = []
            for head in range(heads):
                lanes = pl.ds(head * HEAD, HEAD)
                queries, keys, values = ref(qkv)[0, at, lanes], ref(qkv)[1, :, lanes], ref(qkv)[2, :, lanes]
                grad = ref(grads)[0, at, lanes]
                scores = contract(keys, queries, 1, 1) * HEAD ** (-0.5)
                expo = jnp.exp(scores - jnp.max(scores, 0, keepdims=True))
                probs = expo / jnp.sum(expo, 0, keepdims=True)
                grad_probs = contract(values, grad, 1, 1)
                shared = jnp.sum(grad_probs * probs, 0, keepdims=True)
                score_grad = (HEAD ** (-0.5) * probs * (grad_probs - shared)).astype(LOW)
                parts.append(contract(score_grad, keys, 0, 0))
                key_part = contract(score_grad, queries, 1, 0)
                value_part = contract(probs.astype(LOW), grad, 1, 0)
                if shift == 1:
                    ref(key_total)[head] = key_part
                    ref(value_total)[head] = value_part
                else:
                    ref(key_total)[head] += key_part
                    ref(value_total)[head] += value_part
            ref(buffer)[0, at, :] = jnp.concatenate(parts, -1).astype(LOW)

        moves.task(work)
        moves.head_rows(buffer, result, (0,), rows, width * count, members, shift)

    def finish(ref):
        for plane, total in ((1, key_total), (2, value_total)):
            ref(buffer)[plane] = jnp.concatenate([ref(total)[head] for head in range(heads)], -1).astype(LOW)

    moves.task(finish)
    for shift in (*range(1, MATRICES), 0):
        moves.head_rows(buffer, result, (1, 2), rows, width * count, members, shift)


def mod_row(ref, table, row):
    return ref(table)[pl.ds(row, 1), :]


def project(moves, source, weights, target, count):
    def action(ref):
        width = ref(source).shape[1]

        @pl.loop(0, count // width)
        def _(part):
            cols = pl.ds(pl.multiple_of(part * width, width), width)
            ref(target)[:, cols] = contract(ref(source)[...], ref(weights)[:, cols], 1, 0).astype(LOW)

    moves.task(action)


def embed(ref, state_low, io_weights, mods, pos, embedded, normed_low):
    value = contract(ref(state_low)[...], io_weights, 1, 0) + mods(6) + ref(pos)[...].astype(jnp.float32)
    ref(embedded)[...] = value
    normed, _ = layer_norm(value)
    ref(normed_low)[...] = (normed * (1.0 + mods(1)) + mods(0)).astype(LOW)


def begin_step(ids, members, state, id_rows, active, cond_table, biases, pos, ada, io_low, w_out, w_qkv):
    f32 = jnp.float32
    shards = lax.axis_size(SHARDS)
    (rows, padded), (table_rows, _) = state.shape, cond_table.shape
    width = w_out.shape[0]
    ada_cols = ada.shape[1]
    moves = Moves("begin", ids, 56 * 2**20)
    table = moves.scratch((table_rows, width), f32)
    bias = moves.scratch((1, biases.shape[1] * shards), f32)
    pos_all = moves.scratch((rows, width), LOW)
    id_rows, active, state = [moves.operand(item, pltpu.VMEM) for item in (id_rows, active, state)]
    small = [moves.gather_columns(SHARDS, cond_table, table), moves.gather_columns(SHARDS, biases, bias)]
    pos_moves, pos_local = moves.gather_columns(SHARDS, pos, pos_all)
    ada_weights, ada_load = moves.load(ada)
    vmem = functools.partial(moves.output, space=pltpu.VMEM)
    extras = vmem((ROLL, 8, width), f32)
    cond_vec, silu_low = vmem((shards * ROLL, width), f32), vmem((shards * ROLL, width), LOW)
    embedded, normed_low = vmem((rows, width), f32), vmem((rows, width), LOW)
    state_low, qkv_rows = vmem((rows, padded), LOW), vmem((rows, 3 * width), LOW)
    parts_leaving, parts = [moves.scratch((shards, ROLL, ada_cols), f32) for _ in range(2)]

    def modulate(ref):
        row = lax.broadcasted_iota(jnp.int32, (shards * ROLL, 1), 0)
        ids_here = ref(id_rows)[:, :1]
        value = jnp.zeros((shards * ROLL, width), f32)
        for entry in range(table_rows):
            of_entry = ref(table)[pl.ds(entry, 1), :].astype(LOW).astype(f32)
            chosen = (ids_here == entry) if entry < NI else (lax.rem(row, ROLL) == entry - NI)
            value = value + jnp.where(chosen, of_entry, 0.0)
        ref(cond_vec)[...] = value
        value = (value / (1.0 + jnp.exp(-value))).astype(LOW)
        ref(silu_low)[...] = value
        start = pl.multiple_of(lax.axis_index(SHARDS) * ada_cols, LANES)
        value = contract(value, ref(ada_weights)[...], 1, 0)
        value = value + ref(bias)[:, pl.ds(start, ada_cols)].astype(LOW).astype(f32)
        for sample in range(shards):
            ref(parts_leaving)[sample] = value[sample * ROLL : (sample + 1) * ROLL]
        ref(parts)[lax.axis_index(SHARDS)] = ref(parts_leaving)[lax.axis_index(SHARDS)]

    for numbers, local in small:
        for number in numbers:
            moves.wait_for(number)
        moves.wait_local(local)
    moves.wait_local(ada_load)
    moves.task(modulate)
    modul_moves = []
    for shift in range(1, shards):

        def other(shift=shift):
            return lax.rem(lax.axis_index(SHARDS) + shift, shards)

        number = moves.move(
            (SHARDS, shift),
            lambda other=other: {SHARDS: other()},
            parts_leaving,
            lambda other=other: (other(),),
            parts,
            lambda: (lax.axis_index(SHARDS),),
            later=True,
        )
        modul_moves.append(number)
        moves.start(number)
    weights = moves.gather_twice((io_low.reshape(-1, io_low.shape[-1]), w_out, w_qkv), members)

    def collect(ref):
        bias_row = ref(bias)[:, pl.ds(6 * width, width)].astype(LOW).astype(f32)
        for step in range(ROLL):
            for piece in range(6 * 2):
                start = piece * width // 2
                value = ref(parts)[start // ada_cols, pl.ds(step, 1), pl.ds(start % ada_cols, width // 2)]
                ref(extras)[step, pl.ds(piece // 2, 1), pl.ds(piece % 2 * width // 2, width // 2)] = value
            ref(extras)[step, pl.ds(6, 1), :] = bias_row
            ref(extras)[step, pl.ds(7, 1), :] = ref(active)[pl.ds(step, 1), :]

    def start_step(ref):
        ref(state_low)[...] = ref(state)[...].astype(LOW)
        mods = lambda row: ref(extras)[0, pl.ds(row, 1), :]
        embed(ref, state_low, ref(weights[0][0])[pl.ds(0, padded), :], mods, pos_all, embedded, normed_low)

    for number in modul_moves:
        moves.wait_for(number)
    moves.task(collect)
    for number in (*pos_moves, *weights[0][1]):
        moves.wait_for(number)
    moves.wait_local(pos_local)
    moves.wait_local(weights[0][2])
    moves.task(start_step)
    for target, numbers, local in weights:
        for number in numbers:
            moves.wait_for(number)
        moves.wait_local(local)
        save = moves.save(target, moves.shape(target), LOW)
        moves.start_local(save)
    moves.start_local(moves.save(pos_all, (rows, width), LOW))
    project(moves, normed_low, weights[2][0], qkv_rows, 3 * width)
    return moves.run()


class Tokens:
    def __init__(self, moves, rows, width):
        self.moves = moves
        self.shards = lax.axis_size(SHARDS)
        self.rows = rows
        self.tokens = moves.scratch((self.shards, rows, width), LOW)
        self.own_part = moves.scratch((rows, width), jnp.float32)
        self.leaving = moves.scratch((self.shards, rows, width), LOW)
        self.arriving = moves.scratch((self.shards, rows, width), LOW)

    def me(self):
        return lax.axis_index(SHARDS)

    def back(self, pair, sibling):
        index = lax.rem(self.me() + self.shards - 2 * pair, self.shards)
        return index + 1 - 2 * lax.rem(index, 2) if sibling else index

    def part(self, pair, sibling, work):
        moves = self.moves
        slot = functools.partial(self.back, pair, sibling)

        def action(ref):
            value = work(ref, slot())
            if pair or sibling:
                ref(self.leaving)[slot()] = value.astype(LOW)
            else:
                ref(self.own_part)[...] = value

        moves.task(action)
        if pair or sibling:
            number = moves.move(
                (SHARDS, pair, sibling),
                lambda: {SHARDS: slot()},
                self.leaving,
                lambda: (slot(),),
                self.arriving,
                lambda: (self.me(),),
                later=True,
            )
            moves.start(number)
            self.parts.append(number)

    def run(self, work):
        moves, halves = self.moves, 2
        self.parts = []
        size = self.rows // halves
        pairs = self.shards // 2

        def half(pair, sibling, number):
            return (self.back(pair, sibling), pl.ds(number * size, size))

        firsts = {}
        for pair in range(1, pairs):
            for number in range(halves):
                place = functools.partial(half, 0, False, number)
                firsts[pair, number] = moves.move(
                    (SHARDS, pairs - pair, False),
                    functools.partial(lambda pair: {SHARDS: self.back(pairs - pair, False)}, pair),
                    self.tokens,
                    place,
                    self.tokens,
                    place,
                    later=True,
                )
                moves.start(firsts[pair, number])
        own = functools.partial(self.back, 0, False)
        near = moves.move(
            (SHARDS, 0, True), sibling_peer, self.tokens, lambda: (own(),), self.tokens, lambda: (own(),), later=True
        )
        moves.start(near)
        self.part(0, False, work)
        moves.wait_for(near)
        self.part(0, True, work)
        for pair in range(1, pairs):
            handed = []
            for number in range(halves):
                place = functools.partial(half, pair, False, number)
                handed.append(
                    moves.move(
                        (SHARDS, 0, True),
                        sibling_peer,
                        self.tokens,
                        place,
                        self.tokens,
                        place,
                        (firsts[pair, number],),
                    )
                )
            self.part(pair, False, work)
            for number in handed:
                moves.wait_for(number)
            self.part(pair, True, work)

    def wait(self):
        for number in self.parts:
            self.moves.wait_for(number)

    def total(self, ref):
        value = ref(self.own_part)[...]
        for shift in range(1, self.shards):
            value = value + ref(self.arriving)[lax.rem(self.me() + shift, self.shards)].astype(jnp.float32)
        return value


GELU_SCALE = math.sqrt(2.0 / math.pi)
GELU_CUBE = 0.044715


def gelu_inner(values):
    return jnp.tanh(GELU_SCALE * (values + GELU_CUBE * values * values * values))


def gelu_slope(values):
    inner = gelu_inner(values)
    rise = GELU_SCALE * (1.0 + 3.0 * GELU_CUBE * values * values)
    return 0.5 * (1.0 + inner) + 0.5 * values * (1.0 - inner * inner) * rise


def feed_forward(ids, step, mods, mods_next, mixed, embedded, state, pos, w_out, w_up, w_down, io_all, w_qkv, moment_part):
    f32 = jnp.float32
    last = mods_next is None
    rows, width = mixed.shape
    padded = state.shape[1]
    hidden_count = w_up.shape[1]
    shards = lax.axis_size(SHARDS)
    moves = Moves(f"feed{step}", ids, 56 * 2**20)
    vmem = functools.partial(moves.operand, space=pltpu.VMEM)
    out_weights, out_load = moves.load(w_out)
    mods, mixed, embedded, state = vmem(mods), vmem(mixed), vmem(embedded), vmem(state)
    up_weights, up_load = moves.load(w_up)
    down_weights, down_load = moves.load(w_down)
    io_weights, io_load = moves.load(io_all)
    attended, after_attn, downward, after_mlp = [moves.output((rows, width), f32, pltpu.VMEM) for _ in range(4)]
    normed_c = moves.output((rows, width), LOW, pltpu.VMEM)
    state_next = moves.output((rows, padded), f32, pltpu.VMEM)
    upward = moves.scratch((shards, rows, hidden_count), f32)
    hidden = moves.scratch((shards, rows, hidden_count), LOW)
    feed = Tokens(moves, rows, width)
    saves = [
        moves.save(feed.tokens, (shards, rows, width), LOW),
        moves.save(upward, (shards, rows, hidden_count), f32),
        moves.save(hidden, (shards, rows, hidden_count), LOW),
    ]
    if not last:
        mods_next, pos = vmem(mods_next), vmem(pos)
        qkv_weights, qkv_load = moves.load(w_qkv)
        embedded_next = moves.output((rows, width), f32, pltpu.VMEM)
        normed_next = moves.output((rows, width), LOW, pltpu.VMEM)
        state_low = moves.output((rows, padded), LOW, pltpu.VMEM)
        qkv_next = moves.output((rows, w_qkv.shape[1]), LOW, pltpu.VMEM)
    moves.exchange(PATCHES, moment_part)

    def begin(ref):
        value = contract(ref(mixed)[...], ref(out_weights)[...], 1, 0)
        ref(attended)[...] = value
        value = ref(embedded)[...] + mod_row(ref, mods, 2) * value
        ref(after_attn)[...] = value
        normed, _ = layer_norm(value)
        normed = normed * (1.0 + mod_row(ref, mods, 4)) + mod_row(ref, mods, 3)
        ref(feed.tokens)[feed.me()] = normed.astype(LOW)

    def work(ref, slot):
        value = contract(ref(feed.tokens)[slot], ref(up_weights)[...], 1, 0)
        ref(upward)[slot] = value
        value = (0.5 * value * (1.0 + gelu_inner(value))).astype(LOW)
        ref(hidden)[slot] = value
        return contract(value, ref(down_weights)[...], 1, 1)

    def finish(ref):
        value = feed.total(ref)
        ref(downward)[...] = value
        value = ref(after_attn)[...] + mod_row(ref, mods, 5) * value
        ref(after_mlp)[...] = value
        normed, _ = layer_norm(value)
        normed = normed.astype(LOW)
        ref(normed_c)[...] = normed
        delta = contract(normed, ref(io_weights)[1], 1, 1)
        value = ref(state)[...] + mod_row(ref, mods, 7)[:, :padded] * delta
        ref(state_next)[...] = value
        if not last:
            ref(state_low)[...] = value.astype(LOW)
            mods_there = functools.partial(mod_row, ref, mods_next)
            embed(ref, state_low, ref(io_weights)[0], mods_there, pos, embedded_next, normed_next)

    moves.wait_local(out_load)
    moves.task(begin)
    moves.wait_local(up_load)
    moves.wait_local(down_load)
    feed.run(work)
    for number in saves:
        moves.start_local(number)
    moves.wait_local(io_load)
    feed.wait()
    moves.task(finish)
    if not last:
        moves.wait_local(qkv_load)
        project(moves, normed_next, qkv_weights, qkv_next, w_qkv.shape[1])
    return moves.run()


def feed_back(ids, step, mods, mods_later, later, grad_state, kept, w_out, w_up, w_down, io_all, w_qkv):
    f32 = jnp.float32
    attended, after_attn, downward, after_mlp, upward = kept
    rows, width = attended.shape
    padded = grad_state.shape[1]
    hidden_count = w_up.shape[1]
    shards = lax.axis_size(SHARDS)
    moves = Moves(f"feed_back{step}", ids, 56 * 2**20)
    vmem = functools.partial(moves.operand, space=pltpu.VMEM)
    io_weights, io_load = moves.load(io_all)
    if later is not None:
        qkv_weights, qkv_load = moves.load(w_qkv)
        later = [vmem(item) for item in later]
        mods_later = vmem(mods_later)
        embed_grad = moves.output((rows, width), LOW, pltpu.VMEM)
    down_weights, down_load = moves.load(w_down)
    up_weights, up_load = moves.load(w_up)
    slopes, slopes_load = moves.load(upward)
    out_weights, out_load = moves.load(w_out)
    mods, grad_state = vmem(mods), vmem(grad_state)
    attended, after_attn, downward, after_mlp = [vmem(item) for item in (attended, after_attn, downward, after_mlp)]
    vectors = moves.output((8, width), f32, pltpu.VMEM)
    state_out = moves.output((rows, padded), f32, pltpu.VMEM)
    delta_grad = moves.output((rows, padded), LOW, pltpu.VMEM)
    grad_attn = moves.output((rows, width), f32, pltpu.VMEM)
    attn_grad, mixed_grad = [moves.output((rows, width), LOW, pltpu.VMEM) for _ in range(2)]
    grad_mlp = moves.scratch((rows, width), f32)
    up_grad = moves.scratch((shards, rows, hidden_count), LOW)
    feed = Tokens(moves, rows, width)
    saves = [
        moves.save(feed.tokens, (shards, rows, width), LOW),
        moves.save(up_grad, (shards, rows, hidden_count), LOW),
    ]

    def put(ref, row, value):
        ref(vectors)[pl.ds(row, 1), :] = jnp.sum(value, 0, keepdims=True)

    def before(ref):
        qkv_grad, embedded, grad_later = later
        grad = contract(ref(qkv_grad)[...], ref(qkv_weights)[...], 1, 1)
        normed, inverse = layer_norm(ref(embedded)[...])
        put(ref, 5, grad * normed)
        put(ref, 4, grad)
        grad = grad * (1.0 + mod_row(ref, mods_later, 1))
        grad = ref(grad_later)[...] + norm_back(grad, normed, inverse)
        put(ref, 6, grad)
        grad = grad.astype(LOW)
        ref(embed_grad)[...] = grad
        ref(state_out)[...] = ref(grad_state)[...] + contract(grad, ref(io_weights)[0], 1, 1)

    def begin(ref):
        if later is None:
            ref(state_out)[...] = ref(grad_state)[...]
            ref(vectors)[...] = jnp.zeros((8, width), f32)
        grad = (mod_row(ref, mods, 7)[:, :padded] * ref(state_out)[...]).astype(LOW)
        ref(delta_grad)[...] = grad
        normed, inverse = layer_norm(ref(after_mlp)[...])
        grad = norm_back(contract(grad, ref(io_weights)[1], 1, 0), normed, inverse)
        ref(grad_mlp)[...] = grad
        put(ref, 3, grad * ref(downward)[...])
        ref(feed.tokens)[feed.me()] = (mod_row(ref, mods, 5) * grad).astype(LOW)

    def work(ref, slot):
        value = contract(ref(feed.tokens)[slot], ref(down_weights)[...], 1, 0)
        value = (value * gelu_slope(ref(slopes)[slot])).astype(LOW)
        ref(up_grad)[slot] = value
        return contract(value, ref(up_weights)[...], 1, 1)

    def finish(ref):
        grad = feed.total(ref)
        normed, inverse = layer_norm(ref(after_attn)[...])
        put(ref, 2, grad * normed)
        put(ref, 1, grad)
        grad = ref(grad_mlp)[...] + norm_back(grad * (1.0 + mod_row(ref, mods, 4)), normed, inverse)
        ref(grad_attn)[...] = grad
        put(ref, 0, grad * ref(attended)[...])
        grad = (mod_row(ref, mods, 2) * grad).astype(LOW)
        ref(attn_grad)[...] = grad
        ref(mixed_grad)[...] = contract(grad, ref(out_weights)[...], 1, 1).astype(LOW)

    moves.wait_local(io_load)
    if later is not None:
        moves.wait_local(qkv_load)
        moves.task(before)
    moves.task(begin)
    for number in (down_load, up_load, slopes_load):
        moves.wait_local(number)
    feed.run(work)
    for number in saves:
        moves.start_local(number)
    moves.wait_local(out_load)
    feed.wait()
    moves.task(finish)
    results = moves.run()
    return results if later is not None else [None, *results]


def reduce_step(
    ids, members, group_cols, qkv_grad, embedded, grad_attn, mods, w_qkv, rows_late, rows_early, gathered, mlp, ada
):
    f32 = jnp.float32
    shards, seq_count = lax.axis_size(SHARDS), lax.axis_size(PATCHES)
    rows, width = embedded.shape
    block_rows, most_cols = width, max(group_cols)
    part, ada_cols = width // shards, ada.shape[1]
    up_mine, down_mine, down_leaving = mlp
    moves = Moves("reduce", ids, 60 * 2**20)
    vmem = functools.partial(moves.operand, space=pltpu.VMEM)
    qkv_grad, embedded, grad_attn, mods = vmem(qkv_grad), vmem(embedded), vmem(grad_attn), vmem(mods)
    rows_late, rows_early = vmem(rows_late), vmem(rows_early)

    def shard():
        return lax.axis_index(SHARDS)

    def patch():
        return lax.axis_index(PATCHES)

    def group():
        return patch() // members

    def member():
        return lax.rem(patch(), members)

    def columns(index, size):
        return pl.ds(pl.multiple_of(index * size, LANES), size)

    def await_all(numbers):
        for number in numbers:
            moves.wait_for(number)

    def to_others(axis, source, source_at, target, leave_own=False):
        count = lax.axis_size(axis)
        numbers = []
        for shift in range(1, count):

            def other(shift=shift):
                return lax.rem(lax.axis_index(axis) + shift, count)

            number = moves.move(
                (axis, shift),
                lambda other=other: {axis: other()},
                source,
                lambda other=other: source_at(other()),
                target,
                lambda: (lax.axis_index(axis),),
                later=True,
            )
            moves.start(number)
            numbers.append(number)

        def own(ref):
            ref(target)[lax.axis_index(axis)] = ref(source)[source_at(lax.axis_index(axis))]

        moves.task(own)
        return numbers

    def to_members(source, target, cols):
        numbers = []
        for shift in range(1, members):
            number = moves.move(
                (PATCHES, members, shift),
                functools.partial(member_peer, members, shift),
                source,
                lambda shift=shift: (slice(None), columns(lax.rem(member() + shift, members), cols)),
                target,
                lambda shift=shift: (shift - 1,),
                later=True,
            )
            moves.start(number)
            numbers.append(number)
        return numbers

    def to_group(source, target, which):
        numbers = []
        for shift in range(1, MATRICES):
            number = moves.move(
                (PATCHES, seq_count, shift),
                functools.partial(group_peer, members, shift),
                source,
                None,
                target,
                lambda shift=shift: (shift - 1,),
                sends=lambda shift=shift: group() == (which - shift) % MATRICES,
                takes=lambda: group() == which,
                later=True,
            )
            moves.start(number)
            numbers.append(number)
        return numbers

    def over_rows(action):
        @pl.loop(0, block_rows // GRAM_COLS)
        def _(tile):
            action(pl.ds(pl.multiple_of(tile * GRAM_COLS, GRAM_COLS), GRAM_COLS))

    def weight_grad(lefts, rights, full, low=None):
        depth, cols = moves.shape(lefts[0])[2], moves.shape(rights[0])[2]
        tile_rows = GRAM_COLS if depth % GRAM_COLS == 0 else LANES

        def action(ref):
            @pl.loop(0, depth // tile_rows)
            def _(tile):
                at = pl.ds(pl.multiple_of(tile * tile_rows, tile_rows), tile_rows)
                value = jnp.zeros((tile_rows, cols), f32)
                for left, right in zip(lefts, rights):
                    left_rows = ref(left)[:, :, at].reshape(-1, tile_rows)
                    value = value + contract(left_rows, ref(right)[...].reshape(-1, cols), 0, 0)
                if full is not None:
                    ref(full)[at, :] = value
                if low is not None:
                    ref(low)[at, :] = value.astype(LOW)

        moves.task(action)

    qkv_all = moves.scratch((shards, rows, 3 * part), LOW)
    qkv_moves = moves.along(
        SHARDS,
        qkv_grad,
        qkv_all,
        [(lambda receiver: (slice(None), columns(receiver, 3 * part)), lambda sender: (sender,))],
    )
    qkv_local = len(moves.locals) - 1
    down_arriving = moves.scratch((members - 1, block_rows, group_cols[2]), LOW)
    down_moves = [
        moves.move(
            (PATCHES, members, shift),
            functools.partial(member_peer, members, shift),
            moves.operand(item),
            None,
            down_arriving,
            lambda shift=shift: (shift - 1,),
        )
        for shift, item in enumerate(down_leaving, 1)
    ]
    up_full, up_load = moves.load(up_mine)
    qkv_weights, qkv_load = moves.load(w_qkv)
    loaded = {
        name: [moves.load(steps[step]) for step in range(ROLL) if step in steps] for name, steps in gathered.items()
    }
    down_full, down_load = moves.load(down_mine)
    ada_weights, ada_load = moves.load(ada)

    def ready(*names):
        for name in names:
            for _, number in loaded[name]:
                moves.wait_local(number)
        return [[item for item, _ in loaded[name]] for name in names]

    up_low, down_low = [moves.scratch((block_rows, cols), LOW) for cols in group_cols[1:3]]
    group_target = moves.scratch((MATRICES - 1, block_rows, most_cols), LOW)

    def round_up_grad(ref):
        def action(at):
            ref(up_low)[at, :] = ref(up_full)[at, :].astype(LOW)

        over_rows(action)

    moves.wait_local(up_load)
    moves.task(round_up_grad)
    up_moves = to_group(up_low, group_target, 1)

    embed_low = moves.scratch((rows, width), LOW)
    table = moves.scratch((8, 6 * width), f32)

    def back(ref):
        grad = contract(ref(qkv_grad)[...], ref(qkv_weights)[...], 1, 1)
        normed, inverse = layer_norm(ref(embedded)[...])
        ref(table)[...] = jnp.zeros((8, 6 * width), f32)
        ref(table)[pl.ds(0, 1), pl.ds(0, width)] = jnp.sum(grad, 0, keepdims=True)
        ref(table)[pl.ds(0, 1), pl.ds(width, width)] = jnp.sum(grad * normed, 0, keepdims=True)
        grad = ref(grad_attn)[...] + norm_back(grad * (1.0 + mod_row(ref, mods, 1)), normed, inverse)
        ref(embed_low)[...] = grad.astype(LOW)
        bias_row = jnp.sum(grad, 0, keepdims=True) + mod_row(ref, rows_early, 6)
        for entry in range(4):
            cols = pl.ds((2 + entry) * width, width)
            ref(table)[pl.ds(0, 1), cols] = mod_row(ref, rows_early, entry)
            ref(table)[pl.ds(1, 1), cols] = mod_row(ref, rows_late, entry)
        for entry in range(2):
            ref(table)[pl.ds(1, 1), pl.ds(entry * width, width)] = mod_row(ref, rows_early, 4 + entry)
        for entry in range(shards):
            ref(table)[pl.ds(ROLL, 1), pl.ds(entry * ada_cols, part)] = bias_row[:, entry * part : (entry + 1) * part]

    moves.wait_local(qkv_load)
    moves.task(back)
    embed_all = moves.scratch((shards, rows, part), LOW)
    table_all = moves.scratch((shards, 8, ada_cols), f32)
    embed_moves = to_others(SHARDS, embed_low, lambda there: (slice(None), columns(there, part)), embed_all)
    table_moves = to_others(SHARDS, table, lambda there: (slice(None), columns(there, ada_cols)), table_all)

    out_cols, qkv_cols = group_cols[3], group_cols[0]
    out_full, out_low = moves.scratch((width, part), f32), moves.scratch((width, part), LOW)
    qkv_full, qkv_low = moves.scratch((width, 3 * part), f32), moves.scratch((width, 3 * part), LOW)
    out_arriving = moves.scratch((members - 1, block_rows, out_cols), LOW)
    qkv_arriving = moves.scratch((members - 1, block_rows, qkv_cols), LOW)
    padded = moves.shape(loaded["state"][0][0])[2]
    io_low = moves.scratch((2 * padded, part), LOW)
    io_grads = [moves.scratch((padded, part), f32) for _ in range(2)]
    weight_grad(*ready("mixed", "attn"), out_full, out_low)
    out_moves = to_members(out_low, out_arriving, out_cols)
    weight_grad(*ready("delta", "c"), io_grads[1])
    await_all(qkv_moves)
    moves.wait_local(qkv_local)
    (a_all, qkv_later) = ready("a", "qkv")
    weight_grad(a_all, [qkv_all, *qkv_later], qkv_full, qkv_low)
    qkv_member_moves = to_members(qkv_low, qkv_arriving, qkv_cols)
    await_all(embed_moves)
    (state_all, embed_later) = ready("state", "embed")
    weight_grad(state_all, [embed_all, *embed_later], io_grads[0])
    grad_pos = moves.output((rows, part), f32, pltpu.VMEM)
    io_rows = 2 * padded // seq_count

    def pos_and_io(ref):
        value = jnp.zeros((rows, part), f32)
        for item in (embed_all, *embed_later):
            for sample in range(shards):
                value = value + ref(item)[sample].astype(f32)
        ref(grad_pos)[...] = value
        for number, item in enumerate(io_grads):
            ref(io_low)[pl.ds(number * padded, padded), :] = ref(item)[...].astype(LOW)

    moves.task(pos_and_io)
    io_all = moves.scratch((seq_count, io_rows, part), LOW)
    io_moves = to_others(
        PATCHES, io_low, lambda there: (pl.ds(pl.multiple_of(there * io_rows, io_rows), io_rows),), io_all
    )

    flat, flat_all = moves.scratch((16, ada_cols), LOW), moves.scratch((seq_count, 16, ada_cols), LOW)

    def share(ref):
        pieces = [ref(table_all)[sample, pl.ds(0, ROLL), :] for sample in range(shards)]
        bias_row = sum(ref(table_all)[sample, pl.ds(ROLL, 1), :] for sample in range(shards))
        rest = jnp.zeros((16 - shards * ROLL - 1, ada_cols), f32)
        ref(flat)[...] = jnp.concatenate([*pieces, bias_row, rest], 0).astype(LOW)

    await_all(table_moves)
    moves.task(share)
    flat_moves = to_others(PATCHES, flat, lambda there: (slice(None), slice(None)), flat_all)

    def add_member(full, arriving, target, low, cols):
        def action(ref):
            def add(at):
                value = ref(full)[at, columns(member(), cols)] if target is not full else ref(full)[at, :]
                for shift in range(members - 1):
                    value = value + ref(arriving)[shift, at, :].astype(f32)
                ref(target)[at, :] = value
                if low is not None:
                    ref(low)[at, :] = value.astype(LOW)

            over_rows(add)

        moves.task(action)

    moves.wait_local(down_load)
    await_all(down_moves)
    add_member(down_full, down_arriving, down_full, down_low, group_cols[2])
    down_group_moves = to_group(down_low, group_target, 2)
    out_mine, out_mine_low = moves.scratch((width, out_cols), f32), moves.scratch((width, out_cols), LOW)
    out_target = moves.scratch((MATRICES - 1, block_rows, out_cols), LOW)
    await_all(out_moves)
    add_member(out_full, out_arriving, out_mine, out_mine_low, out_cols)
    out_group_moves = to_group(out_mine_low, out_target, 3)

    modul_all = moves.output((shards * ROLL, ada_cols), f32, pltpu.VMEM)
    tail_all = moves.output((shards, 16, ada_cols), f32, pltpu.VMEM)
    tail = moves.scratch((16, ada_cols), f32)

    def close(ref):
        value = jnp.zeros((16, ada_cols), f32)
        for item in range(seq_count):
            value = value + ref(flat_all)[item].astype(f32)
        modul = value[: shards * ROLL]
        ref(modul_all)[...] = modul
        high = modul.astype(LOW)
        rest = (modul - high.astype(f32)).astype(LOW)
        weights = ref(ada_weights)[...]
        ref(tail)[...] = jnp.zeros((16, ada_cols), f32)
        ref(tail)[pl.ds(0, shards * ROLL), pl.ds(0, width)] = contract(high, weights, 1, 1) + contract(
            rest, weights, 1, 1
        )
        ref(tail)[pl.ds(8, 1), :] = jnp.sum(modul, 0, keepdims=True)
        ref(tail)[pl.ds(9, 1), :] = value[shards * ROLL : shards * ROLL + 1]

    await_all(flat_moves)
    moves.wait_local(ada_load)
    moves.task(close)
    to_others(SHARDS, tail, lambda there: (slice(None), slice(None)), tail_all)

    def has_source():
        return group() < MATRICES - 1

    def is_source():
        return group() > 0

    chain = moves.scratch((width, qkv_cols), f32)
    chain_in, chain_out = [moves.scratch((width, qkv_cols), LOW) for _ in range(2)]
    await_all(qkv_member_moves)
    add_member(qkv_full, qkv_arriving, chain, None, qkv_cols)
    chunk = block_rows // CHAIN_CHUNKS
    for number_of in range(CHAIN_CHUNKS):
        place = (pl.ds(number_of * chunk, chunk),)
        number = moves.move(
            (PATCHES, seq_count, MATRICES - 1),
            functools.partial(group_peer, members, MATRICES - 1),
            chain_out,
            lambda place=place: place,
            chain_in,
            lambda place=place: place,
            sends=is_source,
            takes=has_source,
            later=True,
        )

        def add(ref, place=place):
            def with_arriving():
                ref(chain)[place] += ref(chain_in)[place].astype(f32)

            pl.when(has_source())(with_arriving)
            ref(chain_out)[place] = ref(chain)[place].astype(LOW)

        moves.wait_for(number)
        moves.task(add)
        moves.start(number)

    io_slice = moves.output((io_rows, part), f32, pltpu.VMEM)

    def add_io(ref):
        value = jnp.zeros((io_rows, part), f32)
        for item in range(seq_count):
            value = value + ref(io_all)[item].astype(f32)
        ref(io_slice)[...] = value

    await_all(io_moves)
    moves.task(add_io)

    grad_group = moves.output((block_rows, most_cols), f32, pltpu.VMEM)

    def put(full, target, cols):
        def action(ref):
            def add(at):
                value = ref(full)[at, :]
                if target is not None:
                    for shift in range(MATRICES - 1):
                        value = value + ref(target)[shift, at, pl.ds(0, cols)].astype(f32)
                ref(grad_group)[at, pl.ds(0, cols)] = value
                if cols < most_cols:
                    ref(grad_group)[at, pl.ds(cols, most_cols - cols)] = jnp.zeros((GRAM_COLS, most_cols - cols), f32)

            over_rows(add)

        return action

    def settle(ref):
        entries = ((chain, None), (up_full, group_target), (down_full, group_target), (out_mine, out_target))
        for which, (full, target) in enumerate(entries):
            pl.when(group() == which)(functools.partial(put(full, target, group_cols[which]), ref))

    await_all((*up_moves, *down_group_moves, *out_group_moves))
    moves.task(settle)
    return moves.run()


def newton_schulz(source, gram, poly, once, gram_low, poly_low, once_low, block, block_next):
    size = gram.shape[0]
    eye = jnp.equal(
        lax.broadcasted_iota(jnp.int32, (GRAM_COLS, GRAM_COLS), 0),
        lax.broadcasted_iota(jnp.int32, (GRAM_COLS, GRAM_COLS), 1),
    ).astype(jnp.float32)

    tiles = size // GRAM_COLS

    def tile_at(tile):
        return pl.ds(tile * GRAM_COLS, GRAM_COLS)

    def store(full, low, tile, value, mean, excess):
        cols = tile_at(tile)
        if tile:
            above = pl.ds(0, tile * GRAM_COLS)
            full[above, cols] = value[: tile * GRAM_COLS]
            low[above, cols] = value[: tile * GRAM_COLS].astype(LOW)
            for row in range(tile):
                low[cols, tile_at(row)] = value[row * GRAM_COLS : (row + 1) * GRAM_COLS].T.astype(LOW)
        corner = value[tile * GRAM_COLS :] - excess * eye
        full[cols, cols] = corner
        low[cols, cols] = (corner - mean * eye).astype(LOW)

    def inner(tile, left, right):
        both = left * right
        return 2.0 * jnp.sum(both) - jnp.sum(both[tile * GRAM_COLS :])

    def product_cols(left, right, tile):
        return contract(left[pl.ds(0, (tile + 1) * GRAM_COLS), :], right[:, tile_at(tile)], 1, 0)

    def upper(full, tile):
        return full[pl.ds(0, (tile + 1) * GRAM_COLS), tile_at(tile)]

    def advance(gram_mean, gram_squares, last):
        poly_mean = NS_B * gram_mean + NS_C * gram_squares / size
        total = jnp.float32(0.0)
        for tile in range(tiles):
            own = upper(gram, tile)
            value = product_cols(gram_low, gram_low, tile)
            value = NS_C * value + (NS_B + 2.0 * NS_C * gram_mean) * own
            store(poly, poly_low, tile, value, poly_mean, NS_C * gram_mean * gram_mean)
            total = total + inner(tile, value, own)
        once_mean = total / size - NS_C * gram_mean * gram_mean * gram_mean

        for tile in range(block.shape[1] // GRAM_COLS):
            cols = tile_at(tile)
            value = contract(poly_low[...], block[:, cols], 1, 0)
            block_next[:, cols] = (value + (NS_A + poly_mean) * block[:, cols].astype(jnp.float32)).astype(LOW)
        block[...] = block_next[...]
        if last:
            return None

        total = jnp.float32(0.0)
        for tile in range(tiles):
            own = upper(poly, tile)
            value = product_cols(poly_low, gram_low, tile)
            value = value + poly_mean * upper(gram, tile) + gram_mean * own
            store(once, once_low, tile, value, once_mean, poly_mean * gram_mean)
            total = total + inner(tile, value, own)
        poly_once = total / size - poly_mean * gram_mean * poly_mean
        mean_next = NS_A * NS_A * gram_mean + 2.0 * NS_A * once_mean + poly_once
        excess = poly_mean * once_mean

        total = jnp.float32(0.0)
        for tile in range(tiles):
            value = product_cols(poly_low, once_low, tile)
            value = value + (2.0 * NS_A + poly_mean) * upper(once, tile) + once_mean * upper(poly, tile)
            value = value + NS_A * NS_A * upper(gram, tile)
            store(gram, gram_low, tile, value, mean_next, excess)
            total = total + inner(tile, value, value)
        return mean_next, total - excess * (2.0 * mean_next + excess) * size

    block[...] = source[...]
    mean = jnp.float32(0.0)
    for tile in range(tiles):
        mean = mean + jnp.sum(gram[tile_at(tile), tile_at(tile)] * eye)
    mean = mean / size
    squares = jnp.float32(0.0)
    for tile in range(tiles):
        cols = tile_at(tile)
        value = gram[:, cols]
        gram_low[:, cols] = value.astype(LOW)
        gram_low[cols, cols] = (gram[cols, cols] - mean * eye).astype(LOW)
        squares = squares + jnp.sum(value * value)
    state = lax.fori_loop(0, NS_ITERS - 1, lambda turn, state: advance(*state, False), (mean, squares))
    advance(*state, True)


def fast_body(
    states,
    targets,
    lengths,
    intervals,
    qkv_copy,
    qkv_master,
    qkv_moment,
    out_copy,
    out_master,
    out_moment,
    up_copy,
    up_master,
    up_moment,
    down_copy,
    down_master,
    down_moment,
    ada_copy,
    ada_master,
    ada_first,
    ada_second,
    io_proj,
    io_first,
    io_second,
    cond_table,
    cond_first,
    cond_second,
    pos_table,
    pos_first,
    pos_second,
    biases,
    bias_first,
    bias_second,
):
    ids = {}
    f32 = jnp.float32
    seq_count, shards = lax.axis_size(PATCHES), lax.axis_size(SHARDS)
    seq_index, shard = lax.axis_index(PATCHES), lax.axis_index(SHARDS)
    members = seq_count // MATRICES
    group, member = seq_index // members, lax.rem(seq_index, members)
    samples, local, values_count = states.shape
    table_rows, table_cols = cond_table.shape
    width = table_cols * shards
    ada_cols = ada_copy.shape[1]
    padded = round_up(values_count, LANES)

    value_pad = ((0, 0), (0, padded - values_count))
    state = jnp.pad(states[0].astype(f32), value_pad)
    length = lengths[0]
    id_rows = jnp.broadcast_to(intervals[:, None, None], (shards, ROLL, LANES)).reshape(-1, LANES)
    (
        extras,
        cond_vec,
        silu_low,
        embedded,
        normed_a,
        state_low,
        qkv_rows,
        io_all,
        w_out,
        w_qkv,
        pos,
    ) = begin_step(
        ids,
        members,
        state,
        id_rows,
        jnp.broadcast_to((jnp.arange(ROLL, dtype=jnp.int32)[:, None] < length).astype(f32), (ROLL, width)),
        cond_table,
        biases[None],
        pos_table.astype(LOW),
        ada_copy,
        jnp.pad(io_proj.astype(LOW), ((0, 0), (0, padded - values_count), (0, 0))),
        out_copy,
        qkv_copy,
    )
    io_all = io_all.reshape(2, padded, width)
    masters = (qkv_master, up_master, down_master, out_master)
    momenta = (qkv_moment, up_moment, down_moment, out_moment)
    group_cols = [item.shape[1] // members for item in momenta]
    most_cols = max(group_cols)

    def widen(item):
        return jnp.pad(item, ((0, 0), (0, most_cols - item.shape[1])))

    moment_parts = jnp.stack(
        [
            widen(item[:, part * cols : (part + 1) * cols].astype(LOW))
            for item, cols in zip(momenta, group_cols)
            for part in range(members)
        ]
    )
    half_rows = moment_parts.shape[1] // 2

    counts = jnp.sum((intervals[:, None] == jnp.arange(NI, dtype=jnp.int32)[None]).astype(f32), 0)
    my_id = lax.dynamic_slice_in_dim(intervals, shard, 1)
    id_count = jnp.sum((my_id == jnp.arange(NI, dtype=jnp.int32)).astype(f32) * counts)
    weight = 1.0 / (NI * local * seq_count * values_count * id_count)
    kept = []
    gathered = {}
    moment_halves = []

    for step in range(ROLL):
        moves = Moves(f"attend{step}", ids, 48 * 2**20)
        qkv_out = moves.output((3, local * seq_count, width // seq_count), LOW, pltpu.VMEM)
        mixed_out = moves.output((local, width), LOW, pltpu.VMEM)
        arrivals = moves.rows_to_heads(PATCHES, qkv_rows, 3, qkv_out)
        waiting = moves.gather_pairs(normed_a, hold=True)
        waiting += moves.gather_pairs(state_low, hold=True)
        if step:
            waiting += moves.gather_pairs(kept[-1][2], hold=True)
        add_attention(moves, qkv_out, mixed_out, arrivals, local, members, waiting)
        qkv, mixed, gathered_a, gathered_state, *gathered_mixed = moves.run()
        gathered.setdefault("a", {})[step] = gathered_a
        gathered.setdefault("state", {})[step] = gathered_state
        if step:
            gathered["mixed"] = {step - 1: gathered_mixed[0]}
        *results, moment_half = feed_forward(
            ids,
            step,
            extras[step],
            extras[step + 1] if step + 1 < ROLL else None,
            mixed,
            embedded,
            state,
            pos,
            w_out,
            up_copy,
            down_copy,
            io_all,
            w_qkv,
            moment_parts[:, step * half_rows : (step + 1) * half_rows],
        )
        moment_halves.append(moment_half)
        attended, after_attn, downward, after_mlp, normed_c, state, tokens_b, upward, hidden, *following = results
        kept.append(
            (embedded, qkv, mixed, (attended, after_attn, downward, after_mlp, upward), normed_c, tokens_b, hidden)
        )
        if following:
            embedded, normed_a, state_low, qkv_rows = following

    lat = latitude_weights(local)
    diff = state - jnp.pad(targets[0].astype(f32), value_pad)
    loss_local = weight * jnp.sum(jnp.sum(diff * diff, -1) * lat)
    grad_state = 2.0 * weight * lat[:, None] * diff

    mlp_back = []

    def patch_sum(item, cols):
        mine = lax.dynamic_slice_in_dim(item, member * cols, cols, 1)
        low = item.astype(LOW)
        for shift in range(1, members):
            pairs = [
                (index, index // members * members + (index + shift) % members) for index in range(seq_count)
            ]
            to_member = lax.rem(member + shift, members)
            outgoing = lax.dynamic_slice_in_dim(low, to_member * cols, cols, 1)
            mine = mine + lax.ppermute(outgoing, PATCHES, pairs).astype(f32)
        return mine

    later, mods_later = None, None
    vector_rows = [None] * ROLL

    for step in reversed(range(ROLL)):
        embedded, qkv, mixed, for_feed, normed_c, tokens_b, hidden = kept[step]
        embed_grad, vectors, grad_state, delta_grad, grad_attn, attn_grad, mixed_grad, tokens_down, up_grad = feed_back(
            ids,
            step,
            extras[step],
            mods_later,
            later,
            grad_state,
            for_feed,
            w_out,
            up_copy,
            down_copy,
            io_all,
            w_qkv,
        )
        vector_rows[step] = vectors
        mlp_back.append((tokens_b, up_grad, tokens_down, hidden))
        if step == 0:
            up_total, down_total = [
                sum(rows_product(items[left], items[right]) for items in mlp_back) for left, right in ((0, 1), (2, 3))
            ]
            up_mine = patch_sum(up_total, group_cols[1])
            down_mine = lax.dynamic_slice_in_dim(down_total, member * group_cols[2], group_cols[2], 1)
            down_leaving = [
                lax.dynamic_slice_in_dim(
                    down_total, lax.rem(member + shift, members) * group_cols[2], group_cols[2], 1
                ).astype(LOW)
                for shift in range(1, members)
            ]
        moves = Moves(f"attend_back{step}", ids, 48 * 2**20)
        grads_in = moves.scratch((1, local * seq_count, width // seq_count), LOW)
        result = moves.output((local, 3 * width), LOW, pltpu.VMEM)
        arrivals = moves.rows_to_heads(PATCHES, mixed_grad, 1, grads_in)
        names = ["attn", "c", "delta"]
        moves.exchange_columns(SHARDS, attn_grad)
        moves.exchange_columns(SHARDS, normed_c)
        waiting = moves.gather_pairs(delta_grad, hold=True)
        if step == ROLL - 1:
            waiting += moves.gather_pairs(mixed, hold=True)
            names.append("mixed")
        else:
            moves.exchange_columns(SHARDS, later[0])
            moves.exchange_columns(SHARDS, embed_grad)
            names += ["qkv", "embed"]
        add_attention_back(
            moves, moves.operand(qkv, pltpu.VMEM), grads_in, result, arrivals, local, members, waiting
        )
        qkv_grad, *others = moves.run()
        for name, item in zip(names, others):
            gathered.setdefault(name, {})[step + (name in ("qkv", "embed"))] = item
        later, mods_later = (qkv_grad, embedded, grad_attn), extras[step]

    block_rows = qkv_copy.shape[0]
    grad_pos, modul_all, tail_all, io_slice, grad_group = reduce_step(
        ids,
        members,
        group_cols,
        qkv_grad,
        embedded,
        grad_attn,
        extras[0],
        w_qkv,
        vector_rows[1],
        vector_rows[0],
        gathered,
        (up_mine, down_mine, down_leaving),
        ada_copy,
    )
    io_cols = io_slice.shape[1]
    moves = Moves("finish", ids, 60 * 2**20)
    vmem = functools.partial(moves.operand, space=pltpu.VMEM)
    vmem_out = functools.partial(moves.output, space=pltpu.VMEM)
    full, low = (block_rows, block_rows), (block_rows, most_cols)
    block_part = block_rows // seq_count
    grad_in, io_in, pos_in, modul_in, tail_in = [
        vmem(item) for item in (grad_group, io_slice, grad_pos, modul_all, tail_all)
    ]
    silu_in, cond_in, ids_in = vmem(silu_low), vmem(cond_vec), vmem(id_rows)
    loss_in = vmem(jnp.broadcast_to(loss_local, (1, LANES)))
    moment = moves.scratch((seq_count, block_part, most_cols), LOW)
    moment_loads = [
        moves.keep(
            moves.operand(item),
            None,
            moment,
            lambda half=half: (slice(None), pl.ds(half * half_rows, half_rows)),
        )
        for half, item in enumerate(moment_halves)
    ]
    master_loads = [moves.load(item) for item in masters]
    sums = vmem_out((8, LANES), f32)
    grad_ada = vmem_out((block_part, ada_cols), f32)
    grad_table_all = vmem_out((8, width), f32)
    io_all_parts = vmem_out((seq_count,) + io_slice.shape, LOW)
    fresh = [vmem_out(item.shape, f32) for item in masters]
    fresh_low = [moves.scratch(item.shape, LOW) for item in masters]
    near, far = [moves.scratch((count, 8, LANES), f32) for count in (shards, seq_count)]
    grad_low, source = moves.scratch(low, LOW), moves.scratch(low, LOW)
    io_low = moves.scratch(io_slice.shape, LOW)

    def measure(ref):
        def add(item, totals):
            rows = pl.ds(pl.multiple_of(item * block_part, block_part), block_part)
            old, grad = ref(moment)[item].astype(f32), ref(grad_in)[rows, :]
            ref(grad_low)[rows, :] = grad.astype(LOW)
            return totals[0] + jnp.sum(old * old), totals[1] + jnp.sum(old * grad), totals[2] + jnp.sum(grad * grad)

        zero = jnp.float32(0.0)
        terms = lax.fori_loop(0, seq_count, add, (zero, zero, zero))
        patch = lax.axis_index(PATCHES)
        count = shards * ROLL
        silu_rows = ref(silu_in)[:, pl.ds(pl.multiple_of(patch * block_part, LANES), block_part)]
        silu_rows = jnp.concatenate([silu_rows, jnp.zeros((16 - count, block_part), LOW)], 0)
        modul = jnp.concatenate([ref(modul_in)[...], jnp.zeros((16 - count, ada_cols), f32)], 0)
        modul_high = modul.astype(LOW)
        modul_rest = (modul - modul_high.astype(f32)).astype(LOW)
        value = contract(silu_rows, modul_high, 0, 0) + contract(silu_rows, modul_rest, 0, 0)
        ref(grad_ada)[...] = value
        squares = terms[2] + jnp.sum(value * value)
        squares = squares + jnp.sum(ref(io_in)[...] * ref(io_in)[...]) + jnp.sum(ref(pos_in)[...] * ref(pos_in)[...])
        ref(io_low)[...] = ref(io_in)[...].astype(LOW)
        cond = ref(cond_in)[...]
        gate = 1.0 / (1.0 + jnp.exp(-cond))
        grad_silu = sum(ref(tail_in)[item, pl.ds(0, count), pl.ds(0, width)] for item in range(shards))
        grad_cond = grad_silu * gate * (1.0 + cond * (1.0 - gate))
        row = lax.broadcasted_iota(jnp.int32, (count, 1), 0)
        ref(grad_table_all)[...] = jnp.zeros((8, width), f32)
        for entry in range(table_rows):
            chosen = (ref(ids_in)[:, :1] == entry) if entry < NI else (lax.rem(row, ROLL) == entry - NI)
            value = jnp.sum(jnp.where(chosen, grad_cond, 0.0), 0, keepdims=True)
            ref(grad_table_all)[pl.ds(entry, 1), :] = value
        me = lax.axis_index(SHARDS)
        value = ref(grad_table_all)[:, pl.ds(pl.multiple_of(me * table_cols, LANES), table_cols)]
        once = jnp.sum(value * value)
        for entry, cols in ((8, ada_cols), (9, table_cols)):
            value = ref(tail_in)[me, pl.ds(entry, 1), pl.ds(0, cols)]
            once = once + jnp.sum(value * value)
        squares = squares + jnp.where(patch == 0, once, 0.0)
        lane = lax.broadcasted_iota(jnp.int32, (8, LANES), 1)
        entries = jnp.where(lane == 0, squares, 0.0) + jnp.where(lane == 1, ref(loss_in)[...], 0.0)
        for number, term in enumerate(terms):
            entries = entries + jnp.where(lane == 2 + 3 * (patch // members) + number, term, 0.0)
        ref(near)[me] = entries

    for number in moment_loads:
        moves.wait_local(number)
    moves.task(measure)

    def spread(axis, buffer, at):
        count = lax.axis_size(axis)
        numbers = []
        for shift in range(1, count):
            numbers.append(
                moves.move(
                    (axis, shift),
                    lambda shift=shift: {axis: lax.rem(lax.axis_index(axis) + shift, count)},
                    buffer,
                    at,
                    io_all_parts if buffer is io_low else buffer,
                    lambda: (lax.axis_index(axis),),
                    later=True,
                )
            )
            moves.start(numbers[-1])
        return numbers

    def add_near(ref):
        ref(far)[lax.axis_index(PATCHES)] = jnp.sum(ref(near)[...], 0)

    def scale(ref):
        ref(sums)[...] = jnp.sum(ref(far)[...], 0)
        row = ref(sums)[pl.ds(0, 1), :]
        lane = lax.broadcasted_iota(jnp.int32, (1, LANES), 1)

        def entry(place):
            return jnp.sum(jnp.where(lane == place, row, 0.0), 1, keepdims=True)

        clip = jnp.minimum(1.0, CLIP_LIMIT / (jnp.sqrt(entry(0)) + 1e-06))
        place = 2 + 3 * (lax.axis_index(PATCHES) // members)
        size = MOMENTUM * MOMENTUM * entry(place) + 2.0 * MOMENTUM * clip * entry(place + 1)
        size = jnp.sqrt(jnp.maximum(size + clip * clip * entry(place + 2), 0.0))
        per_size = 1.0 / (size + 1e-07)

        @pl.loop(0, seq_count)
        def _(item):
            rows = pl.ds(pl.multiple_of(item * block_part, block_part), block_part)
            value = MOMENTUM * ref(moment)[item].astype(f32) + clip * ref(grad_in)[rows, :]
            ref(source)[rows, :] = (value * per_size).astype(LOW)

        ref(io_all_parts)[lax.axis_index(PATCHES)] = ref(io_low)[...]

    for number in spread(SHARDS, near, lambda: (lax.axis_index(SHARDS),)):
        moves.wait_for(number)
    moves.task(add_near)
    far_moves = spread(PATCHES, far, lambda: (lax.axis_index(PATCHES),))
    spread(PATCHES, io_low, None)
    for number in far_moves:
        moves.wait_for(number)
    moves.task(scale)

    update = moves.scratch((seq_count, block_part, most_cols), LOW)
    target = moves.scratch((members * shards,) + low, LOW)
    gram, poly, once = [moves.scratch(full, f32) for _ in range(3)]
    gram_low, poly_low, once_low = [moves.scratch(full, LOW) for _ in range(3)]
    state, state_next = [moves.scratch(low, LOW) for _ in range(2)]
    pairs = shards // 2

    def slot(back_member, back_pair, part=None):
        who_member = lax.rem(lax.rem(lax.axis_index(PATCHES), members) + members - back_member, members)
        who_shard = lax.rem(lax.axis_index(SHARDS) + shards - 2 * back_pair, shards)
        index = who_member * shards + who_shard
        return (index,) if part is None else (index, pl.ds(part * block_rows // 2, block_rows // 2))

    def add_gram(place):
        def action(ref):
            (index,) = place()

            @pl.loop(0, block_rows // GRAM_COLS)
            def _(tile):
                cols = pl.ds(pl.multiple_of(tile * GRAM_COLS, GRAM_COLS), GRAM_COLS)
                ref(gram)[:, cols] += contract(ref(target)[index], ref(target)[index, cols, :], 1, 1)

        return action

    def start_gram(ref):
        @pl.loop(0, block_rows // GRAM_COLS)
        def _(tile):
            cols = pl.ds(pl.multiple_of(tile * GRAM_COLS, GRAM_COLS), GRAM_COLS)
            ref(gram)[:, cols] = contract(ref(source)[...], ref(source)[cols, :], 1, 1)

    def pair_peer(shift):
        return {SHARDS: lax.rem(lax.axis_index(SHARDS) + 2 * shift, shards)}

    def row_part(shift):
        there = lax.rem(lax.axis_index(PATCHES) + shift, seq_count)
        size = block_rows // seq_count
        return (pl.ds(pl.multiple_of(there * size, size), size),)

    slot_own = functools.partial(slot, 0, 0)
    by_member = {
        shift: moves.move(
            (PATCHES, members, shift),
            functools.partial(member_peer, members, shift),
            source,
            None,
            target,
            slot_own,
            later=True,
        )
        for shift in range(1, members)
    }
    by_pair = {
        shift: moves.move(
            (SHARDS, 2 * shift), functools.partial(pair_peer, shift), source, None, target, slot_own, later=True
        )
        for shift in range(1, pairs)
    }
    from_sibling = [(moves.move((SHARDS,), sibling_peer, source, None, target, slot_own, later=True), slot_own)]
    for number in (*by_member.values(), *by_pair.values(), from_sibling[0][0]):
        moves.start(number)
    moves.task(start_gram)

    def sibling_place(place):
        def at():
            (index,) = place()
            return (index + 1 - 2 * lax.rem(index, 2),)

        return at

    def hand_on(place, arrivals):
        if len(arrivals) == 1:
            parts = [(place, arrivals[0])]
        else:
            parts = [(functools.partial(place, part), number) for part, number in enumerate(arrivals)]
        numbers = [
            moves.move((SHARDS,), sibling_peer, target, at, target, at, (number,)) for at, number in parts
        ]
        from_sibling.append((numbers, place))
        moves.task(add_gram(place))

    across = []
    for shift_member, first in by_member.items():
        for shift_pair, second in by_pair.items():
            top = functools.partial(slot, shift_member, 0, 0)
            bottom = functools.partial(slot, 0, shift_pair, 1)
            halves = [
                moves.move(
                    (SHARDS, 2 * shift_pair),
                    functools.partial(pair_peer, shift_pair),
                    target,
                    top,
                    target,
                    top,
                    (first,),
                ),
                moves.move(
                    (PATCHES, members, shift_member),
                    functools.partial(member_peer, members, shift_member),
                    target,
                    bottom,
                    target,
                    bottom,
                    (second,),
                ),
            ]
            across.append((functools.partial(slot, shift_member, shift_pair), halves))
    for shift, number in by_member.items():
        hand_on(functools.partial(slot, shift, 0), [number])
    for shift, number in by_pair.items():
        hand_on(functools.partial(slot, 0, shift), [number])
    moves.wait_for(from_sibling[0][0])
    moves.task(add_gram(sibling_place(slot_own)))
    for place, halves in across:
        hand_on(place, halves)
    for numbers, place in from_sibling[1:]:
        for number in numbers:
            moves.wait_for(number)
        moves.task(add_gram(sibling_place(place)))

    grad_rows = moves.output((seq_count, block_rows // seq_count, most_cols), LOW)
    for shift in range(1, seq_count):
        moves.start(
            moves.move(
                (PATCHES, shift),
                lambda shift=shift: {PATCHES: lax.rem(lax.axis_index(PATCHES) + shift, seq_count)},
                grad_low,
                lambda shift=shift: row_part(shift),
                grad_rows,
                lambda: (lax.axis_index(PATCHES),),
                later=True,
            )
        )
    moves.start_local(
        moves.keep(grad_low, lambda: row_part(0), grad_rows, lambda: (lax.axis_index(PATCHES),), True)
    )
    moves.task(
        lambda ref: newton_schulz(
            *[ref(item) for item in (source, gram, poly, once, gram_low, poly_low, once_low, state, state_next)]
        )
    )

    update_moves = []
    for shift in range(1, seq_count):
        update_moves.append(
            moves.move(
                (PATCHES, shift),
                lambda shift=shift: {PATCHES: lax.rem(lax.axis_index(PATCHES) + shift, seq_count)},
                state,
                functools.partial(row_part, shift),
                update,
                lambda: (lax.axis_index(PATCHES),),
                later=True,
            )
        )
        moves.start(update_moves[-1])

    def keep_rows(ref):
        ref(update)[lax.axis_index(PATCHES)] = ref(state)[row_part(0)]

    moves.task(keep_rows)

    def renew(ref):
        for which, (master, _) in enumerate(master_loads):
            cols = group_cols[which]
            rate = RATE_MUON * 0.2 * math.sqrt(masters[which].shape[1] * shards)
            for part in range(members):
                at = (slice(None), pl.ds(part * cols, cols))
                value = ref(update)[which * members + part, :, pl.ds(0, cols)].astype(f32)
                value = ref(master)[at] * (1.0 - RATE_MUON * DECAY_MUON) - rate * value
                ref(fresh[which])[at] = value
                ref(fresh_low[which])[at] = value.astype(LOW)

    for number in update_moves:
        moves.wait_for(number)
    for _, number in master_loads:
        moves.wait_local(number)
    moves.task(renew)

    rows = block_rows // seq_count

    def row_place(back_group):
        who = lax.axis_index(PATCHES) - back_group * members
        return (pl.ds(pl.multiple_of(who * rows, rows), rows),)

    def has_group(offset):
        place = lax.axis_index(PATCHES) // members + offset
        return jnp.logical_and(place >= 0, place < MATRICES)

    def member_copies(source, source_at, target, target_at, after, there):
        for shift in range(1, members):
            moves.move(
                (PATCHES, members, shift),
                functools.partial(member_peer, members, shift),
                source,
                source_at,
                target,
                target_at,
                after,
                there,
                there,
                later=True,
            )
            if not after:
                moves.start(len(moves.moves) - 1)

    places = []
    for item_from in fresh_low:
        item_to = moves.output((rows * seq_count, moves.shape(item_from)[1]), LOW)
        own = functools.partial(row_place, 0)
        moves.start_local(moves.keep(item_from, None, item_to, own, True))
        places.append((item_from, item_to, {}))

    def along_line(distance, way, source, target, numbers):
        both = lambda: jnp.logical_and(has_group(way), has_group(-distance * way))
        place = functools.partial(row_place, distance * way)
        numbers[way] = moves.move(
            (PATCHES, seq_count, way),
            functools.partial(group_peer, members, (MATRICES + way) % MATRICES),
            target if distance else source,
            place if distance else None,
            target,
            place,
            (numbers[way],) if distance else (),
            both,
            functools.partial(has_group, -(distance + 1) * way),
            later=True,
        )
        if not distance:
            moves.start(numbers[way])

    for item_from, item_to, numbers in places:
        for way in (1, -1):
            along_line(0, way, item_from, item_to, numbers)
    for item_from, item_to, numbers in places:
        member_copies(item_from, None, item_to, own, (), None)
    for distance in range(1, MATRICES):
        for item_from, item_to, numbers in places:
            for way in (1, -1):
                number = numbers[way]
                if distance < MATRICES - 1:
                    along_line(distance, way, item_from, item_to, numbers)
                place = functools.partial(row_place, distance * way)
                member_copies(
                    item_to, place, item_to, place, (number,), functools.partial(has_group, -distance * way)
                )
    sums, grad_ada, grad_table_all, io_slices, *rest = moves.run()
    fresh, grad_rows, copies = rest[:MATRICES], rest[MATRICES], rest[MATRICES + 1 :]
    sums = sums[0]
    grad_norm = jnp.sqrt(sums[0])
    loss_total = sums[1]
    clip = jnp.minimum(1.0, CLIP_LIMIT / (grad_norm + 1e-06))
    terms = sums[2 : 2 + 3 * MATRICES].reshape(MATRICES, 3)
    size_squares = MOMENTUM * MOMENTUM * terms[:, 0] + 2.0 * MOMENTUM * clip * terms[:, 1] + clip * clip * terms[:, 2]
    sizes = jnp.sqrt(jnp.maximum(size_squares, 0.0))
    moment_sizes = jnp.stack([sizes[which] for which in (0, 3, 1, 2)]) / CLIP_LIMIT
    moments = [
        MOMENTUM * old
        + clip
        * jnp.concatenate(
            [grad_rows[which * members + part, :, : group_cols[which]] for part in range(members)], -1
        ).astype(f32)
        for which, old in enumerate(momenta)
    ]
    grad_table = lax.dynamic_slice_in_dim(grad_table_all[:table_rows], shard * table_cols, table_cols, 1)
    grad_bias_all = jnp.concatenate([tail_all[:, 8].reshape(-1), tail_all[:, 9, :table_cols].reshape(-1)])
    grad_bias = lax.dynamic_slice_in_dim(grad_bias_all, shard * biases.shape[0], biases.shape[0])
    io_grad = io_slices.reshape(2, padded, io_cols)[:, :values_count].astype(f32)
    ada_res = adam_update(ada_master, ada_first, ada_second, clip * grad_ada, RATE_ADAM)
    io_res = adam_update(io_proj, io_first, io_second, clip * io_grad, RATE_ADAM)
    cond_res = adam_update(cond_table, cond_first, cond_second, clip * grad_table, RATE_TABLE)
    pos_res = adam_update(pos_table, pos_first, pos_second, clip * grad_pos, RATE_TABLE)
    bias_res = adam_update(biases, bias_first, bias_second, clip * grad_bias, RATE_ADAM)
    matrices = []
    for which in (0, 3, 1, 2):
        matrices += [fresh[which], moments[which], copies[which]]
    return (loss_total, grad_norm, moment_sizes, *matrices, *ada_res, *io_res, *cond_res, *pos_res, *bias_res)


def fits_fast(mesh):
    seq, shards = mesh.shape[PATCHES], mesh.shape[SHARDS]
    return HEADS % seq == 0 and (HEADS // seq * HEAD) % LANES == 0 and seq % MATRICES == 0 and shards % 2 == 0


def solution(mesh):
    body = fast_body if fits_fast(mesh) else general_body
    return jax.shard_map(
        body,
        mesh=mesh,
        in_specs=(
            P(SHARDS, PATCHES, None),
            P(SHARDS, PATCHES, None),
            P(SHARDS),
            P(),
            P(None, SHARDS),
            P(PATCHES, SHARDS),
            P(PATCHES, SHARDS),
            P(None, SHARDS),
            P(PATCHES, SHARDS),
            P(PATCHES, SHARDS),
            P(None, SHARDS),
            P(PATCHES, SHARDS),
            P(PATCHES, SHARDS),
            P(None, SHARDS),
            P(PATCHES, SHARDS),
            P(PATCHES, SHARDS),
            P(None, SHARDS),
            P(PATCHES, SHARDS),
            P(PATCHES, SHARDS),
            P(PATCHES, SHARDS),
            P(None, None, SHARDS),
            P(None, None, SHARDS),
            P(None, None, SHARDS),
            P(None, SHARDS),
            P(None, SHARDS),
            P(None, SHARDS),
            P(PATCHES, SHARDS),
            P(PATCHES, SHARDS),
            P(PATCHES, SHARDS),
            P(SHARDS),
            P(SHARDS),
            P(SHARDS),
        ),
        out_specs=(
            P(),
            P(),
            P(),
            P(PATCHES, SHARDS),
            P(PATCHES, SHARDS),
            P(None, SHARDS),
            P(PATCHES, SHARDS),
            P(PATCHES, SHARDS),
            P(None, SHARDS),
            P(PATCHES, SHARDS),
            P(PATCHES, SHARDS),
            P(None, SHARDS),
            P(PATCHES, SHARDS),
            P(PATCHES, SHARDS),
            P(None, SHARDS),
            P(PATCHES, SHARDS),
            P(PATCHES, SHARDS),
            P(PATCHES, SHARDS),
            P(None, None, SHARDS),
            P(None, None, SHARDS),
            P(None, None, SHARDS),
            P(None, SHARDS),
            P(None, SHARDS),
            P(None, SHARDS),
            P(PATCHES, SHARDS),
            P(PATCHES, SHARDS),
            P(PATCHES, SHARDS),
            P(SHARDS),
            P(SHARDS),
            P(SHARDS),
        ),
        check_vma=False,
    )
```

```python
import functools
import math

import jax
import jax.numpy as jnp
from jax import lax
from jax.experimental import pallas as pl
from jax.experimental.pallas import tpu as pltpu
from jax.sharding import PartitionSpec as P

PATCHES = "seq"
SHARDS = "fsdp"
HEADS = 16
HEAD = 64
NI = 3
ROLL = 2
NS_ITERS = 5
STEP_NUM = 10
LON = 32


EPS_NORM = 1e-06
NS_A = 3.4445
NS_B = -4.775
NS_C = 2.0315
MOMENTUM = 0.5
RATE_MUON = 0.15
DECAY_MUON = 0.1
RATE_ADAM = 0.05
RATE_TABLE = 0.5
DECAY_ADAM = 0.1
BETA_FIRST = 0.9
BETA_SECOND = 0.95
CLIP_LIMIT = 0.01
HIGHEST_PRECISION = lax.Precision.HIGHEST


def broadcast(block, axis, owner):
    block = jnp.where(lax.axis_index(axis) == owner, block, jnp.zeros_like(block))
    return lax.psum(block, axis)


def product(left, right):
    return jnp.dot(left, right, preferred_element_type=jnp.float32)


def dot_last(left, right):
    return lax.dot_general(
        left, right, (((left.ndim - 1,), (1,)), ((), ())), preferred_element_type=jnp.float32
    )


def rows_product(left, right):
    flat_left = left.reshape(-1, left.shape[-1])
    flat_right = right.reshape(-1, right.shape[-1])
    return lax.dot_general(
        flat_left, flat_right, (((0,), (0,)), ((), ())), preferred_element_type=jnp.float32
    )


def layer_norm(values):
    centred = values - jnp.mean(values, -1, keepdims=True)
    inverse = lax.rsqrt(jnp.mean(centred * centred, -1, keepdims=True) + EPS_NORM)
    return (centred * inverse, inverse)


def norm_back(grad, normed, inverse):
    return inverse * (
        grad
        - jnp.mean(grad, -1, keepdims=True)
        - normed * jnp.mean(grad * normed, -1, keepdims=True)
    )


def heads_view(values):
    return values.reshape(values.shape[0], values.shape[1], HEADS, HEAD)


def modulation(modul, width):
    return [modul[:, None, column * width : (column + 1) * width] for column in range(6)]


def latitude_weights(local):
    all_patches = local * lax.axis_size(PATCHES)
    band_row = (jnp.arange(all_patches, dtype=jnp.int32) // LON).astype(jnp.float32)
    latitude = (band_row + 0.5) * (math.pi / (all_patches // LON)) - math.pi / 2
    cosine = jnp.cos(latitude)
    weights = cosine / jnp.mean(cosine)
    return lax.dynamic_slice_in_dim(weights, lax.axis_index(PATCHES) * local, local)


def forward_step(weights, state, active, select):
    w_qkv, w_out, w_up, w_down, w_ada, io_all, table, pos, bias = weights
    width = w_out.shape[0]
    cond_vec = jnp.dot(select, table.astype(jnp.float32), precision=HIGHEST_PRECISION)
    silu_low = jax.nn.silu(cond_vec).astype(jnp.bfloat16)
    modul = product(silu_low, w_ada) + bias[: 6 * width].astype(jnp.float32)
    shift1, scale1, gate1, shift2, scale2, gate2 = modulation(modul, width)
    state_low = state.astype(jnp.bfloat16)
    embedded = (
        product(state_low, io_all[0])
        + bias[6 * width :].astype(jnp.float32)
        + pos.astype(jnp.float32)
    )
    normed_one, inverse_one = layer_norm(embedded)
    normed_a = (normed_one * (1.0 + scale1) + shift1).astype(jnp.bfloat16)
    qkv = product(normed_a, w_qkv).astype(jnp.bfloat16)
    queries = qkv[..., :width]
    keys, values = (
        lax.all_gather(qkv[..., width : 2 * width], PATCHES, axis=1, tiled=True),
        lax.all_gather(qkv[..., 2 * width :], PATCHES, axis=1, tiled=True),
    )
    scores = jnp.einsum(
        "sphd,snhd->shpn", heads_view(queries), heads_view(keys), preferred_element_type=jnp.float32
    ) * HEAD ** (-0.5)
    top_score = jnp.max(scores, -1, keepdims=True)
    expo = jnp.exp(scores - top_score)
    total_exp = jnp.sum(expo, -1, keepdims=True)
    log_total = top_score + jnp.log(total_exp)
    probs_low = (expo / total_exp).astype(jnp.bfloat16)
    mixed = jnp.einsum(
        "shpn,snhd->sphd", probs_low, heads_view(values), preferred_element_type=jnp.float32
    )
    mixed_low = mixed.reshape(queries.shape).astype(jnp.bfloat16)
    attended = product(mixed_low, w_out)
    after_attn = embedded + gate1 * attended
    normed_two, inverse_two = layer_norm(after_attn)
    normed_b = (normed_two * (1.0 + scale2) + shift2).astype(jnp.bfloat16)
    upward = product(normed_b, w_up)
    hidden = jax.nn.gelu(upward).astype(jnp.bfloat16)
    downward = dot_last(hidden, w_down)
    after_mlp = after_attn + gate2 * downward
    normed_three, inverse_three = layer_norm(after_mlp)
    normed_c = normed_three.astype(jnp.bfloat16)
    delta = dot_last(normed_c, io_all[1])
    kept = (
        cond_vec,
        silu_low,
        modul,
        state_low,
        normed_one,
        inverse_one,
        normed_a,
        queries,
        keys,
        values,
        log_total,
        mixed_low,
        attended,
        normed_two,
        inverse_two,
        normed_b,
        upward,
        hidden,
        downward,
        normed_three,
        inverse_three,
        normed_c,
    )
    return (state + active * delta, kept)


def backward_step(weights, kept, grad_state, active, select):
    w_qkv, w_out, w_up, w_down, w_ada, io_all, table, pos, bias = weights
    (
        cond_vec,
        silu_low,
        modul,
        state_low,
        normed_one,
        inverse_one,
        normed_a,
        queries,
        keys,
        values,
        log_total,
        mixed_low,
        attended,
        normed_two,
        inverse_two,
        normed_b,
        upward,
        hidden,
        downward,
        normed_three,
        inverse_three,
        normed_c,
    ) = kept
    width = w_out.shape[0]
    shift1, scale1, gate1, shift2, scale2, gate2 = modulation(modul, width)
    delta_grad = (active * grad_state).astype(jnp.bfloat16)
    grad_head = rows_product(delta_grad, normed_c)
    grad_mlp = norm_back(product(delta_grad, io_all[1]), normed_three, inverse_three)
    grad_gate2 = jnp.sum(grad_mlp * downward, 1)
    down_grad = (gate2 * grad_mlp).astype(jnp.bfloat16)
    grad_down = rows_product(down_grad, hidden)
    grad_hidden = product(down_grad, w_down)
    up_grad = jax.vjp(jax.nn.gelu, upward)[1](grad_hidden)[0].astype(jnp.bfloat16)
    grad_up = rows_product(normed_b, up_grad)
    grad_normed_b = dot_last(up_grad, w_up)
    grad_scale2 = jnp.sum(grad_normed_b * normed_two, 1)
    grad_shift2 = jnp.sum(grad_normed_b, 1)
    grad_attn = grad_mlp + norm_back(grad_normed_b * (1.0 + scale2), normed_two, inverse_two)
    grad_gate1 = jnp.sum(grad_attn * attended, 1)
    attn_grad = (gate1 * grad_attn).astype(jnp.bfloat16)
    grad_out = rows_product(mixed_low, attn_grad)
    mixed_grad = dot_last(attn_grad, w_out).astype(jnp.bfloat16)
    q_heads = heads_view(queries)
    k_heads = heads_view(keys)
    v_heads = heads_view(values)
    g_heads = heads_view(mixed_grad)
    scores = jnp.einsum(
        "sphd,snhd->shpn", q_heads, k_heads, preferred_element_type=jnp.float32
    ) * HEAD ** (-0.5)
    probs = jnp.exp(scores - log_total)
    probs_low = probs.astype(jnp.bfloat16)
    grad_probs = jnp.einsum("sphd,snhd->shpn", g_heads, v_heads, preferred_element_type=jnp.float32)
    score_grad = (
        HEAD ** (-0.5) * probs * (grad_probs - jnp.sum(grad_probs * probs, -1, keepdims=True))
    ).astype(jnp.bfloat16)
    grad_queries = jnp.einsum(
        "shpn,snhd->sphd", score_grad, k_heads, preferred_element_type=jnp.float32
    ).reshape(queries.shape)
    key_part = jnp.einsum(
        "shpn,sphd->snhd", score_grad, q_heads, preferred_element_type=jnp.float32
    ).reshape(keys.shape)
    value_part = jnp.einsum(
        "shpn,sphd->snhd", probs_low, g_heads, preferred_element_type=jnp.float32
    ).reshape(values.shape)
    grad_keys, grad_values = (
        lax.psum_scatter(key_part, PATCHES, scatter_dimension=1, tiled=True),
        lax.psum_scatter(value_part, PATCHES, scatter_dimension=1, tiled=True),
    )
    qkv_grad = jnp.concatenate([grad_queries, grad_keys, grad_values], -1).astype(jnp.bfloat16)
    grad_qkv = rows_product(normed_a, qkv_grad)
    grad_normed_a = dot_last(qkv_grad, w_qkv)
    grad_scale1 = jnp.sum(grad_normed_a * normed_one, 1)
    grad_shift1 = jnp.sum(grad_normed_a, 1)
    grad_embedded = grad_attn + norm_back(grad_normed_a * (1.0 + scale1), normed_one, inverse_one)
    embed_grad = grad_embedded.astype(jnp.bfloat16)
    grad_embed = rows_product(state_low, embed_grad)
    grad_prev = grad_state + dot_last(embed_grad, io_all[0])
    grad_modul = jnp.concatenate(
        [grad_shift1, grad_scale1, grad_gate1, grad_shift2, grad_scale2, grad_gate2], -1
    )
    grad_ada = lax.dot_general(
        silu_low.astype(jnp.float32),
        grad_modul,
        (((0,), (0,)), ((), ())),
        precision=HIGHEST_PRECISION,
    )
    grad_silu = lax.dot_general(
        grad_modul, w_ada.astype(jnp.float32), (((1,), (1,)), ((), ())), precision=HIGHEST_PRECISION
    )
    grad_cond = jax.vjp(jax.nn.silu, cond_vec)[1](grad_silu)[0]
    grad_table = lax.dot_general(
        select, grad_cond, (((0,), (0,)), ((), ())), precision=HIGHEST_PRECISION
    )
    grad_bias = jnp.concatenate([jnp.sum(grad_modul, 0), jnp.sum(grad_embedded, (0, 1))])
    grad_pos = jnp.sum(grad_embedded, 0)
    grads = (
        grad_qkv,
        grad_out,
        grad_up,
        grad_down,
        grad_ada,
        jnp.stack([grad_embed, grad_head]),
        grad_table,
        grad_pos,
        grad_bias,
    )
    return (grad_prev, grads)


def gram_part(block_cols):
    return lax.dot_general(
        block_cols, block_cols, (((1,), (1,)), ((), ())), preferred_element_type=jnp.float32
    )


def zero_gram(block_cols):
    return jnp.zeros((block_cols.shape[0], block_cols.shape[0]), jnp.float32)


def newton_step(block_cols, gram):
    gram_low = gram.astype(jnp.bfloat16)
    poly = (NS_B * gram_low.astype(jnp.float32) + NS_C * product(gram_low, gram_low)).astype(
        jnp.bfloat16
    )
    return (NS_A * block_cols.astype(jnp.float32) + product(poly, block_cols)).astype(jnp.bfloat16)


def keep_block(block_cols, gram):
    return block_cols


def adam_update(weight, first, second, grad, rate):
    first_new = BETA_FIRST * first + (1.0 - BETA_FIRST) * grad
    second_new = BETA_SECOND * second + (1.0 - BETA_SECOND) * grad * grad
    unbiased = first_new / (1.0 - BETA_FIRST**STEP_NUM)
    spread = jnp.sqrt(second_new / (1.0 - BETA_SECOND**STEP_NUM)) + 1e-08
    return (weight * (1.0 - rate * DECAY_ADAM) - rate * unbiased / spread, first_new, second_new)


def general_body(
    states,
    targets,
    lengths,
    intervals,
    qkv_copy,
    qkv_master,
    qkv_moment,
    out_copy,
    out_master,
    out_moment,
    up_copy,
    up_master,
    up_moment,
    down_copy,
    down_master,
    down_moment,
    ada_copy,
    ada_master,
    ada_first,
    ada_second,
    io_proj,
    io_first,
    io_second,
    cond_table,
    cond_first,
    cond_second,
    pos_table,
    pos_first,
    pos_second,
    biases,
    bias_first,
    bias_second,
):
    weights = (
        lax.all_gather(qkv_copy, SHARDS, axis=1, tiled=True),
        lax.all_gather(out_copy, SHARDS, axis=1, tiled=True),
        lax.all_gather(up_copy, SHARDS, axis=1, tiled=True),
        lax.all_gather(down_copy, SHARDS, axis=1, tiled=True),
        lax.all_gather(ada_copy, SHARDS, axis=1, tiled=True),
        lax.all_gather(io_proj.astype(jnp.bfloat16), SHARDS, axis=2, tiled=True),
        lax.all_gather(cond_table.astype(jnp.bfloat16), SHARDS, axis=1, tiled=True),
        lax.all_gather(pos_table.astype(jnp.bfloat16), SHARDS, axis=1, tiled=True),
        lax.all_gather(biases.astype(jnp.bfloat16), SHARDS, axis=0, tiled=True),
    )
    samples, local, values_count = states.shape
    table_rows = cond_table.shape[0]
    my_ids = lax.dynamic_slice_in_dim(intervals, lax.axis_index(SHARDS) * samples, samples)
    counts = jnp.sum(
        (intervals[:, None] == jnp.arange(NI, dtype=jnp.int32)[None]).astype(jnp.float32), 0
    )
    id_counts = jnp.sum(
        (my_ids[:, None] == jnp.arange(NI, dtype=jnp.int32)[None]).astype(jnp.float32)
        * counts[None],
        1,
    )
    weight = 1.0 / (NI * local * lax.axis_size(PATCHES) * values_count * id_counts)
    rows_iota = jnp.arange(table_rows, dtype=jnp.int32)
    id_select = (my_ids[:, None] == rows_iota[None]).astype(jnp.float32)
    state = states.astype(jnp.float32)
    seen_states = []
    kept_all = []
    for step in range(ROLL):
        select = id_select + (rows_iota == NI + step).astype(jnp.float32)[None]
        active = (step < lengths).astype(jnp.float32)[:, None, None]
        seen_states.append(state)
        state, kept = forward_step(weights, state, active, select)
        kept_all.append(kept)
    lat = latitude_weights(local)
    diff = state - targets.astype(jnp.float32)
    err = jnp.sum(jnp.sum(diff * diff, -1) * lat[None], -1)
    loss_local = jnp.sum(weight * err)
    grad_state = 2.0 * weight[:, None, None] * lat[None, :, None] * diff
    totals = None
    for step in reversed(range(ROLL)):
        select = id_select + (rows_iota == NI + step).astype(jnp.float32)[None]
        active = (step < lengths).astype(jnp.float32)[:, None, None]
        kept = kept_all[step]
        grad_state, grads = backward_step(weights, kept, grad_state, active, select)
        totals = grads if totals is None else jax.tree.map(jnp.add, totals, grads)
    reduced = (
        lax.psum_scatter(totals[0], SHARDS, scatter_dimension=1, tiled=True),
        lax.psum_scatter(totals[1], SHARDS, scatter_dimension=1, tiled=True),
        lax.psum_scatter(totals[2], SHARDS, scatter_dimension=1, tiled=True),
        lax.psum_scatter(totals[3], SHARDS, scatter_dimension=1, tiled=True),
        lax.psum_scatter(totals[4], SHARDS, scatter_dimension=1, tiled=True),
        lax.psum_scatter(totals[5], SHARDS, scatter_dimension=2, tiled=True),
        lax.psum_scatter(totals[6], SHARDS, scatter_dimension=1, tiled=True),
        lax.psum_scatter(totals[7], SHARDS, scatter_dimension=1, tiled=True),
        lax.psum_scatter(totals[8], SHARDS, scatter_dimension=0, tiled=True),
    )
    large = (
        lax.psum_scatter(reduced[0], PATCHES, scatter_dimension=0, tiled=True),
        lax.psum_scatter(reduced[1], PATCHES, scatter_dimension=0, tiled=True),
        lax.psum_scatter(reduced[2], PATCHES, scatter_dimension=0, tiled=True),
        lax.psum_scatter(reduced[3], PATCHES, scatter_dimension=0, tiled=True),
        lax.psum_scatter(reduced[4], PATCHES, scatter_dimension=0, tiled=True),
    )
    small = lax.psum((reduced[5], reduced[6], reduced[8]), PATCHES)
    grad_pos = reduced[7]
    first_copy = (lax.axis_index(PATCHES) == 0).astype(jnp.float32)
    squares = jnp.sum(grad_pos * grad_pos)
    for item in large:
        squares = squares + jnp.sum(item * item)
    small_squares = jnp.float32(0.0)
    for item in small:
        small_squares = small_squares + jnp.sum(item * item)
    squares, loss_total = lax.psum(
        (squares + first_copy * small_squares, loss_local), (PATCHES, SHARDS)
    )
    grad_norm = jnp.sqrt(squares)
    clip = jnp.minimum(1.0, CLIP_LIMIT / (grad_norm + 1e-06))
    masters = (qkv_master, out_master, up_master, down_master)
    moments = [
        MOMENTUM * old + clip * grad
        for old, grad in zip((qkv_moment, out_moment, up_moment, down_moment), large[:4])
    ]
    norms = lax.psum(
        (
            jnp.sum(moments[0] * moments[0]),
            jnp.sum(moments[1] * moments[1]),
            jnp.sum(moments[2] * moments[2]),
            jnp.sum(moments[3] * moments[3]),
        ),
        (PATCHES, SHARDS),
    )
    sizes = [jnp.sqrt(norms[which]) for which in range(4)]
    moment_sizes = jnp.stack(sizes) / CLIP_LIMIT
    scaled = [(moments[which] / (sizes[which] + 1e-07)).astype(jnp.bfloat16) for which in range(4)]
    columns = (
        lax.all_gather(scaled[0], PATCHES, axis=0, tiled=True),
        lax.all_gather(scaled[1], PATCHES, axis=0, tiled=True),
        lax.all_gather(scaled[2], PATCHES, axis=0, tiled=True),
        lax.all_gather(scaled[3], PATCHES, axis=0, tiled=True),
    )
    seq_index = lax.axis_index(PATCHES)
    seq_count = lax.axis_size(PATCHES)
    owners = [seq_index == which % seq_count for which in range(4)]
    blocks = list(columns)
    for turn in range(NS_ITERS):
        partial_value = [
            lax.cond(owners[which], gram_part, zero_gram, blocks[which]) for which in range(4)
        ]
        grams = lax.psum(
            (partial_value[0], partial_value[1], partial_value[2], partial_value[3]), SHARDS
        )
        blocks = [
            lax.cond(owners[which], newton_step, keep_block, blocks[which], grams[which])
            for which in range(4)
        ]
    blocks = [broadcast(blocks[which], PATCHES, which % seq_count) for which in range(4)]
    row_count = qkv_master.shape[0]
    fresh = []
    for which in range(4):
        my_rows = lax.dynamic_slice_in_dim(
            blocks[which], seq_index * row_count, row_count, 0
        ).astype(jnp.float32)
        all_cols = masters[which].shape[1] * lax.axis_size(SHARDS)
        fresh.append(
            masters[which] * (1.0 - RATE_MUON * DECAY_MUON)
            - RATE_MUON * 0.2 * math.sqrt(all_cols) * my_rows
        )
    copies = (
        lax.all_gather(fresh[0].astype(jnp.bfloat16), PATCHES, axis=0, tiled=True),
        lax.all_gather(fresh[1].astype(jnp.bfloat16), PATCHES, axis=0, tiled=True),
        lax.all_gather(fresh[2].astype(jnp.bfloat16), PATCHES, axis=0, tiled=True),
        lax.all_gather(fresh[3].astype(jnp.bfloat16), PATCHES, axis=0, tiled=True),
    )
    ada_res = adam_update(ada_master, ada_first, ada_second, clip * large[4], RATE_ADAM)
    io_res = adam_update(io_proj, io_first, io_second, clip * small[0], RATE_ADAM)
    cond_res = adam_update(cond_table, cond_first, cond_second, clip * small[1], RATE_TABLE)
    pos_res = adam_update(pos_table, pos_first, pos_second, clip * grad_pos, RATE_TABLE)
    bias_res = adam_update(biases, bias_first, bias_second, clip * small[2], RATE_ADAM)
    return (
        loss_total,
        grad_norm,
        moment_sizes,
        fresh[0],
        moments[0],
        copies[0],
        fresh[1],
        moments[1],
        copies[1],
        fresh[2],
        moments[2],
        copies[2],
        fresh[3],
        moments[3],
        copies[3],
        ada_res[0],
        ada_res[1],
        ada_res[2],
        io_res[0],
        io_res[1],
        io_res[2],
        cond_res[0],
        cond_res[1],
        cond_res[2],
        pos_res[0],
        pos_res[1],
        pos_res[2],
        bias_res[0],
        bias_res[1],
        bias_res[2],
    )


LANES = 128
MATRICES = 4
LOW = jnp.bfloat16
MESH = pl.DeviceIdType.MESH


def round_up(value, unit):
    return -(-value // unit) * unit


def member_peer(members, shift):
    index = lax.axis_index(PATCHES)
    return {PATCHES: index // members * members + lax.rem(lax.rem(index, members) + shift, members)}


def group_peer(members, shift):
    return {PATCHES: lax.rem(lax.axis_index(PATCHES) + shift * members, lax.axis_size(PATCHES))}


def sibling_peer():
    index = lax.axis_index(SHARDS)
    return {SHARDS: index + 1 - 2 * lax.rem(index, 2)}


def where(condition, action):
    if condition is None:
        action()
    else:
        pl.when(condition())(action)


class Moves:
    def __init__(self, name, ids, vmem=None):
        self.name = name
        self.ids = ids
        self.vmem = vmem
        self.operands = []
        self.operand_specs = []
        self.outputs = []
        self.output_specs = []
        self.scratches = []
        self.moves = []
        self.locals = []
        self.steps = []
        self.peers = {}

    def operand(self, array, space=pl.ANY):
        self.operands.append(array)
        self.operand_specs.append(pl.BlockSpec(memory_space=space))
        return (0, len(self.operands) - 1)

    def output(self, shape, dtype, space=pl.ANY):
        self.outputs.append(jax.ShapeDtypeStruct(shape, dtype))
        self.output_specs.append(pl.BlockSpec(memory_space=space))
        return (1, len(self.outputs) - 1)

    def scratch(self, shape, dtype):
        self.scratches.append(pltpu.VMEM(shape, dtype))
        return (2, len(self.scratches) - 1)

    def keep(self, source, source_at, target, target_at, later=False):
        self.locals.append((source, source_at, target, target_at, later))
        return len(self.locals) - 1

    def shape(self, scratch):
        return self.scratches[scratch[1]].shape

    def load(self, array):
        target = self.scratch(array.shape, array.dtype)
        return target, self.keep(self.operand(array), None, target, None)

    def save(self, source, shape, dtype):
        number = self.keep(source, None, self.output(shape, dtype), None, True)
        return number

    def start_local(self, number):
        self.steps.append((self.begin_local, number))

    def begin_local(self, number):
        self.local[number].start()

    def move(
        self, peer_key, peer, source, source_at, target, target_at, after=(), sends=None, takes=None, later=False
    ):
        number = len(self.moves)
        self.peers.setdefault(peer_key, peer)
        self.moves.append((peer_key, source, source_at, target, target_at, sends, takes, later or bool(after)))
        for earlier in after:
            self.steps.append((self.await_move, earlier))
        if after:
            self.steps.append((self.start_move, number))
        return number

    def wait_for(self, number):
        self.steps.append((self.await_move, number))

    def start(self, number):
        self.steps.append((self.start_move, number))

    def wait_local(self, number):
        self.steps.append((self.await_local, number))

    def task(self, action):
        self.steps.append((self.do_task, action))

    def await_move(self, number):
        if number not in self.arrived:
            self.arrived.add(number)
            where(self.moves[number][6], self.remote[number].wait_recv)

    def start_move(self, number):
        where(self.moves[number][5], self.remote[number].start)

    def await_local(self, number):
        if number not in self.kept:
            self.kept.add(number)
            self.local[number].wait()

    def do_task(self, action):
        action(self.ref)

    def ref(self, which):
        return self.refs[which[0]][which[1]]

    def view(self, which, index):
        ref = self.ref(which)
        return ref.at[index()] if index is not None else ref

    def kernel(self, *refs):
        sizes = (len(self.operands), len(self.outputs), len(self.scratches))
        self.refs = (refs[: sizes[0]], refs[sizes[0] : sizes[0] + sizes[1]], refs[sizes[0] + sizes[1] : sum(sizes)])
        local_sem, send_sem, recv_sem = refs[sum(sizes) :]
        self.arrived, self.kept = set(), set()
        devices = {key: peer() for key, peer in self.peers.items()}
        barrier = pltpu.get_barrier_semaphore()
        for device in devices.values():
            pl.semaphore_signal(barrier, inc=1, device_id=device, device_id_type=MESH)
        pl.semaphore_wait(barrier, len(devices))
        self.remote = []
        for number, (key, source, source_at, target, target_at, _, _, later) in enumerate(self.moves):
            self.remote.append(
                pltpu.make_async_remote_copy(
                    src_ref=self.view(source, source_at),
                    dst_ref=self.view(target, target_at),
                    send_sem=send_sem.at[number],
                    recv_sem=recv_sem.at[number],
                    device_id=devices[key],
                    device_id_type=MESH,
                )
            )
            if not later:
                self.start_move(number)
        self.local = [
            pltpu.make_async_copy(self.view(source, source_at), self.view(target, target_at), local_sem.at[number])
            for number, (source, source_at, target, target_at, _) in enumerate(self.locals)
        ]
        for copy, entry in zip(self.local, self.locals):
            if not entry[4]:
                copy.start()
        for action, number in self.steps:
            action(number)
        for number in range(len(self.locals)):
            self.await_local(number)
        for number, copy in enumerate(self.remote):
            self.await_move(number)
            where(self.moves[number][5], copy.wait_send)

    def run(self):
        return pl.pallas_call(
            self.kernel,
            out_shape=self.outputs,
            in_specs=self.operand_specs,
            out_specs=self.output_specs,
            scratch_shapes=[
                *self.scratches,
                pltpu.SemaphoreType.DMA((max(1, len(self.locals)),)),
                pltpu.SemaphoreType.DMA((len(self.moves),)),
                pltpu.SemaphoreType.DMA((len(self.moves),)),
            ],
            compiler_params=pltpu.CompilerParams(
                collective_id=self.ids.setdefault(self.name, len(self.ids)),
                has_side_effects=True,
                vmem_limit_bytes=self.vmem,
            ),
            name=self.name,
        )(*self.operands)

    def along(self, axis, source, target, pairs, later=False):
        numbers = []
        count = lax.axis_size(axis)

        def other(shift):
            return lax.rem(lax.axis_index(axis) + shift, count)

        for shift in range(1, count):
            for source_at, target_at in pairs:
                numbers.append(
                    self.move(
                        (axis, shift),
                        lambda shift=shift: {axis: other(shift)},
                        source,
                        None if source_at is None else (lambda at=source_at, shift=shift: at(other(shift))),
                        target,
                        lambda at=target_at: at(lax.axis_index(axis)),
                        later=later,
                    )
                )
        for source_at, target_at in pairs:
            local = self.keep(
                source,
                None if source_at is None else (lambda at=source_at: at(lax.axis_index(axis))),
                target,
                lambda at=target_at: at(lax.axis_index(axis)),
                later,
            )
            if later:
                self.start_local(local)
        if later:
            for number in numbers:
                self.start(number)
        return numbers

    def gather(self, axis, array):
        target = self.output((lax.axis_size(axis),) + array.shape, array.dtype)
        self.along(axis, self.operand(array), target, [(None, lambda sender: (sender,))])

    def gather_pairs(self, array, parts=1, hold=False):
        shards = lax.axis_size(SHARDS)
        source = self.operand(array)
        target = self.output((shards,) + array.shape, array.dtype)
        rows = array.shape[0] // parts

        def place(back_pair, part):
            return (lax.rem(lax.axis_index(SHARDS) + shards - 2 * back_pair, shards), pl.ds(part * rows, rows))

        firsts = []
        for part in range(parts):
            for pair in range(1, shards // 2):
                number = self.move(
                    (SHARDS, 2 * pair),
                    lambda pair=pair: {SHARDS: lax.rem(lax.axis_index(SHARDS) + 2 * pair, shards)},
                    source,
                    lambda part=part: (pl.ds(part * rows, rows),),
                    target,
                    functools.partial(place, 0, part),
                )
                firsts.append((functools.partial(place, pair, part), number))
        own = lambda: (lax.axis_index(SHARDS),)
        self.move((SHARDS,), sibling_peer, source, None, target, own)
        self.keep(source, None, target, own)
        waiting = [(target, at, number) for at, number in firsts]
        if hold:
            return waiting
        self.to_sibling(waiting)

    def gather_columns(self, axis, array, target):
        width = array.shape[-1]
        lead = (slice(None),) * (array.ndim - 1)
        numbers = self.along(
            axis,
            self.operand(array),
            target,
            [(None, lambda sender: lead + (pl.ds(pl.multiple_of(sender * width, LANES), width),))],
        )
        return numbers, len(self.locals) - 1

    def gather_twice(self, arrays, members, chunks):
        shards = lax.axis_size(SHARDS)
        entries = []
        for array, pieces in zip(arrays, chunks):
            source = self.operand(array)
            width = array.shape[1]
            target = self.scratch((array.shape[0], shards * width), array.dtype)
            rows = array.shape[0] // members // pieces

            def columns(back_pair, width=width):
                who = lax.rem(lax.axis_index(SHARDS) + shards - 2 * back_pair, shards)
                return pl.ds(pl.multiple_of(who * width, LANES), width)

            def piece_rows(back_member, piece, rows=rows, pieces=pieces):
                index = lax.rem(lax.rem(lax.axis_index(PATCHES), members) + members - back_member, members)
                return pl.ds(pl.multiple_of((index * pieces + piece) * rows, rows), rows)

            def place(back_member, back_pair, piece, columns=columns, piece_rows=piece_rows):
                return (piece_rows(back_member, piece), columns(back_pair))

            def mine(piece, piece_rows=piece_rows):
                return (piece_rows(0, piece),)

            def whole(columns=columns):
                return (slice(None), columns(0))

            firsts = [
                (
                    pair,
                    piece,
                    self.move(
                        (SHARDS, 2 * pair),
                        lambda pair=pair: {SHARDS: lax.rem(lax.axis_index(SHARDS) + 2 * pair, shards)},
                        source,
                        functools.partial(mine, piece),
                        target,
                        functools.partial(place, 0, 0, piece),
                    ),
                )
                for piece in range(pieces)
                for pair in range(1, shards // 2)
            ]
            near = self.move((SHARDS,), sibling_peer, source, None, target, whole)
            local = self.keep(source, None, target, whole)
            entries.append((target, place, firsts, [near, *[number for _, _, number in firsts]], local))
        last = []
        for target, place, firsts, numbers, _ in entries:
            for pair, piece, first in firsts:
                near = functools.partial(place, 0, pair, piece)
                for shift in range(1, members):
                    number = self.move(
                        (PATCHES, members, shift),
                        functools.partial(member_peer, members, shift),
                        target,
                        near,
                        target,
                        near,
                        (first,),
                    )
                    last.append((target, functools.partial(place, shift, pair, piece), number, numbers))
                numbers.append(self.move((SHARDS,), sibling_peer, target, near, target, near, (first,)))
        for target, at, number, numbers in last:
            numbers += [number, self.move((SHARDS,), sibling_peer, target, at, target, at, (number,))]
        return [(target, numbers, local) for target, _, _, numbers, local in entries]

    def to_sibling(self, waiting):
        for target, place, number in waiting:
            self.move((SHARDS,), sibling_peer, target, place, target, place, (number,))

    def exchange(self, axis, array, later=False):
        target = self.output(array.shape, array.dtype)
        return self.along(
            axis, self.operand(array), target, [(lambda receiver: (receiver,), lambda sender: (sender,))], later
        )

    def exchange_columns(self, axis, array):
        width = array.shape[-1] // lax.axis_size(axis)
        target = self.output((lax.axis_size(axis), array.shape[0], width), array.dtype)
        self.along(
            axis,
            self.operand(array),
            target,
            [
                (
                    lambda receiver: (slice(None), pl.ds(pl.multiple_of(receiver * width, LANES), width)),
                    lambda sender: (sender,),
                )
            ],
        )

    def rows_to_heads(self, axis, array, planes, target):
        count, rows = lax.axis_size(axis), array.shape[0]
        columns = array.shape[1] // planes
        width = columns // count
        return self.along(
            axis,
            self.operand(array),
            target,
            [
                (
                    lambda receiver, plane=plane: (
                        slice(None),
                        pl.ds(pl.multiple_of(plane * columns + receiver * width, LANES), width),
                    ),
                    lambda sender, plane=plane: (plane, pl.ds(pl.multiple_of(sender * rows, rows), rows)),
                )
                for plane in range(planes)
            ],
        )

    def head_rows(self, source, target, planes, rows, columns, members, back_group):
        count = lax.axis_size(PATCHES)
        width = columns // count
        for shift_member in range(members):
            for plane in planes:

                def peer(shift_member=shift_member):
                    index = lax.axis_index(PATCHES)
                    there = lax.rem(index // members + back_group, MATRICES) * members
                    return there + lax.rem(lax.rem(index, members) + shift_member, members)

                def source_at(peer=peer, plane=plane):
                    return (plane, pl.ds(pl.multiple_of(peer() * rows, rows), rows))

                def target_at(plane=plane):
                    start = plane * columns + lax.axis_index(PATCHES) * width
                    return (slice(None), pl.ds(pl.multiple_of(start, LANES), width))

                if shift_member or back_group:
                    self.start(
                        self.move(
                            (PATCHES, count, back_group, shift_member),
                            lambda peer=peer: {PATCHES: peer()},
                            source,
                            source_at,
                            target,
                            target_at,
                            later=True,
                        )
                    )
                else:

                    def own(ref, source_at=source_at, target_at=target_at):
                        ref(target)[target_at()] = ref(source)[source_at()]

                    self.task(own)


def contract(left, right, left_dim, right_dim):
    return lax.dot_general(
        left, right, (((left_dim,), (right_dim,)), ((), ())), preferred_element_type=jnp.float32
    )


CHAIN_CHUNKS = 8
KERNEL_VMEM = 62 * 2**20
GRAM_COLS = 256


def attend(queries, keys, values):
    scores = contract(queries, keys, 1, 1) * HEAD ** (-0.5)
    expo = jnp.exp(scores - jnp.max(scores, -1, keepdims=True))
    probs = (expo / jnp.sum(expo, -1, keepdims=True)).astype(LOW)
    return contract(probs, values, 1, 0)


def group_rows(rows, members, shift):
    size = rows * members
    there = lax.rem(lax.axis_index(PATCHES) // members + shift, MATRICES)
    return pl.ds(pl.multiple_of(there * size, size), size)


def add_attention(moves, qkv, mixed, arrivals, rows, members, waiting):
    for number in arrivals:
        moves.wait_for(number)
    for number in range(3):
        moves.wait_local(number)
    moves.to_sibling(waiting)
    count = lax.axis_size(PATCHES)
    width = HEADS // count * HEAD
    buffer = moves.scratch((1, rows * count, width), LOW)
    for shift in (*range(1, MATRICES), 0):

        def work(ref, shift=shift):
            at = group_rows(rows, members, shift)
            parts = []
            for head in range(width // HEAD):
                lanes = pl.ds(head * HEAD, HEAD)
                parts.append(attend(ref(qkv)[0, at, lanes], ref(qkv)[1, :, lanes], ref(qkv)[2, :, lanes]))
            ref(buffer)[0, at, :] = jnp.concatenate(parts, -1).astype(LOW)

        moves.task(work)
        moves.head_rows(buffer, mixed, (0,), rows, width * count, members, shift)


def add_attention_back(moves, qkv, grads, result, arrivals, rows, members, waiting):
    for number in arrivals:
        moves.wait_for(number)
    moves.wait_local(0)
    moves.to_sibling(waiting)
    count = lax.axis_size(PATCHES)
    width = HEADS // count * HEAD
    heads = width // HEAD
    buffer = moves.scratch((3, rows * count, width), LOW)
    key_total = moves.scratch((heads, rows * count, HEAD), jnp.float32)
    value_total = moves.scratch((heads, rows * count, HEAD), jnp.float32)
    for shift in (*range(1, MATRICES), 0):

        def work(ref, shift=shift):
            at = group_rows(rows, members, shift)
            parts = []
            for head in range(heads):
                lanes = pl.ds(head * HEAD, HEAD)
                queries, keys, values = ref(qkv)[0, at, lanes], ref(qkv)[1, :, lanes], ref(qkv)[2, :, lanes]
                grad = ref(grads)[0, at, lanes]
                scores = contract(keys, queries, 1, 1) * HEAD ** (-0.5)
                expo = jnp.exp(scores - jnp.max(scores, 0, keepdims=True))
                probs = expo / jnp.sum(expo, 0, keepdims=True)
                grad_probs = contract(values, grad, 1, 1)
                shared = jnp.sum(grad_probs * probs, 0, keepdims=True)
                score_grad = (HEAD ** (-0.5) * probs * (grad_probs - shared)).astype(LOW)
                parts.append(contract(score_grad, keys, 0, 0))
                key_part = contract(score_grad, queries, 1, 0)
                value_part = contract(probs.astype(LOW), grad, 1, 0)
                if shift == 1:
                    ref(key_total)[head] = key_part
                    ref(value_total)[head] = value_part
                else:
                    ref(key_total)[head] += key_part
                    ref(value_total)[head] += value_part
            ref(buffer)[0, at, :] = jnp.concatenate(parts, -1).astype(LOW)

        moves.task(work)
        moves.head_rows(buffer, result, (0,), rows, width * count, members, shift)

    def finish(ref):
        for plane, total in ((1, key_total), (2, value_total)):
            ref(buffer)[plane] = jnp.concatenate([ref(total)[head] for head in range(heads)], -1).astype(LOW)

    moves.task(finish)
    for shift in (*range(1, MATRICES), 0):
        moves.head_rows(buffer, result, (1, 2), rows, width * count, members, shift)


def mod_row(ref, table, row):
    return ref(table)[pl.ds(row, 1), :]


def project(moves, source, weights, target, count):
    def action(ref):
        width = ref(source).shape[1]

        @pl.loop(0, count // width)
        def _(part):
            cols = pl.ds(pl.multiple_of(part * width, width), width)
            ref(target)[:, cols] = contract(ref(source)[...], ref(weights)[:, cols], 1, 0).astype(LOW)

    moves.task(action)


def embed(ref, state_low, io_weights, mods, pos, embedded, normed_low):
    value = contract(ref(state_low)[...], io_weights, 1, 0) + mods(6) + ref(pos)[...].astype(jnp.float32)
    ref(embedded)[...] = value
    normed, _ = layer_norm(value)
    ref(normed_low)[...] = (normed * (1.0 + mods(1)) + mods(0)).astype(LOW)


def begin_step(ids, members, state, id_rows, active, cond_table, biases, pos, ada, io_low, w_out, w_qkv):
    f32 = jnp.float32
    shards = lax.axis_size(SHARDS)
    (rows, padded), (table_rows, _) = state.shape, cond_table.shape
    width = w_out.shape[0]
    ada_cols = ada.shape[1]
    moves = Moves("begin", ids, KERNEL_VMEM)
    table = moves.scratch((table_rows, width), f32)
    bias = moves.scratch((1, biases.shape[1] * shards), f32)
    pos_all = moves.scratch((rows, width), LOW)
    id_rows, active, state = [moves.operand(item, pltpu.VMEM) for item in (id_rows, active, state)]
    small = [moves.gather_columns(SHARDS, cond_table, table), moves.gather_columns(SHARDS, biases, bias)]
    pos_moves, pos_local = moves.gather_columns(SHARDS, pos, pos_all)
    ada_weights, ada_load = moves.load(ada)
    vmem = functools.partial(moves.output, space=pltpu.VMEM)
    extras = vmem((ROLL, 8, width), f32)
    cond_vec, silu_low = vmem((shards * ROLL, width), f32), vmem((shards * ROLL, width), LOW)
    embedded, normed_low = vmem((rows, width), f32), vmem((rows, width), LOW)
    state_low, qkv_rows = vmem((rows, padded), LOW), vmem((rows, 3 * width), LOW)
    parts_leaving, parts = [moves.scratch((shards, ROLL, ada_cols), f32) for _ in range(2)]

    def modulate(ref):
        row = lax.broadcasted_iota(jnp.int32, (shards * ROLL, 1), 0)
        ids_here = ref(id_rows)[:, :1]
        value = jnp.zeros((shards * ROLL, width), f32)
        for entry in range(table_rows):
            of_entry = ref(table)[pl.ds(entry, 1), :].astype(LOW).astype(f32)
            chosen = (ids_here == entry) if entry < NI else (lax.rem(row, ROLL) == entry - NI)
            value = value + jnp.where(chosen, of_entry, 0.0)
        ref(cond_vec)[...] = value
        value = (value / (1.0 + jnp.exp(-value))).astype(LOW)
        ref(silu_low)[...] = value
        start = pl.multiple_of(lax.axis_index(SHARDS) * ada_cols, LANES)
        value = contract(value, ref(ada_weights)[...], 1, 0)
        value = value + ref(bias)[:, pl.ds(start, ada_cols)].astype(LOW).astype(f32)
        for sample in range(shards):
            ref(parts_leaving)[sample] = value[sample * ROLL : (sample + 1) * ROLL]
        ref(parts)[lax.axis_index(SHARDS)] = ref(parts_leaving)[lax.axis_index(SHARDS)]

    for numbers, local in small:
        for number in numbers:
            moves.wait_for(number)
        moves.wait_local(local)
    moves.wait_local(ada_load)
    moves.task(modulate)
    modul_moves = []
    for shift in range(1, shards):

        def other(shift=shift):
            return lax.rem(lax.axis_index(SHARDS) + shift, shards)

        number = moves.move(
            (SHARDS, shift),
            lambda other=other: {SHARDS: other()},
            parts_leaving,
            lambda other=other: (other(),),
            parts,
            lambda: (lax.axis_index(SHARDS),),
            later=True,
        )
        modul_moves.append(number)
        moves.start(number)
    weights = moves.gather_twice((io_low.reshape(-1, io_low.shape[-1]), w_out, w_qkv), members, (1, 1, 4))

    def collect(ref):
        bias_row = ref(bias)[:, pl.ds(6 * width, width)].astype(LOW).astype(f32)
        for step in range(ROLL):
            for piece in range(6 * 2):
                start = piece * width // 2
                value = ref(parts)[start // ada_cols, pl.ds(step, 1), pl.ds(start % ada_cols, width // 2)]
                ref(extras)[step, pl.ds(piece // 2, 1), pl.ds(piece % 2 * width // 2, width // 2)] = value
            ref(extras)[step, pl.ds(6, 1), :] = bias_row
            ref(extras)[step, pl.ds(7, 1), :] = ref(active)[pl.ds(step, 1), :]

    def start_step(ref):
        ref(state_low)[...] = ref(state)[...].astype(LOW)
        mods = lambda row: ref(extras)[0, pl.ds(row, 1), :]
        embed(ref, state_low, ref(weights[0][0])[pl.ds(0, padded), :], mods, pos_all, embedded, normed_low)

    for number in modul_moves:
        moves.wait_for(number)
    moves.task(collect)
    for number in (*pos_moves, *weights[0][1]):
        moves.wait_for(number)
    moves.wait_local(pos_local)
    moves.wait_local(weights[0][2])
    moves.task(start_step)
    for target, numbers, local in weights:
        for number in numbers:
            moves.wait_for(number)
        moves.wait_local(local)
        save = moves.save(target, moves.shape(target), LOW)
        moves.start_local(save)
    moves.start_local(moves.save(pos_all, (rows, width), LOW))
    project(moves, normed_low, weights[2][0], qkv_rows, 3 * width)
    return moves.run()


class Tokens:
    def __init__(self, moves, rows, width):
        self.moves = moves
        self.shards = lax.axis_size(SHARDS)
        self.rows = rows
        self.tokens = moves.scratch((self.shards, rows, width), LOW)
        self.own_part = moves.scratch((rows, width), jnp.float32)
        self.leaving = moves.scratch((self.shards, rows, width), LOW)
        self.arriving = moves.scratch((self.shards, rows, width), LOW)

    def me(self):
        return lax.axis_index(SHARDS)

    def back(self, pair, sibling):
        index = lax.rem(self.me() + self.shards - 2 * pair, self.shards)
        return index + 1 - 2 * lax.rem(index, 2) if sibling else index

    def part(self, pair, sibling, work):
        moves = self.moves
        slot = functools.partial(self.back, pair, sibling)

        def action(ref):
            value = work(ref, slot())
            if pair or sibling:
                ref(self.leaving)[slot()] = value.astype(LOW)
            else:
                ref(self.own_part)[...] = value

        moves.task(action)
        if pair or sibling:
            number = moves.move(
                (SHARDS, pair, sibling),
                lambda: {SHARDS: slot()},
                self.leaving,
                lambda: (slot(),),
                self.arriving,
                lambda: (self.me(),),
                later=True,
            )
            moves.start(number)
            self.parts.append(number)

    def run(self, work):
        moves, halves = self.moves, 2
        self.parts = []
        size = self.rows // halves
        pairs = self.shards // 2

        def half(pair, sibling, number):
            return (self.back(pair, sibling), pl.ds(number * size, size))

        firsts = {}
        for pair in range(1, pairs):
            for number in range(halves):
                place = functools.partial(half, 0, False, number)
                firsts[pair, number] = moves.move(
                    (SHARDS, pairs - pair, False),
                    functools.partial(lambda pair: {SHARDS: self.back(pairs - pair, False)}, pair),
                    self.tokens,
                    place,
                    self.tokens,
                    place,
                    later=True,
                )
                moves.start(firsts[pair, number])
        own = functools.partial(self.back, 0, False)
        near = moves.move(
            (SHARDS, 0, True), sibling_peer, self.tokens, lambda: (own(),), self.tokens, lambda: (own(),), later=True
        )
        moves.start(near)
        self.part(0, False, work)
        moves.wait_for(near)
        self.part(0, True, work)
        for pair in range(1, pairs):
            handed = []
            for number in range(halves):
                place = functools.partial(half, pair, False, number)
                handed.append(
                    moves.move(
                        (SHARDS, 0, True),
                        sibling_peer,
                        self.tokens,
                        place,
                        self.tokens,
                        place,
                        (firsts[pair, number],),
                    )
                )
            self.part(pair, False, work)
            for number in handed:
                moves.wait_for(number)
            self.part(pair, True, work)

    def wait(self):
        for number in self.parts:
            self.moves.wait_for(number)

    def total(self, ref):
        value = ref(self.own_part)[...]
        for shift in range(1, self.shards):
            value = value + ref(self.arriving)[lax.rem(self.me() + shift, self.shards)].astype(jnp.float32)
        return value


TOKENS, UP_GRAD = 1, 2
GELU_SCALE = math.sqrt(2.0 / math.pi)
GELU_CUBE = 0.044715


def gelu_inner(values):
    return jnp.tanh(GELU_SCALE * (values + GELU_CUBE * values * values * values))


def gelu_slope(values):
    inner = gelu_inner(values)
    rise = GELU_SCALE * (1.0 + 3.0 * GELU_CUBE * values * values)
    return 0.5 * (1.0 + inner) + 0.5 * values * (1.0 - inner * inner) * rise


def feed_forward(ids, step, mods, mods_next, mixed, embedded, state, pos, w_out, w_up, w_down, io_all, w_qkv, momenta, members):
    f32 = jnp.float32
    last = mods_next is None
    rows, width = mixed.shape
    padded = state.shape[1]
    hidden_count = w_up.shape[1]
    shards = lax.axis_size(SHARDS)
    moves = Moves(f"feed{step}", ids, KERNEL_VMEM)
    vmem = functools.partial(moves.operand, space=pltpu.VMEM)
    out_weights, out_load = moves.load(w_out)
    mods, mixed, embedded, state = vmem(mods), vmem(mixed), vmem(embedded), vmem(state)
    up_weights, up_load = moves.load(w_up)
    down_weights, down_load = moves.load(w_down)
    io_weights, io_load = moves.load(io_all)
    attended, after_attn, downward, after_mlp = [moves.output((rows, width), f32, pltpu.VMEM) for _ in range(4)]
    normed_c = moves.output((rows, width), LOW, pltpu.VMEM)
    state_next = moves.output((rows, padded), f32, pltpu.VMEM)
    upward = moves.scratch((shards, rows, hidden_count), f32)
    hidden = moves.scratch((shards, rows, hidden_count), LOW)
    feed = Tokens(moves, rows, width)
    saves = [
        moves.save(feed.tokens, (shards, rows, width), LOW),
        moves.save(upward, (shards, rows, hidden_count), f32),
        moves.save(hidden, (shards, rows, hidden_count), LOW),
    ]
    if not last:
        mods_next, pos = vmem(mods_next), vmem(pos)
        qkv_weights, qkv_load = moves.load(w_qkv)
        embedded_next = moves.output((rows, width), f32, pltpu.VMEM)
        normed_next = moves.output((rows, width), LOW, pltpu.VMEM)
        state_low = moves.output((rows, padded), LOW, pltpu.VMEM)
        qkv_next = moves.output((rows, w_qkv.shape[1]), LOW, pltpu.VMEM)
    half = rows // ROLL
    seq_count = lax.axis_size(PATCHES)
    most_cols = max(item.shape[1] for item in momenta) // members
    moment_loads = []
    for item in momenta:
        scratch = moves.scratch((half, item.shape[1]), f32)
        number = moves.keep(moves.operand(item), lambda: (pl.ds(step * half, half),), scratch, None)
        moment_loads.append((scratch, number))
    moment_leaving = moves.scratch((seq_count, half, most_cols), LOW)
    moment_arriving = moves.output((seq_count, half, most_cols), LOW)

    def pack(ref):
        for which, (scratch, _) in enumerate(moment_loads):
            cols = momenta[which].shape[1] // members
            for part in range(members):
                value = ref(scratch)[:, part * cols : (part + 1) * cols].astype(LOW)
                if cols < most_cols:
                    value = jnp.concatenate([value, jnp.zeros((half, most_cols - cols), LOW)], 1)
                ref(moment_leaving)[which * members + part] = value

    def begin(ref):
        value = contract(ref(mixed)[...], ref(out_weights)[...], 1, 0)
        ref(attended)[...] = value
        value = ref(embedded)[...] + mod_row(ref, mods, 2) * value
        ref(after_attn)[...] = value
        normed, _ = layer_norm(value)
        normed = normed * (1.0 + mod_row(ref, mods, 4)) + mod_row(ref, mods, 3)
        ref(feed.tokens)[feed.me()] = normed.astype(LOW)

    def work(ref, slot):
        value = contract(ref(feed.tokens)[slot], ref(up_weights)[...], 1, 0)
        ref(upward)[slot] = value
        value = (0.5 * value * (1.0 + gelu_inner(value))).astype(LOW)
        ref(hidden)[slot] = value
        return contract(value, ref(down_weights)[...], 1, 1)

    def finish(ref):
        value = feed.total(ref)
        ref(downward)[...] = value
        value = ref(after_attn)[...] + mod_row(ref, mods, 5) * value
        ref(after_mlp)[...] = value
        normed, _ = layer_norm(value)
        normed = normed.astype(LOW)
        ref(normed_c)[...] = normed
        delta = contract(normed, ref(io_weights)[1], 1, 1)
        value = ref(state)[...] + mod_row(ref, mods, 7)[:, :padded] * delta
        ref(state_next)[...] = value
        if not last:
            ref(state_low)[...] = value.astype(LOW)
            mods_there = functools.partial(mod_row, ref, mods_next)
            embed(ref, state_low, ref(io_weights)[0], mods_there, pos, embedded_next, normed_next)

    moves.wait_local(out_load)
    moves.task(begin)
    moves.wait_local(up_load)
    moves.wait_local(down_load)
    feed.run(work)
    for number in saves:
        moves.start_local(number)
    for _, number in moment_loads:
        moves.wait_local(number)
    moves.task(pack)
    moves.along(
        PATCHES, moment_leaving, moment_arriving, [(lambda there: (there,), lambda sender: (sender,))], later=True
    )
    moves.wait_local(io_load)
    feed.wait()
    moves.task(finish)
    if not last:
        moves.wait_local(qkv_load)
        project(moves, normed_next, qkv_weights, qkv_next, w_qkv.shape[1])
    return moves.run()


def feed_back(ids, step, mods, mods_later, later, grad_state, kept, w_out, w_up, w_down, io_all, w_qkv, members, pairs):
    f32 = jnp.float32
    attended, after_attn, downward, after_mlp, upward = kept
    rows, width = attended.shape
    padded = grad_state.shape[1]
    hidden_count = w_up.shape[1]
    shards = lax.axis_size(SHARDS)
    moves = Moves(f"feed_back{step}", ids, KERNEL_VMEM)
    vmem = functools.partial(moves.operand, space=pltpu.VMEM)
    io_weights, io_load = moves.load(io_all)
    if later is not None:
        qkv_weights, qkv_load = moves.load(w_qkv)
        later = [vmem(item) for item in later]
        mods_later = vmem(mods_later)
        embed_grad = moves.output((rows, width), LOW, pltpu.VMEM)
    down_weights, down_load = moves.load(w_down)
    up_weights, up_load = moves.load(w_up)
    slopes, slopes_load = moves.load(upward)
    out_weights, out_load = moves.load(w_out)
    mods, grad_state = vmem(mods), vmem(grad_state)
    attended, after_attn, downward, after_mlp = [vmem(item) for item in (attended, after_attn, downward, after_mlp)]
    vectors = moves.output((8, width), f32, pltpu.VMEM)
    state_out = moves.output((rows, padded), f32, pltpu.VMEM)
    delta_grad = moves.output((rows, padded), LOW, pltpu.VMEM)
    grad_attn = moves.output((rows, width), f32, pltpu.VMEM)
    attn_grad, mixed_grad = [moves.output((rows, width), LOW, pltpu.VMEM) for _ in range(2)]
    grad_mlp = moves.scratch((rows, width), f32)
    up_grad = moves.scratch((shards, rows, hidden_count), LOW)
    feed = Tokens(moves, rows, width)
    saves = [
        moves.save(feed.tokens, (shards, rows, width), LOW),
        moves.save(up_grad, (shards, rows, hidden_count), LOW),
    ]

    weight_outputs, weight_tasks = [], []
    if pairs is not None:
        half_cols = hidden_count // members
        whole = moves.scratch((GRAM_COLS, hidden_count), f32)
        for made, operands in pairs:
            mine = moves.output((width, half_cols), f32)
            leaving = [moves.output((width, half_cols), LOW) for _ in range(members - 1)]
            held = moves.scratch((width, half_cols), f32)
            held_low = [moves.scratch((width, half_cols), LOW) for _ in range(members - 1)]
            loads = [[None if item is None else moves.load(item) for item in entry] for entry in operands]
            weight_outputs += [(held, mine)] + list(zip(held_low, leaving))
            weight_tasks.append((made, loads, held, held_low))

    def weight_grad(made, loads, held, held_low):
        def action(ref):
            @pl.loop(0, width // GRAM_COLS)
            def _(tile):
                at = pl.ds(pl.multiple_of(tile * GRAM_COLS, GRAM_COLS), GRAM_COLS)
                value = jnp.zeros((GRAM_COLS, hidden_count), f32)
                for entry in loads:
                    left, right = [made_here if item is None else item[0] for item, made_here in zip(entry, made)]
                    left_rows = ref(left)[:, :, at].reshape(-1, GRAM_COLS)
                    value = value + contract(left_rows, ref(right)[...].reshape(-1, hidden_count), 0, 0)
                ref(whole)[...] = value
                member = lax.rem(lax.axis_index(PATCHES), members)
                for shift in range(members):
                    there = lax.rem(member + shift, members)
                    part = ref(whole)[:, pl.ds(pl.multiple_of(there * half_cols, LANES), half_cols)]
                    if shift:
                        ref(held_low[shift - 1])[at, :] = part.astype(LOW)
                    else:
                        ref(held)[at, :] = part

        return action

    def put(ref, row, value):
        ref(vectors)[pl.ds(row, 1), :] = jnp.sum(value, 0, keepdims=True)

    def before(ref):
        qkv_grad, embedded, grad_later = later
        grad = contract(ref(qkv_grad)[...], ref(qkv_weights)[...], 1, 1)
        normed, inverse = layer_norm(ref(embedded)[...])
        put(ref, 5, grad * normed)
        put(ref, 4, grad)
        grad = grad * (1.0 + mod_row(ref, mods_later, 1))
        grad = ref(grad_later)[...] + norm_back(grad, normed, inverse)
        put(ref, 6, grad)
        grad = grad.astype(LOW)
        ref(embed_grad)[...] = grad
        ref(state_out)[...] = ref(grad_state)[...] + contract(grad, ref(io_weights)[0], 1, 1)

    def begin(ref):
        if later is None:
            ref(state_out)[...] = ref(grad_state)[...]
            ref(vectors)[...] = jnp.zeros((8, width), f32)
        grad = (mod_row(ref, mods, 7)[:, :padded] * ref(state_out)[...]).astype(LOW)
        ref(delta_grad)[...] = grad
        normed, inverse = layer_norm(ref(after_mlp)[...])
        grad = norm_back(contract(grad, ref(io_weights)[1], 1, 0), normed, inverse)
        ref(grad_mlp)[...] = grad
        put(ref, 3, grad * ref(downward)[...])
        ref(feed.tokens)[feed.me()] = (mod_row(ref, mods, 5) * grad).astype(LOW)

    def work(ref, slot):
        value = contract(ref(feed.tokens)[slot], ref(down_weights)[...], 1, 0)
        value = (value * gelu_slope(ref(slopes)[slot])).astype(LOW)
        ref(up_grad)[slot] = value
        return contract(value, ref(up_weights)[...], 1, 1)

    def finish(ref):
        grad = feed.total(ref)
        normed, inverse = layer_norm(ref(after_attn)[...])
        put(ref, 2, grad * normed)
        put(ref, 1, grad)
        grad = ref(grad_mlp)[...] + norm_back(grad * (1.0 + mod_row(ref, mods, 4)), normed, inverse)
        ref(grad_attn)[...] = grad
        put(ref, 0, grad * ref(attended)[...])
        grad = (mod_row(ref, mods, 2) * grad).astype(LOW)
        ref(attn_grad)[...] = grad
        ref(mixed_grad)[...] = contract(grad, ref(out_weights)[...], 1, 1).astype(LOW)

    moves.wait_local(io_load)
    if later is not None:
        moves.wait_local(qkv_load)
        moves.task(before)
    moves.task(begin)
    for number in (down_load, up_load, slopes_load):
        moves.wait_local(number)
    feed.run(work)
    for number in saves:
        moves.start_local(number)
    for made, loads, held, held_low in weight_tasks:
        for entry in loads:
            for item in entry:
                if item is not None:
                    moves.wait_local(item[1])
        made = [feed.tokens if item is TOKENS else up_grad if item is UP_GRAD else None for item in made]
        moves.task(weight_grad(made, loads, held, held_low))
    for held, target in weight_outputs:
        moves.start_local(moves.keep(held, None, target, None, True))
    moves.wait_local(out_load)
    feed.wait()
    moves.task(finish)
    results = moves.run()
    return results if later is not None else [None, *results]


def reduce_step(
    ids, members, group_cols, qkv_grad, embedded, grad_attn, mods, w_qkv, rows_late, rows_early, gathered, mlp, ada
):
    f32 = jnp.float32
    shards, seq_count = lax.axis_size(SHARDS), lax.axis_size(PATCHES)
    rows, width = embedded.shape
    block_rows, most_cols = width, max(group_cols)
    part, ada_cols = width // shards, ada.shape[1]
    up_mine, up_arrived, down_mine, down_leaving = mlp
    moves = Moves("reduce", ids, KERNEL_VMEM)
    vmem = functools.partial(moves.operand, space=pltpu.VMEM)
    qkv_grad, embedded, grad_attn, mods = vmem(qkv_grad), vmem(embedded), vmem(grad_attn), vmem(mods)
    rows_late, rows_early = vmem(rows_late), vmem(rows_early)

    def shard():
        return lax.axis_index(SHARDS)

    def patch():
        return lax.axis_index(PATCHES)

    def group():
        return patch() // members

    def member():
        return lax.rem(patch(), members)

    def columns(index, size):
        return pl.ds(pl.multiple_of(index * size, LANES), size)

    def await_all(numbers):
        for number in numbers:
            moves.wait_for(number)

    def to_others(axis, source, source_at, target, leave_own=False):
        count = lax.axis_size(axis)
        numbers = []
        for shift in range(1, count):

            def other(shift=shift):
                return lax.rem(lax.axis_index(axis) + shift, count)

            number = moves.move(
                (axis, shift),
                lambda other=other: {axis: other()},
                source,
                lambda other=other: source_at(other()),
                target,
                lambda: (lax.axis_index(axis),),
                later=True,
            )
            moves.start(number)
            numbers.append(number)

        def own(ref):
            ref(target)[lax.axis_index(axis)] = ref(source)[source_at(lax.axis_index(axis))]

        moves.task(own)
        return numbers

    def to_members(source, target, cols):
        numbers = []
        for shift in range(1, members):
            number = moves.move(
                (PATCHES, members, shift),
                functools.partial(member_peer, members, shift),
                source,
                lambda shift=shift: (slice(None), columns(lax.rem(member() + shift, members), cols)),
                target,
                lambda shift=shift: (shift - 1,),
                later=True,
            )
            moves.start(number)
            numbers.append(number)
        return numbers

    def to_group(source, target, which):
        numbers = []
        for shift in range(1, MATRICES):
            number = moves.move(
                (PATCHES, seq_count, shift),
                functools.partial(group_peer, members, shift),
                source,
                None,
                target,
                lambda shift=shift: (shift - 1,),
                sends=lambda shift=shift: group() == (which - shift) % MATRICES,
                takes=lambda: group() == which,
                later=True,
            )
            moves.start(number)
            numbers.append(number)
        return numbers

    def over_rows(action):
        @pl.loop(0, block_rows // GRAM_COLS)
        def _(tile):
            action(pl.ds(pl.multiple_of(tile * GRAM_COLS, GRAM_COLS), GRAM_COLS))

    def weight_grad(lefts, rights, full, low=None):
        depth, cols = moves.shape(lefts[0])[2], moves.shape(rights[0])[2]
        tile_rows = GRAM_COLS if depth % GRAM_COLS == 0 else LANES

        def action(ref):
            @pl.loop(0, depth // tile_rows)
            def _(tile):
                at = pl.ds(pl.multiple_of(tile * tile_rows, tile_rows), tile_rows)
                value = jnp.zeros((tile_rows, cols), f32)
                for left, right in zip(lefts, rights):
                    left_rows = ref(left)[:, :, at].reshape(-1, tile_rows)
                    value = value + contract(left_rows, ref(right)[...].reshape(-1, cols), 0, 0)
                if full is not None:
                    ref(full)[at, :] = value
                if low is not None:
                    ref(low)[at, :] = value.astype(LOW)

        moves.task(action)

    qkv_all = moves.scratch((shards, rows, 3 * part), LOW)
    qkv_moves = moves.along(
        SHARDS,
        qkv_grad,
        qkv_all,
        [(lambda receiver: (slice(None), columns(receiver, 3 * part)), lambda sender: (sender,))],
    )
    qkv_local = len(moves.locals) - 1
    down_arriving = moves.scratch((members - 1, block_rows, group_cols[2]), LOW)
    down_moves = [
        moves.move(
            (PATCHES, members, shift),
            functools.partial(member_peer, members, shift),
            moves.operand(item),
            None,
            down_arriving,
            lambda shift=shift: (shift - 1,),
        )
        for shift, item in enumerate(down_leaving, 1)
    ]
    up_full, up_load = moves.load(up_mine)
    up_others = [moves.load(item) for item in up_arrived]
    qkv_weights, qkv_load = moves.load(w_qkv)
    loaded = {
        name: [moves.load(steps[step]) for step in range(ROLL) if step in steps] for name, steps in gathered.items()
    }
    down_full, down_load = moves.load(down_mine)
    ada_weights, ada_load = moves.load(ada)

    def ready(*names):
        for name in names:
            for _, number in loaded[name]:
                moves.wait_local(number)
        return [[item for item, _ in loaded[name]] for name in names]

    up_low, down_low = [moves.scratch((block_rows, cols), LOW) for cols in group_cols[1:3]]
    group_target = moves.scratch((MATRICES - 1, block_rows, most_cols), LOW)

    def round_up_grad(ref):
        def action(at):
            value = ref(up_full)[at, :]
            for item, _ in up_others:
                value = value + ref(item)[at, :].astype(f32)
            ref(up_full)[at, :] = value
            ref(up_low)[at, :] = value.astype(LOW)

        over_rows(action)

    for number in (up_load, *[number for _, number in up_others]):
        moves.wait_local(number)
    moves.task(round_up_grad)
    up_moves = to_group(up_low, group_target, 1)

    embed_low = moves.scratch((rows, width), LOW)
    table = moves.scratch((8, 6 * width), f32)

    def back(ref):
        grad = contract(ref(qkv_grad)[...], ref(qkv_weights)[...], 1, 1)
        normed, inverse = layer_norm(ref(embedded)[...])
        ref(table)[...] = jnp.zeros((8, 6 * width), f32)
        ref(table)[pl.ds(0, 1), pl.ds(0, width)] = jnp.sum(grad, 0, keepdims=True)
        ref(table)[pl.ds(0, 1), pl.ds(width, width)] = jnp.sum(grad * normed, 0, keepdims=True)
        grad = ref(grad_attn)[...] + norm_back(grad * (1.0 + mod_row(ref, mods, 1)), normed, inverse)
        ref(embed_low)[...] = grad.astype(LOW)
        bias_row = jnp.sum(grad, 0, keepdims=True) + mod_row(ref, rows_early, 6)
        for entry in range(4):
            cols = pl.ds((2 + entry) * width, width)
            ref(table)[pl.ds(0, 1), cols] = mod_row(ref, rows_early, entry)
            ref(table)[pl.ds(1, 1), cols] = mod_row(ref, rows_late, entry)
        for entry in range(2):
            ref(table)[pl.ds(1, 1), pl.ds(entry * width, width)] = mod_row(ref, rows_early, 4 + entry)
        for entry in range(shards):
            ref(table)[pl.ds(ROLL, 1), pl.ds(entry * ada_cols, part)] = bias_row[:, entry * part : (entry + 1) * part]

    moves.wait_local(qkv_load)
    moves.task(back)
    embed_all = moves.scratch((shards, rows, part), LOW)
    table_all = moves.scratch((shards, 8, ada_cols), f32)
    embed_moves = to_others(SHARDS, embed_low, lambda there: (slice(None), columns(there, part)), embed_all)
    table_moves = to_others(SHARDS, table, lambda there: (slice(None), columns(there, ada_cols)), table_all)

    out_cols, qkv_cols = group_cols[3], group_cols[0]
    out_full, out_low = moves.scratch((width, part), f32), moves.scratch((width, part), LOW)
    qkv_full, qkv_low = moves.scratch((width, 3 * part), f32), moves.scratch((width, 3 * part), LOW)
    out_arriving = moves.scratch((members - 1, block_rows, out_cols), LOW)
    qkv_arriving = moves.scratch((members - 1, block_rows, qkv_cols), LOW)
    padded = moves.shape(loaded["state"][0][0])[2]
    io_low = moves.scratch((2 * padded, part), LOW)
    io_grads = [moves.scratch((padded, part), f32) for _ in range(2)]
    weight_grad(*ready("mixed", "attn"), out_full, out_low)
    out_moves = to_members(out_low, out_arriving, out_cols)
    weight_grad(*ready("delta", "c"), io_grads[1])
    await_all(qkv_moves)
    moves.wait_local(qkv_local)
    (a_all, qkv_later) = ready("a", "qkv")
    weight_grad(a_all, [qkv_all, *qkv_later], qkv_full, qkv_low)
    qkv_member_moves = to_members(qkv_low, qkv_arriving, qkv_cols)
    await_all(embed_moves)
    (state_all, embed_later) = ready("state", "embed")
    weight_grad(state_all, [embed_all, *embed_later], io_grads[0])
    grad_pos = moves.output((rows, part), f32, pltpu.VMEM)
    io_rows = 2 * padded // seq_count

    def pos_and_io(ref):
        value = jnp.zeros((rows, part), f32)
        for item in (embed_all, *embed_later):
            for sample in range(shards):
                value = value + ref(item)[sample].astype(f32)
        ref(grad_pos)[...] = value
        for number, item in enumerate(io_grads):
            ref(io_low)[pl.ds(number * padded, padded), :] = ref(item)[...].astype(LOW)

    moves.task(pos_and_io)
    io_all = moves.scratch((seq_count, io_rows, part), LOW)
    io_moves = to_others(
        PATCHES, io_low, lambda there: (pl.ds(pl.multiple_of(there * io_rows, io_rows), io_rows),), io_all
    )

    flat, flat_all = moves.scratch((16, ada_cols), LOW), moves.scratch((seq_count, 16, ada_cols), LOW)

    def share(ref):
        pieces = [ref(table_all)[sample, pl.ds(0, ROLL), :] for sample in range(shards)]
        bias_row = sum(ref(table_all)[sample, pl.ds(ROLL, 1), :] for sample in range(shards))
        rest = jnp.zeros((16 - shards * ROLL - 1, ada_cols), f32)
        ref(flat)[...] = jnp.concatenate([*pieces, bias_row, rest], 0).astype(LOW)

    await_all(table_moves)
    moves.task(share)
    flat_moves = to_others(PATCHES, flat, lambda there: (slice(None), slice(None)), flat_all)

    def add_member(full, arriving, target, low, cols):
        def action(ref):
            def add(at):
                value = ref(full)[at, columns(member(), cols)] if target is not full else ref(full)[at, :]
                for shift in range(members - 1):
                    value = value + ref(arriving)[shift, at, :].astype(f32)
                ref(target)[at, :] = value
                if low is not None:
                    ref(low)[at, :] = value.astype(LOW)

            over_rows(add)

        moves.task(action)

    moves.wait_local(down_load)
    await_all(down_moves)
    add_member(down_full, down_arriving, down_full, down_low, group_cols[2])
    down_group_moves = to_group(down_low, group_target, 2)
    out_mine, out_mine_low = moves.scratch((width, out_cols), f32), moves.scratch((width, out_cols), LOW)
    out_target = moves.scratch((MATRICES - 1, block_rows, out_cols), LOW)
    await_all(out_moves)
    add_member(out_full, out_arriving, out_mine, out_mine_low, out_cols)
    out_group_moves = to_group(out_mine_low, out_target, 3)

    modul_all = moves.output((shards * ROLL, ada_cols), f32, pltpu.VMEM)
    tail_all = moves.output((shards, 16, ada_cols), f32, pltpu.VMEM)
    tail = moves.scratch((16, ada_cols), f32)

    def close(ref):
        value = jnp.zeros((16, ada_cols), f32)
        for item in range(seq_count):
            value = value + ref(flat_all)[item].astype(f32)
        modul = value[: shards * ROLL]
        ref(modul_all)[...] = modul
        high = modul.astype(LOW)
        rest = (modul - high.astype(f32)).astype(LOW)
        weights = ref(ada_weights)[...]
        ref(tail)[...] = jnp.zeros((16, ada_cols), f32)
        ref(tail)[pl.ds(0, shards * ROLL), pl.ds(0, width)] = contract(high, weights, 1, 1) + contract(
            rest, weights, 1, 1
        )
        ref(tail)[pl.ds(8, 1), :] = jnp.sum(modul, 0, keepdims=True)
        ref(tail)[pl.ds(9, 1), :] = value[shards * ROLL : shards * ROLL + 1]

    await_all(flat_moves)
    moves.wait_local(ada_load)
    moves.task(close)
    to_others(SHARDS, tail, lambda there: (slice(None), slice(None)), tail_all)

    def has_source():
        return group() < MATRICES - 1

    def is_source():
        return group() > 0

    chain = moves.scratch((width, qkv_cols), f32)
    chain_in, chain_out = [moves.scratch((width, qkv_cols), LOW) for _ in range(2)]
    await_all(qkv_member_moves)
    add_member(qkv_full, qkv_arriving, chain, None, qkv_cols)
    chunk = block_rows // CHAIN_CHUNKS
    for number_of in range(CHAIN_CHUNKS):
        place = (pl.ds(number_of * chunk, chunk),)
        number = moves.move(
            (PATCHES, seq_count, MATRICES - 1),
            functools.partial(group_peer, members, MATRICES - 1),
            chain_out,
            lambda place=place: place,
            chain_in,
            lambda place=place: place,
            sends=is_source,
            takes=has_source,
            later=True,
        )

        def add(ref, place=place):
            def with_arriving():
                ref(chain)[place] += ref(chain_in)[place].astype(f32)

            pl.when(has_source())(with_arriving)
            ref(chain_out)[place] = ref(chain)[place].astype(LOW)

        moves.wait_for(number)
        moves.task(add)
        moves.start(number)

    io_slice = moves.output((io_rows, part), f32, pltpu.VMEM)

    def add_io(ref):
        value = jnp.zeros((io_rows, part), f32)
        for item in range(seq_count):
            value = value + ref(io_all)[item].astype(f32)
        ref(io_slice)[...] = value

    await_all(io_moves)
    moves.task(add_io)

    grad_group = moves.output((block_rows, most_cols), f32, pltpu.VMEM)

    def put(full, target, cols):
        def action(ref):
            def add(at):
                value = ref(full)[at, :]
                if target is not None:
                    for shift in range(MATRICES - 1):
                        value = value + ref(target)[shift, at, pl.ds(0, cols)].astype(f32)
                ref(grad_group)[at, pl.ds(0, cols)] = value
                if cols < most_cols:
                    ref(grad_group)[at, pl.ds(cols, most_cols - cols)] = jnp.zeros((GRAM_COLS, most_cols - cols), f32)

            over_rows(add)

        return action

    def settle(ref):
        entries = ((chain, None), (up_full, group_target), (down_full, group_target), (out_mine, out_target))
        for which, (full, target) in enumerate(entries):
            pl.when(group() == which)(functools.partial(put(full, target, group_cols[which]), ref))

    await_all((*up_moves, *down_group_moves, *out_group_moves))
    moves.task(settle)
    return moves.run()


def newton_schulz(source, gram, poly, once, gram_low, poly_low, once_low, block, block_next):
    size = gram.shape[0]
    eye = jnp.equal(
        lax.broadcasted_iota(jnp.int32, (GRAM_COLS, GRAM_COLS), 0),
        lax.broadcasted_iota(jnp.int32, (GRAM_COLS, GRAM_COLS), 1),
    ).astype(jnp.float32)

    tiles = size // GRAM_COLS

    def tile_at(tile):
        return pl.ds(tile * GRAM_COLS, GRAM_COLS)

    def store(full, low, tile, value, mean, excess):
        cols = tile_at(tile)
        if tile:
            above = pl.ds(0, tile * GRAM_COLS)
            full[above, cols] = value[: tile * GRAM_COLS]
            low[above, cols] = value[: tile * GRAM_COLS].astype(LOW)
            for row in range(tile):
                low[cols, tile_at(row)] = value[row * GRAM_COLS : (row + 1) * GRAM_COLS].T.astype(LOW)
        corner = value[tile * GRAM_COLS :] - excess * eye
        full[cols, cols] = corner
        low[cols, cols] = (corner - mean * eye).astype(LOW)

    def inner(tile, left, right):
        both = left * right
        return 2.0 * jnp.sum(both) - jnp.sum(both[tile * GRAM_COLS :])

    def product_cols(left, right, tile):
        return contract(left[pl.ds(0, (tile + 1) * GRAM_COLS), :], right[:, tile_at(tile)], 1, 0)

    def upper(full, tile):
        return full[pl.ds(0, (tile + 1) * GRAM_COLS), tile_at(tile)]

    def advance(gram_mean, gram_squares, last):
        poly_mean = NS_B * gram_mean + NS_C * gram_squares / size
        total = jnp.float32(0.0)
        for tile in range(tiles):
            own = upper(gram, tile)
            value = product_cols(gram_low, gram_low, tile)
            value = NS_C * value + (NS_B + 2.0 * NS_C * gram_mean) * own
            store(poly, poly_low, tile, value, poly_mean, NS_C * gram_mean * gram_mean)
            total = total + inner(tile, value, own)
        once_mean = total / size - NS_C * gram_mean * gram_mean * gram_mean

        for tile in range(block.shape[1] // GRAM_COLS):
            cols = tile_at(tile)
            value = contract(poly_low[...], block[:, cols], 1, 0)
            block_next[:, cols] = (value + (NS_A + poly_mean) * block[:, cols].astype(jnp.float32)).astype(LOW)
        block[...] = block_next[...]
        if last:
            return None

        total = jnp.float32(0.0)
        for tile in range(tiles):
            own = upper(poly, tile)
            value = product_cols(poly_low, gram_low, tile)
            value = value + poly_mean * upper(gram, tile) + gram_mean * own
            store(once, once_low, tile, value, once_mean, poly_mean * gram_mean)
            total = total + inner(tile, value, own)
        poly_once = total / size - poly_mean * gram_mean * poly_mean
        mean_next = NS_A * NS_A * gram_mean + 2.0 * NS_A * once_mean + poly_once
        excess = poly_mean * once_mean

        total = jnp.float32(0.0)
        for tile in range(tiles):
            value = product_cols(poly_low, once_low, tile)
            value = value + (2.0 * NS_A + poly_mean) * upper(once, tile) + once_mean * upper(poly, tile)
            value = value + NS_A * NS_A * upper(gram, tile)
            store(gram, gram_low, tile, value, mean_next, excess)
            total = total + inner(tile, value, value)
        return mean_next, total - excess * (2.0 * mean_next + excess) * size

    block[...] = source[...]
    mean = jnp.float32(0.0)
    for tile in range(tiles):
        mean = mean + jnp.sum(gram[tile_at(tile), tile_at(tile)] * eye)
    mean = mean / size
    squares = jnp.float32(0.0)
    for tile in range(tiles):
        cols = tile_at(tile)
        value = gram[:, cols]
        gram_low[:, cols] = value.astype(LOW)
        gram_low[cols, cols] = (gram[cols, cols] - mean * eye).astype(LOW)
        squares = squares + jnp.sum(value * value)
    state = lax.fori_loop(0, NS_ITERS - 1, lambda turn, state: advance(*state, False), (mean, squares))
    advance(*state, True)


def fast_body(
    states,
    targets,
    lengths,
    intervals,
    qkv_copy,
    qkv_master,
    qkv_moment,
    out_copy,
    out_master,
    out_moment,
    up_copy,
    up_master,
    up_moment,
    down_copy,
    down_master,
    down_moment,
    ada_copy,
    ada_master,
    ada_first,
    ada_second,
    io_proj,
    io_first,
    io_second,
    cond_table,
    cond_first,
    cond_second,
    pos_table,
    pos_first,
    pos_second,
    biases,
    bias_first,
    bias_second,
):
    ids = {}
    f32 = jnp.float32
    seq_count, shards = lax.axis_size(PATCHES), lax.axis_size(SHARDS)
    seq_index, shard = lax.axis_index(PATCHES), lax.axis_index(SHARDS)
    members = seq_count // MATRICES
    group, member = seq_index // members, lax.rem(seq_index, members)
    samples, local, values_count = states.shape
    table_rows, table_cols = cond_table.shape
    width = table_cols * shards
    ada_cols = ada_copy.shape[1]
    padded = round_up(values_count, LANES)

    value_pad = ((0, 0), (0, padded - values_count))
    state = jnp.pad(states[0].astype(f32), value_pad)
    length = lengths[0]
    id_rows = jnp.broadcast_to(intervals[:, None, None], (shards, ROLL, LANES)).reshape(-1, LANES)
    (
        extras,
        cond_vec,
        silu_low,
        embedded,
        normed_a,
        state_low,
        qkv_rows,
        io_all,
        w_out,
        w_qkv,
        pos,
    ) = begin_step(
        ids,
        members,
        state,
        id_rows,
        jnp.broadcast_to((jnp.arange(ROLL, dtype=jnp.int32)[:, None] < length).astype(f32), (ROLL, width)),
        cond_table,
        biases[None],
        pos_table.astype(LOW),
        ada_copy,
        jnp.pad(io_proj.astype(LOW), ((0, 0), (0, padded - values_count), (0, 0))),
        out_copy,
        qkv_copy,
    )
    io_all = io_all.reshape(2, padded, width)
    masters = (qkv_master, up_master, down_master, out_master)
    momenta = (qkv_moment, up_moment, down_moment, out_moment)
    group_cols = [item.shape[1] // members for item in momenta]
    most_cols = max(group_cols)

    half_rows = local // ROLL

    counts = jnp.sum((intervals[:, None] == jnp.arange(NI, dtype=jnp.int32)[None]).astype(f32), 0)
    my_id = lax.dynamic_slice_in_dim(intervals, shard, 1)
    id_count = jnp.sum((my_id == jnp.arange(NI, dtype=jnp.int32)).astype(f32) * counts)
    weight = 1.0 / (NI * local * seq_count * values_count * id_count)
    kept = []
    gathered = {}
    moment_halves = []

    for step in range(ROLL):
        moves = Moves(f"attend{step}", ids, KERNEL_VMEM)
        qkv_out = moves.output((3, local * seq_count, width // seq_count), LOW, pltpu.VMEM)
        mixed_out = moves.output((local, width), LOW, pltpu.VMEM)
        arrivals = moves.rows_to_heads(PATCHES, qkv_rows, 3, qkv_out)
        waiting = moves.gather_pairs(normed_a, hold=True)
        waiting += moves.gather_pairs(state_low, hold=True)
        if step:
            waiting += moves.gather_pairs(kept[-1][2], hold=True)
        add_attention(moves, qkv_out, mixed_out, arrivals, local, members, waiting)
        qkv, mixed, gathered_a, gathered_state, *gathered_mixed = moves.run()
        gathered.setdefault("a", {})[step] = gathered_a
        gathered.setdefault("state", {})[step] = gathered_state
        if step:
            gathered["mixed"] = {step - 1: gathered_mixed[0]}
        *results, moment_half = feed_forward(
            ids,
            step,
            extras[step],
            extras[step + 1] if step + 1 < ROLL else None,
            mixed,
            embedded,
            state,
            pos,
            w_out,
            up_copy,
            down_copy,
            io_all,
            w_qkv,
            momenta,
            members,
        )
        moment_halves.append(moment_half)
        attended, after_attn, downward, after_mlp, normed_c, state, tokens_b, upward, hidden, *following = results
        kept.append(
            (embedded, qkv, mixed, (attended, after_attn, downward, after_mlp, upward), normed_c, tokens_b, hidden)
        )
        if following:
            embedded, normed_a, state_low, qkv_rows = following

    lat = latitude_weights(local)
    diff = state - jnp.pad(targets[0].astype(f32), value_pad)
    loss_local = weight * jnp.sum(jnp.sum(diff * diff, -1) * lat)
    grad_state = 2.0 * weight * lat[:, None] * diff

    mlp_back = []

    later, mods_later = None, None
    vector_rows = [None] * ROLL

    for step in reversed(range(ROLL)):
        embedded, qkv, mixed, for_feed, normed_c, tokens_b, hidden = kept[step]
        pairs = None
        if step == 0:
            pairs = (
                ((None, UP_GRAD), [(tokens_b, None), *[(item[0], item[1]) for item in mlp_back]]),
                ((TOKENS, None), [(None, hidden), *[(item[2], item[3]) for item in mlp_back]]),
            )
        results = feed_back(
            ids,
            step,
            extras[step],
            mods_later,
            later,
            grad_state,
            for_feed,
            w_out,
            up_copy,
            down_copy,
            io_all,
            w_qkv,
            members,
            pairs,
        )
        embed_grad, vectors, grad_state, delta_grad, grad_attn, attn_grad, mixed_grad, *results = results
        tokens_down, up_grad, *weight_grads = results
        vector_rows[step] = vectors
        mlp_back.append((tokens_b, up_grad, tokens_down, hidden))
        if step == 0:
            up_mine, *up_leaving = weight_grads[:members]
            down_mine, *down_leaving = weight_grads[members:]
            up_arrived = []
            for shift, item in enumerate(up_leaving, 1):
                routes = [
                    (index, index // members * members + (index + shift) % members) for index in range(seq_count)
                ]
                up_arrived.append(lax.ppermute(item, PATCHES, routes))
        moves = Moves(f"attend_back{step}", ids, KERNEL_VMEM)
        grads_in = moves.scratch((1, local * seq_count, width // seq_count), LOW)
        result = moves.output((local, 3 * width), LOW, pltpu.VMEM)
        arrivals = moves.rows_to_heads(PATCHES, mixed_grad, 1, grads_in)
        names = ["attn", "c", "delta"]
        moves.exchange_columns(SHARDS, attn_grad)
        moves.exchange_columns(SHARDS, normed_c)
        waiting = moves.gather_pairs(delta_grad, hold=True)
        if step == ROLL - 1:
            waiting += moves.gather_pairs(mixed, hold=True)
            names.append("mixed")
        else:
            moves.exchange_columns(SHARDS, later[0])
            moves.exchange_columns(SHARDS, embed_grad)
            names += ["qkv", "embed"]
        add_attention_back(
            moves, moves.operand(qkv, pltpu.VMEM), grads_in, result, arrivals, local, members, waiting
        )
        qkv_grad, *others = moves.run()
        for name, item in zip(names, others):
            gathered.setdefault(name, {})[step + (name in ("qkv", "embed"))] = item
        later, mods_later = (qkv_grad, embedded, grad_attn), extras[step]

    block_rows = qkv_copy.shape[0]
    grad_pos, modul_all, tail_all, io_slice, grad_group = reduce_step(
        ids,
        members,
        group_cols,
        qkv_grad,
        embedded,
        grad_attn,
        extras[0],
        w_qkv,
        vector_rows[1],
        vector_rows[0],
        gathered,
        (up_mine, up_arrived, down_mine, down_leaving),
        ada_copy,
    )
    io_cols = io_slice.shape[1]
    moves = Moves("finish", ids, KERNEL_VMEM)
    vmem = functools.partial(moves.operand, space=pltpu.VMEM)
    vmem_out = functools.partial(moves.output, space=pltpu.VMEM)
    full, low = (block_rows, block_rows), (block_rows, most_cols)
    block_part = block_rows // seq_count
    grad_in, io_in, pos_in, modul_in, tail_in = [
        vmem(item) for item in (grad_group, io_slice, grad_pos, modul_all, tail_all)
    ]
    silu_in, cond_in, ids_in = vmem(silu_low), vmem(cond_vec), vmem(id_rows)
    loss_in = vmem(jnp.broadcast_to(loss_local, (1, LANES)))
    moment = moves.scratch((seq_count, block_part, most_cols), LOW)
    moment_loads = [
        moves.keep(
            moves.operand(item),
            None,
            moment,
            lambda half=half: (slice(None), pl.ds(half * half_rows, half_rows)),
        )
        for half, item in enumerate(moment_halves)
    ]
    master_loads = [moves.load(item) for item in masters]
    sums = vmem_out((8, LANES), f32)
    grad_ada = vmem_out((block_part, ada_cols), f32)
    grad_table_all = vmem_out((8, width), f32)
    io_all_parts = vmem_out((seq_count,) + io_slice.shape, LOW)
    fresh = [vmem_out(item.shape, f32) for item in masters]
    fresh_low = [moves.scratch(item.shape, LOW) for item in masters]
    near, far = [moves.scratch((count, 8, LANES), f32) for count in (shards, seq_count)]
    grad_low, source = moves.scratch(low, LOW), moves.scratch(low, LOW)
    io_low = moves.scratch(io_slice.shape, LOW)

    def measure(ref):
        def add(item, totals):
            rows = pl.ds(pl.multiple_of(item * block_part, block_part), block_part)
            old, grad = ref(moment)[item].astype(f32), ref(grad_in)[rows, :]
            ref(grad_low)[rows, :] = grad.astype(LOW)
            return totals[0] + jnp.sum(old * old), totals[1] + jnp.sum(old * grad), totals[2] + jnp.sum(grad * grad)

        zero = jnp.float32(0.0)
        terms = lax.fori_loop(0, seq_count, add, (zero, zero, zero))
        patch = lax.axis_index(PATCHES)
        count = shards * ROLL
        silu_rows = ref(silu_in)[:, pl.ds(pl.multiple_of(patch * block_part, LANES), block_part)]
        silu_rows = jnp.concatenate([silu_rows, jnp.zeros((16 - count, block_part), LOW)], 0)
        modul = jnp.concatenate([ref(modul_in)[...], jnp.zeros((16 - count, ada_cols), f32)], 0)
        modul_high = modul.astype(LOW)
        modul_rest = (modul - modul_high.astype(f32)).astype(LOW)
        value = contract(silu_rows, modul_high, 0, 0) + contract(silu_rows, modul_rest, 0, 0)
        ref(grad_ada)[...] = value
        squares = terms[2] + jnp.sum(value * value)
        squares = squares + jnp.sum(ref(io_in)[...] * ref(io_in)[...]) + jnp.sum(ref(pos_in)[...] * ref(pos_in)[...])
        ref(io_low)[...] = ref(io_in)[...].astype(LOW)
        cond = ref(cond_in)[...]
        gate = 1.0 / (1.0 + jnp.exp(-cond))
        grad_silu = sum(ref(tail_in)[item, pl.ds(0, count), pl.ds(0, width)] for item in range(shards))
        grad_cond = grad_silu * gate * (1.0 + cond * (1.0 - gate))
        row = lax.broadcasted_iota(jnp.int32, (count, 1), 0)
        ref(grad_table_all)[...] = jnp.zeros((8, width), f32)
        for entry in range(table_rows):
            chosen = (ref(ids_in)[:, :1] == entry) if entry < NI else (lax.rem(row, ROLL) == entry - NI)
            value = jnp.sum(jnp.where(chosen, grad_cond, 0.0), 0, keepdims=True)
            ref(grad_table_all)[pl.ds(entry, 1), :] = value
        me = lax.axis_index(SHARDS)
        value = ref(grad_table_all)[:, pl.ds(pl.multiple_of(me * table_cols, LANES), table_cols)]
        once = jnp.sum(value * value)
        for entry, cols in ((8, ada_cols), (9, table_cols)):
            value = ref(tail_in)[me, pl.ds(entry, 1), pl.ds(0, cols)]
            once = once + jnp.sum(value * value)
        squares = squares + jnp.where(patch == 0, once, 0.0)
        lane = lax.broadcasted_iota(jnp.int32, (8, LANES), 1)
        entries = jnp.where(lane == 0, squares, 0.0) + jnp.where(lane == 1, ref(loss_in)[...], 0.0)
        for number, term in enumerate(terms):
            entries = entries + jnp.where(lane == 2 + 3 * (patch // members) + number, term, 0.0)
        ref(near)[me] = entries

    for number in moment_loads:
        moves.wait_local(number)
    moves.task(measure)

    def spread(axis, buffer, at):
        count = lax.axis_size(axis)
        numbers = []
        for shift in range(1, count):
            numbers.append(
                moves.move(
                    (axis, shift),
                    lambda shift=shift: {axis: lax.rem(lax.axis_index(axis) + shift, count)},
                    buffer,
                    at,
                    io_all_parts if buffer is io_low else buffer,
                    lambda: (lax.axis_index(axis),),
                    later=True,
                )
            )
            moves.start(numbers[-1])
        return numbers

    def add_near(ref):
        ref(far)[lax.axis_index(PATCHES)] = jnp.sum(ref(near)[...], 0)

    def scale(ref):
        ref(sums)[...] = jnp.sum(ref(far)[...], 0)
        row = ref(sums)[pl.ds(0, 1), :]
        lane = lax.broadcasted_iota(jnp.int32, (1, LANES), 1)

        def entry(place):
            return jnp.sum(jnp.where(lane == place, row, 0.0), 1, keepdims=True)

        clip = jnp.minimum(1.0, CLIP_LIMIT / (jnp.sqrt(entry(0)) + 1e-06))
        place = 2 + 3 * (lax.axis_index(PATCHES) // members)
        size = MOMENTUM * MOMENTUM * entry(place) + 2.0 * MOMENTUM * clip * entry(place + 1)
        size = jnp.sqrt(jnp.maximum(size + clip * clip * entry(place + 2), 0.0))
        per_size = 1.0 / (size + 1e-07)

        @pl.loop(0, seq_count)
        def _(item):
            rows = pl.ds(pl.multiple_of(item * block_part, block_part), block_part)
            value = MOMENTUM * ref(moment)[item].astype(f32) + clip * ref(grad_in)[rows, :]
            ref(source)[rows, :] = (value * per_size).astype(LOW)

        ref(io_all_parts)[lax.axis_index(PATCHES)] = ref(io_low)[...]

    for number in spread(SHARDS, near, lambda: (lax.axis_index(SHARDS),)):
        moves.wait_for(number)
    moves.task(add_near)
    far_moves = spread(PATCHES, far, lambda: (lax.axis_index(PATCHES),))
    spread(PATCHES, io_low, None)
    for number in far_moves:
        moves.wait_for(number)
    moves.task(scale)

    update = moves.scratch((seq_count, block_part, most_cols), LOW)
    target = moves.scratch((members * shards,) + low, LOW)
    gram, poly, once = [moves.scratch(full, f32) for _ in range(3)]
    gram_low, poly_low, once_low = [moves.scratch(full, LOW) for _ in range(3)]
    state, state_next = [moves.scratch(low, LOW) for _ in range(2)]
    pairs = shards // 2

    def slot(back_member, back_pair, part=None):
        who_member = lax.rem(lax.rem(lax.axis_index(PATCHES), members) + members - back_member, members)
        who_shard = lax.rem(lax.axis_index(SHARDS) + shards - 2 * back_pair, shards)
        index = who_member * shards + who_shard
        return (index,) if part is None else (index, pl.ds(part * block_rows // 2, block_rows // 2))

    def add_gram(place):
        def action(ref):
            (index,) = place()

            @pl.loop(0, block_rows // GRAM_COLS)
            def _(tile):
                cols = pl.ds(pl.multiple_of(tile * GRAM_COLS, GRAM_COLS), GRAM_COLS)
                ref(gram)[:, cols] += contract(ref(target)[index], ref(target)[index, cols, :], 1, 1)

        return action

    def start_gram(ref):
        @pl.loop(0, block_rows // GRAM_COLS)
        def _(tile):
            cols = pl.ds(pl.multiple_of(tile * GRAM_COLS, GRAM_COLS), GRAM_COLS)
            ref(gram)[:, cols] = contract(ref(source)[...], ref(source)[cols, :], 1, 1)

    def pair_peer(shift):
        return {SHARDS: lax.rem(lax.axis_index(SHARDS) + 2 * shift, shards)}

    def row_part(shift):
        there = lax.rem(lax.axis_index(PATCHES) + shift, seq_count)
        size = block_rows // seq_count
        return (pl.ds(pl.multiple_of(there * size, size), size),)

    slot_own = functools.partial(slot, 0, 0)
    by_member = {
        shift: moves.move(
            (PATCHES, members, shift),
            functools.partial(member_peer, members, shift),
            source,
            None,
            target,
            slot_own,
            later=True,
        )
        for shift in range(1, members)
    }
    by_pair = {
        shift: moves.move(
            (SHARDS, 2 * shift), functools.partial(pair_peer, shift), source, None, target, slot_own, later=True
        )
        for shift in range(1, pairs)
    }
    from_sibling = [(moves.move((SHARDS,), sibling_peer, source, None, target, slot_own, later=True), slot_own)]
    for number in (*by_member.values(), *by_pair.values(), from_sibling[0][0]):
        moves.start(number)
    moves.task(start_gram)

    def sibling_place(place):
        def at():
            (index,) = place()
            return (index + 1 - 2 * lax.rem(index, 2),)

        return at

    def hand_on(place, arrivals):
        if len(arrivals) == 1:
            parts = [(place, arrivals[0])]
        else:
            parts = [(functools.partial(place, part), number) for part, number in enumerate(arrivals)]
        numbers = [
            moves.move((SHARDS,), sibling_peer, target, at, target, at, (number,)) for at, number in parts
        ]
        from_sibling.append((numbers, place))
        moves.task(add_gram(place))

    across = []
    for shift_member, first in by_member.items():
        for shift_pair, second in by_pair.items():
            top = functools.partial(slot, shift_member, 0, 0)
            bottom = functools.partial(slot, 0, shift_pair, 1)
            halves = [
                moves.move(
                    (SHARDS, 2 * shift_pair),
                    functools.partial(pair_peer, shift_pair),
                    target,
                    top,
                    target,
                    top,
                    (first,),
                ),
                moves.move(
                    (PATCHES, members, shift_member),
                    functools.partial(member_peer, members, shift_member),
                    target,
                    bottom,
                    target,
                    bottom,
                    (second,),
                ),
            ]
            across.append((functools.partial(slot, shift_member, shift_pair), halves))
    for shift, number in by_member.items():
        hand_on(functools.partial(slot, shift, 0), [number])
    for shift, number in by_pair.items():
        hand_on(functools.partial(slot, 0, shift), [number])
    moves.wait_for(from_sibling[0][0])
    moves.task(add_gram(sibling_place(slot_own)))
    for place, halves in across:
        hand_on(place, halves)
    for numbers, place in from_sibling[1:]:
        for number in numbers:
            moves.wait_for(number)
        moves.task(add_gram(sibling_place(place)))

    grad_rows = moves.output((seq_count, block_rows // seq_count, most_cols), LOW)
    for shift in range(1, seq_count):
        moves.start(
            moves.move(
                (PATCHES, shift),
                lambda shift=shift: {PATCHES: lax.rem(lax.axis_index(PATCHES) + shift, seq_count)},
                grad_low,
                lambda shift=shift: row_part(shift),
                grad_rows,
                lambda: (lax.axis_index(PATCHES),),
                later=True,
            )
        )
    moves.start_local(
        moves.keep(grad_low, lambda: row_part(0), grad_rows, lambda: (lax.axis_index(PATCHES),), True)
    )
    moves.task(
        lambda ref: newton_schulz(
            *[ref(item) for item in (source, gram, poly, once, gram_low, poly_low, once_low, state, state_next)]
        )
    )

    update_moves = []
    for shift in range(1, seq_count):
        update_moves.append(
            moves.move(
                (PATCHES, shift),
                lambda shift=shift: {PATCHES: lax.rem(lax.axis_index(PATCHES) + shift, seq_count)},
                state,
                functools.partial(row_part, shift),
                update,
                lambda: (lax.axis_index(PATCHES),),
                later=True,
            )
        )
        moves.start(update_moves[-1])

    def keep_rows(ref):
        ref(update)[lax.axis_index(PATCHES)] = ref(state)[row_part(0)]

    moves.task(keep_rows)

    def renew(ref):
        for which, (master, _) in enumerate(master_loads):
            cols = group_cols[which]
            rate = RATE_MUON * 0.2 * math.sqrt(masters[which].shape[1] * shards)
            for part in range(members):
                at = (slice(None), pl.ds(part * cols, cols))
                value = ref(update)[which * members + part, :, pl.ds(0, cols)].astype(f32)
                value = ref(master)[at] * (1.0 - RATE_MUON * DECAY_MUON) - rate * value
                ref(fresh[which])[at] = value
                ref(fresh_low[which])[at] = value.astype(LOW)

    for number in update_moves:
        moves.wait_for(number)
    for _, number in master_loads:
        moves.wait_local(number)
    moves.task(renew)

    rows = block_rows // seq_count

    def row_place(back_group):
        who = lax.axis_index(PATCHES) - back_group * members
        return (pl.ds(pl.multiple_of(who * rows, rows), rows),)

    def has_group(offset):
        place = lax.axis_index(PATCHES) // members + offset
        return jnp.logical_and(place >= 0, place < MATRICES)

    def member_copies(source, source_at, target, target_at, after, there):
        for shift in range(1, members):
            moves.move(
                (PATCHES, members, shift),
                functools.partial(member_peer, members, shift),
                source,
                source_at,
                target,
                target_at,
                after,
                there,
                there,
                later=True,
            )
            if not after:
                moves.start(len(moves.moves) - 1)

    places = []
    for item_from in fresh_low:
        item_to = moves.output((rows * seq_count, moves.shape(item_from)[1]), LOW)
        own = functools.partial(row_place, 0)
        moves.start_local(moves.keep(item_from, None, item_to, own, True))
        places.append((item_from, item_to, {}))

    def along_line(distance, way, source, target, numbers):
        both = lambda: jnp.logical_and(has_group(way), has_group(-distance * way))
        place = functools.partial(row_place, distance * way)
        numbers[way] = moves.move(
            (PATCHES, seq_count, way),
            functools.partial(group_peer, members, (MATRICES + way) % MATRICES),
            target if distance else source,
            place if distance else None,
            target,
            place,
            (numbers[way],) if distance else (),
            both,
            functools.partial(has_group, -(distance + 1) * way),
            later=True,
        )
        if not distance:
            moves.start(numbers[way])

    for item_from, item_to, numbers in places:
        for way in (1, -1):
            along_line(0, way, item_from, item_to, numbers)
    for item_from, item_to, numbers in places:
        member_copies(item_from, None, item_to, own, (), None)
    for distance in range(1, MATRICES):
        for item_from, item_to, numbers in places:
            for way in (1, -1):
                number = numbers[way]
                if distance < MATRICES - 1:
                    along_line(distance, way, item_from, item_to, numbers)
                place = functools.partial(row_place, distance * way)
                member_copies(
                    item_to, place, item_to, place, (number,), functools.partial(has_group, -distance * way)
                )
    sums, grad_ada, grad_table_all, io_slices, *rest = moves.run()
    fresh, grad_rows, copies = rest[:MATRICES], rest[MATRICES], rest[MATRICES + 1 :]
    sums = sums[0]
    grad_norm = jnp.sqrt(sums[0])
    loss_total = sums[1]
    clip = jnp.minimum(1.0, CLIP_LIMIT / (grad_norm + 1e-06))
    terms = sums[2 : 2 + 3 * MATRICES].reshape(MATRICES, 3)
    size_squares = MOMENTUM * MOMENTUM * terms[:, 0] + 2.0 * MOMENTUM * clip * terms[:, 1] + clip * clip * terms[:, 2]
    sizes = jnp.sqrt(jnp.maximum(size_squares, 0.0))
    moment_sizes = jnp.stack([sizes[which] for which in (0, 3, 1, 2)]) / CLIP_LIMIT
    moments = [
        MOMENTUM * old
        + clip
        * jnp.concatenate(
            [grad_rows[which * members + part, :, : group_cols[which]] for part in range(members)], -1
        ).astype(f32)
        for which, old in enumerate(momenta)
    ]
    grad_table = lax.dynamic_slice_in_dim(grad_table_all[:table_rows], shard * table_cols, table_cols, 1)
    grad_bias_all = jnp.concatenate([tail_all[:, 8].reshape(-1), tail_all[:, 9, :table_cols].reshape(-1)])
    grad_bias = lax.dynamic_slice_in_dim(grad_bias_all, shard * biases.shape[0], biases.shape[0])
    io_grad = io_slices.reshape(2, padded, io_cols)[:, :values_count].astype(f32)
    ada_res = adam_update(ada_master, ada_first, ada_second, clip * grad_ada, RATE_ADAM)
    io_res = adam_update(io_proj, io_first, io_second, clip * io_grad, RATE_ADAM)
    cond_res = adam_update(cond_table, cond_first, cond_second, clip * grad_table, RATE_TABLE)
    pos_res = adam_update(pos_table, pos_first, pos_second, clip * grad_pos, RATE_TABLE)
    bias_res = adam_update(biases, bias_first, bias_second, clip * grad_bias, RATE_ADAM)
    matrices = []
    for which in (0, 3, 1, 2):
        matrices += [fresh[which], moments[which], copies[which]]
    return (loss_total, grad_norm, moment_sizes, *matrices, *ada_res, *io_res, *cond_res, *pos_res, *bias_res)


def fits_fast(mesh):
    seq, shards = mesh.shape[PATCHES], mesh.shape[SHARDS]
    return HEADS % seq == 0 and (HEADS // seq * HEAD) % LANES == 0 and seq % MATRICES == 0 and shards % 2 == 0


def solution(mesh):
    body = fast_body if fits_fast(mesh) else general_body
    return jax.shard_map(
        body,
        mesh=mesh,
        in_specs=(
            P(SHARDS, PATCHES, None),
            P(SHARDS, PATCHES, None),
            P(SHARDS),
            P(),
            P(None, SHARDS),
            P(PATCHES, SHARDS),
            P(PATCHES, SHARDS),
            P(None, SHARDS),
            P(PATCHES, SHARDS),
            P(PATCHES, SHARDS),
            P(None, SHARDS),
            P(PATCHES, SHARDS),
            P(PATCHES, SHARDS),
            P(None, SHARDS),
            P(PATCHES, SHARDS),
            P(PATCHES, SHARDS),
            P(None, SHARDS),
            P(PATCHES, SHARDS),
            P(PATCHES, SHARDS),
            P(PATCHES, SHARDS),
            P(None, None, SHARDS),
            P(None, None, SHARDS),
            P(None, None, SHARDS),
            P(None, SHARDS),
            P(None, SHARDS),
            P(None, SHARDS),
            P(PATCHES, SHARDS),
            P(PATCHES, SHARDS),
            P(PATCHES, SHARDS),
            P(SHARDS),
            P(SHARDS),
            P(SHARDS),
        ),
        out_specs=(
            P(),
            P(),
            P(),
            P(PATCHES, SHARDS),
            P(PATCHES, SHARDS),
            P(None, SHARDS),
            P(PATCHES, SHARDS),
            P(PATCHES, SHARDS),
            P(None, SHARDS),
            P(PATCHES, SHARDS),
            P(PATCHES, SHARDS),
            P(None, SHARDS),
            P(PATCHES, SHARDS),
            P(PATCHES, SHARDS),
            P(None, SHARDS),
            P(PATCHES, SHARDS),
            P(PATCHES, SHARDS),
            P(PATCHES, SHARDS),
            P(None, None, SHARDS),
            P(None, None, SHARDS),
            P(None, None, SHARDS),
            P(None, SHARDS),
            P(None, SHARDS),
            P(None, SHARDS),
            P(PATCHES, SHARDS),
            P(PATCHES, SHARDS),
            P(PATCHES, SHARDS),
            P(SHARDS),
            P(SHARDS),
            P(SHARDS),
        ),
        check_vma=False,
    )
```

```python
import functools
import math

import jax
import jax.numpy as jnp
from jax import lax
from jax.experimental import pallas as pl
from jax.experimental.pallas import tpu as pltpu
from jax.sharding import PartitionSpec as P

PATCHES = "seq"
SHARDS = "fsdp"
HEADS = 16
HEAD = 64
NI = 3
ROLL = 2
NS_ITERS = 5
STEP_NUM = 10
LON = 32


EPS_NORM = 1e-06
NS_A = 3.4445
NS_B = -4.775
NS_C = 2.0315
MOMENTUM = 0.5
RATE_MUON = 0.15
DECAY_MUON = 0.1
RATE_ADAM = 0.05
RATE_TABLE = 0.5
DECAY_ADAM = 0.1
BETA_FIRST = 0.9
BETA_SECOND = 0.95
CLIP_LIMIT = 0.01
HIGHEST_PRECISION = lax.Precision.HIGHEST


def broadcast(block, axis, owner):
    block = jnp.where(lax.axis_index(axis) == owner, block, jnp.zeros_like(block))
    return lax.psum(block, axis)


def product(left, right):
    return jnp.dot(left, right, preferred_element_type=jnp.float32)


def dot_last(left, right):
    return lax.dot_general(
        left, right, (((left.ndim - 1,), (1,)), ((), ())), preferred_element_type=jnp.float32
    )


def rows_product(left, right):
    flat_left = left.reshape(-1, left.shape[-1])
    flat_right = right.reshape(-1, right.shape[-1])
    return lax.dot_general(
        flat_left, flat_right, (((0,), (0,)), ((), ())), preferred_element_type=jnp.float32
    )


def layer_norm(values):
    centred = values - jnp.mean(values, -1, keepdims=True)
    inverse = lax.rsqrt(jnp.mean(centred * centred, -1, keepdims=True) + EPS_NORM)
    return (centred * inverse, inverse)


def norm_back(grad, normed, inverse):
    return inverse * (
        grad
        - jnp.mean(grad, -1, keepdims=True)
        - normed * jnp.mean(grad * normed, -1, keepdims=True)
    )


def heads_view(values):
    return values.reshape(values.shape[0], values.shape[1], HEADS, HEAD)


def modulation(modul, width):
    return [modul[:, None, column * width : (column + 1) * width] for column in range(6)]


def latitude_weights(local):
    all_patches = local * lax.axis_size(PATCHES)
    band_row = (jnp.arange(all_patches, dtype=jnp.int32) // LON).astype(jnp.float32)
    latitude = (band_row + 0.5) * (math.pi / (all_patches // LON)) - math.pi / 2
    cosine = jnp.cos(latitude)
    weights = cosine / jnp.mean(cosine)
    return lax.dynamic_slice_in_dim(weights, lax.axis_index(PATCHES) * local, local)


def forward_step(weights, state, active, select):
    w_qkv, w_out, w_up, w_down, w_ada, io_all, table, pos, bias = weights
    width = w_out.shape[0]
    cond_vec = jnp.dot(select, table.astype(jnp.float32), precision=HIGHEST_PRECISION)
    silu_low = jax.nn.silu(cond_vec).astype(jnp.bfloat16)
    modul = product(silu_low, w_ada) + bias[: 6 * width].astype(jnp.float32)
    shift1, scale1, gate1, shift2, scale2, gate2 = modulation(modul, width)
    state_low = state.astype(jnp.bfloat16)
    embedded = (
        product(state_low, io_all[0])
        + bias[6 * width :].astype(jnp.float32)
        + pos.astype(jnp.float32)
    )
    normed_one, inverse_one = layer_norm(embedded)
    normed_a = (normed_one * (1.0 + scale1) + shift1).astype(jnp.bfloat16)
    qkv = product(normed_a, w_qkv).astype(jnp.bfloat16)
    queries = qkv[..., :width]
    keys, values = (
        lax.all_gather(qkv[..., width : 2 * width], PATCHES, axis=1, tiled=True),
        lax.all_gather(qkv[..., 2 * width :], PATCHES, axis=1, tiled=True),
    )
    scores = jnp.einsum(
        "sphd,snhd->shpn", heads_view(queries), heads_view(keys), preferred_element_type=jnp.float32
    ) * HEAD ** (-0.5)
    top_score = jnp.max(scores, -1, keepdims=True)
    expo = jnp.exp(scores - top_score)
    total_exp = jnp.sum(expo, -1, keepdims=True)
    log_total = top_score + jnp.log(total_exp)
    probs_low = (expo / total_exp).astype(jnp.bfloat16)
    mixed = jnp.einsum(
        "shpn,snhd->sphd", probs_low, heads_view(values), preferred_element_type=jnp.float32
    )
    mixed_low = mixed.reshape(queries.shape).astype(jnp.bfloat16)
    attended = product(mixed_low, w_out)
    after_attn = embedded + gate1 * attended
    normed_two, inverse_two = layer_norm(after_attn)
    normed_b = (normed_two * (1.0 + scale2) + shift2).astype(jnp.bfloat16)
    upward = product(normed_b, w_up)
    hidden = jax.nn.gelu(upward).astype(jnp.bfloat16)
    downward = dot_last(hidden, w_down)
    after_mlp = after_attn + gate2 * downward
    normed_three, inverse_three = layer_norm(after_mlp)
    normed_c = normed_three.astype(jnp.bfloat16)
    delta = dot_last(normed_c, io_all[1])
    kept = (
        cond_vec,
        silu_low,
        modul,
        state_low,
        normed_one,
        inverse_one,
        normed_a,
        queries,
        keys,
        values,
        log_total,
        mixed_low,
        attended,
        normed_two,
        inverse_two,
        normed_b,
        upward,
        hidden,
        downward,
        normed_three,
        inverse_three,
        normed_c,
    )
    return (state + active * delta, kept)


def backward_step(weights, kept, grad_state, active, select):
    w_qkv, w_out, w_up, w_down, w_ada, io_all, table, pos, bias = weights
    (
        cond_vec,
        silu_low,
        modul,
        state_low,
        normed_one,
        inverse_one,
        normed_a,
        queries,
        keys,
        values,
        log_total,
        mixed_low,
        attended,
        normed_two,
        inverse_two,
        normed_b,
        upward,
        hidden,
        downward,
        normed_three,
        inverse_three,
        normed_c,
    ) = kept
    width = w_out.shape[0]
    shift1, scale1, gate1, shift2, scale2, gate2 = modulation(modul, width)
    delta_grad = (active * grad_state).astype(jnp.bfloat16)
    grad_head = rows_product(delta_grad, normed_c)
    grad_mlp = norm_back(product(delta_grad, io_all[1]), normed_three, inverse_three)
    grad_gate2 = jnp.sum(grad_mlp * downward, 1)
    down_grad = (gate2 * grad_mlp).astype(jnp.bfloat16)
    grad_down = rows_product(down_grad, hidden)
    grad_hidden = product(down_grad, w_down)
    up_grad = jax.vjp(jax.nn.gelu, upward)[1](grad_hidden)[0].astype(jnp.bfloat16)
    grad_up = rows_product(normed_b, up_grad)
    grad_normed_b = dot_last(up_grad, w_up)
    grad_scale2 = jnp.sum(grad_normed_b * normed_two, 1)
    grad_shift2 = jnp.sum(grad_normed_b, 1)
    grad_attn = grad_mlp + norm_back(grad_normed_b * (1.0 + scale2), normed_two, inverse_two)
    grad_gate1 = jnp.sum(grad_attn * attended, 1)
    attn_grad = (gate1 * grad_attn).astype(jnp.bfloat16)
    grad_out = rows_product(mixed_low, attn_grad)
    mixed_grad = dot_last(attn_grad, w_out).astype(jnp.bfloat16)
    q_heads = heads_view(queries)
    k_heads = heads_view(keys)
    v_heads = heads_view(values)
    g_heads = heads_view(mixed_grad)
    scores = jnp.einsum(
        "sphd,snhd->shpn", q_heads, k_heads, preferred_element_type=jnp.float32
    ) * HEAD ** (-0.5)
    probs = jnp.exp(scores - log_total)
    probs_low = probs.astype(jnp.bfloat16)
    grad_probs = jnp.einsum("sphd,snhd->shpn", g_heads, v_heads, preferred_element_type=jnp.float32)
    score_grad = (
        HEAD ** (-0.5) * probs * (grad_probs - jnp.sum(grad_probs * probs, -1, keepdims=True))
    ).astype(jnp.bfloat16)
    grad_queries = jnp.einsum(
        "shpn,snhd->sphd", score_grad, k_heads, preferred_element_type=jnp.float32
    ).reshape(queries.shape)
    key_part = jnp.einsum(
        "shpn,sphd->snhd", score_grad, q_heads, preferred_element_type=jnp.float32
    ).reshape(keys.shape)
    value_part = jnp.einsum(
        "shpn,sphd->snhd", probs_low, g_heads, preferred_element_type=jnp.float32
    ).reshape(values.shape)
    grad_keys, grad_values = (
        lax.psum_scatter(key_part, PATCHES, scatter_dimension=1, tiled=True),
        lax.psum_scatter(value_part, PATCHES, scatter_dimension=1, tiled=True),
    )
    qkv_grad = jnp.concatenate([grad_queries, grad_keys, grad_values], -1).astype(jnp.bfloat16)
    grad_qkv = rows_product(normed_a, qkv_grad)
    grad_normed_a = dot_last(qkv_grad, w_qkv)
    grad_scale1 = jnp.sum(grad_normed_a * normed_one, 1)
    grad_shift1 = jnp.sum(grad_normed_a, 1)
    grad_embedded = grad_attn + norm_back(grad_normed_a * (1.0 + scale1), normed_one, inverse_one)
    embed_grad = grad_embedded.astype(jnp.bfloat16)
    grad_embed = rows_product(state_low, embed_grad)
    grad_prev = grad_state + dot_last(embed_grad, io_all[0])
    grad_modul = jnp.concatenate(
        [grad_shift1, grad_scale1, grad_gate1, grad_shift2, grad_scale2, grad_gate2], -1
    )
    grad_ada = lax.dot_general(
        silu_low.astype(jnp.float32),
        grad_modul,
        (((0,), (0,)), ((), ())),
        precision=HIGHEST_PRECISION,
    )
    grad_silu = lax.dot_general(
        grad_modul, w_ada.astype(jnp.float32), (((1,), (1,)), ((), ())), precision=HIGHEST_PRECISION
    )
    grad_cond = jax.vjp(jax.nn.silu, cond_vec)[1](grad_silu)[0]
    grad_table = lax.dot_general(
        select, grad_cond, (((0,), (0,)), ((), ())), precision=HIGHEST_PRECISION
    )
    grad_bias = jnp.concatenate([jnp.sum(grad_modul, 0), jnp.sum(grad_embedded, (0, 1))])
    grad_pos = jnp.sum(grad_embedded, 0)
    grads = (
        grad_qkv,
        grad_out,
        grad_up,
        grad_down,
        grad_ada,
        jnp.stack([grad_embed, grad_head]),
        grad_table,
        grad_pos,
        grad_bias,
    )
    return (grad_prev, grads)


def gram_part(block_cols):
    return lax.dot_general(
        block_cols, block_cols, (((1,), (1,)), ((), ())), preferred_element_type=jnp.float32
    )


def zero_gram(block_cols):
    return jnp.zeros((block_cols.shape[0], block_cols.shape[0]), jnp.float32)


def newton_step(block_cols, gram):
    gram_low = gram.astype(jnp.bfloat16)
    poly = (NS_B * gram_low.astype(jnp.float32) + NS_C * product(gram_low, gram_low)).astype(
        jnp.bfloat16
    )
    return (NS_A * block_cols.astype(jnp.float32) + product(poly, block_cols)).astype(jnp.bfloat16)


def keep_block(block_cols, gram):
    return block_cols


def adam_update(weight, first, second, grad, rate):
    first_new = BETA_FIRST * first + (1.0 - BETA_FIRST) * grad
    second_new = BETA_SECOND * second + (1.0 - BETA_SECOND) * grad * grad
    unbiased = first_new / (1.0 - BETA_FIRST**STEP_NUM)
    spread = jnp.sqrt(second_new / (1.0 - BETA_SECOND**STEP_NUM)) + 1e-08
    return (weight * (1.0 - rate * DECAY_ADAM) - rate * unbiased / spread, first_new, second_new)


def general_body(
    states,
    targets,
    lengths,
    intervals,
    qkv_copy,
    qkv_master,
    qkv_moment,
    out_copy,
    out_master,
    out_moment,
    up_copy,
    up_master,
    up_moment,
    down_copy,
    down_master,
    down_moment,
    ada_copy,
    ada_master,
    ada_first,
    ada_second,
    io_proj,
    io_first,
    io_second,
    cond_table,
    cond_first,
    cond_second,
    pos_table,
    pos_first,
    pos_second,
    biases,
    bias_first,
    bias_second,
):
    weights = (
        lax.all_gather(qkv_copy, SHARDS, axis=1, tiled=True),
        lax.all_gather(out_copy, SHARDS, axis=1, tiled=True),
        lax.all_gather(up_copy, SHARDS, axis=1, tiled=True),
        lax.all_gather(down_copy, SHARDS, axis=1, tiled=True),
        lax.all_gather(ada_copy, SHARDS, axis=1, tiled=True),
        lax.all_gather(io_proj.astype(jnp.bfloat16), SHARDS, axis=2, tiled=True),
        lax.all_gather(cond_table.astype(jnp.bfloat16), SHARDS, axis=1, tiled=True),
        lax.all_gather(pos_table.astype(jnp.bfloat16), SHARDS, axis=1, tiled=True),
        lax.all_gather(biases.astype(jnp.bfloat16), SHARDS, axis=0, tiled=True),
    )
    samples, local, values_count = states.shape
    table_rows = cond_table.shape[0]
    my_ids = lax.dynamic_slice_in_dim(intervals, lax.axis_index(SHARDS) * samples, samples)
    counts = jnp.sum(
        (intervals[:, None] == jnp.arange(NI, dtype=jnp.int32)[None]).astype(jnp.float32), 0
    )
    id_counts = jnp.sum(
        (my_ids[:, None] == jnp.arange(NI, dtype=jnp.int32)[None]).astype(jnp.float32)
        * counts[None],
        1,
    )
    weight = 1.0 / (NI * local * lax.axis_size(PATCHES) * values_count * id_counts)
    rows_iota = jnp.arange(table_rows, dtype=jnp.int32)
    id_select = (my_ids[:, None] == rows_iota[None]).astype(jnp.float32)
    state = states.astype(jnp.float32)
    seen_states = []
    kept_all = []
    for step in range(ROLL):
        select = id_select + (rows_iota == NI + step).astype(jnp.float32)[None]
        active = (step < lengths).astype(jnp.float32)[:, None, None]
        seen_states.append(state)
        state, kept = forward_step(weights, state, active, select)
        kept_all.append(kept)
    lat = latitude_weights(local)
    diff = state - targets.astype(jnp.float32)
    err = jnp.sum(jnp.sum(diff * diff, -1) * lat[None], -1)
    loss_local = jnp.sum(weight * err)
    grad_state = 2.0 * weight[:, None, None] * lat[None, :, None] * diff
    totals = None
    for step in reversed(range(ROLL)):
        select = id_select + (rows_iota == NI + step).astype(jnp.float32)[None]
        active = (step < lengths).astype(jnp.float32)[:, None, None]
        kept = kept_all[step]
        grad_state, grads = backward_step(weights, kept, grad_state, active, select)
        totals = grads if totals is None else jax.tree.map(jnp.add, totals, grads)
    reduced = (
        lax.psum_scatter(totals[0], SHARDS, scatter_dimension=1, tiled=True),
        lax.psum_scatter(totals[1], SHARDS, scatter_dimension=1, tiled=True),
        lax.psum_scatter(totals[2], SHARDS, scatter_dimension=1, tiled=True),
        lax.psum_scatter(totals[3], SHARDS, scatter_dimension=1, tiled=True),
        lax.psum_scatter(totals[4], SHARDS, scatter_dimension=1, tiled=True),
        lax.psum_scatter(totals[5], SHARDS, scatter_dimension=2, tiled=True),
        lax.psum_scatter(totals[6], SHARDS, scatter_dimension=1, tiled=True),
        lax.psum_scatter(totals[7], SHARDS, scatter_dimension=1, tiled=True),
        lax.psum_scatter(totals[8], SHARDS, scatter_dimension=0, tiled=True),
    )
    large = (
        lax.psum_scatter(reduced[0], PATCHES, scatter_dimension=0, tiled=True),
        lax.psum_scatter(reduced[1], PATCHES, scatter_dimension=0, tiled=True),
        lax.psum_scatter(reduced[2], PATCHES, scatter_dimension=0, tiled=True),
        lax.psum_scatter(reduced[3], PATCHES, scatter_dimension=0, tiled=True),
        lax.psum_scatter(reduced[4], PATCHES, scatter_dimension=0, tiled=True),
    )
    small = lax.psum((reduced[5], reduced[6], reduced[8]), PATCHES)
    grad_pos = reduced[7]
    first_copy = (lax.axis_index(PATCHES) == 0).astype(jnp.float32)
    squares = jnp.sum(grad_pos * grad_pos)
    for item in large:
        squares = squares + jnp.sum(item * item)
    small_squares = jnp.float32(0.0)
    for item in small:
        small_squares = small_squares + jnp.sum(item * item)
    squares, loss_total = lax.psum(
        (squares + first_copy * small_squares, loss_local), (PATCHES, SHARDS)
    )
    grad_norm = jnp.sqrt(squares)
    clip = jnp.minimum(1.0, CLIP_LIMIT / (grad_norm + 1e-06))
    masters = (qkv_master, out_master, up_master, down_master)
    moments = [
        MOMENTUM * old + clip * grad
        for old, grad in zip((qkv_moment, out_moment, up_moment, down_moment), large[:4])
    ]
    norms = lax.psum(
        (
            jnp.sum(moments[0] * moments[0]),
            jnp.sum(moments[1] * moments[1]),
            jnp.sum(moments[2] * moments[2]),
            jnp.sum(moments[3] * moments[3]),
        ),
        (PATCHES, SHARDS),
    )
    sizes = [jnp.sqrt(norms[which]) for which in range(4)]
    moment_sizes = jnp.stack(sizes) / CLIP_LIMIT
    scaled = [(moments[which] / (sizes[which] + 1e-07)).astype(jnp.bfloat16) for which in range(4)]
    columns = (
        lax.all_gather(scaled[0], PATCHES, axis=0, tiled=True),
        lax.all_gather(scaled[1], PATCHES, axis=0, tiled=True),
        lax.all_gather(scaled[2], PATCHES, axis=0, tiled=True),
        lax.all_gather(scaled[3], PATCHES, axis=0, tiled=True),
    )
    seq_index = lax.axis_index(PATCHES)
    seq_count = lax.axis_size(PATCHES)
    owners = [seq_index == which % seq_count for which in range(4)]
    blocks = list(columns)
    for turn in range(NS_ITERS):
        partial_value = [
            lax.cond(owners[which], gram_part, zero_gram, blocks[which]) for which in range(4)
        ]
        grams = lax.psum(
            (partial_value[0], partial_value[1], partial_value[2], partial_value[3]), SHARDS
        )
        blocks = [
            lax.cond(owners[which], newton_step, keep_block, blocks[which], grams[which])
            for which in range(4)
        ]
    blocks = [broadcast(blocks[which], PATCHES, which % seq_count) for which in range(4)]
    row_count = qkv_master.shape[0]
    fresh = []
    for which in range(4):
        my_rows = lax.dynamic_slice_in_dim(
            blocks[which], seq_index * row_count, row_count, 0
        ).astype(jnp.float32)
        all_cols = masters[which].shape[1] * lax.axis_size(SHARDS)
        fresh.append(
            masters[which] * (1.0 - RATE_MUON * DECAY_MUON)
            - RATE_MUON * 0.2 * math.sqrt(all_cols) * my_rows
        )
    copies = (
        lax.all_gather(fresh[0].astype(jnp.bfloat16), PATCHES, axis=0, tiled=True),
        lax.all_gather(fresh[1].astype(jnp.bfloat16), PATCHES, axis=0, tiled=True),
        lax.all_gather(fresh[2].astype(jnp.bfloat16), PATCHES, axis=0, tiled=True),
        lax.all_gather(fresh[3].astype(jnp.bfloat16), PATCHES, axis=0, tiled=True),
    )
    ada_res = adam_update(ada_master, ada_first, ada_second, clip * large[4], RATE_ADAM)
    io_res = adam_update(io_proj, io_first, io_second, clip * small[0], RATE_ADAM)
    cond_res = adam_update(cond_table, cond_first, cond_second, clip * small[1], RATE_TABLE)
    pos_res = adam_update(pos_table, pos_first, pos_second, clip * grad_pos, RATE_TABLE)
    bias_res = adam_update(biases, bias_first, bias_second, clip * small[2], RATE_ADAM)
    return (
        loss_total,
        grad_norm,
        moment_sizes,
        fresh[0],
        moments[0],
        copies[0],
        fresh[1],
        moments[1],
        copies[1],
        fresh[2],
        moments[2],
        copies[2],
        fresh[3],
        moments[3],
        copies[3],
        ada_res[0],
        ada_res[1],
        ada_res[2],
        io_res[0],
        io_res[1],
        io_res[2],
        cond_res[0],
        cond_res[1],
        cond_res[2],
        pos_res[0],
        pos_res[1],
        pos_res[2],
        bias_res[0],
        bias_res[1],
        bias_res[2],
    )


LANES = 128
MATRICES = 4
LOW = jnp.bfloat16
MESH = pl.DeviceIdType.MESH


def round_up(value, unit):
    return -(-value // unit) * unit


def member_peer(members, shift):
    index = lax.axis_index(PATCHES)
    return {PATCHES: index // members * members + lax.rem(lax.rem(index, members) + shift, members)}


def group_peer(members, shift):
    return {PATCHES: lax.rem(lax.axis_index(PATCHES) + shift * members, lax.axis_size(PATCHES))}


def sibling_peer():
    index = lax.axis_index(SHARDS)
    return {SHARDS: index + 1 - 2 * lax.rem(index, 2)}


def where(condition, action):
    if condition is None:
        action()
    else:
        pl.when(condition())(action)


class Moves:
    def __init__(self, name, ids, vmem=None):
        self.name = name
        self.ids = ids
        self.vmem = vmem
        self.operands = []
        self.operand_specs = []
        self.outputs = []
        self.output_specs = []
        self.scratches = []
        self.moves = []
        self.locals = []
        self.steps = []
        self.peers = {}

    def operand(self, array, space=pl.ANY):
        self.operands.append(array)
        self.operand_specs.append(pl.BlockSpec(memory_space=space))
        return (0, len(self.operands) - 1)

    def output(self, shape, dtype, space=pl.ANY):
        self.outputs.append(jax.ShapeDtypeStruct(shape, dtype))
        self.output_specs.append(pl.BlockSpec(memory_space=space))
        return (1, len(self.outputs) - 1)

    def scratch(self, shape, dtype):
        self.scratches.append(pltpu.VMEM(shape, dtype))
        return (2, len(self.scratches) - 1)

    def keep(self, source, source_at, target, target_at, later=False):
        self.locals.append((source, source_at, target, target_at, later))
        return len(self.locals) - 1

    def shape(self, scratch):
        return self.scratches[scratch[1]].shape

    def load(self, array):
        target = self.scratch(array.shape, array.dtype)
        return target, self.keep(self.operand(array), None, target, None)

    def save(self, source, shape, dtype):
        number = self.keep(source, None, self.output(shape, dtype), None, True)
        return number

    def start_local(self, number):
        self.steps.append((self.begin_local, number))

    def begin_local(self, number):
        self.local[number].start()

    def move(
        self, peer_key, peer, source, source_at, target, target_at, after=(), sends=None, takes=None, later=False
    ):
        number = len(self.moves)
        self.peers.setdefault(peer_key, peer)
        self.moves.append((peer_key, source, source_at, target, target_at, sends, takes, later or bool(after)))
        for earlier in after:
            self.steps.append((self.await_move, earlier))
        if after:
            self.steps.append((self.start_move, number))
        return number

    def wait_for(self, number):
        self.steps.append((self.await_move, number))

    def start(self, number):
        self.steps.append((self.start_move, number))

    def wait_local(self, number):
        self.steps.append((self.await_local, number))

    def task(self, action):
        self.steps.append((self.do_task, action))

    def await_move(self, number):
        if number not in self.arrived:
            self.arrived.add(number)
            where(self.moves[number][6], self.remote[number].wait_recv)

    def start_move(self, number):
        where(self.moves[number][5], self.remote[number].start)

    def await_local(self, number):
        if number not in self.kept:
            self.kept.add(number)
            self.local[number].wait()

    def do_task(self, action):
        action(self.ref)

    def ref(self, which):
        return self.refs[which[0]][which[1]]

    def view(self, which, index):
        ref = self.ref(which)
        return ref.at[index()] if index is not None else ref

    def kernel(self, *refs):
        sizes = (len(self.operands), len(self.outputs), len(self.scratches))
        self.refs = (refs[: sizes[0]], refs[sizes[0] : sizes[0] + sizes[1]], refs[sizes[0] + sizes[1] : sum(sizes)])
        local_sem, send_sem, recv_sem = refs[sum(sizes) :]
        self.arrived, self.kept = set(), set()
        devices = {key: peer() for key, peer in self.peers.items()}
        barrier = pltpu.get_barrier_semaphore()
        for device in devices.values():
            pl.semaphore_signal(barrier, inc=1, device_id=device, device_id_type=MESH)
        pl.semaphore_wait(barrier, len(devices))
        self.remote = []
        for number, (key, source, source_at, target, target_at, _, _, later) in enumerate(self.moves):
            self.remote.append(
                pltpu.make_async_remote_copy(
                    src_ref=self.view(source, source_at),
                    dst_ref=self.view(target, target_at),
                    send_sem=send_sem.at[number],
                    recv_sem=recv_sem.at[number],
                    device_id=devices[key],
                    device_id_type=MESH,
                )
            )
            if not later:
                self.start_move(number)
        self.local = [
            pltpu.make_async_copy(self.view(source, source_at), self.view(target, target_at), local_sem.at[number])
            for number, (source, source_at, target, target_at, _) in enumerate(self.locals)
        ]
        for copy, entry in zip(self.local, self.locals):
            if not entry[4]:
                copy.start()
        for action, number in self.steps:
            action(number)
        for number in range(len(self.locals)):
            self.await_local(number)
        for number, copy in enumerate(self.remote):
            self.await_move(number)
            where(self.moves[number][5], copy.wait_send)

    def run(self):
        return pl.pallas_call(
            self.kernel,
            out_shape=self.outputs,
            in_specs=self.operand_specs,
            out_specs=self.output_specs,
            scratch_shapes=[
                *self.scratches,
                pltpu.SemaphoreType.DMA((max(1, len(self.locals)),)),
                pltpu.SemaphoreType.DMA((len(self.moves),)),
                pltpu.SemaphoreType.DMA((len(self.moves),)),
            ],
            compiler_params=pltpu.CompilerParams(
                collective_id=self.ids.setdefault(self.name, len(self.ids)),
                has_side_effects=True,
                vmem_limit_bytes=self.vmem,
            ),
            name=self.name,
        )(*self.operands)

    def along(self, axis, source, target, pairs, later=False):
        numbers = []
        count = lax.axis_size(axis)

        def other(shift):
            return lax.rem(lax.axis_index(axis) + shift, count)

        for shift in range(1, count):
            for source_at, target_at in pairs:
                numbers.append(
                    self.move(
                        (axis, shift),
                        lambda shift=shift: {axis: other(shift)},
                        source,
                        None if source_at is None else (lambda at=source_at, shift=shift: at(other(shift))),
                        target,
                        lambda at=target_at: at(lax.axis_index(axis)),
                        later=later,
                    )
                )
        for source_at, target_at in pairs:
            local = self.keep(
                source,
                None if source_at is None else (lambda at=source_at: at(lax.axis_index(axis))),
                target,
                lambda at=target_at: at(lax.axis_index(axis)),
                later,
            )
            if later:
                self.start_local(local)
        if later:
            for number in numbers:
                self.start(number)
        return numbers

    def gather(self, axis, array):
        target = self.output((lax.axis_size(axis),) + array.shape, array.dtype)
        self.along(axis, self.operand(array), target, [(None, lambda sender: (sender,))])

    def gather_pairs(self, array, parts=1, hold=False):
        shards = lax.axis_size(SHARDS)
        source = self.operand(array)
        target = self.output((shards,) + array.shape, array.dtype)
        rows = array.shape[0] // parts

        def place(back_pair, part):
            return (lax.rem(lax.axis_index(SHARDS) + shards - 2 * back_pair, shards), pl.ds(part * rows, rows))

        firsts = []
        for part in range(parts):
            for pair in range(1, shards // 2):
                number = self.move(
                    (SHARDS, 2 * pair),
                    lambda pair=pair: {SHARDS: lax.rem(lax.axis_index(SHARDS) + 2 * pair, shards)},
                    source,
                    lambda part=part: (pl.ds(part * rows, rows),),
                    target,
                    functools.partial(place, 0, part),
                )
                firsts.append((functools.partial(place, pair, part), number))
        own = lambda: (lax.axis_index(SHARDS),)
        self.move((SHARDS,), sibling_peer, source, None, target, own)
        self.keep(source, None, target, own)
        waiting = [(target, at, number) for at, number in firsts]
        if hold:
            return waiting
        self.to_sibling(waiting)

    def gather_columns(self, axis, array, target):
        width = array.shape[-1]
        lead = (slice(None),) * (array.ndim - 1)
        numbers = self.along(
            axis,
            self.operand(array),
            target,
            [(None, lambda sender: lead + (pl.ds(pl.multiple_of(sender * width, LANES), width),))],
        )
        return numbers, len(self.locals) - 1

    def gather_twice(self, arrays, members, chunks):
        shards = lax.axis_size(SHARDS)
        entries = []
        for array, pieces in zip(arrays, chunks):
            source = self.operand(array)
            width = array.shape[1]
            target = self.scratch((array.shape[0], shards * width), array.dtype)
            rows = array.shape[0] // members // pieces

            def columns(back_pair, width=width):
                who = lax.rem(lax.axis_index(SHARDS) + shards - 2 * back_pair, shards)
                return pl.ds(pl.multiple_of(who * width, LANES), width)

            def piece_rows(back_member, piece, rows=rows, pieces=pieces):
                index = lax.rem(lax.rem(lax.axis_index(PATCHES), members) + members - back_member, members)
                return pl.ds(pl.multiple_of((index * pieces + piece) * rows, rows), rows)

            def place(back_member, back_pair, piece, columns=columns, piece_rows=piece_rows):
                return (piece_rows(back_member, piece), columns(back_pair))

            def mine(piece, piece_rows=piece_rows):
                return (piece_rows(0, piece),)

            def whole(columns=columns):
                return (slice(None), columns(0))

            firsts = [
                (
                    pair,
                    piece,
                    self.move(
                        (SHARDS, 2 * pair),
                        lambda pair=pair: {SHARDS: lax.rem(lax.axis_index(SHARDS) + 2 * pair, shards)},
                        source,
                        functools.partial(mine, piece),
                        target,
                        functools.partial(place, 0, 0, piece),
                    ),
                )
                for piece in range(pieces)
                for pair in range(1, shards // 2)
            ]
            near = self.move((SHARDS,), sibling_peer, source, None, target, whole)
            local = self.keep(source, None, target, whole)
            entries.append((target, place, firsts, [near, *[number for _, _, number in firsts]], local))
        last = []
        for target, place, firsts, numbers, _ in entries:
            for pair, piece, first in firsts:
                near = functools.partial(place, 0, pair, piece)
                for shift in range(1, members):
                    number = self.move(
                        (PATCHES, members, shift),
                        functools.partial(member_peer, members, shift),
                        target,
                        near,
                        target,
                        near,
                        (first,),
                    )
                    last.append((target, functools.partial(place, shift, pair, piece), number, numbers))
                numbers.append(self.move((SHARDS,), sibling_peer, target, near, target, near, (first,)))
        for target, at, number, numbers in last:
            numbers += [number, self.move((SHARDS,), sibling_peer, target, at, target, at, (number,))]
        return [(target, numbers, local) for target, _, _, numbers, local in entries]

    def to_sibling(self, waiting):
        for target, place, number in waiting:
            self.move((SHARDS,), sibling_peer, target, place, target, place, (number,))

    def exchange(self, axis, array, later=False):
        target = self.output(array.shape, array.dtype)
        return self.along(
            axis, self.operand(array), target, [(lambda receiver: (receiver,), lambda sender: (sender,))], later
        )

    def exchange_columns(self, axis, array):
        width = array.shape[-1] // lax.axis_size(axis)
        target = self.output((lax.axis_size(axis), array.shape[0], width), array.dtype)
        self.along(
            axis,
            self.operand(array),
            target,
            [
                (
                    lambda receiver: (slice(None), pl.ds(pl.multiple_of(receiver * width, LANES), width)),
                    lambda sender: (sender,),
                )
            ],
        )

    def rows_to_heads(self, axis, array, planes, target):
        count, rows = lax.axis_size(axis), array.shape[0]
        columns = array.shape[1] // planes
        width = columns // count
        return self.along(
            axis,
            self.operand(array),
            target,
            [
                (
                    lambda receiver, plane=plane: (
                        slice(None),
                        pl.ds(pl.multiple_of(plane * columns + receiver * width, LANES), width),
                    ),
                    lambda sender, plane=plane: (plane, pl.ds(pl.multiple_of(sender * rows, rows), rows)),
                )
                for plane in range(planes)
            ],
        )

    def head_rows(self, source, target, planes, rows, columns, members, back_group):
        count = lax.axis_size(PATCHES)
        width = columns // count
        for shift_member in range(members):
            for plane in planes:

                def peer(shift_member=shift_member):
                    index = lax.axis_index(PATCHES)
                    there = lax.rem(index // members + back_group, MATRICES) * members
                    return there + lax.rem(lax.rem(index, members) + shift_member, members)

                def source_at(peer=peer, plane=plane):
                    return (plane, pl.ds(pl.multiple_of(peer() * rows, rows), rows))

                def target_at(plane=plane):
                    start = plane * columns + lax.axis_index(PATCHES) * width
                    return (slice(None), pl.ds(pl.multiple_of(start, LANES), width))

                if shift_member or back_group:
                    self.start(
                        self.move(
                            (PATCHES, count, back_group, shift_member),
                            lambda peer=peer: {PATCHES: peer()},
                            source,
                            source_at,
                            target,
                            target_at,
                            later=True,
                        )
                    )
                else:

                    def own(ref, source_at=source_at, target_at=target_at):
                        ref(target)[target_at()] = ref(source)[source_at()]

                    self.task(own)


def contract(left, right, left_dim, right_dim):
    return lax.dot_general(
        left, right, (((left_dim,), (right_dim,)), ((), ())), preferred_element_type=jnp.float32
    )


CHAIN_CHUNKS = 8
DOWN_CHUNKS = 4
KERNEL_VMEM = 62 * 2**20
UPDATE_BLOCKS = 4
GRAM_COLS = 256


def attend(queries, keys, values):
    scores = contract(queries, keys, 1, 1) * HEAD ** (-0.5)
    expo = jnp.exp(scores - jnp.max(scores, -1, keepdims=True))
    probs = (expo / jnp.sum(expo, -1, keepdims=True)).astype(LOW)
    return contract(probs, values, 1, 0)


def group_rows(rows, members, shift):
    size = rows * members
    there = lax.rem(lax.axis_index(PATCHES) // members + shift, MATRICES)
    return pl.ds(pl.multiple_of(there * size, size), size)


def add_attention(moves, qkv, mixed, arrivals, rows, members, waiting):
    for number in arrivals:
        moves.wait_for(number)
    for number in range(3):
        moves.wait_local(number)
    moves.to_sibling(waiting)
    count = lax.axis_size(PATCHES)
    width = HEADS // count * HEAD
    buffer = moves.scratch((1, rows * count, width), LOW)
    for shift in (*range(1, MATRICES), 0):

        def work(ref, shift=shift):
            at = group_rows(rows, members, shift)
            parts = []
            for head in range(width // HEAD):
                lanes = pl.ds(head * HEAD, HEAD)
                parts.append(attend(ref(qkv)[0, at, lanes], ref(qkv)[1, :, lanes], ref(qkv)[2, :, lanes]))
            ref(buffer)[0, at, :] = jnp.concatenate(parts, -1).astype(LOW)

        moves.task(work)
        moves.head_rows(buffer, mixed, (0,), rows, width * count, members, shift)


def add_attention_back(moves, qkv, grads, result, arrivals, rows, members, waiting):
    for number in arrivals:
        moves.wait_for(number)
    moves.wait_local(0)
    moves.to_sibling(waiting)
    count = lax.axis_size(PATCHES)
    width = HEADS // count * HEAD
    heads = width // HEAD
    buffer = moves.scratch((3, rows * count, width), LOW)
    key_total = moves.scratch((heads, rows * count, HEAD), jnp.float32)
    value_total = moves.scratch((heads, rows * count, HEAD), jnp.float32)
    for shift in (*range(1, MATRICES), 0):

        def work(ref, shift=shift):
            at = group_rows(rows, members, shift)
            parts = []
            for head in range(heads):
                lanes = pl.ds(head * HEAD, HEAD)
                queries, keys, values = ref(qkv)[0, at, lanes], ref(qkv)[1, :, lanes], ref(qkv)[2, :, lanes]
                grad = ref(grads)[0, at, lanes]
                scores = contract(keys, queries, 1, 1) * HEAD ** (-0.5)
                expo = jnp.exp(scores - jnp.max(scores, 0, keepdims=True))
                probs = expo / jnp.sum(expo, 0, keepdims=True)
                grad_probs = contract(values, grad, 1, 1)
                shared = jnp.sum(grad_probs * probs, 0, keepdims=True)
                score_grad = (HEAD ** (-0.5) * probs * (grad_probs - shared)).astype(LOW)
                parts.append(contract(score_grad, keys, 0, 0))
                key_part = contract(score_grad, queries, 1, 0)
                value_part = contract(probs.astype(LOW), grad, 1, 0)
                if shift == 1:
                    ref(key_total)[head] = key_part
                    ref(value_total)[head] = value_part
                else:
                    ref(key_total)[head] += key_part
                    ref(value_total)[head] += value_part
            ref(buffer)[0, at, :] = jnp.concatenate(parts, -1).astype(LOW)

        moves.task(work)
        moves.head_rows(buffer, result, (0,), rows, width * count, members, shift)

    def finish(ref):
        for plane, total in ((1, key_total), (2, value_total)):
            ref(buffer)[plane] = jnp.concatenate([ref(total)[head] for head in range(heads)], -1).astype(LOW)

    moves.task(finish)
    for shift in (*range(1, MATRICES), 0):
        moves.head_rows(buffer, result, (1, 2), rows, width * count, members, shift)


def mod_row(ref, table, row):
    return ref(table)[pl.ds(row, 1), :]


def project(moves, source, weights, target, count):
    def action(ref):
        width = ref(source).shape[1]

        @pl.loop(0, count // width)
        def _(part):
            cols = pl.ds(pl.multiple_of(part * width, width), width)
            ref(target)[:, cols] = contract(ref(source)[...], ref(weights)[:, cols], 1, 0).astype(LOW)

    moves.task(action)


def embed(ref, state_low, io_weights, mods, pos, embedded, normed_low):
    value = contract(ref(state_low)[...], io_weights, 1, 0) + mods(6) + ref(pos)[...].astype(jnp.float32)
    ref(embedded)[...] = value
    normed, _ = layer_norm(value)
    ref(normed_low)[...] = (normed * (1.0 + mods(1)) + mods(0)).astype(LOW)


def begin_step(ids, members, state, id_rows, active, cond_table, biases, pos, ada, io_low, w_out, w_qkv):
    f32 = jnp.float32
    shards = lax.axis_size(SHARDS)
    (rows, padded), (table_rows, _) = state.shape, cond_table.shape
    width = w_out.shape[0]
    ada_cols = ada.shape[1]
    moves = Moves("begin", ids, KERNEL_VMEM)
    table = moves.scratch((table_rows, width), f32)
    bias = moves.scratch((1, biases.shape[1] * shards), f32)
    pos_all = moves.scratch((rows, width), LOW)
    id_rows, active, state = [moves.operand(item, pltpu.VMEM) for item in (id_rows, active, state)]
    small = [moves.gather_columns(SHARDS, cond_table, table), moves.gather_columns(SHARDS, biases, bias)]
    pos_moves, pos_local = moves.gather_columns(SHARDS, pos, pos_all)
    ada_weights, ada_load = moves.load(ada)
    vmem = functools.partial(moves.output, space=pltpu.VMEM)
    extras = vmem((ROLL, 8, width), f32)
    cond_vec, silu_low = vmem((shards * ROLL, width), f32), vmem((shards * ROLL, width), LOW)
    embedded, normed_low = vmem((rows, width), f32), vmem((rows, width), LOW)
    state_low, qkv_rows = vmem((rows, padded), LOW), vmem((rows, 3 * width), LOW)
    parts_leaving, parts = [moves.scratch((shards, ROLL, ada_cols), f32) for _ in range(2)]

    def modulate(ref):
        row = lax.broadcasted_iota(jnp.int32, (shards * ROLL, 1), 0)
        ids_here = ref(id_rows)[:, :1]
        value = jnp.zeros((shards * ROLL, width), f32)
        for entry in range(table_rows):
            of_entry = ref(table)[pl.ds(entry, 1), :].astype(LOW).astype(f32)
            chosen = (ids_here == entry) if entry < NI else (lax.rem(row, ROLL) == entry - NI)
            value = value + jnp.where(chosen, of_entry, 0.0)
        ref(cond_vec)[...] = value
        value = (value / (1.0 + jnp.exp(-value))).astype(LOW)
        ref(silu_low)[...] = value
        start = pl.multiple_of(lax.axis_index(SHARDS) * ada_cols, LANES)
        value = contract(value, ref(ada_weights)[...], 1, 0)
        value = value + ref(bias)[:, pl.ds(start, ada_cols)].astype(LOW).astype(f32)
        for sample in range(shards):
            ref(parts_leaving)[sample] = value[sample * ROLL : (sample + 1) * ROLL]
        ref(parts)[lax.axis_index(SHARDS)] = ref(parts_leaving)[lax.axis_index(SHARDS)]

    for numbers, local in small:
        for number in numbers:
            moves.wait_for(number)
        moves.wait_local(local)
    moves.wait_local(ada_load)
    moves.task(modulate)
    modul_moves = []
    for shift in range(1, shards):

        def other(shift=shift):
            return lax.rem(lax.axis_index(SHARDS) + shift, shards)

        number = moves.move(
            (SHARDS, shift),
            lambda other=other: {SHARDS: other()},
            parts_leaving,
            lambda other=other: (other(),),
            parts,
            lambda: (lax.axis_index(SHARDS),),
            later=True,
        )
        modul_moves.append(number)
        moves.start(number)
    weights = moves.gather_twice((io_low.reshape(-1, io_low.shape[-1]), w_out, w_qkv), members, (1, 1, 4))

    def collect(ref):
        bias_row = ref(bias)[:, pl.ds(6 * width, width)].astype(LOW).astype(f32)
        for step in range(ROLL):
            for piece in range(6 * 2):
                start = piece * width // 2
                value = ref(parts)[start // ada_cols, pl.ds(step, 1), pl.ds(start % ada_cols, width // 2)]
                ref(extras)[step, pl.ds(piece // 2, 1), pl.ds(piece % 2 * width // 2, width // 2)] = value
            ref(extras)[step, pl.ds(6, 1), :] = bias_row
            ref(extras)[step, pl.ds(7, 1), :] = ref(active)[pl.ds(step, 1), :]

    def start_step(ref):
        ref(state_low)[...] = ref(state)[...].astype(LOW)
        mods = lambda row: ref(extras)[0, pl.ds(row, 1), :]
        embed(ref, state_low, ref(weights[0][0])[pl.ds(0, padded), :], mods, pos_all, embedded, normed_low)

    for number in modul_moves:
        moves.wait_for(number)
    moves.task(collect)
    for number in (*pos_moves, *weights[0][1]):
        moves.wait_for(number)
    moves.wait_local(pos_local)
    moves.wait_local(weights[0][2])
    moves.task(start_step)
    for target, numbers, local in weights:
        for number in numbers:
            moves.wait_for(number)
        moves.wait_local(local)
        save = moves.save(target, moves.shape(target), LOW)
        moves.start_local(save)
    moves.start_local(moves.save(pos_all, (rows, width), LOW))
    project(moves, normed_low, weights[2][0], qkv_rows, 3 * width)
    return moves.run()


class Tokens:
    def __init__(self, moves, rows, width):
        self.moves = moves
        self.shards = lax.axis_size(SHARDS)
        self.rows = rows
        self.tokens = moves.scratch((self.shards, rows, width), LOW)
        self.own_part = moves.scratch((rows, width), jnp.float32)
        self.leaving = moves.scratch((self.shards, rows, width), LOW)
        self.arriving = moves.scratch((self.shards, rows, width), LOW)

    def me(self):
        return lax.axis_index(SHARDS)

    def back(self, pair, sibling):
        index = lax.rem(self.me() + self.shards - 2 * pair, self.shards)
        return index + 1 - 2 * lax.rem(index, 2) if sibling else index

    def part(self, pair, sibling, work):
        moves = self.moves
        slot = functools.partial(self.back, pair, sibling)

        def action(ref):
            value = work(ref, slot())
            if pair or sibling:
                ref(self.leaving)[slot()] = value.astype(LOW)
            else:
                ref(self.own_part)[...] = value

        moves.task(action)
        if pair or sibling:
            number = moves.move(
                (SHARDS, pair, sibling),
                lambda: {SHARDS: slot()},
                self.leaving,
                lambda: (slot(),),
                self.arriving,
                lambda: (self.me(),),
                later=True,
            )
            moves.start(number)
            self.parts.append(number)

    def run(self, work):
        moves, halves = self.moves, 2
        self.parts = []
        size = self.rows // halves
        pairs = self.shards // 2

        def half(pair, sibling, number):
            return (self.back(pair, sibling), pl.ds(number * size, size))

        firsts = {}
        for pair in range(1, pairs):
            for number in range(halves):
                place = functools.partial(half, 0, False, number)
                firsts[pair, number] = moves.move(
                    (SHARDS, pairs - pair, False),
                    functools.partial(lambda pair: {SHARDS: self.back(pairs - pair, False)}, pair),
                    self.tokens,
                    place,
                    self.tokens,
                    place,
                    later=True,
                )
                moves.start(firsts[pair, number])
        own = functools.partial(self.back, 0, False)
        near = moves.move(
            (SHARDS, 0, True), sibling_peer, self.tokens, lambda: (own(),), self.tokens, lambda: (own(),), later=True
        )
        moves.start(near)
        self.part(0, False, work)
        moves.wait_for(near)
        self.part(0, True, work)
        for pair in range(1, pairs):
            handed = []
            for number in range(halves):
                place = functools.partial(half, pair, False, number)
                handed.append(
                    moves.move(
                        (SHARDS, 0, True),
                        sibling_peer,
                        self.tokens,
                        place,
                        self.tokens,
                        place,
                        (firsts[pair, number],),
                    )
                )
            self.part(pair, False, work)
            for number in handed:
                moves.wait_for(number)
            self.part(pair, True, work)

    def wait(self):
        for number in self.parts:
            self.moves.wait_for(number)

    def total(self, ref):
        value = ref(self.own_part)[...]
        for shift in range(1, self.shards):
            value = value + ref(self.arriving)[lax.rem(self.me() + shift, self.shards)].astype(jnp.float32)
        return value


TOKENS, UP_GRAD = 1, 2
GELU_SCALE = math.sqrt(2.0 / math.pi)
GELU_CUBE = 0.044715


def gelu_inner(values):
    return jnp.tanh(GELU_SCALE * (values + GELU_CUBE * values * values * values))


def gelu_slope(values):
    inner = gelu_inner(values)
    rise = GELU_SCALE * (1.0 + 3.0 * GELU_CUBE * values * values)
    return 0.5 * (1.0 + inner) + 0.5 * values * (1.0 - inner * inner) * rise


def feed_forward(ids, step, mods, mods_next, mixed, embedded, state, pos, w_out, w_up, w_down, io_all, w_qkv, momenta, members):
    f32 = jnp.float32
    last = mods_next is None
    rows, width = mixed.shape
    padded = state.shape[1]
    hidden_count = w_up.shape[1]
    shards = lax.axis_size(SHARDS)
    moves = Moves(f"feed{step}", ids, KERNEL_VMEM)
    vmem = functools.partial(moves.operand, space=pltpu.VMEM)
    out_weights, out_load = moves.load(w_out)
    mods, mixed, embedded, state = vmem(mods), vmem(mixed), vmem(embedded), vmem(state)
    up_weights, up_load = moves.load(w_up)
    down_weights, down_load = moves.load(w_down)
    io_weights, io_load = moves.load(io_all)
    attended, after_attn, downward, after_mlp = [moves.output((rows, width), f32, pltpu.VMEM) for _ in range(4)]
    normed_c = moves.output((rows, width), LOW, pltpu.VMEM)
    state_next = moves.output((rows, padded), f32, pltpu.VMEM)
    upward = moves.scratch((shards, rows, hidden_count), f32)
    hidden = moves.scratch((shards, rows, hidden_count), LOW)
    feed = Tokens(moves, rows, width)
    saves = [
        moves.save(feed.tokens, (shards, rows, width), LOW),
        moves.save(upward, (shards, rows, hidden_count), f32),
        moves.save(hidden, (shards, rows, hidden_count), LOW),
    ]
    if not last:
        mods_next, pos = vmem(mods_next), vmem(pos)
        qkv_weights, qkv_load = moves.load(w_qkv)
        embedded_next = moves.output((rows, width), f32, pltpu.VMEM)
        normed_next = moves.output((rows, width), LOW, pltpu.VMEM)
        state_low = moves.output((rows, padded), LOW, pltpu.VMEM)
        qkv_next = moves.output((rows, w_qkv.shape[1]), LOW, pltpu.VMEM)
    half = rows // ROLL
    seq_count = lax.axis_size(PATCHES)
    most_cols = max(item.shape[1] for item in momenta) // members
    moment_loads = []
    for item in momenta:
        scratch = moves.scratch((half, item.shape[1]), f32)
        number = moves.keep(moves.operand(item), lambda: (pl.ds(step * half, half),), scratch, None)
        moment_loads.append((scratch, number))
    moment_leaving = moves.scratch((seq_count, half, most_cols), LOW)
    moment_arriving = moves.output((seq_count, half, most_cols), LOW)

    def pack(ref):
        for which, (scratch, _) in enumerate(moment_loads):
            cols = momenta[which].shape[1] // members
            for part in range(members):
                value = ref(scratch)[:, part * cols : (part + 1) * cols].astype(LOW)
                if cols < most_cols:
                    value = jnp.concatenate([value, jnp.zeros((half, most_cols - cols), LOW)], 1)
                ref(moment_leaving)[which * members + part] = value

    def begin(ref):
        value = contract(ref(mixed)[...], ref(out_weights)[...], 1, 0)
        ref(attended)[...] = value
        value = ref(embedded)[...] + mod_row(ref, mods, 2) * value
        ref(after_attn)[...] = value
        normed, _ = layer_norm(value)
        normed = normed * (1.0 + mod_row(ref, mods, 4)) + mod_row(ref, mods, 3)
        ref(feed.tokens)[feed.me()] = normed.astype(LOW)

    def work(ref, slot):
        value = contract(ref(feed.tokens)[slot], ref(up_weights)[...], 1, 0)
        ref(upward)[slot] = value
        value = (0.5 * value * (1.0 + gelu_inner(value))).astype(LOW)
        ref(hidden)[slot] = value
        return contract(value, ref(down_weights)[...], 1, 1)

    def finish(ref):
        value = feed.total(ref)
        ref(downward)[...] = value
        value = ref(after_attn)[...] + mod_row(ref, mods, 5) * value
        ref(after_mlp)[...] = value
        normed, _ = layer_norm(value)
        normed = normed.astype(LOW)
        ref(normed_c)[...] = normed
        delta = contract(normed, ref(io_weights)[1], 1, 1)
        value = ref(state)[...] + mod_row(ref, mods, 7)[:, :padded] * delta
        ref(state_next)[...] = value
        if not last:
            ref(state_low)[...] = value.astype(LOW)
            mods_there = functools.partial(mod_row, ref, mods_next)
            embed(ref, state_low, ref(io_weights)[0], mods_there, pos, embedded_next, normed_next)

    moves.wait_local(out_load)
    moves.task(begin)
    moves.wait_local(up_load)
    moves.wait_local(down_load)
    feed.run(work)
    for number in saves:
        moves.start_local(number)
    for _, number in moment_loads:
        moves.wait_local(number)
    moves.task(pack)
    moves.along(
        PATCHES, moment_leaving, moment_arriving, [(lambda there: (there,), lambda sender: (sender,))], later=True
    )
    moves.wait_local(io_load)
    feed.wait()
    moves.task(finish)
    if not last:
        moves.wait_local(qkv_load)
        project(moves, normed_next, qkv_weights, qkv_next, w_qkv.shape[1])
    return moves.run()


def feed_back(ids, step, mods, mods_later, later, grad_state, kept, w_out, w_up, w_down, io_all, w_qkv, members, pairs):
    f32 = jnp.float32
    attended, after_attn, downward, after_mlp, upward = kept
    rows, width = attended.shape
    padded = grad_state.shape[1]
    hidden_count = w_up.shape[1]
    shards = lax.axis_size(SHARDS)
    moves = Moves(f"feed_back{step}", ids, KERNEL_VMEM)
    vmem = functools.partial(moves.operand, space=pltpu.VMEM)
    io_weights, io_load = moves.load(io_all)
    if later is not None:
        qkv_weights, qkv_load = moves.load(w_qkv)
        later = [vmem(item) for item in later]
        mods_later = vmem(mods_later)
        embed_grad = moves.output((rows, width), LOW, pltpu.VMEM)
    down_weights, down_load = moves.load(w_down)
    up_weights, up_load = moves.load(w_up)
    slopes, slopes_load = moves.load(upward)
    out_weights, out_load = moves.load(w_out)
    mods, grad_state = vmem(mods), vmem(grad_state)
    attended, after_attn, downward, after_mlp = [vmem(item) for item in (attended, after_attn, downward, after_mlp)]
    vectors = moves.output((8, width), f32, pltpu.VMEM)
    state_out = moves.output((rows, padded), f32, pltpu.VMEM)
    delta_grad = moves.output((rows, padded), LOW, pltpu.VMEM)
    grad_attn = moves.output((rows, width), f32, pltpu.VMEM)
    attn_grad, mixed_grad = [moves.output((rows, width), LOW, pltpu.VMEM) for _ in range(2)]
    grad_mlp = moves.scratch((rows, width), f32)
    up_grad = moves.scratch((shards, rows, hidden_count), LOW)
    feed = Tokens(moves, rows, width)
    saves = [
        moves.save(feed.tokens, (shards, rows, width), LOW),
        moves.save(up_grad, (shards, rows, hidden_count), LOW),
    ]

    weight_outputs, weight_tasks = [], []
    if pairs is not None:
        half_cols = hidden_count // members
        whole = moves.scratch((GRAM_COLS, hidden_count), f32)
        for made, operands in pairs:
            mine = moves.output((width, half_cols), f32)
            leaving = [moves.output((width, half_cols), LOW) for _ in range(members - 1)]
            held = moves.scratch((width, half_cols), f32)
            held_low = [moves.scratch((width, half_cols), LOW) for _ in range(members - 1)]
            loads = [[None if item is None else moves.load(item) for item in entry] for entry in operands]
            weight_outputs += [(held, mine)] + list(zip(held_low, leaving))
            weight_tasks.append((made, loads, held, held_low))

    def weight_grad(made, loads, held, held_low):
        def action(ref):
            @pl.loop(0, width // GRAM_COLS)
            def _(tile):
                at = pl.ds(pl.multiple_of(tile * GRAM_COLS, GRAM_COLS), GRAM_COLS)
                value = jnp.zeros((GRAM_COLS, hidden_count), f32)
                for entry in loads:
                    left, right = [made_here if item is None else item[0] for item, made_here in zip(entry, made)]
                    left_rows = ref(left)[:, :, at].reshape(-1, GRAM_COLS)
                    value = value + contract(left_rows, ref(right)[...].reshape(-1, hidden_count), 0, 0)
                ref(whole)[...] = value
                member = lax.rem(lax.axis_index(PATCHES), members)
                for shift in range(members):
                    there = lax.rem(member + shift, members)
                    part = ref(whole)[:, pl.ds(pl.multiple_of(there * half_cols, LANES), half_cols)]
                    if shift:
                        ref(held_low[shift - 1])[at, :] = part.astype(LOW)
                    else:
                        ref(held)[at, :] = part

        return action

    def put(ref, row, value):
        ref(vectors)[pl.ds(row, 1), :] = jnp.sum(value, 0, keepdims=True)

    def before(ref):
        qkv_grad, embedded, grad_later = later
        grad = contract(ref(qkv_grad)[...], ref(qkv_weights)[...], 1, 1)
        normed, inverse = layer_norm(ref(embedded)[...])
        put(ref, 5, grad * normed)
        put(ref, 4, grad)
        grad = grad * (1.0 + mod_row(ref, mods_later, 1))
        grad = ref(grad_later)[...] + norm_back(grad, normed, inverse)
        put(ref, 6, grad)
        grad = grad.astype(LOW)
        ref(embed_grad)[...] = grad
        ref(state_out)[...] = ref(grad_state)[...] + contract(grad, ref(io_weights)[0], 1, 1)

    def begin(ref):
        if later is None:
            ref(state_out)[...] = ref(grad_state)[...]
            ref(vectors)[...] = jnp.zeros((8, width), f32)
        grad = (mod_row(ref, mods, 7)[:, :padded] * ref(state_out)[...]).astype(LOW)
        ref(delta_grad)[...] = grad
        normed, inverse = layer_norm(ref(after_mlp)[...])
        grad = norm_back(contract(grad, ref(io_weights)[1], 1, 0), normed, inverse)
        ref(grad_mlp)[...] = grad
        put(ref, 3, grad * ref(downward)[...])
        ref(feed.tokens)[feed.me()] = (mod_row(ref, mods, 5) * grad).astype(LOW)

    def work(ref, slot):
        value = contract(ref(feed.tokens)[slot], ref(down_weights)[...], 1, 0)
        value = (value * gelu_slope(ref(slopes)[slot])).astype(LOW)
        ref(up_grad)[slot] = value
        return contract(value, ref(up_weights)[...], 1, 1)

    def finish(ref):
        grad = feed.total(ref)
        normed, inverse = layer_norm(ref(after_attn)[...])
        put(ref, 2, grad * normed)
        put(ref, 1, grad)
        grad = ref(grad_mlp)[...] + norm_back(grad * (1.0 + mod_row(ref, mods, 4)), normed, inverse)
        ref(grad_attn)[...] = grad
        put(ref, 0, grad * ref(attended)[...])
        grad = (mod_row(ref, mods, 2) * grad).astype(LOW)
        ref(attn_grad)[...] = grad
        ref(mixed_grad)[...] = contract(grad, ref(out_weights)[...], 1, 1).astype(LOW)

    moves.wait_local(io_load)
    if later is not None:
        moves.wait_local(qkv_load)
        moves.task(before)
    moves.task(begin)
    for number in (down_load, up_load, slopes_load):
        moves.wait_local(number)
    feed.run(work)
    for number in saves:
        moves.start_local(number)
    for made, loads, held, held_low in weight_tasks:
        for entry in loads:
            for item in entry:
                if item is not None:
                    moves.wait_local(item[1])
        made = [feed.tokens if item is TOKENS else up_grad if item is UP_GRAD else None for item in made]
        moves.task(weight_grad(made, loads, held, held_low))
    for held, target in weight_outputs:
        moves.start_local(moves.keep(held, None, target, None, True))
    moves.wait_local(out_load)
    feed.wait()
    moves.task(finish)
    results = moves.run()
    return results if later is not None else [None, *results]


def reduce_step(
    ids, members, group_cols, qkv_grad, embedded, grad_attn, mods, w_qkv, rows_late, rows_early, gathered, mlp, ada
):
    f32 = jnp.float32
    shards, seq_count = lax.axis_size(SHARDS), lax.axis_size(PATCHES)
    rows, width = embedded.shape
    block_rows, most_cols = width, max(group_cols)
    part, ada_cols = width // shards, ada.shape[1]
    up_mine, up_arrived, down_mine, down_leaving = mlp
    moves = Moves("reduce", ids, KERNEL_VMEM)
    vmem = functools.partial(moves.operand, space=pltpu.VMEM)
    qkv_grad, embedded, grad_attn, mods = vmem(qkv_grad), vmem(embedded), vmem(grad_attn), vmem(mods)
    rows_late, rows_early = vmem(rows_late), vmem(rows_early)

    def shard():
        return lax.axis_index(SHARDS)

    def patch():
        return lax.axis_index(PATCHES)

    def group():
        return patch() // members

    def member():
        return lax.rem(patch(), members)

    def columns(index, size):
        return pl.ds(pl.multiple_of(index * size, LANES), size)

    def await_all(numbers):
        for number in numbers:
            moves.wait_for(number)

    def to_others(axis, source, source_at, target, leave_own=False):
        count = lax.axis_size(axis)
        numbers = []
        for shift in range(1, count):

            def other(shift=shift):
                return lax.rem(lax.axis_index(axis) + shift, count)

            number = moves.move(
                (axis, shift),
                lambda other=other: {axis: other()},
                source,
                lambda other=other: source_at(other()),
                target,
                lambda: (lax.axis_index(axis),),
                later=True,
            )
            moves.start(number)
            numbers.append(number)

        def own(ref):
            ref(target)[lax.axis_index(axis)] = ref(source)[source_at(lax.axis_index(axis))]

        moves.task(own)
        return numbers

    def to_members(source, target, cols):
        numbers = []
        for shift in range(1, members):
            number = moves.move(
                (PATCHES, members, shift),
                functools.partial(member_peer, members, shift),
                source,
                lambda shift=shift: (slice(None), columns(lax.rem(member() + shift, members), cols)),
                target,
                lambda shift=shift: (shift - 1,),
                later=True,
            )
            moves.start(number)
            numbers.append(number)
        return numbers

    def to_group(source, target, which):
        numbers = []
        for shift in range(1, MATRICES):
            number = moves.move(
                (PATCHES, seq_count, shift),
                functools.partial(group_peer, members, shift),
                source,
                None,
                target,
                lambda shift=shift: (shift - 1,),
                sends=lambda shift=shift: group() == (which - shift) % MATRICES,
                takes=lambda: group() == which,
                later=True,
            )
            moves.start(number)
            numbers.append(number)
        return numbers

    def over_rows(action):
        @pl.loop(0, block_rows // GRAM_COLS)
        def _(tile):
            action(pl.ds(pl.multiple_of(tile * GRAM_COLS, GRAM_COLS), GRAM_COLS))

    def weight_grad(lefts, rights, full, low=None):
        depth, cols = moves.shape(lefts[0])[2], moves.shape(rights[0])[2]
        tile_rows = GRAM_COLS if depth % GRAM_COLS == 0 else LANES

        def action(ref):
            @pl.loop(0, depth // tile_rows)
            def _(tile):
                at = pl.ds(pl.multiple_of(tile * tile_rows, tile_rows), tile_rows)
                value = jnp.zeros((tile_rows, cols), f32)
                for left, right in zip(lefts, rights):
                    left_rows = ref(left)[:, :, at].reshape(-1, tile_rows)
                    value = value + contract(left_rows, ref(right)[...].reshape(-1, cols), 0, 0)
                if full is not None:
                    ref(full)[at, :] = value
                if low is not None:
                    ref(low)[at, :] = value.astype(LOW)

        moves.task(action)

    qkv_all = moves.scratch((shards, rows, 3 * part), LOW)
    qkv_moves = moves.along(
        SHARDS,
        qkv_grad,
        qkv_all,
        [(lambda receiver: (slice(None), columns(receiver, 3 * part)), lambda sender: (sender,))],
    )
    qkv_local = len(moves.locals) - 1
    down_arriving = moves.scratch((members - 1, block_rows, group_cols[2]), LOW)
    down_moves = [
        moves.move(
            (PATCHES, members, shift),
            functools.partial(member_peer, members, shift),
            moves.operand(item),
            None,
            down_arriving,
            lambda shift=shift: (shift - 1,),
        )
        for shift, item in enumerate(down_leaving, 1)
    ]
    up_full, up_load = moves.load(up_mine)
    up_others = [moves.load(item) for item in up_arrived]
    qkv_weights, qkv_load = moves.load(w_qkv)
    loaded = {
        name: [moves.load(steps[step]) for step in range(ROLL) if step in steps] for name, steps in gathered.items()
    }
    down_full, down_load = moves.load(down_mine)
    ada_weights, ada_load = moves.load(ada)

    def ready(*names):
        for name in names:
            for _, number in loaded[name]:
                moves.wait_local(number)
        return [[item for item, _ in loaded[name]] for name in names]

    up_low, down_low = [moves.scratch((block_rows, cols), LOW) for cols in group_cols[1:3]]
    group_target, up_target = [moves.scratch((MATRICES - 1, block_rows, most_cols), LOW) for _ in range(2)]

    def round_up_grad(ref):
        def action(at):
            value = ref(up_full)[at, :]
            for item, _ in up_others:
                value = value + ref(item)[at, :].astype(f32)
            ref(up_full)[at, :] = value
            ref(up_low)[at, :] = value.astype(LOW)

        over_rows(action)

    for number in (up_load, *[number for _, number in up_others]):
        moves.wait_local(number)
    moves.task(round_up_grad)
    up_moves = to_group(up_low, up_target, 1)

    embed_low = moves.scratch((rows, width), LOW)
    table = moves.scratch((8, 6 * width), f32)

    def back(ref):
        grad = contract(ref(qkv_grad)[...], ref(qkv_weights)[...], 1, 1)
        normed, inverse = layer_norm(ref(embedded)[...])
        ref(table)[...] = jnp.zeros((8, 6 * width), f32)
        ref(table)[pl.ds(0, 1), pl.ds(0, width)] = jnp.sum(grad, 0, keepdims=True)
        ref(table)[pl.ds(0, 1), pl.ds(width, width)] = jnp.sum(grad * normed, 0, keepdims=True)
        grad = ref(grad_attn)[...] + norm_back(grad * (1.0 + mod_row(ref, mods, 1)), normed, inverse)
        ref(embed_low)[...] = grad.astype(LOW)
        bias_row = jnp.sum(grad, 0, keepdims=True) + mod_row(ref, rows_early, 6)
        for entry in range(4):
            cols = pl.ds((2 + entry) * width, width)
            ref(table)[pl.ds(0, 1), cols] = mod_row(ref, rows_early, entry)
            ref(table)[pl.ds(1, 1), cols] = mod_row(ref, rows_late, entry)
        for entry in range(2):
            ref(table)[pl.ds(1, 1), pl.ds(entry * width, width)] = mod_row(ref, rows_early, 4 + entry)
        for entry in range(shards):
            ref(table)[pl.ds(ROLL, 1), pl.ds(entry * ada_cols, part)] = bias_row[:, entry * part : (entry + 1) * part]

    moves.wait_local(qkv_load)
    moves.task(back)
    embed_all = moves.scratch((shards, rows, part), LOW)
    table_all = moves.scratch((shards, 8, ada_cols), f32)
    embed_moves = to_others(SHARDS, embed_low, lambda there: (slice(None), columns(there, part)), embed_all)
    table_moves = to_others(SHARDS, table, lambda there: (slice(None), columns(there, ada_cols)), table_all)

    out_cols, qkv_cols = group_cols[3], group_cols[0]
    out_full, out_low = moves.scratch((width, part), f32), moves.scratch((width, part), LOW)
    qkv_full, qkv_low = moves.scratch((width, 3 * part), f32), moves.scratch((width, 3 * part), LOW)
    out_arriving = moves.scratch((members - 1, block_rows, out_cols), LOW)
    qkv_arriving = moves.scratch((members - 1, block_rows, qkv_cols), LOW)
    padded = moves.shape(loaded["state"][0][0])[2]
    io_low = moves.scratch((2 * padded, part), LOW)
    io_grads = [moves.scratch((padded, part), f32) for _ in range(2)]
    weight_grad(*ready("mixed", "attn"), out_full, out_low)
    out_moves = to_members(out_low, out_arriving, out_cols)
    weight_grad(*ready("delta", "c"), io_grads[1])
    await_all(qkv_moves)
    moves.wait_local(qkv_local)
    (a_all, qkv_later) = ready("a", "qkv")
    weight_grad(a_all, [qkv_all, *qkv_later], qkv_full, qkv_low)
    qkv_member_moves = to_members(qkv_low, qkv_arriving, qkv_cols)
    await_all(embed_moves)
    (state_all, embed_later) = ready("state", "embed")
    weight_grad(state_all, [embed_all, *embed_later], io_grads[0])
    grad_pos = moves.output((rows, part), f32, pltpu.VMEM)
    io_rows = 2 * padded // seq_count

    def pos_and_io(ref):
        value = jnp.zeros((rows, part), f32)
        for item in (embed_all, *embed_later):
            for sample in range(shards):
                value = value + ref(item)[sample].astype(f32)
        ref(grad_pos)[...] = value
        for number, item in enumerate(io_grads):
            ref(io_low)[pl.ds(number * padded, padded), :] = ref(item)[...].astype(LOW)

    moves.task(pos_and_io)
    io_all = moves.scratch((seq_count, io_rows, part), LOW)
    io_moves = to_others(
        PATCHES, io_low, lambda there: (pl.ds(pl.multiple_of(there * io_rows, io_rows), io_rows),), io_all
    )

    flat, flat_all = moves.scratch((16, ada_cols), LOW), moves.scratch((seq_count, 16, ada_cols), LOW)

    def share(ref):
        pieces = [ref(table_all)[sample, pl.ds(0, ROLL), :] for sample in range(shards)]
        bias_row = sum(ref(table_all)[sample, pl.ds(ROLL, 1), :] for sample in range(shards))
        rest = jnp.zeros((16 - shards * ROLL - 1, ada_cols), f32)
        ref(flat)[...] = jnp.concatenate([*pieces, bias_row, rest], 0).astype(LOW)

    await_all(table_moves)
    moves.task(share)
    flat_moves = to_others(PATCHES, flat, lambda there: (slice(None), slice(None)), flat_all)

    def add_member(full, arriving, target, low, cols):
        def action(ref):
            def add(at):
                value = ref(full)[at, columns(member(), cols)] if target is not full else ref(full)[at, :]
                for shift in range(members - 1):
                    value = value + ref(arriving)[shift, at, :].astype(f32)
                ref(target)[at, :] = value
                if low is not None:
                    ref(low)[at, :] = value.astype(LOW)

            over_rows(add)

        moves.task(action)

    moves.wait_local(down_load)
    await_all(down_moves)
    add_member(down_full, down_arriving, down_full, down_low, group_cols[2])

    hops = [(0, 1, down_low, 0), (1, 2, down_low, 1), (3, 2, down_low, 2)]
    down_chunk = block_rows // DOWN_CHUNKS
    down_hops = []
    for sender, receiver, source, place in hops:
        numbers = []
        for piece in range(DOWN_CHUNKS if place < 2 else 1):
            at = pl.ds(piece * down_chunk, down_chunk) if place < 2 else slice(None)
            shift = (receiver - sender) % MATRICES
            numbers.append(
                moves.move(
                    (PATCHES, seq_count, shift),
                    functools.partial(group_peer, members, shift),
                    source,
                    lambda at=at: (at,),
                    group_target,
                    lambda at=at, place=place: (place, at),
                    sends=lambda sender=sender: group() == sender,
                    takes=lambda receiver=receiver: group() == receiver,
                    later=True,
                )
            )
        down_hops.append(numbers)
    for number in (*down_hops[0], *down_hops[2]):
        moves.start(number)
    out_mine, out_mine_low = moves.scratch((width, out_cols), f32), moves.scratch((width, out_cols), LOW)
    out_target = moves.scratch((MATRICES - 1, block_rows, out_cols), LOW)
    await_all(out_moves)
    add_member(out_full, out_arriving, out_mine, out_mine_low, out_cols)
    out_group_moves = to_group(out_mine_low, out_target, 3)

    modul_all = moves.output((shards * ROLL, ada_cols), f32, pltpu.VMEM)
    tail_all = moves.output((shards, 16, ada_cols), f32, pltpu.VMEM)
    tail = moves.scratch((16, ada_cols), f32)

    def close(ref):
        value = jnp.zeros((16, ada_cols), f32)
        for item in range(seq_count):
            value = value + ref(flat_all)[item].astype(f32)
        modul = value[: shards * ROLL]
        ref(modul_all)[...] = modul
        high = modul.astype(LOW)
        rest = (modul - high.astype(f32)).astype(LOW)
        weights = ref(ada_weights)[...]
        ref(tail)[...] = jnp.zeros((16, ada_cols), f32)
        ref(tail)[pl.ds(0, shards * ROLL), pl.ds(0, width)] = contract(high, weights, 1, 1) + contract(
            rest, weights, 1, 1
        )
        ref(tail)[pl.ds(8, 1), :] = jnp.sum(modul, 0, keepdims=True)
        ref(tail)[pl.ds(9, 1), :] = value[shards * ROLL : shards * ROLL + 1]

    await_all(flat_moves)
    moves.wait_local(ada_load)
    moves.task(close)
    to_others(SHARDS, tail, lambda there: (slice(None), slice(None)), tail_all)

    for piece, (number, following) in enumerate(zip(*down_hops[:2])):
        at = pl.ds(piece * down_chunk, down_chunk)

        def add_down(ref, at=at):
            def sum_up():
                value = ref(down_full)[at, :] + ref(group_target)[0, at, :].astype(f32)
                ref(down_low)[at, :] = value.astype(LOW)

            pl.when(group() == 1)(sum_up)

        moves.wait_for(number)
        moves.task(add_down)
        moves.start(following)

    def has_source():
        return group() < MATRICES - 1

    def is_source():
        return group() > 0

    chain = moves.scratch((width, qkv_cols), f32)
    chain_in, chain_out = [moves.scratch((width, qkv_cols), LOW) for _ in range(2)]
    await_all(qkv_member_moves)
    add_member(qkv_full, qkv_arriving, chain, None, qkv_cols)
    chunk = block_rows // CHAIN_CHUNKS
    for number_of in range(CHAIN_CHUNKS):
        place = (pl.ds(number_of * chunk, chunk),)
        number = moves.move(
            (PATCHES, seq_count, MATRICES - 1),
            functools.partial(group_peer, members, MATRICES - 1),
            chain_out,
            lambda place=place: place,
            chain_in,
            lambda place=place: place,
            sends=is_source,
            takes=has_source,
            later=True,
        )

        def add(ref, place=place):
            def with_arriving():
                ref(chain)[place] += ref(chain_in)[place].astype(f32)

            pl.when(has_source())(with_arriving)
            ref(chain_out)[place] = ref(chain)[place].astype(LOW)

        moves.wait_for(number)
        moves.task(add)
        moves.start(number)

    io_slice = moves.output((io_rows, part), f32, pltpu.VMEM)

    def add_io(ref):
        value = jnp.zeros((io_rows, part), f32)
        for item in range(seq_count):
            value = value + ref(io_all)[item].astype(f32)
        ref(io_slice)[...] = value

    await_all(io_moves)
    moves.task(add_io)

    grad_group = moves.output((block_rows, most_cols), f32, pltpu.VMEM)

    def put(full, target, places, cols):
        def action(ref):
            def add(at):
                value = ref(full)[at, :]
                for place in places:
                    value = value + ref(target)[place, at, pl.ds(0, cols)].astype(f32)
                ref(grad_group)[at, pl.ds(0, cols)] = value
                if cols < most_cols:
                    ref(grad_group)[at, pl.ds(cols, most_cols - cols)] = jnp.zeros((GRAM_COLS, most_cols - cols), f32)

            over_rows(add)

        return action

    def settle(ref):
        every = range(MATRICES - 1)
        entries = ((chain, None, ()), (up_full, up_target, every), (down_full, group_target, (1, 2)), (out_mine, out_target, every))
        for which, (full, target, places) in enumerate(entries):
            pl.when(group() == which)(functools.partial(put(full, target, places, group_cols[which]), ref))

    await_all((*up_moves, *down_hops[1], *down_hops[2], *out_group_moves))
    moves.task(settle)
    return moves.run()


def update_kernel(members, sums_ref, *refs):
    row = sums_ref[pl.ds(0, 1), :]
    lane = lax.broadcasted_iota(jnp.int32, (1, LANES), 1)
    squares = jnp.sum(jnp.where(lane == 0, row, 0.0), 1, keepdims=True)
    clip = jnp.minimum(1.0, CLIP_LIMIT / (jnp.sqrt(squares) + 1e-06))
    adam_in, (rows_ref, *momenta), out = refs[:8], refs[8 : 9 + MATRICES], refs[9 + MATRICES :]
    for number, rate in enumerate((RATE_ADAM, RATE_TABLE)):
        weight, first, second, grad = [item[...] for item in adam_in[4 * number : 4 * number + 4]]
        for place, value in enumerate(adam_update(weight, first, second, clip * grad, rate)):
            out[3 * number + place][...] = value
    for which, old in enumerate(momenta):
        cols = old.shape[1] // members
        for part in range(members):
            at = (slice(None), pl.ds(part * cols, cols))
            grad = rows_ref[which * members + part, :, pl.ds(0, cols)].astype(jnp.float32)
            out[6 + which][at] = MOMENTUM * old[at] + clip * grad


def update_all(members, sums, ada, pos, grad_rows, momenta):
    rows = ada[0].shape[0]
    block = rows // UPDATE_BLOCKS

    def spec(item):
        return pl.BlockSpec((block, item.shape[1]), lambda step: (step, 0))

    arrays = [*ada, *pos]
    results = [*ada[:3], *pos[:3], *momenta]
    return pl.pallas_call(
        functools.partial(update_kernel, members),
        out_shape=[jax.ShapeDtypeStruct(item.shape, jnp.float32) for item in results],
        grid=(UPDATE_BLOCKS,),
        in_specs=[
            pl.BlockSpec(sums.shape, lambda step: (0, 0)),
            *[spec(item) for item in arrays],
            pl.BlockSpec((grad_rows.shape[0], block, grad_rows.shape[2]), lambda step: (0, step, 0)),
            *[spec(item) for item in momenta],
        ],
        out_specs=[spec(item) for item in results],
        compiler_params=pltpu.CompilerParams(vmem_limit_bytes=KERNEL_VMEM),
        name="update",
    )(sums, *arrays, grad_rows, *momenta)


def newton_schulz(source, gram, poly, once, gram_low, poly_low, once_low, block, block_next):
    size = gram.shape[0]
    eye = jnp.equal(
        lax.broadcasted_iota(jnp.int32, (GRAM_COLS, GRAM_COLS), 0),
        lax.broadcasted_iota(jnp.int32, (GRAM_COLS, GRAM_COLS), 1),
    ).astype(jnp.float32)

    tiles = size // GRAM_COLS

    def tile_at(tile):
        return pl.ds(tile * GRAM_COLS, GRAM_COLS)

    def store(full, low, tile, value, mean, excess):
        cols = tile_at(tile)
        if tile:
            above = pl.ds(0, tile * GRAM_COLS)
            full[above, cols] = value[: tile * GRAM_COLS]
            low[above, cols] = value[: tile * GRAM_COLS].astype(LOW)
            for row in range(tile):
                low[cols, tile_at(row)] = value[row * GRAM_COLS : (row + 1) * GRAM_COLS].T.astype(LOW)
        corner = value[tile * GRAM_COLS :] - excess * eye
        full[cols, cols] = corner
        low[cols, cols] = (corner - mean * eye).astype(LOW)

    def inner(tile, left, right):
        both = left * right
        return 2.0 * jnp.sum(both) - jnp.sum(both[tile * GRAM_COLS :])

    def product_cols(left, right, tile):
        return contract(left[pl.ds(0, (tile + 1) * GRAM_COLS), :], right[:, tile_at(tile)], 1, 0)

    def upper(full, tile):
        return full[pl.ds(0, (tile + 1) * GRAM_COLS), tile_at(tile)]

    def advance(gram_mean, gram_squares, last):
        poly_mean = NS_B * gram_mean + NS_C * gram_squares / size
        total = jnp.float32(0.0)
        for tile in range(tiles):
            own = upper(gram, tile)
            value = product_cols(gram_low, gram_low, tile)
            value = NS_C * value + (NS_B + 2.0 * NS_C * gram_mean) * own
            store(poly, poly_low, tile, value, poly_mean, NS_C * gram_mean * gram_mean)
            total = total + inner(tile, value, own)
        once_mean = total / size - NS_C * gram_mean * gram_mean * gram_mean

        for tile in range(block.shape[1] // GRAM_COLS):
            cols = tile_at(tile)
            value = contract(poly_low[...], block[:, cols], 1, 0)
            block_next[:, cols] = (value + (NS_A + poly_mean) * block[:, cols].astype(jnp.float32)).astype(LOW)
        block[...] = block_next[...]
        if last:
            return None

        total = jnp.float32(0.0)
        for tile in range(tiles):
            own = upper(poly, tile)
            value = product_cols(poly_low, gram_low, tile)
            value = value + poly_mean * upper(gram, tile) + gram_mean * own
            store(once, once_low, tile, value, once_mean, poly_mean * gram_mean)
            total = total + inner(tile, value, own)
        poly_once = total / size - poly_mean * gram_mean * poly_mean
        mean_next = NS_A * NS_A * gram_mean + 2.0 * NS_A * once_mean + poly_once
        excess = poly_mean * once_mean

        total = jnp.float32(0.0)
        for tile in range(tiles):
            value = product_cols(poly_low, once_low, tile)
            value = value + (2.0 * NS_A + poly_mean) * upper(once, tile) + once_mean * upper(poly, tile)
            value = value + NS_A * NS_A * upper(gram, tile)
            store(gram, gram_low, tile, value, mean_next, excess)
            total = total + inner(tile, value, value)
        return mean_next, total - excess * (2.0 * mean_next + excess) * size

    block[...] = source[...]
    mean = jnp.float32(0.0)
    for tile in range(tiles):
        mean = mean + jnp.sum(gram[tile_at(tile), tile_at(tile)] * eye)
    mean = mean / size
    squares = jnp.float32(0.0)
    for tile in range(tiles):
        cols = tile_at(tile)
        value = gram[:, cols]
        gram_low[:, cols] = value.astype(LOW)
        gram_low[cols, cols] = (gram[cols, cols] - mean * eye).astype(LOW)
        squares = squares + jnp.sum(value * value)
    state = lax.fori_loop(0, NS_ITERS - 1, lambda turn, state: advance(*state, False), (mean, squares))
    advance(*state, True)


def fast_body(
    states,
    targets,
    lengths,
    intervals,
    qkv_copy,
    qkv_master,
    qkv_moment,
    out_copy,
    out_master,
    out_moment,
    up_copy,
    up_master,
    up_moment,
    down_copy,
    down_master,
    down_moment,
    ada_copy,
    ada_master,
    ada_first,
    ada_second,
    io_proj,
    io_first,
    io_second,
    cond_table,
    cond_first,
    cond_second,
    pos_table,
    pos_first,
    pos_second,
    biases,
    bias_first,
    bias_second,
):
    ids = {}
    f32 = jnp.float32
    seq_count, shards = lax.axis_size(PATCHES), lax.axis_size(SHARDS)
    seq_index, shard = lax.axis_index(PATCHES), lax.axis_index(SHARDS)
    members = seq_count // MATRICES
    group, member = seq_index // members, lax.rem(seq_index, members)
    samples, local, values_count = states.shape
    table_rows, table_cols = cond_table.shape
    width = table_cols * shards
    ada_cols = ada_copy.shape[1]
    padded = round_up(values_count, LANES)

    value_pad = ((0, 0), (0, padded - values_count))
    state = jnp.pad(states[0].astype(f32), value_pad)
    length = lengths[0]
    id_rows = jnp.broadcast_to(intervals[:, None, None], (shards, ROLL, LANES)).reshape(-1, LANES)
    (
        extras,
        cond_vec,
        silu_low,
        embedded,
        normed_a,
        state_low,
        qkv_rows,
        io_all,
        w_out,
        w_qkv,
        pos,
    ) = begin_step(
        ids,
        members,
        state,
        id_rows,
        jnp.broadcast_to((jnp.arange(ROLL, dtype=jnp.int32)[:, None] < length).astype(f32), (ROLL, width)),
        cond_table,
        biases[None],
        pos_table.astype(LOW),
        ada_copy,
        jnp.pad(io_proj.astype(LOW), ((0, 0), (0, padded - values_count), (0, 0))),
        out_copy,
        qkv_copy,
    )
    io_all = io_all.reshape(2, padded, width)
    masters = (qkv_master, up_master, down_master, out_master)
    momenta = (qkv_moment, up_moment, down_moment, out_moment)
    group_cols = [item.shape[1] // members for item in momenta]
    most_cols = max(group_cols)

    half_rows = local // ROLL

    counts = jnp.sum((intervals[:, None] == jnp.arange(NI, dtype=jnp.int32)[None]).astype(f32), 0)
    my_id = lax.dynamic_slice_in_dim(intervals, shard, 1)
    id_count = jnp.sum((my_id == jnp.arange(NI, dtype=jnp.int32)).astype(f32) * counts)
    weight = 1.0 / (NI * local * seq_count * values_count * id_count)
    kept = []
    gathered = {}
    moment_halves = []

    for step in range(ROLL):
        moves = Moves(f"attend{step}", ids, KERNEL_VMEM)
        qkv_out = moves.output((3, local * seq_count, width // seq_count), LOW, pltpu.VMEM)
        mixed_out = moves.output((local, width), LOW, pltpu.VMEM)
        arrivals = moves.rows_to_heads(PATCHES, qkv_rows, 3, qkv_out)
        waiting = moves.gather_pairs(normed_a, hold=True)
        waiting += moves.gather_pairs(state_low, hold=True)
        if step:
            waiting += moves.gather_pairs(kept[-1][2], hold=True)
        add_attention(moves, qkv_out, mixed_out, arrivals, local, members, waiting)
        qkv, mixed, gathered_a, gathered_state, *gathered_mixed = moves.run()
        gathered.setdefault("a", {})[step] = gathered_a
        gathered.setdefault("state", {})[step] = gathered_state
        if step:
            gathered["mixed"] = {step - 1: gathered_mixed[0]}
        *results, moment_half = feed_forward(
            ids,
            step,
            extras[step],
            extras[step + 1] if step + 1 < ROLL else None,
            mixed,
            embedded,
            state,
            pos,
            w_out,
            up_copy,
            down_copy,
            io_all,
            w_qkv,
            momenta,
            members,
        )
        moment_halves.append(moment_half)
        attended, after_attn, downward, after_mlp, normed_c, state, tokens_b, upward, hidden, *following = results
        kept.append(
            (embedded, qkv, mixed, (attended, after_attn, downward, after_mlp, upward), normed_c, tokens_b, hidden)
        )
        if following:
            embedded, normed_a, state_low, qkv_rows = following

    lat = latitude_weights(local)
    diff = state - jnp.pad(targets[0].astype(f32), value_pad)
    loss_local = weight * jnp.sum(jnp.sum(diff * diff, -1) * lat)
    grad_state = 2.0 * weight * lat[:, None] * diff

    mlp_back = []

    later, mods_later = None, None
    vector_rows = [None] * ROLL

    for step in reversed(range(ROLL)):
        embedded, qkv, mixed, for_feed, normed_c, tokens_b, hidden = kept[step]
        pairs = None
        if step == 0:
            pairs = (
                ((None, UP_GRAD), [(tokens_b, None), *[(item[0], item[1]) for item in mlp_back]]),
                ((TOKENS, None), [(None, hidden), *[(item[2], item[3]) for item in mlp_back]]),
            )
        results = feed_back(
            ids,
            step,
            extras[step],
            mods_later,
            later,
            grad_state,
            for_feed,
            w_out,
            up_copy,
            down_copy,
            io_all,
            w_qkv,
            members,
            pairs,
        )
        embed_grad, vectors, grad_state, delta_grad, grad_attn, attn_grad, mixed_grad, *results = results
        tokens_down, up_grad, *weight_grads = results
        vector_rows[step] = vectors
        mlp_back.append((tokens_b, up_grad, tokens_down, hidden))
        if step == 0:
            up_mine, *up_leaving = weight_grads[:members]
            down_mine, *down_leaving = weight_grads[members:]
            up_arrived = []
            for shift, item in enumerate(up_leaving, 1):
                routes = [
                    (index, index // members * members + (index + shift) % members) for index in range(seq_count)
                ]
                up_arrived.append(lax.ppermute(item, PATCHES, routes))
        moves = Moves(f"attend_back{step}", ids, KERNEL_VMEM)
        grads_in = moves.scratch((1, local * seq_count, width // seq_count), LOW)
        result = moves.output((local, 3 * width), LOW, pltpu.VMEM)
        arrivals = moves.rows_to_heads(PATCHES, mixed_grad, 1, grads_in)
        names = ["attn", "c", "delta"]
        moves.exchange_columns(SHARDS, attn_grad)
        moves.exchange_columns(SHARDS, normed_c)
        waiting = moves.gather_pairs(delta_grad, hold=True)
        if step == ROLL - 1:
            waiting += moves.gather_pairs(mixed, hold=True)
            names.append("mixed")
        else:
            moves.exchange_columns(SHARDS, later[0])
            moves.exchange_columns(SHARDS, embed_grad)
            names += ["qkv", "embed"]
        add_attention_back(
            moves, moves.operand(qkv, pltpu.VMEM), grads_in, result, arrivals, local, members, waiting
        )
        qkv_grad, *others = moves.run()
        for name, item in zip(names, others):
            gathered.setdefault(name, {})[step + (name in ("qkv", "embed"))] = item
        later, mods_later = (qkv_grad, embedded, grad_attn), extras[step]

    block_rows = qkv_copy.shape[0]
    grad_pos, modul_all, tail_all, io_slice, grad_group = reduce_step(
        ids,
        members,
        group_cols,
        qkv_grad,
        embedded,
        grad_attn,
        extras[0],
        w_qkv,
        vector_rows[1],
        vector_rows[0],
        gathered,
        (up_mine, up_arrived, down_mine, down_leaving),
        ada_copy,
    )
    io_cols = io_slice.shape[1]
    moves = Moves("finish", ids, KERNEL_VMEM)
    vmem = functools.partial(moves.operand, space=pltpu.VMEM)
    vmem_out = functools.partial(moves.output, space=pltpu.VMEM)
    full, low = (block_rows, block_rows), (block_rows, most_cols)
    block_part = block_rows // seq_count
    grad_in, io_in, pos_in, modul_in, tail_in = [
        vmem(item) for item in (grad_group, io_slice, grad_pos, modul_all, tail_all)
    ]
    silu_in, cond_in, ids_in = vmem(silu_low), vmem(cond_vec), vmem(id_rows)
    loss_in = vmem(jnp.broadcast_to(loss_local, (1, LANES)))
    moment = moves.scratch((seq_count, block_part, most_cols), LOW)
    moment_loads = [
        moves.keep(
            moves.operand(item),
            None,
            moment,
            lambda half=half: (slice(None), pl.ds(half * half_rows, half_rows)),
        )
        for half, item in enumerate(moment_halves)
    ]
    master_loads = [moves.load(item) for item in masters]
    sums = vmem_out((8, LANES), f32)
    grad_ada = vmem_out((block_part, ada_cols), f32)
    grad_table_all = vmem_out((8, width), f32)
    io_all_parts = vmem_out((seq_count,) + io_slice.shape, LOW)
    fresh = [vmem_out(item.shape, f32) for item in masters]
    fresh_low = [moves.scratch(item.shape, LOW) for item in masters]
    near, far = [moves.scratch((count, 8, LANES), f32) for count in (shards, seq_count)]
    grad_low, source = moves.scratch(low, LOW), moves.scratch(low, LOW)
    io_low = moves.scratch(io_slice.shape, LOW)

    def measure(ref):
        def add(item, totals):
            rows = pl.ds(pl.multiple_of(item * block_part, block_part), block_part)
            old, grad = ref(moment)[item].astype(f32), ref(grad_in)[rows, :]
            ref(grad_low)[rows, :] = grad.astype(LOW)
            return totals[0] + jnp.sum(old * old), totals[1] + jnp.sum(old * grad), totals[2] + jnp.sum(grad * grad)

        zero = jnp.float32(0.0)
        terms = lax.fori_loop(0, seq_count, add, (zero, zero, zero))
        patch = lax.axis_index(PATCHES)
        count = shards * ROLL
        silu_rows = ref(silu_in)[:, pl.ds(pl.multiple_of(patch * block_part, LANES), block_part)]
        silu_rows = jnp.concatenate([silu_rows, jnp.zeros((16 - count, block_part), LOW)], 0)
        modul = jnp.concatenate([ref(modul_in)[...], jnp.zeros((16 - count, ada_cols), f32)], 0)
        modul_high = modul.astype(LOW)
        modul_rest = (modul - modul_high.astype(f32)).astype(LOW)
        value = contract(silu_rows, modul_high, 0, 0) + contract(silu_rows, modul_rest, 0, 0)
        ref(grad_ada)[...] = value
        squares = terms[2] + jnp.sum(value * value)
        squares = squares + jnp.sum(ref(io_in)[...] * ref(io_in)[...]) + jnp.sum(ref(pos_in)[...] * ref(pos_in)[...])
        ref(io_low)[...] = ref(io_in)[...].astype(LOW)
        cond = ref(cond_in)[...]
        gate = 1.0 / (1.0 + jnp.exp(-cond))
        grad_silu = sum(ref(tail_in)[item, pl.ds(0, count), pl.ds(0, width)] for item in range(shards))
        grad_cond = grad_silu * gate * (1.0 + cond * (1.0 - gate))
        row = lax.broadcasted_iota(jnp.int32, (count, 1), 0)
        ref(grad_table_all)[...] = jnp.zeros((8, width), f32)
        for entry in range(table_rows):
            chosen = (ref(ids_in)[:, :1] == entry) if entry < NI else (lax.rem(row, ROLL) == entry - NI)
            value = jnp.sum(jnp.where(chosen, grad_cond, 0.0), 0, keepdims=True)
            ref(grad_table_all)[pl.ds(entry, 1), :] = value
        me = lax.axis_index(SHARDS)
        value = ref(grad_table_all)[:, pl.ds(pl.multiple_of(me * table_cols, LANES), table_cols)]
        once = jnp.sum(value * value)
        for entry, cols in ((8, ada_cols), (9, table_cols)):
            value = ref(tail_in)[me, pl.ds(entry, 1), pl.ds(0, cols)]
            once = once + jnp.sum(value * value)
        squares = squares + jnp.where(patch == 0, once, 0.0)
        lane = lax.broadcasted_iota(jnp.int32, (8, LANES), 1)
        entries = jnp.where(lane == 0, squares, 0.0) + jnp.where(lane == 1, ref(loss_in)[...], 0.0)
        for number, term in enumerate(terms):
            entries = entries + jnp.where(lane == 2 + 3 * (patch // members) + number, term, 0.0)
        ref(near)[me] = entries

    for number in moment_loads:
        moves.wait_local(number)
    moves.task(measure)

    def spread(axis, buffer, at):
        count = lax.axis_size(axis)
        numbers = []
        for shift in range(1, count):
            numbers.append(
                moves.move(
                    (axis, shift),
                    lambda shift=shift: {axis: lax.rem(lax.axis_index(axis) + shift, count)},
                    buffer,
                    at,
                    io_all_parts if buffer is io_low else buffer,
                    lambda: (lax.axis_index(axis),),
                    later=True,
                )
            )
            moves.start(numbers[-1])
        return numbers

    def add_near(ref):
        ref(far)[lax.axis_index(PATCHES)] = jnp.sum(ref(near)[...], 0)

    def scale(ref):
        ref(sums)[...] = jnp.sum(ref(far)[...], 0)
        row = ref(sums)[pl.ds(0, 1), :]
        lane = lax.broadcasted_iota(jnp.int32, (1, LANES), 1)

        def entry(place):
            return jnp.sum(jnp.where(lane == place, row, 0.0), 1, keepdims=True)

        clip = jnp.minimum(1.0, CLIP_LIMIT / (jnp.sqrt(entry(0)) + 1e-06))
        place = 2 + 3 * (lax.axis_index(PATCHES) // members)
        size = MOMENTUM * MOMENTUM * entry(place) + 2.0 * MOMENTUM * clip * entry(place + 1)
        size = jnp.sqrt(jnp.maximum(size + clip * clip * entry(place + 2), 0.0))
        per_size = 1.0 / (size + 1e-07)

        @pl.loop(0, seq_count)
        def _(item):
            rows = pl.ds(pl.multiple_of(item * block_part, block_part), block_part)
            value = MOMENTUM * ref(moment)[item].astype(f32) + clip * ref(grad_in)[rows, :]
            ref(source)[rows, :] = (value * per_size).astype(LOW)

        ref(io_all_parts)[lax.axis_index(PATCHES)] = ref(io_low)[...]

    for number in spread(SHARDS, near, lambda: (lax.axis_index(SHARDS),)):
        moves.wait_for(number)
    moves.task(add_near)
    far_moves = spread(PATCHES, far, lambda: (lax.axis_index(PATCHES),))
    spread(PATCHES, io_low, None)
    for number in far_moves:
        moves.wait_for(number)
    moves.task(scale)

    update = moves.scratch((seq_count, block_part, most_cols), LOW)
    target = moves.scratch((members * shards,) + low, LOW)
    gram, poly, once = [moves.scratch(full, f32) for _ in range(3)]
    gram_low, poly_low, once_low = [moves.scratch(full, LOW) for _ in range(3)]
    state, state_next = [moves.scratch(low, LOW) for _ in range(2)]
    pairs = shards // 2

    def slot(back_member, back_pair, part=None):
        who_member = lax.rem(lax.rem(lax.axis_index(PATCHES), members) + members - back_member, members)
        who_shard = lax.rem(lax.axis_index(SHARDS) + shards - 2 * back_pair, shards)
        index = who_member * shards + who_shard
        return (index,) if part is None else (index, pl.ds(part * block_rows // 2, block_rows // 2))

    def add_gram(place):
        def action(ref):
            (index,) = place()

            @pl.loop(0, block_rows // GRAM_COLS)
            def _(tile):
                cols = pl.ds(pl.multiple_of(tile * GRAM_COLS, GRAM_COLS), GRAM_COLS)
                ref(gram)[:, cols] += contract(ref(target)[index], ref(target)[index, cols, :], 1, 1)

        return action

    def start_gram(ref):
        @pl.loop(0, block_rows // GRAM_COLS)
        def _(tile):
            cols = pl.ds(pl.multiple_of(tile * GRAM_COLS, GRAM_COLS), GRAM_COLS)
            ref(gram)[:, cols] = contract(ref(source)[...], ref(source)[cols, :], 1, 1)

    def pair_peer(shift):
        return {SHARDS: lax.rem(lax.axis_index(SHARDS) + 2 * shift, shards)}

    def row_part(shift):
        there = lax.rem(lax.axis_index(PATCHES) + shift, seq_count)
        size = block_rows // seq_count
        return (pl.ds(pl.multiple_of(there * size, size), size),)

    slot_own = functools.partial(slot, 0, 0)
    by_member = {
        shift: moves.move(
            (PATCHES, members, shift),
            functools.partial(member_peer, members, shift),
            source,
            None,
            target,
            slot_own,
            later=True,
        )
        for shift in range(1, members)
    }
    by_pair = {
        shift: moves.move(
            (SHARDS, 2 * shift), functools.partial(pair_peer, shift), source, None, target, slot_own, later=True
        )
        for shift in range(1, pairs)
    }
    from_sibling = [(moves.move((SHARDS,), sibling_peer, source, None, target, slot_own, later=True), slot_own)]
    for number in (*by_member.values(), *by_pair.values(), from_sibling[0][0]):
        moves.start(number)
    moves.task(start_gram)

    def sibling_place(place):
        def at():
            (index,) = place()
            return (index + 1 - 2 * lax.rem(index, 2),)

        return at

    def hand_on(place, arrivals):
        if len(arrivals) == 1:
            parts = [(place, arrivals[0])]
        else:
            parts = [(functools.partial(place, part), number) for part, number in enumerate(arrivals)]
        numbers = [
            moves.move((SHARDS,), sibling_peer, target, at, target, at, (number,)) for at, number in parts
        ]
        from_sibling.append((numbers, place))
        moves.task(add_gram(place))

    across = []
    for shift_member, first in by_member.items():
        for shift_pair, second in by_pair.items():
            top = functools.partial(slot, shift_member, 0, 0)
            bottom = functools.partial(slot, 0, shift_pair, 1)
            halves = [
                moves.move(
                    (SHARDS, 2 * shift_pair),
                    functools.partial(pair_peer, shift_pair),
                    target,
                    top,
                    target,
                    top,
                    (first,),
                ),
                moves.move(
                    (PATCHES, members, shift_member),
                    functools.partial(member_peer, members, shift_member),
                    target,
                    bottom,
                    target,
                    bottom,
                    (second,),
                ),
            ]
            across.append((functools.partial(slot, shift_member, shift_pair), halves))
    for shift, number in by_member.items():
        hand_on(functools.partial(slot, shift, 0), [number])
    for shift, number in by_pair.items():
        hand_on(functools.partial(slot, 0, shift), [number])
    moves.wait_for(from_sibling[0][0])
    moves.task(add_gram(sibling_place(slot_own)))
    for place, halves in across:
        hand_on(place, halves)
    for numbers, place in from_sibling[1:]:
        for number in numbers:
            moves.wait_for(number)
        moves.task(add_gram(sibling_place(place)))

    grad_rows = moves.output((seq_count, block_rows // seq_count, most_cols), LOW)
    for shift in range(1, seq_count):
        moves.start(
            moves.move(
                (PATCHES, shift),
                lambda shift=shift: {PATCHES: lax.rem(lax.axis_index(PATCHES) + shift, seq_count)},
                grad_low,
                lambda shift=shift: row_part(shift),
                grad_rows,
                lambda: (lax.axis_index(PATCHES),),
                later=True,
            )
        )
    moves.start_local(
        moves.keep(grad_low, lambda: row_part(0), grad_rows, lambda: (lax.axis_index(PATCHES),), True)
    )
    moves.task(
        lambda ref: newton_schulz(
            *[ref(item) for item in (source, gram, poly, once, gram_low, poly_low, once_low, state, state_next)]
        )
    )

    update_moves = []
    for shift in range(1, seq_count):
        update_moves.append(
            moves.move(
                (PATCHES, shift),
                lambda shift=shift: {PATCHES: lax.rem(lax.axis_index(PATCHES) + shift, seq_count)},
                state,
                functools.partial(row_part, shift),
                update,
                lambda: (lax.axis_index(PATCHES),),
                later=True,
            )
        )
        moves.start(update_moves[-1])

    def keep_rows(ref):
        ref(update)[lax.axis_index(PATCHES)] = ref(state)[row_part(0)]

    moves.task(keep_rows)

    def renew(ref):
        for which, (master, _) in enumerate(master_loads):
            cols = group_cols[which]
            rate = RATE_MUON * 0.2 * math.sqrt(masters[which].shape[1] * shards)
            for part in range(members):
                at = (slice(None), pl.ds(part * cols, cols))
                value = ref(update)[which * members + part, :, pl.ds(0, cols)].astype(f32)
                value = ref(master)[at] * (1.0 - RATE_MUON * DECAY_MUON) - rate * value
                ref(fresh[which])[at] = value
                ref(fresh_low[which])[at] = value.astype(LOW)

    for number in update_moves:
        moves.wait_for(number)
    for _, number in master_loads:
        moves.wait_local(number)
    moves.task(renew)

    rows = block_rows // seq_count

    def row_place(back_group, back_member, start, size):
        seq_me = lax.axis_index(PATCHES)
        who = (seq_me // members - back_group) * members
        who = who + lax.rem(lax.rem(seq_me, members) + members - back_member, members)
        return (pl.ds(pl.multiple_of(who * rows + start, 16), size),)

    def has_group(offset):
        place = lax.axis_index(PATCHES) // members + offset
        return jnp.logical_and(place >= 0, place < MATRICES)

    def to_members(item_from, from_at, item_to, place, after, there):
        numbers = []
        for shift in range(1, members):
            numbers.append(
                moves.move(
                    (PATCHES, members, shift),
                    functools.partial(member_peer, members, shift),
                    item_from,
                    from_at,
                    item_to,
                    place,
                    after,
                    there,
                    there,
                    later=True,
                )
            )
            if not after:
                moves.start(numbers[-1])
        return numbers

    def along_line(distance, way, item_from, from_at, item_to, back_member, start, size, after):
        both = lambda: jnp.logical_and(has_group(way), has_group(-distance * way))
        number = moves.move(
            (PATCHES, seq_count, way),
            functools.partial(group_peer, members, (MATRICES + way) % MATRICES),
            item_from,
            from_at,
            item_to,
            functools.partial(row_place, distance * way, back_member, start, size),
            after,
            both,
            functools.partial(has_group, -(distance + 1) * way),
            later=True,
        )
        if not after:
            moves.start(number)
        return number

    items = []
    for which, item_from in enumerate(fresh_low):
        item_to = moves.output((rows * seq_count, moves.shape(item_from)[1]), LOW)
        place = functools.partial(row_place, 0, 0, 0, rows)
        moves.start_local(moves.keep(item_from, None, item_to, place, True))
        if which:
            items.append((item_from, item_to, 0, rows, False))
        else:
            items.append((item_from, item_to, rows // 2, rows // 2, True))
            items.append((item_from, item_to, 0, rows // 2, False))
    lines = []
    for item_from, item_to, start, size, members_first in items:
        from_at = lambda start=start, size=size: (pl.ds(start, size),)
        place = functools.partial(row_place, 0, 0, start, size)
        if members_first:
            crossing = to_members(item_from, from_at, item_to, place, (), None)
        for way in (1, -1):
            number = along_line(0, way, item_from, from_at, item_to, 0, start, size, ())
            lines.append([number, way, item_to, 0, start, size, members_first])
    for item_from, item_to, start, size, members_first in items:
        if not members_first:
            from_at = lambda start=start, size=size: (pl.ds(start, size),)
            to_members(item_from, from_at, item_to, functools.partial(row_place, 0, 0, start, size), (), None)
    for item_from, item_to, start, size, members_first in items:
        if members_first:
            for back_member, number in enumerate(crossing, 1):
                place = functools.partial(row_place, 0, back_member, start, size)
                for way in (1, -1):
                    following = along_line(0, way, item_to, place, item_to, back_member, start, size, (number,))
                    lines.append([following, way, item_to, back_member, start, size, True])
    for distance in range(1, MATRICES):
        for line in lines:
            number, way, item_to, back_member, start, size, members_first = line
            place = functools.partial(row_place, distance * way, back_member, start, size)
            if distance < MATRICES - 1:
                line[0] = along_line(
                    distance, way, item_to, place, item_to, back_member, start, size, (number,)
                )
            if not members_first:
                there = functools.partial(has_group, -distance * way)
                to_members(item_to, place, item_to, place, (number,), there)
    sums, grad_ada, grad_table_all, io_slices, *rest = moves.run()
    fresh, grad_rows, copies = rest[:MATRICES], rest[MATRICES], rest[MATRICES + 1 :]
    updated = update_all(
        members,
        sums,
        (ada_master, ada_first, ada_second, grad_ada),
        (pos_table, pos_first, pos_second, grad_pos),
        grad_rows,
        momenta,
    )
    ada_res, pos_res, moments = updated[:3], updated[3:6], updated[6:]
    sums = sums[0]
    grad_norm = jnp.sqrt(sums[0])
    loss_total = sums[1]
    clip = jnp.minimum(1.0, CLIP_LIMIT / (grad_norm + 1e-06))
    terms = sums[2 : 2 + 3 * MATRICES].reshape(MATRICES, 3)
    size_squares = MOMENTUM * MOMENTUM * terms[:, 0] + 2.0 * MOMENTUM * clip * terms[:, 1] + clip * clip * terms[:, 2]
    sizes = jnp.sqrt(jnp.maximum(size_squares, 0.0))
    moment_sizes = jnp.stack([sizes[which] for which in (0, 3, 1, 2)]) / CLIP_LIMIT
    grad_table = lax.dynamic_slice_in_dim(grad_table_all[:table_rows], shard * table_cols, table_cols, 1)
    grad_bias_all = jnp.concatenate([tail_all[:, 8].reshape(-1), tail_all[:, 9, :table_cols].reshape(-1)])
    grad_bias = lax.dynamic_slice_in_dim(grad_bias_all, shard * biases.shape[0], biases.shape[0])
    io_grad = io_slices.reshape(2, padded, io_cols)[:, :values_count].astype(f32)
    io_res = adam_update(io_proj, io_first, io_second, clip * io_grad, RATE_ADAM)
    cond_res = adam_update(cond_table, cond_first, cond_second, clip * grad_table, RATE_TABLE)
    bias_res = adam_update(biases, bias_first, bias_second, clip * grad_bias, RATE_ADAM)
    matrices = []
    for which in (0, 3, 1, 2):
        matrices += [fresh[which], moments[which], copies[which]]
    return (loss_total, grad_norm, moment_sizes, *matrices, *ada_res, *io_res, *cond_res, *pos_res, *bias_res)


def fits_fast(mesh):
    seq, shards = mesh.shape[PATCHES], mesh.shape[SHARDS]
    return HEADS % seq == 0 and (HEADS // seq * HEAD) % LANES == 0 and seq % MATRICES == 0 and shards % 2 == 0


def solution(mesh):
    body = fast_body if fits_fast(mesh) else general_body
    return jax.shard_map(
        body,
        mesh=mesh,
        in_specs=(
            P(SHARDS, PATCHES, None),
            P(SHARDS, PATCHES, None),
            P(SHARDS),
            P(),
            P(None, SHARDS),
            P(PATCHES, SHARDS),
            P(PATCHES, SHARDS),
            P(None, SHARDS),
            P(PATCHES, SHARDS),
            P(PATCHES, SHARDS),
            P(None, SHARDS),
            P(PATCHES, SHARDS),
            P(PATCHES, SHARDS),
            P(None, SHARDS),
            P(PATCHES, SHARDS),
            P(PATCHES, SHARDS),
            P(None, SHARDS),
            P(PATCHES, SHARDS),
            P(PATCHES, SHARDS),
            P(PATCHES, SHARDS),
            P(None, None, SHARDS),
            P(None, None, SHARDS),
            P(None, None, SHARDS),
            P(None, SHARDS),
            P(None, SHARDS),
            P(None, SHARDS),
            P(PATCHES, SHARDS),
            P(PATCHES, SHARDS),
            P(PATCHES, SHARDS),
            P(SHARDS),
            P(SHARDS),
            P(SHARDS),
        ),
        out_specs=(
            P(),
            P(),
            P(),
            P(PATCHES, SHARDS),
            P(PATCHES, SHARDS),
            P(None, SHARDS),
            P(PATCHES, SHARDS),
            P(PATCHES, SHARDS),
            P(None, SHARDS),
            P(PATCHES, SHARDS),
            P(PATCHES, SHARDS),
            P(None, SHARDS),
            P(PATCHES, SHARDS),
            P(PATCHES, SHARDS),
            P(None, SHARDS),
            P(PATCHES, SHARDS),
            P(PATCHES, SHARDS),
            P(PATCHES, SHARDS),
            P(None, None, SHARDS),
            P(None, None, SHARDS),
            P(None, None, SHARDS),
            P(None, SHARDS),
            P(None, SHARDS),
            P(None, SHARDS),
            P(PATCHES, SHARDS),
            P(PATCHES, SHARDS),
            P(PATCHES, SHARDS),
            P(SHARDS),
            P(SHARDS),
            P(SHARDS),
        ),
        check_vma=False,
    )
```

```python
import functools
import math

import jax
import jax.numpy as jnp
from jax import lax
from jax.experimental import pallas as pl
from jax.experimental.pallas import tpu as pltpu
from jax.sharding import PartitionSpec as P

PATCHES = "seq"
SHARDS = "fsdp"
HEADS = 16
HEAD = 64
NI = 3
ROLL = 2
NS_ITERS = 5
STEP_NUM = 10
LON = 32


EPS_NORM = 1e-06
NS_A = 3.4445
NS_B = -4.775
NS_C = 2.0315
MOMENTUM = 0.5
RATE_MUON = 0.15
DECAY_MUON = 0.1
RATE_ADAM = 0.05
RATE_TABLE = 0.5
DECAY_ADAM = 0.1
BETA_FIRST = 0.9
BETA_SECOND = 0.95
CLIP_LIMIT = 0.01
HIGHEST_PRECISION = lax.Precision.HIGHEST


def broadcast(block, axis, owner):
    block = jnp.where(lax.axis_index(axis) == owner, block, jnp.zeros_like(block))
    return lax.psum(block, axis)


def product(left, right):
    return jnp.dot(left, right, preferred_element_type=jnp.float32)


def dot_last(left, right):
    return lax.dot_general(
        left, right, (((left.ndim - 1,), (1,)), ((), ())), preferred_element_type=jnp.float32
    )


def rows_product(left, right):
    flat_left = left.reshape(-1, left.shape[-1])
    flat_right = right.reshape(-1, right.shape[-1])
    return lax.dot_general(
        flat_left, flat_right, (((0,), (0,)), ((), ())), preferred_element_type=jnp.float32
    )


def layer_norm(values):
    centred = values - jnp.mean(values, -1, keepdims=True)
    inverse = lax.rsqrt(jnp.mean(centred * centred, -1, keepdims=True) + EPS_NORM)
    return (centred * inverse, inverse)


def norm_back(grad, normed, inverse):
    return inverse * (
        grad
        - jnp.mean(grad, -1, keepdims=True)
        - normed * jnp.mean(grad * normed, -1, keepdims=True)
    )


def heads_view(values):
    return values.reshape(values.shape[0], values.shape[1], HEADS, HEAD)


def modulation(modul, width):
    return [modul[:, None, column * width : (column + 1) * width] for column in range(6)]


def latitude_weights(local):
    all_patches = local * lax.axis_size(PATCHES)
    band_row = (jnp.arange(all_patches, dtype=jnp.int32) // LON).astype(jnp.float32)
    latitude = (band_row + 0.5) * (math.pi / (all_patches // LON)) - math.pi / 2
    cosine = jnp.cos(latitude)
    weights = cosine / jnp.mean(cosine)
    return lax.dynamic_slice_in_dim(weights, lax.axis_index(PATCHES) * local, local)


def forward_step(weights, state, active, select):
    w_qkv, w_out, w_up, w_down, w_ada, io_all, table, pos, bias = weights
    width = w_out.shape[0]
    cond_vec = jnp.dot(select, table.astype(jnp.float32), precision=HIGHEST_PRECISION)
    silu_low = jax.nn.silu(cond_vec).astype(jnp.bfloat16)
    modul = product(silu_low, w_ada) + bias[: 6 * width].astype(jnp.float32)
    shift1, scale1, gate1, shift2, scale2, gate2 = modulation(modul, width)
    state_low = state.astype(jnp.bfloat16)
    embedded = (
        product(state_low, io_all[0])
        + bias[6 * width :].astype(jnp.float32)
        + pos.astype(jnp.float32)
    )
    normed_one, inverse_one = layer_norm(embedded)
    normed_a = (normed_one * (1.0 + scale1) + shift1).astype(jnp.bfloat16)
    qkv = product(normed_a, w_qkv).astype(jnp.bfloat16)
    queries = qkv[..., :width]
    keys, values = (
        lax.all_gather(qkv[..., width : 2 * width], PATCHES, axis=1, tiled=True),
        lax.all_gather(qkv[..., 2 * width :], PATCHES, axis=1, tiled=True),
    )
    scores = jnp.einsum(
        "sphd,snhd->shpn", heads_view(queries), heads_view(keys), preferred_element_type=jnp.float32
    ) * HEAD ** (-0.5)
    top_score = jnp.max(scores, -1, keepdims=True)
    expo = jnp.exp(scores - top_score)
    total_exp = jnp.sum(expo, -1, keepdims=True)
    log_total = top_score + jnp.log(total_exp)
    probs_low = (expo / total_exp).astype(jnp.bfloat16)
    mixed = jnp.einsum(
        "shpn,snhd->sphd", probs_low, heads_view(values), preferred_element_type=jnp.float32
    )
    mixed_low = mixed.reshape(queries.shape).astype(jnp.bfloat16)
    attended = product(mixed_low, w_out)
    after_attn = embedded + gate1 * attended
    normed_two, inverse_two = layer_norm(after_attn)
    normed_b = (normed_two * (1.0 + scale2) + shift2).astype(jnp.bfloat16)
    upward = product(normed_b, w_up)
    hidden = jax.nn.gelu(upward).astype(jnp.bfloat16)
    downward = dot_last(hidden, w_down)
    after_mlp = after_attn + gate2 * downward
    normed_three, inverse_three = layer_norm(after_mlp)
    normed_c = normed_three.astype(jnp.bfloat16)
    delta = dot_last(normed_c, io_all[1])
    kept = (
        cond_vec,
        silu_low,
        modul,
        state_low,
        normed_one,
        inverse_one,
        normed_a,
        queries,
        keys,
        values,
        log_total,
        mixed_low,
        attended,
        normed_two,
        inverse_two,
        normed_b,
        upward,
        hidden,
        downward,
        normed_three,
        inverse_three,
        normed_c,
    )
    return (state + active * delta, kept)


def backward_step(weights, kept, grad_state, active, select):
    w_qkv, w_out, w_up, w_down, w_ada, io_all, table, pos, bias = weights
    (
        cond_vec,
        silu_low,
        modul,
        state_low,
        normed_one,
        inverse_one,
        normed_a,
        queries,
        keys,
        values,
        log_total,
        mixed_low,
        attended,
        normed_two,
        inverse_two,
        normed_b,
        upward,
        hidden,
        downward,
        normed_three,
        inverse_three,
        normed_c,
    ) = kept
    width = w_out.shape[0]
    shift1, scale1, gate1, shift2, scale2, gate2 = modulation(modul, width)
    delta_grad = (active * grad_state).astype(jnp.bfloat16)
    grad_head = rows_product(delta_grad, normed_c)
    grad_mlp = norm_back(product(delta_grad, io_all[1]), normed_three, inverse_three)
    grad_gate2 = jnp.sum(grad_mlp * downward, 1)
    down_grad = (gate2 * grad_mlp).astype(jnp.bfloat16)
    grad_down = rows_product(down_grad, hidden)
    grad_hidden = product(down_grad, w_down)
    up_grad = jax.vjp(jax.nn.gelu, upward)[1](grad_hidden)[0].astype(jnp.bfloat16)
    grad_up = rows_product(normed_b, up_grad)
    grad_normed_b = dot_last(up_grad, w_up)
    grad_scale2 = jnp.sum(grad_normed_b * normed_two, 1)
    grad_shift2 = jnp.sum(grad_normed_b, 1)
    grad_attn = grad_mlp + norm_back(grad_normed_b * (1.0 + scale2), normed_two, inverse_two)
    grad_gate1 = jnp.sum(grad_attn * attended, 1)
    attn_grad = (gate1 * grad_attn).astype(jnp.bfloat16)
    grad_out = rows_product(mixed_low, attn_grad)
    mixed_grad = dot_last(attn_grad, w_out).astype(jnp.bfloat16)
    q_heads = heads_view(queries)
    k_heads = heads_view(keys)
    v_heads = heads_view(values)
    g_heads = heads_view(mixed_grad)
    scores = jnp.einsum(
        "sphd,snhd->shpn", q_heads, k_heads, preferred_element_type=jnp.float32
    ) * HEAD ** (-0.5)
    probs = jnp.exp(scores - log_total)
    probs_low = probs.astype(jnp.bfloat16)
    grad_probs = jnp.einsum("sphd,snhd->shpn", g_heads, v_heads, preferred_element_type=jnp.float32)
    score_grad = (
        HEAD ** (-0.5) * probs * (grad_probs - jnp.sum(grad_probs * probs, -1, keepdims=True))
    ).astype(jnp.bfloat16)
    grad_queries = jnp.einsum(
        "shpn,snhd->sphd", score_grad, k_heads, preferred_element_type=jnp.float32
    ).reshape(queries.shape)
    key_part = jnp.einsum(
        "shpn,sphd->snhd", score_grad, q_heads, preferred_element_type=jnp.float32
    ).reshape(keys.shape)
    value_part = jnp.einsum(
        "shpn,sphd->snhd", probs_low, g_heads, preferred_element_type=jnp.float32
    ).reshape(values.shape)
    grad_keys, grad_values = (
        lax.psum_scatter(key_part, PATCHES, scatter_dimension=1, tiled=True),
        lax.psum_scatter(value_part, PATCHES, scatter_dimension=1, tiled=True),
    )
    qkv_grad = jnp.concatenate([grad_queries, grad_keys, grad_values], -1).astype(jnp.bfloat16)
    grad_qkv = rows_product(normed_a, qkv_grad)
    grad_normed_a = dot_last(qkv_grad, w_qkv)
    grad_scale1 = jnp.sum(grad_normed_a * normed_one, 1)
    grad_shift1 = jnp.sum(grad_normed_a, 1)
    grad_embedded = grad_attn + norm_back(grad_normed_a * (1.0 + scale1), normed_one, inverse_one)
    embed_grad = grad_embedded.astype(jnp.bfloat16)
    grad_embed = rows_product(state_low, embed_grad)
    grad_prev = grad_state + dot_last(embed_grad, io_all[0])
    grad_modul = jnp.concatenate(
        [grad_shift1, grad_scale1, grad_gate1, grad_shift2, grad_scale2, grad_gate2], -1
    )
    grad_ada = lax.dot_general(
        silu_low.astype(jnp.float32),
        grad_modul,
        (((0,), (0,)), ((), ())),
        precision=HIGHEST_PRECISION,
    )
    grad_silu = lax.dot_general(
        grad_modul, w_ada.astype(jnp.float32), (((1,), (1,)), ((), ())), precision=HIGHEST_PRECISION
    )
    grad_cond = jax.vjp(jax.nn.silu, cond_vec)[1](grad_silu)[0]
    grad_table = lax.dot_general(
        select, grad_cond, (((0,), (0,)), ((), ())), precision=HIGHEST_PRECISION
    )
    grad_bias = jnp.concatenate([jnp.sum(grad_modul, 0), jnp.sum(grad_embedded, (0, 1))])
    grad_pos = jnp.sum(grad_embedded, 0)
    grads = (
        grad_qkv,
        grad_out,
        grad_up,
        grad_down,
        grad_ada,
        jnp.stack([grad_embed, grad_head]),
        grad_table,
        grad_pos,
        grad_bias,
    )
    return (grad_prev, grads)


def gram_part(block_cols):
    return lax.dot_general(
        block_cols, block_cols, (((1,), (1,)), ((), ())), preferred_element_type=jnp.float32
    )


def zero_gram(block_cols):
    return jnp.zeros((block_cols.shape[0], block_cols.shape[0]), jnp.float32)


def newton_step(block_cols, gram):
    gram_low = gram.astype(jnp.bfloat16)
    poly = (NS_B * gram_low.astype(jnp.float32) + NS_C * product(gram_low, gram_low)).astype(
        jnp.bfloat16
    )
    return (NS_A * block_cols.astype(jnp.float32) + product(poly, block_cols)).astype(jnp.bfloat16)


def keep_block(block_cols, gram):
    return block_cols


def adam_update(weight, first, second, grad, rate):
    first_new = BETA_FIRST * first + (1.0 - BETA_FIRST) * grad
    second_new = BETA_SECOND * second + (1.0 - BETA_SECOND) * grad * grad
    unbiased = first_new / (1.0 - BETA_FIRST**STEP_NUM)
    spread = jnp.sqrt(second_new / (1.0 - BETA_SECOND**STEP_NUM)) + 1e-08
    return (weight * (1.0 - rate * DECAY_ADAM) - rate * unbiased / spread, first_new, second_new)


def general_body(
    states,
    targets,
    lengths,
    intervals,
    qkv_copy,
    qkv_master,
    qkv_moment,
    out_copy,
    out_master,
    out_moment,
    up_copy,
    up_master,
    up_moment,
    down_copy,
    down_master,
    down_moment,
    ada_copy,
    ada_master,
    ada_first,
    ada_second,
    io_proj,
    io_first,
    io_second,
    cond_table,
    cond_first,
    cond_second,
    pos_table,
    pos_first,
    pos_second,
    biases,
    bias_first,
    bias_second,
):
    weights = (
        lax.all_gather(qkv_copy, SHARDS, axis=1, tiled=True),
        lax.all_gather(out_copy, SHARDS, axis=1, tiled=True),
        lax.all_gather(up_copy, SHARDS, axis=1, tiled=True),
        lax.all_gather(down_copy, SHARDS, axis=1, tiled=True),
        lax.all_gather(ada_copy, SHARDS, axis=1, tiled=True),
        lax.all_gather(io_proj.astype(jnp.bfloat16), SHARDS, axis=2, tiled=True),
        lax.all_gather(cond_table.astype(jnp.bfloat16), SHARDS, axis=1, tiled=True),
        lax.all_gather(pos_table.astype(jnp.bfloat16), SHARDS, axis=1, tiled=True),
        lax.all_gather(biases.astype(jnp.bfloat16), SHARDS, axis=0, tiled=True),
    )
    samples, local, values_count = states.shape
    table_rows = cond_table.shape[0]
    my_ids = lax.dynamic_slice_in_dim(intervals, lax.axis_index(SHARDS) * samples, samples)
    counts = jnp.sum(
        (intervals[:, None] == jnp.arange(NI, dtype=jnp.int32)[None]).astype(jnp.float32), 0
    )
    id_counts = jnp.sum(
        (my_ids[:, None] == jnp.arange(NI, dtype=jnp.int32)[None]).astype(jnp.float32)
        * counts[None],
        1,
    )
    weight = 1.0 / (NI * local * lax.axis_size(PATCHES) * values_count * id_counts)
    rows_iota = jnp.arange(table_rows, dtype=jnp.int32)
    id_select = (my_ids[:, None] == rows_iota[None]).astype(jnp.float32)
    state = states.astype(jnp.float32)
    seen_states = []
    kept_all = []
    for step in range(ROLL):
        select = id_select + (rows_iota == NI + step).astype(jnp.float32)[None]
        active = (step < lengths).astype(jnp.float32)[:, None, None]
        seen_states.append(state)
        state, kept = forward_step(weights, state, active, select)
        kept_all.append(kept)
    lat = latitude_weights(local)
    diff = state - targets.astype(jnp.float32)
    err = jnp.sum(jnp.sum(diff * diff, -1) * lat[None], -1)
    loss_local = jnp.sum(weight * err)
    grad_state = 2.0 * weight[:, None, None] * lat[None, :, None] * diff
    totals = None
    for step in reversed(range(ROLL)):
        select = id_select + (rows_iota == NI + step).astype(jnp.float32)[None]
        active = (step < lengths).astype(jnp.float32)[:, None, None]
        kept = kept_all[step]
        grad_state, grads = backward_step(weights, kept, grad_state, active, select)
        totals = grads if totals is None else jax.tree.map(jnp.add, totals, grads)
    reduced = (
        lax.psum_scatter(totals[0], SHARDS, scatter_dimension=1, tiled=True),
        lax.psum_scatter(totals[1], SHARDS, scatter_dimension=1, tiled=True),
        lax.psum_scatter(totals[2], SHARDS, scatter_dimension=1, tiled=True),
        lax.psum_scatter(totals[3], SHARDS, scatter_dimension=1, tiled=True),
        lax.psum_scatter(totals[4], SHARDS, scatter_dimension=1, tiled=True),
        lax.psum_scatter(totals[5], SHARDS, scatter_dimension=2, tiled=True),
        lax.psum_scatter(totals[6], SHARDS, scatter_dimension=1, tiled=True),
        lax.psum_scatter(totals[7], SHARDS, scatter_dimension=1, tiled=True),
        lax.psum_scatter(totals[8], SHARDS, scatter_dimension=0, tiled=True),
    )
    large = (
        lax.psum_scatter(reduced[0], PATCHES, scatter_dimension=0, tiled=True),
        lax.psum_scatter(reduced[1], PATCHES, scatter_dimension=0, tiled=True),
        lax.psum_scatter(reduced[2], PATCHES, scatter_dimension=0, tiled=True),
        lax.psum_scatter(reduced[3], PATCHES, scatter_dimension=0, tiled=True),
        lax.psum_scatter(reduced[4], PATCHES, scatter_dimension=0, tiled=True),
    )
    small = lax.psum((reduced[5], reduced[6], reduced[8]), PATCHES)
    grad_pos = reduced[7]
    first_copy = (lax.axis_index(PATCHES) == 0).astype(jnp.float32)
    squares = jnp.sum(grad_pos * grad_pos)
    for item in large:
        squares = squares + jnp.sum(item * item)
    small_squares = jnp.float32(0.0)
    for item in small:
        small_squares = small_squares + jnp.sum(item * item)
    squares, loss_total = lax.psum(
        (squares + first_copy * small_squares, loss_local), (PATCHES, SHARDS)
    )
    grad_norm = jnp.sqrt(squares)
    clip = jnp.minimum(1.0, CLIP_LIMIT / (grad_norm + 1e-06))
    masters = (qkv_master, out_master, up_master, down_master)
    moments = [
        MOMENTUM * old + clip * grad
        for old, grad in zip((qkv_moment, out_moment, up_moment, down_moment), large[:4])
    ]
    norms = lax.psum(
        (
            jnp.sum(moments[0] * moments[0]),
            jnp.sum(moments[1] * moments[1]),
            jnp.sum(moments[2] * moments[2]),
            jnp.sum(moments[3] * moments[3]),
        ),
        (PATCHES, SHARDS),
    )
    sizes = [jnp.sqrt(norms[which]) for which in range(4)]
    moment_sizes = jnp.stack(sizes) / CLIP_LIMIT
    scaled = [(moments[which] / (sizes[which] + 1e-07)).astype(jnp.bfloat16) for which in range(4)]
    columns = (
        lax.all_gather(scaled[0], PATCHES, axis=0, tiled=True),
        lax.all_gather(scaled[1], PATCHES, axis=0, tiled=True),
        lax.all_gather(scaled[2], PATCHES, axis=0, tiled=True),
        lax.all_gather(scaled[3], PATCHES, axis=0, tiled=True),
    )
    seq_index = lax.axis_index(PATCHES)
    seq_count = lax.axis_size(PATCHES)
    owners = [seq_index == which % seq_count for which in range(4)]
    blocks = list(columns)
    for turn in range(NS_ITERS):
        partial_value = [
            lax.cond(owners[which], gram_part, zero_gram, blocks[which]) for which in range(4)
        ]
        grams = lax.psum(
            (partial_value[0], partial_value[1], partial_value[2], partial_value[3]), SHARDS
        )
        blocks = [
            lax.cond(owners[which], newton_step, keep_block, blocks[which], grams[which])
            for which in range(4)
        ]
    blocks = [broadcast(blocks[which], PATCHES, which % seq_count) for which in range(4)]
    row_count = qkv_master.shape[0]
    fresh = []
    for which in range(4):
        my_rows = lax.dynamic_slice_in_dim(
            blocks[which], seq_index * row_count, row_count, 0
        ).astype(jnp.float32)
        all_cols = masters[which].shape[1] * lax.axis_size(SHARDS)
        fresh.append(
            masters[which] * (1.0 - RATE_MUON * DECAY_MUON)
            - RATE_MUON * 0.2 * math.sqrt(all_cols) * my_rows
        )
    copies = (
        lax.all_gather(fresh[0].astype(jnp.bfloat16), PATCHES, axis=0, tiled=True),
        lax.all_gather(fresh[1].astype(jnp.bfloat16), PATCHES, axis=0, tiled=True),
        lax.all_gather(fresh[2].astype(jnp.bfloat16), PATCHES, axis=0, tiled=True),
        lax.all_gather(fresh[3].astype(jnp.bfloat16), PATCHES, axis=0, tiled=True),
    )
    ada_res = adam_update(ada_master, ada_first, ada_second, clip * large[4], RATE_ADAM)
    io_res = adam_update(io_proj, io_first, io_second, clip * small[0], RATE_ADAM)
    cond_res = adam_update(cond_table, cond_first, cond_second, clip * small[1], RATE_TABLE)
    pos_res = adam_update(pos_table, pos_first, pos_second, clip * grad_pos, RATE_TABLE)
    bias_res = adam_update(biases, bias_first, bias_second, clip * small[2], RATE_ADAM)
    return (
        loss_total,
        grad_norm,
        moment_sizes,
        fresh[0],
        moments[0],
        copies[0],
        fresh[1],
        moments[1],
        copies[1],
        fresh[2],
        moments[2],
        copies[2],
        fresh[3],
        moments[3],
        copies[3],
        ada_res[0],
        ada_res[1],
        ada_res[2],
        io_res[0],
        io_res[1],
        io_res[2],
        cond_res[0],
        cond_res[1],
        cond_res[2],
        pos_res[0],
        pos_res[1],
        pos_res[2],
        bias_res[0],
        bias_res[1],
        bias_res[2],
    )


LANES = 128
MATRICES = 4
LOW = jnp.bfloat16
MESH = pl.DeviceIdType.MESH


def round_up(value, unit):
    return -(-value // unit) * unit


def member_peer(members, shift):
    index = lax.axis_index(PATCHES)
    return {PATCHES: index // members * members + lax.rem(lax.rem(index, members) + shift, members)}


def group_peer(members, shift):
    return {PATCHES: lax.rem(lax.axis_index(PATCHES) + shift * members, lax.axis_size(PATCHES))}


def sibling_peer():
    index = lax.axis_index(SHARDS)
    return {SHARDS: index + 1 - 2 * lax.rem(index, 2)}


def where(condition, action):
    if condition is None:
        action()
    else:
        pl.when(condition())(action)


class Moves:
    def __init__(self, name, ids, vmem=None):
        self.name = name
        self.ids = ids
        self.vmem = vmem
        self.operands = []
        self.operand_specs = []
        self.outputs = []
        self.output_specs = []
        self.scratches = []
        self.moves = []
        self.locals = []
        self.steps = []
        self.peers = {}

    def operand(self, array, space=pl.ANY):
        self.operands.append(array)
        self.operand_specs.append(pl.BlockSpec(memory_space=space))
        return (0, len(self.operands) - 1)

    def output(self, shape, dtype, space=pl.ANY):
        self.outputs.append(jax.ShapeDtypeStruct(shape, dtype))
        self.output_specs.append(pl.BlockSpec(memory_space=space))
        return (1, len(self.outputs) - 1)

    def scratch(self, shape, dtype):
        self.scratches.append(pltpu.VMEM(shape, dtype))
        return (2, len(self.scratches) - 1)

    def keep(self, source, source_at, target, target_at, later=False):
        self.locals.append((source, source_at, target, target_at, later))
        return len(self.locals) - 1

    def shape(self, scratch):
        return self.scratches[scratch[1]].shape

    def load(self, array):
        target = self.scratch(array.shape, array.dtype)
        return target, self.keep(self.operand(array), None, target, None)

    def prefetch(self, array):
        target, number = self.load(array)
        self.steps.insert(0, (self.await_local, number))
        return target

    def save(self, source, shape, dtype):
        number = self.keep(source, None, self.output(shape, dtype), None, True)
        return number

    def start_local(self, number):
        self.steps.append((self.begin_local, number))

    def begin_local(self, number):
        self.local[number].start()

    def move(
        self, peer_key, peer, source, source_at, target, target_at, after=(), sends=None, takes=None, later=False
    ):
        number = len(self.moves)
        self.peers.setdefault(peer_key, peer)
        self.moves.append((peer_key, source, source_at, target, target_at, sends, takes, later or bool(after)))
        for earlier in after:
            self.steps.append((self.await_move, earlier))
        if after:
            self.steps.append((self.start_move, number))
        return number

    def wait_for(self, number):
        self.steps.append((self.await_move, number))

    def start(self, number):
        self.steps.append((self.start_move, number))

    def wait_local(self, number):
        self.steps.append((self.await_local, number))

    def task(self, action):
        self.steps.append((self.do_task, action))

    def await_move(self, number):
        if number not in self.arrived:
            self.arrived.add(number)
            where(self.moves[number][6], self.remote[number].wait_recv)

    def start_move(self, number):
        where(self.moves[number][5], self.remote[number].start)

    def await_local(self, number):
        if number not in self.kept:
            self.kept.add(number)
            self.local[number].wait()

    def do_task(self, action):
        action(self.ref)

    def ref(self, which):
        return self.refs[which[0]][which[1]]

    def view(self, which, index):
        ref = self.ref(which)
        return ref.at[index()] if index is not None else ref

    def kernel(self, *refs):
        sizes = (len(self.operands), len(self.outputs), len(self.scratches))
        self.refs = (refs[: sizes[0]], refs[sizes[0] : sizes[0] + sizes[1]], refs[sizes[0] + sizes[1] : sum(sizes)])
        local_sem, send_sem, recv_sem = refs[sum(sizes) :]
        self.arrived, self.kept = set(), set()
        self.local = [
            pltpu.make_async_copy(self.view(source, source_at), self.view(target, target_at), local_sem.at[number])
            for number, (source, source_at, target, target_at, _) in enumerate(self.locals)
        ]
        for copy, entry in zip(self.local, self.locals):
            if not entry[4]:
                copy.start()
        devices = {key: peer() for key, peer in self.peers.items()}
        barrier = pltpu.get_barrier_semaphore()
        for device in devices.values():
            pl.semaphore_signal(barrier, inc=1, device_id=device, device_id_type=MESH)
        pl.semaphore_wait(barrier, len(devices))
        self.remote = []
        for number, (key, source, source_at, target, target_at, _, _, later) in enumerate(self.moves):
            self.remote.append(
                pltpu.make_async_remote_copy(
                    src_ref=self.view(source, source_at),
                    dst_ref=self.view(target, target_at),
                    send_sem=send_sem.at[number],
                    recv_sem=recv_sem.at[number],
                    device_id=devices[key],
                    device_id_type=MESH,
                )
            )
            if not later:
                self.start_move(number)
        for action, number in self.steps:
            action(number)
        for number in range(len(self.locals)):
            self.await_local(number)
        for number, copy in enumerate(self.remote):
            self.await_move(number)
            where(self.moves[number][5], copy.wait_send)

    def run(self):
        return pl.pallas_call(
            self.kernel,
            out_shape=self.outputs,
            in_specs=self.operand_specs,
            out_specs=self.output_specs,
            scratch_shapes=[
                *self.scratches,
                pltpu.SemaphoreType.DMA((max(1, len(self.locals)),)),
                pltpu.SemaphoreType.DMA((len(self.moves),)),
                pltpu.SemaphoreType.DMA((len(self.moves),)),
            ],
            compiler_params=pltpu.CompilerParams(
                collective_id=self.ids.setdefault(self.name, len(self.ids)),
                has_side_effects=True,
                vmem_limit_bytes=self.vmem,
            ),
            name=self.name,
        )(*self.operands)

    def along(self, axis, source, target, pairs, later=False):
        numbers = []
        count = lax.axis_size(axis)

        def other(shift):
            return lax.rem(lax.axis_index(axis) + shift, count)

        for shift in range(1, count):
            for source_at, target_at in pairs:
                numbers.append(
                    self.move(
                        (axis, shift),
                        lambda shift=shift: {axis: other(shift)},
                        source,
                        None if source_at is None else (lambda at=source_at, shift=shift: at(other(shift))),
                        target,
                        lambda at=target_at: at(lax.axis_index(axis)),
                        later=later,
                    )
                )
        for source_at, target_at in pairs:
            local = self.keep(
                source,
                None if source_at is None else (lambda at=source_at: at(lax.axis_index(axis))),
                target,
                lambda at=target_at: at(lax.axis_index(axis)),
                later,
            )
            if later:
                self.start_local(local)
        if later:
            for number in numbers:
                self.start(number)
        return numbers

    def gather(self, axis, array):
        target = self.output((lax.axis_size(axis),) + array.shape, array.dtype)
        self.along(axis, self.operand(array), target, [(None, lambda sender: (sender,))])

    def gather_pairs(self, array, parts=1, hold=False):
        shards = lax.axis_size(SHARDS)
        source = self.operand(array)
        target = self.output((shards,) + array.shape, array.dtype)
        rows = array.shape[0] // parts

        def place(back_pair, part):
            return (lax.rem(lax.axis_index(SHARDS) + shards - 2 * back_pair, shards), pl.ds(part * rows, rows))

        firsts = []
        for part in range(parts):
            for pair in range(1, shards // 2):
                number = self.move(
                    (SHARDS, 2 * pair),
                    lambda pair=pair: {SHARDS: lax.rem(lax.axis_index(SHARDS) + 2 * pair, shards)},
                    source,
                    lambda part=part: (pl.ds(part * rows, rows),),
                    target,
                    functools.partial(place, 0, part),
                )
                firsts.append((functools.partial(place, pair, part), number))
        own = lambda: (lax.axis_index(SHARDS),)
        self.move((SHARDS,), sibling_peer, source, None, target, own)
        self.keep(source, None, target, own)
        waiting = [(target, at, number) for at, number in firsts]
        if hold:
            return waiting
        self.to_sibling(waiting)

    def gather_columns(self, axis, array, target):
        width = array.shape[-1]
        lead = (slice(None),) * (array.ndim - 1)
        numbers = self.along(
            axis,
            self.operand(array),
            target,
            [(None, lambda sender: lead + (pl.ds(pl.multiple_of(sender * width, LANES), width),))],
        )
        return numbers, len(self.locals) - 1

    def gather_twice(self, arrays, members, chunks):
        shards = lax.axis_size(SHARDS)
        entries = []
        for array, pieces in zip(arrays, chunks):
            source = self.operand(array)
            width = array.shape[1]
            target = self.scratch((array.shape[0], shards * width), array.dtype)
            rows = array.shape[0] // members // pieces

            def columns(back_pair, width=width):
                who = lax.rem(lax.axis_index(SHARDS) + shards - 2 * back_pair, shards)
                return pl.ds(pl.multiple_of(who * width, LANES), width)

            def piece_rows(back_member, piece, rows=rows, pieces=pieces):
                index = lax.rem(lax.rem(lax.axis_index(PATCHES), members) + members - back_member, members)
                return pl.ds(pl.multiple_of((index * pieces + piece) * rows, rows), rows)

            def place(back_member, back_pair, piece, columns=columns, piece_rows=piece_rows):
                return (piece_rows(back_member, piece), columns(back_pair))

            def mine(piece, piece_rows=piece_rows):
                return (piece_rows(0, piece),)

            def whole(columns=columns):
                return (slice(None), columns(0))

            firsts = [
                (
                    pair,
                    piece,
                    self.move(
                        (SHARDS, 2 * pair),
                        lambda pair=pair: {SHARDS: lax.rem(lax.axis_index(SHARDS) + 2 * pair, shards)},
                        source,
                        functools.partial(mine, piece),
                        target,
                        functools.partial(place, 0, 0, piece),
                    ),
                )
                for piece in range(pieces)
                for pair in range(1, shards // 2)
            ]
            near = self.move((SHARDS,), sibling_peer, source, None, target, whole)
            local = self.keep(source, None, target, whole)
            entries.append((target, place, firsts, [near, *[number for _, _, number in firsts]], local))
        last = []
        for target, place, firsts, numbers, _ in entries:
            for pair, piece, first in firsts:
                near = functools.partial(place, 0, pair, piece)
                for shift in range(1, members):
                    number = self.move(
                        (PATCHES, members, shift),
                        functools.partial(member_peer, members, shift),
                        target,
                        near,
                        target,
                        near,
                        (first,),
                    )
                    last.append((target, functools.partial(place, shift, pair, piece), number, numbers))
                numbers.append(self.move((SHARDS,), sibling_peer, target, near, target, near, (first,)))
        for target, at, number, numbers in last:
            numbers += [number, self.move((SHARDS,), sibling_peer, target, at, target, at, (number,))]
        return [(target, numbers, local) for target, _, _, numbers, local in entries]

    def to_sibling(self, waiting):
        for target, place, number in waiting:
            self.move((SHARDS,), sibling_peer, target, place, target, place, (number,))

    def exchange(self, axis, array, later=False):
        target = self.output(array.shape, array.dtype)
        return self.along(
            axis, self.operand(array), target, [(lambda receiver: (receiver,), lambda sender: (sender,))], later
        )

    def exchange_columns(self, axis, array):
        width = array.shape[-1] // lax.axis_size(axis)
        target = self.output((lax.axis_size(axis), array.shape[0], width), array.dtype)
        self.along(
            axis,
            self.operand(array),
            target,
            [
                (
                    lambda receiver: (slice(None), pl.ds(pl.multiple_of(receiver * width, LANES), width)),
                    lambda sender: (sender,),
                )
            ],
        )

    def rows_to_heads(self, axis, array, planes, target):
        count, rows = lax.axis_size(axis), array.shape[0]
        columns = array.shape[1] // planes
        width = columns // count
        return self.along(
            axis,
            self.operand(array),
            target,
            [
                (
                    lambda receiver, plane=plane: (
                        slice(None),
                        pl.ds(pl.multiple_of(plane * columns + receiver * width, LANES), width),
                    ),
                    lambda sender, plane=plane: (plane, pl.ds(pl.multiple_of(sender * rows, rows), rows)),
                )
                for plane in range(planes)
            ],
        )

    def head_rows(self, source, target, planes, rows, columns, members, back_group):
        count = lax.axis_size(PATCHES)
        width = columns // count
        for shift_member in range(members):
            for plane in planes:

                def peer(shift_member=shift_member):
                    index = lax.axis_index(PATCHES)
                    there = lax.rem(index // members + back_group, MATRICES) * members
                    return there + lax.rem(lax.rem(index, members) + shift_member, members)

                def source_at(peer=peer, plane=plane):
                    return (plane, pl.ds(pl.multiple_of(peer() * rows, rows), rows))

                def target_at(plane=plane):
                    start = plane * columns + lax.axis_index(PATCHES) * width
                    return (slice(None), pl.ds(pl.multiple_of(start, LANES), width))

                if shift_member or back_group:
                    self.start(
                        self.move(
                            (PATCHES, count, back_group, shift_member),
                            lambda peer=peer: {PATCHES: peer()},
                            source,
                            source_at,
                            target,
                            target_at,
                            later=True,
                        )
                    )
                else:

                    def own(ref, source_at=source_at, target_at=target_at):
                        ref(target)[target_at()] = ref(source)[source_at()]

                    self.task(own)


def contract(left, right, left_dim, right_dim):
    return lax.dot_general(
        left, right, (((left_dim,), (right_dim,)), ((), ())), preferred_element_type=jnp.float32
    )


CHAIN_CHUNKS = 8
DOWN_CHUNKS = 4
KERNEL_VMEM = 62 * 2**20
UPDATE_BLOCKS = 4
GRAM_COLS = 256


def attend(queries, keys, values):
    scores = contract(queries, keys, 1, 1) * HEAD ** (-0.5)
    expo = jnp.exp(scores - jnp.max(scores, -1, keepdims=True))
    probs = (expo / jnp.sum(expo, -1, keepdims=True)).astype(LOW)
    return contract(probs, values, 1, 0)


def group_rows(rows, members, shift):
    size = rows * members
    there = lax.rem(lax.axis_index(PATCHES) // members + shift, MATRICES)
    return pl.ds(pl.multiple_of(there * size, size), size)


def add_attention(moves, qkv, mixed, arrivals, rows, members, waiting):
    for number in arrivals:
        moves.wait_for(number)
    for number in range(3):
        moves.wait_local(number)
    moves.to_sibling(waiting)
    count = lax.axis_size(PATCHES)
    width = HEADS // count * HEAD
    buffer = moves.scratch((1, rows * count, width), LOW)
    for shift in (*range(1, MATRICES), 0):

        def work(ref, shift=shift):
            at = group_rows(rows, members, shift)
            parts = []
            for head in range(width // HEAD):
                lanes = pl.ds(head * HEAD, HEAD)
                parts.append(attend(ref(qkv)[0, at, lanes], ref(qkv)[1, :, lanes], ref(qkv)[2, :, lanes]))
            ref(buffer)[0, at, :] = jnp.concatenate(parts, -1).astype(LOW)

        moves.task(work)
        moves.head_rows(buffer, mixed, (0,), rows, width * count, members, shift)


def add_attention_back(moves, qkv, grads, result, arrivals, rows, members, waiting):
    for number in arrivals:
        moves.wait_for(number)
    moves.wait_local(0)
    moves.to_sibling(waiting)
    count = lax.axis_size(PATCHES)
    width = HEADS // count * HEAD
    heads = width // HEAD
    buffer = moves.scratch((3, rows * count, width), LOW)
    key_total = moves.scratch((heads, rows * count, HEAD), jnp.float32)
    value_total = moves.scratch((heads, rows * count, HEAD), jnp.float32)
    for shift in (*range(1, MATRICES), 0):

        def work(ref, shift=shift):
            at = group_rows(rows, members, shift)
            parts = []
            for head in range(heads):
                lanes = pl.ds(head * HEAD, HEAD)
                queries, keys, values = ref(qkv)[0, at, lanes], ref(qkv)[1, :, lanes], ref(qkv)[2, :, lanes]
                grad = ref(grads)[0, at, lanes]
                scores = contract(keys, queries, 1, 1) * HEAD ** (-0.5)
                expo = jnp.exp(scores - jnp.max(scores, 0, keepdims=True))
                probs = expo / jnp.sum(expo, 0, keepdims=True)
                grad_probs = contract(values, grad, 1, 1)
                shared = jnp.sum(grad_probs * probs, 0, keepdims=True)
                score_grad = (HEAD ** (-0.5) * probs * (grad_probs - shared)).astype(LOW)
                parts.append(contract(score_grad, keys, 0, 0))
                key_part = contract(score_grad, queries, 1, 0)
                value_part = contract(probs.astype(LOW), grad, 1, 0)
                if shift == 1:
                    ref(key_total)[head] = key_part
                    ref(value_total)[head] = value_part
                else:
                    ref(key_total)[head] += key_part
                    ref(value_total)[head] += value_part
            ref(buffer)[0, at, :] = jnp.concatenate(parts, -1).astype(LOW)

        moves.task(work)
        moves.head_rows(buffer, result, (0,), rows, width * count, members, shift)

    def finish(ref):
        for plane, total in ((1, key_total), (2, value_total)):
            ref(buffer)[plane] = jnp.concatenate([ref(total)[head] for head in range(heads)], -1).astype(LOW)

    moves.task(finish)
    for shift in (*range(1, MATRICES), 0):
        moves.head_rows(buffer, result, (1, 2), rows, width * count, members, shift)


def mod_row(ref, table, row):
    return ref(table)[pl.ds(row, 1), :]


def project(moves, source, weights, target, count):
    def action(ref):
        width = ref(source).shape[1]

        @pl.loop(0, count // width)
        def _(part):
            cols = pl.ds(pl.multiple_of(part * width, width), width)
            ref(target)[:, cols] = contract(ref(source)[...], ref(weights)[:, cols], 1, 0).astype(LOW)

    moves.task(action)


def embed(ref, state_low, io_weights, mods, pos, embedded, normed_low):
    value = contract(ref(state_low)[...], io_weights, 1, 0) + mods(6) + ref(pos)[...].astype(jnp.float32)
    ref(embedded)[...] = value
    normed, _ = layer_norm(value)
    ref(normed_low)[...] = (normed * (1.0 + mods(1)) + mods(0)).astype(LOW)


def begin_step(ids, members, state, id_rows, active, cond_table, biases, pos, ada, io_low, w_out, w_qkv):
    f32 = jnp.float32
    shards = lax.axis_size(SHARDS)
    (rows, padded), (table_rows, _) = state.shape, cond_table.shape
    width = w_out.shape[0]
    ada_cols = ada.shape[1]
    moves = Moves("begin", ids, KERNEL_VMEM)
    table = moves.scratch((table_rows, width), f32)
    bias = moves.scratch((1, biases.shape[1] * shards), f32)
    pos_all = moves.scratch((rows, width), LOW)
    id_rows, active, state = [moves.prefetch(item) for item in (id_rows, active, state)]
    small = [moves.gather_columns(SHARDS, cond_table, table), moves.gather_columns(SHARDS, biases, bias)]
    pos_moves, pos_local = moves.gather_columns(SHARDS, pos, pos_all)
    ada_weights, ada_load = moves.load(ada)
    vmem = functools.partial(moves.output, space=pltpu.VMEM)
    extras = vmem((ROLL, 8, width), f32)
    cond_vec, silu_low = vmem((shards * ROLL, width), f32), vmem((shards * ROLL, width), LOW)
    embedded, normed_low = vmem((rows, width), f32), vmem((rows, width), LOW)
    state_low, qkv_rows = vmem((rows, padded), LOW), vmem((rows, 3 * width), LOW)
    parts_leaving, parts = [moves.scratch((shards, ROLL, ada_cols), f32) for _ in range(2)]

    def modulate(ref):
        row = lax.broadcasted_iota(jnp.int32, (shards * ROLL, 1), 0)
        ids_here = ref(id_rows)[:, :1]
        value = jnp.zeros((shards * ROLL, width), f32)
        for entry in range(table_rows):
            of_entry = ref(table)[pl.ds(entry, 1), :].astype(LOW).astype(f32)
            chosen = (ids_here == entry) if entry < NI else (lax.rem(row, ROLL) == entry - NI)
            value = value + jnp.where(chosen, of_entry, 0.0)
        ref(cond_vec)[...] = value
        value = (value / (1.0 + jnp.exp(-value))).astype(LOW)
        ref(silu_low)[...] = value
        start = pl.multiple_of(lax.axis_index(SHARDS) * ada_cols, LANES)
        value = contract(value, ref(ada_weights)[...], 1, 0)
        value = value + ref(bias)[:, pl.ds(start, ada_cols)].astype(LOW).astype(f32)
        for sample in range(shards):
            ref(parts_leaving)[sample] = value[sample * ROLL : (sample + 1) * ROLL]
        ref(parts)[lax.axis_index(SHARDS)] = ref(parts_leaving)[lax.axis_index(SHARDS)]

    for numbers, local in small:
        for number in numbers:
            moves.wait_for(number)
        moves.wait_local(local)
    moves.wait_local(ada_load)
    moves.task(modulate)
    modul_moves = []
    for shift in range(1, shards):

        def other(shift=shift):
            return lax.rem(lax.axis_index(SHARDS) + shift, shards)

        number = moves.move(
            (SHARDS, shift),
            lambda other=other: {SHARDS: other()},
            parts_leaving,
            lambda other=other: (other(),),
            parts,
            lambda: (lax.axis_index(SHARDS),),
            later=True,
        )
        modul_moves.append(number)
        moves.start(number)
    weights = moves.gather_twice((io_low.reshape(-1, io_low.shape[-1]), w_out, w_qkv), members, (1, 1, 4))

    def collect(ref):
        bias_row = ref(bias)[:, pl.ds(6 * width, width)].astype(LOW).astype(f32)
        for step in range(ROLL):
            for piece in range(6 * 2):
                start = piece * width // 2
                value = ref(parts)[start // ada_cols, pl.ds(step, 1), pl.ds(start % ada_cols, width // 2)]
                ref(extras)[step, pl.ds(piece // 2, 1), pl.ds(piece % 2 * width // 2, width // 2)] = value
            ref(extras)[step, pl.ds(6, 1), :] = bias_row
            ref(extras)[step, pl.ds(7, 1), :] = ref(active)[pl.ds(step, 1), :]

    def start_step(ref):
        ref(state_low)[...] = ref(state)[...].astype(LOW)
        mods = lambda row: ref(extras)[0, pl.ds(row, 1), :]
        embed(ref, state_low, ref(weights[0][0])[pl.ds(0, padded), :], mods, pos_all, embedded, normed_low)

    for number in modul_moves:
        moves.wait_for(number)
    moves.task(collect)
    for number in (*pos_moves, *weights[0][1]):
        moves.wait_for(number)
    moves.wait_local(pos_local)
    moves.wait_local(weights[0][2])
    moves.task(start_step)
    for target, numbers, local in weights:
        for number in numbers:
            moves.wait_for(number)
        moves.wait_local(local)
        save = moves.save(target, moves.shape(target), LOW)
        moves.start_local(save)
    moves.start_local(moves.save(pos_all, (rows, width), LOW))
    project(moves, normed_low, weights[2][0], qkv_rows, 3 * width)
    return moves.run()


class Tokens:
    def __init__(self, moves, rows, width):
        self.moves = moves
        self.shards = lax.axis_size(SHARDS)
        self.rows = rows
        self.tokens = moves.scratch((self.shards, rows, width), LOW)
        self.own_part = moves.scratch((rows, width), jnp.float32)
        self.leaving = moves.scratch((self.shards, rows, width), LOW)
        self.arriving = moves.scratch((self.shards, rows, width), LOW)

    def me(self):
        return lax.axis_index(SHARDS)

    def back(self, pair, sibling):
        index = lax.rem(self.me() + self.shards - 2 * pair, self.shards)
        return index + 1 - 2 * lax.rem(index, 2) if sibling else index

    def part(self, pair, sibling, work):
        moves = self.moves
        slot = functools.partial(self.back, pair, sibling)

        def action(ref):
            value = work(ref, slot())
            if pair or sibling:
                ref(self.leaving)[slot()] = value.astype(LOW)
            else:
                ref(self.own_part)[...] = value

        moves.task(action)
        if pair or sibling:
            number = moves.move(
                (SHARDS, pair, sibling),
                lambda: {SHARDS: slot()},
                self.leaving,
                lambda: (slot(),),
                self.arriving,
                lambda: (self.me(),),
                later=True,
            )
            moves.start(number)
            self.parts.append(number)

    def run(self, work):
        moves, halves = self.moves, 2
        self.parts = []
        size = self.rows // halves
        pairs = self.shards // 2

        def half(pair, sibling, number):
            return (self.back(pair, sibling), pl.ds(number * size, size))

        firsts = {}
        for pair in range(1, pairs):
            for number in range(halves):
                place = functools.partial(half, 0, False, number)
                firsts[pair, number] = moves.move(
                    (SHARDS, pairs - pair, False),
                    functools.partial(lambda pair: {SHARDS: self.back(pairs - pair, False)}, pair),
                    self.tokens,
                    place,
                    self.tokens,
                    place,
                    later=True,
                )
                moves.start(firsts[pair, number])
        own = functools.partial(self.back, 0, False)
        near = moves.move(
            (SHARDS, 0, True), sibling_peer, self.tokens, lambda: (own(),), self.tokens, lambda: (own(),), later=True
        )
        moves.start(near)
        self.part(0, False, work)
        moves.wait_for(near)
        self.part(0, True, work)
        for pair in range(1, pairs):
            handed = []
            for number in range(halves):
                place = functools.partial(half, pair, False, number)
                handed.append(
                    moves.move(
                        (SHARDS, 0, True),
                        sibling_peer,
                        self.tokens,
                        place,
                        self.tokens,
                        place,
                        (firsts[pair, number],),
                    )
                )
            self.part(pair, False, work)
            for number in handed:
                moves.wait_for(number)
            self.part(pair, True, work)

    def wait(self):
        for number in self.parts:
            self.moves.wait_for(number)

    def total(self, ref):
        value = ref(self.own_part)[...]
        for shift in range(1, self.shards):
            value = value + ref(self.arriving)[lax.rem(self.me() + shift, self.shards)].astype(jnp.float32)
        return value


TOKENS, UP_GRAD = 1, 2
GELU_SCALE = math.sqrt(2.0 / math.pi)
GELU_CUBE = 0.044715


def gelu_inner(values):
    return jnp.tanh(GELU_SCALE * (values + GELU_CUBE * values * values * values))


def gelu_slope(values):
    inner = gelu_inner(values)
    rise = GELU_SCALE * (1.0 + 3.0 * GELU_CUBE * values * values)
    return 0.5 * (1.0 + inner) + 0.5 * values * (1.0 - inner * inner) * rise


def feed_forward(ids, step, mods, mods_next, mixed, embedded, state, pos, w_out, w_up, w_down, io_all, w_qkv, momenta, members):
    f32 = jnp.float32
    last = mods_next is None
    rows, width = mixed.shape
    padded = state.shape[1]
    hidden_count = w_up.shape[1]
    shards = lax.axis_size(SHARDS)
    moves = Moves(f"feed{step}", ids, KERNEL_VMEM)
    vmem = moves.prefetch
    out_weights, out_load = moves.load(w_out)
    mods, mixed, embedded, state = vmem(mods), vmem(mixed), vmem(embedded), vmem(state)
    up_weights, up_load = moves.load(w_up)
    down_weights, down_load = moves.load(w_down)
    io_weights, io_load = moves.load(io_all)
    attended, after_attn, downward, after_mlp = [moves.output((rows, width), f32, pltpu.VMEM) for _ in range(4)]
    normed_c = moves.output((rows, width), LOW, pltpu.VMEM)
    state_next = moves.output((rows, padded), f32, pltpu.VMEM)
    upward = moves.scratch((shards, rows, hidden_count), f32)
    hidden = moves.scratch((shards, rows, hidden_count), LOW)
    feed = Tokens(moves, rows, width)
    saves = [
        moves.save(feed.tokens, (shards, rows, width), LOW),
        moves.save(upward, (shards, rows, hidden_count), f32),
        moves.save(hidden, (shards, rows, hidden_count), LOW),
    ]
    if not last:
        mods_next, pos = vmem(mods_next), vmem(pos)
        qkv_weights, qkv_load = moves.load(w_qkv)
        embedded_next = moves.output((rows, width), f32, pltpu.VMEM)
        normed_next = moves.output((rows, width), LOW, pltpu.VMEM)
        state_low = moves.output((rows, padded), LOW, pltpu.VMEM)
        qkv_next = moves.output((rows, w_qkv.shape[1]), LOW, pltpu.VMEM)
    half = rows // ROLL
    seq_count = lax.axis_size(PATCHES)
    most_cols = max(item.shape[1] for item in momenta) // members
    moment_loads = []
    for item in momenta:
        scratch = moves.scratch((half, item.shape[1]), f32)
        number = moves.keep(moves.operand(item), lambda: (pl.ds(step * half, half),), scratch, None)
        moment_loads.append((scratch, number))
    moment_leaving = moves.scratch((seq_count, half, most_cols), LOW)
    moment_arriving = moves.output((seq_count, half, most_cols), LOW)

    def pack(ref):
        for which, (scratch, _) in enumerate(moment_loads):
            cols = momenta[which].shape[1] // members
            for part in range(members):
                value = ref(scratch)[:, part * cols : (part + 1) * cols].astype(LOW)
                if cols < most_cols:
                    value = jnp.concatenate([value, jnp.zeros((half, most_cols - cols), LOW)], 1)
                ref(moment_leaving)[which * members + part] = value

    def begin(ref):
        value = contract(ref(mixed)[...], ref(out_weights)[...], 1, 0)
        ref(attended)[...] = value
        value = ref(embedded)[...] + mod_row(ref, mods, 2) * value
        ref(after_attn)[...] = value
        normed, _ = layer_norm(value)
        normed = normed * (1.0 + mod_row(ref, mods, 4)) + mod_row(ref, mods, 3)
        ref(feed.tokens)[feed.me()] = normed.astype(LOW)

    def work(ref, slot):
        value = contract(ref(feed.tokens)[slot], ref(up_weights)[...], 1, 0)
        ref(upward)[slot] = value
        value = (0.5 * value * (1.0 + gelu_inner(value))).astype(LOW)
        ref(hidden)[slot] = value
        return contract(value, ref(down_weights)[...], 1, 1)

    def finish(ref):
        value = feed.total(ref)
        ref(downward)[...] = value
        value = ref(after_attn)[...] + mod_row(ref, mods, 5) * value
        ref(after_mlp)[...] = value
        normed, _ = layer_norm(value)
        normed = normed.astype(LOW)
        ref(normed_c)[...] = normed
        delta = contract(normed, ref(io_weights)[1], 1, 1)
        value = ref(state)[...] + mod_row(ref, mods, 7)[:, :padded] * delta
        ref(state_next)[...] = value
        if not last:
            ref(state_low)[...] = value.astype(LOW)
            mods_there = functools.partial(mod_row, ref, mods_next)
            embed(ref, state_low, ref(io_weights)[0], mods_there, pos, embedded_next, normed_next)

    moves.wait_local(out_load)
    moves.task(begin)
    moves.wait_local(up_load)
    moves.wait_local(down_load)
    feed.run(work)
    for number in saves:
        moves.start_local(number)
    for _, number in moment_loads:
        moves.wait_local(number)
    moves.task(pack)
    moves.along(
        PATCHES, moment_leaving, moment_arriving, [(lambda there: (there,), lambda sender: (sender,))], later=True
    )
    moves.wait_local(io_load)
    feed.wait()
    moves.task(finish)
    if not last:
        moves.wait_local(qkv_load)
        project(moves, normed_next, qkv_weights, qkv_next, w_qkv.shape[1])
    return moves.run()


def feed_back(ids, step, mods, mods_later, later, grad_state, kept, w_out, w_up, w_down, io_all, w_qkv, members, pairs):
    f32 = jnp.float32
    attended, after_attn, downward, after_mlp, upward = kept
    rows, width = attended.shape
    padded = grad_state.shape[1]
    hidden_count = w_up.shape[1]
    shards = lax.axis_size(SHARDS)
    moves = Moves(f"feed_back{step}", ids, KERNEL_VMEM)
    vmem = moves.prefetch
    io_weights, io_load = moves.load(io_all)
    if later is not None:
        qkv_weights, qkv_load = moves.load(w_qkv)
        later = [vmem(item) for item in later]
        mods_later = vmem(mods_later)
        embed_grad = moves.output((rows, width), LOW, pltpu.VMEM)
    down_weights, down_load = moves.load(w_down)
    up_weights, up_load = moves.load(w_up)
    slopes, slopes_load = moves.load(upward)
    out_weights, out_load = moves.load(w_out)
    mods, grad_state = vmem(mods), vmem(grad_state)
    attended, after_attn, downward, after_mlp = [vmem(item) for item in (attended, after_attn, downward, after_mlp)]
    vectors = moves.output((8, width), f32, pltpu.VMEM)
    state_out = moves.output((rows, padded), f32, pltpu.VMEM)
    delta_grad = moves.output((rows, padded), LOW, pltpu.VMEM)
    grad_attn = moves.output((rows, width), f32, pltpu.VMEM)
    attn_grad, mixed_grad = [moves.output((rows, width), LOW, pltpu.VMEM) for _ in range(2)]
    grad_mlp = moves.scratch((rows, width), f32)
    up_grad = moves.scratch((shards, rows, hidden_count), LOW)
    feed = Tokens(moves, rows, width)
    saves = [
        moves.save(feed.tokens, (shards, rows, width), LOW),
        moves.save(up_grad, (shards, rows, hidden_count), LOW),
    ]

    weight_outputs, weight_tasks = [], []
    if pairs is not None:
        half_cols = hidden_count // members
        whole = moves.scratch((GRAM_COLS, hidden_count), f32)
        for made, operands in pairs:
            mine = moves.output((width, half_cols), f32)
            leaving = [moves.output((width, half_cols), LOW) for _ in range(members - 1)]
            held = moves.scratch((width, half_cols), f32)
            held_low = [moves.scratch((width, half_cols), LOW) for _ in range(members - 1)]
            loads = [[None if item is None else moves.load(item) for item in entry] for entry in operands]
            weight_outputs += [(held, mine)] + list(zip(held_low, leaving))
            weight_tasks.append((made, loads, held, held_low))

    def weight_grad(made, loads, held, held_low):
        def action(ref):
            @pl.loop(0, width // GRAM_COLS)
            def _(tile):
                at = pl.ds(pl.multiple_of(tile * GRAM_COLS, GRAM_COLS), GRAM_COLS)
                value = jnp.zeros((GRAM_COLS, hidden_count), f32)
                for entry in loads:
                    left, right = [made_here if item is None else item[0] for item, made_here in zip(entry, made)]
                    left_rows = ref(left)[:, :, at].reshape(-1, GRAM_COLS)
                    value = value + contract(left_rows, ref(right)[...].reshape(-1, hidden_count), 0, 0)
                ref(whole)[...] = value
                member = lax.rem(lax.axis_index(PATCHES), members)
                for shift in range(members):
                    there = lax.rem(member + shift, members)
                    part = ref(whole)[:, pl.ds(pl.multiple_of(there * half_cols, LANES), half_cols)]
                    if shift:
                        ref(held_low[shift - 1])[at, :] = part.astype(LOW)
                    else:
                        ref(held)[at, :] = part

        return action

    def put(ref, row, value):
        ref(vectors)[pl.ds(row, 1), :] = jnp.sum(value, 0, keepdims=True)

    def before(ref):
        qkv_grad, embedded, grad_later = later
        grad = contract(ref(qkv_grad)[...], ref(qkv_weights)[...], 1, 1)
        normed, inverse = layer_norm(ref(embedded)[...])
        put(ref, 5, grad * normed)
        put(ref, 4, grad)
        grad = grad * (1.0 + mod_row(ref, mods_later, 1))
        grad = ref(grad_later)[...] + norm_back(grad, normed, inverse)
        put(ref, 6, grad)
        grad = grad.astype(LOW)
        ref(embed_grad)[...] = grad
        ref(state_out)[...] = ref(grad_state)[...] + contract(grad, ref(io_weights)[0], 1, 1)

    def begin(ref):
        if later is None:
            ref(state_out)[...] = ref(grad_state)[...]
            ref(vectors)[...] = jnp.zeros((8, width), f32)
        grad = (mod_row(ref, mods, 7)[:, :padded] * ref(state_out)[...]).astype(LOW)
        ref(delta_grad)[...] = grad
        normed, inverse = layer_norm(ref(after_mlp)[...])
        grad = norm_back(contract(grad, ref(io_weights)[1], 1, 0), normed, inverse)
        ref(grad_mlp)[...] = grad
        put(ref, 3, grad * ref(downward)[...])
        ref(feed.tokens)[feed.me()] = (mod_row(ref, mods, 5) * grad).astype(LOW)

    def work(ref, slot):
        value = contract(ref(feed.tokens)[slot], ref(down_weights)[...], 1, 0)
        value = (value * gelu_slope(ref(slopes)[slot])).astype(LOW)
        ref(up_grad)[slot] = value
        return contract(value, ref(up_weights)[...], 1, 1)

    def finish(ref):
        grad = feed.total(ref)
        normed, inverse = layer_norm(ref(after_attn)[...])
        put(ref, 2, grad * normed)
        put(ref, 1, grad)
        grad = ref(grad_mlp)[...] + norm_back(grad * (1.0 + mod_row(ref, mods, 4)), normed, inverse)
        ref(grad_attn)[...] = grad
        put(ref, 0, grad * ref(attended)[...])
        grad = (mod_row(ref, mods, 2) * grad).astype(LOW)
        ref(attn_grad)[...] = grad
        ref(mixed_grad)[...] = contract(grad, ref(out_weights)[...], 1, 1).astype(LOW)

    moves.wait_local(io_load)
    if later is not None:
        moves.wait_local(qkv_load)
        moves.task(before)
    moves.task(begin)
    for number in (down_load, up_load, slopes_load):
        moves.wait_local(number)
    feed.run(work)
    for number in saves:
        moves.start_local(number)
    for made, loads, held, held_low in weight_tasks:
        for entry in loads:
            for item in entry:
                if item is not None:
                    moves.wait_local(item[1])
        made = [feed.tokens if item is TOKENS else up_grad if item is UP_GRAD else None for item in made]
        moves.task(weight_grad(made, loads, held, held_low))
    for held, target in weight_outputs:
        moves.start_local(moves.keep(held, None, target, None, True))
    moves.wait_local(out_load)
    feed.wait()
    moves.task(finish)
    results = moves.run()
    return results if later is not None else [None, *results]


def reduce_step(
    ids, members, group_cols, qkv_grad, embedded, grad_attn, mods, w_qkv, rows_late, rows_early, gathered, mlp, ada
):
    f32 = jnp.float32
    shards, seq_count = lax.axis_size(SHARDS), lax.axis_size(PATCHES)
    rows, width = embedded.shape
    block_rows, most_cols = width, max(group_cols)
    part, ada_cols = width // shards, ada.shape[1]
    up_mine, up_arrived, down_mine, down_leaving = mlp
    moves = Moves("reduce", ids, KERNEL_VMEM)
    vmem = moves.prefetch
    qkv_source = moves.operand(qkv_grad)
    qkv_grad, embedded, grad_attn, mods = vmem(qkv_grad), vmem(embedded), vmem(grad_attn), vmem(mods)
    rows_late, rows_early = vmem(rows_late), vmem(rows_early)

    def shard():
        return lax.axis_index(SHARDS)

    def patch():
        return lax.axis_index(PATCHES)

    def group():
        return patch() // members

    def member():
        return lax.rem(patch(), members)

    def columns(index, size):
        return pl.ds(pl.multiple_of(index * size, LANES), size)

    def await_all(numbers):
        for number in numbers:
            moves.wait_for(number)

    def to_others(axis, source, source_at, target, leave_own=False):
        count = lax.axis_size(axis)
        numbers = []
        for shift in range(1, count):

            def other(shift=shift):
                return lax.rem(lax.axis_index(axis) + shift, count)

            number = moves.move(
                (axis, shift),
                lambda other=other: {axis: other()},
                source,
                lambda other=other: source_at(other()),
                target,
                lambda: (lax.axis_index(axis),),
                later=True,
            )
            moves.start(number)
            numbers.append(number)

        def own(ref):
            ref(target)[lax.axis_index(axis)] = ref(source)[source_at(lax.axis_index(axis))]

        moves.task(own)
        return numbers

    def to_members(source, target, cols):
        numbers = []
        for shift in range(1, members):
            number = moves.move(
                (PATCHES, members, shift),
                functools.partial(member_peer, members, shift),
                source,
                lambda shift=shift: (slice(None), columns(lax.rem(member() + shift, members), cols)),
                target,
                lambda shift=shift: (shift - 1,),
                later=True,
            )
            moves.start(number)
            numbers.append(number)
        return numbers

    def to_group(source, target, which):
        numbers = []
        for shift in range(1, MATRICES):
            number = moves.move(
                (PATCHES, seq_count, shift),
                functools.partial(group_peer, members, shift),
                source,
                None,
                target,
                lambda shift=shift: (shift - 1,),
                sends=lambda shift=shift: group() == (which - shift) % MATRICES,
                takes=lambda: group() == which,
                later=True,
            )
            moves.start(number)
            numbers.append(number)
        return numbers

    def over_rows(action):
        @pl.loop(0, block_rows // GRAM_COLS)
        def _(tile):
            action(pl.ds(pl.multiple_of(tile * GRAM_COLS, GRAM_COLS), GRAM_COLS))

    def weight_grad(lefts, rights, full, low=None):
        depth, cols = moves.shape(lefts[0])[2], moves.shape(rights[0])[2]
        tile_rows = GRAM_COLS if depth % GRAM_COLS == 0 else LANES

        def action(ref):
            @pl.loop(0, depth // tile_rows)
            def _(tile):
                at = pl.ds(pl.multiple_of(tile * tile_rows, tile_rows), tile_rows)
                value = jnp.zeros((tile_rows, cols), f32)
                for left, right in zip(lefts, rights):
                    left_rows = ref(left)[:, :, at].reshape(-1, tile_rows)
                    value = value + contract(left_rows, ref(right)[...].reshape(-1, cols), 0, 0)
                if full is not None:
                    ref(full)[at, :] = value
                if low is not None:
                    ref(low)[at, :] = value.astype(LOW)

        moves.task(action)

    qkv_all = moves.scratch((shards, rows, 3 * part), LOW)
    qkv_moves = moves.along(
        SHARDS,
        qkv_source,
        qkv_all,
        [(lambda receiver: (slice(None), columns(receiver, 3 * part)), lambda sender: (sender,))],
    )
    qkv_local = len(moves.locals) - 1
    down_arriving = moves.scratch((members - 1, block_rows, group_cols[2]), LOW)
    down_moves = [
        moves.move(
            (PATCHES, members, shift),
            functools.partial(member_peer, members, shift),
            moves.operand(item),
            None,
            down_arriving,
            lambda shift=shift: (shift - 1,),
        )
        for shift, item in enumerate(down_leaving, 1)
    ]
    up_full, up_load = moves.load(up_mine)
    up_others = [moves.load(item) for item in up_arrived]
    qkv_weights, qkv_load = moves.load(w_qkv)
    loaded = {
        name: [moves.load(steps[step]) for step in range(ROLL) if step in steps] for name, steps in gathered.items()
    }
    down_full, down_load = moves.load(down_mine)
    ada_weights, ada_load = moves.load(ada)

    def ready(*names):
        for name in names:
            for _, number in loaded[name]:
                moves.wait_local(number)
        return [[item for item, _ in loaded[name]] for name in names]

    up_low, down_low = [moves.scratch((block_rows, cols), LOW) for cols in group_cols[1:3]]
    group_target, up_target = [moves.scratch((MATRICES - 1, block_rows, most_cols), LOW) for _ in range(2)]

    def round_up_grad(ref):
        def action(at):
            value = ref(up_full)[at, :]
            for item, _ in up_others:
                value = value + ref(item)[at, :].astype(f32)
            ref(up_full)[at, :] = value
            ref(up_low)[at, :] = value.astype(LOW)

        over_rows(action)

    for number in (up_load, *[number for _, number in up_others]):
        moves.wait_local(number)
    moves.task(round_up_grad)
    up_moves = to_group(up_low, up_target, 1)

    embed_low = moves.scratch((rows, width), LOW)
    table = moves.scratch((8, 6 * width), f32)

    def back(ref):
        grad = contract(ref(qkv_grad)[...], ref(qkv_weights)[...], 1, 1)
        normed, inverse = layer_norm(ref(embedded)[...])
        ref(table)[...] = jnp.zeros((8, 6 * width), f32)
        ref(table)[pl.ds(0, 1), pl.ds(0, width)] = jnp.sum(grad, 0, keepdims=True)
        ref(table)[pl.ds(0, 1), pl.ds(width, width)] = jnp.sum(grad * normed, 0, keepdims=True)
        grad = ref(grad_attn)[...] + norm_back(grad * (1.0 + mod_row(ref, mods, 1)), normed, inverse)
        ref(embed_low)[...] = grad.astype(LOW)
        bias_row = jnp.sum(grad, 0, keepdims=True) + mod_row(ref, rows_early, 6)
        for entry in range(4):
            cols = pl.ds((2 + entry) * width, width)
            ref(table)[pl.ds(0, 1), cols] = mod_row(ref, rows_early, entry)
            ref(table)[pl.ds(1, 1), cols] = mod_row(ref, rows_late, entry)
        for entry in range(2):
            ref(table)[pl.ds(1, 1), pl.ds(entry * width, width)] = mod_row(ref, rows_early, 4 + entry)
        for entry in range(shards):
            ref(table)[pl.ds(ROLL, 1), pl.ds(entry * ada_cols, part)] = bias_row[:, entry * part : (entry + 1) * part]

    moves.wait_local(qkv_load)
    moves.task(back)
    embed_all = moves.scratch((shards, rows, part), LOW)
    table_all = moves.scratch((shards, 8, ada_cols), f32)
    embed_moves = to_others(SHARDS, embed_low, lambda there: (slice(None), columns(there, part)), embed_all)
    table_moves = to_others(SHARDS, table, lambda there: (slice(None), columns(there, ada_cols)), table_all)

    out_cols, qkv_cols = group_cols[3], group_cols[0]
    out_full, out_low = moves.scratch((width, part), f32), moves.scratch((width, part), LOW)
    qkv_full, qkv_low = moves.scratch((width, 3 * part), f32), moves.scratch((width, 3 * part), LOW)
    out_arriving = moves.scratch((members - 1, block_rows, out_cols), LOW)
    qkv_arriving = moves.scratch((members - 1, block_rows, qkv_cols), LOW)
    padded = moves.shape(loaded["state"][0][0])[2]
    io_low = moves.scratch((2 * padded, part), LOW)
    io_grads = [moves.scratch((padded, part), f32) for _ in range(2)]
    weight_grad(*ready("mixed", "attn"), out_full, out_low)
    out_moves = to_members(out_low, out_arriving, out_cols)
    weight_grad(*ready("delta", "c"), io_grads[1])
    await_all(qkv_moves)
    moves.wait_local(qkv_local)
    (a_all, qkv_later) = ready("a", "qkv")
    weight_grad(a_all, [qkv_all, *qkv_later], qkv_full, qkv_low)
    qkv_member_moves = to_members(qkv_low, qkv_arriving, qkv_cols)
    await_all(embed_moves)
    (state_all, embed_later) = ready("state", "embed")
    weight_grad(state_all, [embed_all, *embed_later], io_grads[0])
    grad_pos = moves.output((rows, part), f32, pltpu.VMEM)
    io_rows = 2 * padded // seq_count

    def pos_and_io(ref):
        value = jnp.zeros((rows, part), f32)
        for item in (embed_all, *embed_later):
            for sample in range(shards):
                value = value + ref(item)[sample].astype(f32)
        ref(grad_pos)[...] = value
        for number, item in enumerate(io_grads):
            ref(io_low)[pl.ds(number * padded, padded), :] = ref(item)[...].astype(LOW)

    moves.task(pos_and_io)
    io_all = moves.scratch((seq_count, io_rows, part), LOW)
    io_moves = to_others(
        PATCHES, io_low, lambda there: (pl.ds(pl.multiple_of(there * io_rows, io_rows), io_rows),), io_all
    )

    flat, flat_all = moves.scratch((16, ada_cols), LOW), moves.scratch((seq_count, 16, ada_cols), LOW)

    def share(ref):
        pieces = [ref(table_all)[sample, pl.ds(0, ROLL), :] for sample in range(shards)]
        bias_row = sum(ref(table_all)[sample, pl.ds(ROLL, 1), :] for sample in range(shards))
        rest = jnp.zeros((16 - shards * ROLL - 1, ada_cols), f32)
        ref(flat)[...] = jnp.concatenate([*pieces, bias_row, rest], 0).astype(LOW)

    await_all(table_moves)
    moves.task(share)
    flat_moves = to_others(PATCHES, flat, lambda there: (slice(None), slice(None)), flat_all)

    def add_member(full, arriving, target, low, cols):
        def action(ref):
            def add(at):
                value = ref(full)[at, columns(member(), cols)] if target is not full else ref(full)[at, :]
                for shift in range(members - 1):
                    value = value + ref(arriving)[shift, at, :].astype(f32)
                ref(target)[at, :] = value
                if low is not None:
                    ref(low)[at, :] = value.astype(LOW)

            over_rows(add)

        moves.task(action)

    moves.wait_local(down_load)
    await_all(down_moves)
    add_member(down_full, down_arriving, down_full, down_low, group_cols[2])

    hops = [(0, 1, down_low, 0), (1, 2, down_low, 1), (3, 2, down_low, 2)]
    down_chunk = block_rows // DOWN_CHUNKS
    down_hops = []
    for sender, receiver, source, place in hops:
        numbers = []
        for piece in range(DOWN_CHUNKS if place < 2 else 1):
            at = pl.ds(piece * down_chunk, down_chunk) if place < 2 else slice(None)
            shift = (receiver - sender) % MATRICES
            numbers.append(
                moves.move(
                    (PATCHES, seq_count, shift),
                    functools.partial(group_peer, members, shift),
                    source,
                    lambda at=at: (at,),
                    group_target,
                    lambda at=at, place=place: (place, at),
                    sends=lambda sender=sender: group() == sender,
                    takes=lambda receiver=receiver: group() == receiver,
                    later=True,
                )
            )
        down_hops.append(numbers)
    for number in (*down_hops[0], *down_hops[2]):
        moves.start(number)
    out_mine, out_mine_low = moves.scratch((width, out_cols), f32), moves.scratch((width, out_cols), LOW)
    out_target = moves.scratch((MATRICES - 1, block_rows, out_cols), LOW)
    await_all(out_moves)
    add_member(out_full, out_arriving, out_mine, out_mine_low, out_cols)
    out_group_moves = to_group(out_mine_low, out_target, 3)

    modul_all = moves.output((shards * ROLL, ada_cols), f32, pltpu.VMEM)
    tail_all = moves.output((shards, 16, ada_cols), f32, pltpu.VMEM)
    tail = moves.scratch((16, ada_cols), f32)

    def close(ref):
        value = jnp.zeros((16, ada_cols), f32)
        for item in range(seq_count):
            value = value + ref(flat_all)[item].astype(f32)
        modul = value[: shards * ROLL]
        ref(modul_all)[...] = modul
        high = modul.astype(LOW)
        rest = (modul - high.astype(f32)).astype(LOW)
        weights = ref(ada_weights)[...]
        ref(tail)[...] = jnp.zeros((16, ada_cols), f32)
        ref(tail)[pl.ds(0, shards * ROLL), pl.ds(0, width)] = contract(high, weights, 1, 1) + contract(
            rest, weights, 1, 1
        )
        ref(tail)[pl.ds(8, 1), :] = jnp.sum(modul, 0, keepdims=True)
        ref(tail)[pl.ds(9, 1), :] = value[shards * ROLL : shards * ROLL + 1]

    await_all(flat_moves)
    moves.wait_local(ada_load)
    moves.task(close)
    to_others(SHARDS, tail, lambda there: (slice(None), slice(None)), tail_all)

    def hand_down(piece):
        number, following = down_hops[0][piece], down_hops[1][piece]
        at = pl.ds(piece * down_chunk, down_chunk)

        def add_down(ref, at=at):
            def sum_up():
                value = ref(down_full)[at, :] + ref(group_target)[0, at, :].astype(f32)
                ref(down_low)[at, :] = value.astype(LOW)

            pl.when(group() == 1)(sum_up)

        moves.wait_for(number)
        moves.task(add_down)
        moves.start(following)

    def has_source():
        return group() < MATRICES - 1

    def is_source():
        return group() > 0

    chain = moves.scratch((width, qkv_cols), f32)
    chain_in, chain_out = [moves.scratch((width, qkv_cols), LOW) for _ in range(2)]
    await_all(qkv_member_moves)
    add_member(qkv_full, qkv_arriving, chain, None, qkv_cols)
    chunk = block_rows // CHAIN_CHUNKS
    for number_of in range(CHAIN_CHUNKS):
        place = (pl.ds(number_of * chunk, chunk),)
        number = moves.move(
            (PATCHES, seq_count, MATRICES - 1),
            functools.partial(group_peer, members, MATRICES - 1),
            chain_out,
            lambda place=place: place,
            chain_in,
            lambda place=place: place,
            sends=is_source,
            takes=has_source,
            later=True,
        )

        def add(ref, place=place):
            def with_arriving():
                ref(chain)[place] += ref(chain_in)[place].astype(f32)

            pl.when(has_source())(with_arriving)
            ref(chain_out)[place] = ref(chain)[place].astype(LOW)

        moves.wait_for(number)
        moves.task(add)
        moves.start(number)
        turns = CHAIN_CHUNKS // DOWN_CHUNKS
        if number_of % turns == turns - 1:
            hand_down(number_of // turns)

    io_slice = moves.output((io_rows, part), f32, pltpu.VMEM)

    def add_io(ref):
        value = jnp.zeros((io_rows, part), f32)
        for item in range(seq_count):
            value = value + ref(io_all)[item].astype(f32)
        ref(io_slice)[...] = value

    await_all(io_moves)
    moves.task(add_io)

    grad_group = moves.output((block_rows, most_cols), f32, pltpu.VMEM)

    def put(full, target, places, cols):
        def action(ref):
            def add(at):
                value = ref(full)[at, :]
                for place in places:
                    value = value + ref(target)[place, at, pl.ds(0, cols)].astype(f32)
                ref(grad_group)[at, pl.ds(0, cols)] = value
                if cols < most_cols:
                    ref(grad_group)[at, pl.ds(cols, most_cols - cols)] = jnp.zeros((GRAM_COLS, most_cols - cols), f32)

            over_rows(add)

        return action

    def settle(ref):
        every = range(MATRICES - 1)
        entries = ((chain, None, ()), (up_full, up_target, every), (down_full, group_target, (1, 2)), (out_mine, out_target, every))
        for which, (full, target, places) in enumerate(entries):
            pl.when(group() == which)(functools.partial(put(full, target, places, group_cols[which]), ref))

    await_all((*up_moves, *down_hops[1], *down_hops[2], *out_group_moves))
    moves.task(settle)
    return moves.run()


def update_kernel(members, sums_ref, *refs):
    row = sums_ref[pl.ds(0, 1), :]
    lane = lax.broadcasted_iota(jnp.int32, (1, LANES), 1)
    squares = jnp.sum(jnp.where(lane == 0, row, 0.0), 1, keepdims=True)
    clip = jnp.minimum(1.0, CLIP_LIMIT / (jnp.sqrt(squares) + 1e-06))
    adam_in, (rows_ref, *momenta), out = refs[:8], refs[8 : 9 + MATRICES], refs[9 + MATRICES :]
    for number, rate in enumerate((RATE_ADAM, RATE_TABLE)):
        weight, first, second, grad = [item[...] for item in adam_in[4 * number : 4 * number + 4]]
        for place, value in enumerate(adam_update(weight, first, second, clip * grad, rate)):
            out[3 * number + place][...] = value
    for which, old in enumerate(momenta):
        cols = old.shape[1] // members
        for part in range(members):
            at = (slice(None), pl.ds(part * cols, cols))
            grad = rows_ref[which * members + part, :, pl.ds(0, cols)].astype(jnp.float32)
            out[6 + which][at] = MOMENTUM * old[at] + clip * grad


def update_all(members, sums, ada, pos, grad_rows, momenta):
    rows = ada[0].shape[0]
    block = rows // UPDATE_BLOCKS

    def spec(item):
        return pl.BlockSpec((block, item.shape[1]), lambda step: (step, 0))

    arrays = [*ada, *pos]
    results = [*ada[:3], *pos[:3], *momenta]
    return pl.pallas_call(
        functools.partial(update_kernel, members),
        out_shape=[jax.ShapeDtypeStruct(item.shape, jnp.float32) for item in results],
        grid=(UPDATE_BLOCKS,),
        in_specs=[
            pl.BlockSpec(sums.shape, lambda step: (0, 0)),
            *[spec(item) for item in arrays],
            pl.BlockSpec((grad_rows.shape[0], block, grad_rows.shape[2]), lambda step: (0, step, 0)),
            *[spec(item) for item in momenta],
        ],
        out_specs=[spec(item) for item in results],
        compiler_params=pltpu.CompilerParams(vmem_limit_bytes=KERNEL_VMEM),
        name="update",
    )(sums, *arrays, grad_rows, *momenta)


def newton_schulz(source, gram, poly, once, gram_low, poly_low, once_low, block, block_next):
    size = gram.shape[0]
    eye = jnp.equal(
        lax.broadcasted_iota(jnp.int32, (GRAM_COLS, GRAM_COLS), 0),
        lax.broadcasted_iota(jnp.int32, (GRAM_COLS, GRAM_COLS), 1),
    ).astype(jnp.float32)

    tiles = size // GRAM_COLS

    def tile_at(tile):
        return pl.ds(tile * GRAM_COLS, GRAM_COLS)

    def store(full, low, tile, value, mean, excess):
        cols = tile_at(tile)
        if tile:
            above = pl.ds(0, tile * GRAM_COLS)
            full[above, cols] = value[: tile * GRAM_COLS]
            low[above, cols] = value[: tile * GRAM_COLS].astype(LOW)
            for row in range(tile):
                low[cols, tile_at(row)] = value[row * GRAM_COLS : (row + 1) * GRAM_COLS].T.astype(LOW)
        corner = value[tile * GRAM_COLS :] - excess * eye
        full[cols, cols] = corner
        low[cols, cols] = (corner - mean * eye).astype(LOW)

    def inner(tile, left, right):
        both = left * right
        return 2.0 * jnp.sum(both) - jnp.sum(both[tile * GRAM_COLS :])

    def product_cols(left, right, tile):
        return contract(left[pl.ds(0, (tile + 1) * GRAM_COLS), :], right[:, tile_at(tile)], 1, 0)

    def upper(full, tile):
        return full[pl.ds(0, (tile + 1) * GRAM_COLS), tile_at(tile)]

    def advance(gram_mean, gram_squares, last):
        poly_mean = NS_B * gram_mean + NS_C * gram_squares / size
        total = jnp.float32(0.0)
        for tile in range(tiles):
            own = upper(gram, tile)
            value = product_cols(gram_low, gram_low, tile)
            value = NS_C * value + (NS_B + 2.0 * NS_C * gram_mean) * own
            store(poly, poly_low, tile, value, poly_mean, NS_C * gram_mean * gram_mean)
            total = total + inner(tile, value, own)
        once_mean = total / size - NS_C * gram_mean * gram_mean * gram_mean

        for tile in range(block.shape[1] // GRAM_COLS):
            cols = tile_at(tile)
            value = contract(poly_low[...], block[:, cols], 1, 0)
            block_next[:, cols] = (value + (NS_A + poly_mean) * block[:, cols].astype(jnp.float32)).astype(LOW)
        block[...] = block_next[...]
        if last:
            return None

        total = jnp.float32(0.0)
        for tile in range(tiles):
            own = upper(poly, tile)
            value = product_cols(poly_low, gram_low, tile)
            value = value + poly_mean * upper(gram, tile) + gram_mean * own
            store(once, once_low, tile, value, once_mean, poly_mean * gram_mean)
            total = total + inner(tile, value, own)
        poly_once = total / size - poly_mean * gram_mean * poly_mean
        mean_next = NS_A * NS_A * gram_mean + 2.0 * NS_A * once_mean + poly_once
        excess = poly_mean * once_mean

        total = jnp.float32(0.0)
        for tile in range(tiles):
            value = product_cols(poly_low, once_low, tile)
            value = value + (2.0 * NS_A + poly_mean) * upper(once, tile) + once_mean * upper(poly, tile)
            value = value + NS_A * NS_A * upper(gram, tile)
            store(gram, gram_low, tile, value, mean_next, excess)
            total = total + inner(tile, value, value)
        return mean_next, total - excess * (2.0 * mean_next + excess) * size

    block[...] = source[...]
    mean = jnp.float32(0.0)
    for tile in range(tiles):
        mean = mean + jnp.sum(gram[tile_at(tile), tile_at(tile)] * eye)
    mean = mean / size
    squares = jnp.float32(0.0)
    for tile in range(tiles):
        cols = tile_at(tile)
        value = gram[:, cols]
        gram_low[:, cols] = value.astype(LOW)
        gram_low[cols, cols] = (gram[cols, cols] - mean * eye).astype(LOW)
        squares = squares + jnp.sum(value * value)
    state = lax.fori_loop(0, NS_ITERS - 1, lambda turn, state: advance(*state, False), (mean, squares))
    advance(*state, True)


def fast_body(
    states,
    targets,
    lengths,
    intervals,
    qkv_copy,
    qkv_master,
    qkv_moment,
    out_copy,
    out_master,
    out_moment,
    up_copy,
    up_master,
    up_moment,
    down_copy,
    down_master,
    down_moment,
    ada_copy,
    ada_master,
    ada_first,
    ada_second,
    io_proj,
    io_first,
    io_second,
    cond_table,
    cond_first,
    cond_second,
    pos_table,
    pos_first,
    pos_second,
    biases,
    bias_first,
    bias_second,
):
    ids = {}
    f32 = jnp.float32
    seq_count, shards = lax.axis_size(PATCHES), lax.axis_size(SHARDS)
    seq_index, shard = lax.axis_index(PATCHES), lax.axis_index(SHARDS)
    members = seq_count // MATRICES
    group, member = seq_index // members, lax.rem(seq_index, members)
    samples, local, values_count = states.shape
    table_rows, table_cols = cond_table.shape
    width = table_cols * shards
    ada_cols = ada_copy.shape[1]
    padded = round_up(values_count, LANES)

    value_pad = ((0, 0), (0, padded - values_count))
    state = jnp.pad(states[0].astype(f32), value_pad)
    length = lengths[0]
    id_rows = jnp.broadcast_to(intervals[:, None, None], (shards, ROLL, LANES)).reshape(-1, LANES)
    (
        extras,
        cond_vec,
        silu_low,
        embedded,
        normed_a,
        state_low,
        qkv_rows,
        io_all,
        w_out,
        w_qkv,
        pos,
    ) = begin_step(
        ids,
        members,
        state,
        id_rows,
        jnp.broadcast_to((jnp.arange(ROLL, dtype=jnp.int32)[:, None] < length).astype(f32), (ROLL, width)),
        cond_table,
        biases[None],
        pos_table.astype(LOW),
        ada_copy,
        jnp.pad(io_proj.astype(LOW), ((0, 0), (0, padded - values_count), (0, 0))),
        out_copy,
        qkv_copy,
    )
    io_all = io_all.reshape(2, padded, width)
    masters = (qkv_master, up_master, down_master, out_master)
    momenta = (qkv_moment, up_moment, down_moment, out_moment)
    group_cols = [item.shape[1] // members for item in momenta]
    most_cols = max(group_cols)

    half_rows = local // ROLL

    id_count = jnp.sum((intervals == lax.dynamic_slice_in_dim(intervals, shard, 1)).astype(f32))
    weight = 1.0 / (NI * local * seq_count * values_count * id_count)
    kept = []
    gathered = {}
    moment_halves = []

    for step in range(ROLL):
        moves = Moves(f"attend{step}", ids, KERNEL_VMEM)
        qkv_out = moves.output((3, local * seq_count, width // seq_count), LOW, pltpu.VMEM)
        mixed_out = moves.output((local, width), LOW, pltpu.VMEM)
        arrivals = moves.rows_to_heads(PATCHES, qkv_rows, 3, qkv_out)
        waiting = moves.gather_pairs(normed_a, hold=True)
        waiting += moves.gather_pairs(state_low, hold=True)
        if step:
            waiting += moves.gather_pairs(kept[-1][2], hold=True)
        add_attention(moves, qkv_out, mixed_out, arrivals, local, members, waiting)
        qkv, mixed, gathered_a, gathered_state, *gathered_mixed = moves.run()
        gathered.setdefault("a", {})[step] = gathered_a
        gathered.setdefault("state", {})[step] = gathered_state
        if step:
            gathered["mixed"] = {step - 1: gathered_mixed[0]}
        *results, moment_half = feed_forward(
            ids,
            step,
            extras[step],
            extras[step + 1] if step + 1 < ROLL else None,
            mixed,
            embedded,
            state,
            pos,
            w_out,
            up_copy,
            down_copy,
            io_all,
            w_qkv,
            momenta,
            members,
        )
        moment_halves.append(moment_half)
        attended, after_attn, downward, after_mlp, normed_c, state, tokens_b, upward, hidden, *following = results
        kept.append(
            (embedded, qkv, mixed, (attended, after_attn, downward, after_mlp, upward), normed_c, tokens_b, hidden)
        )
        if following:
            embedded, normed_a, state_low, qkv_rows = following

    lat = latitude_weights(local)
    diff = state - jnp.pad(targets[0].astype(f32), value_pad)
    loss_local = weight * jnp.sum(jnp.sum(diff * diff, -1) * lat)
    grad_state = 2.0 * weight * lat[:, None] * diff

    mlp_back = []

    later, mods_later = None, None
    vector_rows = [None] * ROLL

    for step in reversed(range(ROLL)):
        embedded, qkv, mixed, for_feed, normed_c, tokens_b, hidden = kept[step]
        pairs = None
        if step == 0:
            pairs = (
                ((None, UP_GRAD), [(tokens_b, None), *[(item[0], item[1]) for item in mlp_back]]),
                ((TOKENS, None), [(None, hidden), *[(item[2], item[3]) for item in mlp_back]]),
            )
        results = feed_back(
            ids,
            step,
            extras[step],
            mods_later,
            later,
            grad_state,
            for_feed,
            w_out,
            up_copy,
            down_copy,
            io_all,
            w_qkv,
            members,
            pairs,
        )
        embed_grad, vectors, grad_state, delta_grad, grad_attn, attn_grad, mixed_grad, *results = results
        tokens_down, up_grad, *weight_grads = results
        vector_rows[step] = vectors
        mlp_back.append((tokens_b, up_grad, tokens_down, hidden))
        if step == 0:
            up_mine, *up_leaving = weight_grads[:members]
            down_mine, *down_leaving = weight_grads[members:]
            up_arrived = []
            for shift, item in enumerate(up_leaving, 1):
                routes = [
                    (index, index // members * members + (index + shift) % members) for index in range(seq_count)
                ]
                up_arrived.append(lax.ppermute(item, PATCHES, routes))
        moves = Moves(f"attend_back{step}", ids, KERNEL_VMEM)
        grads_in = moves.scratch((1, local * seq_count, width // seq_count), LOW)
        result = moves.output((local, 3 * width), LOW, pltpu.VMEM)
        arrivals = moves.rows_to_heads(PATCHES, mixed_grad, 1, grads_in)
        names = ["attn", "c", "delta"]
        moves.exchange_columns(SHARDS, attn_grad)
        moves.exchange_columns(SHARDS, normed_c)
        waiting = moves.gather_pairs(delta_grad, hold=True)
        if step == ROLL - 1:
            waiting += moves.gather_pairs(mixed, hold=True)
            names.append("mixed")
        else:
            moves.exchange_columns(SHARDS, later[0])
            moves.exchange_columns(SHARDS, embed_grad)
            names += ["qkv", "embed"]
        add_attention_back(
            moves, moves.prefetch(qkv), grads_in, result, arrivals, local, members, waiting
        )
        qkv_grad, *others = moves.run()
        for name, item in zip(names, others):
            gathered.setdefault(name, {})[step + (name in ("qkv", "embed"))] = item
        later, mods_later = (qkv_grad, embedded, grad_attn), extras[step]

    block_rows = qkv_copy.shape[0]
    grad_pos, modul_all, tail_all, io_slice, grad_group = reduce_step(
        ids,
        members,
        group_cols,
        qkv_grad,
        embedded,
        grad_attn,
        extras[0],
        w_qkv,
        vector_rows[1],
        vector_rows[0],
        gathered,
        (up_mine, up_arrived, down_mine, down_leaving),
        ada_copy,
    )
    io_cols = io_slice.shape[1]
    moves = Moves("finish", ids, KERNEL_VMEM)
    vmem = moves.prefetch
    vmem_out = functools.partial(moves.output, space=pltpu.VMEM)
    full, low = (block_rows, block_rows), (block_rows, most_cols)
    block_part = block_rows // seq_count
    grad_in, io_in, pos_in, modul_in, tail_in = [
        vmem(item) for item in (grad_group, io_slice, grad_pos, modul_all, tail_all)
    ]
    silu_in, cond_in, ids_in = vmem(silu_low), vmem(cond_vec), vmem(id_rows)
    loss_in = vmem(jnp.broadcast_to(loss_local, (1, LANES)))
    moment = moves.scratch((seq_count, block_part, most_cols), LOW)
    moment_loads = [
        moves.keep(
            moves.operand(item),
            None,
            moment,
            lambda half=half: (slice(None), pl.ds(half * half_rows, half_rows)),
        )
        for half, item in enumerate(moment_halves)
    ]
    master_loads = [moves.load(item) for item in masters]
    sums = vmem_out((8, LANES), f32)
    grad_ada = vmem_out((block_part, ada_cols), f32)
    grad_table_all = vmem_out((8, width), f32)
    io_all_parts = vmem_out((seq_count,) + io_slice.shape, LOW)
    fresh = [vmem_out(item.shape, f32) for item in masters]
    fresh_low = [moves.scratch(item.shape, LOW) for item in masters]
    near, far = [moves.scratch((count, 8, LANES), f32) for count in (shards, seq_count)]
    grad_low, source = moves.scratch(low, LOW), moves.scratch(low, LOW)
    io_low = moves.scratch(io_slice.shape, LOW)

    def measure(ref):
        def add(item, totals):
            rows = pl.ds(pl.multiple_of(item * block_part, block_part), block_part)
            old, grad = ref(moment)[item].astype(f32), ref(grad_in)[rows, :]
            ref(grad_low)[rows, :] = grad.astype(LOW)
            return totals[0] + jnp.sum(old * old), totals[1] + jnp.sum(old * grad), totals[2] + jnp.sum(grad * grad)

        zero = jnp.float32(0.0)
        terms = lax.fori_loop(0, seq_count, add, (zero, zero, zero))
        patch = lax.axis_index(PATCHES)
        count = shards * ROLL
        silu_rows = ref(silu_in)[:, pl.ds(pl.multiple_of(patch * block_part, LANES), block_part)]
        silu_rows = jnp.concatenate([silu_rows, jnp.zeros((16 - count, block_part), LOW)], 0)
        modul = jnp.concatenate([ref(modul_in)[...], jnp.zeros((16 - count, ada_cols), f32)], 0)
        modul_high = modul.astype(LOW)
        modul_rest = (modul - modul_high.astype(f32)).astype(LOW)
        value = contract(silu_rows, modul_high, 0, 0) + contract(silu_rows, modul_rest, 0, 0)
        ref(grad_ada)[...] = value
        squares = terms[2] + jnp.sum(value * value)
        squares = squares + jnp.sum(ref(io_in)[...] * ref(io_in)[...]) + jnp.sum(ref(pos_in)[...] * ref(pos_in)[...])
        ref(io_low)[...] = ref(io_in)[...].astype(LOW)
        cond = ref(cond_in)[...]
        gate = 1.0 / (1.0 + jnp.exp(-cond))
        grad_silu = sum(ref(tail_in)[item, pl.ds(0, count), pl.ds(0, width)] for item in range(shards))
        grad_cond = grad_silu * gate * (1.0 + cond * (1.0 - gate))
        row = lax.broadcasted_iota(jnp.int32, (count, 1), 0)
        ref(grad_table_all)[...] = jnp.zeros((8, width), f32)
        for entry in range(table_rows):
            chosen = (ref(ids_in)[:, :1] == entry) if entry < NI else (lax.rem(row, ROLL) == entry - NI)
            value = jnp.sum(jnp.where(chosen, grad_cond, 0.0), 0, keepdims=True)
            ref(grad_table_all)[pl.ds(entry, 1), :] = value
        me = lax.axis_index(SHARDS)
        value = ref(grad_table_all)[:, pl.ds(pl.multiple_of(me * table_cols, LANES), table_cols)]
        once = jnp.sum(value * value)
        for entry, cols in ((8, ada_cols), (9, table_cols)):
            value = ref(tail_in)[me, pl.ds(entry, 1), pl.ds(0, cols)]
            once = once + jnp.sum(value * value)
        squares = squares + jnp.where(patch == 0, once, 0.0)
        lane = lax.broadcasted_iota(jnp.int32, (8, LANES), 1)
        entries = jnp.where(lane == 0, squares, 0.0) + jnp.where(lane == 1, ref(loss_in)[...], 0.0)
        for number, term in enumerate(terms):
            entries = entries + jnp.where(lane == 2 + 3 * (patch // members) + number, term, 0.0)
        ref(near)[me] = entries

    for number in moment_loads:
        moves.wait_local(number)
    moves.task(measure)

    def spread(axis, buffer, at):
        count = lax.axis_size(axis)
        numbers = []
        for shift in range(1, count):
            numbers.append(
                moves.move(
                    (axis, shift),
                    lambda shift=shift: {axis: lax.rem(lax.axis_index(axis) + shift, count)},
                    buffer,
                    at,
                    io_all_parts if buffer is io_low else buffer,
                    lambda: (lax.axis_index(axis),),
                    later=True,
                )
            )
            moves.start(numbers[-1])
        return numbers

    def add_near(ref):
        ref(far)[lax.axis_index(PATCHES)] = jnp.sum(ref(near)[...], 0)

    def scale(ref):
        ref(sums)[...] = jnp.sum(ref(far)[...], 0)
        row = ref(sums)[pl.ds(0, 1), :]
        lane = lax.broadcasted_iota(jnp.int32, (1, LANES), 1)

        def entry(place):
            return jnp.sum(jnp.where(lane == place, row, 0.0), 1, keepdims=True)

        clip = jnp.minimum(1.0, CLIP_LIMIT / (jnp.sqrt(entry(0)) + 1e-06))
        place = 2 + 3 * (lax.axis_index(PATCHES) // members)
        size = MOMENTUM * MOMENTUM * entry(place) + 2.0 * MOMENTUM * clip * entry(place + 1)
        size = jnp.sqrt(jnp.maximum(size + clip * clip * entry(place + 2), 0.0))
        per_size = 1.0 / (size + 1e-07)

        @pl.loop(0, seq_count)
        def _(item):
            rows = pl.ds(pl.multiple_of(item * block_part, block_part), block_part)
            value = MOMENTUM * ref(moment)[item].astype(f32) + clip * ref(grad_in)[rows, :]
            ref(source)[rows, :] = (value * per_size).astype(LOW)

        ref(io_all_parts)[lax.axis_index(PATCHES)] = ref(io_low)[...]

    for number in spread(SHARDS, near, lambda: (lax.axis_index(SHARDS),)):
        moves.wait_for(number)
    moves.task(add_near)
    far_moves = spread(PATCHES, far, lambda: (lax.axis_index(PATCHES),))
    spread(PATCHES, io_low, None)
    for number in far_moves:
        moves.wait_for(number)
    moves.task(scale)

    update = moves.scratch((seq_count, block_part, most_cols), LOW)
    target = moves.scratch((members * shards,) + low, LOW)
    gram, poly, once = [moves.scratch(full, f32) for _ in range(3)]
    gram_low, poly_low, once_low = [moves.scratch(full, LOW) for _ in range(3)]
    state, state_next = [moves.scratch(low, LOW) for _ in range(2)]
    pairs = shards // 2

    def slot(back_member, back_pair, part=None):
        who_member = lax.rem(lax.rem(lax.axis_index(PATCHES), members) + members - back_member, members)
        who_shard = lax.rem(lax.axis_index(SHARDS) + shards - 2 * back_pair, shards)
        index = who_member * shards + who_shard
        return (index,) if part is None else (index, pl.ds(part * block_rows // 2, block_rows // 2))

    def add_gram(place):
        def action(ref):
            (index,) = place()

            @pl.loop(0, block_rows // GRAM_COLS)
            def _(tile):
                cols = pl.ds(pl.multiple_of(tile * GRAM_COLS, GRAM_COLS), GRAM_COLS)
                ref(gram)[:, cols] += contract(ref(target)[index], ref(target)[index, cols, :], 1, 1)

        return action

    def start_gram(ref):
        @pl.loop(0, block_rows // GRAM_COLS)
        def _(tile):
            cols = pl.ds(pl.multiple_of(tile * GRAM_COLS, GRAM_COLS), GRAM_COLS)
            ref(gram)[:, cols] = contract(ref(source)[...], ref(source)[cols, :], 1, 1)

    def pair_peer(shift):
        return {SHARDS: lax.rem(lax.axis_index(SHARDS) + 2 * shift, shards)}

    def row_part(shift):
        there = lax.rem(lax.axis_index(PATCHES) + shift, seq_count)
        size = block_rows // seq_count
        return (pl.ds(pl.multiple_of(there * size, size), size),)

    slot_own = functools.partial(slot, 0, 0)
    by_member = {
        shift: moves.move(
            (PATCHES, members, shift),
            functools.partial(member_peer, members, shift),
            source,
            None,
            target,
            slot_own,
            later=True,
        )
        for shift in range(1, members)
    }
    by_pair = {
        shift: moves.move(
            (SHARDS, 2 * shift), functools.partial(pair_peer, shift), source, None, target, slot_own, later=True
        )
        for shift in range(1, pairs)
    }
    from_sibling = [(moves.move((SHARDS,), sibling_peer, source, None, target, slot_own, later=True), slot_own)]
    for number in (*by_member.values(), *by_pair.values(), from_sibling[0][0]):
        moves.start(number)
    moves.task(start_gram)

    def sibling_place(place):
        def at():
            (index,) = place()
            return (index + 1 - 2 * lax.rem(index, 2),)

        return at

    def hand_on(place, arrivals):
        if len(arrivals) == 1:
            parts = [(place, arrivals[0])]
        else:
            parts = [(functools.partial(place, part), number) for part, number in enumerate(arrivals)]
        numbers = [
            moves.move((SHARDS,), sibling_peer, target, at, target, at, (number,)) for at, number in parts
        ]
        from_sibling.append((numbers, place))
        moves.task(add_gram(place))

    across = []
    for shift_member, first in by_member.items():
        for shift_pair, second in by_pair.items():
            top = functools.partial(slot, shift_member, 0, 0)
            bottom = functools.partial(slot, 0, shift_pair, 1)
            halves = [
                moves.move(
                    (SHARDS, 2 * shift_pair),
                    functools.partial(pair_peer, shift_pair),
                    target,
                    top,
                    target,
                    top,
                    (first,),
                ),
                moves.move(
                    (PATCHES, members, shift_member),
                    functools.partial(member_peer, members, shift_member),
                    target,
                    bottom,
                    target,
                    bottom,
                    (second,),
                ),
            ]
            across.append((functools.partial(slot, shift_member, shift_pair), halves))
    for shift, number in by_member.items():
        hand_on(functools.partial(slot, shift, 0), [number])
    for shift, number in by_pair.items():
        hand_on(functools.partial(slot, 0, shift), [number])
    moves.wait_for(from_sibling[0][0])
    moves.task(add_gram(sibling_place(slot_own)))
    for place, halves in across:
        hand_on(place, halves)
    for numbers, place in from_sibling[1:]:
        for number in numbers:
            moves.wait_for(number)
        moves.task(add_gram(sibling_place(place)))

    grad_rows = moves.output((seq_count, block_rows // seq_count, most_cols), LOW)
    for shift in range(1, seq_count):
        moves.start(
            moves.move(
                (PATCHES, shift),
                lambda shift=shift: {PATCHES: lax.rem(lax.axis_index(PATCHES) + shift, seq_count)},
                grad_low,
                lambda shift=shift: row_part(shift),
                grad_rows,
                lambda: (lax.axis_index(PATCHES),),
                later=True,
            )
        )
    moves.start_local(
        moves.keep(grad_low, lambda: row_part(0), grad_rows, lambda: (lax.axis_index(PATCHES),), True)
    )
    moves.task(
        lambda ref: newton_schulz(
            *[ref(item) for item in (source, gram, poly, once, gram_low, poly_low, once_low, state, state_next)]
        )
    )

    update_moves = []
    for shift in range(1, seq_count):
        update_moves.append(
            moves.move(
                (PATCHES, shift),
                lambda shift=shift: {PATCHES: lax.rem(lax.axis_index(PATCHES) + shift, seq_count)},
                state,
                functools.partial(row_part, shift),
                update,
                lambda: (lax.axis_index(PATCHES),),
                later=True,
            )
        )
        moves.start(update_moves[-1])

    def keep_rows(ref):
        ref(update)[lax.axis_index(PATCHES)] = ref(state)[row_part(0)]

    moves.task(keep_rows)

    def renew(ref):
        for which, (master, _) in enumerate(master_loads):
            cols = group_cols[which]
            rate = RATE_MUON * 0.2 * math.sqrt(masters[which].shape[1] * shards)
            for part in range(members):
                at = (slice(None), pl.ds(part * cols, cols))
                value = ref(update)[which * members + part, :, pl.ds(0, cols)].astype(f32)
                value = ref(master)[at] * (1.0 - RATE_MUON * DECAY_MUON) - rate * value
                ref(fresh[which])[at] = value
                ref(fresh_low[which])[at] = value.astype(LOW)

    for number in update_moves:
        moves.wait_for(number)
    for _, number in master_loads:
        moves.wait_local(number)
    moves.task(renew)

    rows = block_rows // seq_count

    def row_place(back_group, back_member, start, size):
        seq_me = lax.axis_index(PATCHES)
        who = (seq_me // members - back_group) * members
        who = who + lax.rem(lax.rem(seq_me, members) + members - back_member, members)
        return (pl.ds(pl.multiple_of(who * rows + start, 16), size),)

    def has_group(offset):
        place = lax.axis_index(PATCHES) // members + offset
        return jnp.logical_and(place >= 0, place < MATRICES)

    def to_members(item_from, from_at, item_to, place, after, there):
        numbers = []
        for shift in range(1, members):
            numbers.append(
                moves.move(
                    (PATCHES, members, shift),
                    functools.partial(member_peer, members, shift),
                    item_from,
                    from_at,
                    item_to,
                    place,
                    after,
                    there,
                    there,
                    later=True,
                )
            )
            if not after:
                moves.start(numbers[-1])
        return numbers

    def along_line(distance, way, item_from, from_at, item_to, back_member, start, size, after):
        both = lambda: jnp.logical_and(has_group(way), has_group(-distance * way))
        number = moves.move(
            (PATCHES, seq_count, way),
            functools.partial(group_peer, members, (MATRICES + way) % MATRICES),
            item_from,
            from_at,
            item_to,
            functools.partial(row_place, distance * way, back_member, start, size),
            after,
            both,
            functools.partial(has_group, -(distance + 1) * way),
            later=True,
        )
        if not after:
            moves.start(number)
        return number

    items = []
    for which, item_from in enumerate(fresh_low):
        item_to = moves.output((rows * seq_count, moves.shape(item_from)[1]), LOW)
        place = functools.partial(row_place, 0, 0, 0, rows)
        moves.start_local(moves.keep(item_from, None, item_to, place, True))
        if which:
            items.append((item_from, item_to, 0, rows, False))
        else:
            items.append((item_from, item_to, rows // 2, rows // 2, True))
            items.append((item_from, item_to, 0, rows // 2, False))
    lines = []
    for item_from, item_to, start, size, members_first in items:
        from_at = lambda start=start, size=size: (pl.ds(start, size),)
        place = functools.partial(row_place, 0, 0, start, size)
        if members_first:
            crossing = to_members(item_from, from_at, item_to, place, (), None)
        for way in (1, -1):
            number = along_line(0, way, item_from, from_at, item_to, 0, start, size, ())
            lines.append([number, way, item_to, 0, start, size, members_first])
    for item_from, item_to, start, size, members_first in items:
        if not members_first:
            from_at = lambda start=start, size=size: (pl.ds(start, size),)
            to_members(item_from, from_at, item_to, functools.partial(row_place, 0, 0, start, size), (), None)
    for item_from, item_to, start, size, members_first in items:
        if members_first:
            for back_member, number in enumerate(crossing, 1):
                place = functools.partial(row_place, 0, back_member, start, size)
                for way in (1, -1):
                    following = along_line(0, way, item_to, place, item_to, back_member, start, size, (number,))
                    lines.append([following, way, item_to, back_member, start, size, True])
    for distance in range(1, MATRICES):
        for line in lines:
            number, way, item_to, back_member, start, size, members_first = line
            place = functools.partial(row_place, distance * way, back_member, start, size)
            if distance < MATRICES - 1:
                line[0] = along_line(
                    distance, way, item_to, place, item_to, back_member, start, size, (number,)
                )
            if not members_first:
                there = functools.partial(has_group, -distance * way)
                to_members(item_to, place, item_to, place, (number,), there)
    sums, grad_ada, grad_table_all, io_slices, *rest = moves.run()
    fresh, grad_rows, copies = rest[:MATRICES], rest[MATRICES], rest[MATRICES + 1 :]
    updated = update_all(
        members,
        sums,
        (ada_master, ada_first, ada_second, grad_ada),
        (pos_table, pos_first, pos_second, grad_pos),
        grad_rows,
        momenta,
    )
    ada_res, pos_res, moments = updated[:3], updated[3:6], updated[6:]
    sums = sums[0]
    grad_norm = jnp.sqrt(sums[0])
    loss_total = sums[1]
    clip = jnp.minimum(1.0, CLIP_LIMIT / (grad_norm + 1e-06))
    terms = sums[2 : 2 + 3 * MATRICES].reshape(MATRICES, 3)
    size_squares = MOMENTUM * MOMENTUM * terms[:, 0] + 2.0 * MOMENTUM * clip * terms[:, 1] + clip * clip * terms[:, 2]
    sizes = jnp.sqrt(jnp.maximum(size_squares, 0.0))
    moment_sizes = jnp.stack([sizes[which] for which in (0, 3, 1, 2)]) / CLIP_LIMIT
    grad_table = lax.dynamic_slice_in_dim(grad_table_all[:table_rows], shard * table_cols, table_cols, 1)
    grad_bias_all = jnp.concatenate([tail_all[:, 8].reshape(-1), tail_all[:, 9, :table_cols].reshape(-1)])
    grad_bias = lax.dynamic_slice_in_dim(grad_bias_all, shard * biases.shape[0], biases.shape[0])
    io_grad = io_slices.reshape(2, padded, io_cols)[:, :values_count].astype(f32)
    io_res = adam_update(io_proj, io_first, io_second, clip * io_grad, RATE_ADAM)
    cond_res = adam_update(cond_table, cond_first, cond_second, clip * grad_table, RATE_TABLE)
    bias_res = adam_update(biases, bias_first, bias_second, clip * grad_bias, RATE_ADAM)
    matrices = []
    for which in (0, 3, 1, 2):
        matrices += [fresh[which], moments[which], copies[which]]
    return (loss_total, grad_norm, moment_sizes, *matrices, *ada_res, *io_res, *cond_res, *pos_res, *bias_res)


def fits_fast(mesh):
    seq, shards = mesh.shape[PATCHES], mesh.shape[SHARDS]
    return HEADS % seq == 0 and (HEADS // seq * HEAD) % LANES == 0 and seq % MATRICES == 0 and shards % 2 == 0


def solution(mesh):
    body = fast_body if fits_fast(mesh) else general_body
    return jax.shard_map(
        body,
        mesh=mesh,
        in_specs=(
            P(SHARDS, PATCHES, None),
            P(SHARDS, PATCHES, None),
            P(SHARDS),
            P(),
            P(None, SHARDS),
            P(PATCHES, SHARDS),
            P(PATCHES, SHARDS),
            P(None, SHARDS),
            P(PATCHES, SHARDS),
            P(PATCHES, SHARDS),
            P(None, SHARDS),
            P(PATCHES, SHARDS),
            P(PATCHES, SHARDS),
            P(None, SHARDS),
            P(PATCHES, SHARDS),
            P(PATCHES, SHARDS),
            P(None, SHARDS),
            P(PATCHES, SHARDS),
            P(PATCHES, SHARDS),
            P(PATCHES, SHARDS),
            P(None, None, SHARDS),
            P(None, None, SHARDS),
            P(None, None, SHARDS),
            P(None, SHARDS),
            P(None, SHARDS),
            P(None, SHARDS),
            P(PATCHES, SHARDS),
            P(PATCHES, SHARDS),
            P(PATCHES, SHARDS),
            P(SHARDS),
            P(SHARDS),
            P(SHARDS),
        ),
        out_specs=(
            P(),
            P(),
            P(),
            P(PATCHES, SHARDS),
            P(PATCHES, SHARDS),
            P(None, SHARDS),
            P(PATCHES, SHARDS),
            P(PATCHES, SHARDS),
            P(None, SHARDS),
            P(PATCHES, SHARDS),
            P(PATCHES, SHARDS),
            P(None, SHARDS),
            P(PATCHES, SHARDS),
            P(PATCHES, SHARDS),
            P(None, SHARDS),
            P(PATCHES, SHARDS),
            P(PATCHES, SHARDS),
            P(PATCHES, SHARDS),
            P(None, None, SHARDS),
            P(None, None, SHARDS),
            P(None, None, SHARDS),
            P(None, SHARDS),
            P(None, SHARDS),
            P(None, SHARDS),
            P(PATCHES, SHARDS),
            P(PATCHES, SHARDS),
            P(PATCHES, SHARDS),
            P(SHARDS),
            P(SHARDS),
            P(SHARDS),
        ),
        check_vma=False,
    )
```

```python
import functools
import math

import jax
import jax.numpy as jnp
import numpy as np
from jax import lax
from jax.experimental import pallas as pl
from jax.experimental.pallas import tpu as pltpu
from jax.sharding import PartitionSpec as P

PATCHES = "seq"
SHARDS = "fsdp"
HEADS = 16
HEAD = 64
NI = 3
ROLL = 2
NS_ITERS = 5
STEP_NUM = 10
LON = 32


EPS_NORM = 1e-06
NS_A = 3.4445
NS_B = -4.775
NS_C = 2.0315
MOMENTUM = 0.5
RATE_MUON = 0.15
DECAY_MUON = 0.1
RATE_ADAM = 0.05
RATE_TABLE = 0.5
DECAY_ADAM = 0.1
BETA_FIRST = 0.9
BETA_SECOND = 0.95
CLIP_LIMIT = 0.01
HIGHEST_PRECISION = lax.Precision.HIGHEST


def broadcast(block, axis, owner):
    block = jnp.where(lax.axis_index(axis) == owner, block, jnp.zeros_like(block))
    return lax.psum(block, axis)


def product(left, right):
    return jnp.dot(left, right, preferred_element_type=jnp.float32)


def dot_last(left, right):
    return lax.dot_general(
        left, right, (((left.ndim - 1,), (1,)), ((), ())), preferred_element_type=jnp.float32
    )


def rows_product(left, right):
    flat_left = left.reshape(-1, left.shape[-1])
    flat_right = right.reshape(-1, right.shape[-1])
    return lax.dot_general(
        flat_left, flat_right, (((0,), (0,)), ((), ())), preferred_element_type=jnp.float32
    )


def layer_norm(values):
    centred = values - jnp.mean(values, -1, keepdims=True)
    inverse = lax.rsqrt(jnp.mean(centred * centred, -1, keepdims=True) + EPS_NORM)
    return (centred * inverse, inverse)


def norm_back(grad, normed, inverse):
    return inverse * (
        grad
        - jnp.mean(grad, -1, keepdims=True)
        - normed * jnp.mean(grad * normed, -1, keepdims=True)
    )


def heads_view(values):
    return values.reshape(values.shape[0], values.shape[1], HEADS, HEAD)


def modulation(modul, width):
    return [modul[:, None, column * width : (column + 1) * width] for column in range(6)]


def latitude_weights(local):
    all_patches = local * lax.axis_size(PATCHES)
    band_row = (jnp.arange(all_patches, dtype=jnp.int32) // LON).astype(jnp.float32)
    latitude = (band_row + 0.5) * (math.pi / (all_patches // LON)) - math.pi / 2
    cosine = jnp.cos(latitude)
    weights = cosine / jnp.mean(cosine)
    return lax.dynamic_slice_in_dim(weights, lax.axis_index(PATCHES) * local, local)


def forward_step(weights, state, active, select):
    w_qkv, w_out, w_up, w_down, w_ada, io_all, table, pos, bias = weights
    width = w_out.shape[0]
    cond_vec = jnp.dot(select, table.astype(jnp.float32), precision=HIGHEST_PRECISION)
    silu_low = jax.nn.silu(cond_vec).astype(jnp.bfloat16)
    modul = product(silu_low, w_ada) + bias[: 6 * width].astype(jnp.float32)
    shift1, scale1, gate1, shift2, scale2, gate2 = modulation(modul, width)
    state_low = state.astype(jnp.bfloat16)
    embedded = (
        product(state_low, io_all[0])
        + bias[6 * width :].astype(jnp.float32)
        + pos.astype(jnp.float32)
    )
    normed_one, inverse_one = layer_norm(embedded)
    normed_a = (normed_one * (1.0 + scale1) + shift1).astype(jnp.bfloat16)
    qkv = product(normed_a, w_qkv).astype(jnp.bfloat16)
    queries = qkv[..., :width]
    keys, values = (
        lax.all_gather(qkv[..., width : 2 * width], PATCHES, axis=1, tiled=True),
        lax.all_gather(qkv[..., 2 * width :], PATCHES, axis=1, tiled=True),
    )
    scores = jnp.einsum(
        "sphd,snhd->shpn", heads_view(queries), heads_view(keys), preferred_element_type=jnp.float32
    ) * HEAD ** (-0.5)
    top_score = jnp.max(scores, -1, keepdims=True)
    expo = jnp.exp(scores - top_score)
    total_exp = jnp.sum(expo, -1, keepdims=True)
    log_total = top_score + jnp.log(total_exp)
    probs_low = (expo / total_exp).astype(jnp.bfloat16)
    mixed = jnp.einsum(
        "shpn,snhd->sphd", probs_low, heads_view(values), preferred_element_type=jnp.float32
    )
    mixed_low = mixed.reshape(queries.shape).astype(jnp.bfloat16)
    attended = product(mixed_low, w_out)
    after_attn = embedded + gate1 * attended
    normed_two, inverse_two = layer_norm(after_attn)
    normed_b = (normed_two * (1.0 + scale2) + shift2).astype(jnp.bfloat16)
    upward = product(normed_b, w_up)
    hidden = jax.nn.gelu(upward).astype(jnp.bfloat16)
    downward = dot_last(hidden, w_down)
    after_mlp = after_attn + gate2 * downward
    normed_three, inverse_three = layer_norm(after_mlp)
    normed_c = normed_three.astype(jnp.bfloat16)
    delta = dot_last(normed_c, io_all[1])
    kept = (
        cond_vec,
        silu_low,
        modul,
        state_low,
        normed_one,
        inverse_one,
        normed_a,
        queries,
        keys,
        values,
        log_total,
        mixed_low,
        attended,
        normed_two,
        inverse_two,
        normed_b,
        upward,
        hidden,
        downward,
        normed_three,
        inverse_three,
        normed_c,
    )
    return (state + active * delta, kept)


def backward_step(weights, kept, grad_state, active, select):
    w_qkv, w_out, w_up, w_down, w_ada, io_all, table, pos, bias = weights
    (
        cond_vec,
        silu_low,
        modul,
        state_low,
        normed_one,
        inverse_one,
        normed_a,
        queries,
        keys,
        values,
        log_total,
        mixed_low,
        attended,
        normed_two,
        inverse_two,
        normed_b,
        upward,
        hidden,
        downward,
        normed_three,
        inverse_three,
        normed_c,
    ) = kept
    width = w_out.shape[0]
    shift1, scale1, gate1, shift2, scale2, gate2 = modulation(modul, width)
    delta_grad = (active * grad_state).astype(jnp.bfloat16)
    grad_head = rows_product(delta_grad, normed_c)
    grad_mlp = norm_back(product(delta_grad, io_all[1]), normed_three, inverse_three)
    grad_gate2 = jnp.sum(grad_mlp * downward, 1)
    down_grad = (gate2 * grad_mlp).astype(jnp.bfloat16)
    grad_down = rows_product(down_grad, hidden)
    grad_hidden = product(down_grad, w_down)
    up_grad = jax.vjp(jax.nn.gelu, upward)[1](grad_hidden)[0].astype(jnp.bfloat16)
    grad_up = rows_product(normed_b, up_grad)
    grad_normed_b = dot_last(up_grad, w_up)
    grad_scale2 = jnp.sum(grad_normed_b * normed_two, 1)
    grad_shift2 = jnp.sum(grad_normed_b, 1)
    grad_attn = grad_mlp + norm_back(grad_normed_b * (1.0 + scale2), normed_two, inverse_two)
    grad_gate1 = jnp.sum(grad_attn * attended, 1)
    attn_grad = (gate1 * grad_attn).astype(jnp.bfloat16)
    grad_out = rows_product(mixed_low, attn_grad)
    mixed_grad = dot_last(attn_grad, w_out).astype(jnp.bfloat16)
    q_heads = heads_view(queries)
    k_heads = heads_view(keys)
    v_heads = heads_view(values)
    g_heads = heads_view(mixed_grad)
    scores = jnp.einsum(
        "sphd,snhd->shpn", q_heads, k_heads, preferred_element_type=jnp.float32
    ) * HEAD ** (-0.5)
    probs = jnp.exp(scores - log_total)
    probs_low = probs.astype(jnp.bfloat16)
    grad_probs = jnp.einsum("sphd,snhd->shpn", g_heads, v_heads, preferred_element_type=jnp.float32)
    score_grad = (
        HEAD ** (-0.5) * probs * (grad_probs - jnp.sum(grad_probs * probs, -1, keepdims=True))
    ).astype(jnp.bfloat16)
    grad_queries = jnp.einsum(
        "shpn,snhd->sphd", score_grad, k_heads, preferred_element_type=jnp.float32
    ).reshape(queries.shape)
    key_part = jnp.einsum(
        "shpn,sphd->snhd", score_grad, q_heads, preferred_element_type=jnp.float32
    ).reshape(keys.shape)
    value_part = jnp.einsum(
        "shpn,sphd->snhd", probs_low, g_heads, preferred_element_type=jnp.float32
    ).reshape(values.shape)
    grad_keys, grad_values = (
        lax.psum_scatter(key_part, PATCHES, scatter_dimension=1, tiled=True),
        lax.psum_scatter(value_part, PATCHES, scatter_dimension=1, tiled=True),
    )
    qkv_grad = jnp.concatenate([grad_queries, grad_keys, grad_values], -1).astype(jnp.bfloat16)
    grad_qkv = rows_product(normed_a, qkv_grad)
    grad_normed_a = dot_last(qkv_grad, w_qkv)
    grad_scale1 = jnp.sum(grad_normed_a * normed_one, 1)
    grad_shift1 = jnp.sum(grad_normed_a, 1)
    grad_embedded = grad_attn + norm_back(grad_normed_a * (1.0 + scale1), normed_one, inverse_one)
    embed_grad = grad_embedded.astype(jnp.bfloat16)
    grad_embed = rows_product(state_low, embed_grad)
    grad_prev = grad_state + dot_last(embed_grad, io_all[0])
    grad_modul = jnp.concatenate(
        [grad_shift1, grad_scale1, grad_gate1, grad_shift2, grad_scale2, grad_gate2], -1
    )
    grad_ada = lax.dot_general(
        silu_low.astype(jnp.float32),
        grad_modul,
        (((0,), (0,)), ((), ())),
        precision=HIGHEST_PRECISION,
    )
    grad_silu = lax.dot_general(
        grad_modul, w_ada.astype(jnp.float32), (((1,), (1,)), ((), ())), precision=HIGHEST_PRECISION
    )
    grad_cond = jax.vjp(jax.nn.silu, cond_vec)[1](grad_silu)[0]
    grad_table = lax.dot_general(
        select, grad_cond, (((0,), (0,)), ((), ())), precision=HIGHEST_PRECISION
    )
    grad_bias = jnp.concatenate([jnp.sum(grad_modul, 0), jnp.sum(grad_embedded, (0, 1))])
    grad_pos = jnp.sum(grad_embedded, 0)
    grads = (
        grad_qkv,
        grad_out,
        grad_up,
        grad_down,
        grad_ada,
        jnp.stack([grad_embed, grad_head]),
        grad_table,
        grad_pos,
        grad_bias,
    )
    return (grad_prev, grads)


def gram_part(block_cols):
    return lax.dot_general(
        block_cols, block_cols, (((1,), (1,)), ((), ())), preferred_element_type=jnp.float32
    )


def zero_gram(block_cols):
    return jnp.zeros((block_cols.shape[0], block_cols.shape[0]), jnp.float32)


def newton_step(block_cols, gram):
    gram_low = gram.astype(jnp.bfloat16)
    poly = (NS_B * gram_low.astype(jnp.float32) + NS_C * product(gram_low, gram_low)).astype(
        jnp.bfloat16
    )
    return (NS_A * block_cols.astype(jnp.float32) + product(poly, block_cols)).astype(jnp.bfloat16)


def keep_block(block_cols, gram):
    return block_cols


def adam_update(weight, first, second, grad, rate):
    first_new = BETA_FIRST * first + (1.0 - BETA_FIRST) * grad
    second_new = BETA_SECOND * second + (1.0 - BETA_SECOND) * grad * grad
    unbiased = first_new / (1.0 - BETA_FIRST**STEP_NUM)
    spread = jnp.sqrt(second_new / (1.0 - BETA_SECOND**STEP_NUM)) + 1e-08
    return (weight * (1.0 - rate * DECAY_ADAM) - rate * unbiased / spread, first_new, second_new)


def general_body(
    states,
    targets,
    lengths,
    intervals,
    qkv_copy,
    qkv_master,
    qkv_moment,
    out_copy,
    out_master,
    out_moment,
    up_copy,
    up_master,
    up_moment,
    down_copy,
    down_master,
    down_moment,
    ada_copy,
    ada_master,
    ada_first,
    ada_second,
    io_proj,
    io_first,
    io_second,
    cond_table,
    cond_first,
    cond_second,
    pos_table,
    pos_first,
    pos_second,
    biases,
    bias_first,
    bias_second,
):
    weights = (
        lax.all_gather(qkv_copy, SHARDS, axis=1, tiled=True),
        lax.all_gather(out_copy, SHARDS, axis=1, tiled=True),
        lax.all_gather(up_copy, SHARDS, axis=1, tiled=True),
        lax.all_gather(down_copy, SHARDS, axis=1, tiled=True),
        lax.all_gather(ada_copy, SHARDS, axis=1, tiled=True),
        lax.all_gather(io_proj.astype(jnp.bfloat16), SHARDS, axis=2, tiled=True),
        lax.all_gather(cond_table.astype(jnp.bfloat16), SHARDS, axis=1, tiled=True),
        lax.all_gather(pos_table.astype(jnp.bfloat16), SHARDS, axis=1, tiled=True),
        lax.all_gather(biases.astype(jnp.bfloat16), SHARDS, axis=0, tiled=True),
    )
    samples, local, values_count = states.shape
    table_rows = cond_table.shape[0]
    my_ids = lax.dynamic_slice_in_dim(intervals, lax.axis_index(SHARDS) * samples, samples)
    counts = jnp.sum(
        (intervals[:, None] == jnp.arange(NI, dtype=jnp.int32)[None]).astype(jnp.float32), 0
    )
    id_counts = jnp.sum(
        (my_ids[:, None] == jnp.arange(NI, dtype=jnp.int32)[None]).astype(jnp.float32)
        * counts[None],
        1,
    )
    weight = 1.0 / (NI * local * lax.axis_size(PATCHES) * values_count * id_counts)
    rows_iota = jnp.arange(table_rows, dtype=jnp.int32)
    id_select = (my_ids[:, None] == rows_iota[None]).astype(jnp.float32)
    state = states.astype(jnp.float32)
    seen_states = []
    kept_all = []
    for step in range(ROLL):
        select = id_select + (rows_iota == NI + step).astype(jnp.float32)[None]
        active = (step < lengths).astype(jnp.float32)[:, None, None]
        seen_states.append(state)
        state, kept = forward_step(weights, state, active, select)
        kept_all.append(kept)
    lat = latitude_weights(local)
    diff = state - targets.astype(jnp.float32)
    err = jnp.sum(jnp.sum(diff * diff, -1) * lat[None], -1)
    loss_local = jnp.sum(weight * err)
    grad_state = 2.0 * weight[:, None, None] * lat[None, :, None] * diff
    totals = None
    for step in reversed(range(ROLL)):
        select = id_select + (rows_iota == NI + step).astype(jnp.float32)[None]
        active = (step < lengths).astype(jnp.float32)[:, None, None]
        kept = kept_all[step]
        grad_state, grads = backward_step(weights, kept, grad_state, active, select)
        totals = grads if totals is None else jax.tree.map(jnp.add, totals, grads)
    reduced = (
        lax.psum_scatter(totals[0], SHARDS, scatter_dimension=1, tiled=True),
        lax.psum_scatter(totals[1], SHARDS, scatter_dimension=1, tiled=True),
        lax.psum_scatter(totals[2], SHARDS, scatter_dimension=1, tiled=True),
        lax.psum_scatter(totals[3], SHARDS, scatter_dimension=1, tiled=True),
        lax.psum_scatter(totals[4], SHARDS, scatter_dimension=1, tiled=True),
        lax.psum_scatter(totals[5], SHARDS, scatter_dimension=2, tiled=True),
        lax.psum_scatter(totals[6], SHARDS, scatter_dimension=1, tiled=True),
        lax.psum_scatter(totals[7], SHARDS, scatter_dimension=1, tiled=True),
        lax.psum_scatter(totals[8], SHARDS, scatter_dimension=0, tiled=True),
    )
    large = (
        lax.psum_scatter(reduced[0], PATCHES, scatter_dimension=0, tiled=True),
        lax.psum_scatter(reduced[1], PATCHES, scatter_dimension=0, tiled=True),
        lax.psum_scatter(reduced[2], PATCHES, scatter_dimension=0, tiled=True),
        lax.psum_scatter(reduced[3], PATCHES, scatter_dimension=0, tiled=True),
        lax.psum_scatter(reduced[4], PATCHES, scatter_dimension=0, tiled=True),
    )
    small = lax.psum((reduced[5], reduced[6], reduced[8]), PATCHES)
    grad_pos = reduced[7]
    first_copy = (lax.axis_index(PATCHES) == 0).astype(jnp.float32)
    squares = jnp.sum(grad_pos * grad_pos)
    for item in large:
        squares = squares + jnp.sum(item * item)
    small_squares = jnp.float32(0.0)
    for item in small:
        small_squares = small_squares + jnp.sum(item * item)
    squares, loss_total = lax.psum(
        (squares + first_copy * small_squares, loss_local), (PATCHES, SHARDS)
    )
    grad_norm = jnp.sqrt(squares)
    clip = jnp.minimum(1.0, CLIP_LIMIT / (grad_norm + 1e-06))
    masters = (qkv_master, out_master, up_master, down_master)
    moments = [
        MOMENTUM * old + clip * grad
        for old, grad in zip((qkv_moment, out_moment, up_moment, down_moment), large[:4])
    ]
    norms = lax.psum(
        (
            jnp.sum(moments[0] * moments[0]),
            jnp.sum(moments[1] * moments[1]),
            jnp.sum(moments[2] * moments[2]),
            jnp.sum(moments[3] * moments[3]),
        ),
        (PATCHES, SHARDS),
    )
    sizes = [jnp.sqrt(norms[which]) for which in range(4)]
    moment_sizes = jnp.stack(sizes) / CLIP_LIMIT
    scaled = [(moments[which] / (sizes[which] + 1e-07)).astype(jnp.bfloat16) for which in range(4)]
    columns = (
        lax.all_gather(scaled[0], PATCHES, axis=0, tiled=True),
        lax.all_gather(scaled[1], PATCHES, axis=0, tiled=True),
        lax.all_gather(scaled[2], PATCHES, axis=0, tiled=True),
        lax.all_gather(scaled[3], PATCHES, axis=0, tiled=True),
    )
    seq_index = lax.axis_index(PATCHES)
    seq_count = lax.axis_size(PATCHES)
    owners = [seq_index == which % seq_count for which in range(4)]
    blocks = list(columns)
    for turn in range(NS_ITERS):
        partial_value = [
            lax.cond(owners[which], gram_part, zero_gram, blocks[which]) for which in range(4)
        ]
        grams = lax.psum(
            (partial_value[0], partial_value[1], partial_value[2], partial_value[3]), SHARDS
        )
        blocks = [
            lax.cond(owners[which], newton_step, keep_block, blocks[which], grams[which])
            for which in range(4)
        ]
    blocks = [broadcast(blocks[which], PATCHES, which % seq_count) for which in range(4)]
    row_count = qkv_master.shape[0]
    fresh = []
    for which in range(4):
        my_rows = lax.dynamic_slice_in_dim(
            blocks[which], seq_index * row_count, row_count, 0
        ).astype(jnp.float32)
        all_cols = masters[which].shape[1] * lax.axis_size(SHARDS)
        fresh.append(
            masters[which] * (1.0 - RATE_MUON * DECAY_MUON)
            - RATE_MUON * 0.2 * math.sqrt(all_cols) * my_rows
        )
    copies = (
        lax.all_gather(fresh[0].astype(jnp.bfloat16), PATCHES, axis=0, tiled=True),
        lax.all_gather(fresh[1].astype(jnp.bfloat16), PATCHES, axis=0, tiled=True),
        lax.all_gather(fresh[2].astype(jnp.bfloat16), PATCHES, axis=0, tiled=True),
        lax.all_gather(fresh[3].astype(jnp.bfloat16), PATCHES, axis=0, tiled=True),
    )
    ada_res = adam_update(ada_master, ada_first, ada_second, clip * large[4], RATE_ADAM)
    io_res = adam_update(io_proj, io_first, io_second, clip * small[0], RATE_ADAM)
    cond_res = adam_update(cond_table, cond_first, cond_second, clip * small[1], RATE_TABLE)
    pos_res = adam_update(pos_table, pos_first, pos_second, clip * grad_pos, RATE_TABLE)
    bias_res = adam_update(biases, bias_first, bias_second, clip * small[2], RATE_ADAM)
    return (
        loss_total,
        grad_norm,
        moment_sizes,
        fresh[0],
        moments[0],
        copies[0],
        fresh[1],
        moments[1],
        copies[1],
        fresh[2],
        moments[2],
        copies[2],
        fresh[3],
        moments[3],
        copies[3],
        ada_res[0],
        ada_res[1],
        ada_res[2],
        io_res[0],
        io_res[1],
        io_res[2],
        cond_res[0],
        cond_res[1],
        cond_res[2],
        pos_res[0],
        pos_res[1],
        pos_res[2],
        bias_res[0],
        bias_res[1],
        bias_res[2],
    )


LANES = 128
MATRICES = 4
LOW = jnp.bfloat16
MESH = pl.DeviceIdType.MESH


def round_up(value, unit):
    return -(-value // unit) * unit


def member_peer(members, shift):
    index = lax.axis_index(PATCHES)
    return {PATCHES: index // members * members + lax.rem(lax.rem(index, members) + shift, members)}


def group_peer(members, shift):
    return {PATCHES: lax.rem(lax.axis_index(PATCHES) + shift * members, lax.axis_size(PATCHES))}


def sibling_peer():
    index = lax.axis_index(SHARDS)
    return {SHARDS: index + 1 - 2 * lax.rem(index, 2)}


def where(condition, action):
    if condition is None:
        action()
    else:
        pl.when(condition())(action)


class Moves:
    def __init__(self, name, ids, vmem=None):
        self.name = name
        self.ids = ids
        self.vmem = vmem
        self.operands = []
        self.operand_specs = []
        self.outputs = []
        self.output_specs = []
        self.scratches = []
        self.moves = []
        self.locals = []
        self.steps = []
        self.peers = {}
        self.delivered = {}

    def operand(self, array, space=pl.ANY):
        self.operands.append(array)
        self.operand_specs.append(pl.BlockSpec(memory_space=space))
        return (0, len(self.operands) - 1)

    def output(self, shape, dtype, space=pl.ANY):
        self.outputs.append(jax.ShapeDtypeStruct(shape, dtype))
        self.output_specs.append(pl.BlockSpec(memory_space=space))
        return (1, len(self.outputs) - 1)

    def scratch(self, shape, dtype):
        self.scratches.append(pltpu.VMEM(shape, dtype))
        return (2, len(self.scratches) - 1)

    def keep(self, source, source_at, target, target_at, later=False):
        self.locals.append((source, source_at, target, target_at, later))
        return len(self.locals) - 1

    def shape(self, scratch):
        return self.scratches[scratch[1]].shape

    def load(self, array):
        target = self.scratch(array.shape, array.dtype)
        return target, self.keep(self.operand(array), None, target, None)

    def prefetch(self, array):
        target, number = self.load(array)
        self.steps.insert(0, (self.await_local, number))
        return target

    def save(self, source, shape, dtype):
        number = self.keep(source, None, self.output(shape, dtype), None, True)
        return number

    def deliver(self, shape, dtype):
        source = self.scratch(shape, dtype)
        self.delivered[source] = self.save(source, shape, dtype)
        return source

    def hand_over(self, *sources):
        for source in sources:
            self.start_local(self.delivered.pop(source))

    def start_local(self, number):
        self.steps.append((self.begin_local, number))

    def begin_local(self, number):
        self.local[number].start()

    def move(
        self, peer_key, peer, source, source_at, target, target_at, after=(), sends=None, takes=None, later=False
    ):
        number = len(self.moves)
        self.peers.setdefault(peer_key, peer)
        self.moves.append((peer_key, source, source_at, target, target_at, sends, takes, later or bool(after)))
        for earlier in after:
            self.steps.append((self.await_move, earlier))
        if after:
            self.steps.append((self.start_move, number))
        return number

    def wait_for(self, number):
        self.steps.append((self.await_move, number))

    def start(self, number):
        self.steps.append((self.start_move, number))

    def wait_local(self, number):
        self.steps.append((self.await_local, number))

    def task(self, action):
        self.steps.append((self.do_task, action))

    def await_move(self, number):
        if number not in self.arrived:
            self.arrived.add(number)
            where(self.moves[number][6], self.remote[number].wait_recv)

    def start_move(self, number):
        where(self.moves[number][5], self.remote[number].start)

    def await_local(self, number):
        if number not in self.kept:
            self.kept.add(number)
            self.local[number].wait()

    def do_task(self, action):
        action(self.ref)

    def ref(self, which):
        return self.refs[which[0]][which[1]]

    def view(self, which, index):
        ref = self.ref(which)
        return ref.at[index()] if index is not None else ref

    def kernel(self, *refs):
        sizes = (len(self.operands), len(self.outputs), len(self.scratches))
        self.refs = (refs[: sizes[0]], refs[sizes[0] : sizes[0] + sizes[1]], refs[sizes[0] + sizes[1] : sum(sizes)])
        local_sem, send_sem, recv_sem = refs[sum(sizes) :]
        self.arrived, self.kept = set(), set()
        self.local = [
            pltpu.make_async_copy(self.view(source, source_at), self.view(target, target_at), local_sem.at[number])
            for number, (source, source_at, target, target_at, _) in enumerate(self.locals)
        ]
        for copy, entry in zip(self.local, self.locals):
            if not entry[4]:
                copy.start()
        devices = {key: peer() for key, peer in self.peers.items()}
        barrier = pltpu.get_barrier_semaphore()
        for device in devices.values():
            pl.semaphore_signal(barrier, inc=1, device_id=device, device_id_type=MESH)
        pl.semaphore_wait(barrier, len(devices))
        self.remote = []
        for number, (key, source, source_at, target, target_at, _, _, later) in enumerate(self.moves):
            self.remote.append(
                pltpu.make_async_remote_copy(
                    src_ref=self.view(source, source_at),
                    dst_ref=self.view(target, target_at),
                    send_sem=send_sem.at[number],
                    recv_sem=recv_sem.at[number],
                    device_id=devices[key],
                    device_id_type=MESH,
                )
            )
            if not later:
                self.start_move(number)
        for action, number in self.steps:
            action(number)
        for number in range(len(self.locals)):
            self.await_local(number)
        for number, copy in enumerate(self.remote):
            self.await_move(number)
            where(self.moves[number][5], copy.wait_send)

    def run(self):
        self.hand_over(*list(self.delivered))
        return pl.pallas_call(
            self.kernel,
            out_shape=self.outputs,
            in_specs=self.operand_specs,
            out_specs=self.output_specs,
            scratch_shapes=[
                *self.scratches,
                pltpu.SemaphoreType.DMA((max(1, len(self.locals)),)),
                pltpu.SemaphoreType.DMA((len(self.moves),)),
                pltpu.SemaphoreType.DMA((len(self.moves),)),
            ],
            compiler_params=pltpu.CompilerParams(
                collective_id=self.ids.setdefault(self.name, len(self.ids)),
                has_side_effects=True,
                vmem_limit_bytes=self.vmem,
            ),
            name=self.name,
        )(*self.operands)

    def along(self, axis, source, target, pairs, later=False):
        numbers = []
        count = lax.axis_size(axis)

        def other(shift):
            return lax.rem(lax.axis_index(axis) + shift, count)

        for shift in range(1, count):
            for source_at, target_at in pairs:
                numbers.append(
                    self.move(
                        (axis, shift),
                        lambda shift=shift: {axis: other(shift)},
                        source,
                        None if source_at is None else (lambda at=source_at, shift=shift: at(other(shift))),
                        target,
                        lambda at=target_at: at(lax.axis_index(axis)),
                        later=later,
                    )
                )
        for source_at, target_at in pairs:
            local = self.keep(
                source,
                None if source_at is None else (lambda at=source_at: at(lax.axis_index(axis))),
                target,
                lambda at=target_at: at(lax.axis_index(axis)),
                later,
            )
            if later:
                self.start_local(local)
        if later:
            for number in numbers:
                self.start(number)
        return numbers

    def gather(self, axis, array):
        target = self.output((lax.axis_size(axis),) + array.shape, array.dtype)
        self.along(axis, self.operand(array), target, [(None, lambda sender: (sender,))])

    def gather_pairs(self, array, parts=1, hold=False):
        shards = lax.axis_size(SHARDS)
        source = self.operand(array)
        target = self.output((shards,) + array.shape, array.dtype)
        rows = array.shape[0] // parts

        def place(back_pair, part):
            return (lax.rem(lax.axis_index(SHARDS) + shards - 2 * back_pair, shards), pl.ds(part * rows, rows))

        firsts = []
        for part in range(parts):
            for pair in range(1, shards // 2):
                number = self.move(
                    (SHARDS, 2 * pair),
                    lambda pair=pair: {SHARDS: lax.rem(lax.axis_index(SHARDS) + 2 * pair, shards)},
                    source,
                    lambda part=part: (pl.ds(part * rows, rows),),
                    target,
                    functools.partial(place, 0, part),
                )
                firsts.append((functools.partial(place, pair, part), number))
        own = lambda: (lax.axis_index(SHARDS),)
        self.move((SHARDS,), sibling_peer, source, None, target, own)
        self.keep(source, None, target, own)
        waiting = [(target, at, number) for at, number in firsts]
        if hold:
            return waiting
        self.to_sibling(waiting)

    def gather_columns(self, axis, array, target):
        width = array.shape[-1]
        lead = (slice(None),) * (array.ndim - 1)
        numbers = self.along(
            axis,
            self.operand(array),
            target,
            [(None, lambda sender: lead + (pl.ds(pl.multiple_of(sender * width, LANES), width),))],
        )
        return numbers, len(self.locals) - 1

    def gather_twice(self, arrays, members, chunks):
        shards = lax.axis_size(SHARDS)
        entries = []
        for array, pieces in zip(arrays, chunks):
            source = self.operand(array)
            width = array.shape[1]
            target = self.scratch((array.shape[0], shards * width), array.dtype)
            rows = array.shape[0] // members // pieces

            def columns(back_pair, width=width):
                who = lax.rem(lax.axis_index(SHARDS) + shards - 2 * back_pair, shards)
                return pl.ds(pl.multiple_of(who * width, LANES), width)

            def piece_rows(back_member, piece, rows=rows, pieces=pieces):
                index = lax.rem(lax.rem(lax.axis_index(PATCHES), members) + members - back_member, members)
                return pl.ds(pl.multiple_of((index * pieces + piece) * rows, rows), rows)

            def place(back_member, back_pair, piece, columns=columns, piece_rows=piece_rows):
                return (piece_rows(back_member, piece), columns(back_pair))

            def mine(piece, piece_rows=piece_rows):
                return (piece_rows(0, piece),)

            def whole(columns=columns):
                return (slice(None), columns(0))

            firsts = [
                (
                    pair,
                    piece,
                    self.move(
                        (SHARDS, 2 * pair),
                        lambda pair=pair: {SHARDS: lax.rem(lax.axis_index(SHARDS) + 2 * pair, shards)},
                        source,
                        functools.partial(mine, piece),
                        target,
                        functools.partial(place, 0, 0, piece),
                    ),
                )
                for piece in range(pieces)
                for pair in range(1, shards // 2)
            ]
            near = self.move((SHARDS,), sibling_peer, source, None, target, whole)
            local = self.keep(source, None, target, whole)
            entries.append((target, place, firsts, [near, *[number for _, _, number in firsts]], local))
        last = []
        for target, place, firsts, numbers, _ in entries:
            for pair, piece, first in firsts:
                near = functools.partial(place, 0, pair, piece)
                for shift in range(1, members):
                    number = self.move(
                        (PATCHES, members, shift),
                        functools.partial(member_peer, members, shift),
                        target,
                        near,
                        target,
                        near,
                        (first,),
                    )
                    last.append((target, functools.partial(place, shift, pair, piece), number, numbers))
                numbers.append(self.move((SHARDS,), sibling_peer, target, near, target, near, (first,)))
        for target, at, number, numbers in last:
            numbers += [number, self.move((SHARDS,), sibling_peer, target, at, target, at, (number,))]
        return [(target, numbers, local) for target, _, _, numbers, local in entries]

    def to_sibling(self, waiting):
        for target, place, number in waiting:
            self.move((SHARDS,), sibling_peer, target, place, target, place, (number,))

    def exchange_columns(self, axis, array):
        width = array.shape[-1] // lax.axis_size(axis)
        target = self.output((lax.axis_size(axis), array.shape[0], width), array.dtype)
        self.along(
            axis,
            self.operand(array),
            target,
            [
                (
                    lambda receiver: (slice(None), pl.ds(pl.multiple_of(receiver * width, LANES), width)),
                    lambda sender: (sender,),
                )
            ],
        )

    def rows_to_heads(self, axis, array, planes, target):
        count, rows = lax.axis_size(axis), array.shape[0]
        columns = array.shape[1] // planes
        width = columns // count
        return self.along(
            axis,
            self.operand(array),
            target,
            [
                (
                    lambda receiver, plane=plane: (
                        slice(None),
                        pl.ds(pl.multiple_of(plane * columns + receiver * width, LANES), width),
                    ),
                    lambda sender, plane=plane: (plane, pl.ds(pl.multiple_of(sender * rows, rows), rows)),
                )
                for plane in range(planes)
            ],
        )

    def head_rows(self, source, target, planes, rows, columns, members, back_group):
        count = lax.axis_size(PATCHES)
        width = columns // count
        for shift_member in range(members):
            for plane in planes:

                def peer(shift_member=shift_member):
                    index = lax.axis_index(PATCHES)
                    there = lax.rem(index // members + back_group, MATRICES) * members
                    return there + lax.rem(lax.rem(index, members) + shift_member, members)

                def source_at(peer=peer, plane=plane):
                    return (plane, pl.ds(pl.multiple_of(peer() * rows, rows), rows))

                def target_at(plane=plane):
                    start = plane * columns + lax.axis_index(PATCHES) * width
                    return (slice(None), pl.ds(pl.multiple_of(start, LANES), width))

                if shift_member or back_group:
                    self.start(
                        self.move(
                            (PATCHES, count, back_group, shift_member),
                            lambda peer=peer: {PATCHES: peer()},
                            source,
                            source_at,
                            target,
                            target_at,
                            later=True,
                        )
                    )
                else:

                    def own(ref, source_at=source_at, target_at=target_at):
                        ref(target)[target_at()] = ref(source)[source_at()]

                    self.task(own)


def contract(left, right, left_dim, right_dim):
    return lax.dot_general(
        left, right, (((left_dim,), (right_dim,)), ((), ())), preferred_element_type=jnp.float32
    )


CHAIN_CHUNKS = 8
DOWN_CHUNKS = 4
KERNEL_VMEM = 62 * 2**20
UPDATE_BLOCKS = 4
GRAM_COLS = 256


def attend(queries, keys, values):
    scores = contract(queries, keys, 1, 1) * HEAD ** (-0.5)
    expo = jnp.exp(scores - jnp.max(scores, -1, keepdims=True))
    probs = (expo / jnp.sum(expo, -1, keepdims=True)).astype(LOW)
    return contract(probs, values, 1, 0)


def group_rows(rows, members, shift):
    size = rows * members
    there = lax.rem(lax.axis_index(PATCHES) // members + shift, MATRICES)
    return pl.ds(pl.multiple_of(there * size, size), size)


def add_attention(moves, qkv, mixed, arrivals, planes, rows, members, waiting):
    for number in arrivals:
        moves.wait_for(number)
    for number in planes:
        moves.wait_local(number)
    moves.hand_over(qkv)
    moves.to_sibling(waiting)
    count = lax.axis_size(PATCHES)
    width = HEADS // count * HEAD
    buffer = moves.scratch((1, rows * count, width), LOW)
    for shift in (*range(1, MATRICES), 0):

        def work(ref, shift=shift):
            at = group_rows(rows, members, shift)
            parts = []
            for head in range(width // HEAD):
                lanes = pl.ds(head * HEAD, HEAD)
                parts.append(attend(ref(qkv)[0, at, lanes], ref(qkv)[1, :, lanes], ref(qkv)[2, :, lanes]))
            ref(buffer)[0, at, :] = jnp.concatenate(parts, -1).astype(LOW)

        moves.task(work)
        moves.head_rows(buffer, mixed, (0,), rows, width * count, members, shift)


def add_attention_back(moves, qkv, grads, result, arrivals, rows, members, waiting):
    for number in arrivals:
        moves.wait_for(number)
    moves.wait_local(0)
    moves.to_sibling(waiting)
    count = lax.axis_size(PATCHES)
    width = HEADS // count * HEAD
    heads = width // HEAD
    buffer = moves.scratch((3, rows * count, width), LOW)
    key_total = moves.scratch((heads, rows * count, HEAD), jnp.float32)
    value_total = moves.scratch((heads, rows * count, HEAD), jnp.float32)
    for shift in (*range(1, MATRICES), 0):

        def work(ref, shift=shift):
            at = group_rows(rows, members, shift)
            parts = []
            for head in range(heads):
                lanes = pl.ds(head * HEAD, HEAD)
                queries, keys, values = ref(qkv)[0, at, lanes], ref(qkv)[1, :, lanes], ref(qkv)[2, :, lanes]
                grad = ref(grads)[0, at, lanes]
                scores = contract(keys, queries, 1, 1) * HEAD ** (-0.5)
                expo = jnp.exp(scores - jnp.max(scores, 0, keepdims=True))
                probs = expo / jnp.sum(expo, 0, keepdims=True)
                grad_probs = contract(values, grad, 1, 1)
                shared = jnp.sum(grad_probs * probs, 0, keepdims=True)
                score_grad = (HEAD ** (-0.5) * probs * (grad_probs - shared)).astype(LOW)
                parts.append(contract(score_grad, keys, 0, 0))
                key_part = contract(score_grad, queries, 1, 0)
                value_part = contract(probs.astype(LOW), grad, 1, 0)
                if shift == 1:
                    ref(key_total)[head] = key_part
                    ref(value_total)[head] = value_part
                else:
                    ref(key_total)[head] += key_part
                    ref(value_total)[head] += value_part
            ref(buffer)[0, at, :] = jnp.concatenate(parts, -1).astype(LOW)

        moves.task(work)
        moves.head_rows(buffer, result, (0,), rows, width * count, members, shift)

    def finish(ref):
        for plane, total in ((1, key_total), (2, value_total)):
            ref(buffer)[plane] = jnp.concatenate([ref(total)[head] for head in range(heads)], -1).astype(LOW)

    moves.task(finish)
    for shift in (*range(1, MATRICES), 0):
        moves.head_rows(buffer, result, (1, 2), rows, width * count, members, shift)


def mod_row(ref, table, row):
    return ref(table)[pl.ds(row, 1), :]


def project(moves, source, weights, target, count):
    def action(ref):
        width = ref(source).shape[1]

        @pl.loop(0, count // width)
        def _(part):
            cols = pl.ds(pl.multiple_of(part * width, width), width)
            ref(target)[:, cols] = contract(ref(source)[...], ref(weights)[:, cols], 1, 0).astype(LOW)

    moves.task(action)


def embed(ref, state_low, io_weights, mods, pos, embedded, normed_low):
    value = contract(ref(state_low)[...], io_weights, 1, 0) + mods(6) + ref(pos)[...].astype(jnp.float32)
    ref(embedded)[...] = value
    normed, _ = layer_norm(value)
    ref(normed_low)[...] = (normed * (1.0 + mods(1)) + mods(0)).astype(LOW)


def begin_step(ids, members, state, id_rows, active, cond_table, biases, pos, ada, io_low, w_out, w_qkv):
    f32 = jnp.float32
    shards = lax.axis_size(SHARDS)
    (rows, padded), (table_rows, _) = state.shape, cond_table.shape
    width = w_out.shape[0]
    ada_cols = ada.shape[1]
    moves = Moves("begin", ids, KERNEL_VMEM)
    table = moves.scratch((table_rows, width), f32)
    bias = moves.scratch((1, biases.shape[1] * shards), f32)
    pos_all = moves.scratch((rows, width), LOW)
    id_rows, active, state = [moves.prefetch(item) for item in (id_rows, active, state)]
    small = [moves.gather_columns(SHARDS, cond_table, table), moves.gather_columns(SHARDS, biases, bias)]
    pos_moves, pos_local = moves.gather_columns(SHARDS, pos, pos_all)
    ada_weights, ada_load = moves.load(ada)
    vmem = moves.deliver
    extras = vmem((ROLL, 8, width), f32)
    cond_vec, silu_low = vmem((shards * ROLL, width), f32), vmem((shards * ROLL, width), LOW)
    embedded, normed_low = vmem((rows, width), f32), vmem((rows, width), LOW)
    state_low, qkv_rows = vmem((rows, padded), LOW), vmem((rows, 3 * width), LOW)
    parts_leaving, parts = [moves.scratch((shards, ROLL, ada_cols), f32) for _ in range(2)]

    def modulate(ref):
        row = lax.broadcasted_iota(jnp.int32, (shards * ROLL, 1), 0)
        ids_here = ref(id_rows)[:, :1]
        value = jnp.zeros((shards * ROLL, width), f32)
        for entry in range(table_rows):
            of_entry = ref(table)[pl.ds(entry, 1), :].astype(LOW).astype(f32)
            chosen = (ids_here == entry) if entry < NI else (lax.rem(row, ROLL) == entry - NI)
            value = value + jnp.where(chosen, of_entry, 0.0)
        ref(cond_vec)[...] = value
        value = (value / (1.0 + jnp.exp(-value))).astype(LOW)
        ref(silu_low)[...] = value
        start = pl.multiple_of(lax.axis_index(SHARDS) * ada_cols, LANES)
        value = contract(value, ref(ada_weights)[...], 1, 0)
        value = value + ref(bias)[:, pl.ds(start, ada_cols)].astype(LOW).astype(f32)
        for sample in range(shards):
            ref(parts_leaving)[sample] = value[sample * ROLL : (sample + 1) * ROLL]
        ref(parts)[lax.axis_index(SHARDS)] = ref(parts_leaving)[lax.axis_index(SHARDS)]

    for numbers, local in small:
        for number in numbers:
            moves.wait_for(number)
        moves.wait_local(local)
    moves.wait_local(ada_load)
    moves.task(modulate)
    modul_moves = []
    for shift in range(1, shards):

        def other(shift=shift):
            return lax.rem(lax.axis_index(SHARDS) + shift, shards)

        number = moves.move(
            (SHARDS, shift),
            lambda other=other: {SHARDS: other()},
            parts_leaving,
            lambda other=other: (other(),),
            parts,
            lambda: (lax.axis_index(SHARDS),),
            later=True,
        )
        modul_moves.append(number)
        moves.start(number)
    weights = moves.gather_twice((io_low.reshape(-1, io_low.shape[-1]), w_out, w_qkv), members, (1, 1, 4))

    def collect(ref):
        bias_row = ref(bias)[:, pl.ds(6 * width, width)].astype(LOW).astype(f32)
        for step in range(ROLL):
            for piece in range(6 * 2):
                start = piece * width // 2
                value = ref(parts)[start // ada_cols, pl.ds(step, 1), pl.ds(start % ada_cols, width // 2)]
                ref(extras)[step, pl.ds(piece // 2, 1), pl.ds(piece % 2 * width // 2, width // 2)] = value
            ref(extras)[step, pl.ds(6, 1), :] = bias_row
            ref(extras)[step, pl.ds(7, 1), :] = ref(active)[pl.ds(step, 1), :]

    def start_step(ref):
        ref(state_low)[...] = ref(state)[...].astype(LOW)
        mods = lambda row: ref(extras)[0, pl.ds(row, 1), :]
        embed(ref, state_low, ref(weights[0][0])[pl.ds(0, padded), :], mods, pos_all, embedded, normed_low)

    for number in modul_moves:
        moves.wait_for(number)
    moves.task(collect)
    for number in (*pos_moves, *weights[0][1]):
        moves.wait_for(number)
    moves.wait_local(pos_local)
    moves.wait_local(weights[0][2])
    moves.task(start_step)
    for target, numbers, local in weights:
        for number in numbers:
            moves.wait_for(number)
        moves.wait_local(local)
        save = moves.save(target, moves.shape(target), LOW)
        moves.start_local(save)
    moves.start_local(moves.save(pos_all, (rows, width), LOW))
    moves.hand_over(extras, cond_vec, silu_low, embedded, normed_low, state_low)
    project(moves, normed_low, weights[2][0], qkv_rows, 3 * width)
    return moves.run()


class Tokens:
    def __init__(self, moves, rows, width):
        self.moves = moves
        self.shards = lax.axis_size(SHARDS)
        self.rows = rows
        self.tokens = moves.scratch((self.shards, rows, width), LOW)
        self.own_part = moves.scratch((rows, width), jnp.float32)
        self.leaving = moves.scratch((self.shards, rows, width), LOW)
        self.arriving = moves.scratch((self.shards, rows, width), LOW)

    def me(self):
        return lax.axis_index(SHARDS)

    def back(self, pair, sibling):
        index = lax.rem(self.me() + self.shards - 2 * pair, self.shards)
        return index + 1 - 2 * lax.rem(index, 2) if sibling else index

    def part(self, pair, sibling, work):
        moves = self.moves
        slot = functools.partial(self.back, pair, sibling)

        def action(ref):
            value = work(ref, slot())
            if pair or sibling:
                ref(self.leaving)[slot()] = value.astype(LOW)
            else:
                ref(self.own_part)[...] = value

        moves.task(action)
        if pair or sibling:
            number = moves.move(
                (SHARDS, pair, sibling),
                lambda: {SHARDS: slot()},
                self.leaving,
                lambda: (slot(),),
                self.arriving,
                lambda: (self.me(),),
                later=True,
            )
            moves.start(number)
            self.parts.append(number)

    def run(self, work):
        moves, halves = self.moves, 2
        self.parts = []
        size = self.rows // halves
        pairs = self.shards // 2

        def half(pair, sibling, number):
            return (self.back(pair, sibling), pl.ds(number * size, size))

        firsts = {}
        for pair in range(1, pairs):
            for number in range(halves):
                place = functools.partial(half, 0, False, number)
                firsts[pair, number] = moves.move(
                    (SHARDS, pairs - pair, False),
                    functools.partial(lambda pair: {SHARDS: self.back(pairs - pair, False)}, pair),
                    self.tokens,
                    place,
                    self.tokens,
                    place,
                    later=True,
                )
                moves.start(firsts[pair, number])
        own = functools.partial(self.back, 0, False)
        near = moves.move(
            (SHARDS, 0, True), sibling_peer, self.tokens, lambda: (own(),), self.tokens, lambda: (own(),), later=True
        )
        moves.start(near)
        self.part(0, False, work)
        moves.wait_for(near)
        self.part(0, True, work)
        for pair in range(1, pairs):
            handed = []
            for number in range(halves):
                place = functools.partial(half, pair, False, number)
                handed.append(
                    moves.move(
                        (SHARDS, 0, True),
                        sibling_peer,
                        self.tokens,
                        place,
                        self.tokens,
                        place,
                        (firsts[pair, number],),
                    )
                )
            self.part(pair, False, work)
            for number in handed:
                moves.wait_for(number)
            self.part(pair, True, work)

    def wait(self):
        for number in self.parts:
            self.moves.wait_for(number)

    def total(self, ref):
        value = ref(self.own_part)[...]
        for shift in range(1, self.shards):
            value = value + ref(self.arriving)[lax.rem(self.me() + shift, self.shards)].astype(jnp.float32)
        return value


TOKENS, UP_GRAD = 1, 2
GELU_SCALE = math.sqrt(2.0 / math.pi)
GELU_CUBE = 0.044715


def gelu_inner(values):
    return jnp.tanh(GELU_SCALE * (values + GELU_CUBE * values * values * values))


def gelu_slope(values):
    inner = gelu_inner(values)
    rise = GELU_SCALE * (1.0 + 3.0 * GELU_CUBE * values * values)
    return 0.5 * (1.0 + inner) + 0.5 * values * (1.0 - inner * inner) * rise


def feed_forward(ids, step, mods, mods_next, mixed, embedded, state, pos, w_out, w_up, w_down, io_all, w_qkv, momenta, members):
    f32 = jnp.float32
    last = mods_next is None
    rows, width = mixed.shape
    padded = state.shape[1]
    hidden_count = w_up.shape[1]
    shards = lax.axis_size(SHARDS)
    moves = Moves(f"feed{step}", ids, KERNEL_VMEM)
    vmem = moves.prefetch
    out_weights, out_load = moves.load(w_out)
    mods, mixed, embedded, state = vmem(mods), vmem(mixed), vmem(embedded), vmem(state)
    up_weights, up_load = moves.load(w_up)
    down_weights, down_load = moves.load(w_down)
    io_weights, io_load = moves.load(io_all)
    attended, after_attn, downward, after_mlp = [moves.deliver((rows, width), f32) for _ in range(4)]
    normed_c = moves.deliver((rows, width), LOW)
    state_next = moves.deliver((rows, padded), f32)
    upward = moves.scratch((shards, rows, hidden_count), f32)
    hidden = moves.scratch((shards, rows, hidden_count), LOW)
    feed = Tokens(moves, rows, width)
    saves = [
        moves.save(feed.tokens, (shards, rows, width), LOW),
        moves.save(upward, (shards, rows, hidden_count), f32),
        moves.save(hidden, (shards, rows, hidden_count), LOW),
    ]
    if not last:
        mods_next, pos = vmem(mods_next), vmem(pos)
        qkv_weights, qkv_load = moves.load(w_qkv)
        embedded_next = moves.deliver((rows, width), f32)
        normed_next = moves.deliver((rows, width), LOW)
        state_low = moves.deliver((rows, padded), LOW)
        qkv_next = moves.deliver((rows, w_qkv.shape[1]), LOW)
    half = rows // ROLL
    seq_count = lax.axis_size(PATCHES)
    most_cols = max(item.shape[1] for item in momenta) // members
    moment_loads = []
    for item in momenta:
        scratch = moves.scratch((half, item.shape[1]), f32)
        number = moves.keep(moves.operand(item), lambda: (pl.ds(step * half, half),), scratch, None)
        moment_loads.append((scratch, number))
    moment_leaving = moves.scratch((seq_count, half, most_cols), LOW)
    moment_arriving = moves.output((seq_count, half, most_cols), LOW)

    def pack(ref):
        for which, (scratch, _) in enumerate(moment_loads):
            cols = momenta[which].shape[1] // members
            for part in range(members):
                value = ref(scratch)[:, part * cols : (part + 1) * cols].astype(LOW)
                if cols < most_cols:
                    value = jnp.concatenate([value, jnp.zeros((half, most_cols - cols), LOW)], 1)
                ref(moment_leaving)[which * members + part] = value

    def begin(ref):
        value = contract(ref(mixed)[...], ref(out_weights)[...], 1, 0)
        ref(attended)[...] = value
        value = ref(embedded)[...] + mod_row(ref, mods, 2) * value
        ref(after_attn)[...] = value
        normed, _ = layer_norm(value)
        normed = normed * (1.0 + mod_row(ref, mods, 4)) + mod_row(ref, mods, 3)
        ref(feed.tokens)[feed.me()] = normed.astype(LOW)

    def work(ref, slot):
        value = contract(ref(feed.tokens)[slot], ref(up_weights)[...], 1, 0)
        ref(upward)[slot] = value
        value = (0.5 * value * (1.0 + gelu_inner(value))).astype(LOW)
        ref(hidden)[slot] = value
        return contract(value, ref(down_weights)[...], 1, 1)

    def finish(ref):
        value = feed.total(ref)
        ref(downward)[...] = value
        value = ref(after_attn)[...] + mod_row(ref, mods, 5) * value
        ref(after_mlp)[...] = value
        normed, _ = layer_norm(value)
        normed = normed.astype(LOW)
        ref(normed_c)[...] = normed
        delta = contract(normed, ref(io_weights)[1], 1, 1)
        value = ref(state)[...] + mod_row(ref, mods, 7)[:, :padded] * delta
        ref(state_next)[...] = value
        if not last:
            ref(state_low)[...] = value.astype(LOW)
            mods_there = functools.partial(mod_row, ref, mods_next)
            embed(ref, state_low, ref(io_weights)[0], mods_there, pos, embedded_next, normed_next)

    moves.wait_local(out_load)
    moves.task(begin)
    moves.hand_over(attended, after_attn)
    moves.wait_local(up_load)
    moves.wait_local(down_load)
    feed.run(work)
    for number in saves:
        moves.start_local(number)
    for _, number in moment_loads:
        moves.wait_local(number)
    moves.task(pack)
    moves.along(
        PATCHES, moment_leaving, moment_arriving, [(lambda there: (there,), lambda sender: (sender,))], later=True
    )
    moves.wait_local(io_load)
    feed.wait()
    moves.task(finish)
    moves.hand_over(downward, after_mlp, normed_c, state_next)
    if not last:
        moves.hand_over(embedded_next, normed_next, state_low)
        moves.wait_local(qkv_load)
        project(moves, normed_next, qkv_weights, qkv_next, w_qkv.shape[1])
    return moves.run()


def feed_back(ids, step, mods, mods_later, later, grad_state, kept, w_out, w_up, w_down, io_all, w_qkv, members, pairs):
    f32 = jnp.float32
    attended, after_attn, downward, after_mlp, upward = kept
    rows, width = attended.shape
    padded = grad_state.shape[1]
    hidden_count = w_up.shape[1]
    shards = lax.axis_size(SHARDS)
    moves = Moves(f"feed_back{step}", ids, KERNEL_VMEM)
    vmem = moves.prefetch
    io_weights, io_load = moves.load(io_all)
    if later is not None:
        qkv_weights, qkv_load = moves.load(w_qkv)
        later = [vmem(item) for item in later]
        mods_later = vmem(mods_later)
        embed_grad = moves.deliver((rows, width), LOW)
    down_weights, down_load = moves.load(w_down)
    up_weights, up_load = moves.load(w_up)
    slopes, slopes_load = moves.load(upward)
    out_weights, out_load = moves.load(w_out)
    mods, grad_state = vmem(mods), vmem(grad_state)
    attended, after_attn, downward, after_mlp = [vmem(item) for item in (attended, after_attn, downward, after_mlp)]
    vectors = moves.deliver((8, width), f32)
    state_out = moves.deliver((rows, padded), f32)
    delta_grad = moves.deliver((rows, padded), LOW)
    grad_attn = moves.deliver((rows, width), f32)
    attn_grad, mixed_grad = [moves.deliver((rows, width), LOW) for _ in range(2)]
    grad_mlp = moves.scratch((rows, width), f32)
    up_grad = moves.scratch((shards, rows, hidden_count), LOW)
    feed = Tokens(moves, rows, width)
    saves = [
        moves.save(feed.tokens, (shards, rows, width), LOW),
        moves.save(up_grad, (shards, rows, hidden_count), LOW),
    ]

    weight_outputs, weight_tasks = [], []
    if pairs is not None:
        half_cols = hidden_count // members
        whole = moves.scratch((GRAM_COLS, hidden_count), f32)
        for made, operands in pairs:
            mine = moves.output((width, half_cols), f32)
            leaving = [moves.output((width, half_cols), LOW) for _ in range(members - 1)]
            held = moves.scratch((width, half_cols), f32)
            held_low = [moves.scratch((width, half_cols), LOW) for _ in range(members - 1)]
            loads = [[None if item is None else moves.load(item) for item in entry] for entry in operands]
            weight_outputs += [(held, mine)] + list(zip(held_low, leaving))
            weight_tasks.append((made, loads, held, held_low))

    def weight_grad(made, loads, held, held_low):
        def action(ref):
            @pl.loop(0, width // GRAM_COLS)
            def _(tile):
                at = pl.ds(pl.multiple_of(tile * GRAM_COLS, GRAM_COLS), GRAM_COLS)
                value = jnp.zeros((GRAM_COLS, hidden_count), f32)
                for entry in loads:
                    left, right = [made_here if item is None else item[0] for item, made_here in zip(entry, made)]
                    left_rows = ref(left)[:, :, at].reshape(-1, GRAM_COLS)
                    value = value + contract(left_rows, ref(right)[...].reshape(-1, hidden_count), 0, 0)
                ref(whole)[...] = value
                member = lax.rem(lax.axis_index(PATCHES), members)
                for shift in range(members):
                    there = lax.rem(member + shift, members)
                    part = ref(whole)[:, pl.ds(pl.multiple_of(there * half_cols, LANES), half_cols)]
                    if shift:
                        ref(held_low[shift - 1])[at, :] = part.astype(LOW)
                    else:
                        ref(held)[at, :] = part

        return action

    def put(ref, row, value):
        ref(vectors)[pl.ds(row, 1), :] = jnp.sum(value, 0, keepdims=True)

    def before(ref):
        qkv_grad, embedded, grad_later = later
        grad = contract(ref(qkv_grad)[...], ref(qkv_weights)[...], 1, 1)
        normed, inverse = layer_norm(ref(embedded)[...])
        put(ref, 5, grad * normed)
        put(ref, 4, grad)
        grad = grad * (1.0 + mod_row(ref, mods_later, 1))
        grad = ref(grad_later)[...] + norm_back(grad, normed, inverse)
        put(ref, 6, grad)
        grad = grad.astype(LOW)
        ref(embed_grad)[...] = grad
        ref(state_out)[...] = ref(grad_state)[...] + contract(grad, ref(io_weights)[0], 1, 1)

    def begin(ref):
        if later is None:
            ref(state_out)[...] = ref(grad_state)[...]
            ref(vectors)[...] = jnp.zeros((8, width), f32)
        grad = (mod_row(ref, mods, 7)[:, :padded] * ref(state_out)[...]).astype(LOW)
        ref(delta_grad)[...] = grad
        normed, inverse = layer_norm(ref(after_mlp)[...])
        grad = norm_back(contract(grad, ref(io_weights)[1], 1, 0), normed, inverse)
        ref(grad_mlp)[...] = grad
        put(ref, 3, grad * ref(downward)[...])
        ref(feed.tokens)[feed.me()] = (mod_row(ref, mods, 5) * grad).astype(LOW)

    def work(ref, slot):
        value = contract(ref(feed.tokens)[slot], ref(down_weights)[...], 1, 0)
        value = (value * gelu_slope(ref(slopes)[slot])).astype(LOW)
        ref(up_grad)[slot] = value
        return contract(value, ref(up_weights)[...], 1, 1)

    def finish(ref):
        grad = feed.total(ref)
        normed, inverse = layer_norm(ref(after_attn)[...])
        put(ref, 2, grad * normed)
        put(ref, 1, grad)
        grad = ref(grad_mlp)[...] + norm_back(grad * (1.0 + mod_row(ref, mods, 4)), normed, inverse)
        ref(grad_attn)[...] = grad
        put(ref, 0, grad * ref(attended)[...])
        grad = (mod_row(ref, mods, 2) * grad).astype(LOW)
        ref(attn_grad)[...] = grad
        ref(mixed_grad)[...] = contract(grad, ref(out_weights)[...], 1, 1).astype(LOW)

    moves.wait_local(io_load)
    if later is not None:
        moves.wait_local(qkv_load)
        moves.task(before)
    moves.task(begin)
    moves.hand_over(state_out, delta_grad)
    if later is not None:
        moves.hand_over(embed_grad)
    for number in (down_load, up_load, slopes_load):
        moves.wait_local(number)
    feed.run(work)
    for number in saves:
        moves.start_local(number)
    for made, loads, held, held_low in weight_tasks:
        for entry in loads:
            for item in entry:
                if item is not None:
                    moves.wait_local(item[1])
        made = [feed.tokens if item is TOKENS else up_grad if item is UP_GRAD else None for item in made]
        moves.task(weight_grad(made, loads, held, held_low))
    for held, target in weight_outputs:
        moves.start_local(moves.keep(held, None, target, None, True))
    moves.wait_local(out_load)
    feed.wait()
    moves.task(finish)
    results = moves.run()
    return results if later is not None else [None, *results]


def reduce_step(
    ids, members, group_cols, qkv_grad, embedded, grad_attn, mods, w_qkv, rows_late, rows_early, gathered, mlp, ada
):
    f32 = jnp.float32
    shards, seq_count = lax.axis_size(SHARDS), lax.axis_size(PATCHES)
    rows, width = embedded.shape
    block_rows, most_cols = width, max(group_cols)
    part, ada_cols = width // shards, ada.shape[1]
    up_mine, up_arrived, down_mine, down_leaving = mlp
    moves = Moves("reduce", ids, KERNEL_VMEM)
    vmem = moves.prefetch
    qkv_source = moves.operand(qkv_grad)
    qkv_grad, embedded, grad_attn, mods = vmem(qkv_grad), vmem(embedded), vmem(grad_attn), vmem(mods)
    rows_late, rows_early = vmem(rows_late), vmem(rows_early)

    def shard():
        return lax.axis_index(SHARDS)

    def patch():
        return lax.axis_index(PATCHES)

    def group():
        return patch() // members

    def member():
        return lax.rem(patch(), members)

    def columns(index, size):
        return pl.ds(pl.multiple_of(index * size, LANES), size)

    def await_all(numbers):
        for number in numbers:
            moves.wait_for(number)

    def to_others(axis, source, source_at, target, leave_own=False):
        count = lax.axis_size(axis)
        numbers = []
        for shift in range(1, count):

            def other(shift=shift):
                return lax.rem(lax.axis_index(axis) + shift, count)

            number = moves.move(
                (axis, shift),
                lambda other=other: {axis: other()},
                source,
                lambda other=other: source_at(other()),
                target,
                lambda: (lax.axis_index(axis),),
                later=True,
            )
            moves.start(number)
            numbers.append(number)

        def own(ref):
            ref(target)[lax.axis_index(axis)] = ref(source)[source_at(lax.axis_index(axis))]

        moves.task(own)
        return numbers

    def to_members(source, target, cols):
        numbers = []
        for shift in range(1, members):
            number = moves.move(
                (PATCHES, members, shift),
                functools.partial(member_peer, members, shift),
                source,
                lambda shift=shift: (slice(None), columns(lax.rem(member() + shift, members), cols)),
                target,
                lambda shift=shift: (shift - 1,),
                later=True,
            )
            moves.start(number)
            numbers.append(number)
        return numbers

    def to_group(source, target, which):
        numbers = []
        for shift in range(1, MATRICES):
            number = moves.move(
                (PATCHES, seq_count, shift),
                functools.partial(group_peer, members, shift),
                source,
                None,
                target,
                lambda shift=shift: (shift - 1,),
                sends=lambda shift=shift: group() == (which - shift) % MATRICES,
                takes=lambda: group() == which,
                later=True,
            )
            moves.start(number)
            numbers.append(number)
        return numbers

    def over_rows(action):
        @pl.loop(0, block_rows // GRAM_COLS)
        def _(tile):
            action(pl.ds(pl.multiple_of(tile * GRAM_COLS, GRAM_COLS), GRAM_COLS))

    def weight_grad(lefts, rights, full, low=None):
        depth, cols = moves.shape(lefts[0])[2], moves.shape(rights[0])[2]
        tile_rows = GRAM_COLS if depth % GRAM_COLS == 0 else LANES

        def action(ref):
            @pl.loop(0, depth // tile_rows)
            def _(tile):
                at = pl.ds(pl.multiple_of(tile * tile_rows, tile_rows), tile_rows)
                value = jnp.zeros((tile_rows, cols), f32)
                for left, right in zip(lefts, rights):
                    left_rows = ref(left)[:, :, at].reshape(-1, tile_rows)
                    value = value + contract(left_rows, ref(right)[...].reshape(-1, cols), 0, 0)
                if full is not None:
                    ref(full)[at, :] = value
                if low is not None:
                    ref(low)[at, :] = value.astype(LOW)

        moves.task(action)

    qkv_all = moves.scratch((shards, rows, 3 * part), LOW)
    qkv_moves = moves.along(
        SHARDS,
        qkv_source,
        qkv_all,
        [(lambda receiver: (slice(None), columns(receiver, 3 * part)), lambda sender: (sender,))],
    )
    qkv_local = len(moves.locals) - 1
    down_arriving = moves.scratch((members - 1, block_rows, group_cols[2]), LOW)
    down_moves = [
        moves.move(
            (PATCHES, members, shift),
            functools.partial(member_peer, members, shift),
            moves.operand(item),
            None,
            down_arriving,
            lambda shift=shift: (shift - 1,),
        )
        for shift, item in enumerate(down_leaving, 1)
    ]
    up_full, up_load = moves.load(up_mine)
    up_others = [moves.load(item) for item in up_arrived]
    qkv_weights, qkv_load = moves.load(w_qkv)
    loaded = {
        name: [moves.load(steps[step]) for step in range(ROLL) if step in steps] for name, steps in gathered.items()
    }
    down_full, down_load = moves.load(down_mine)
    ada_weights, ada_load = moves.load(ada)

    def ready(*names):
        for name in names:
            for _, number in loaded[name]:
                moves.wait_local(number)
        return [[item for item, _ in loaded[name]] for name in names]

    up_low, down_low = [moves.scratch((block_rows, cols), LOW) for cols in group_cols[1:3]]
    group_target, up_target = [moves.scratch((MATRICES - 1, block_rows, most_cols), LOW) for _ in range(2)]

    def round_up_grad(ref):
        def action(at):
            value = ref(up_full)[at, :]
            for item, _ in up_others:
                value = value + ref(item)[at, :].astype(f32)
            ref(up_full)[at, :] = value
            ref(up_low)[at, :] = value.astype(LOW)

        over_rows(action)

    for number in (up_load, *[number for _, number in up_others]):
        moves.wait_local(number)
    moves.task(round_up_grad)
    up_moves = to_group(up_low, up_target, 1)

    embed_low = moves.scratch((rows, width), LOW)
    table = moves.scratch((8, 6 * width), f32)

    def back(ref):
        grad = contract(ref(qkv_grad)[...], ref(qkv_weights)[...], 1, 1)
        normed, inverse = layer_norm(ref(embedded)[...])
        ref(table)[...] = jnp.zeros((8, 6 * width), f32)
        ref(table)[pl.ds(0, 1), pl.ds(0, width)] = jnp.sum(grad, 0, keepdims=True)
        ref(table)[pl.ds(0, 1), pl.ds(width, width)] = jnp.sum(grad * normed, 0, keepdims=True)
        grad = ref(grad_attn)[...] + norm_back(grad * (1.0 + mod_row(ref, mods, 1)), normed, inverse)
        ref(embed_low)[...] = grad.astype(LOW)
        bias_row = jnp.sum(grad, 0, keepdims=True) + mod_row(ref, rows_early, 6)
        for entry in range(4):
            cols = pl.ds((2 + entry) * width, width)
            ref(table)[pl.ds(0, 1), cols] = mod_row(ref, rows_early, entry)
            ref(table)[pl.ds(1, 1), cols] = mod_row(ref, rows_late, entry)
        for entry in range(2):
            ref(table)[pl.ds(1, 1), pl.ds(entry * width, width)] = mod_row(ref, rows_early, 4 + entry)
        for entry in range(shards):
            ref(table)[pl.ds(ROLL, 1), pl.ds(entry * ada_cols, part)] = bias_row[:, entry * part : (entry + 1) * part]

    moves.wait_local(qkv_load)
    moves.task(back)
    embed_all = moves.scratch((shards, rows, part), LOW)
    table_all = moves.scratch((shards, 8, ada_cols), f32)
    embed_moves = to_others(SHARDS, embed_low, lambda there: (slice(None), columns(there, part)), embed_all)
    table_moves = to_others(SHARDS, table, lambda there: (slice(None), columns(there, ada_cols)), table_all)

    out_cols, qkv_cols = group_cols[3], group_cols[0]
    out_full, out_low = moves.scratch((width, part), f32), moves.scratch((width, part), LOW)
    qkv_full, qkv_low = moves.scratch((width, 3 * part), f32), moves.scratch((width, 3 * part), LOW)
    out_arriving = moves.scratch((members - 1, block_rows, out_cols), LOW)
    qkv_arriving = moves.scratch((members - 1, block_rows, qkv_cols), LOW)
    padded = moves.shape(loaded["state"][0][0])[2]
    io_low = moves.scratch((2 * padded, part), LOW)
    io_grads = [moves.scratch((padded, part), f32) for _ in range(2)]
    weight_grad(*ready("mixed", "attn"), out_full, out_low)
    out_moves = to_members(out_low, out_arriving, out_cols)
    weight_grad(*ready("delta", "c"), io_grads[1])
    await_all(qkv_moves)
    moves.wait_local(qkv_local)
    (a_all, qkv_later) = ready("a", "qkv")
    weight_grad(a_all, [qkv_all, *qkv_later], qkv_full, qkv_low)
    qkv_member_moves = to_members(qkv_low, qkv_arriving, qkv_cols)
    await_all(embed_moves)
    (state_all, embed_later) = ready("state", "embed")
    weight_grad(state_all, [embed_all, *embed_later], io_grads[0])
    grad_pos = moves.deliver((rows, part), f32)
    io_rows = 2 * padded // seq_count

    def pos_and_io(ref):
        value = jnp.zeros((rows, part), f32)
        for item in (embed_all, *embed_later):
            for sample in range(shards):
                value = value + ref(item)[sample].astype(f32)
        ref(grad_pos)[...] = value
        for number, item in enumerate(io_grads):
            ref(io_low)[pl.ds(number * padded, padded), :] = ref(item)[...].astype(LOW)

    moves.task(pos_and_io)
    io_all = moves.scratch((seq_count, io_rows, part), LOW)
    io_moves = to_others(
        PATCHES, io_low, lambda there: (pl.ds(pl.multiple_of(there * io_rows, io_rows), io_rows),), io_all
    )

    flat, flat_all = moves.scratch((16, ada_cols), LOW), moves.scratch((seq_count, 16, ada_cols), LOW)

    def share(ref):
        pieces = [ref(table_all)[sample, pl.ds(0, ROLL), :] for sample in range(shards)]
        bias_row = sum(ref(table_all)[sample, pl.ds(ROLL, 1), :] for sample in range(shards))
        rest = jnp.zeros((16 - shards * ROLL - 1, ada_cols), f32)
        ref(flat)[...] = jnp.concatenate([*pieces, bias_row, rest], 0).astype(LOW)

    await_all(table_moves)
    moves.task(share)
    flat_moves = to_others(PATCHES, flat, lambda there: (slice(None), slice(None)), flat_all)

    def add_member(full, arriving, target, low, cols):
        def action(ref):
            def add(at):
                value = ref(full)[at, columns(member(), cols)] if target is not full else ref(full)[at, :]
                for shift in range(members - 1):
                    value = value + ref(arriving)[shift, at, :].astype(f32)
                ref(target)[at, :] = value
                if low is not None:
                    ref(low)[at, :] = value.astype(LOW)

            over_rows(add)

        moves.task(action)

    moves.wait_local(down_load)
    await_all(down_moves)
    add_member(down_full, down_arriving, down_full, down_low, group_cols[2])

    hops = [(0, 1, down_low, 0), (1, 2, down_low, 1), (3, 2, down_low, 2)]
    down_chunk = block_rows // DOWN_CHUNKS
    down_hops = []
    for sender, receiver, source, place in hops:
        numbers = []
        for piece in range(DOWN_CHUNKS if place < 2 else 1):
            at = pl.ds(piece * down_chunk, down_chunk) if place < 2 else slice(None)
            shift = (receiver - sender) % MATRICES
            numbers.append(
                moves.move(
                    (PATCHES, seq_count, shift),
                    functools.partial(group_peer, members, shift),
                    source,
                    lambda at=at: (at,),
                    group_target,
                    lambda at=at, place=place: (place, at),
                    sends=lambda sender=sender: group() == sender,
                    takes=lambda receiver=receiver: group() == receiver,
                    later=True,
                )
            )
        down_hops.append(numbers)
    for number in (*down_hops[0], *down_hops[2]):
        moves.start(number)
    out_mine, out_mine_low = moves.scratch((width, out_cols), f32), moves.scratch((width, out_cols), LOW)
    out_target = moves.scratch((MATRICES - 1, block_rows, out_cols), LOW)
    await_all(out_moves)
    add_member(out_full, out_arriving, out_mine, out_mine_low, out_cols)
    out_group_moves = to_group(out_mine_low, out_target, 3)

    modul_all = moves.deliver((shards * ROLL, ada_cols), f32)
    tail_all = moves.output((shards, 16, ada_cols), f32, pltpu.VMEM)
    tail = moves.scratch((16, ada_cols), f32)

    def close(ref):
        value = jnp.zeros((16, ada_cols), f32)
        for item in range(seq_count):
            value = value + ref(flat_all)[item].astype(f32)
        modul = value[: shards * ROLL]
        ref(modul_all)[...] = modul
        high = modul.astype(LOW)
        rest = (modul - high.astype(f32)).astype(LOW)
        weights = ref(ada_weights)[...]
        ref(tail)[...] = jnp.zeros((16, ada_cols), f32)
        ref(tail)[pl.ds(0, shards * ROLL), pl.ds(0, width)] = contract(high, weights, 1, 1) + contract(
            rest, weights, 1, 1
        )
        ref(tail)[pl.ds(8, 1), :] = jnp.sum(modul, 0, keepdims=True)
        ref(tail)[pl.ds(9, 1), :] = value[shards * ROLL : shards * ROLL + 1]

    await_all(flat_moves)
    moves.wait_local(ada_load)
    moves.task(close)
    to_others(SHARDS, tail, lambda there: (slice(None), slice(None)), tail_all)
    moves.hand_over(grad_pos, modul_all)

    def hand_down(piece):
        number, following = down_hops[0][piece], down_hops[1][piece]
        at = pl.ds(piece * down_chunk, down_chunk)

        def add_down(ref, at=at):
            def sum_up():
                value = ref(down_full)[at, :] + ref(group_target)[0, at, :].astype(f32)
                ref(down_low)[at, :] = value.astype(LOW)

            pl.when(group() == 1)(sum_up)

        moves.wait_for(number)
        moves.task(add_down)
        moves.start(following)

    def has_source():
        return group() < MATRICES - 1

    def is_source():
        return group() > 0

    chain = moves.scratch((width, qkv_cols), f32)
    chain_in, chain_out = [moves.scratch((width, qkv_cols), LOW) for _ in range(2)]
    await_all(qkv_member_moves)
    add_member(qkv_full, qkv_arriving, chain, None, qkv_cols)
    chunk = block_rows // CHAIN_CHUNKS
    for number_of in range(CHAIN_CHUNKS):
        place = (pl.ds(number_of * chunk, chunk),)
        number = moves.move(
            (PATCHES, seq_count, MATRICES - 1),
            functools.partial(group_peer, members, MATRICES - 1),
            chain_out,
            lambda place=place: place,
            chain_in,
            lambda place=place: place,
            sends=is_source,
            takes=has_source,
            later=True,
        )

        def add(ref, place=place):
            def with_arriving():
                ref(chain)[place] += ref(chain_in)[place].astype(f32)

            pl.when(has_source())(with_arriving)
            ref(chain_out)[place] = ref(chain)[place].astype(LOW)

        moves.wait_for(number)
        moves.task(add)
        moves.start(number)
        turns = CHAIN_CHUNKS // DOWN_CHUNKS
        if number_of % turns == turns - 1:
            hand_down(number_of // turns)

    io_slice = moves.deliver((io_rows, part), f32)

    def add_io(ref):
        value = jnp.zeros((io_rows, part), f32)
        for item in range(seq_count):
            value = value + ref(io_all)[item].astype(f32)
        ref(io_slice)[...] = value

    await_all(io_moves)
    moves.task(add_io)

    grad_group = moves.deliver((block_rows, most_cols), f32)

    def put(full, target, places, cols):
        def action(ref):
            def add(at):
                value = ref(full)[at, :]
                for place in places:
                    value = value + ref(target)[place, at, pl.ds(0, cols)].astype(f32)
                ref(grad_group)[at, pl.ds(0, cols)] = value
                if cols < most_cols:
                    ref(grad_group)[at, pl.ds(cols, most_cols - cols)] = jnp.zeros((GRAM_COLS, most_cols - cols), f32)

            over_rows(add)

        return action

    def settle(ref):
        every = range(MATRICES - 1)
        entries = ((chain, None, ()), (up_full, up_target, every), (down_full, group_target, (1, 2)), (out_mine, out_target, every))
        for which, (full, target, places) in enumerate(entries):
            pl.when(group() == which)(functools.partial(put(full, target, places, group_cols[which]), ref))

    await_all((*up_moves, *down_hops[1], *down_hops[2], *out_group_moves))
    moves.task(settle)
    return moves.run()


def update_kernel(members, sums_ref, *refs):
    row = sums_ref[pl.ds(0, 1), :]
    lane = lax.broadcasted_iota(jnp.int32, (1, LANES), 1)
    squares = jnp.sum(jnp.where(lane == 0, row, 0.0), 1, keepdims=True)
    clip = jnp.minimum(1.0, CLIP_LIMIT / (jnp.sqrt(squares) + 1e-06))
    adam_in, (rows_ref, *momenta), out = refs[:8], refs[8 : 9 + MATRICES], refs[9 + MATRICES :]
    for number, rate in enumerate((RATE_ADAM, RATE_TABLE)):
        weight, first, second, grad = [item[...] for item in adam_in[4 * number : 4 * number + 4]]
        for place, value in enumerate(adam_update(weight, first, second, clip * grad, rate)):
            out[3 * number + place][...] = value
    for which, old in enumerate(momenta):
        cols = old.shape[1] // members
        for part in range(members):
            at = (slice(None), pl.ds(part * cols, cols))
            grad = rows_ref[which * members + part, :, pl.ds(0, cols)].astype(jnp.float32)
            out[6 + which][at] = MOMENTUM * old[at] + clip * grad


def update_all(members, sums, ada, pos, grad_rows, momenta):
    rows = ada[0].shape[0]
    block = rows // UPDATE_BLOCKS

    def spec(item):
        return pl.BlockSpec((block, item.shape[1]), lambda step: (step, 0))

    arrays = [*ada, *pos]
    results = [*ada[:3], *pos[:3], *momenta]
    return pl.pallas_call(
        functools.partial(update_kernel, members),
        out_shape=[jax.ShapeDtypeStruct(item.shape, jnp.float32) for item in results],
        grid=(UPDATE_BLOCKS,),
        in_specs=[
            pl.BlockSpec(sums.shape, lambda step: (0, 0)),
            *[spec(item) for item in arrays],
            pl.BlockSpec((grad_rows.shape[0], block, grad_rows.shape[2]), lambda step: (0, step, 0)),
            *[spec(item) for item in momenta],
        ],
        out_specs=[spec(item) for item in results],
        compiler_params=pltpu.CompilerParams(vmem_limit_bytes=KERNEL_VMEM),
        name="update",
    )(sums, *arrays, grad_rows, *momenta)


def newton_schulz(source, gram, poly, once, gram_low, poly_low, once_low, block, block_next):
    size = gram.shape[0]
    eye = jnp.equal(
        lax.broadcasted_iota(jnp.int32, (GRAM_COLS, GRAM_COLS), 0),
        lax.broadcasted_iota(jnp.int32, (GRAM_COLS, GRAM_COLS), 1),
    ).astype(jnp.float32)

    tiles = size // GRAM_COLS

    def tile_at(tile):
        return pl.ds(tile * GRAM_COLS, GRAM_COLS)

    def store(full, low, tile, value, mean, excess):
        cols = tile_at(tile)
        if tile:
            above = pl.ds(0, tile * GRAM_COLS)
            full[above, cols] = value[: tile * GRAM_COLS]
            low[above, cols] = value[: tile * GRAM_COLS].astype(LOW)
            for row in range(tile):
                low[cols, tile_at(row)] = value[row * GRAM_COLS : (row + 1) * GRAM_COLS].T.astype(LOW)
        corner = value[tile * GRAM_COLS :] - excess * eye
        full[cols, cols] = corner
        low[cols, cols] = (corner - mean * eye).astype(LOW)

    def inner(tile, left, right):
        both = left * right
        return 2.0 * jnp.sum(both) - jnp.sum(both[tile * GRAM_COLS :])

    def product_cols(left, right, tile):
        return contract(left[pl.ds(0, (tile + 1) * GRAM_COLS), :], right[:, tile_at(tile)], 1, 0)

    def upper(full, tile):
        return full[pl.ds(0, (tile + 1) * GRAM_COLS), tile_at(tile)]

    def advance(gram_mean, gram_squares, last):
        poly_mean = NS_B * gram_mean + NS_C * gram_squares / size
        total = jnp.float32(0.0)
        for tile in range(tiles):
            own = upper(gram, tile)
            value = product_cols(gram_low, gram_low, tile)
            value = NS_C * value + (NS_B + 2.0 * NS_C * gram_mean) * own
            store(poly, poly_low, tile, value, poly_mean, NS_C * gram_mean * gram_mean)
            total = total + inner(tile, value, own)
        once_mean = total / size - NS_C * gram_mean * gram_mean * gram_mean

        for tile in range(block.shape[1] // GRAM_COLS):
            cols = tile_at(tile)
            value = contract(poly_low[...], block[:, cols], 1, 0)
            block_next[:, cols] = (value + (NS_A + poly_mean) * block[:, cols].astype(jnp.float32)).astype(LOW)
        block[...] = block_next[...]
        if last:
            return None

        total = jnp.float32(0.0)
        for tile in range(tiles):
            own = upper(poly, tile)
            value = product_cols(poly_low, gram_low, tile)
            value = value + poly_mean * upper(gram, tile) + gram_mean * own
            store(once, once_low, tile, value, once_mean, poly_mean * gram_mean)
            total = total + inner(tile, value, own)
        poly_once = total / size - poly_mean * gram_mean * poly_mean
        mean_next = NS_A * NS_A * gram_mean + 2.0 * NS_A * once_mean + poly_once
        excess = poly_mean * once_mean

        total = jnp.float32(0.0)
        for tile in range(tiles):
            value = product_cols(poly_low, once_low, tile)
            value = value + (2.0 * NS_A + poly_mean) * upper(once, tile) + once_mean * upper(poly, tile)
            value = value + NS_A * NS_A * upper(gram, tile)
            store(gram, gram_low, tile, value, mean_next, excess)
            total = total + inner(tile, value, value)
        return mean_next, total - excess * (2.0 * mean_next + excess) * size

    block[...] = source[...]
    mean = jnp.float32(0.0)
    for tile in range(tiles):
        mean = mean + jnp.sum(gram[tile_at(tile), tile_at(tile)] * eye)
    mean = mean / size
    squares = jnp.float32(0.0)
    for tile in range(tiles):
        cols = tile_at(tile)
        value = gram[:, cols]
        gram_low[:, cols] = value.astype(LOW)
        gram_low[cols, cols] = (gram[cols, cols] - mean * eye).astype(LOW)
        squares = squares + jnp.sum(value * value)
    state = lax.fori_loop(0, NS_ITERS - 1, lambda turn, state: advance(*state, False), (mean, squares))
    advance(*state, True)


def fast_body(
    states,
    targets,
    lengths,
    intervals,
    qkv_copy,
    qkv_master,
    qkv_moment,
    out_copy,
    out_master,
    out_moment,
    up_copy,
    up_master,
    up_moment,
    down_copy,
    down_master,
    down_moment,
    ada_copy,
    ada_master,
    ada_first,
    ada_second,
    io_proj,
    io_first,
    io_second,
    cond_table,
    cond_first,
    cond_second,
    pos_table,
    pos_first,
    pos_second,
    biases,
    bias_first,
    bias_second,
):
    ids = {}
    f32 = jnp.float32
    seq_count, shards = lax.axis_size(PATCHES), lax.axis_size(SHARDS)
    seq_index, shard = lax.axis_index(PATCHES), lax.axis_index(SHARDS)
    members = seq_count // MATRICES
    group, member = seq_index // members, lax.rem(seq_index, members)
    samples, local, values_count = states.shape
    table_rows, table_cols = cond_table.shape
    width = table_cols * shards
    ada_cols = ada_copy.shape[1]
    padded = round_up(values_count, LANES)

    value_pad = ((0, 0), (0, padded - values_count))
    state = jnp.pad(states[0].astype(f32), value_pad)
    length = lengths[0]
    id_rows = jnp.broadcast_to(intervals[:, None, None], (shards, ROLL, LANES)).reshape(-1, LANES)
    (
        extras,
        cond_vec,
        silu_low,
        embedded,
        normed_a,
        state_low,
        qkv_rows,
        io_all,
        w_out,
        w_qkv,
        pos,
    ) = begin_step(
        ids,
        members,
        state,
        id_rows,
        jnp.broadcast_to((jnp.arange(ROLL, dtype=jnp.int32)[:, None] < length).astype(f32), (ROLL, width)),
        cond_table,
        biases[None],
        pos_table.astype(LOW),
        ada_copy,
        jnp.pad(io_proj.astype(LOW), ((0, 0), (0, padded - values_count), (0, 0))),
        out_copy,
        qkv_copy,
    )
    io_all = io_all.reshape(2, padded, width)
    masters = (qkv_master, up_master, down_master, out_master)
    momenta = (qkv_moment, up_moment, down_moment, out_moment)
    group_cols = [item.shape[1] // members for item in momenta]
    most_cols = max(group_cols)

    half_rows = local // ROLL

    id_count = jnp.sum((intervals == lax.dynamic_slice_in_dim(intervals, shard, 1)).astype(f32))
    weight = 1.0 / (NI * local * seq_count * values_count * id_count)
    kept = []
    gathered = {}
    moment_halves = []

    for step in range(ROLL):
        moves = Moves(f"attend{step}", ids, KERNEL_VMEM)
        qkv_out = moves.deliver((3, local * seq_count, width // seq_count), LOW)
        mixed_out = moves.output((local, width), LOW, pltpu.VMEM)
        arrivals = moves.rows_to_heads(PATCHES, qkv_rows, 3, qkv_out)
        planes = range(len(moves.locals) - 3, len(moves.locals))
        waiting = moves.gather_pairs(normed_a, hold=True)
        waiting += moves.gather_pairs(state_low, hold=True)
        if step:
            waiting += moves.gather_pairs(kept[-1][2], hold=True)
        add_attention(moves, qkv_out, mixed_out, arrivals, planes, local, members, waiting)
        qkv, mixed, gathered_a, gathered_state, *gathered_mixed = moves.run()
        gathered.setdefault("a", {})[step] = gathered_a
        gathered.setdefault("state", {})[step] = gathered_state
        if step:
            gathered["mixed"] = {step - 1: gathered_mixed[0]}
        *results, moment_half = feed_forward(
            ids,
            step,
            extras[step],
            extras[step + 1] if step + 1 < ROLL else None,
            mixed,
            embedded,
            state,
            pos,
            w_out,
            up_copy,
            down_copy,
            io_all,
            w_qkv,
            momenta,
            members,
        )
        moment_halves.append(moment_half)
        attended, after_attn, downward, after_mlp, normed_c, state, tokens_b, upward, hidden, *following = results
        kept.append(
            (embedded, qkv, mixed, (attended, after_attn, downward, after_mlp, upward), normed_c, tokens_b, hidden)
        )
        if following:
            embedded, normed_a, state_low, qkv_rows = following

    bands = (np.arange(local * seq_count) // LON + 0.5) * (math.pi / (local * seq_count // LON)) - math.pi / 2
    cosines = np.cos(bands) / np.mean(np.cos(bands))
    lat = lax.dynamic_slice_in_dim(jnp.asarray(cosines, f32), seq_index * local, local)
    diff = state - jnp.pad(targets[0].astype(f32), value_pad)
    loss_local = weight * jnp.sum(jnp.sum(diff * diff, -1) * lat)
    grad_state = 2.0 * weight * lat[:, None] * diff

    mlp_back = []

    later, mods_later = None, None
    vector_rows = [None] * ROLL

    for step in reversed(range(ROLL)):
        embedded, qkv, mixed, for_feed, normed_c, tokens_b, hidden = kept[step]
        pairs = None
        if step == 0:
            pairs = (
                ((None, UP_GRAD), [(tokens_b, None), *[(item[0], item[1]) for item in mlp_back]]),
                ((TOKENS, None), [(None, hidden), *[(item[2], item[3]) for item in mlp_back]]),
            )
        results = feed_back(
            ids,
            step,
            extras[step],
            mods_later,
            later,
            grad_state,
            for_feed,
            w_out,
            up_copy,
            down_copy,
            io_all,
            w_qkv,
            members,
            pairs,
        )
        embed_grad, vectors, grad_state, delta_grad, grad_attn, attn_grad, mixed_grad, *results = results
        tokens_down, up_grad, *weight_grads = results
        vector_rows[step] = vectors
        mlp_back.append((tokens_b, up_grad, tokens_down, hidden))
        if step == 0:
            up_mine, *up_leaving = weight_grads[:members]
            down_mine, *down_leaving = weight_grads[members:]
            up_arrived = []
            for shift, item in enumerate(up_leaving, 1):
                routes = [
                    (index, index // members * members + (index + shift) % members) for index in range(seq_count)
                ]
                up_arrived.append(lax.ppermute(item, PATCHES, routes))
        moves = Moves(f"attend_back{step}", ids, KERNEL_VMEM)
        grads_in = moves.scratch((1, local * seq_count, width // seq_count), LOW)
        result = moves.output((local, 3 * width), LOW, pltpu.VMEM)
        arrivals = moves.rows_to_heads(PATCHES, mixed_grad, 1, grads_in)
        names = ["attn", "c", "delta"]
        moves.exchange_columns(SHARDS, attn_grad)
        moves.exchange_columns(SHARDS, normed_c)
        waiting = moves.gather_pairs(delta_grad, hold=True)
        if step == ROLL - 1:
            waiting += moves.gather_pairs(mixed, hold=True)
            names.append("mixed")
        else:
            moves.exchange_columns(SHARDS, later[0])
            moves.exchange_columns(SHARDS, embed_grad)
            names += ["qkv", "embed"]
        add_attention_back(
            moves, moves.prefetch(qkv), grads_in, result, arrivals, local, members, waiting
        )
        qkv_grad, *others = moves.run()
        for name, item in zip(names, others):
            gathered.setdefault(name, {})[step + (name in ("qkv", "embed"))] = item
        later, mods_later = (qkv_grad, embedded, grad_attn), extras[step]

    block_rows = qkv_copy.shape[0]
    grad_pos, modul_all, tail_all, io_slice, grad_group = reduce_step(
        ids,
        members,
        group_cols,
        qkv_grad,
        embedded,
        grad_attn,
        extras[0],
        w_qkv,
        vector_rows[1],
        vector_rows[0],
        gathered,
        (up_mine, up_arrived, down_mine, down_leaving),
        ada_copy,
    )
    io_cols = io_slice.shape[1]
    moves = Moves("finish", ids, KERNEL_VMEM)
    vmem = moves.prefetch
    vmem_out = functools.partial(moves.output, space=pltpu.VMEM)
    full, low = (block_rows, block_rows), (block_rows, most_cols)
    block_part = block_rows // seq_count
    grad_in, io_in, pos_in, modul_in, tail_in = [
        vmem(item) for item in (grad_group, io_slice, grad_pos, modul_all, tail_all)
    ]
    silu_in, cond_in, ids_in = vmem(silu_low), vmem(cond_vec), vmem(id_rows)
    loss_in = vmem(jnp.broadcast_to(loss_local, (1, LANES)))
    moment = moves.scratch((seq_count, block_part, most_cols), LOW)
    moment_loads = [
        moves.keep(
            moves.operand(item),
            None,
            moment,
            lambda half=half: (slice(None), pl.ds(half * half_rows, half_rows)),
        )
        for half, item in enumerate(moment_halves)
    ]
    master_loads = [moves.load(item) for item in masters]
    sums = moves.deliver((8, LANES), f32)
    grad_ada = moves.deliver((block_part, ada_cols), f32)
    grad_table_all = moves.deliver((8, width), f32)
    io_all_parts = vmem_out((seq_count,) + io_slice.shape, LOW)
    fresh = [moves.deliver(item.shape, f32) for item in masters]
    fresh_low = [moves.scratch(item.shape, LOW) for item in masters]
    near, far = [moves.scratch((count, 8, LANES), f32) for count in (shards, seq_count)]
    grad_low, source = moves.scratch(low, LOW), moves.scratch(low, LOW)
    io_low = moves.scratch(io_slice.shape, LOW)

    def measure(ref):
        def add(item, totals):
            rows = pl.ds(pl.multiple_of(item * block_part, block_part), block_part)
            old, grad = ref(moment)[item].astype(f32), ref(grad_in)[rows, :]
            ref(grad_low)[rows, :] = grad.astype(LOW)
            return totals[0] + jnp.sum(old * old), totals[1] + jnp.sum(old * grad), totals[2] + jnp.sum(grad * grad)

        zero = jnp.float32(0.0)
        terms = lax.fori_loop(0, seq_count, add, (zero, zero, zero))
        patch = lax.axis_index(PATCHES)
        count = shards * ROLL
        silu_rows = ref(silu_in)[:, pl.ds(pl.multiple_of(patch * block_part, LANES), block_part)]
        silu_rows = jnp.concatenate([silu_rows, jnp.zeros((16 - count, block_part), LOW)], 0)
        modul = jnp.concatenate([ref(modul_in)[...], jnp.zeros((16 - count, ada_cols), f32)], 0)
        modul_high = modul.astype(LOW)
        modul_rest = (modul - modul_high.astype(f32)).astype(LOW)
        value = contract(silu_rows, modul_high, 0, 0) + contract(silu_rows, modul_rest, 0, 0)
        ref(grad_ada)[...] = value
        squares = terms[2] + jnp.sum(value * value)
        squares = squares + jnp.sum(ref(io_in)[...] * ref(io_in)[...]) + jnp.sum(ref(pos_in)[...] * ref(pos_in)[...])
        ref(io_low)[...] = ref(io_in)[...].astype(LOW)
        cond = ref(cond_in)[...]
        gate = 1.0 / (1.0 + jnp.exp(-cond))
        grad_silu = sum(ref(tail_in)[item, pl.ds(0, count), pl.ds(0, width)] for item in range(shards))
        grad_cond = grad_silu * gate * (1.0 + cond * (1.0 - gate))
        row = lax.broadcasted_iota(jnp.int32, (count, 1), 0)
        ref(grad_table_all)[...] = jnp.zeros((8, width), f32)
        for entry in range(table_rows):
            chosen = (ref(ids_in)[:, :1] == entry) if entry < NI else (lax.rem(row, ROLL) == entry - NI)
            value = jnp.sum(jnp.where(chosen, grad_cond, 0.0), 0, keepdims=True)
            ref(grad_table_all)[pl.ds(entry, 1), :] = value
        me = lax.axis_index(SHARDS)
        value = ref(grad_table_all)[:, pl.ds(pl.multiple_of(me * table_cols, LANES), table_cols)]
        once = jnp.sum(value * value)
        for entry, cols in ((8, ada_cols), (9, table_cols)):
            value = ref(tail_in)[me, pl.ds(entry, 1), pl.ds(0, cols)]
            once = once + jnp.sum(value * value)
        squares = squares + jnp.where(patch == 0, once, 0.0)
        lane = lax.broadcasted_iota(jnp.int32, (8, LANES), 1)
        entries = jnp.where(lane == 0, squares, 0.0) + jnp.where(lane == 1, ref(loss_in)[...], 0.0)
        for number, term in enumerate(terms):
            entries = entries + jnp.where(lane == 2 + 3 * (patch // members) + number, term, 0.0)
        ref(near)[me] = entries

    for number in moment_loads:
        moves.wait_local(number)
    moves.task(measure)

    def spread(axis, buffer, at):
        count = lax.axis_size(axis)
        numbers = []
        for shift in range(1, count):
            numbers.append(
                moves.move(
                    (axis, shift),
                    lambda shift=shift: {axis: lax.rem(lax.axis_index(axis) + shift, count)},
                    buffer,
                    at,
                    io_all_parts if buffer is io_low else buffer,
                    lambda: (lax.axis_index(axis),),
                    later=True,
                )
            )
            moves.start(numbers[-1])
        return numbers

    def add_near(ref):
        ref(far)[lax.axis_index(PATCHES)] = jnp.sum(ref(near)[...], 0)

    def scale(ref):
        ref(sums)[...] = jnp.sum(ref(far)[...], 0)
        row = ref(sums)[pl.ds(0, 1), :]
        lane = lax.broadcasted_iota(jnp.int32, (1, LANES), 1)

        def entry(place):
            return jnp.sum(jnp.where(lane == place, row, 0.0), 1, keepdims=True)

        clip = jnp.minimum(1.0, CLIP_LIMIT / (jnp.sqrt(entry(0)) + 1e-06))
        place = 2 + 3 * (lax.axis_index(PATCHES) // members)
        size = MOMENTUM * MOMENTUM * entry(place) + 2.0 * MOMENTUM * clip * entry(place + 1)
        size = jnp.sqrt(jnp.maximum(size + clip * clip * entry(place + 2), 0.0))
        per_size = 1.0 / (size + 1e-07)

        @pl.loop(0, seq_count)
        def _(item):
            rows = pl.ds(pl.multiple_of(item * block_part, block_part), block_part)
            value = MOMENTUM * ref(moment)[item].astype(f32) + clip * ref(grad_in)[rows, :]
            ref(source)[rows, :] = (value * per_size).astype(LOW)

        ref(io_all_parts)[lax.axis_index(PATCHES)] = ref(io_low)[...]

    for number in spread(SHARDS, near, lambda: (lax.axis_index(SHARDS),)):
        moves.wait_for(number)
    moves.task(add_near)
    far_moves = spread(PATCHES, far, lambda: (lax.axis_index(PATCHES),))
    spread(PATCHES, io_low, None)
    for number in far_moves:
        moves.wait_for(number)
    moves.task(scale)

    update = moves.scratch((seq_count, block_part, most_cols), LOW)
    target = moves.scratch((members * shards,) + low, LOW)
    gram, poly, once = [moves.scratch(full, f32) for _ in range(3)]
    gram_low, poly_low, once_low = [moves.scratch(full, LOW) for _ in range(3)]
    state, state_next = [moves.scratch(low, LOW) for _ in range(2)]
    pairs = shards // 2

    def slot(back_member, back_pair, part=None):
        who_member = lax.rem(lax.rem(lax.axis_index(PATCHES), members) + members - back_member, members)
        who_shard = lax.rem(lax.axis_index(SHARDS) + shards - 2 * back_pair, shards)
        index = who_member * shards + who_shard
        return (index,) if part is None else (index, pl.ds(part * block_rows // 2, block_rows // 2))

    def add_gram(place):
        def action(ref):
            (index,) = place()

            @pl.loop(0, block_rows // GRAM_COLS)
            def _(tile):
                cols = pl.ds(pl.multiple_of(tile * GRAM_COLS, GRAM_COLS), GRAM_COLS)
                ref(gram)[:, cols] += contract(ref(target)[index], ref(target)[index, cols, :], 1, 1)

        return action

    def start_gram(ref):
        @pl.loop(0, block_rows // GRAM_COLS)
        def _(tile):
            cols = pl.ds(pl.multiple_of(tile * GRAM_COLS, GRAM_COLS), GRAM_COLS)
            ref(gram)[:, cols] = contract(ref(source)[...], ref(source)[cols, :], 1, 1)

    def pair_peer(shift):
        return {SHARDS: lax.rem(lax.axis_index(SHARDS) + 2 * shift, shards)}

    def row_part(shift):
        there = lax.rem(lax.axis_index(PATCHES) + shift, seq_count)
        size = block_rows // seq_count
        return (pl.ds(pl.multiple_of(there * size, size), size),)

    slot_own = functools.partial(slot, 0, 0)
    by_member = {
        shift: moves.move(
            (PATCHES, members, shift),
            functools.partial(member_peer, members, shift),
            source,
            None,
            target,
            slot_own,
            later=True,
        )
        for shift in range(1, members)
    }
    by_pair = {
        shift: moves.move(
            (SHARDS, 2 * shift), functools.partial(pair_peer, shift), source, None, target, slot_own, later=True
        )
        for shift in range(1, pairs)
    }
    from_sibling = [(moves.move((SHARDS,), sibling_peer, source, None, target, slot_own, later=True), slot_own)]
    for number in (*by_member.values(), *by_pair.values(), from_sibling[0][0]):
        moves.start(number)
    moves.task(start_gram)

    def sibling_place(place):
        def at():
            (index,) = place()
            return (index + 1 - 2 * lax.rem(index, 2),)

        return at

    def hand_on(place, arrivals):
        if len(arrivals) == 1:
            parts = [(place, arrivals[0])]
        else:
            parts = [(functools.partial(place, part), number) for part, number in enumerate(arrivals)]
        numbers = [
            moves.move((SHARDS,), sibling_peer, target, at, target, at, (number,)) for at, number in parts
        ]
        from_sibling.append((numbers, place))
        moves.task(add_gram(place))

    across = []
    for shift_member, first in by_member.items():
        for shift_pair, second in by_pair.items():
            top = functools.partial(slot, shift_member, 0, 0)
            bottom = functools.partial(slot, 0, shift_pair, 1)
            halves = [
                moves.move(
                    (SHARDS, 2 * shift_pair),
                    functools.partial(pair_peer, shift_pair),
                    target,
                    top,
                    target,
                    top,
                    (first,),
                ),
                moves.move(
                    (PATCHES, members, shift_member),
                    functools.partial(member_peer, members, shift_member),
                    target,
                    bottom,
                    target,
                    bottom,
                    (second,),
                ),
            ]
            across.append((functools.partial(slot, shift_member, shift_pair), halves))
    for shift, number in by_member.items():
        hand_on(functools.partial(slot, shift, 0), [number])
    for shift, number in by_pair.items():
        hand_on(functools.partial(slot, 0, shift), [number])
    moves.wait_for(from_sibling[0][0])
    moves.task(add_gram(sibling_place(slot_own)))
    for place, halves in across:
        hand_on(place, halves)
    for numbers, place in from_sibling[1:]:
        for number in numbers:
            moves.wait_for(number)
        moves.task(add_gram(sibling_place(place)))

    grad_rows = moves.output((seq_count, block_rows // seq_count, most_cols), LOW)
    for shift in range(1, seq_count):
        moves.start(
            moves.move(
                (PATCHES, shift),
                lambda shift=shift: {PATCHES: lax.rem(lax.axis_index(PATCHES) + shift, seq_count)},
                grad_low,
                lambda shift=shift: row_part(shift),
                grad_rows,
                lambda: (lax.axis_index(PATCHES),),
                later=True,
            )
        )
    moves.start_local(
        moves.keep(grad_low, lambda: row_part(0), grad_rows, lambda: (lax.axis_index(PATCHES),), True)
    )
    moves.task(
        lambda ref: newton_schulz(
            *[ref(item) for item in (source, gram, poly, once, gram_low, poly_low, once_low, state, state_next)]
        )
    )

    update_moves = []
    for shift in range(1, seq_count):
        update_moves.append(
            moves.move(
                (PATCHES, shift),
                lambda shift=shift: {PATCHES: lax.rem(lax.axis_index(PATCHES) + shift, seq_count)},
                state,
                functools.partial(row_part, shift),
                update,
                lambda: (lax.axis_index(PATCHES),),
                later=True,
            )
        )
        moves.start(update_moves[-1])

    def keep_rows(ref):
        ref(update)[lax.axis_index(PATCHES)] = ref(state)[row_part(0)]

    moves.task(keep_rows)

    def renew(ref):
        for which, (master, _) in enumerate(master_loads):
            cols = group_cols[which]
            rate = RATE_MUON * 0.2 * math.sqrt(masters[which].shape[1] * shards)
            for part in range(members):
                at = (slice(None), pl.ds(part * cols, cols))
                value = ref(update)[which * members + part, :, pl.ds(0, cols)].astype(f32)
                value = ref(master)[at] * (1.0 - RATE_MUON * DECAY_MUON) - rate * value
                ref(fresh[which])[at] = value
                ref(fresh_low[which])[at] = value.astype(LOW)

    for number in update_moves:
        moves.wait_for(number)
    for _, number in master_loads:
        moves.wait_local(number)
    moves.task(renew)
    moves.hand_over(sums, grad_ada, grad_table_all, *fresh)

    rows = block_rows // seq_count

    def row_place(back_group, back_member, start, size):
        seq_me = lax.axis_index(PATCHES)
        who = (seq_me // members - back_group) * members
        who = who + lax.rem(lax.rem(seq_me, members) + members - back_member, members)
        return (pl.ds(pl.multiple_of(who * rows + start, 16), size),)

    def has_group(offset):
        place = lax.axis_index(PATCHES) // members + offset
        return jnp.logical_and(place >= 0, place < MATRICES)

    def to_members(item_from, from_at, item_to, place, after, there):
        numbers = []
        for shift in range(1, members):
            numbers.append(
                moves.move(
                    (PATCHES, members, shift),
                    functools.partial(member_peer, members, shift),
                    item_from,
                    from_at,
                    item_to,
                    place,
                    after,
                    there,
                    there,
                    later=True,
                )
            )
            if not after:
                moves.start(numbers[-1])
        return numbers

    def along_line(distance, way, item_from, from_at, item_to, back_member, start, size, after):
        both = lambda: jnp.logical_and(has_group(way), has_group(-distance * way))
        number = moves.move(
            (PATCHES, seq_count, way),
            functools.partial(group_peer, members, (MATRICES + way) % MATRICES),
            item_from,
            from_at,
            item_to,
            functools.partial(row_place, distance * way, back_member, start, size),
            after,
            both,
            functools.partial(has_group, -(distance + 1) * way),
            later=True,
        )
        if not after:
            moves.start(number)
        return number

    items = []
    for which, item_from in enumerate(fresh_low):
        item_to = moves.output((rows * seq_count, moves.shape(item_from)[1]), LOW)
        place = functools.partial(row_place, 0, 0, 0, rows)
        moves.start_local(moves.keep(item_from, None, item_to, place, True))
        if which:
            items.append((item_from, item_to, 0, rows, False))
        else:
            items.append((item_from, item_to, rows // 2, rows // 2, True))
            items.append((item_from, item_to, 0, rows // 2, False))
    lines = []
    for item_from, item_to, start, size, members_first in items:
        from_at = lambda start=start, size=size: (pl.ds(start, size),)
        place = functools.partial(row_place, 0, 0, start, size)
        if members_first:
            crossing = to_members(item_from, from_at, item_to, place, (), None)
        for way in (1, -1):
            number = along_line(0, way, item_from, from_at, item_to, 0, start, size, ())
            lines.append([number, way, item_to, 0, start, size, members_first])
    for item_from, item_to, start, size, members_first in items:
        if not members_first:
            from_at = lambda start=start, size=size: (pl.ds(start, size),)
            to_members(item_from, from_at, item_to, functools.partial(row_place, 0, 0, start, size), (), None)
    for item_from, item_to, start, size, members_first in items:
        if members_first:
            for back_member, number in enumerate(crossing, 1):
                place = functools.partial(row_place, 0, back_member, start, size)
                for way in (1, -1):
                    following = along_line(0, way, item_to, place, item_to, back_member, start, size, (number,))
                    lines.append([following, way, item_to, back_member, start, size, True])
    for distance in range(1, MATRICES):
        for line in lines:
            number, way, item_to, back_member, start, size, members_first = line
            place = functools.partial(row_place, distance * way, back_member, start, size)
            if distance < MATRICES - 1:
                line[0] = along_line(
                    distance, way, item_to, place, item_to, back_member, start, size, (number,)
                )
            if not members_first:
                there = functools.partial(has_group, -distance * way)
                to_members(item_to, place, item_to, place, (number,), there)
    sums, grad_ada, grad_table_all, io_slices, *rest = moves.run()
    fresh, grad_rows, copies = rest[:MATRICES], rest[MATRICES], rest[MATRICES + 1 :]
    updated = update_all(
        members,
        sums,
        (ada_master, ada_first, ada_second, grad_ada),
        (pos_table, pos_first, pos_second, grad_pos),
        grad_rows,
        momenta,
    )
    ada_res, pos_res, moments = updated[:3], updated[3:6], updated[6:]
    sums = sums[0]
    grad_norm = jnp.sqrt(sums[0])
    loss_total = sums[1]
    clip = jnp.minimum(1.0, CLIP_LIMIT / (grad_norm + 1e-06))
    terms = sums[2 : 2 + 3 * MATRICES].reshape(MATRICES, 3)
    size_squares = MOMENTUM * MOMENTUM * terms[:, 0] + 2.0 * MOMENTUM * clip * terms[:, 1] + clip * clip * terms[:, 2]
    sizes = jnp.sqrt(jnp.maximum(size_squares, 0.0))
    moment_sizes = jnp.stack([sizes[which] for which in (0, 3, 1, 2)]) / CLIP_LIMIT
    grad_table = lax.dynamic_slice_in_dim(grad_table_all[:table_rows], shard * table_cols, table_cols, 1)
    grad_bias_all = jnp.concatenate([tail_all[:, 8].reshape(-1), tail_all[:, 9, :table_cols].reshape(-1)])
    grad_bias = lax.dynamic_slice_in_dim(grad_bias_all, shard * biases.shape[0], biases.shape[0])
    io_grad = io_slices.reshape(2, padded, io_cols)[:, :values_count].astype(f32)
    io_res = adam_update(io_proj, io_first, io_second, clip * io_grad, RATE_ADAM)
    cond_res = adam_update(cond_table, cond_first, cond_second, clip * grad_table, RATE_TABLE)
    bias_res = adam_update(biases, bias_first, bias_second, clip * grad_bias, RATE_ADAM)
    matrices = []
    for which in (0, 3, 1, 2):
        matrices += [fresh[which], moments[which], copies[which]]
    return (loss_total, grad_norm, moment_sizes, *matrices, *ada_res, *io_res, *cond_res, *pos_res, *bias_res)


def fits_fast(mesh):
    seq, shards = mesh.shape[PATCHES], mesh.shape[SHARDS]
    return HEADS % seq == 0 and (HEADS // seq * HEAD) % LANES == 0 and seq % MATRICES == 0 and shards % 2 == 0


def solution(mesh):
    body = fast_body if fits_fast(mesh) else general_body
    return jax.shard_map(
        body,
        mesh=mesh,
        in_specs=(
            P(SHARDS, PATCHES, None),
            P(SHARDS, PATCHES, None),
            P(SHARDS),
            P(),
            P(None, SHARDS),
            P(PATCHES, SHARDS),
            P(PATCHES, SHARDS),
            P(None, SHARDS),
            P(PATCHES, SHARDS),
            P(PATCHES, SHARDS),
            P(None, SHARDS),
            P(PATCHES, SHARDS),
            P(PATCHES, SHARDS),
            P(None, SHARDS),
            P(PATCHES, SHARDS),
            P(PATCHES, SHARDS),
            P(None, SHARDS),
            P(PATCHES, SHARDS),
            P(PATCHES, SHARDS),
            P(PATCHES, SHARDS),
            P(None, None, SHARDS),
            P(None, None, SHARDS),
            P(None, None, SHARDS),
            P(None, SHARDS),
            P(None, SHARDS),
            P(None, SHARDS),
            P(PATCHES, SHARDS),
            P(PATCHES, SHARDS),
            P(PATCHES, SHARDS),
            P(SHARDS),
            P(SHARDS),
            P(SHARDS),
        ),
        out_specs=(
            P(),
            P(),
            P(),
            P(PATCHES, SHARDS),
            P(PATCHES, SHARDS),
            P(None, SHARDS),
            P(PATCHES, SHARDS),
            P(PATCHES, SHARDS),
            P(None, SHARDS),
            P(PATCHES, SHARDS),
            P(PATCHES, SHARDS),
            P(None, SHARDS),
            P(PATCHES, SHARDS),
            P(PATCHES, SHARDS),
            P(None, SHARDS),
            P(PATCHES, SHARDS),
            P(PATCHES, SHARDS),
            P(PATCHES, SHARDS),
            P(None, None, SHARDS),
            P(None, None, SHARDS),
            P(None, None, SHARDS),
            P(None, SHARDS),
            P(None, SHARDS),
            P(None, SHARDS),
            P(PATCHES, SHARDS),
            P(PATCHES, SHARDS),
            P(PATCHES, SHARDS),
            P(SHARDS),
            P(SHARDS),
            P(SHARDS),
        ),
        check_vma=False,
    )
```
